32 devices in a mesh: dp: 8 (over y, x, core), tensor: 4 (over z).
Axes of the slice: x: 2, y: 2, z: 4, core: 2. Of those that a mesh axis runs over, the one named last changes fastest.
Arguments:
- tokens: bfloat16 [16384, 1536], P(('dp', 'tensor')), may hold values from -6 to 6
- cotangent: bfloat16 [16384, 1536], P(('dp', 'tensor')), may hold values from -6 to 6
- seq_lengths: int32 [8, 4], P('dp'), may hold values from 1 to 1537, as said below
- attn_gain: bfloat16 [1536], P('dp'), may hold values from 0.25 to 1.75
- q_weight: bfloat16 [1536, 1536], P('dp', 'tensor'), may hold values from -0.15625 to 0.15625
- key_projection: bfloat16 [1536, 768], P('dp', 'tensor'), may hold values from -0.15625 to 0.15625
- value_projection: bfloat16 [1536, 768], P('dp', 'tensor'), may hold values from -0.15625 to 0.15625
- out_weight: bfloat16 [1536, 1536], P('dp', 'tensor'), may hold values from -0.875 to 0.875
- mlp_gain: bfloat16 [1536], P('dp'), may hold values from 0.25 to 1.75
- gate_weight: bfloat16 [1536, 4096], P('dp', 'tensor'), may hold values from -0.15625 to 0.15625
- up_weight: bfloat16 [1536, 4096], P('dp', 'tensor'), may hold values from -0.15625 to 0.15625
- down_weight: bfloat16 [1536, 4096], P('dp', 'tensor'), may hold values from -0.09375 to 0.09375
Outputs:
- output: bfloat16 [16384, 1536], P(('dp', 'tensor'))
- input_grad: float32 [16384, 1536], P(('dp', 'tensor'))
- attn_gain_grad: float32 [1536], P('dp')
- q_weight_grad: float32 [1536, 1536], P('dp', 'tensor')
- k_weight_grad: float32 [1536, 768], P('dp', 'tensor')
- v_weight_grad: float32 [1536, 768], P('dp', 'tensor')
- out_weight_grad: float32 [1536, 1536], P('dp', 'tensor')
- mlp_gain_grad: float32 [1536], P('dp')
- gate_weight_grad: float32 [1536, 4096], P('dp', 'tensor')
- up_weight_grad: float32 [1536, 4096], P('dp', 'tensor')
- down_weight_grad: float32 [1536, 4096], P('dp', 'tensor')
The draws below stay inside these ranges and needn't reach their ends.
Inputs may be any that keep to these rules, and one draw needn't show every extreme that they name: Each row of seq_lengths sums to 2048. In each row one document, at a position drawn from the seed, has exactly 1537 tokens; the other documents of the row together hold 511 tokens.
All inputs are finite; a program needn't handle non-finite values.
Results may differ from the reference program's by a relative error of at most 0.02.
Values may be sent and summed in bfloat16 or wider, within the bound.
No kernel may reach another device: no remote copies, remote signals or barrier semaphores. Data moves between devices by JAX's collectives and lax.ppermute only.
A program may use at most 192 MiB of HBM per device.

```python
import jax
import jax.numpy as jnp
from jax import lax

MODEL_WIDTH = 1536
HD = 96
FF = 4096
SEQS = 4
HQ = 1536
KEY_VALUE_COLS = 768
GROUP = 2048
ROWS = 512
BLOCK = 512
GROUPS = 8
TOKENS = 16384


def draw_seq_lengths(key, part):
    key = jax.random.fold_in(key, 7)
    score_key, place_key = jax.random.split(key)
    short_total = ROWS - 1
    candidates = ROWS - 2
    raw_scores = jax.random.randint(score_key, (GROUPS, max(candidates, 1)), 0, 4096)
    distinct = raw_scores * max(candidates, 1) + jnp.arange(max(candidates, 1), dtype=jnp.int32)[None, :]
    order = jnp.argsort(distinct, axis=1, stable=True).astype(jnp.int32)
    cuts = jnp.sort(order[:, :SEQS - 2] + 1, axis=1).astype(jnp.int32)
    zeros = jnp.zeros((GROUPS, 1), jnp.int32)
    ends = jnp.full((GROUPS, 1), short_total, jnp.int32)
    bounds = jnp.concatenate([zeros, cuts, ends], axis=1)
    shorts = (bounds[:, 1:] - bounds[:, :-1]).astype(jnp.int32)
    placed = jax.random.randint(place_key, (GROUPS, 1), 0, SEQS)
    slots = jnp.arange(SEQS, dtype=jnp.int32)[None, :]
    source = jnp.clip(slots - (slots > placed).astype(jnp.int32), 0, SEQS - 2)
    picked = jnp.take_along_axis(shorts, source, axis=1)
    return jnp.where(slots == placed, GROUP - short_total, picked).astype(jnp.int32)


def strengthened(drawn, stream_key, source, target, parts, factor):
    owner, partner = [(jnp.arange(drawn.shape[axis_at]) // (drawn.shape[axis_at] // parts)).reshape([-1 if axis == axis_at else 1 for axis in range(drawn.ndim)]) for axis_at in (source, target)]
    chosen = jax.random.permutation(stream_key, parts)[partner]
    strong = (owner == chosen) | (owner == (partner + parts // 2) % parts)
    return jnp.where(strong, factor * drawn, drawn)


def shard_levels(key, shape, pieces, least, top_value):
    factor_of = 1.0
    for axis_at, parts in pieces:
        draws = jax.random.uniform(jax.random.fold_in(jax.random.fold_in(key, 6), axis_at), (parts,), jnp.float32, least / len(pieces), top_value / len(pieces))
        factor_of = factor_of * jnp.repeat(jnp.exp(draws), shape[axis_at] // parts).reshape((-1,) + (1,) * (len(shape) - 1 - axis_at))
    return factor_of


def centred(stream_key, extent, scale, reach, pieces=(), kind=jnp.bfloat16):
    gain = shard_levels(stream_key, extent, pieces, -0.22, 0.18) if pieces else 1.0
    array = jax.random.normal(stream_key, extent, jnp.float32) * scale * gain
    return jnp.minimum(jnp.maximum(array, -reach), reach).astype(kind)


def gaussian_with(rng, extent, width, bound, cuts, heavy, kind=jnp.bfloat16):
    values = width * jax.random.normal(rng, extent, jnp.float32)
    if cuts:
        values = values * shard_levels(rng, extent, cuts, -0.22, 0.18)
    return jnp.clip(strengthened(values, jax.random.fold_in(rng, 3), *heavy), -bound, bound).astype(kind)


def setup_inputs(seed: int = 0) -> dict:
    keys = jax.random.split(jax.random.key(seed), 13)
    return {
        "tokens": centred(keys[0], (TOKENS, MODEL_WIDTH), 1.0, 6.0, ((0, 32),)),
        "cotangent": gaussian_with(keys[1], (TOKENS, MODEL_WIDTH), 1.0, 6.0, ((0, 32),), (0, 1, 32, 2.75)),
        "seq_lengths": draw_seq_lengths(jax.random.fold_in(keys[12], 71), 0),
        "attn_gain": jnp.clip(1.0 + 0.15 * jax.random.normal(keys[3], (MODEL_WIDTH,), jnp.float32), 0.25, 1.75).astype(jnp.bfloat16),
        "q_weight": centred(keys[4], (MODEL_WIDTH, HQ), MODEL_WIDTH ** -0.5, 0.15625, ((0, 8), (1, 4))),
        "key_projection": centred(keys[5], (MODEL_WIDTH, KEY_VALUE_COLS), MODEL_WIDTH ** -0.5, 0.15625, ((0, 8), (1, 4))),
        "value_projection": centred(keys[6], (MODEL_WIDTH, KEY_VALUE_COLS), MODEL_WIDTH ** -0.5, 0.15625, ((0, 8), (1, 4))),
        "out_weight": centred(keys[7], (MODEL_WIDTH, HQ), (HQ // 32) ** -0.5, 0.875, ((0, 8), (1, 4))),
        "mlp_gain": jnp.clip(1.0 + 0.15 * jax.random.normal(keys[8], (MODEL_WIDTH,), jnp.float32), 0.25, 1.75).astype(jnp.bfloat16),
        "gate_weight": centred(keys[9], (MODEL_WIDTH, FF), MODEL_WIDTH ** -0.5, 0.15625, ((0, 8), (1, 4))),
        "up_weight": centred(keys[10], (MODEL_WIDTH, FF), MODEL_WIDTH ** -0.5, 0.15625, ((0, 8), (1, 4))),
        "down_weight": centred(keys[11], (MODEL_WIDTH, FF), FF ** -0.5, 0.09375, ((0, 8), (1, 4))),
    }


EPSILON = 1e-05
ROTARY_BASE = 100000.0
PRECISE = lax.Precision.HIGHEST

@jax.custom_vjp
def low(v):
    return lax.optimization_barrier(v.astype(jnp.bfloat16)).astype(jnp.float32)

@jax.custom_vjp
def low_back(v):
    return v

def low_keep(v):
    return (low(v), None)

def low_pass(kept, grad):
    return (grad,)

def back_keep(v):
    return (v, None)

def back_low(kept, grad):
    return (low(grad),)
low.defvjp(low_keep, low_pass)
low_back.defvjp(back_keep, back_low)

def document_layout(lengths, group_rows):
    flat_lengths = lengths.reshape(-1).astype(jnp.int32)
    doc_ends = jnp.cumsum(flat_lengths).astype(jnp.int32)
    positions = jnp.arange(group_rows, dtype=jnp.int32)
    passed = (positions[:, None] >= doc_ends[None, :]).astype(jnp.int32)
    doc_ids = lax.optimization_barrier(jnp.sum(passed, axis=1)).astype(jnp.int32)
    doc_starts = lax.optimization_barrier(jnp.sum(passed * flat_lengths[None, :], axis=1)).astype(jnp.int32)
    return (doc_ids, positions - doc_starts)

def rotary_tables(positions, head_size):
    half_size = head_size // 2
    exponents = jnp.arange(half_size, dtype=jnp.float32) * (2.0 / head_size)
    inverse = ROTARY_BASE ** (-exponents)
    angles = positions.astype(jnp.float32)[:, None] * inverse[None, :]
    return (jnp.cos(angles), jnp.sin(angles))

def rotate(values, cosine, sine, direction):
    row_total = values.shape[0]
    half_size = cosine.shape[1]
    halves = values.reshape(row_total, -1, 2, half_size)
    first_half = halves[:, :, 0, :]
    latter_half = halves[:, :, 1, :]
    cos_part = cosine[:, None, :]
    sin_part = sine[:, None, :] * direction
    new_first = first_half * cos_part - latter_half * sin_part
    new_second = latter_half * cos_part + first_half * sin_part
    return jnp.stack([new_first, new_second], axis=2).reshape(row_total, -1)

def matmul(left, right):
    return jnp.dot(left, right, precision=PRECISE)

def layer(values, params, doc_ids, cosine, sine):
    gain_one, w_query, w_key, w_value, w_out, gain_two, w_gate, w_up, w_down = params
    row_total = values.shape[0]
    scale_one = lax.rsqrt(lax.optimization_barrier(jnp.mean(values * values, axis=-1, keepdims=True)) + EPSILON)
    norm_one = low(values * scale_one * gain_one)
    q_lin = low_back(matmul(norm_one, w_query))
    k_lin = low_back(matmul(norm_one, w_key))
    value_rows = low(low_back(matmul(norm_one, w_value)))
    q_rot = low(rotate(q_lin, cosine, sine, 1.0))
    k_rot = low(rotate(k_lin, cosine, sine, 1.0))
    kv_heads = k_rot.shape[1] // HD
    group_ratio = q_rot.shape[1] // k_rot.shape[1]
    head_keys = k_rot.reshape(row_total, kv_heads, HD)
    value_heads = value_rows.reshape(row_total, kv_heads, HD)
    query_blocks = q_rot.reshape(row_total // BLOCK, BLOCK, kv_heads, group_ratio, HD)
    row_numbers = jnp.arange(row_total, dtype=jnp.int32)
    doc_blocks = doc_ids.reshape(row_total // BLOCK, BLOCK)
    row_blocks = row_numbers.reshape(row_total // BLOCK, BLOCK)

    def attend(block_args):
        query_block, doc_query, row_query = block_args
        scores = low_back(jnp.einsum('qgrd,kgd->grqk', query_block, head_keys, precision=PRECISE) * HD ** (-0.5))
        allowed = (doc_query[:, None] == doc_ids[None, :]) & (row_numbers[None, :] <= row_query[:, None])
        scores = jnp.where(allowed[None, None], scores, -1e+30)
        probs_low = low(jax.nn.softmax(scores, axis=-1))
        return jnp.einsum('grqk,kgd->qgrd', probs_low, value_heads, precision=PRECISE)
    context = lax.map(jax.checkpoint(attend), (query_blocks, doc_blocks, row_blocks))
    context = low(low_back(context.reshape(row_total, -1)))
    mid = values + low_back(matmul(context, w_out.T))
    scale_two = lax.rsqrt(lax.optimization_barrier(jnp.mean(mid * mid, axis=-1, keepdims=True)) + EPSILON)
    norm_two = low(mid * scale_two * gain_two)
    gate_lin = low_back(matmul(norm_two, w_gate))
    up_lin = low_back(matmul(norm_two, w_up))
    hidden = low(jax.nn.silu(gate_lin) * up_lin)
    return mid + low_back(matmul(hidden, w_down.T))

def reference(tokens, cotangent, seq_lengths, attn_gain, q_weight, key_projection, value_projection, out_weight, mlp_gain, gate_weight, up_weight, down_weight):
    params = tuple((weight.astype(jnp.float32) for weight in (attn_gain, q_weight, key_projection, value_projection, out_weight, mlp_gain, gate_weight, up_weight, down_weight)))
    inputs = tokens.astype(jnp.float32).reshape(GROUPS, GROUP, MODEL_WIDTH)
    upstreams = cotangent.astype(jnp.float32).reshape(GROUPS, GROUP, MODEL_WIDTH)

    def group_step(totals, group_data):
        values, upstream, lengths = group_data
        doc_ids, positions = document_layout(lengths, GROUP)
        cosine, sine = rotary_tables(positions, HD)

        def forward(layer_in, layer_params):
            return layer(layer_in, layer_params, doc_ids, cosine, sine)
        result, pullback = jax.vjp(forward, values, params)
        grad_in, grad_params = pullback(upstream)
        totals = jax.tree.map(jnp.add, totals, grad_params)
        return (totals, (result.astype(jnp.bfloat16), grad_in))
    initial = jax.tree.map(jnp.zeros_like, params)
    totals, (outputs, grads_in) = lax.scan(group_step, initial, (inputs, upstreams, seq_lengths))
    return (outputs.reshape(TOKENS, MODEL_WIDTH), grads_in.reshape(TOKENS, MODEL_WIDTH), totals[0], totals[1], totals[2], totals[3], totals[4], totals[5], totals[6], totals[7], totals[8])
```

```python
import functools
import math

import jax
import jax.numpy as jnp
import numpy as np
from jax import lax
from jax.experimental import pallas as pl
from jax.experimental.pallas import tpu as pltpu
from jax.sharding import Mesh
from jax.sharding import PartitionSpec as P

HD = 96
HALF = HD // 2
PAD = 128
TILE = 256

EPSILON = 1e-05
ROTARY_BASE = 100000.0
MASKED = -1e30
LOG2E = math.log2(math.e)

AXES = ("yx", "core", "zh", "zl")
FLIP = [(0, 1), (1, 0)]


def norm_rows(values, gain):
    row_scale = lax.rsqrt(jnp.mean(values * values, axis=-1, keepdims=True) + EPSILON)
    return (row_scale, (values * row_scale * gain).astype(jnp.bfloat16))


def norm_back(values, row_scale, gain, upstream):
    weighted = upstream * gain
    inner_sum = jnp.mean(weighted * values, axis=-1, keepdims=True)
    grad_in = row_scale * weighted - values * (row_scale * row_scale * row_scale) * inner_sum
    gain_part = jnp.sum(upstream * (values * row_scale), axis=0)
    return (grad_in, gain_part)


def document_layout(lengths, group_rows):
    flat_lengths = lengths.reshape(-1)
    doc_ends = jnp.cumsum(flat_lengths)
    rows = jnp.arange(group_rows, dtype=jnp.int32)
    passed = (rows[:, None] >= doc_ends[None, :]).astype(jnp.int32)
    return (rows, jnp.sum(passed * flat_lengths[None, :], axis=1))


def rotary_tables(positions):
    exponents = jnp.arange(HALF, dtype=jnp.float32) * (2.0 / HD)
    inverse = ROTARY_BASE ** (-exponents)
    angles = positions.astype(jnp.float32)[:, None] * inverse[None, :]
    cosine, sine = jnp.cos(angles), jnp.sin(angles)
    gap = jnp.zeros((positions.shape[0], PAD // 2 - HALF), jnp.float32)
    return (
        jnp.concatenate([cosine, gap, cosine, gap], axis=1),
        jnp.concatenate([-sine, gap, sine, gap], axis=1),
    )


def head_spread(heads):
    spread = np.zeros((heads * HD, heads * PAD), np.float32)
    for head in range(heads):
        for half in range(2):
            for i in range(HALF):
                spread[head * HD + half * HALF + i, head * PAD + half * (PAD // 2) + i] = 1.0
    return spread


def rows_product(left, right):
    return lax.dot_general(
        left, right, (((0,), (0,)), ((), ())), preferred_element_type=jnp.float32
    )


def times_transpose(left, right):
    return lax.dot_general(
        left, right, (((1,), (1,)), ((), ())), preferred_element_type=jnp.float32
    )


def dot32(left, right):
    return jnp.dot(left, right, preferred_element_type=jnp.float32)


def turn(x, cosine, sine):
    return x * cosine + pltpu.roll(x, PAD // 2, 1) * sine


def tile_scores(keys, queries, first_key, start, diagonal, masked):
    scores = times_transpose(keys, queries)
    if masked or diagonal:
        key_at = lax.broadcasted_iota(jnp.int32, scores.shape, 0)
        allowed = key_at + first_key >= start
        if diagonal:
            query_at = lax.rem(lax.broadcasted_iota(jnp.int32, scores.shape, 1), TILE)
            allowed = allowed & (key_at <= query_at)
        scores = jnp.where(allowed, scores, MASKED)
    return scores


def forward_kernel(
    q_heads, off, low, full, qkv, cosine, sine, start, spread_q, spread_kv, gather_q,
    context, log_sum, q_s, k_s, vt_s, acc,
):
    tiles, kv_heads = q_s.shape[0], q_s.shape[1]
    ratio = q_heads // kv_heads
    q_cols = q_heads * HD
    aligned = q_cols % PAD == 0
    scale = LOG2E * HD ** (-0.5)

    def prepare(t, carry):
        x = qkv[pl.ds(pl.multiple_of(off[t], TILE), TILE), :]
        cos_t = cosine[pl.ds(pl.multiple_of(t * TILE, TILE), TILE), :]
        sin_t = sine[pl.ds(pl.multiple_of(t * TILE, TILE), TILE), :]
        q = dot32(x[:, :q_cols] if aligned else x, spread_q[...])
        kv = dot32(x[:, q_cols:] if aligned else x, spread_kv[...])
        for h in range(kv_heads):
            key = turn(kv[:, h * PAD : (h + 1) * PAD], cos_t, sin_t)
            k_s[h, t] = key.astype(jnp.bfloat16)
            value = kv[:, (kv_heads + h) * PAD : (kv_heads + h + 1) * PAD]
            vt_s[h, t] = value.T.astype(jnp.bfloat16)
            for r in range(ratio):
                at = h * ratio + r
                query = turn(q[:, at * PAD : (at + 1) * PAD], cos_t, sin_t) * scale
                q_s[t, h, r * TILE : (r + 1) * TILE, :] = query.astype(jnp.bfloat16)
        return carry

    lax.fori_loop(0, tiles, prepare, 0)

    def query_tile(i, carry):
        acc[...] = jnp.zeros_like(acc)
        start_i = start[i]

        def step(j, state, diagonal, masked):
            new = []
            for h in range(kv_heads):
                top, total = state[h]
                s = tile_scores(k_s[h, j], q_s[i, h], j * TILE, start_i, diagonal, masked)
                peak = jnp.maximum(top, jnp.max(s, axis=0, keepdims=True))
                p = jnp.exp2(s - peak)
                fade = jnp.exp2(top - peak)
                total = total * fade + jnp.sum(p, axis=0, keepdims=True)
                acc[h] = acc[h] * fade + dot32(vt_s[h, j], p.astype(jnp.bfloat16))
                new.append((peak, total))
            return tuple(new)

        lanes = ratio * TILE
        state = tuple(
            (jnp.full((1, lanes), MASKED, jnp.float32), jnp.zeros((1, lanes), jnp.float32))
            for h in range(kv_heads)
        )
        state = lax.fori_loop(low[i], full[i], lambda j, s: step(j, s, False, True), state)
        state = lax.fori_loop(full[i], i, lambda j, s: step(j, s, False, False), state)
        state = step(i, state, True, True)
        parts = []
        for h in range(kv_heads):
            peak, total = state[h]
            log_sum[i * kv_heads + h] = peak + jnp.log(total) * LOG2E
            out = (acc[h] * (1.0 / total)).T
            for r in range(ratio):
                parts.append(out[r * TILE : (r + 1) * TILE, :])
        wide = jnp.concatenate(parts, axis=1).astype(jnp.bfloat16)
        at = pl.ds(pl.multiple_of(off[i], TILE), TILE)
        context[at, :] = dot32(wide, gather_q[...]).astype(jnp.bfloat16)
        return carry

    lax.fori_loop(0, tiles, query_tile, 0)


def backward_kernel(
    q_heads, off, low, full, qkv, d_context, context, cosine, sine, start, log_sum,
    spread_q, spread_kv, spread_o, gather_q, gather_kv,
    d_qkv, q_s, k_s, kt_s, v_s, do_s, delta_s, dq_acc, dk_acc, dv_acc, dq_s,
):
    tiles, kv_heads = q_s.shape[0], q_s.shape[1]
    ratio = q_heads // kv_heads
    q_cols = q_heads * HD
    aligned = q_cols % PAD == 0
    scale = HD ** (-0.5)

    def tables(t):
        at = pl.ds(pl.multiple_of(t * TILE, TILE), TILE)
        return cosine[at, :], sine[at, :]

    def prepare(t, carry):
        at = pl.ds(pl.multiple_of(off[t], TILE), TILE)
        x = qkv[at, :]
        cos_t, sin_t = tables(t)
        q = dot32(x[:, :q_cols] if aligned else x, spread_q[...])
        kv = dot32(x[:, q_cols:] if aligned else x, spread_kv[...])
        d_out = dot32(d_context[at, :], spread_o[...])
        out = dot32(context[at, :], spread_o[...])
        for h in range(kv_heads):
            key = turn(kv[:, h * PAD : (h + 1) * PAD], cos_t, sin_t)
            k_s[h, t] = key.astype(jnp.bfloat16)
            kt_s[h, t] = key.T.astype(jnp.bfloat16)
            value = kv[:, (kv_heads + h) * PAD : (kv_heads + h + 1) * PAD]
            v_s[h, t] = value.astype(jnp.bfloat16)
            dk_acc[h, t] = jnp.zeros((TILE, PAD), jnp.float32)
            dv_acc[h, t] = jnp.zeros((TILE, PAD), jnp.float32)
            for r in range(ratio):
                cols = slice((h * ratio + r) * PAD, (h * ratio + r + 1) * PAD)
                rows = slice(r * TILE, (r + 1) * TILE)
                query = turn(q[:, cols], cos_t, sin_t) * (scale * LOG2E)
                q_s[t, h, rows, :] = query.astype(jnp.bfloat16)
                do_s[t, h, rows, :] = d_out[:, cols].astype(jnp.bfloat16)
                product = (d_out[:, cols] * out[:, cols]).T
                delta_s[t * kv_heads + h, :, rows] = jnp.sum(product, axis=0, keepdims=True)
        return carry

    lax.fori_loop(0, tiles, prepare, 0)

    def query_tile(i, carry):
        dq_acc[...] = jnp.zeros_like(dq_acc)
        start_i = start[i]

        def step(j, diagonal, masked):
            for h in range(kv_heads):
                queries, d_out = q_s[i, h], do_s[i, h]
                s = tile_scores(k_s[h, j], queries, j * TILE, start_i, diagonal, masked)
                p = jnp.exp2(s - log_sum[i * kv_heads + h])
                d_p = times_transpose(v_s[h, j], d_out)
                d_s = (p * (d_p - delta_s[i * kv_heads + h])).astype(jnp.bfloat16)
                dv_acc[h, j] += dot32(p.astype(jnp.bfloat16), d_out)
                dk_acc[h, j] += dot32(d_s, queries)
                dq_acc[h] += dot32(kt_s[h, j], d_s)

        def loop(first, last, masked):
            def run(j, c):
                step(j, False, masked)
                return c

            lax.fori_loop(first, last, run, 0)

        loop(low[i], full[i], True)
        loop(full[i], i, False)
        step(i, True, True)
        cos_t, sin_t = tables(i)
        for h in range(kv_heads):
            grad = dq_acc[h].T * scale
            for r in range(ratio):
                piece = turn(grad[r * TILE : (r + 1) * TILE, :], cos_t, -sin_t)
                at = (h * ratio + r) * PAD
                dq_s[i, :, at : at + PAD] = piece.astype(jnp.bfloat16)
        return carry

    lax.fori_loop(0, tiles, query_tile, 0)

    def finish(t, carry):
        cos_t, sin_t = tables(t)
        keys = [turn(dk_acc[h, t] * (1.0 / LOG2E), cos_t, -sin_t) for h in range(kv_heads)]
        values = [dv_acc[h, t] for h in range(kv_heads)]
        wide = jnp.concatenate(keys + values, axis=1).astype(jnp.bfloat16)
        at = pl.ds(pl.multiple_of(off[t], TILE), TILE)
        d_q = dot32(dq_s[t], gather_q[...])
        d_kv = dot32(wide, gather_kv[...])
        if aligned:
            d_qkv[at, :q_cols] = d_q.astype(jnp.bfloat16)
            d_qkv[at, q_cols:] = d_kv.astype(jnp.bfloat16)
        else:
            d_qkv[at, :] = (d_q + d_kv).astype(jnp.bfloat16)
        return carry

    lax.fori_loop(0, tiles, finish, 0)


def spreads(q_heads, kv_heads):
    q, kv = head_spread(q_heads), head_spread(2 * kv_heads)
    full_q, full_kv = q, kv
    if (q_heads * HD) % PAD:
        full_q = np.concatenate([q, np.zeros((kv.shape[0], q.shape[1]), np.float32)])
        full_kv = np.concatenate([np.zeros((q.shape[0], kv.shape[1]), np.float32), kv])
    return tuple(jnp.asarray(m, jnp.bfloat16) for m in (full_q, full_kv, q))


SMEM = pl.BlockSpec(memory_space=pltpu.SMEM)
VMEM = pl.BlockSpec(memory_space=pltpu.VMEM)


def attention_cost(rows, q_heads, products):
    pairs = q_heads * rows * rows // 2
    return pl.CostEstimate(
        flops=products * 2 * pairs * PAD, bytes_accessed=rows * q_heads * HD * 12, transcendentals=pairs
    )


def attend(qkv, layout, q_heads, kv_heads):
    off, low, full, cosine, sine, start = layout
    rows = qkv.shape[0]
    tiles = rows // TILE
    lanes = (q_heads // kv_heads) * TILE
    spread_q, spread_kv, spread_o = spreads(q_heads, kv_heads)
    bf16, f32 = jnp.bfloat16, jnp.float32
    return pl.pallas_call(
        functools.partial(forward_kernel, q_heads),
        out_shape=(
            jax.ShapeDtypeStruct((rows, q_heads * HD), bf16),
            jax.ShapeDtypeStruct((tiles * kv_heads, 1, lanes), f32),
        ),
        in_specs=[SMEM] * 3 + [VMEM] * 7,
        out_specs=(VMEM, VMEM),
        scratch_shapes=[
            pltpu.VMEM((tiles, kv_heads, lanes, PAD), bf16),
            pltpu.VMEM((kv_heads, tiles, TILE, PAD), bf16),
            pltpu.VMEM((kv_heads, tiles, PAD, TILE), bf16),
            pltpu.VMEM((kv_heads, PAD, lanes), f32),
        ],
        compiler_params=pltpu.CompilerParams(vmem_limit_bytes=48 * 2**20),
        cost_estimate=attention_cost(rows, q_heads, 2),
        name="attention_forward",
    )(off, low, full, qkv, cosine, sine, start, spread_q, spread_kv, spread_o.T)


def attend_back(qkv, d_context, context, log_sum, layout, q_heads, kv_heads):
    off, low, full, cosine, sine, start = layout
    rows = qkv.shape[0]
    tiles = rows // TILE
    lanes = (q_heads // kv_heads) * TILE
    spread_q, spread_kv, spread_o = spreads(q_heads, kv_heads)
    bf16, f32 = jnp.bfloat16, jnp.float32
    return pl.pallas_call(
        functools.partial(backward_kernel, q_heads),
        out_shape=jax.ShapeDtypeStruct(qkv.shape, bf16),
        in_specs=[SMEM] * 3 + [VMEM] * 12,
        out_specs=VMEM,
        scratch_shapes=[
            pltpu.VMEM((tiles, kv_heads, lanes, PAD), bf16),
            pltpu.VMEM((kv_heads, tiles, TILE, PAD), bf16),
            pltpu.VMEM((kv_heads, tiles, PAD, TILE), bf16),
            pltpu.VMEM((kv_heads, tiles, TILE, PAD), bf16),
            pltpu.VMEM((tiles, kv_heads, lanes, PAD), bf16),
            pltpu.VMEM((tiles * kv_heads, 1, lanes), f32),
            pltpu.VMEM((kv_heads, PAD, lanes), f32),
            pltpu.VMEM((kv_heads, tiles, TILE, PAD), f32),
            pltpu.VMEM((kv_heads, tiles, TILE, PAD), f32),
            pltpu.VMEM((tiles, TILE, q_heads * PAD), bf16),
        ],
        compiler_params=pltpu.CompilerParams(vmem_limit_bytes=56 * 2**20),
        cost_estimate=attention_cost(rows, q_heads, 5),
        name="attention_backward",
    )(
        off, low, full, qkv, d_context, context, cosine, sine, start, log_sum,
        spread_q, spread_kv, spread_o, spread_q.T, spread_kv.T,
    )


def flip(x, axis):
    return lax.ppermute(x, axis, FLIP)


def swap(x):
    return lax.ppermute(x, ("core", "zh"), [(0, 0), (1, 2), (2, 1), (3, 3)])


def from_near(x, k):
    n = lax.axis_size("zl")
    return x if k == 0 else lax.ppermute(x, "zl", [((j + k) % n, j) for j in range(n)])


def to_near(x, k):
    n = lax.axis_size("zl")
    return lax.ppermute(x, "zl", [(j, (j + k) % n) for j in range(n)])


def gather_rows(x):
    near = jnp.concatenate([from_near(x, k) for k in range(lax.axis_size("zl"))], axis=0)
    return jnp.concatenate([near, flip(near, "core")], axis=0)


def scatter_rows(x, rows):
    half = x.shape[0] // 2
    other = flip(x[half:].astype(jnp.bfloat16), "core")
    total = None
    for k in range(lax.axis_size("zl")):
        at = slice(k * rows, (k + 1) * rows)
        part = x[at].astype(jnp.float32) + other[at].astype(jnp.float32)
        if k == 0:
            total = part
        else:
            total = total + to_near(part.astype(jnp.bfloat16), k).astype(jnp.float32)
    return total


def gather_weight(w):
    core, zh = lax.axis_index("core"), lax.axis_index("zh")
    far = flip(w, "zh")
    mine = jnp.where(core == zh, w, far)
    give = jnp.where(core == zh, far, w)
    taken = flip(give, "core")
    pair = jnp.concatenate(
        [jnp.where(core == 0, mine, taken), jnp.where(core == 0, taken, mine)], axis=0
    )
    return lax.all_gather(pair, "yx", axis=0, tiled=True)


def scatter_grad(grad):
    core, zh = lax.axis_index("core"), lax.axis_index("zh")
    part = lax.psum_scatter(grad, "yx", scatter_dimension=0, tiled=True)
    half = part.shape[0] // 2
    upper, lower = part[:half], part[half:]
    mine = jnp.where(core == 0, upper, lower)
    taken = flip(jnp.where(core == 0, lower, upper), "core")
    keep = jnp.where(core == zh, mine, taken)
    give = jnp.where(core == zh, taken, mine)
    return keep.astype(jnp.float32) + flip(give, "zh").astype(jnp.float32)


def body(
    tokens,
    cotangent,
    seq_lengths,
    attn_gain,
    q_weight,
    key_projection,
    value_projection,
    out_weight,
    mlp_gain,
    gate_weight,
    up_weight,
    down_weight,
):
    bf16, f32 = jnp.bfloat16, jnp.float32
    core, zl = lax.axis_index("core"), lax.axis_index("zl")
    near = lax.axis_size("zl")
    rows = tokens.shape[0]
    group_rows = 2 * near * rows
    query_cols, key_cols = q_weight.shape[1], key_projection.shape[1]
    q_heads, kv_heads = query_cols // HD, key_cols // HD
    hidden_cols = gate_weight.shape[1]

    w_project = gather_weight(jnp.concatenate([q_weight, key_projection, value_projection], axis=1))
    gains = lax.all_gather(jnp.stack([attn_gain, mlp_gain]), ("yx", "core"), axis=1, tiled=True)
    gain_one, gain_two = gains[0].astype(f32), gains[1].astype(f32)
    w_out = gather_weight(out_weight)
    w_gate_up = gather_weight(jnp.concatenate([gate_weight, up_weight], axis=1))
    w_down = gather_weight(down_weight)

    own_tokens = swap(tokens)
    own_cotangent = swap(cotangent)
    lengths = swap(seq_lengths)

    tile = jnp.arange(group_rows // TILE, dtype=jnp.int32)
    block = tile * TILE // rows
    place = ((block // near) ^ core) * near + (block % near - zl) % near
    off = place * rows + tile * TILE % rows
    row_at, doc_start = document_layout(lengths, group_rows)
    tile_start = doc_start.reshape(-1, TILE)
    low = tile_start[:, 0] // TILE
    full = jnp.minimum((tile_start[:, -1] + TILE - 1) // TILE, tile)
    cosine, sine = rotary_tables(row_at - doc_start)
    start = jnp.tile(tile_start[:, None, :], (1, 1, q_heads // kv_heads))
    layout = (off, low, full, cosine, sine, start)

    residual = own_tokens.astype(f32)
    scale_one, norm_one = norm_rows(residual, gain_one)
    norm_one_all = gather_rows(norm_one)
    qkv = dot32(norm_one_all, w_project).astype(bf16)
    context, log_sum = attend(qkv, layout, q_heads, kv_heads)
    mid = residual + scatter_rows(times_transpose(context, w_out).astype(bf16), rows)
    scale_two, norm_two = norm_rows(mid, gain_two)
    norm_two_all = gather_rows(norm_two)
    gate_up = dot32(norm_two_all, w_gate_up)
    gate_lin, up_lin = gate_up[:, :hidden_cols], gate_up[:, hidden_cols:]
    sigmoid_gate = jax.nn.sigmoid(gate_lin)
    silu_gate = gate_lin * sigmoid_gate
    hidden = (silu_gate * up_lin).astype(bf16)
    grad_rows = gather_rows(own_cotangent)
    d_hidden = dot32(grad_rows, w_down)
    d_gate = (d_hidden * up_lin * sigmoid_gate * (1.0 + gate_lin * (1.0 - sigmoid_gate))).astype(bf16)
    d_up = (d_hidden * silu_gate).astype(bf16)
    d_gate_up = jnp.concatenate([d_gate, d_up], axis=1)
    d_norm_two = scatter_rows(times_transpose(d_gate_up, w_gate_up).astype(bf16), rows)
    grad_down = scatter_grad(rows_product(grad_rows, hidden).astype(bf16))
    grad_gate_up = scatter_grad(rows_product(norm_two_all, d_gate_up).astype(bf16))
    mid_back, gain_two_part = norm_back(mid, scale_two, gain_two, d_norm_two)
    d_mid = own_cotangent.astype(f32) + mid_back
    d_attn_all = gather_rows(d_mid.astype(bf16))
    d_context = dot32(d_attn_all, w_out).astype(bf16)
    grad_out = scatter_grad(rows_product(d_attn_all, context).astype(bf16))
    output = swap((mid + scatter_rows(times_transpose(hidden, w_down).astype(bf16), rows)).astype(bf16))
    d_project = attend_back(qkv, d_context, context, log_sum, layout, q_heads, kv_heads)
    d_norm_one = scatter_rows(times_transpose(d_project, w_project).astype(bf16), rows)
    grad_project = scatter_grad(rows_product(norm_one_all, d_project).astype(bf16))
    input_back, gain_one_part = norm_back(residual, scale_one, gain_one, d_norm_one)
    input_grad = swap((d_mid + input_back).astype(bf16)).astype(f32)
    gain_sums = lax.psum(jnp.stack([gain_one_part, gain_two_part]), AXES)
    width = attn_gain.shape[0]
    first = (lax.axis_index("yx") * 2 + core) * width
    gain_grads = lax.dynamic_slice_in_dim(gain_sums, first, width, 1)
    return (
        output,
        input_grad,
        gain_grads[0],
        grad_project[:, :query_cols],
        grad_project[:, query_cols : query_cols + key_cols],
        grad_project[:, query_cols + key_cols :],
        grad_out,
        gain_grads[1],
        grad_gate_up[:, :hidden_cols],
        grad_gate_up[:, hidden_cols:],
        grad_down,
    )


def solution(mesh):
    dp, tensor = mesh.shape["dp"], mesh.shape["tensor"]
    fine = Mesh(mesh.devices.reshape(dp // 2, 2, 2, tensor // 2), AXES)
    by_rows, by_dp, by_both = P(AXES, None), P(("yx", "core")), P(("yx", "core"), ("zh", "zl"))
    return jax.shard_map(
        body,
        mesh=fine,
        in_specs=(
            by_rows, by_rows, P(("yx", "core"), None), by_dp, by_both, by_both, by_both, by_both,
            by_dp, by_both, by_both, by_both,
        ),
        out_specs=(
            by_rows, by_rows, by_dp, by_both, by_both, by_both, by_both, by_dp, by_both, by_both, by_both,
        ),
        check_vma=False,
    )
```

```python
import functools
import math

import jax
import jax.numpy as jnp
import numpy as np
from jax import lax
from jax.experimental import pallas as pl
from jax.experimental.pallas import tpu as pltpu
from jax.sharding import Mesh
from jax.sharding import PartitionSpec as P

HD = 96
HALF = HD // 2
PAD = 128
SUB = 256
TILE = 512

EPSILON = 1e-05
ROTARY_BASE = 100000.0
MASKED = -1e30
LOG2E = math.log2(math.e)

AXES = ("yx", "core", "zh", "zl")
FLIP = [(0, 1), (1, 0)]


def norm_rows(values, gain):
    row_scale = lax.rsqrt(jnp.mean(values * values, axis=-1, keepdims=True) + EPSILON)
    return (row_scale, (values * row_scale * gain).astype(jnp.bfloat16))


def norm_back(values, row_scale, gain, upstream):
    weighted = upstream * gain
    inner_sum = jnp.mean(weighted * values, axis=-1, keepdims=True)
    grad_in = row_scale * weighted - values * (row_scale * row_scale * row_scale) * inner_sum
    gain_part = jnp.sum(upstream * (values * row_scale), axis=0)
    return (grad_in, gain_part)


def document_layout(lengths, group_rows):
    flat_lengths = lengths.reshape(-1)
    doc_ends = jnp.cumsum(flat_lengths)
    rows = jnp.arange(group_rows, dtype=jnp.int32)
    passed = (rows[:, None] >= doc_ends[None, :]).astype(jnp.int32)
    return (rows, jnp.sum(passed * flat_lengths[None, :], axis=1))


def rotary_tables(positions):
    exponents = jnp.arange(HALF, dtype=jnp.float32) * (2.0 / HD)
    inverse = ROTARY_BASE ** (-exponents)
    angles = positions.astype(jnp.float32)[:, None] * inverse[None, :]
    cosine, sine = jnp.cos(angles), jnp.sin(angles)
    gap = jnp.zeros((positions.shape[0], PAD // 2 - HALF), jnp.float32)
    return (
        jnp.concatenate([cosine, gap, cosine, gap], axis=1),
        jnp.concatenate([-sine, gap, sine, gap], axis=1),
    )


def rows_product(left, right):
    return lax.dot_general(
        left, right, (((0,), (0,)), ((), ())), preferred_element_type=jnp.float32
    )


def times_transpose(left, right):
    return lax.dot_general(
        left, right, (((1,), (1,)), ((), ())), preferred_element_type=jnp.float32
    )


def dot32(left, right):
    return jnp.dot(left, right, preferred_element_type=jnp.float32)


def after(x, *earlier):
    return lax.optimization_barrier((x, *earlier))[0]


def spread(columns, heads):
    matrix = np.zeros((columns, len(heads) * PAD), np.float32)
    for at, first in enumerate(heads):
        for half in range(2):
            for i in range(HALF):
                matrix[first + half * HALF + i, at * PAD + half * (PAD // 2) + i] = 1.0
    return matrix


def turn(x, cosine, sine):
    return x * cosine + pltpu.roll(x, PAD // 2, 1) * sine


def rows_at(t, size):
    return pl.ds(pl.multiple_of(t * size, size), size)


def forward_kernel(pieces, ratio, more, *refs):
    place, low, full, cosine, sine, start, spread_in, gather_out = refs[:8]
    qkv, refs = refs[8 : 8 + pieces], refs[8 + pieces :]
    earlier = ()
    if more:
        earlier, refs = refs[:pieces], refs[pieces:]
    context, refs = refs[:pieces], refs[pieces:]
    log_sum, q_s, k_s, v_s, s_s, top_s, acc = refs
    tiles = q_s.shape[0]
    piece_subs = qkv[0].shape[0] // SUB
    scale = LOG2E * HD ** (-0.5)
    ones_lane = lax.broadcasted_iota(jnp.int32, (SUB, PAD), 1) == PAD - 1

    for k in range(pieces):

        def prepare(r, carry, k=k):
            t = place[k * piece_subs + r]
            wide = dot32(qkv[k][rows_at(r, SUB), :], spread_in[...])
            at = rows_at(t, SUB)
            cos_t, sin_t = cosine[at, :], sine[at, :]
            tile, half = t // (TILE // SUB), t % (TILE // SUB)
            for h in range(ratio):
                query = turn(wide[:, h * PAD : (h + 1) * PAD], cos_t, sin_t) * scale
                first = pl.multiple_of(h * TILE + half * SUB, SUB)
                q_s[tile, pl.ds(first, SUB), :] = query.astype(jnp.bfloat16)
            key = turn(wide[:, ratio * PAD : (ratio + 1) * PAD], cos_t, sin_t)
            k_s[at, :] = key.astype(jnp.bfloat16)
            value = jnp.where(ones_lane, 1.0, wide[:, (ratio + 1) * PAD :])
            v_s[at, :] = value.astype(jnp.bfloat16)
            return carry

        lax.fori_loop(0, piece_subs, prepare, 0)

    def query_tile(i, carry):
        queries = q_s[i]
        starts = jnp.concatenate([start[rows_at(i, TILE), :]] * ratio, axis=0)
        top_s[...] = jnp.full_like(top_s, MASKED)

        def scores(j, masked, diagonal):
            s = times_transpose(queries, k_s[rows_at(j, TILE), :])
            if masked:
                key_at = lax.broadcasted_iota(jnp.int32, s.shape, 1)
                allowed = key_at + j * TILE >= starts
                if diagonal:
                    query_at = lax.rem(lax.broadcasted_iota(jnp.int32, s.shape, 0), TILE)
                    allowed = allowed & (key_at <= query_at)
                s = jnp.where(allowed, s, MASKED)
            s_s[j] = s
            peak = s[:, :PAD]
            for c in range(1, TILE // PAD):
                peak = jnp.maximum(peak, s[:, c * PAD : (c + 1) * PAD])
            top_s[...] = jnp.maximum(top_s[...], peak)

        def loop(first, last, masked):
            def run(j, c):
                scores(j, masked, False)
                return c

            lax.fori_loop(first, last, run, 0)

        loop(low[i], full[i], True)
        loop(full[i], i, False)
        scores(i, True, True)
        top = jnp.max(top_s[...], axis=1, keepdims=True)
        acc[...] = jnp.zeros_like(acc)

        def weigh(j, c):
            p = jnp.exp2(s_s[j] - top).astype(jnp.bfloat16)
            acc[...] += dot32(p, v_s[rows_at(j, TILE), :])
            return c

        lax.fori_loop(low[i], i + 1, weigh, 0)
        total = acc[:, PAD - 1 :]
        out = acc[...] * (1.0 / total)
        sums = jnp.broadcast_to(top + jnp.log(total) * LOG2E, (ratio * TILE, PAD))
        log_sum[i] = sums.T[:1, :]
        wide = jnp.concatenate(
            [out[h * TILE : (h + 1) * TILE, :] for h in range(ratio)], axis=1
        ).astype(jnp.bfloat16)
        packed = dot32(wide, gather_out[...])
        subs = tiles * (TILE // SUB)
        for half in range(TILE // SUB):
            r = place[subs + i * (TILE // SUB) + half]
            part = packed[half * SUB : (half + 1) * SUB, :].astype(jnp.bfloat16)
            for k in range(pieces):

                @pl.when(r // piece_subs == k)
                def store(k=k, part=part, r=r):
                    at = rows_at(r % piece_subs, SUB)
                    context[k][at, :] = part + earlier[k][at, :] if more else part

        return carry

    lax.fori_loop(0, tiles, query_tile, 0)


def backward_kernel(pieces, ratio, more, *refs):
    place, low, full, cosine, sine, start, log_sum, spread_in, spread_out, gather_in = refs[:10]
    refs = refs[10:]
    qkv, d_context, context, refs = (
        refs[:pieces], refs[pieces : 2 * pieces], refs[2 * pieces : 3 * pieces], refs[3 * pieces :],
    )
    earlier = ()
    if more:
        earlier, refs = refs[:pieces], refs[pieces:]
    d_qkv, refs = refs[:pieces], refs[pieces:]
    q_s, k_s, kt_s, v_s, do_s, delta_s, dq_acc, dk_acc, dv_acc, dq_s = refs
    tiles = q_s.shape[0]
    piece_subs = qkv[0].shape[0] // SUB
    scale = HD ** (-0.5)

    for k in range(pieces):

        def prepare(r, carry, k=k):
            t = place[k * piece_subs + r]
            rel = rows_at(r, SUB)
            wide = dot32(qkv[k][rel, :], spread_in[...])
            d_out = dot32(d_context[k][rel, :], spread_out[...])
            out = dot32(context[k][rel, :], spread_out[...])
            at = rows_at(t, SUB)
            cos_t, sin_t = cosine[at, :], sine[at, :]
            tile, half = t // (TILE // SUB), t % (TILE // SUB)
            for h in range(ratio):
                cols = slice(h * PAD, (h + 1) * PAD)
                rows = pl.ds(pl.multiple_of(h * TILE + half * SUB, SUB), SUB)
                query = turn(wide[:, cols], cos_t, sin_t) * (scale * LOG2E)
                q_s[tile, rows, :] = query.astype(jnp.bfloat16)
                do_s[tile, rows, :] = d_out[:, cols].astype(jnp.bfloat16)
                delta = jnp.sum((d_out[:, cols] * out[:, cols]).T, axis=0, keepdims=True)
                delta_s[tile, :, rows] = delta
            key = turn(wide[:, ratio * PAD : (ratio + 1) * PAD], cos_t, sin_t)
            k_s[at, :] = key.astype(jnp.bfloat16)
            kt_s[tile, half] = key.T.astype(jnp.bfloat16)
            v_s[at, :] = wide[:, (ratio + 1) * PAD :].astype(jnp.bfloat16)
            return carry

        lax.fori_loop(0, piece_subs, prepare, 0)

    dk_acc[...] = jnp.zeros_like(dk_acc)
    dv_acc[...] = jnp.zeros_like(dv_acc)

    def query_tile(i, carry):
        dq_acc[...] = jnp.zeros_like(dq_acc)

        def step(j, masked, diagonal):
            at = rows_at(j, TILE)
            queries, d_out = q_s[i], do_s[i]
            s = times_transpose(k_s[at, :], queries)
            if masked:
                key_at = lax.broadcasted_iota(jnp.int32, s.shape, 0)
                allowed = key_at + j * TILE >= start[i]
                if diagonal:
                    query_at = lax.rem(lax.broadcasted_iota(jnp.int32, s.shape, 1), TILE)
                    allowed = allowed & (key_at <= query_at)
                s = jnp.where(allowed, s, MASKED)
            p = jnp.exp2(s - log_sum[i])
            d_p = times_transpose(v_s[at, :], d_out)
            d_s = (p * (d_p - delta_s[i])).astype(jnp.bfloat16)
            dv_acc[at, :] += dot32(p.astype(jnp.bfloat16), d_out)
            dk_acc[at, :] += dot32(d_s, queries)
            total = dot32(kt_s[j, 0], d_s[:SUB, :])
            for half in range(1, TILE // SUB):
                total += dot32(kt_s[j, half], d_s[half * SUB : (half + 1) * SUB, :])
            dq_acc[...] += total

        def loop(first, last, masked):
            def run(j, c):
                step(j, masked, False)
                return c

            lax.fori_loop(first, last, run, 0)

        loop(low[i], full[i], True)
        loop(full[i], i, False)
        step(i, True, True)
        at = rows_at(i, TILE)
        cos_t, sin_t = cosine[at, :], sine[at, :]
        grad = dq_acc[...].T * scale
        for h in range(ratio):
            piece = turn(grad[h * TILE : (h + 1) * TILE, :], cos_t, -sin_t)
            dq_s[at, h * PAD : (h + 1) * PAD] = piece.astype(jnp.bfloat16)
        return carry

    lax.fori_loop(0, tiles, query_tile, 0)

    for k in range(pieces):

        def finish(r, carry, k=k):
            at = rows_at(place[k * piece_subs + r], SUB)
            key = turn(dk_acc[at, :] * (1.0 / LOG2E), cosine[at, :], -sine[at, :])
            wide = jnp.concatenate(
                [dq_s[at, :], key.astype(jnp.bfloat16), dv_acc[at, :].astype(jnp.bfloat16)], axis=1
            )
            packed = dot32(wide, gather_in[...]).astype(jnp.bfloat16)
            rel = rows_at(r, SUB)
            d_qkv[k][rel, :] = packed + earlier[k][rel, :] if more else packed
            return carry

        lax.fori_loop(0, piece_subs, finish, 0)


SMEM = pl.BlockSpec(memory_space=pltpu.SMEM)
VMEM = pl.BlockSpec(memory_space=pltpu.VMEM)
ANY = pl.BlockSpec(memory_space=pl.ANY)


def attention_cost(rows, heads, products):
    pairs = heads * rows * rows * 5 // 8
    return pl.CostEstimate(
        flops=products * 4 * pairs * PAD, bytes_accessed=rows * 8192, transcendentals=pairs
    )


def head_matrices(head, q_heads, kv_heads):
    ratio = q_heads // kv_heads
    queries = [(head * ratio + r) * HD for r in range(ratio)]
    key, value = (q_heads + head) * HD, (q_heads + kv_heads + head) * HD
    inner = spread((q_heads + 2 * kv_heads) * HD, [*queries, key, value])
    outer = spread(q_heads * HD, queries)
    return jnp.asarray(inner, jnp.bfloat16), jnp.asarray(outer, jnp.bfloat16)


def attend(qkv, layout, q_heads, kv_heads):
    place, low, full, cosine, sine, start_column, start_row = layout
    pieces, ratio = len(qkv), q_heads // kv_heads
    rows = pieces * qkv[0].shape[0]
    tiles, lanes = rows // TILE, ratio * TILE
    bf16, f32 = jnp.bfloat16, jnp.float32
    context, sums = [], []
    for head in range(kv_heads):
        inner, outer = head_matrices(head, q_heads, kv_heads)
        *context, log_sum = pl.pallas_call(
            functools.partial(forward_kernel, pieces, ratio, head > 0),
            out_shape=[
                *(jax.ShapeDtypeStruct((x.shape[0], q_heads * HD), bf16) for x in qkv),
                jax.ShapeDtypeStruct((tiles, 1, lanes), f32),
            ],
            in_specs=[SMEM] * 3 + [VMEM] * (5 + pieces + len(context)),
            out_specs=[VMEM] * (pieces + 1),
            scratch_shapes=[
                pltpu.VMEM((tiles, lanes, PAD), bf16),
                pltpu.VMEM((rows, PAD), bf16),
                pltpu.VMEM((rows, PAD), bf16),
                pltpu.VMEM((tiles, lanes, TILE), f32),
                pltpu.VMEM((lanes, PAD), f32),
                pltpu.VMEM((lanes, PAD), f32),
            ],
            compiler_params=pltpu.CompilerParams(vmem_limit_bytes=48 * 2**20),
            cost_estimate=attention_cost(rows, ratio, 2),
            name=f"attention_forward_{head}",
        )(place, low, full, cosine, sine, start_column, inner, outer.T, *qkv, *context)
        sums.append(log_sum)
    return context, sums


def attend_back(qkv, d_context, context, sums, layout, q_heads, kv_heads):
    place, low, full, cosine, sine, start_column, start_row = layout
    pieces, ratio = len(qkv), q_heads // kv_heads
    rows = pieces * qkv[0].shape[0]
    tiles, lanes = rows // TILE, ratio * TILE
    bf16, f32 = jnp.bfloat16, jnp.float32
    d_qkv = []
    for head in range(kv_heads):
        inner, outer = head_matrices(head, q_heads, kv_heads)
        d_qkv = pl.pallas_call(
            functools.partial(backward_kernel, pieces, ratio, head > 0),
            out_shape=[jax.ShapeDtypeStruct(x.shape, bf16) for x in qkv],
            in_specs=[SMEM] * 3 + [VMEM] * (7 + 3 * pieces + len(d_qkv)),
            out_specs=[VMEM] * pieces,
            scratch_shapes=[
                pltpu.VMEM((tiles, lanes, PAD), bf16),
                pltpu.VMEM((rows, PAD), bf16),
                pltpu.VMEM((tiles, TILE // SUB, PAD, SUB), bf16),
                pltpu.VMEM((rows, PAD), bf16),
                pltpu.VMEM((tiles, lanes, PAD), bf16),
                pltpu.VMEM((tiles, 1, lanes), f32),
                pltpu.VMEM((PAD, lanes), f32),
                pltpu.VMEM((rows, PAD), f32),
                pltpu.VMEM((rows, PAD), f32),
                pltpu.VMEM((rows, ratio * PAD), bf16),
            ],
            compiler_params=pltpu.CompilerParams(vmem_limit_bytes=56 * 2**20),
            cost_estimate=attention_cost(rows, ratio, 5),
            name=f"attention_backward_{head}",
        )(
            place, low, full, cosine, sine, start_row, sums[head], inner, outer, inner.T,
            *qkv, *d_context, *context, *d_qkv,
        )
    return d_qkv


def mlp_kernel(blocks, more, me, own_n, sib_n, own_c, sib_c, *refs):
    gate_up, refs = refs[:blocks], refs[blocks:]
    down, refs = refs[:blocks], refs[blocks:]
    refs = refs[4:] if more else refs
    norm_all, grad_all, hidden_all, d_gate_up_all, d_norm, out, refs = *refs[:6], refs[6:]
    w_gate_up, w_down, gate_sems, down_sems = refs
    i, steps = pl.program_id(0), pl.num_programs(0)
    deep = gate_up[0].shape[0]
    hidden_cols = w_down.shape[1]

    def copies(sources, target, sems):
        return [
            pltpu.make_async_copy(
                sources[j], target.at[pl.ds(pl.multiple_of((me[0] ^ j) * deep, deep), deep), :], sems.at[j]
            )
            for j in range(blocks)
        ]

    first = copies(gate_up, w_gate_up, gate_sems)
    second = copies(down, w_down, down_sems)

    @pl.when(i == 0)
    def fetch():
        for copy in first + second:
            copy.start()

    @pl.when(i < steps // 2)
    def from_own():
        norm_all[...] = own_n[...]
        grad_all[...] = own_c[...]

    @pl.when(i >= steps // 2)
    def from_sibling():
        norm_all[...] = sib_n[...]
        grad_all[...] = sib_c[...]

    @pl.when(i == 0)
    def arrive():
        for copy in first + second:
            copy.wait()

    x, dy = norm_all[...], grad_all[...]
    width = min(512, hidden_cols)
    for at in range(0, hidden_cols, width):
        cols = slice(at, at + width)
        gate = dot32(x, w_gate_up[:, cols])
        up = dot32(x, w_gate_up[:, hidden_cols + at : hidden_cols + at + width])
        d_hidden = dot32(dy, w_down[:, cols])
        sigmoid = 1.0 / (1.0 + jnp.exp(-gate))
        silu = gate * sigmoid
        hidden_all[:, cols] = (silu * up).astype(jnp.bfloat16)
        d_gate = d_hidden * up * sigmoid * (1.0 + gate * (1.0 - sigmoid))
        d_gate_up_all[:, cols] = d_gate.astype(jnp.bfloat16)
        d_up = (d_hidden * silu).astype(jnp.bfloat16)
        d_gate_up_all[:, hidden_cols + at : hidden_cols + at + width] = d_up
    d_norm[...] = times_transpose(d_gate_up_all[...], w_gate_up[...]).astype(jnp.bfloat16)
    out[...] = times_transpose(hidden_all[...], w_down[...]).astype(jnp.bfloat16)


def mlp_piece(k, pieces, me, norm, grad, gate_up, down, earlier):
    rows, width = norm[0].shape
    steps = 2 * rows // SUB
    blocks, hidden_cols = len(down), down[0].shape[1]
    bf16 = jnp.bfloat16
    all_rows = pieces * 2 * rows

    def own(i):
        return (jnp.minimum(i, steps // 2 - 1), 0)

    def sibling(i):
        return (jnp.maximum(i - steps // 2, 0), 0)

    def filled(i):
        return (k * steps + i, 0)

    shapes = [(all_rows, width), (all_rows, width), (all_rows, hidden_cols), (all_rows, 2 * hidden_cols)]
    flops = 2 * rows * width * hidden_cols * 2 * 6
    return pl.pallas_call(
        functools.partial(mlp_kernel, blocks, bool(earlier)),
        grid=(steps,),
        out_shape=[
            *(jax.ShapeDtypeStruct(shape, bf16) for shape in shapes),
            jax.ShapeDtypeStruct((2 * rows, width), bf16),
            jax.ShapeDtypeStruct((2 * rows, width), bf16),
        ],
        in_specs=[
            SMEM,
            pl.BlockSpec((SUB, width), own),
            pl.BlockSpec((SUB, width), sibling),
            pl.BlockSpec((SUB, width), own),
            pl.BlockSpec((SUB, width), sibling),
            *[ANY] * (2 * blocks + len(earlier)),
        ],
        out_specs=[
            *(pl.BlockSpec((SUB, shape[1]), filled) for shape in shapes),
            pl.BlockSpec((SUB, width), lambda i: (i, 0)),
            pl.BlockSpec((SUB, width), lambda i: (i, 0)),
        ],
        scratch_shapes=[
            pltpu.VMEM((width, 2 * hidden_cols), bf16),
            pltpu.VMEM((width, hidden_cols), bf16),
            pltpu.SemaphoreType.DMA((blocks,)),
            pltpu.SemaphoreType.DMA((blocks,)),
        ],
        input_output_aliases={5 + 2 * blocks + n: n for n in range(len(earlier))},
        compiler_params=pltpu.CompilerParams(vmem_limit_bytes=56 * 2**20),
        cost_estimate=pl.CostEstimate(
            flops=flops, bytes_accessed=flops // 512, transcendentals=2 * rows * hidden_cols
        ),
        name=f"mlp_{k}",
    )(me, *norm, *grad, *gate_up, *down, *earlier)


def flip(x, axis):
    return lax.ppermute(x, axis, FLIP)


def swap(x):
    return lax.ppermute(x, ("core", "zh"), [(0, 0), (1, 2), (2, 1), (3, 3)])


def from_near(x, k):
    n = lax.axis_size("zl")
    return lax.ppermute(x, "zl", [((j + k) % n, j) for j in range(n)])


def to_near(x, k):
    n = lax.axis_size("zl")
    return lax.ppermute(x, "zl", [(j, (j + k) % n) for j in range(n)])


def across(x, j):
    n = lax.axis_size("yx")
    return lax.ppermute(x, "yx", [(a, a ^ j) for a in range(n)])


def cross_z(w):
    return cross_core(w, flip(w, "zh"))


def cross_core(w, far):
    core, zh = lax.axis_index("core"), lax.axis_index("zh")
    mine = jnp.where(core == zh, w, far)
    taken = flip(jnp.where(core == zh, far, w), "core")
    return jnp.concatenate(
        [jnp.where(core == 0, mine, taken), jnp.where(core == 0, taken, mine)], axis=0
    )


def all_yx(x):
    return [x] + [across(x, j) for j in range(1, lax.axis_size("yx"))]


def in_order(blocks, axis=0):
    size = blocks[0].shape[axis]
    shape = list(blocks[0].shape)
    shape[axis] = size * len(blocks)
    whole = jnp.zeros(shape, blocks[0].dtype)
    me = lax.axis_index("yx")
    for j, block in enumerate(blocks):
        whole = lax.dynamic_update_slice_in_dim(whole, block, (me ^ j) * size, axis)
    return whole


def sum_yx(grad):
    count = lax.axis_size("yx")
    size = grad.shape[0] // count
    me = lax.axis_index("yx")

    def block(j):
        return lax.dynamic_slice_in_dim(grad, (me ^ j) * size, size, 0)

    taken = [across(block(j), j) for j in range(1, count)]
    total = block(0).astype(jnp.float32)
    for part in taken:
        total = total + part.astype(jnp.float32)
    return total.astype(jnp.bfloat16)


def home(part):
    core, zh = lax.axis_index("core"), lax.axis_index("zh")
    half = part.shape[0] // 2
    upper, lower = part[:half], part[half:]
    mine = jnp.where(core == 0, upper, lower)
    taken = flip(jnp.where(core == 0, lower, upper), "core")
    keep = jnp.where(core == zh, mine, taken)
    give = jnp.where(core == zh, taken, mine)
    return keep.astype(jnp.float32) + flip(give, "zh").astype(jnp.float32)


def sum_everywhere(x):
    x = x + flip(x, "core")
    x = x + sum(to_near(x, k) for k in range(1, lax.axis_size("zl")))
    x = x + flip(x, "zh")
    j = 1
    while j < lax.axis_size("yx"):
        x = x + across(x, j)
        j *= 2
    return x


def body(
    tokens,
    cotangent,
    seq_lengths,
    attn_gain,
    q_weight,
    key_projection,
    value_projection,
    out_weight,
    mlp_gain,
    gate_weight,
    up_weight,
    down_weight,
):
    bf16, f32 = jnp.bfloat16, jnp.float32
    core, zl, yx = lax.axis_index("core"), lax.axis_index("zl"), lax.axis_index("yx")
    near = lax.axis_size("zl")
    others = range(1, near)
    rows = tokens.shape[0]
    group_rows = 2 * near * rows
    query_cols, key_cols = q_weight.shape[1], key_projection.shape[1]
    q_heads, kv_heads = query_cols // HD, key_cols // HD
    hidden_cols = gate_weight.shape[1]

    qkv_shard = jnp.concatenate([q_weight, key_projection, value_projection], axis=1)
    qkv_far = flip(qkv_shard, "zh")
    part_rows = rows // 2
    upper = swap(tokens[:part_rows])
    lower = swap(after(tokens[part_rows:], upper))
    lengths = swap(seq_lengths)
    gains = jnp.stack([attn_gain, mlp_gain])
    gain_sib = flip(gains, "core")
    gain_pair = jnp.concatenate(
        [jnp.where(core == 0, gains, gain_sib), jnp.where(core == 0, gain_sib, gains)], axis=1
    )
    gain_all = in_order(all_yx(gain_pair), axis=1).astype(f32)
    gain_one, gain_two = gain_all[0], gain_all[1]
    w_project = in_order(all_yx(cross_core(qkv_shard, qkv_far)))
    out_far = flip(after(out_weight, lower), "zh")
    gate_up_shard = after(jnp.concatenate([gate_weight, up_weight], axis=1), lower)
    gate_up_far = flip(gate_up_shard, "zh")
    down_far = flip(after(down_weight, gate_up_far), "zh")
    own_cotangent = swap(after(cotangent, down_far))

    subs = jnp.arange(group_rows // SUB, dtype=jnp.int32)
    per_device = rows // SUB
    source, within = subs // per_device, subs % per_device
    there_core, there_zl = (source % 2) ^ core, (source // 2 + zl) % near
    to_order = (there_core * near + there_zl) * per_device + within
    from_order = (((source % near - zl) % near) * 2 + ((source // near) ^ core)) * per_device + within
    place = jnp.concatenate([to_order, from_order])
    row_at, doc_start = document_layout(lengths, group_rows)
    tile_start = doc_start.reshape(-1, TILE)
    tile = jnp.arange(group_rows // TILE, dtype=jnp.int32)
    low = tile_start[:, 0] // TILE
    full = jnp.minimum((tile_start[:, -1] + TILE - 1) // TILE, tile)
    cosine, sine = rotary_tables(row_at - doc_start)
    start_row = jnp.tile(tile_start[:, None, :], (1, 1, q_heads // kv_heads))
    layout = (place, low, full, cosine, sine, doc_start[:, None], start_row)

    parts = [upper.astype(f32), lower.astype(f32)]
    scaled = [norm_rows(part, gain_one) for part in parts]
    residual = jnp.concatenate(parts, axis=0)
    scale_one = jnp.concatenate([scale for scale, _ in scaled], axis=0)
    own_parts = [norm for _, norm in scaled]
    far_parts = [[from_near(part, k) for part in own_parts] for k in others]
    norm_one = [
        jnp.concatenate(some + [flip(part, "core") for part in some], axis=0)
        for some in [own_parts, *far_parts]
    ]
    qkv = [dot32(norm, w_project).astype(bf16) for norm in norm_one]
    context, sums = attend(qkv, layout, q_heads, kv_heads)

    out_pair = cross_core(out_weight, out_far)
    out_quarters = [out_pair] + [from_near(after(out_pair, qkv[-1]), k) for k in others]
    w_out_near = in_order(all_yx(jnp.concatenate(out_quarters, axis=1)))
    w_out_sib = flip(w_out_near, "core")
    quarters = [context[0]] + [None] * (near - 1)
    for k in others:
        quarters[near - k] = to_near(context[k], k)
    context_near = jnp.concatenate([q[:rows] for q in quarters], axis=1)
    context_sib = jnp.concatenate([flip(q[rows:], "core") for q in quarters], axis=1)
    mid = residual + times_transpose(context_near, w_out_near) + times_transpose(context_sib, w_out_sib)
    scale_two, norm_two = norm_rows(mid, gain_two)

    gate_up = all_yx(cross_core(gate_up_shard, gate_up_far))
    down = all_yx(cross_core(down_weight, down_far))
    me = yx.astype(jnp.int32).reshape(1)
    norm_far = [from_near(norm_two, k) for k in others]
    cot_source = after(own_cotangent, *norm_far)
    cot_far = [from_near(cot_source, k) for k in others]
    earlier, d_norms, outs = [], [], []
    for k in range(near):
        norm = norm_two if k == 0 else norm_far[k - 1]
        grad = own_cotangent if k == 0 else cot_far[k - 1]
        pair_n, pair_c = [norm, flip(norm, "core")], [grad, flip(grad, "core")]
        *earlier, d_norm, out = mlp_piece(k, near, me, pair_n, pair_c, gate_up, down, earlier)
        d_norms.append(d_norm[:rows].astype(f32) + flip(d_norm[rows:], "core").astype(f32))
        outs.append(out[:rows].astype(f32) + flip(out[rows:], "core").astype(f32))
    norm_two_all, grad_all, hidden_all, d_gate_up_all = earlier
    d_norm_two = d_norms[0]
    for k in others:
        d_norm_two = d_norm_two + to_near(d_norms[k].astype(bf16), k).astype(f32)
    grad_down = sum_yx(rows_product(grad_all, hidden_all).astype(bf16))
    grad_gate_up = sum_yx(rows_product(norm_two_all, d_gate_up_all).astype(bf16))
    mid_back, gain_two_part = norm_back(mid, scale_two, gain_two, d_norm_two)
    d_mid = own_cotangent.astype(f32) + mid_back
    d_attn = d_mid.astype(bf16)

    d_context_sib = flip(dot32(d_attn, w_out_sib).astype(bf16), "core")
    d_context_near = dot32(d_attn, w_out_near).astype(bf16)
    both = [
        jnp.concatenate(
            [d_context_near[:, k * query_cols : (k + 1) * query_cols],
             d_context_sib[:, k * query_cols : (k + 1) * query_cols]], axis=0)
        for k in range(near)
    ]
    d_context = [both[0]] + [None] * (near - 1)
    for k in others:
        d_context[near - k] = to_near(both[k], k)
    grad_out = rows_product(d_attn, context_near) + flip(
        rows_product(d_attn, context_sib).astype(bf16), "core"
    ).astype(f32)
    grad_out = sum_yx(grad_out.astype(bf16))
    out_total = outs[0]
    for k in others:
        out_total = out_total + to_near(after(outs[k].astype(bf16), *d_context), k).astype(f32)
    output = swap((mid + out_total).astype(bf16))
    d_qkv = attend_back(qkv, d_context, context, sums, layout, q_heads, kv_heads)

    total = None
    for k in reversed(range(near)):
        part = times_transpose(d_qkv[k], w_project).astype(bf16)
        part = part[:rows].astype(f32) + flip(part[rows:], "core").astype(f32)
        if k:
            part = to_near(part.astype(bf16), k).astype(f32)
        total = part if total is None else total + part
    input_back, gain_one_part = norm_back(residual, scale_one, gain_one, total)
    input_grad = swap((d_mid + input_back).astype(bf16)).astype(f32)
    gain_sums = sum_everywhere(jnp.stack([gain_one_part, gain_two_part]))
    width = attn_gain.shape[0]
    gain_grads = lax.dynamic_slice_in_dim(gain_sums, (yx * 2 + core) * width, width, 1)
    grad_project = sum(rows_product(norm, d) for norm, d in zip(norm_one, d_qkv, strict=True))
    grad_project = home(sum_yx(grad_project.astype(bf16)))
    grad_out_quarter = grad_out[:, :query_cols].astype(f32)
    for k in others:
        moved = to_near(grad_out[:, k * query_cols : (k + 1) * query_cols], k)
        grad_out_quarter = grad_out_quarter + moved.astype(f32)
    grad_out = home(grad_out_quarter.astype(bf16))
    grad_down, grad_gate_up = home(grad_down), home(grad_gate_up)
    return (
        output,
        input_grad,
        gain_grads[0],
        grad_project[:, :query_cols],
        grad_project[:, query_cols : query_cols + key_cols],
        grad_project[:, query_cols + key_cols :],
        grad_out,
        gain_grads[1],
        grad_gate_up[:, :hidden_cols],
        grad_gate_up[:, hidden_cols:],
        grad_down,
    )


def solution(mesh):
    dp, tensor = mesh.shape["dp"], mesh.shape["tensor"]
    fine = Mesh(mesh.devices.reshape(dp // 2, 2, 2, tensor // 2), AXES)
    by_rows, by_dp, by_both = P(AXES, None), P(("yx", "core")), P(("yx", "core"), ("zh", "zl"))
    return jax.shard_map(
        body,
        mesh=fine,
        in_specs=(
            by_rows, by_rows, P(("yx", "core"), None), by_dp, by_both, by_both, by_both, by_both,
            by_dp, by_both, by_both, by_both,
        ),
        out_specs=(
            by_rows, by_rows, by_dp, by_both, by_both, by_both, by_both, by_dp, by_both, by_both, by_both,
        ),
        check_vma=False,
    )
```

```python
import functools
import math

import jax
import jax.numpy as jnp
import numpy as np
from jax import lax
from jax.experimental import pallas as pl
from jax.experimental.pallas import tpu as pltpu
from jax.sharding import Mesh
from jax.sharding import PartitionSpec as P

HD = 96
HALF = HD // 2
PAD = 128
SUB = 256
TILE = 512

EPSILON = 1e-05
ROTARY_BASE = 100000.0
MASKED = -1e30
LOG2E = math.log2(math.e)

AXES = ("yx", "core", "zh", "zl")
FLIP = [(0, 1), (1, 0)]


def norm_rows(values, gain):
    row_scale = lax.rsqrt(jnp.mean(values * values, axis=-1, keepdims=True) + EPSILON)
    return (row_scale, (values * row_scale * gain).astype(jnp.bfloat16))


def norm_back(values, row_scale, gain, upstream):
    weighted = upstream * gain
    inner_sum = jnp.mean(weighted * values, axis=-1, keepdims=True)
    grad_in = row_scale * weighted - values * (row_scale * row_scale * row_scale) * inner_sum
    gain_part = jnp.sum(upstream * (values * row_scale), axis=0)
    return (grad_in, gain_part)


def document_layout(lengths, group_rows):
    flat_lengths = lengths.reshape(-1)
    doc_ends = jnp.cumsum(flat_lengths)
    rows = jnp.arange(group_rows, dtype=jnp.int32)
    passed = (rows[:, None] >= doc_ends[None, :]).astype(jnp.int32)
    return (rows, jnp.sum(passed * flat_lengths[None, :], axis=1))


def rotary_tables(positions):
    exponents = jnp.arange(HALF, dtype=jnp.float32) * (2.0 / HD)
    inverse = ROTARY_BASE ** (-exponents)
    angles = positions.astype(jnp.float32)[:, None] * inverse[None, :]
    cosine, sine = jnp.cos(angles), jnp.sin(angles)
    gap = jnp.zeros((positions.shape[0], PAD // 2 - HALF), jnp.float32)
    return (
        jnp.concatenate([cosine, gap, cosine, gap], axis=1),
        jnp.concatenate([-sine, gap, sine, gap], axis=1),
    )


def rows_product(left, right):
    return lax.dot_general(
        left, right, (((0,), (0,)), ((), ())), preferred_element_type=jnp.float32
    )


def times_transpose(left, right):
    return lax.dot_general(
        left, right, (((1,), (1,)), ((), ())), preferred_element_type=jnp.float32
    )


def dot32(left, right):
    return jnp.dot(left, right, preferred_element_type=jnp.float32)


def after(x, *earlier):
    return lax.optimization_barrier((x, *earlier))[0]


def spread(columns, heads):
    matrix = np.zeros((columns, len(heads) * PAD), np.float32)
    for at, first in enumerate(heads):
        for half in range(2):
            for i in range(HALF):
                matrix[first + half * HALF + i, at * PAD + half * (PAD // 2) + i] = 1.0
    return matrix


def turn(x, cosine, sine):
    return x * cosine + pltpu.roll(x, PAD // 2, 1) * sine


def rows_at(t, size):
    return pl.ds(pl.multiple_of(t * size, size), size)


def forward_kernel(pieces, ratio, more, *refs):
    place, low, full, cosine, sine, start, spread_in, gather_out = refs[:8]
    qkv, refs = refs[8 : 8 + pieces], refs[8 + pieces :]
    earlier = ()
    if more:
        earlier, refs = refs[:pieces], refs[pieces:]
    context, refs = refs[:pieces], refs[pieces:]
    log_sum, q_s, k_s, v_s, s_s, top_s, acc = refs
    tiles = q_s.shape[0]
    piece_subs = qkv[0].shape[0] // SUB
    scale = LOG2E * HD ** (-0.5)
    ones_lane = lax.broadcasted_iota(jnp.int32, (SUB, PAD), 1) == PAD - 1

    for k in range(pieces):

        def prepare(r, carry, k=k):
            t = place[k * piece_subs + r]
            wide = dot32(qkv[k][rows_at(r, SUB), :], spread_in[...])
            at = rows_at(t, SUB)
            cos_t, sin_t = cosine[at, :], sine[at, :]
            tile, half = t // (TILE // SUB), t % (TILE // SUB)
            for h in range(ratio):
                query = turn(wide[:, h * PAD : (h + 1) * PAD], cos_t, sin_t) * scale
                first = pl.multiple_of(h * TILE + half * SUB, SUB)
                q_s[tile, pl.ds(first, SUB), :] = query.astype(jnp.bfloat16)
            key = turn(wide[:, ratio * PAD : (ratio + 1) * PAD], cos_t, sin_t)
            k_s[at, :] = key.astype(jnp.bfloat16)
            value = jnp.where(ones_lane, 1.0, wide[:, (ratio + 1) * PAD :])
            v_s[at, :] = value.astype(jnp.bfloat16)
            return carry

        lax.fori_loop(0, piece_subs, prepare, 0)

    def query_tile(i, carry):
        queries = q_s[i]
        starts = jnp.concatenate([start[rows_at(i, TILE), :]] * ratio, axis=0)
        top_s[...] = jnp.full_like(top_s, MASKED)

        def scores(j, masked, diagonal):
            s = times_transpose(queries, k_s[rows_at(j, TILE), :])
            if masked:
                key_at = lax.broadcasted_iota(jnp.int32, s.shape, 1)
                allowed = key_at + j * TILE >= starts
                if diagonal:
                    query_at = lax.rem(lax.broadcasted_iota(jnp.int32, s.shape, 0), TILE)
                    allowed = allowed & (key_at <= query_at)
                s = jnp.where(allowed, s, MASKED)
            s_s[j] = s
            peak = s[:, :PAD]
            for c in range(1, TILE // PAD):
                peak = jnp.maximum(peak, s[:, c * PAD : (c + 1) * PAD])
            top_s[...] = jnp.maximum(top_s[...], peak)

        def loop(first, last, masked):
            def run(j, c):
                scores(j, masked, False)
                return c

            lax.fori_loop(first, last, run, 0)

        loop(low[i], full[i], True)
        loop(full[i], i, False)
        scores(i, True, True)
        top = jnp.max(top_s[...], axis=1, keepdims=True)
        acc[...] = jnp.zeros_like(acc)

        def weigh(j, c):
            p = jnp.exp2(s_s[j] - top).astype(jnp.bfloat16)
            acc[...] += dot32(p, v_s[rows_at(j, TILE), :])
            return c

        lax.fori_loop(low[i], i + 1, weigh, 0)
        total = acc[:, PAD - 1 :]
        out = acc[...] * (1.0 / total)
        sums = jnp.broadcast_to(top + jnp.log(total) * LOG2E, (ratio * TILE, PAD))
        log_sum[i] = sums.T[:1, :]
        wide = jnp.concatenate(
            [out[h * TILE : (h + 1) * TILE, :] for h in range(ratio)], axis=1
        ).astype(jnp.bfloat16)
        packed = dot32(wide, gather_out[...])
        subs = tiles * (TILE // SUB)
        for half in range(TILE // SUB):
            r = place[subs + i * (TILE // SUB) + half]
            part = packed[half * SUB : (half + 1) * SUB, :].astype(jnp.bfloat16)
            for k in range(pieces):

                @pl.when(r // piece_subs == k)
                def store(k=k, part=part, r=r):
                    at = rows_at(r % piece_subs, SUB)
                    context[k][at, :] = part + earlier[k][at, :] if more else part

        return carry

    lax.fori_loop(0, tiles, query_tile, 0)


def backward_kernel(pieces, ratio, *refs):
    place, low, full, cosine, sine, start, refs = *refs[:6], refs[6:]
    heads = refs[0].shape[0]
    spread_in, spread_out, gather_in, refs = *refs[:3], refs[3:]
    log_sum, refs = refs[:heads], refs[heads:]
    qkv, d_context, context, d_qkv, refs = (
        *(refs[n * pieces : (n + 1) * pieces] for n in range(4)), refs[4 * pieces :],
    )
    q_s, k_s, kt_s, v_s, do_s, delta_s, log_s, dq_acc, dk_acc, dv_acc, dq_s = refs
    tiles = q_s.shape[0]
    piece_subs = qkv[0].shape[0] // SUB
    scale = HD ** (-0.5)
    per_tile = TILE // SUB

    for k in range(pieces):

        def prepare(r, carry, k=k):
            t = place[k * piece_subs + r]
            rel = rows_at(r, SUB)
            at = rows_at(t, SUB)
            cos_t, sin_t = cosine[at, :], sine[at, :]
            for g in range(heads):
                wide = dot32(qkv[k][rel, :], spread_in[g])
                d_out = dot32(d_context[k][rel, :], spread_out[g])
                out = dot32(context[k][rel, :], spread_out[g])
                for h in range(ratio):
                    cols = slice(h * PAD, (h + 1) * PAD)
                    rows = slice(h * SUB, (h + 1) * SUB)
                    query = turn(wide[:, cols], cos_t, sin_t) * (scale * LOG2E)
                    q_s[t, g, rows, :] = query.astype(jnp.bfloat16)
                    do_s[t, g, rows, :] = d_out[:, cols].astype(jnp.bfloat16)
                    delta = jnp.sum((d_out[:, cols] * out[:, cols]).T, axis=0, keepdims=True)
                    delta_s[t * heads + g, :, rows] = delta
                    first = pl.multiple_of(h * TILE + t % per_tile * SUB, SUB)
                    log_s[t * heads + g, :, rows] = log_sum[g][t // per_tile, :, pl.ds(first, SUB)]
                key = turn(wide[:, ratio * PAD : (ratio + 1) * PAD], cos_t, sin_t)
                k_s[g, t] = key.astype(jnp.bfloat16)
                kt_s[g, t] = key.T.astype(jnp.bfloat16)
                v_s[g, t] = wide[:, (ratio + 1) * PAD :].astype(jnp.bfloat16)
                dk_acc[g, t] = jnp.zeros((SUB, PAD), jnp.float32)
                dv_acc[g, t] = jnp.zeros((SUB, PAD), jnp.float32)
            return carry

        lax.fori_loop(0, piece_subs, prepare, 0)

    def query_tile(i, carry):
        dq_acc[...] = jnp.zeros_like(dq_acc)

        def step(j, masked, diagonal):
            for g in range(heads):
                queries, d_out = q_s[i, g], do_s[i, g]
                s = times_transpose(k_s[g, j], queries)
                if masked:
                    key_at = lax.broadcasted_iota(jnp.int32, s.shape, 0)
                    allowed = key_at + j * SUB >= start[i]
                    if diagonal:
                        query_at = lax.rem(lax.broadcasted_iota(jnp.int32, s.shape, 1), SUB)
                        allowed = allowed & (key_at <= query_at)
                    s = jnp.where(allowed, s, MASKED)
                p = jnp.exp2(s - log_s[i * heads + g])
                d_p = times_transpose(v_s[g, j], d_out)
                d_s = (p * (d_p - delta_s[i * heads + g])).astype(jnp.bfloat16)
                dv_acc[g, j] += dot32(p.astype(jnp.bfloat16), d_out)
                dk_acc[g, j] += dot32(d_s, queries)
                dq_acc[g] += dot32(kt_s[g, j], d_s)

        def loop(first, last, masked):
            def run(j, c):
                step(j, masked, False)
                return c

            lax.fori_loop(first, last, run, 0)

        loop(low[i], full[i], True)
        loop(full[i], i, False)
        step(i, True, True)
        at = rows_at(i, SUB)
        cos_t, sin_t = cosine[at, :], sine[at, :]
        for g in range(heads):
            grad = dq_acc[g].T * scale
            for h in range(ratio):
                piece = turn(grad[h * SUB : (h + 1) * SUB, :], cos_t, -sin_t)
                dq_s[g, i, :, h * PAD : (h + 1) * PAD] = piece.astype(jnp.bfloat16)
        return carry

    lax.fori_loop(0, tiles, query_tile, 0)

    for k in range(pieces):

        def finish(r, carry, k=k):
            t = place[k * piece_subs + r]
            at = rows_at(t, SUB)
            packed = None
            for g in range(heads):
                key = turn(dk_acc[g, t] * (1.0 / LOG2E), cosine[at, :], -sine[at, :])
                wide = jnp.concatenate(
                    [dq_s[g, t], key.astype(jnp.bfloat16), dv_acc[g, t].astype(jnp.bfloat16)], axis=1
                )
                part = dot32(wide, gather_in[g])
                packed = part if packed is None else packed + part
            d_qkv[k][rows_at(r, SUB), :] = packed.astype(jnp.bfloat16)
            return carry

        lax.fori_loop(0, piece_subs, finish, 0)


SMEM = pl.BlockSpec(memory_space=pltpu.SMEM)
VMEM = pl.BlockSpec(memory_space=pltpu.VMEM)
ANY = pl.BlockSpec(memory_space=pl.ANY)


def attention_cost(rows, heads, products):
    pairs = heads * rows * rows * 5 // 8
    return pl.CostEstimate(
        flops=products * 4 * pairs * PAD, bytes_accessed=rows * 8192, transcendentals=pairs
    )


def head_matrices(head, q_heads, kv_heads):
    ratio = q_heads // kv_heads
    queries = [(head * ratio + r) * HD for r in range(ratio)]
    key, value = (q_heads + head) * HD, (q_heads + kv_heads + head) * HD
    inner = spread((q_heads + 2 * kv_heads) * HD, [*queries, key, value])
    outer = spread(q_heads * HD, queries)
    return jnp.asarray(inner, jnp.bfloat16), jnp.asarray(outer, jnp.bfloat16)


def attend(qkv, layout, q_heads, kv_heads, between):
    place, low, full, cosine, sine, start_column = layout
    pieces, ratio = len(qkv), q_heads // kv_heads
    rows = pieces * qkv[0].shape[0]
    tiles, lanes = rows // TILE, ratio * TILE
    bf16, f32 = jnp.bfloat16, jnp.float32
    context, sums = [], []
    for head in range(kv_heads):
        inner, outer = head_matrices(head, q_heads, kv_heads)
        *context, log_sum = pl.pallas_call(
            functools.partial(forward_kernel, pieces, ratio, head > 0),
            out_shape=[
                *(jax.ShapeDtypeStruct((x.shape[0], q_heads * HD), bf16) for x in qkv),
                jax.ShapeDtypeStruct((tiles, 1, lanes), f32),
            ],
            in_specs=[SMEM] * 3 + [VMEM] * (5 + pieces + len(context)),
            out_specs=[VMEM] * (pieces + 1),
            scratch_shapes=[
                pltpu.VMEM((tiles, lanes, PAD), bf16),
                pltpu.VMEM((rows, PAD), bf16),
                pltpu.VMEM((rows, PAD), bf16),
                pltpu.VMEM((tiles, lanes, TILE), f32),
                pltpu.VMEM((lanes, PAD), f32),
                pltpu.VMEM((lanes, PAD), f32),
            ],
            compiler_params=pltpu.CompilerParams(vmem_limit_bytes=48 * 2**20),
            cost_estimate=attention_cost(rows, ratio, 2),
            name=f"attention_forward_{head}",
        )(place, low, full, cosine, sine, start_column, inner, outer.T, *qkv, *context)
        sums.append(log_sum)
        if head == 0:
            context = list(lax.optimization_barrier((*context, *between(context)))[:pieces])
    return context, sums


def attend_back(qkv, d_context, context, sums, layout, q_heads, kv_heads):
    place, low, full, cosine, sine, start_row = layout
    pieces, ratio = len(qkv), q_heads // kv_heads
    rows = pieces * qkv[0].shape[0]
    tiles, lanes = rows // SUB, ratio * SUB
    bf16, f32 = jnp.bfloat16, jnp.float32
    pairs = [head_matrices(head, q_heads, kv_heads) for head in range(kv_heads)]
    inner = jnp.stack([inner for inner, _ in pairs])
    outer = jnp.stack([outer for _, outer in pairs])
    return pl.pallas_call(
        functools.partial(backward_kernel, pieces, ratio),
        out_shape=[jax.ShapeDtypeStruct(x.shape, bf16) for x in qkv],
        in_specs=[SMEM] * 3 + [VMEM] * (6 + kv_heads + 3 * pieces),
        out_specs=[VMEM] * pieces,
        scratch_shapes=[
            pltpu.VMEM((tiles, kv_heads, lanes, PAD), bf16),
            pltpu.VMEM((kv_heads, tiles, SUB, PAD), bf16),
            pltpu.VMEM((kv_heads, tiles, PAD, SUB), bf16),
            pltpu.VMEM((kv_heads, tiles, SUB, PAD), bf16),
            pltpu.VMEM((tiles, kv_heads, lanes, PAD), bf16),
            pltpu.VMEM((tiles * kv_heads, 1, lanes), f32),
            pltpu.VMEM((tiles * kv_heads, 1, lanes), f32),
            pltpu.VMEM((kv_heads, PAD, lanes), f32),
            pltpu.VMEM((kv_heads, tiles, SUB, PAD), f32),
            pltpu.VMEM((kv_heads, tiles, SUB, PAD), f32),
            pltpu.VMEM((kv_heads, tiles, SUB, ratio * PAD), bf16),
        ],
        compiler_params=pltpu.CompilerParams(vmem_limit_bytes=56 * 2**20),
        cost_estimate=attention_cost(rows, q_heads, 5),
        name="attention_backward",
    )(
        place, low, full, cosine, sine, start_row, inner, outer, jnp.swapaxes(inner, 1, 2),
        *sums, *qkv, *d_context, *context,
    )


def fetch(me, sources, target, sems):
    deep = sources[0].shape[0]
    return [
        pltpu.make_async_copy(
            source, target.at[pl.ds(pl.multiple_of((me[0] ^ j) * deep, deep), deep), :], sems.at[j]
        )
        for j, source in enumerate(sources)
    ]


def own_or_sibling(own, sibling, target):
    i, steps = pl.program_id(0), pl.num_programs(0)

    @pl.when(i < steps // 2)
    def from_own():
        target[...] = own[...]

    @pl.when(i >= steps // 2)
    def from_sibling():
        target[...] = sibling[...]


def gate_kernel(blocks, more, me, own, sibling, *refs):
    gate_up, refs = refs[:blocks], refs[blocks:]
    norm_all, gate_up_all, hidden_all, weight, sems = refs[3 if more else 0 :]
    hidden_cols = hidden_all.shape[1]
    copies = fetch(me, gate_up, weight, sems)

    @pl.when(pl.program_id(0) == 0)
    def first():
        for copy in copies:
            copy.start()
        for copy in copies:
            copy.wait()

    own_or_sibling(own, sibling, norm_all)
    x = norm_all[...]
    width = min(512, hidden_cols)
    for at in range(0, hidden_cols, width):
        gate_at = slice(at, at + width)
        up_at = slice(hidden_cols + at, hidden_cols + at + width)
        gate = dot32(x, weight[:, gate_at])
        up = dot32(x, weight[:, up_at])
        gate_up_all[:, gate_at] = gate
        gate_up_all[:, up_at] = up
        hidden_all[:, gate_at] = (gate * (1.0 / (1.0 + jnp.exp(-gate))) * up).astype(jnp.bfloat16)


def gate_back_kernel(blocks, more, me, own, sibling, down, gate_up_all, *refs):
    gate_up, refs = refs[:blocks], refs[blocks:]
    grad_all, d_gate_up_all, d_norm, weight, sems = refs[2 if more else 0 :]
    hidden_cols = down.shape[1]
    copies = fetch(me, gate_up, weight, sems)
    start = pl.program_id(0) == 0

    @pl.when(start)
    def first():
        for copy in copies:
            copy.start()

    own_or_sibling(own, sibling, grad_all)
    dy = grad_all[...]
    width = min(512, hidden_cols)
    for at in range(0, hidden_cols, width):
        gate_at = slice(at, at + width)
        up_at = slice(hidden_cols + at, hidden_cols + at + width)
        d_hidden = dot32(dy, down[:, gate_at])
        gate, up = gate_up_all[:, gate_at], gate_up_all[:, up_at]
        sigmoid = 1.0 / (1.0 + jnp.exp(-gate))
        d_gate = d_hidden * up * sigmoid * (1.0 + gate * (1.0 - sigmoid))
        d_gate_up_all[:, gate_at] = d_gate.astype(jnp.bfloat16)
        d_gate_up_all[:, up_at] = (d_hidden * (gate * sigmoid)).astype(jnp.bfloat16)

    @pl.when(start)
    def arrive():
        for copy in copies:
            copy.wait()

    d_norm[...] = times_transpose(d_gate_up_all[...], weight[...]).astype(jnp.bfloat16)


def piece_call(kernel, name, k, pieces, me, pair, whole, tiled, gate_up, earlier, outs, products):
    rows, width = pair[0].shape
    steps = 2 * rows // SUB
    blocks = len(gate_up)

    def own(i):
        return (jnp.minimum(i, steps // 2 - 1), 0)

    def sibling(i):
        return (jnp.maximum(i - steps // 2, 0), 0)

    def filled(i):
        return (k * steps + i, 0)

    flops = products * 2 * rows * 2 * width * gate_up[0].shape[1] // 2
    first_earlier = 3 + len(whole) + len(tiled) + blocks
    return pl.pallas_call(
        functools.partial(kernel, blocks, bool(earlier)),
        grid=(steps,),
        out_shape=[
            jax.ShapeDtypeStruct(((pieces if all_rows else 1) * 2 * rows, cols), kind)
            for cols, kind, all_rows in outs
        ],
        in_specs=[
            SMEM,
            pl.BlockSpec((SUB, width), own),
            pl.BlockSpec((SUB, width), sibling),
            *(pl.BlockSpec(x.shape, lambda i: (0, 0)) for x in whole),
            *(pl.BlockSpec((SUB, x.shape[1]), filled) for x in tiled),
            *[ANY] * (blocks + len(earlier)),
        ],
        out_specs=[
            pl.BlockSpec((SUB, cols), filled if all_rows else lambda i: (i, 0))
            for cols, kind, all_rows in outs
        ],
        scratch_shapes=[
            pltpu.VMEM((blocks * gate_up[0].shape[0], gate_up[0].shape[1]), jnp.bfloat16),
            pltpu.SemaphoreType.DMA((blocks,)),
        ],
        input_output_aliases={first_earlier + n: n for n in range(len(earlier))},
        compiler_params=pltpu.CompilerParams(vmem_limit_bytes=56 * 2**20),
        cost_estimate=pl.CostEstimate(
            flops=flops, bytes_accessed=flops // 512, transcendentals=2 * rows * gate_up[0].shape[1] // 2
        ),
        name=f"{name}_{k}",
    )(me, *pair, *whole, *tiled, *gate_up, *earlier)


def flip(x, axis):
    return lax.ppermute(x, axis, FLIP)


def swap(x):
    return lax.ppermute(x, ("core", "zh"), [(0, 0), (1, 2), (2, 1), (3, 3)])


def from_near(x, k):
    n = lax.axis_size("zl")
    return lax.ppermute(x, "zl", [((j + k) % n, j) for j in range(n)])


def to_near(x, k):
    n = lax.axis_size("zl")
    return lax.ppermute(x, "zl", [(j, (j + k) % n) for j in range(n)])


def across(x, j):
    n = lax.axis_size("yx")
    return lax.ppermute(x, "yx", [(a, a ^ j) for a in range(n)])


def cross_z(w):
    return cross_core(w, flip(w, "zh"))


def cross_core(w, far):
    core, zh = lax.axis_index("core"), lax.axis_index("zh")
    mine = jnp.where(core == zh, w, far)
    taken = flip(jnp.where(core == zh, far, w), "core")
    return jnp.concatenate(
        [jnp.where(core == 0, mine, taken), jnp.where(core == 0, taken, mine)], axis=0
    )


def all_yx(x):
    count = lax.axis_size("yx")
    if count != 4:
        return [x] + [across(x, j) for j in range(1, count)]
    half = x.shape[0] // 2
    first, second = across(x, 1), across(x, 2)
    upper, lower = across(second[:half], 1), across(first[half:], 2)
    return [x, first, second, jnp.concatenate([upper, lower], axis=0)]


def in_order(blocks, axis=0):
    size = blocks[0].shape[axis]
    shape = list(blocks[0].shape)
    shape[axis] = size * len(blocks)
    whole = jnp.zeros(shape, blocks[0].dtype)
    me = lax.axis_index("yx")
    for j, block in enumerate(blocks):
        whole = lax.dynamic_update_slice_in_dim(whole, block, (me ^ j) * size, axis)
    return whole


def block_of(grad, j):
    size = grad.shape[0] // lax.axis_size("yx")
    return lax.dynamic_slice_in_dim(grad, (lax.axis_index("yx") ^ j) * size, size, 0)


def send_yx(grad):
    count = lax.axis_size("yx")
    if count != 4:
        return [across(block_of(grad, j), j) for j in range(1, count)]
    far = block_of(grad, 3)
    half = far.shape[0] // 2
    return [across(far[:half], 1), across(far[half:], 2)]


def join_yx(grad, taken):
    if lax.axis_size("yx") != 4:
        return taken, block_of(grad, 0)
    half = taken[0].shape[0]
    one, two = block_of(grad, 1), block_of(grad, 2)
    one = jnp.concatenate([one[:half], one[half:] + taken[1]], axis=0)
    two = jnp.concatenate([two[:half] + taken[0], two[half:]], axis=0)
    return [across(one, 1), across(two, 2)], block_of(grad, 0)


def total_yx(taken, own):
    total = own.astype(jnp.float32)
    for part in taken:
        total = total + part.astype(jnp.float32)
    return total.astype(jnp.bfloat16)


def home_core(part):
    core, zh = lax.axis_index("core"), lax.axis_index("zh")
    half = part.shape[0] // 2
    upper, lower = part[:half], part[half:]
    mine = jnp.where(core == 0, upper, lower)
    taken = flip(jnp.where(core == 0, lower, upper), "core")
    return jnp.where(core == zh, mine, taken), jnp.where(core == zh, taken, mine)


def home(keep, give):
    return keep.astype(jnp.float32) + flip(give, "zh").astype(jnp.float32)


def body(
    tokens,
    cotangent,
    seq_lengths,
    attn_gain,
    q_weight,
    key_projection,
    value_projection,
    out_weight,
    mlp_gain,
    gate_weight,
    up_weight,
    down_weight,
):
    bf16, f32 = jnp.bfloat16, jnp.float32
    core, zl, yx = lax.axis_index("core"), lax.axis_index("zl"), lax.axis_index("yx")
    near = lax.axis_size("zl")
    others = range(1, near)
    rows = tokens.shape[0]
    group_rows = 2 * near * rows
    query_cols, key_cols = q_weight.shape[1], key_projection.shape[1]
    qkv_cols = query_cols + 2 * key_cols
    q_heads, kv_heads = query_cols // HD, key_cols // HD
    hidden_cols = gate_weight.shape[1]
    deep = q_weight.shape[0]
    me = yx.astype(jnp.int32).reshape(1)

    qkv_shard = jnp.concatenate([q_weight, key_projection, value_projection], axis=1)
    gain_rows = jnp.concatenate([attn_gain, mlp_gain, jnp.zeros((qkv_cols + query_cols - 2 * deep,), bf16)])
    gain_rows = jnp.concatenate([gain_rows[None], jnp.zeros((15, gain_rows.shape[0]), bf16)], axis=0)
    shard = jnp.concatenate([jnp.concatenate([qkv_shard, out_weight], axis=1), gain_rows], axis=0)
    shard_far = flip(shard, "zh")
    part_rows = rows // 2
    upper = swap(tokens[:part_rows])
    lengths = swap(seq_lengths)
    pair = cross_core(shard, shard_far)
    qkv_blocks = all_yx(pair[:, :qkv_cols])
    lower = swap(after(tokens[part_rows:], upper, pair))

    step = deep + 16
    w_project = in_order([jnp.concatenate([x[:deep], x[step : step + deep]]) for x in qkv_blocks])
    gain_all = in_order(
        [
            jnp.concatenate([x[deep, : 2 * deep].reshape(2, deep), x[step + deep, : 2 * deep].reshape(2, deep)], axis=1)
            for x in qkv_blocks
        ],
        axis=1,
    ).astype(f32)
    gain_one, gain_two = gain_all[0], gain_all[1]

    subs = jnp.arange(group_rows // SUB, dtype=jnp.int32)
    per_device = rows // SUB
    source, within = subs // per_device, subs % per_device
    there_core, there_zl = (source % 2) ^ core, (source // 2 + zl) % near
    to_order = (there_core * near + there_zl) * per_device + within
    from_order = (((source % near - zl) % near) * 2 + ((source // near) ^ core)) * per_device + within
    place = jnp.concatenate([to_order, from_order])
    row_at, doc_start = document_layout(lengths, group_rows)
    cosine, sine = rotary_tables(row_at - doc_start)

    def bounds(size):
        tile_start = doc_start.reshape(-1, size)
        tile = jnp.arange(group_rows // size, dtype=jnp.int32)
        low = tile_start[:, 0] // size
        return low, jnp.minimum((tile_start[:, -1] + size - 1) // size, tile)

    start_row = jnp.tile(doc_start.reshape(-1, 1, SUB), (1, 1, q_heads // kv_heads))
    layout = (place, *bounds(TILE), cosine, sine, doc_start[:, None])
    layout_back = (place, *bounds(SUB), cosine, sine, start_row)

    parts = [upper.astype(f32), lower.astype(f32)]
    scaled = [norm_rows(part, gain_one) for part in parts]
    residual = jnp.concatenate(parts, axis=0)
    scale_one = jnp.concatenate([scale for scale, _ in scaled], axis=0)
    own_parts = [norm for _, norm in scaled]
    far_parts = [[from_near(part, k) for part in own_parts] for k in others]
    own_norm = jnp.concatenate(own_parts, axis=0)
    norm_one = [jnp.concatenate([own_norm, flip(own_norm, "core")], axis=0)]
    qkv = [dot32(norm_one[0], w_project).astype(bf16)]
    gate_up_shard = jnp.concatenate([gate_weight, up_weight], axis=1)
    gate_up_far = flip(after(gate_up_shard, lower, qkv[0]), "zh")
    for parts_k in far_parts:
        far_norm = jnp.concatenate(parts_k, axis=0)
        norm_one.append(jnp.concatenate([far_norm, flip(far_norm, "core")], axis=0))
        qkv.append(dot32(norm_one[-1], w_project).astype(bf16))
    out_pair = pair[:, qkv_cols:]
    out_pair = jnp.concatenate([out_pair[:deep], out_pair[step : step + deep]], axis=0)
    out_quarters = [out_pair] + [from_near(after(out_pair, qkv[-1]), k) for k in others]

    gate_up_pair = []

    def keep_pair(context):
        gate_up_pair.append(cross_core(gate_up_shard, after(gate_up_far, *context)))
        return gate_up_pair

    context, sums = attend(qkv, layout, q_heads, kv_heads, keep_pair)
    gate_up = all_yx(gate_up_pair[0])
    own_cotangent = swap(after(cotangent, gate_up_pair[0]))
    w_out_near = in_order(all_yx(jnp.concatenate(out_quarters, axis=1)))
    w_out_sib = flip(w_out_near, "core")

    quarters = [context[0]] + [None] * (near - 1)
    for k in others:
        quarters[near - k] = to_near(context[k], k)
    own_context = jnp.concatenate([q[:rows] for q in quarters], axis=1)
    sib_context = flip(jnp.concatenate([q[rows:] for q in quarters], axis=1), "core")
    down_far = flip(after(down_weight, own_context, own_cotangent), "zh")
    mid = residual + times_transpose(own_context, w_out_near) + times_transpose(sib_context, w_out_sib)
    scale_two, norm_two = norm_rows(mid, gain_two)

    norm_sib = flip(norm_two, "core")
    norm_far = [from_near(norm_two, k) for k in others]
    down_pair = cross_core(down_weight, after(down_far, norm_sib))
    down_blocks = all_yx(down_pair)
    outs = [(norm_two.shape[1], bf16, True), (2 * hidden_cols, f32, True), (hidden_cols, bf16, True)]
    earlier = piece_call(
        gate_kernel, "gate", 0, near, me, [norm_two, norm_sib], [], [], gate_up, [], outs, 2
    )
    cot_source = after(own_cotangent, *norm_far)
    cot_far = [from_near(cot_source, k) for k in others]
    cot_sib = flip(after(own_cotangent, norm_sib), "core")
    for k in others:
        far_pair = [norm_far[k - 1], flip(norm_far[k - 1], "core")]
        earlier = piece_call(gate_kernel, "gate", k, near, me, far_pair, [], [], gate_up, earlier, outs, 2)
    norm_two_all, gate_up_all, hidden_all = earlier
    w_down = in_order(down_blocks)
    out_all = times_transpose(hidden_all, w_down).astype(bf16)
    out_sib = flip(
        jnp.concatenate([out_all[(2 * k + 1) * rows : (2 * k + 2) * rows] for k in range(near)], axis=0), "core"
    )
    out_parts = [
        out_all[2 * k * rows : (2 * k + 1) * rows].astype(f32) + out_sib[k * rows : (k + 1) * rows].astype(f32)
        for k in range(near)
    ]
    out_total = out_parts[0]
    outs = [(norm_two.shape[1], bf16, True), (2 * hidden_cols, bf16, True), (norm_two.shape[1], bf16, False)]
    earlier, d_norms = [], []
    for k in range(near):
        grad = own_cotangent if k == 0 else cot_far[k - 1]
        grad_sib = cot_sib if k == 0 else flip(grad, "core")
        *earlier, d_norm = piece_call(
            gate_back_kernel, "gate_back", k, near, me, [grad, grad_sib], [w_down], [gate_up_all], gate_up,
            earlier, outs, 3,
        )
        d_norms.append(d_norm[:rows].astype(f32) + flip(d_norm[rows:], "core").astype(f32))
    grad_all, d_gate_up_all = earlier
    for k in others:
        out_total = out_total + to_near(after(out_parts[k].astype(bf16), *cot_far), k).astype(f32)
    d_norm_two = d_norms[0]
    sent = [d_norms[k].astype(bf16) for k in others]
    for k in others:
        d_norm_two = d_norm_two + to_near(sent[k - 1], k).astype(f32)
    grad_down = rows_product(after(grad_all, *sent), hidden_all).astype(bf16)
    down_taken = send_yx(grad_down)
    grad_gate_up = rows_product(after(norm_two_all, grad_down), d_gate_up_all).astype(bf16)
    gate_up_taken = send_yx(grad_gate_up)
    d_norm_two = after(d_norm_two, grad_gate_up)
    mid_back, gain_two_part = norm_back(mid, scale_two, gain_two, d_norm_two)
    d_mid = own_cotangent.astype(f32) + mid_back
    d_attn = d_mid.astype(bf16)

    d_context_sib = flip(dot32(d_attn, w_out_sib).astype(bf16), "core")
    d_context_near = dot32(d_attn, w_out_near).astype(bf16)
    both = [
        jnp.concatenate(
            [d_context_near[:, k * query_cols : (k + 1) * query_cols],
             d_context_sib[:, k * query_cols : (k + 1) * query_cols]], axis=0)
        for k in range(near)
    ]
    d_context = [both[0]] + [None] * (near - 1)
    for k in others:
        d_context[near - k] = to_near(both[k], k)
    down_moved, down_own = join_yx(grad_down, [after(x, *both) for x in down_taken])
    gate_up_moved, gate_up_own = join_yx(grad_gate_up, [after(x, *both) for x in gate_up_taken])
    grad_out_near = rows_product(after(d_attn, *both), own_context)
    grad_out_sib = flip(rows_product(after(d_attn, *both), sib_context).astype(bf16), "core")
    output = swap(after((mid + out_total).astype(bf16), *d_context))
    d_context = list(lax.optimization_barrier((*d_context, grad_out_near, output))[:near])
    d_qkv = attend_back(qkv, d_context, context, sums, layout_back, q_heads, kv_heads)

    far_first = []
    for k in reversed(range(near)):
        part = times_transpose(d_qkv[k], w_project).astype(bf16)
        part = part[:rows].astype(f32) + flip(part[rows:], "core").astype(f32)
        far_first.append(part if k == 0 else part.astype(bf16))
    total = far_first[-1]
    for k in others:
        total = total + to_near(far_first[near - 1 - k], k).astype(f32)
    ready = far_first[0]
    grad_project = sum(rows_product(after(norm, ready), d) for norm, d in zip(norm_one, d_qkv, strict=True))
    grad_project = grad_project.astype(bf16)
    project_taken = send_yx(grad_project)
    down_keep, down_give = home_core(total_yx([after(x, grad_project) for x in down_moved], down_own))
    grad_down = home(down_keep, down_give)
    gate_up_keep, gate_up_give = home_core(total_yx([after(x, down_give) for x in gate_up_moved], gate_up_own))
    grad_gate_up = home(gate_up_keep, gate_up_give)
    grad_out = (grad_out_near + after(grad_out_sib, grad_project).astype(f32)).astype(bf16)
    out_taken = send_yx(grad_out)
    project_moved, project_own = join_yx(grad_project, project_taken)
    out_moved, out_own = join_yx(grad_out, out_taken)
    input_back, gain_one_part = norm_back(residual, scale_one, gain_one, total)
    input_grad_own = (d_mid + input_back).astype(bf16)
    input_grad = swap(input_grad_own).astype(f32)
    grad_project = home(*home_core(total_yx([after(x, input_grad_own) for x in project_moved], project_own)))
    grad_out = total_yx([after(x, input_grad_own) for x in out_moved], out_own)
    grad_out_quarter = grad_out[:, :query_cols].astype(f32)
    for k in others:
        moved = to_near(grad_out[:, k * query_cols : (k + 1) * query_cols], k)
        grad_out_quarter = grad_out_quarter + moved.astype(f32)
    grad_out = home(*home_core(grad_out_quarter.astype(bf16)))
    gain_grads = lax.psum(
        jnp.stack(
            [
                jnp.sum(qkv_shard.astype(f32) * grad_project, axis=1),
                jnp.sum(gate_up_shard.astype(f32) * grad_gate_up, axis=1),
            ]
        ),
        ("zh", "zl"),
    ) / jnp.stack([attn_gain, mlp_gain]).astype(f32)
    return (
        output,
        input_grad,
        gain_grads[0],
        grad_project[:, :query_cols],
        grad_project[:, query_cols : query_cols + key_cols],
        grad_project[:, query_cols + key_cols :],
        grad_out,
        gain_grads[1],
        grad_gate_up[:, :hidden_cols],
        grad_gate_up[:, hidden_cols:],
        grad_down,
    )


def solution(mesh):
    dp, tensor = mesh.shape["dp"], mesh.shape["tensor"]
    fine = Mesh(mesh.devices.reshape(dp // 2, 2, 2, tensor // 2), AXES)
    by_rows, by_dp, by_both = P(AXES, None), P(("yx", "core")), P(("yx", "core"), ("zh", "zl"))
    return jax.shard_map(
        body,
        mesh=fine,
        in_specs=(
            by_rows, by_rows, P(("yx", "core"), None), by_dp, by_both, by_both, by_both, by_both,
            by_dp, by_both, by_both, by_both,
        ),
        out_specs=(
            by_rows, by_rows, by_dp, by_both, by_both, by_both, by_both, by_dp, by_both, by_both, by_both,
        ),
        check_vma=False,
    )
```

```python
import functools
import math

import jax
import jax.numpy as jnp
import numpy as np
from jax import lax
from jax.experimental import pallas as pl
from jax.experimental.pallas import tpu as pltpu
from jax.sharding import Mesh
from jax.sharding import PartitionSpec as P

HD = 96
HALF = HD // 2
PAD = 128
SUB = 256
TILE = 512

EPSILON = 1e-05
ROTARY_BASE = 100000.0
MASKED = -1e30
LOG2E = math.log2(math.e)

AXES = ("yx", "core", "zh", "zl")
FLIP = [(0, 1), (1, 0)]


def norm_rows(values, gain):
    row_scale = lax.rsqrt(jnp.mean(values * values, axis=-1, keepdims=True) + EPSILON)
    return (row_scale, (values * row_scale * gain).astype(jnp.bfloat16))


def norm_back(values, row_scale, gain, upstream):
    weighted = upstream * gain
    inner_sum = jnp.mean(weighted * values, axis=-1, keepdims=True)
    grad_in = row_scale * weighted - values * (row_scale * row_scale * row_scale) * inner_sum
    gain_part = jnp.sum(upstream * (values * row_scale), axis=0)
    return (grad_in, gain_part)


def document_layout(lengths, group_rows):
    flat_lengths = lengths.reshape(-1)
    doc_ends = jnp.cumsum(flat_lengths)
    rows = jnp.arange(group_rows, dtype=jnp.int32)
    passed = (rows[:, None] >= doc_ends[None, :]).astype(jnp.int32)
    return (rows, jnp.sum(passed * flat_lengths[None, :], axis=1))


def rotary_tables(positions):
    exponents = jnp.arange(HALF, dtype=jnp.float32) * (2.0 / HD)
    inverse = ROTARY_BASE ** (-exponents)
    angles = positions.astype(jnp.float32)[:, None] * inverse[None, :]
    cosine, sine = jnp.cos(angles), jnp.sin(angles)
    gap = jnp.zeros((positions.shape[0], PAD // 2 - HALF), jnp.float32)
    return (
        jnp.concatenate([cosine, gap, cosine, gap], axis=1),
        jnp.concatenate([-sine, gap, sine, gap], axis=1),
    )


def rows_product(left, right):
    return lax.dot_general(
        left, right, (((0,), (0,)), ((), ())), preferred_element_type=jnp.float32
    )


def times_transpose(left, right):
    return lax.dot_general(
        left, right, (((1,), (1,)), ((), ())), preferred_element_type=jnp.float32
    )


def dot32(left, right):
    return jnp.dot(left, right, preferred_element_type=jnp.float32)


def stage(*values):
    return lax.optimization_barrier(values)


def spread(columns, heads):
    matrix = np.zeros((columns, len(heads) * PAD), np.float32)
    for at, first in enumerate(heads):
        for half in range(2):
            for i in range(HALF):
                matrix[first + half * HALF + i, at * PAD + half * (PAD // 2) + i] = 1.0
    return matrix


def turn(x, cosine, sine):
    return x * cosine + pltpu.roll(x, PAD // 2, 1) * sine


def rows_at(t, size):
    return pl.ds(pl.multiple_of(t * size, size), size)


def forward_kernel(pieces, ratio, *refs):
    place, low, full, cosine, sine, start, spread_in, gather_out = refs[:8]
    heads = spread_in.shape[0]
    refs = refs[8:]
    qkv, context, refs = refs[:pieces], refs[pieces : 2 * pieces], refs[2 * pieces :]
    log_sum, refs = refs[:heads], refs[heads:]
    q_s, k_s, v_s, s_s, top_s, acc = refs
    tiles = q_s.shape[0]
    piece_subs = qkv[0].shape[0] // SUB
    scale = LOG2E * HD ** (-0.5)
    ones_lane = lax.broadcasted_iota(jnp.int32, (SUB, PAD), 1) == PAD - 1

    for k in range(pieces):

        def prepare(r, carry, k=k):
            t = place[k * piece_subs + r]
            at = rows_at(t, SUB)
            cos_t, sin_t = cosine[at, :], sine[at, :]
            tile, half = t // (TILE // SUB), t % (TILE // SUB)
            for g in range(heads):
                wide = dot32(qkv[k][rows_at(r, SUB), :], spread_in[g])
                for h in range(ratio):
                    query = turn(wide[:, h * PAD : (h + 1) * PAD], cos_t, sin_t) * scale
                    first = pl.multiple_of(h * TILE + half * SUB, SUB)
                    q_s[tile, g, pl.ds(first, SUB), :] = query.astype(jnp.bfloat16)
                key = turn(wide[:, ratio * PAD : (ratio + 1) * PAD], cos_t, sin_t)
                k_s[g, at, :] = key.astype(jnp.bfloat16)
                value = jnp.where(ones_lane, 1.0, wide[:, (ratio + 1) * PAD :])
                v_s[g, at, :] = value.astype(jnp.bfloat16)
            return carry

        lax.fori_loop(0, piece_subs, prepare, 0)

    def query_tile(i, carry):
        starts = jnp.concatenate([start[rows_at(i, TILE), :]] * ratio, axis=0)
        top_s[...] = jnp.full_like(top_s, MASKED)

        def scores(j, masked, diagonal):
            for g in range(heads):
                s = times_transpose(q_s[i, g], k_s[g, rows_at(j, TILE), :])
                if masked:
                    key_at = lax.broadcasted_iota(jnp.int32, s.shape, 1)
                    allowed = key_at + j * TILE >= starts
                    if diagonal:
                        query_at = lax.rem(lax.broadcasted_iota(jnp.int32, s.shape, 0), TILE)
                        allowed = allowed & (key_at <= query_at)
                    s = jnp.where(allowed, s, MASKED)
                s_s[g, j] = s
                peak = s[:, :PAD]
                for c in range(1, TILE // PAD):
                    peak = jnp.maximum(peak, s[:, c * PAD : (c + 1) * PAD])
                top_s[g] = jnp.maximum(top_s[g], peak)

        def loop(first, last, masked):
            def run(j, c):
                scores(j, masked, False)
                return c

            lax.fori_loop(first, last, run, 0)

        loop(low[i], full[i], True)
        loop(full[i], i, False)
        scores(i, True, True)
        tops = [jnp.max(top_s[g], axis=1, keepdims=True) for g in range(heads)]
        acc[...] = jnp.zeros_like(acc)

        def weigh(j, c):
            for g in range(heads):
                p = jnp.exp2(s_s[g, j] - tops[g]).astype(jnp.bfloat16)
                acc[g] += dot32(p, v_s[g, rows_at(j, TILE), :])
            return c

        lax.fori_loop(low[i], i + 1, weigh, 0)
        packed = None
        for g in range(heads):
            total = acc[g][:, PAD - 1 :]
            out = acc[g] * (1.0 / total)
            sums = jnp.broadcast_to(tops[g] + jnp.log(total) * LOG2E, (ratio * TILE, PAD))
            log_sum[g][i] = sums.T[:1, :]
            wide = jnp.concatenate(
                [out[h * TILE : (h + 1) * TILE, :] for h in range(ratio)], axis=1
            ).astype(jnp.bfloat16)
            part = dot32(wide, gather_out[g])
            packed = part if packed is None else packed + part
        subs = tiles * (TILE // SUB)
        for half in range(TILE // SUB):
            r = place[subs + i * (TILE // SUB) + half]
            part = packed[half * SUB : (half + 1) * SUB, :].astype(jnp.bfloat16)
            for k in range(pieces):

                @pl.when(r // piece_subs == k)
                def store(k=k, part=part, r=r):
                    context[k][rows_at(r % piece_subs, SUB), :] = part

        return carry

    lax.fori_loop(0, tiles, query_tile, 0)


def backward_kernel(pieces, ratio, *refs):
    place, low, full, cosine, sine, start, refs = *refs[:6], refs[6:]
    heads = refs[0].shape[0]
    spread_in, spread_out, gather_in, refs = *refs[:3], refs[3:]
    log_sum, refs = refs[:heads], refs[heads:]
    qkv, d_context, context, d_qkv, refs = (
        *(refs[n * pieces : (n + 1) * pieces] for n in range(4)), refs[4 * pieces :],
    )
    q_s, k_s, kt_s, v_s, do_s, delta_s, log_s, dq_acc, dk_acc, dv_acc, dq_s = refs
    tiles = q_s.shape[0]
    piece_subs = qkv[0].shape[0] // SUB
    scale = HD ** (-0.5)
    per_tile = TILE // SUB

    for k in range(pieces):

        def prepare(r, carry, k=k):
            t = place[k * piece_subs + r]
            rel = rows_at(r, SUB)
            at = rows_at(t, SUB)
            cos_t, sin_t = cosine[at, :], sine[at, :]
            for g in range(heads):
                wide = dot32(qkv[k][rel, :], spread_in[g])
                d_out = dot32(d_context[k][rel, :], spread_out[g])
                out = dot32(context[k][rel, :], spread_out[g])
                for h in range(ratio):
                    cols = slice(h * PAD, (h + 1) * PAD)
                    rows = slice(h * SUB, (h + 1) * SUB)
                    query = turn(wide[:, cols], cos_t, sin_t) * (scale * LOG2E)
                    q_s[t, g, rows, :] = query.astype(jnp.bfloat16)
                    do_s[t, g, rows, :] = d_out[:, cols].astype(jnp.bfloat16)
                    delta = jnp.sum((d_out[:, cols] * out[:, cols]).T, axis=0, keepdims=True)
                    delta_s[t * heads + g, :, rows] = delta
                    first = pl.multiple_of(h * TILE + t % per_tile * SUB, SUB)
                    log_s[t * heads + g, :, rows] = log_sum[g][t // per_tile, :, pl.ds(first, SUB)]
                key = turn(wide[:, ratio * PAD : (ratio + 1) * PAD], cos_t, sin_t)
                k_s[g, t] = key.astype(jnp.bfloat16)
                kt_s[g, t] = key.T.astype(jnp.bfloat16)
                v_s[g, t] = wide[:, (ratio + 1) * PAD :].astype(jnp.bfloat16)
                dk_acc[g, t] = jnp.zeros((SUB, PAD), jnp.float32)
                dv_acc[g, t] = jnp.zeros((SUB, PAD), jnp.float32)
            return carry

        lax.fori_loop(0, piece_subs, prepare, 0)

    def query_tile(i, carry):
        dq_acc[...] = jnp.zeros_like(dq_acc)

        def step(j, masked, diagonal):
            for g in range(heads):
                queries, d_out = q_s[i, g], do_s[i, g]
                s = times_transpose(k_s[g, j], queries)
                if masked:
                    key_at = lax.broadcasted_iota(jnp.int32, s.shape, 0)
                    allowed = key_at + j * SUB >= start[i]
                    if diagonal:
                        query_at = lax.rem(lax.broadcasted_iota(jnp.int32, s.shape, 1), SUB)
                        allowed = allowed & (key_at <= query_at)
                    s = jnp.where(allowed, s, MASKED)
                p = jnp.exp2(s - log_s[i * heads + g])
                d_p = times_transpose(v_s[g, j], d_out)
                d_s = (p * (d_p - delta_s[i * heads + g])).astype(jnp.bfloat16)
                dv_acc[g, j] += dot32(p.astype(jnp.bfloat16), d_out)
                dk_acc[g, j] += dot32(d_s, queries)
                dq_acc[g] += dot32(kt_s[g, j], d_s)

        def loop(first, last, masked):
            def run(j, c):
                step(j, masked, False)
                return c

            lax.fori_loop(first, last, run, 0)

        loop(low[i], full[i], True)
        loop(full[i], i, False)
        step(i, True, True)
        at = rows_at(i, SUB)
        cos_t, sin_t = cosine[at, :], sine[at, :]
        for g in range(heads):
            grad = dq_acc[g].T * scale
            for h in range(ratio):
                piece = turn(grad[h * SUB : (h + 1) * SUB, :], cos_t, -sin_t)
                dq_s[g, i, :, h * PAD : (h + 1) * PAD] = piece.astype(jnp.bfloat16)
        return carry

    lax.fori_loop(0, tiles, query_tile, 0)

    for k in range(pieces):

        def finish(r, carry, k=k):
            t = place[k * piece_subs + r]
            at = rows_at(t, SUB)
            packed = None
            for g in range(heads):
                key = turn(dk_acc[g, t] * (1.0 / LOG2E), cosine[at, :], -sine[at, :])
                wide = jnp.concatenate(
                    [dq_s[g, t], key.astype(jnp.bfloat16), dv_acc[g, t].astype(jnp.bfloat16)], axis=1
                )
                part = dot32(wide, gather_in[g])
                packed = part if packed is None else packed + part
            d_qkv[k][rows_at(r, SUB), :] = packed.astype(jnp.bfloat16)
            return carry

        lax.fori_loop(0, piece_subs, finish, 0)


SMEM = pl.BlockSpec(memory_space=pltpu.SMEM)
VMEM = pl.BlockSpec(memory_space=pltpu.VMEM)
ANY = pl.BlockSpec(memory_space=pl.ANY)


def attention_cost(rows, heads, products):
    pairs = heads * rows * rows * 5 // 8
    return pl.CostEstimate(
        flops=products * 4 * pairs * PAD, bytes_accessed=rows * 8192, transcendentals=pairs
    )


def head_matrices(head, q_heads, kv_heads):
    ratio = q_heads // kv_heads
    queries = [(head * ratio + r) * HD for r in range(ratio)]
    key, value = (q_heads + head) * HD, (q_heads + kv_heads + head) * HD
    inner = spread((q_heads + 2 * kv_heads) * HD, [*queries, key, value])
    outer = spread(q_heads * HD, queries)
    return jnp.asarray(inner, jnp.bfloat16), jnp.asarray(outer, jnp.bfloat16)


def stacked_matrices(q_heads, kv_heads):
    pairs = [head_matrices(head, q_heads, kv_heads) for head in range(kv_heads)]
    return jnp.stack([inner for inner, _ in pairs]), jnp.stack([outer for _, outer in pairs])


def attend(qkv, layout, q_heads, kv_heads):
    place, low, full, cosine, sine, start_column = layout
    pieces, ratio = len(qkv), q_heads // kv_heads
    rows = pieces * qkv[0].shape[0]
    tiles, lanes = rows // TILE, ratio * TILE
    bf16, f32 = jnp.bfloat16, jnp.float32
    inner, outer = stacked_matrices(q_heads, kv_heads)
    outs = pl.pallas_call(
        functools.partial(forward_kernel, pieces, ratio),
        out_shape=[
            *(jax.ShapeDtypeStruct((x.shape[0], q_heads * HD), bf16) for x in qkv),
            *[jax.ShapeDtypeStruct((tiles, 1, lanes), f32)] * kv_heads,
        ],
        in_specs=[SMEM] * 3 + [VMEM] * (5 + pieces),
        out_specs=[VMEM] * (pieces + kv_heads),
        scratch_shapes=[
            pltpu.VMEM((tiles, kv_heads, lanes, PAD), bf16),
            pltpu.VMEM((kv_heads, rows, PAD), bf16),
            pltpu.VMEM((kv_heads, rows, PAD), bf16),
            pltpu.VMEM((kv_heads, tiles, lanes, TILE), f32),
            pltpu.VMEM((kv_heads, lanes, PAD), f32),
            pltpu.VMEM((kv_heads, lanes, PAD), f32),
        ],
        compiler_params=pltpu.CompilerParams(vmem_limit_bytes=56 * 2**20),
        cost_estimate=attention_cost(rows, q_heads, 2),
        name="attention_forward",
    )(place, low, full, cosine, sine, start_column, inner, jnp.swapaxes(outer, 1, 2), *qkv)
    return outs[:pieces], outs[pieces:]


def attend_back(qkv, d_context, context, sums, layout, q_heads, kv_heads):
    place, low, full, cosine, sine, start_row = layout
    pieces, ratio = len(qkv), q_heads // kv_heads
    rows = pieces * qkv[0].shape[0]
    tiles, lanes = rows // SUB, ratio * SUB
    bf16, f32 = jnp.bfloat16, jnp.float32
    inner, outer = stacked_matrices(q_heads, kv_heads)
    return pl.pallas_call(
        functools.partial(backward_kernel, pieces, ratio),
        out_shape=[jax.ShapeDtypeStruct(x.shape, bf16) for x in qkv],
        in_specs=[SMEM] * 3 + [VMEM] * (6 + kv_heads + 3 * pieces),
        out_specs=[VMEM] * pieces,
        scratch_shapes=[
            pltpu.VMEM((tiles, kv_heads, lanes, PAD), bf16),
            pltpu.VMEM((kv_heads, tiles, SUB, PAD), bf16),
            pltpu.VMEM((kv_heads, tiles, PAD, SUB), bf16),
            pltpu.VMEM((kv_heads, tiles, SUB, PAD), bf16),
            pltpu.VMEM((tiles, kv_heads, lanes, PAD), bf16),
            pltpu.VMEM((tiles * kv_heads, 1, lanes), f32),
            pltpu.VMEM((tiles * kv_heads, 1, lanes), f32),
            pltpu.VMEM((kv_heads, PAD, lanes), f32),
            pltpu.VMEM((kv_heads, tiles, SUB, PAD), f32),
            pltpu.VMEM((kv_heads, tiles, SUB, PAD), f32),
            pltpu.VMEM((kv_heads, tiles, SUB, ratio * PAD), bf16),
        ],
        compiler_params=pltpu.CompilerParams(vmem_limit_bytes=56 * 2**20),
        cost_estimate=attention_cost(rows, q_heads, 5),
        name="attention_backward",
    )(
        place, low, full, cosine, sine, start_row, inner, outer, jnp.swapaxes(inner, 1, 2),
        *sums, *qkv, *d_context, *context,
    )


def fetch(me, sources, target, sems):
    deep = sources[0].shape[0]
    return [
        pltpu.make_async_copy(
            source, target.at[pl.ds(pl.multiple_of((me[0] ^ j) * deep, deep), deep), :], sems.at[j]
        )
        for j, source in enumerate(sources)
    ]


def own_or_sibling(own, sibling, target):
    i, steps = pl.program_id(0), pl.num_programs(0)

    @pl.when(i < steps // 2)
    def from_own():
        target[...] = own[...]

    @pl.when(i >= steps // 2)
    def from_sibling():
        target[...] = sibling[...]


def gate_kernel(blocks, more, me, own, sibling, *refs):
    gate_up, refs = refs[:blocks], refs[blocks:]
    norm_all, gate_up_all, hidden_all, weight, sems = refs[3 if more else 0 :]
    hidden_cols = hidden_all.shape[1]
    copies = fetch(me, gate_up, weight, sems)

    @pl.when(pl.program_id(0) == 0)
    def first():
        for copy in copies:
            copy.start()
        for copy in copies:
            copy.wait()

    own_or_sibling(own, sibling, norm_all)
    x = norm_all[...]
    width = min(512, hidden_cols)
    for at in range(0, hidden_cols, width):
        gate_at = slice(at, at + width)
        up_at = slice(hidden_cols + at, hidden_cols + at + width)
        gate = dot32(x, weight[:, gate_at])
        up = dot32(x, weight[:, up_at])
        gate_up_all[:, gate_at] = gate
        gate_up_all[:, up_at] = up
        hidden_all[:, gate_at] = (gate * (1.0 / (1.0 + jnp.exp(-gate))) * up).astype(jnp.bfloat16)


def gate_back_kernel(blocks, more, me, own, sibling, down, gate_up_all, *refs):
    gate_up, refs = refs[:blocks], refs[blocks:]
    grad_all, d_gate_up_all, d_norm, weight, sems = refs[2 if more else 0 :]
    hidden_cols = down.shape[1]
    copies = fetch(me, gate_up, weight, sems)
    start = pl.program_id(0) == 0

    @pl.when(start)
    def first():
        for copy in copies:
            copy.start()

    own_or_sibling(own, sibling, grad_all)
    dy = grad_all[...]
    width = min(512, hidden_cols)
    for at in range(0, hidden_cols, width):
        gate_at = slice(at, at + width)
        up_at = slice(hidden_cols + at, hidden_cols + at + width)
        d_hidden = dot32(dy, down[:, gate_at])
        gate, up = gate_up_all[:, gate_at], gate_up_all[:, up_at]
        sigmoid = 1.0 / (1.0 + jnp.exp(-gate))
        d_gate = d_hidden * up * sigmoid * (1.0 + gate * (1.0 - sigmoid))
        d_gate_up_all[:, gate_at] = d_gate.astype(jnp.bfloat16)
        d_gate_up_all[:, up_at] = (d_hidden * (gate * sigmoid)).astype(jnp.bfloat16)

    @pl.when(start)
    def arrive():
        for copy in copies:
            copy.wait()

    d_norm[...] = times_transpose(d_gate_up_all[...], weight[...]).astype(jnp.bfloat16)


def piece_call(kernel, name, k, pieces, me, pair, whole, tiled, gate_up, earlier, outs, products):
    rows, width = pair[0].shape
    steps = 2 * rows // SUB
    blocks = len(gate_up)

    def own(i):
        return (jnp.minimum(i, steps // 2 - 1), 0)

    def sibling(i):
        return (jnp.maximum(i - steps // 2, 0), 0)

    def filled(i):
        return (k * steps + i, 0)

    flops = products * 2 * rows * 2 * width * gate_up[0].shape[1] // 2
    first_earlier = 3 + len(whole) + len(tiled) + blocks
    return pl.pallas_call(
        functools.partial(kernel, blocks, bool(earlier)),
        grid=(steps,),
        out_shape=[
            jax.ShapeDtypeStruct(((pieces if all_rows else 1) * 2 * rows, cols), kind)
            for cols, kind, all_rows in outs
        ],
        in_specs=[
            SMEM,
            pl.BlockSpec((SUB, width), own),
            pl.BlockSpec((SUB, width), sibling),
            *(pl.BlockSpec(x.shape, lambda i: (0, 0)) for x in whole),
            *(pl.BlockSpec((SUB, x.shape[1]), filled) for x in tiled),
            *[ANY] * (blocks + len(earlier)),
        ],
        out_specs=[
            pl.BlockSpec((SUB, cols), filled if all_rows else lambda i: (i, 0))
            for cols, kind, all_rows in outs
        ],
        scratch_shapes=[
            pltpu.VMEM((blocks * gate_up[0].shape[0], gate_up[0].shape[1]), jnp.bfloat16),
            pltpu.SemaphoreType.DMA((blocks,)),
        ],
        input_output_aliases={first_earlier + n: n for n in range(len(earlier))},
        compiler_params=pltpu.CompilerParams(vmem_limit_bytes=56 * 2**20),
        cost_estimate=pl.CostEstimate(
            flops=flops, bytes_accessed=flops // 512, transcendentals=2 * rows * gate_up[0].shape[1] // 2
        ),
        name=f"{name}_{k}",
    )(me, *pair, *whole, *tiled, *gate_up, *earlier)


def flip(x, axis):
    return lax.ppermute(x, axis, FLIP)


def swap(x):
    return lax.ppermute(x, ("core", "zh"), [(0, 0), (1, 2), (2, 1), (3, 3)])


def from_near(x, k):
    n = lax.axis_size("zl")
    return lax.ppermute(x, "zl", [((j + k) % n, j) for j in range(n)])


def to_near(x, k):
    n = lax.axis_size("zl")
    return lax.ppermute(x, "zl", [(j, (j + k) % n) for j in range(n)])


def across(x, j):
    n = lax.axis_size("yx")
    return lax.ppermute(x, "yx", [(a, a ^ j) for a in range(n)])


def cross_z(w):
    return cross_core(w, flip(w, "zh"))


def cross_core(w, far):
    core, zh = lax.axis_index("core"), lax.axis_index("zh")
    mine = jnp.where(core == zh, w, far)
    taken = flip(jnp.where(core == zh, far, w), "core")
    return jnp.concatenate(
        [jnp.where(core == 0, mine, taken), jnp.where(core == 0, taken, mine)], axis=0
    )


def neighbours(x):
    count = lax.axis_size("yx")
    return [across(x, j) for j in range(1, count if count != 4 else 3)]


def diagonal(taken):
    if lax.axis_size("yx") != 4:
        return []
    half = taken[0].shape[0] // 2
    return [across(taken[1][:half], 1), across(taken[0][half:], 2)]


def blocks_of(own, taken, halves):
    return [own, *taken, *([jnp.concatenate(halves, axis=0)] if halves else [])]


def in_order(blocks, axis=0):
    size = blocks[0].shape[axis]
    shape = list(blocks[0].shape)
    shape[axis] = size * len(blocks)
    whole = jnp.zeros(shape, blocks[0].dtype)
    me = lax.axis_index("yx")
    for j, block in enumerate(blocks):
        whole = lax.dynamic_update_slice_in_dim(whole, block, (me ^ j) * size, axis)
    return whole


def block_of(grad, j):
    size = grad.shape[0] // lax.axis_size("yx")
    return lax.dynamic_slice_in_dim(grad, (lax.axis_index("yx") ^ j) * size, size, 0)


def send_yx(grad):
    count = lax.axis_size("yx")
    if count != 4:
        return [across(block_of(grad, j), j) for j in range(1, count)]
    far = block_of(grad, 3)
    half = far.shape[0] // 2
    return [across(far[:half], 1), across(far[half:], 2)]


def join_yx(grad, taken):
    if lax.axis_size("yx") != 4:
        return taken, block_of(grad, 0)
    half = taken[0].shape[0]
    one, two = block_of(grad, 1), block_of(grad, 2)
    one = jnp.concatenate([one[:half], one[half:] + taken[1]], axis=0)
    two = jnp.concatenate([two[:half] + taken[0], two[half:]], axis=0)
    return [across(one, 1), across(two, 2)], block_of(grad, 0)


def total_yx(taken, own):
    total = own.astype(jnp.float32)
    for part in taken:
        total = total + part.astype(jnp.float32)
    return total.astype(jnp.bfloat16)


def home_core(part):
    core, zh = lax.axis_index("core"), lax.axis_index("zh")
    half = part.shape[0] // 2
    upper, lower = part[:half], part[half:]
    mine = jnp.where(core == 0, upper, lower)
    taken = flip(jnp.where(core == 0, lower, upper), "core")
    return jnp.where(core == zh, mine, taken), jnp.where(core == zh, taken, mine)


def home(keep, give):
    return keep.astype(jnp.float32) + flip(give, "zh").astype(jnp.float32)


def body(
    tokens,
    cotangent,
    seq_lengths,
    attn_gain,
    q_weight,
    key_projection,
    value_projection,
    out_weight,
    mlp_gain,
    gate_weight,
    up_weight,
    down_weight,
):
    bf16, f32 = jnp.bfloat16, jnp.float32
    core, zl, yx = lax.axis_index("core"), lax.axis_index("zl"), lax.axis_index("yx")
    near = lax.axis_size("zl")
    others = range(1, near)
    rows = tokens.shape[0]
    group_rows = 2 * near * rows
    query_cols, key_cols = q_weight.shape[1], key_projection.shape[1]
    qkv_cols = query_cols + 2 * key_cols
    q_heads, kv_heads = query_cols // HD, key_cols // HD
    hidden_cols = gate_weight.shape[1]
    deep = q_weight.shape[0]
    me = yx.astype(jnp.int32).reshape(1)

    qkv_shard = jnp.concatenate([q_weight, key_projection, value_projection], axis=1)
    gain_rows = jnp.concatenate([attn_gain, mlp_gain, jnp.zeros((qkv_cols + query_cols - 2 * deep,), bf16)])
    gain_rows = jnp.concatenate([gain_rows[None], jnp.zeros((15, gain_rows.shape[0]), bf16)], axis=0)
    shard = jnp.concatenate([jnp.concatenate([qkv_shard, out_weight], axis=1), gain_rows], axis=0)
    part_rows = rows // 2
    shard_far = flip(shard, "zh")
    upper = swap(tokens[:part_rows])
    lengths = swap(seq_lengths)
    shard_far, upper, lengths, second_part = stage(shard_far, upper, lengths, tokens[part_rows:])

    lower = swap(second_part)
    upper_far = [from_near(upper, k) for k in others]
    pair = cross_core(shard, shard_far)
    taken = neighbours(pair)
    step = deep + 16
    out_pair = jnp.concatenate([pair[:deep, qkv_cols:], pair[step : step + deep, qkv_cols:]], axis=0)
    out_far = [from_near(out_pair, k) for k in others]

    subs = jnp.arange(group_rows // SUB, dtype=jnp.int32)
    per_device = rows // SUB
    source, within = subs // per_device, subs % per_device
    there_core, there_zl = (source % 2) ^ core, (source // 2 + zl) % near
    to_order = (there_core * near + there_zl) * per_device + within
    from_order = (((source % near - zl) % near) * 2 + ((source // near) ^ core)) * per_device + within
    place = jnp.concatenate([to_order, from_order])
    row_at, doc_start = document_layout(lengths, group_rows)
    cosine, sine = rotary_tables(row_at - doc_start)

    def bounds(size):
        tile_start = doc_start.reshape(-1, size)
        tile = jnp.arange(group_rows // size, dtype=jnp.int32)
        low = tile_start[:, 0] // size
        return low, jnp.minimum((tile_start[:, -1] + size - 1) // size, tile)

    start_row = jnp.tile(doc_start.reshape(-1, 1, SUB), (1, 1, q_heads // kv_heads))
    layout = (place, *bounds(TILE), cosine, sine, doc_start[:, None])
    layout_back = (place, *bounds(SUB), cosine, sine, start_row)
    lower, *moved = stage(lower, *upper_far, *taken, *out_far, *layout, *layout_back)
    upper_far, moved = moved[: near - 1], moved[near - 1 :]
    taken, moved = moved[: len(taken)], moved[len(taken) :]
    out_far, moved = moved[: near - 1], moved[near - 1 :]
    layout, layout_back = moved[: len(layout)], moved[len(layout) :]

    lower_far = [from_near(lower, k) for k in others]
    halves = diagonal(taken)
    own = jnp.concatenate([upper, lower], axis=0)
    own_sib = flip(own, "core")
    blocks = blocks_of(pair, taken, halves)
    whole = in_order([jnp.concatenate([x[:deep], x[step : step + deep]], axis=0) for x in blocks])
    w_project, w_out_first = whole[:, :qkv_cols], whole[:, qkv_cols:]
    gain_all = in_order(
        [
            jnp.concatenate([x[deep, : 2 * deep].reshape(2, deep), x[step + deep, : 2 * deep].reshape(2, deep)], axis=1)
            for x in blocks
        ],
        axis=1,
    ).astype(f32)
    gain_one, gain_two = gain_all[0], gain_all[1]

    def project(parts):
        values = jnp.concatenate(parts, axis=0).astype(f32)
        norm = norm_rows(values, gain_one)[1]
        return norm, dot32(norm, w_project).astype(bf16)

    norm_near, qkv_near = project([own, own_sib])
    gate_up_shard = jnp.concatenate([gate_weight, up_weight], axis=1)
    qkv_near, own, gate_up_shard, *moved = stage(qkv_near, own, gate_up_shard, *lower_far, *out_far)
    lower_far, out_far = moved[: near - 1], moved[near - 1 :]

    gate_up_far = flip(gate_up_shard, "zh")
    out_taken = [neighbours(x) for x in out_far]
    norm_one, qkv = [norm_near], [qkv_near]
    for k in others:
        far = jnp.concatenate([upper_far[k - 1], lower_far[k - 1]], axis=0)
        norm, projected = project([far, flip(far, "core")])
        norm_one.append(norm)
        qkv.append(projected)
    residual = own.astype(f32)
    scale_one = lax.rsqrt(jnp.mean(residual * residual, axis=-1, keepdims=True) + EPSILON)
    context, sums = attend(qkv, layout, q_heads, kv_heads)
    out_halves = [diagonal(x) for x in out_taken]
    w_out_near = jnp.concatenate(
        [w_out_first, *(in_order(blocks_of(x, t, h)) for x, t, h in zip(out_far, out_taken, out_halves, strict=True))],
        axis=1,
    )
    cotangent, gate_up_far, w_out_near, *context = stage(cotangent, gate_up_far, w_out_near, *context)

    moved_context = [to_near(context[k], k) for k in others]
    gate_up_pair = cross_core(gate_up_shard, gate_up_far)
    gate_up_taken = neighbours(gate_up_pair)
    own_cotangent = swap(cotangent)
    w_out_sib = flip(w_out_near, "core")
    own_cotangent, w_out_sib, down_shard, *moved = stage(
        own_cotangent, w_out_sib, down_weight, *moved_context, *gate_up_taken
    )
    moved_context, gate_up_taken = moved[: near - 1], moved[near - 1 :]

    gate_up_halves = diagonal(gate_up_taken)
    down_far = flip(down_shard, "zh")
    quarters = [context[0]] + [None] * (near - 1)
    for k in others:
        quarters[near - k] = moved_context[k - 1]
    own_context = jnp.concatenate([q[:rows] for q in quarters], axis=1)
    sib_context = flip(jnp.concatenate([q[rows:] for q in quarters], axis=1), "core")
    mid = residual + times_transpose(own_context, w_out_near) + times_transpose(sib_context, w_out_sib)
    scale_two, norm_two = norm_rows(mid, gain_two)
    norm_two, down_far, own_cotangent, *gate_up_halves = stage(norm_two, down_far, own_cotangent, *gate_up_halves)

    norm_far = [from_near(norm_two, k) for k in others]
    norm_sib = flip(norm_two, "core")
    gate_up = blocks_of(gate_up_pair, gate_up_taken, gate_up_halves)
    down_pair = cross_core(down_shard, down_far)
    down_taken = neighbours(down_pair)
    cot_sib = flip(own_cotangent, "core")
    outs = [(norm_two.shape[1], bf16, True), (2 * hidden_cols, f32, True), (hidden_cols, bf16, True)]
    earlier = piece_call(gate_kernel, "gate", 0, near, me, [norm_two, norm_sib], [], [], gate_up, [], outs, 2)
    own_cotangent, cot_sib, *moved = stage(own_cotangent, cot_sib, *norm_far, *down_taken, *earlier)
    norm_far, moved = moved[: near - 1], moved[near - 1 :]
    down_taken, earlier = moved[: len(down_taken)], moved[len(down_taken) :]

    cot_far = [from_near(own_cotangent, k) for k in others]
    down_halves = diagonal(down_taken)
    for k in others:
        far_pair = [norm_far[k - 1], flip(norm_far[k - 1], "core")]
        earlier = piece_call(gate_kernel, "gate", k, near, me, far_pair, [], [], gate_up, earlier, outs, 2)
    norm_two_all, gate_up_all, hidden_all = earlier
    w_down = in_order(blocks_of(down_pair, down_taken, down_halves))
    outs = [(norm_two.shape[1], bf16, True), (2 * hidden_cols, bf16, True), (norm_two.shape[1], bf16, False)]
    *earlier, d_norm_near = piece_call(
        gate_back_kernel, "gate_back", 0, near, me, [own_cotangent, cot_sib], [w_down], [gate_up_all], gate_up,
        [], outs, 3,
    )
    out_all = times_transpose(hidden_all, w_down).astype(bf16)
    out_own = jnp.concatenate([out_all[2 * k * rows : (2 * k + 1) * rows] for k in range(near)], axis=0)
    out_sib = jnp.concatenate([out_all[(2 * k + 1) * rows : (2 * k + 2) * rows] for k in range(near)], axis=0)
    out_both = (out_own.astype(f32) + flip(out_sib, "core").astype(f32)).astype(bf16)
    out_both, d_norm_near, *moved = stage(out_both, d_norm_near, *cot_far, *earlier)
    cot_far, earlier = moved[: near - 1], moved[near - 1 :]

    out_moved = [to_near(out_both[k * rows : (k + 1) * rows], k) for k in others]
    d_norms = [d_norm_near]
    for k in others:
        *earlier, d_norm = piece_call(
            gate_back_kernel, "gate_back", k, near, me, [cot_far[k - 1], flip(cot_far[k - 1], "core")], [w_down],
            [gate_up_all], gate_up, earlier, outs, 3,
        )
        d_norms.append(d_norm)
    d_norm_sums = [d[:rows].astype(f32) + flip(d[rows:], "core").astype(f32) for d in d_norms]
    d_norm_sent = [d_norm_sums[k].astype(bf16) for k in others]
    *moved, grad_all, d_gate_up_all = stage(*d_norm_sent, *out_moved, *earlier)
    d_norm_sent, out_moved = moved[: near - 1], moved[near - 1 :]

    d_norm_moved = [to_near(d_norm_sent[k - 1], k) for k in others]
    grad_gate_up = rows_product(norm_two_all, d_gate_up_all).astype(bf16)
    gate_up_sent = send_yx(grad_gate_up)
    grad_down = rows_product(grad_all, hidden_all).astype(bf16)
    output_own = mid + out_both[:rows].astype(f32)
    for part in out_moved:
        output_own = output_own + part.astype(f32)
    output_own = output_own.astype(bf16)
    output_own, grad_down, grad_gate_up, *moved = stage(
        output_own, grad_down, grad_gate_up, *d_norm_moved, *gate_up_sent
    )
    d_norm_moved, gate_up_sent = moved[: near - 1], moved[near - 1 :]

    output = swap(output_own)
    gate_up_moved, gate_up_own = join_yx(grad_gate_up, gate_up_sent)
    down_sent = send_yx(grad_down)
    d_norm_two = d_norm_sums[0]
    for part in d_norm_moved:
        d_norm_two = d_norm_two + part.astype(f32)
    mid_back, _ = norm_back(mid, scale_two, gain_two, d_norm_two)
    d_mid = own_cotangent.astype(f32) + mid_back
    d_attn = d_mid.astype(bf16)
    d_context_sib = flip(dot32(d_attn, w_out_sib).astype(bf16), "core")
    d_context_near = dot32(d_attn, w_out_near).astype(bf16)
    both = [
        jnp.concatenate(
            [d_context_near[:, k * query_cols : (k + 1) * query_cols],
             d_context_sib[:, k * query_cols : (k + 1) * query_cols]], axis=0)
        for k in range(near)
    ]
    d_attn, *moved = stage(d_attn, *both, *down_sent)
    both, down_sent = moved[:near], moved[near:]

    d_context = [both[0]] + [None] * (near - 1)
    for k in others:
        d_context[near - k] = to_near(both[k], k)
    grad_out_near = rows_product(d_attn, own_context)
    grad_out_sib = flip(rows_product(d_attn, sib_context).astype(bf16), "core")
    grad_out = (grad_out_near + grad_out_sib.astype(f32)).astype(bf16)
    output, grad_out, *moved = stage(output, grad_out, *d_context, *gate_up_moved)
    d_context, gate_up_moved = moved[:near], moved[near:]

    down_moved, down_own = join_yx(grad_down, down_sent)
    out_sent = send_yx(grad_out)
    gate_up_keep, gate_up_give = home_core(total_yx(gate_up_moved, gate_up_own))
    gate_up_home = flip(gate_up_give, "zh")
    gate_up_give, *d_context = stage(gate_up_give, *d_context)
    d_qkv = attend_back(qkv, d_context, context, sums, layout_back, q_heads, kv_heads)
    gate_up_home, *moved = stage(gate_up_home, *d_qkv, *down_moved, *out_sent)
    d_qkv, moved = moved[:near], moved[near:]
    down_moved, out_sent = moved[: len(down_moved)], moved[len(down_moved) :]

    far_first = []
    for k in reversed(range(near)):
        part = times_transpose(d_qkv[k], w_project).astype(bf16)
        part = part[:rows].astype(f32) + flip(part[rows:], "core").astype(f32)
        far_first.append(part if k == 0 else part.astype(bf16))
    total = far_first[-1]
    d_moved = [to_near(far_first[near - 1 - k], k) for k in others]
    grad_project = sum(rows_product(norm, d) for norm, d in zip(norm_one, d_qkv, strict=True))
    grad_project = grad_project.astype(bf16)
    project_sent = send_yx(grad_project)
    out_moved, out_own = join_yx(grad_out, out_sent)
    down_keep, down_give = home_core(total_yx(down_moved, down_own))
    down_home = flip(down_give, "zh")
    down_home, *moved = stage(down_home, *d_moved, *project_sent, *out_moved)
    d_moved, moved = moved[: near - 1], moved[near - 1 :]
    project_sent, out_moved = moved[: len(project_sent)], moved[len(project_sent) :]

    project_moved, project_own = join_yx(grad_project, project_sent)
    for part in d_moved:
        total = total + part.astype(f32)
    input_back, _ = norm_back(residual, scale_one, gain_one, total)
    input_grad = swap((d_mid + input_back).astype(bf16)).astype(f32)
    grad_out = total_yx(out_moved, out_own)
    grad_out_quarter = grad_out[:, :query_cols].astype(f32)
    for k in others:
        moved = to_near(grad_out[:, k * query_cols : (k + 1) * query_cols], k)
        grad_out_quarter = grad_out_quarter + moved.astype(f32)
    grad_out = home(*home_core(grad_out_quarter.astype(bf16)))
    grad_project = home(*home_core(total_yx(project_moved, project_own)))
    grad_gate_up = gate_up_keep.astype(f32) + gate_up_home.astype(f32)
    grad_down = down_keep.astype(f32) + down_home.astype(f32)
    gain_grads = lax.psum(
        jnp.stack(
            [
                jnp.sum(qkv_shard.astype(f32) * grad_project, axis=1),
                jnp.sum(gate_up_shard.astype(f32) * grad_gate_up, axis=1),
            ]
        ),
        ("zh", "zl"),
    ) / jnp.stack([attn_gain, mlp_gain]).astype(f32)
    return (
        output,
        input_grad,
        gain_grads[0],
        grad_project[:, :query_cols],
        grad_project[:, query_cols : query_cols + key_cols],
        grad_project[:, query_cols + key_cols :],
        grad_out,
        gain_grads[1],
        grad_gate_up[:, :hidden_cols],
        grad_gate_up[:, hidden_cols:],
        grad_down,
    )


def solution(mesh):
    dp, tensor = mesh.shape["dp"], mesh.shape["tensor"]
    fine = Mesh(mesh.devices.reshape(dp // 2, 2, 2, tensor // 2), AXES)
    by_rows, by_dp, by_both = P(AXES, None), P(("yx", "core")), P(("yx", "core"), ("zh", "zl"))
    return jax.shard_map(
        body,
        mesh=fine,
        in_specs=(
            by_rows, by_rows, P(("yx", "core"), None), by_dp, by_both, by_both, by_both, by_both,
            by_dp, by_both, by_both, by_both,
        ),
        out_specs=(
            by_rows, by_rows, by_dp, by_both, by_both, by_both, by_both, by_dp, by_both, by_both, by_both,
        ),
        check_vma=False,
    )
```

```python
import functools
import math

import jax
import jax.numpy as jnp
import numpy as np
from jax import lax
from jax.experimental import pallas as pl
from jax.experimental.pallas import tpu as pltpu
from jax.sharding import Mesh
from jax.sharding import PartitionSpec as P

HD = 96
HALF = HD // 2
PAD = 128
SUB = 256
TILE = 512

EPSILON = 1e-05
ROTARY_BASE = 100000.0
MASKED = -1e30
LOG2E = math.log2(math.e)

AXES = ("yx", "core", "zh", "zl")
FLIP = [(0, 1), (1, 0)]


def norm_rows(values, gain):
    row_scale = lax.rsqrt(jnp.mean(values * values, axis=-1, keepdims=True) + EPSILON)
    return (row_scale, (values * row_scale * gain).astype(jnp.bfloat16))


def norm_back(values, row_scale, gain, upstream):
    weighted = upstream * gain
    inner_sum = jnp.mean(weighted * values, axis=-1, keepdims=True)
    grad_in = row_scale * weighted - values * (row_scale * row_scale * row_scale) * inner_sum
    gain_part = jnp.sum(upstream * (values * row_scale), axis=0)
    return (grad_in, gain_part)


def document_layout(lengths, group_rows):
    flat_lengths = lengths.reshape(-1)
    doc_ends = jnp.cumsum(flat_lengths)
    rows = jnp.arange(group_rows, dtype=jnp.int32)
    passed = (rows[:, None] >= doc_ends[None, :]).astype(jnp.int32)
    return (rows, jnp.sum(passed * flat_lengths[None, :], axis=1))


def rotary_tables(positions):
    exponents = jnp.arange(HALF, dtype=jnp.float32) * (2.0 / HD)
    inverse = ROTARY_BASE ** (-exponents)
    angles = positions.astype(jnp.float32)[:, None] * inverse[None, :]
    cosine, sine = jnp.cos(angles), jnp.sin(angles)
    gap = jnp.zeros((positions.shape[0], PAD // 2 - HALF), jnp.float32)
    return (
        jnp.concatenate([cosine, gap, cosine, gap], axis=1),
        jnp.concatenate([-sine, gap, sine, gap], axis=1),
    )


def rows_product(left, right):
    return lax.dot_general(
        left, right, (((0,), (0,)), ((), ())), preferred_element_type=jnp.float32
    )


def times_transpose(left, right):
    return lax.dot_general(
        left, right, (((1,), (1,)), ((), ())), preferred_element_type=jnp.float32
    )


def dot32(left, right):
    return jnp.dot(left, right, preferred_element_type=jnp.float32)


def stage(*values):
    return lax.optimization_barrier(values)


def spread(columns, heads):
    matrix = np.zeros((columns, len(heads) * PAD), np.float32)
    for at, first in enumerate(heads):
        for half in range(2):
            for i in range(HALF):
                matrix[first + half * HALF + i, at * PAD + half * (PAD // 2) + i] = 1.0
    return matrix


def turn(x, cosine, sine):
    return x * cosine + pltpu.roll(x, PAD // 2, 1) * sine


def rows_at(t, size):
    return pl.ds(pl.multiple_of(t * size, size), size)


def forward_kernel(pieces, ratio, *refs):
    place, low, full, cosine, sine, start, spread_in, gather_out = refs[:8]
    heads = spread_in.shape[0]
    refs = refs[8:]
    qkv, context, refs = refs[0], refs[1 : 1 + pieces], refs[1 + pieces :]
    log_sum, refs = refs[:heads], refs[heads:]
    q_s, k_s, v_s, s_s, top_s, acc = refs
    tiles = q_s.shape[0]
    all_subs = qkv.shape[0] // SUB
    piece_subs = all_subs // pieces
    scale = LOG2E * HD ** (-0.5)
    ones_lane = lax.broadcasted_iota(jnp.int32, (SUB, PAD), 1) == PAD - 1

    def prepare(r, carry):
        t = place[r]
        at = rows_at(t, SUB)
        cos_t, sin_t = cosine[at, :], sine[at, :]
        tile, half = t // (TILE // SUB), t % (TILE // SUB)
        for g in range(heads):
            wide = dot32(qkv[rows_at(r, SUB), :], spread_in[g])
            for h in range(ratio):
                query = turn(wide[:, h * PAD : (h + 1) * PAD], cos_t, sin_t) * scale
                first = pl.multiple_of(h * TILE + half * SUB, SUB)
                q_s[tile, g, pl.ds(first, SUB), :] = query.astype(jnp.bfloat16)
            key = turn(wide[:, ratio * PAD : (ratio + 1) * PAD], cos_t, sin_t)
            k_s[g, at, :] = key.astype(jnp.bfloat16)
            value = jnp.where(ones_lane, 1.0, wide[:, (ratio + 1) * PAD :])
            v_s[g, at, :] = value.astype(jnp.bfloat16)
        return carry

    lax.fori_loop(0, all_subs, prepare, 0)

    def query_tile(i, carry):
        starts = jnp.concatenate([start[rows_at(i, TILE), :]] * ratio, axis=0)
        top_s[...] = jnp.full_like(top_s, MASKED)

        def scores(j, masked, diagonal):
            for g in range(heads):
                s = times_transpose(q_s[i, g], k_s[g, rows_at(j, TILE), :])
                if masked:
                    key_at = lax.broadcasted_iota(jnp.int32, s.shape, 1)
                    allowed = key_at + j * TILE >= starts
                    if diagonal:
                        query_at = lax.rem(lax.broadcasted_iota(jnp.int32, s.shape, 0), TILE)
                        allowed = allowed & (key_at <= query_at)
                    s = jnp.where(allowed, s, MASKED)
                s_s[g, j] = s
                peak = s[:, :PAD]
                for c in range(1, TILE // PAD):
                    peak = jnp.maximum(peak, s[:, c * PAD : (c + 1) * PAD])
                top_s[g] = jnp.maximum(top_s[g], peak)

        def loop(first, last, masked):
            def run(j, c):
                scores(j, masked, False)
                return c

            lax.fori_loop(first, last, run, 0)

        loop(low[i], full[i], True)
        loop(full[i], i, False)
        scores(i, True, True)
        tops = [jnp.max(top_s[g], axis=1, keepdims=True) for g in range(heads)]
        acc[...] = jnp.zeros_like(acc)

        def weigh(j, c):
            for g in range(heads):
                p = jnp.exp2(s_s[g, j] - tops[g]).astype(jnp.bfloat16)
                acc[g] += dot32(p, v_s[g, rows_at(j, TILE), :])
            return c

        lax.fori_loop(low[i], i + 1, weigh, 0)
        packed = None
        for g in range(heads):
            total = acc[g][:, PAD - 1 :]
            out = acc[g] * (1.0 / total)
            sums = jnp.broadcast_to(tops[g] + jnp.log(total) * LOG2E, (ratio * TILE, PAD))
            log_sum[g][i] = sums.T[:1, :]
            wide = jnp.concatenate(
                [out[h * TILE : (h + 1) * TILE, :] for h in range(ratio)], axis=1
            ).astype(jnp.bfloat16)
            part = dot32(wide, gather_out[g])
            packed = part if packed is None else packed + part
        subs = tiles * (TILE // SUB)
        for half in range(TILE // SUB):
            r = place[subs + i * (TILE // SUB) + half]
            part = packed[half * SUB : (half + 1) * SUB, :].astype(jnp.bfloat16)
            for k in range(pieces):

                @pl.when(r // piece_subs == k)
                def store(k=k, part=part, r=r):
                    context[k][rows_at(r % piece_subs, SUB), :] = part

        return carry

    lax.fori_loop(0, tiles, query_tile, 0)


def backward_kernel(pieces, ratio, more, *refs):
    place, low, full, cosine, sine, start, refs = *refs[:6], refs[6:]
    heads = refs[0].shape[0]
    spread_in, spread_out, gather_in, refs = *refs[:3], refs[3:]
    log_sum, refs = refs[:heads], refs[heads:]
    d_context, context, qkv, refs = refs[:pieces], refs[pieces : 2 * pieces], refs[2 * pieces], refs[2 * pieces + 1 :]
    earlier, refs = (refs[0], refs[1:]) if more else (None, refs)
    d_qkv, refs = refs[0], refs[1:]
    q_s, k_s, kt_s, v_s, do_s, delta_s, log_s, dq_acc, dk_acc, dv_acc, dq_s = refs
    tiles = q_s.shape[0]
    all_subs = qkv.shape[0] // SUB
    piece_subs = all_subs // pieces
    scale = HD ** (-0.5)
    per_tile = TILE // SUB

    for k in range(pieces):

        def prepare(r, carry, k=k):
            t = place[k * piece_subs + r]
            rel = rows_at(r, SUB)
            at = rows_at(t, SUB)
            cos_t, sin_t = cosine[at, :], sine[at, :]
            for g in range(heads):
                wide = dot32(qkv[rows_at(k * piece_subs + r, SUB), :], spread_in[g])
                d_out = dot32(d_context[k][rel, :], spread_out[g])
                out = dot32(context[k][rel, :], spread_out[g])
                for h in range(ratio):
                    cols = slice(h * PAD, (h + 1) * PAD)
                    rows = slice(h * SUB, (h + 1) * SUB)
                    query = turn(wide[:, cols], cos_t, sin_t) * (scale * LOG2E)
                    q_s[t, g, rows, :] = query.astype(jnp.bfloat16)
                    do_s[t, g, rows, :] = d_out[:, cols].astype(jnp.bfloat16)
                    delta = jnp.sum((d_out[:, cols] * out[:, cols]).T, axis=0, keepdims=True)
                    delta_s[t * heads + g, :, rows] = delta
                    first = pl.multiple_of(h * TILE + t % per_tile * SUB, SUB)
                    log_s[t * heads + g, :, rows] = log_sum[g][t // per_tile, :, pl.ds(first, SUB)]
                key = turn(wide[:, ratio * PAD : (ratio + 1) * PAD], cos_t, sin_t)
                k_s[g, t] = key.astype(jnp.bfloat16)
                kt_s[g, t] = key.T.astype(jnp.bfloat16)
                v_s[g, t] = wide[:, (ratio + 1) * PAD :].astype(jnp.bfloat16)
                dk_acc[g, t] = jnp.zeros((SUB, PAD), jnp.float32)
                dv_acc[g, t] = jnp.zeros((SUB, PAD), jnp.float32)
            return carry

        lax.fori_loop(0, piece_subs, prepare, 0)

    def query_tile(i, carry):
        dq_acc[...] = jnp.zeros_like(dq_acc)

        def step(j, masked, diagonal):
            for g in range(heads):
                queries, d_out = q_s[i, g], do_s[i, g]
                s = times_transpose(k_s[g, j], queries)
                if masked:
                    key_at = lax.broadcasted_iota(jnp.int32, s.shape, 0)
                    allowed = key_at + j * SUB >= start[i]
                    if diagonal:
                        query_at = lax.rem(lax.broadcasted_iota(jnp.int32, s.shape, 1), SUB)
                        allowed = allowed & (key_at <= query_at)
                    s = jnp.where(allowed, s, MASKED)
                p = jnp.exp2(s - log_s[i * heads + g])
                d_p = times_transpose(v_s[g, j], d_out)
                d_s = (p * (d_p - delta_s[i * heads + g])).astype(jnp.bfloat16)
                dv_acc[g, j] += dot32(p.astype(jnp.bfloat16), d_out)
                dk_acc[g, j] += dot32(d_s, queries)
                dq_acc[g] += dot32(kt_s[g, j], d_s)

        def loop(first, last, masked):
            def run(j, c):
                step(j, masked, False)
                return c

            lax.fori_loop(first, last, run, 0)

        loop(low[i], full[i], True)
        loop(full[i], i, False)
        step(i, True, True)
        at = rows_at(i, SUB)
        cos_t, sin_t = cosine[at, :], sine[at, :]
        for g in range(heads):
            grad = dq_acc[g].T * scale
            for h in range(ratio):
                piece = turn(grad[h * SUB : (h + 1) * SUB, :], cos_t, -sin_t)
                dq_s[g, i, :, h * PAD : (h + 1) * PAD] = piece.astype(jnp.bfloat16)
        return carry

    lax.fori_loop(0, tiles, query_tile, 0)

    def finish(r, carry):
        t = place[r]
        at = rows_at(t, SUB)
        rel = rows_at(r, SUB)
        packed = None
        for g in range(heads):
            key = turn(dk_acc[g, t] * (1.0 / LOG2E), cosine[at, :], -sine[at, :])
            wide = jnp.concatenate(
                [dq_s[g, t], key.astype(jnp.bfloat16), dv_acc[g, t].astype(jnp.bfloat16)], axis=1
            )
            part = dot32(wide, gather_in[g])
            packed = part if packed is None else packed + part
        packed = packed.astype(jnp.bfloat16)
        d_qkv[rel, :] = packed + earlier[rel, :] if more else packed
        return carry

    lax.fori_loop(0, all_subs, finish, 0)


SMEM = pl.BlockSpec(memory_space=pltpu.SMEM)
VMEM = pl.BlockSpec(memory_space=pltpu.VMEM)
ANY = pl.BlockSpec(memory_space=pl.ANY)


def small_cost(transcendentals=0):
    return pl.CostEstimate(flops=1 << 20, bytes_accessed=1 << 16, transcendentals=transcendentals)


def head_matrices(head, q_heads, kv_heads):
    ratio = q_heads // kv_heads
    queries = [(head * ratio + r) * HD for r in range(ratio)]
    key, value = (q_heads + head) * HD, (q_heads + kv_heads + head) * HD
    inner = spread((q_heads + 2 * kv_heads) * HD, [*queries, key, value])
    outer = spread(q_heads * HD, queries)
    return jnp.asarray(inner, jnp.bfloat16), jnp.asarray(outer, jnp.bfloat16)


def stacked_matrices(q_heads, kv_heads):
    pairs = [head_matrices(head, q_heads, kv_heads) for head in range(kv_heads)]
    return jnp.stack([inner for inner, _ in pairs]), jnp.stack([outer for _, outer in pairs])


def attend(qkv, pieces, layout, q_heads, kv_heads):
    place, low, full, cosine, sine, start_column = layout
    ratio, rows = q_heads // kv_heads, qkv.shape[0]
    tiles, lanes = rows // TILE, ratio * TILE
    bf16, f32 = jnp.bfloat16, jnp.float32
    inner, outer = stacked_matrices(q_heads, kv_heads)
    outs = pl.pallas_call(
        functools.partial(forward_kernel, pieces, ratio),
        out_shape=[
            *[jax.ShapeDtypeStruct((rows // pieces, q_heads * HD), bf16)] * pieces,
            *[jax.ShapeDtypeStruct((tiles, 1, lanes), f32)] * kv_heads,
        ],
        in_specs=[SMEM] * 3 + [VMEM] * 6,
        out_specs=[VMEM] * (pieces + kv_heads),
        scratch_shapes=[
            pltpu.VMEM((tiles, kv_heads, lanes, PAD), bf16),
            pltpu.VMEM((kv_heads, rows, PAD), bf16),
            pltpu.VMEM((kv_heads, rows, PAD), bf16),
            pltpu.VMEM((kv_heads, tiles, lanes, TILE), f32),
            pltpu.VMEM((kv_heads, lanes, PAD), f32),
            pltpu.VMEM((kv_heads, lanes, PAD), f32),
        ],
        compiler_params=pltpu.CompilerParams(vmem_limit_bytes=56 * 2**20),
        cost_estimate=small_cost(),
        name="attention_forward",
    )(place, low, full, cosine, sine, start_column, inner, jnp.swapaxes(outer, 1, 2), qkv)
    return outs[:pieces], outs[pieces:]


def attend_back(heads, qkv, d_context, context, sums, earlier, layout, q_heads, kv_heads):
    place, low, full, cosine, sine, start_row = layout
    pieces, ratio, rows = len(context), q_heads // kv_heads, qkv.shape[0]
    tiles, lanes, count = rows // SUB, ratio * SUB, len(heads)
    bf16, f32 = jnp.bfloat16, jnp.float32
    inner, outer = stacked_matrices(q_heads, kv_heads)
    inner, outer = inner[heads[0] : heads[0] + count], outer[heads[0] : heads[0] + count]
    return pl.pallas_call(
        functools.partial(backward_kernel, pieces, ratio, bool(earlier)),
        out_shape=jax.ShapeDtypeStruct(qkv.shape, bf16),
        in_specs=[SMEM] * 3 + [VMEM] * (7 + count + 2 * pieces + len(earlier)),
        out_specs=VMEM,
        scratch_shapes=[
            pltpu.VMEM((tiles, count, lanes, PAD), bf16),
            pltpu.VMEM((count, tiles, SUB, PAD), bf16),
            pltpu.VMEM((count, tiles, PAD, SUB), bf16),
            pltpu.VMEM((count, tiles, SUB, PAD), bf16),
            pltpu.VMEM((tiles, count, lanes, PAD), bf16),
            pltpu.VMEM((tiles * count, 1, lanes), f32),
            pltpu.VMEM((tiles * count, 1, lanes), f32),
            pltpu.VMEM((count, PAD, lanes), f32),
            pltpu.VMEM((count, tiles, SUB, PAD), f32),
            pltpu.VMEM((count, tiles, SUB, PAD), f32),
            pltpu.VMEM((count, tiles, SUB, ratio * PAD), bf16),
        ],
        compiler_params=pltpu.CompilerParams(vmem_limit_bytes=56 * 2**20),
        cost_estimate=small_cost(),
        name=f"attention_backward_{heads[0]}",
    )(
        place, low, full, cosine, sine, start_row, inner, outer, jnp.swapaxes(inner, 1, 2),
        *[sums[h] for h in heads], *d_context, *context, qkv, *earlier,
    )


def fetch(me, where, deep, sources, target, sems):
    copies = []
    for n, (source, (j, first)) in enumerate(zip(sources, where, strict=True)):
        rows = source.shape[0]
        at = pl.ds(pl.multiple_of((me[0] ^ j) * deep + first, 16), rows)
        if source.shape[1] != target.shape[1]:
            source = source.at[:, : target.shape[1]]
        copies.append(pltpu.make_async_copy(source, target.at[at, :], sems.at[n]))
    return copies


def project_kernel(where, deep, more, me, gain, *refs):
    parts, refs = refs[:4], refs[4:]
    sources, refs = refs[: len(where)], refs[len(where) :]
    norm_all, qkv_all, weight, sems, rows_s = refs[2 if more else 0 :]
    i = pl.program_id(0)
    copies = fetch(me, where, deep, sources, weight, sems)

    @pl.when(i == 0)
    def first():
        for copy in copies:
            copy.start()

    for n, part in enumerate(parts):

        @pl.when(i == n)
        def take(part=part):
            rows_s[...] = part[...]

    x = rows_s[...].astype(jnp.float32)
    scale = lax.rsqrt(jnp.mean(x * x, axis=-1, keepdims=True) + EPSILON)
    norm_all[...] = (x * scale * gain[...]).astype(jnp.bfloat16)

    @pl.when(i == 0)
    def arrive():
        for copy in copies:
            copy.wait()

    qkv_all[...] = dot32(norm_all[...], weight[...]).astype(jnp.bfloat16)


def project_piece(k, pieces, me, gain, parts, blocks, cols, earlier):
    rows, width = parts[0].shape
    arrays, where, deep = blocks
    shapes = [(pieces * 4 * rows, width), (pieces * 4 * rows, cols)]

    def filled(i):
        return (k * 4 + i, 0)

    return pl.pallas_call(
        functools.partial(project_kernel, where, deep, bool(earlier)),
        grid=(4,),
        out_shape=[jax.ShapeDtypeStruct(shape, jnp.bfloat16) for shape in shapes],
        in_specs=[
            SMEM,
            pl.BlockSpec((1, width), lambda i: (0, 0)),
            *[pl.BlockSpec((rows, width), lambda i: (0, 0))] * 4,
            *[ANY] * (len(arrays) + len(earlier)),
        ],
        out_specs=[pl.BlockSpec((rows, shape[1]), filled) for shape in shapes],
        scratch_shapes=[
            pltpu.VMEM((width, cols), jnp.bfloat16),
            pltpu.SemaphoreType.DMA((len(arrays),)),
            pltpu.VMEM((rows, width), jnp.bfloat16),
        ],
        input_output_aliases={6 + len(arrays) + n: n for n in range(len(earlier))},
        compiler_params=pltpu.CompilerParams(vmem_limit_bytes=40 * 2**20),
        cost_estimate=small_cost(),
        name=f"project_{k}",
    )(me, gain, *parts, *arrays, *earlier)


def own_or_sibling(own, sibling, target):
    i, steps = pl.program_id(0), pl.num_programs(0)

    @pl.when(i < steps // 2)
    def from_own():
        target[...] = own[...]

    @pl.when(i >= steps // 2)
    def from_sibling():
        target[...] = sibling[...]


def gate_kernel(where, deep, more, me, own, sibling, *refs):
    gate_up, refs = refs[: len(where)], refs[len(where) :]
    norm_all, gate_up_all, hidden_all, weight, sems = refs[3 if more else 0 :]
    hidden_cols = hidden_all.shape[1]
    copies = fetch(me, where, deep, gate_up, weight, sems)

    @pl.when(pl.program_id(0) == 0)
    def first():
        for copy in copies:
            copy.start()
        for copy in copies:
            copy.wait()

    own_or_sibling(own, sibling, norm_all)
    x = norm_all[...]
    width = min(512, hidden_cols)
    for at in range(0, hidden_cols, width):
        gate_at = slice(at, at + width)
        up_at = slice(hidden_cols + at, hidden_cols + at + width)
        gate = dot32(x, weight[:, gate_at])
        up = dot32(x, weight[:, up_at])
        gate_up_all[:, gate_at] = gate
        gate_up_all[:, up_at] = up
        hidden_all[:, gate_at] = (gate * (1.0 / (1.0 + jnp.exp(-gate))) * up).astype(jnp.bfloat16)


def gate_back_kernel(where, deep, more, me, own, sibling, down, gate_up_all, *refs):
    gate_up, refs = refs[: len(where)], refs[len(where) :]
    grad_all, d_gate_up_all, d_norm_own, d_norm_sib, weight, sems = refs[2 if more else 0 :]
    hidden_cols = down.shape[1]
    copies = fetch(me, where, deep, gate_up, weight, sems)
    start = pl.program_id(0) == 0

    @pl.when(start)
    def first():
        for copy in copies:
            copy.start()

    own_or_sibling(own, sibling, grad_all)
    dy = grad_all[...]
    width = min(512, hidden_cols)
    for at in range(0, hidden_cols, width):
        gate_at = slice(at, at + width)
        up_at = slice(hidden_cols + at, hidden_cols + at + width)
        d_hidden = dot32(dy, down[:, gate_at])
        gate, up = gate_up_all[:, gate_at], gate_up_all[:, up_at]
        sigmoid = 1.0 / (1.0 + jnp.exp(-gate))
        d_gate = d_hidden * up * sigmoid * (1.0 + gate * (1.0 - sigmoid))
        d_gate_up_all[:, gate_at] = d_gate.astype(jnp.bfloat16)
        d_gate_up_all[:, up_at] = (d_hidden * (gate * sigmoid)).astype(jnp.bfloat16)

    @pl.when(start)
    def arrive():
        for copy in copies:
            copy.wait()

    d_norm = times_transpose(d_gate_up_all[...], weight[...]).astype(jnp.bfloat16)
    halfway = pl.num_programs(0) // 2

    @pl.when(pl.program_id(0) < halfway)
    def to_own():
        d_norm_own[...] = d_norm

    @pl.when(pl.program_id(0) >= halfway)
    def to_sibling():
        d_norm_sib[...] = d_norm


def piece_call(kernel, name, k, pieces, me, pair, whole, tiled, gate_up, earlier, outs):
    rows, width = pair[0].shape
    steps = 2 * rows // SUB
    arrays, where, deep = gate_up
    blocks = len(arrays)
    both_cols = arrays[0].shape[1]

    def own(i):
        return (jnp.minimum(i, steps // 2 - 1), 0)

    def sibling(i):
        return (jnp.maximum(i - steps // 2, 0), 0)

    def filled(i):
        return (k * steps + i, 0)

    maps = {"all": filled, "own": own, "sibling": sibling}
    first_earlier = 3 + len(whole) + len(tiled) + blocks
    return pl.pallas_call(
        functools.partial(kernel, where, deep, bool(earlier)),
        grid=(steps,),
        out_shape=[
            jax.ShapeDtypeStruct((pieces * 2 * rows if span == "all" else rows, cols), kind)
            for cols, kind, span in outs
        ],
        in_specs=[
            SMEM,
            pl.BlockSpec((SUB, width), own),
            pl.BlockSpec((SUB, width), sibling),
            *(pl.BlockSpec(x.shape, lambda i: (0, 0)) for x in whole),
            *(pl.BlockSpec((SUB, x.shape[1]), filled) for x in tiled),
            *[ANY] * (blocks + len(earlier)),
        ],
        out_specs=[
            pl.BlockSpec((SUB, cols), maps[span]) for cols, kind, span in outs
        ],
        scratch_shapes=[
            pltpu.VMEM((width, both_cols), jnp.bfloat16),
            pltpu.SemaphoreType.DMA((blocks,)),
        ],
        input_output_aliases={first_earlier + n: n for n in range(len(earlier))},
        compiler_params=pltpu.CompilerParams(vmem_limit_bytes=56 * 2**20),
        cost_estimate=small_cost(),
        name=f"{name}_{k}",
    )(me, *pair, *whole, *tiled, *arrays, *earlier)


def flip(x, axis):
    return lax.ppermute(x, axis, FLIP)


def swap(x):
    return lax.ppermute(x, ("core", "zh"), [(0, 0), (1, 2), (2, 1), (3, 3)])


def from_near(x, k):
    n = lax.axis_size("zl")
    return lax.ppermute(x, "zl", [((j + k) % n, j) for j in range(n)])


def to_near(x, k):
    n = lax.axis_size("zl")
    return lax.ppermute(x, "zl", [(j, (j + k) % n) for j in range(n)])


def across(x, j):
    n = lax.axis_size("yx")
    return lax.ppermute(x, "yx", [(a, a ^ j) for a in range(n)])


def cross_z(w):
    return cross_core(w, flip(w, "zh"))


def cross_core(w, far):
    core, zh = lax.axis_index("core"), lax.axis_index("zh")
    mine = jnp.where(core == zh, w, far)
    taken = flip(jnp.where(core == zh, far, w), "core")
    return jnp.concatenate(
        [jnp.where(core == 0, mine, taken), jnp.where(core == 0, taken, mine)], axis=0
    )


def neighbours(x):
    count = lax.axis_size("yx")
    return [across(x, j) for j in range(1, count if count != 4 else 3)]


def diagonal(taken):
    if lax.axis_size("yx") != 4:
        return []
    half = taken[0].shape[0] // 2
    return [across(taken[1][:half], 1), across(taken[0][half:], 2)]


def blocks_of(own, taken, halves):
    deep = own.shape[0]
    arrays = [own, *taken]
    where = [(j, 0) for j in range(len(arrays))]
    for n, half in enumerate(halves):
        arrays.append(half)
        where.append((3, n * deep // 2))
    return arrays, tuple(where), deep


def in_order(blocks, cols=slice(None)):
    arrays, where, deep = blocks
    arrays = [x[:, cols] for x in arrays]
    whole = jnp.zeros((sum(x.shape[0] for x in arrays), arrays[0].shape[1]), arrays[0].dtype)
    me = lax.axis_index("yx")
    for x, (j, first) in zip(arrays, where, strict=True):
        whole = lax.dynamic_update_slice_in_dim(whole, x, (me ^ j) * deep + first, 0)
    return whole


def block_of(grad, j):
    size = grad.shape[0] // lax.axis_size("yx")
    return lax.dynamic_slice_in_dim(grad, (lax.axis_index("yx") ^ j) * size, size, 0)


def send_yx(grad):
    count = lax.axis_size("yx")
    if count != 4:
        return [across(block_of(grad, j), j) for j in range(1, count)]
    far = block_of(grad, 3)
    half = far.shape[0] // 2
    return [across(far[:half], 1), across(far[half:], 2)]


def join_yx(grad, taken):
    if lax.axis_size("yx") != 4:
        return taken, block_of(grad, 0)
    half = taken[0].shape[0]
    one, two = block_of(grad, 1), block_of(grad, 2)
    one = jnp.concatenate([one[:half], one[half:] + taken[1]], axis=0)
    two = jnp.concatenate([two[:half] + taken[0], two[half:]], axis=0)
    return [across(one, 1), across(two, 2)], block_of(grad, 0)


def total_yx(taken, own):
    total = own.astype(jnp.float32)
    for part in taken:
        total = total + part.astype(jnp.float32)
    return total.astype(jnp.bfloat16)


def home_core(part):
    core, zh = lax.axis_index("core"), lax.axis_index("zh")
    half = part.shape[0] // 2
    upper, lower = part[:half], part[half:]
    mine = jnp.where(core == 0, upper, lower)
    taken = flip(jnp.where(core == 0, lower, upper), "core")
    return jnp.where(core == zh, mine, taken), jnp.where(core == zh, taken, mine)


def home(keep, give):
    return keep.astype(jnp.float32) + flip(give, "zh").astype(jnp.float32)


def body(
    tokens,
    cotangent,
    seq_lengths,
    attn_gain,
    q_weight,
    key_projection,
    value_projection,
    out_weight,
    mlp_gain,
    gate_weight,
    up_weight,
    down_weight,
):
    bf16, f32 = jnp.bfloat16, jnp.float32
    core, zl, yx = lax.axis_index("core"), lax.axis_index("zl"), lax.axis_index("yx")
    near = lax.axis_size("zl")
    others = range(1, near)
    rows = tokens.shape[0]
    group_rows = 2 * near * rows
    query_cols, key_cols = q_weight.shape[1], key_projection.shape[1]
    qkv_cols = query_cols + 2 * key_cols
    q_heads, kv_heads = query_cols // HD, key_cols // HD
    hidden_cols = gate_weight.shape[1]
    me = yx.astype(jnp.int32).reshape(1)

    qkv_shard = jnp.concatenate([q_weight, key_projection, value_projection], axis=1)
    gate_up_shard = jnp.concatenate([gate_weight, up_weight], axis=1)
    part_rows = rows // 2
    upper = swap(tokens[:part_rows])
    shard = jnp.concatenate([qkv_shard, out_weight], axis=1)
    shard_far = flip(shard, "zh")
    lengths = swap(seq_lengths)
    gains = lax.all_gather(jnp.stack([attn_gain, mlp_gain]), ("yx", "core"), axis=1, tiled=True).astype(f32)
    gain_one, gain_two = gains[0], gains[1]
    shard_far, upper, lengths, second_part = stage(shard_far, upper, lengths, tokens[part_rows:])

    lower = swap(second_part)
    upper_far = [from_near(upper, k) for k in others]
    pair = cross_core(shard, shard_far)
    taken = neighbours(pair)
    upper_sib = flip(upper, "core")

    subs = jnp.arange(group_rows // SUB, dtype=jnp.int32)
    per_device = rows // SUB
    source, within = subs // per_device, subs % per_device
    there_core, there_zl = (source % 2) ^ core, (source // 2 + zl) % near
    to_order = (there_core * near + there_zl) * per_device + within
    from_order = (((source % near - zl) % near) * 2 + ((source // near) ^ core)) * per_device + within
    place = jnp.concatenate([to_order, from_order])
    row_at, doc_start = document_layout(lengths, group_rows)
    cosine, sine = rotary_tables(row_at - doc_start)

    def bounds(size):
        tile_start = doc_start.reshape(-1, size)
        tile = jnp.arange(group_rows // size, dtype=jnp.int32)
        low = tile_start[:, 0] // size
        return low, jnp.minimum((tile_start[:, -1] + size - 1) // size, tile)

    start_row = jnp.tile(doc_start.reshape(-1, 1, SUB), (1, 1, q_heads // kv_heads))
    layout = (place, *bounds(TILE), cosine, sine, doc_start[:, None])
    layout_back = (place, *bounds(SUB), cosine, sine, start_row)
    lower, upper_sib, *moved = stage(lower, upper_sib, *upper_far, *taken, *layout, *layout_back)
    upper_far, moved = moved[: near - 1], moved[near - 1 :]
    taken, moved = moved[: len(taken)], moved[len(taken) :]
    layout, layout_back = moved[: len(layout)], moved[len(layout) :]

    lower_far = [from_near(lower, k) for k in others]
    lower_sib = flip(lower, "core")
    upper_far_sib = [flip(x, "core") for x in upper_far]
    blocks = blocks_of(pair, taken, diagonal(taken))
    gain_row = gain_one[None]
    normed = project_piece(0, near, me, gain_row, [upper, lower, upper_sib, lower_sib], blocks, qkv_cols, [])
    w_out_first = in_order(blocks, slice(qkv_cols, qkv_cols + query_cols))
    w_out_first, gate_up_shard, *moved = stage(w_out_first, gate_up_shard, *lower_far, *upper_far_sib, *normed)
    lower_far, upper_far_sib, normed = moved[: near - 1], moved[near - 1 : 2 * near - 2], moved[2 * near - 2 :]

    gate_up_far = flip(gate_up_shard, "zh")
    w_out_parts = [w_out_first] + [from_near(w_out_first, k) for k in others]
    for k in others:
        parts = [upper_far[k - 1], lower_far[k - 1], upper_far_sib[k - 1], flip(lower_far[k - 1], "core")]
        normed = project_piece(k, near, me, gain_row, parts, blocks, qkv_cols, normed)
    norm_one, qkv = normed
    context, sums = attend(qkv, near, layout, q_heads, kv_heads)
    gate_up_far, down_shard, *moved = stage(gate_up_far, down_weight, *context, *w_out_parts)
    context, w_out_parts = moved[:near], moved[near:]

    moved_context = [to_near(context[k], k) for k in others]
    down_far = flip(down_shard, "zh")
    gate_up_pair = cross_core(gate_up_shard, gate_up_far)
    gate_up_taken = neighbours(gate_up_pair)
    w_out_near = jnp.concatenate(w_out_parts, axis=1)
    w_out_sib = flip(w_out_near, "core")
    residual = jnp.concatenate([upper, lower], axis=0).astype(f32)
    scale_one = lax.rsqrt(jnp.mean(residual * residual, axis=-1, keepdims=True) + EPSILON)
    w_project = in_order(blocks, slice(0, qkv_cols))
    w_out_sib, w_project, scale_one, cotangent, *moved_context = stage(
        w_out_sib, w_project, scale_one, cotangent, *moved_context
    )

    own_cotangent = swap(cotangent)
    quarters = [context[0]] + [None] * (near - 1)
    for k in others:
        quarters[near - k] = moved_context[k - 1]
    own_context = jnp.concatenate([q[:rows] for q in quarters], axis=1)
    sib_context = flip(jnp.concatenate([q[rows:] for q in quarters], axis=1), "core")
    mid = residual + times_transpose(own_context, w_out_near) + times_transpose(sib_context, w_out_sib)
    scale_two, norm_two = norm_rows(mid, gain_two)
    norm_two, down_far, *gate_up_taken = stage(norm_two, down_far, *gate_up_taken)

    norm_far = [from_near(norm_two, k) for k in others]
    norm_sib = flip(norm_two, "core")
    gate_up = blocks_of(gate_up_pair, gate_up_taken, diagonal(gate_up_taken))
    down_pair = cross_core(down_shard, down_far)
    down_taken = neighbours(down_pair)
    outs = [(norm_two.shape[1], bf16, "all"), (2 * hidden_cols, f32, "all"), (hidden_cols, bf16, "all")]
    earlier = piece_call(gate_kernel, "gate", 0, near, me, [norm_two, norm_sib], [], [], gate_up, [], outs)
    own_cotangent, *moved = stage(own_cotangent, *norm_far, *down_taken, *earlier)
    norm_far, moved = moved[: near - 1], moved[near - 1 :]
    down_taken, earlier = moved[: len(down_taken)], moved[len(down_taken) :]

    cot_far = [from_near(own_cotangent, k) for k in others]
    cot_sib = flip(own_cotangent, "core")
    for k in others:
        far_pair = [norm_far[k - 1], flip(norm_far[k - 1], "core")]
        earlier = piece_call(gate_kernel, "gate", k, near, me, far_pair, [], [], gate_up, earlier, outs)
    norm_two_all, gate_up_all, hidden_all = earlier
    w_down = in_order(blocks_of(down_pair, down_taken, diagonal(down_taken)))

    def out_part(k):
        own, sib = (hidden_all[(2 * k + e) * rows : (2 * k + e + 1) * rows] for e in range(2))
        taken = flip(times_transpose(sib, w_down).astype(bf16), "core")
        return times_transpose(own, w_down) + taken.astype(f32)

    out_far = [out_part(k).astype(bf16) for k in others]
    outs = [(norm_two.shape[1], bf16, "all"), (2 * hidden_cols, bf16, "all")]
    outs += [(norm_two.shape[1], bf16, "own"), (norm_two.shape[1], bf16, "sibling")]
    grad_all, d_gate_up_all, *d_norm_near = piece_call(
        gate_back_kernel, "gate_back", 0, near, me, [own_cotangent, cot_sib], [w_down], [gate_up_all], gate_up, [], outs
    )
    grad_all, d_gate_up_all, hidden_all, *moved = stage(grad_all, d_gate_up_all, hidden_all, *d_norm_near, *cot_far, *out_far)
    d_norm_near, cot_far, out_far = moved[:2], moved[2 : near + 1], moved[near + 1 :]

    out_moved = [to_near(out_far[k - 1], k) for k in others]
    d_norm_sent = []
    for k in others:
        grad_all, d_gate_up_all, d_own, d_sib = piece_call(
            gate_back_kernel, "gate_back", k, near, me, [cot_far[k - 1], flip(cot_far[k - 1], "core")], [w_down],
            [gate_up_all], gate_up, [grad_all, d_gate_up_all], outs,
        )
        d_norm_sent.append((d_own.astype(f32) + flip(d_sib, "core").astype(f32)).astype(bf16))
    d_norm_two = d_norm_near[0].astype(f32) + flip(d_norm_near[1], "core").astype(f32)
    grad_all, d_gate_up_all, d_norm_two, *moved = stage(grad_all, d_gate_up_all, d_norm_two, *d_norm_sent, *out_moved)
    d_norm_sent, out_moved = moved[: near - 1], moved[near - 1 :]

    moved_upper = [to_near(d_norm_sent[k - 1][:part_rows], k) for k in others]
    grad_gate_up = rows_product(norm_two_all, d_gate_up_all).astype(bf16)
    grad_gate_up, grad_all, *moved = stage(grad_gate_up, grad_all, *moved_upper, *d_norm_sent)
    moved_upper, d_norm_sent = moved[: near - 1], moved[near - 1 :]

    moved_lower = [to_near(d_norm_sent[k - 1][part_rows:], k) for k in others]
    gate_up_part = lax.psum_scatter(grad_gate_up, "yx", scatter_dimension=0, tiled=True)
    grad_down = rows_product(grad_all, hidden_all).astype(bf16)
    output_own = mid + out_part(0)
    for part in out_moved:
        output_own = output_own + part.astype(f32)
    output_own = output_own.astype(bf16)
    output_own, grad_down, d_norm_two, *moved_lower = stage(output_own, grad_down, d_norm_two, *moved_lower)

    output = swap(output_own)
    down_part = lax.psum_scatter(grad_down, "yx", scatter_dimension=0, tiled=True)
    for one, two in zip(moved_upper, moved_lower, strict=True):
        d_norm_two = d_norm_two + jnp.concatenate([one, two], axis=0).astype(f32)
    mid_back, _ = norm_back(mid, scale_two, gain_two, d_norm_two)
    d_mid = own_cotangent.astype(f32) + mid_back
    d_attn = d_mid.astype(bf16)
    d_context_sib = flip(dot32(d_attn, w_out_sib).astype(bf16), "core")
    d_context_near = dot32(d_attn, w_out_near).astype(bf16)
    both = [
        jnp.concatenate(
            [d_context_near[:, k * query_cols : (k + 1) * query_cols],
             d_context_sib[:, k * query_cols : (k + 1) * query_cols]], axis=0)
        for k in range(near)
    ]
    d_attn, *both = stage(d_attn, *both)

    d_context = [both[0]] + [None] * (near - 1)
    for k in others:
        d_context[near - k] = to_near(both[k], k)
    grad_out_sib = flip(rows_product(d_attn, sib_context).astype(bf16), "core")
    grad_out = (rows_product(d_attn, own_context) + grad_out_sib.astype(f32)).astype(bf16)
    output, grad_out, *d_context = stage(output, grad_out, *d_context)

    grad_out_moved = [to_near(grad_out[:, k * query_cols : (k + 1) * query_cols], k) for k in others]
    d_qkv = attend_back([0], qkv, d_context, context, sums, [], layout_back, q_heads, kv_heads)
    d_qkv, gate_up_part, *grad_out_moved = stage(d_qkv, gate_up_part, *grad_out_moved)

    gate_up_keep, gate_up_give = home_core(gate_up_part)
    grad_out_quarter = grad_out[:, :query_cols].astype(f32)
    for part in grad_out_moved:
        grad_out_quarter = grad_out_quarter + part.astype(f32)
    grad_out_quarter = grad_out_quarter.astype(bf16)
    d_qkv, gate_up_give, grad_out_quarter = stage(d_qkv, gate_up_give, grad_out_quarter)
    gate_up_home = flip(gate_up_give, "zh")
    out_part_sum = lax.psum_scatter(grad_out_quarter, "yx", scatter_dimension=0, tiled=True)
    for head in range(1, kv_heads):
        d_qkv = attend_back([head], qkv, d_context, context, sums, [d_qkv], layout_back, q_heads, kv_heads)
    d_qkv, gate_up_home, down_part = stage(d_qkv, gate_up_home, down_part)

    def back_part(k):
        own, sib = (d_qkv[(2 * k + e) * rows : (2 * k + e + 1) * rows] for e in range(2))
        taken = flip(times_transpose(sib, w_project).astype(bf16), "core")
        return times_transpose(own, w_project) + taken.astype(f32)

    d_sent = [back_part(k).astype(bf16) for k in others]
    d_qkv, down_part, *d_sent = stage(d_qkv, down_part, *d_sent)

    d_upper = [to_near(d_sent[k - 1][:part_rows], k) for k in others]
    grad_project = rows_product(norm_one, d_qkv).astype(bf16)
    total = back_part(0)
    project_sent = send_yx(grad_project)
    down_keep, down_give = home_core(down_part)
    total, grad_project, down_give, *moved = stage(total, grad_project, down_give, *d_upper, *d_sent, *project_sent)
    d_upper, d_sent, project_sent = moved[: near - 1], moved[near - 1 : 2 * near - 2], moved[2 * near - 2 :]

    d_lower = [to_near(d_sent[k - 1][part_rows:], k) for k in others]
    project_moved, project_own = join_yx(grad_project, project_sent)

    def input_part(at, moved):
        part = total[at]
        for x in moved:
            part = part + x.astype(f32)
        back, _ = norm_back(residual[at], scale_one[at], gain_one, part)
        return (d_mid[at] + back).astype(bf16)

    input_upper = swap(input_part(slice(0, part_rows), d_upper))
    total, input_upper, out_part_sum, *moved = stage(total, input_upper, out_part_sum, *d_lower, *project_moved)
    d_lower, project_moved = moved[: near - 1], moved[near - 1 :]

    input_lower = swap(input_part(slice(part_rows, rows), d_lower))
    grad_project = home(*home_core(total_yx(project_moved, project_own)))
    grad_out = home(*home_core(out_part_sum))
    grad_gate_up = gate_up_keep.astype(f32) + gate_up_home.astype(f32)
    grad_down = down_keep.astype(f32) + flip(down_give, "zh").astype(f32)
    input_grad = jnp.concatenate([input_upper, input_lower], axis=0).astype(f32)
    gain_grads = lax.psum(
        jnp.stack(
            [
                jnp.sum(qkv_shard.astype(f32) * grad_project, axis=1),
                jnp.sum(gate_up_shard.astype(f32) * grad_gate_up, axis=1),
            ]
        ),
        ("zh", "zl"),
    ) / jnp.stack([attn_gain, mlp_gain]).astype(f32)
    return (
        output,
        input_grad,
        gain_grads[0],
        grad_project[:, :query_cols],
        grad_project[:, query_cols : query_cols + key_cols],
        grad_project[:, query_cols + key_cols :],
        grad_out,
        gain_grads[1],
        grad_gate_up[:, :hidden_cols],
        grad_gate_up[:, hidden_cols:],
        grad_down,
    )


def solution(mesh):
    dp, tensor = mesh.shape["dp"], mesh.shape["tensor"]
    fine = Mesh(mesh.devices.reshape(dp // 2, 2, 2, tensor // 2), AXES)
    by_rows, by_dp, by_both = P(AXES, None), P(("yx", "core")), P(("yx", "core"), ("zh", "zl"))
    return jax.shard_map(
        body,
        mesh=fine,
        in_specs=(
            by_rows, by_rows, P(("yx", "core"), None), by_dp, by_both, by_both, by_both, by_both,
            by_dp, by_both, by_both, by_both,
        ),
        out_specs=(
            by_rows, by_rows, by_dp, by_both, by_both, by_both, by_both, by_dp, by_both, by_both, by_both,
        ),
        check_vma=False,
    )
```

```python
import functools
import math

import jax
import jax.numpy as jnp
import numpy as np
from jax import lax
from jax.experimental import pallas as pl
from jax.experimental.pallas import tpu as pltpu
from jax.sharding import Mesh
from jax.sharding import PartitionSpec as P

HD = 96
HALF = HD // 2
PAD = 128
PARTS = 4
SUB = 256
TILE = 512

EPSILON = 1e-05
ROTARY_BASE = 100000.0
MASKED = -1e30
LOG2E = math.log2(math.e)

AXES = ("yx", "core", "zh", "zl")
FLIP = [(0, 1), (1, 0)]


def norm_rows(values, gain):
    row_scale = lax.rsqrt(jnp.mean(values * values, axis=-1, keepdims=True) + EPSILON)
    return (row_scale, (values * row_scale * gain).astype(jnp.bfloat16))


def norm_back(values, row_scale, gain, upstream):
    weighted = upstream * gain
    inner_sum = jnp.mean(weighted * values, axis=-1, keepdims=True)
    grad_in = row_scale * weighted - values * (row_scale * row_scale * row_scale) * inner_sum
    gain_part = jnp.sum(upstream * (values * row_scale), axis=0)
    return (grad_in, gain_part)


def document_layout(lengths, group_rows):
    flat_lengths = lengths.reshape(-1)
    doc_ends = jnp.cumsum(flat_lengths)
    rows = jnp.arange(group_rows, dtype=jnp.int32)
    passed = (rows[:, None] >= doc_ends[None, :]).astype(jnp.int32)
    return (rows, jnp.sum(passed * flat_lengths[None, :], axis=1))


def rotary_tables(positions):
    exponents = jnp.arange(HALF, dtype=jnp.float32) * (2.0 / HD)
    inverse = ROTARY_BASE ** (-exponents)
    angles = positions.astype(jnp.float32)[:, None] * inverse[None, :]
    cosine, sine = jnp.cos(angles), jnp.sin(angles)
    gap = jnp.zeros((positions.shape[0], PAD // 2 - HALF), jnp.float32)
    return (
        jnp.concatenate([cosine, gap, cosine, gap], axis=1),
        jnp.concatenate([-sine, gap, sine, gap], axis=1),
    )


def rows_product(left, right):
    return lax.dot_general(
        left, right, (((0,), (0,)), ((), ())), preferred_element_type=jnp.float32
    )


def times_transpose(left, right):
    return lax.dot_general(
        left, right, (((1,), (1,)), ((), ())), preferred_element_type=jnp.float32
    )


def dot32(left, right):
    return jnp.dot(left, right, preferred_element_type=jnp.float32)


def stage(*values):
    return lax.optimization_barrier(values)


def spread(columns, heads):
    matrix = np.zeros((columns, len(heads) * PAD), np.float32)
    for at, first in enumerate(heads):
        for half in range(2):
            for i in range(HALF):
                matrix[first + half * HALF + i, at * PAD + half * (PAD // 2) + i] = 1.0
    return matrix


def turn(x, cosine, sine):
    return x * cosine + pltpu.roll(x, PAD // 2, 1) * sine


def rows_at(t, size):
    return pl.ds(pl.multiple_of(t * size, size), size)


def forward_kernel(pieces, ratio, *refs):
    place, low, full, cosine, sine, start, spread_in, gather_out = refs[:8]
    heads = spread_in.shape[0]
    refs = refs[8:]
    qkv, context, refs = refs[0], refs[1 : 1 + pieces], refs[1 + pieces :]
    log_sum, refs = refs[:heads], refs[heads:]
    q_s, k_s, v_s, s_s, top_s, acc = refs
    tiles = q_s.shape[0]
    all_subs = qkv.shape[0] // SUB
    piece_subs = all_subs // pieces
    scale = LOG2E * HD ** (-0.5)
    ones_lane = lax.broadcasted_iota(jnp.int32, (SUB, PAD), 1) == PAD - 1

    def prepare(r, carry):
        t = place[r]
        at = rows_at(t, SUB)
        cos_t, sin_t = cosine[at, :], sine[at, :]
        tile, half = t // (TILE // SUB), t % (TILE // SUB)
        for g in range(heads):
            wide = dot32(qkv[rows_at(r, SUB), :], spread_in[g])
            for h in range(ratio):
                query = turn(wide[:, h * PAD : (h + 1) * PAD], cos_t, sin_t) * scale
                first = pl.multiple_of(h * TILE + half * SUB, SUB)
                q_s[tile, g, pl.ds(first, SUB), :] = query.astype(jnp.bfloat16)
            key = turn(wide[:, ratio * PAD : (ratio + 1) * PAD], cos_t, sin_t)
            k_s[g, at, :] = key.astype(jnp.bfloat16)
            value = jnp.where(ones_lane, 1.0, wide[:, (ratio + 1) * PAD :])
            v_s[g, at, :] = value.astype(jnp.bfloat16)
        return carry

    lax.fori_loop(0, all_subs, prepare, 0)

    def query_tile(i, carry):
        starts = jnp.concatenate([start[rows_at(i, TILE), :]] * ratio, axis=0)
        top_s[...] = jnp.full_like(top_s, MASKED)

        def scores(j, masked, diagonal):
            for g in range(heads):
                s = times_transpose(q_s[i, g], k_s[g, rows_at(j, TILE), :])
                if masked:
                    key_at = lax.broadcasted_iota(jnp.int32, s.shape, 1)
                    allowed = key_at + j * TILE >= starts
                    if diagonal:
                        query_at = lax.rem(lax.broadcasted_iota(jnp.int32, s.shape, 0), TILE)
                        allowed = allowed & (key_at <= query_at)
                    s = jnp.where(allowed, s, MASKED)
                s_s[g, j] = s
                peak = s[:, :PAD]
                for c in range(1, TILE // PAD):
                    peak = jnp.maximum(peak, s[:, c * PAD : (c + 1) * PAD])
                top_s[g] = jnp.maximum(top_s[g], peak)

        def loop(first, last, masked):
            def run(j, c):
                scores(j, masked, False)
                return c

            lax.fori_loop(first, last, run, 0)

        loop(low[i], full[i], True)
        loop(full[i], i, False)
        scores(i, True, True)
        tops = [jnp.max(top_s[g], axis=1, keepdims=True) for g in range(heads)]
        acc[...] = jnp.zeros_like(acc)

        def weigh(j, c):
            for g in range(heads):
                p = jnp.exp2(s_s[g, j] - tops[g]).astype(jnp.bfloat16)
                acc[g] += dot32(p, v_s[g, rows_at(j, TILE), :])
            return c

        lax.fori_loop(low[i], i + 1, weigh, 0)
        packed = None
        for g in range(heads):
            total = acc[g][:, PAD - 1 :]
            out = acc[g] * (1.0 / total)
            sums = jnp.broadcast_to(tops[g] + jnp.log(total) * LOG2E, (ratio * TILE, PAD))
            log_sum[g][i] = sums.T[:1, :]
            wide = jnp.concatenate(
                [out[h * TILE : (h + 1) * TILE, :] for h in range(ratio)], axis=1
            ).astype(jnp.bfloat16)
            part = dot32(wide, gather_out[g])
            packed = part if packed is None else packed + part
        subs = tiles * (TILE // SUB)
        for half in range(TILE // SUB):
            r = place[subs + i * (TILE // SUB) + half]
            part = packed[half * SUB : (half + 1) * SUB, :].astype(jnp.bfloat16)
            for k in range(pieces):

                @pl.when(r // piece_subs == k)
                def store(k=k, part=part, r=r):
                    context[k][rows_at(r % piece_subs, SUB), :] = part

        return carry

    lax.fori_loop(0, tiles, query_tile, 0)


def backward_kernel(pieces, ratio, more, *refs):
    place, low, full, cosine, sine, start, refs = *refs[:6], refs[6:]
    heads = refs[0].shape[0]
    spread_in, spread_out, gather_in, refs = *refs[:3], refs[3:]
    log_sum, refs = refs[:heads], refs[heads:]
    d_context, context, qkv, refs = refs[:pieces], refs[pieces : 2 * pieces], refs[2 * pieces], refs[2 * pieces + 1 :]
    earlier, refs = (refs[0], refs[1:]) if more else (None, refs)
    d_qkv, refs = refs[0], refs[1:]
    q_s, k_s, kt_s, v_s, do_s, delta_s, log_s, dq_acc, dk_acc, dv_acc, dq_s = refs
    tiles = q_s.shape[0]
    all_subs = qkv.shape[0] // SUB
    piece_subs = all_subs // pieces
    scale = HD ** (-0.5)
    per_tile = TILE // SUB

    for k in range(pieces):

        def prepare(r, carry, k=k):
            t = place[k * piece_subs + r]
            rel = rows_at(r, SUB)
            at = rows_at(t, SUB)
            cos_t, sin_t = cosine[at, :], sine[at, :]
            for g in range(heads):
                wide = dot32(qkv[rows_at(k * piece_subs + r, SUB), :], spread_in[g])
                d_out = dot32(d_context[k][rel, :], spread_out[g])
                out = dot32(context[k][rel, :], spread_out[g])
                for h in range(ratio):
                    cols = slice(h * PAD, (h + 1) * PAD)
                    rows = slice(h * SUB, (h + 1) * SUB)
                    query = turn(wide[:, cols], cos_t, sin_t) * (scale * LOG2E)
                    q_s[t, g, rows, :] = query.astype(jnp.bfloat16)
                    do_s[t, g, rows, :] = d_out[:, cols].astype(jnp.bfloat16)
                    delta = jnp.sum((d_out[:, cols] * out[:, cols]).T, axis=0, keepdims=True)
                    delta_s[t * heads + g, :, rows] = delta
                    first = pl.multiple_of(h * TILE + t % per_tile * SUB, SUB)
                    log_s[t * heads + g, :, rows] = log_sum[g][t // per_tile, :, pl.ds(first, SUB)]
                key = turn(wide[:, ratio * PAD : (ratio + 1) * PAD], cos_t, sin_t)
                k_s[g, t] = key.astype(jnp.bfloat16)
                kt_s[g, t] = key.T.astype(jnp.bfloat16)
                v_s[g, t] = wide[:, (ratio + 1) * PAD :].astype(jnp.bfloat16)
                dk_acc[g, t] = jnp.zeros((SUB, PAD), jnp.float32)
                dv_acc[g, t] = jnp.zeros((SUB, PAD), jnp.float32)
            return carry

        lax.fori_loop(0, piece_subs, prepare, 0)

    def query_tile(i, carry):
        dq_acc[...] = jnp.zeros_like(dq_acc)

        def step(j, masked, diagonal):
            for g in range(heads):
                queries, d_out = q_s[i, g], do_s[i, g]
                s = times_transpose(k_s[g, j], queries)
                if masked:
                    key_at = lax.broadcasted_iota(jnp.int32, s.shape, 0)
                    allowed = key_at + j * SUB >= start[i]
                    if diagonal:
                        query_at = lax.rem(lax.broadcasted_iota(jnp.int32, s.shape, 1), SUB)
                        allowed = allowed & (key_at <= query_at)
                    s = jnp.where(allowed, s, MASKED)
                p = jnp.exp2(s - log_s[i * heads + g])
                d_p = times_transpose(v_s[g, j], d_out)
                d_s = (p * (d_p - delta_s[i * heads + g])).astype(jnp.bfloat16)
                dv_acc[g, j] += dot32(p.astype(jnp.bfloat16), d_out)
                dk_acc[g, j] += dot32(d_s, queries)
                dq_acc[g] += dot32(kt_s[g, j], d_s)

        def loop(first, last, masked):
            def run(j, c):
                step(j, masked, False)
                return c

            lax.fori_loop(first, last, run, 0)

        loop(low[i], full[i], True)
        loop(full[i], i, False)
        step(i, True, True)
        at = rows_at(i, SUB)
        cos_t, sin_t = cosine[at, :], sine[at, :]
        for g in range(heads):
            grad = dq_acc[g].T * scale
            for h in range(ratio):
                piece = turn(grad[h * SUB : (h + 1) * SUB, :], cos_t, -sin_t)
                dq_s[g, i, :, h * PAD : (h + 1) * PAD] = piece.astype(jnp.bfloat16)
        return carry

    lax.fori_loop(0, tiles, query_tile, 0)

    def finish(r, carry):
        t = place[r]
        at = rows_at(t, SUB)
        rel = rows_at(r, SUB)
        packed = None
        for g in range(heads):
            key = turn(dk_acc[g, t] * (1.0 / LOG2E), cosine[at, :], -sine[at, :])
            wide = jnp.concatenate(
                [dq_s[g, t], key.astype(jnp.bfloat16), dv_acc[g, t].astype(jnp.bfloat16)], axis=1
            )
            part = dot32(wide, gather_in[g])
            packed = part if packed is None else packed + part
        packed = packed.astype(jnp.bfloat16)
        d_qkv[rel, :] = packed + earlier[rel, :] if more else packed
        return carry

    lax.fori_loop(0, all_subs, finish, 0)


SMEM = pl.BlockSpec(memory_space=pltpu.SMEM)
VMEM = pl.BlockSpec(memory_space=pltpu.VMEM)
ANY = pl.BlockSpec(memory_space=pl.ANY)


def small_cost(transcendentals=0):
    return pl.CostEstimate(flops=1 << 20, bytes_accessed=1 << 16, transcendentals=transcendentals)


def head_matrices(head, q_heads, kv_heads):
    ratio = q_heads // kv_heads
    queries = [(head * ratio + r) * HD for r in range(ratio)]
    key, value = (q_heads + head) * HD, (q_heads + kv_heads + head) * HD
    inner = spread((q_heads + 2 * kv_heads) * HD, [*queries, key, value])
    outer = spread(q_heads * HD, queries)
    return jnp.asarray(inner, jnp.bfloat16), jnp.asarray(outer, jnp.bfloat16)


def stacked_matrices(q_heads, kv_heads):
    pairs = [head_matrices(head, q_heads, kv_heads) for head in range(kv_heads)]
    return jnp.stack([inner for inner, _ in pairs]), jnp.stack([outer for _, outer in pairs])


def attend(qkv, pieces, layout, q_heads, kv_heads):
    place, low, full, cosine, sine, start_column = layout
    ratio, rows = q_heads // kv_heads, qkv.shape[0]
    tiles, lanes = rows // TILE, ratio * TILE
    bf16, f32 = jnp.bfloat16, jnp.float32
    inner, outer = stacked_matrices(q_heads, kv_heads)
    outs = pl.pallas_call(
        functools.partial(forward_kernel, pieces, ratio),
        out_shape=[
            *[jax.ShapeDtypeStruct((rows // pieces, q_heads * HD), bf16)] * pieces,
            *[jax.ShapeDtypeStruct((tiles, 1, lanes), f32)] * kv_heads,
        ],
        in_specs=[SMEM] * 3 + [VMEM] * 6,
        out_specs=[VMEM] * (pieces + kv_heads),
        scratch_shapes=[
            pltpu.VMEM((tiles, kv_heads, lanes, PAD), bf16),
            pltpu.VMEM((kv_heads, rows, PAD), bf16),
            pltpu.VMEM((kv_heads, rows, PAD), bf16),
            pltpu.VMEM((kv_heads, tiles, lanes, TILE), f32),
            pltpu.VMEM((kv_heads, lanes, PAD), f32),
            pltpu.VMEM((kv_heads, lanes, PAD), f32),
        ],
        compiler_params=pltpu.CompilerParams(vmem_limit_bytes=60 * 2**20),
        cost_estimate=small_cost(),
        name="attention_forward",
    )(place, low, full, cosine, sine, start_column, inner, jnp.swapaxes(outer, 1, 2), qkv)
    return outs[:pieces], outs[pieces:]


def attend_back(heads, qkv, d_context, context, sums, earlier, layout, q_heads, kv_heads):
    place, low, full, cosine, sine, start_row = layout
    pieces, ratio, rows = len(context), q_heads // kv_heads, qkv.shape[0]
    tiles, lanes, count = rows // SUB, ratio * SUB, len(heads)
    bf16, f32 = jnp.bfloat16, jnp.float32
    inner, outer = stacked_matrices(q_heads, kv_heads)
    inner, outer = inner[heads[0] : heads[0] + count], outer[heads[0] : heads[0] + count]
    return pl.pallas_call(
        functools.partial(backward_kernel, pieces, ratio, bool(earlier)),
        out_shape=jax.ShapeDtypeStruct(qkv.shape, bf16),
        in_specs=[SMEM] * 3 + [VMEM] * (7 + count + 2 * pieces + len(earlier)),
        out_specs=VMEM,
        scratch_shapes=[
            pltpu.VMEM((tiles, count, lanes, PAD), bf16),
            pltpu.VMEM((count, tiles, SUB, PAD), bf16),
            pltpu.VMEM((count, tiles, PAD, SUB), bf16),
            pltpu.VMEM((count, tiles, SUB, PAD), bf16),
            pltpu.VMEM((tiles, count, lanes, PAD), bf16),
            pltpu.VMEM((tiles * count, 1, lanes), f32),
            pltpu.VMEM((tiles * count, 1, lanes), f32),
            pltpu.VMEM((count, PAD, lanes), f32),
            pltpu.VMEM((count, tiles, SUB, PAD), f32),
            pltpu.VMEM((count, tiles, SUB, PAD), f32),
            pltpu.VMEM((count, tiles, SUB, ratio * PAD), bf16),
        ],
        compiler_params=pltpu.CompilerParams(vmem_limit_bytes=60 * 2**20),
        cost_estimate=small_cost(),
        name=f"attention_backward_{heads[0]}",
    )(
        place, low, full, cosine, sine, start_row, inner, outer, jnp.swapaxes(inner, 1, 2),
        *[sums[h] for h in heads], *d_context, *context, qkv, *earlier,
    )


def fetch(me, where, deep, sources, target, sems):
    copies = []
    for n, (source, (j, first)) in enumerate(zip(sources, where, strict=True)):
        rows = source.shape[0]
        at = pl.ds(pl.multiple_of((me[0] ^ j) * deep + first, 16), rows)
        if source.shape[1] != target.shape[1]:
            source = source.at[:, : target.shape[1]]
        copies.append(pltpu.make_async_copy(source, target.at[at, :], sems.at[n]))
    return copies


def project_kernel(where, deep, more, me, *refs):
    parts, gain, refs = refs[:PARTS], refs[PARTS], refs[PARTS + 1 :]
    sources, refs = refs[: len(where)], refs[len(where) :]
    norm_all, qkv_all, weight, sems, rows_s = refs[2 if more else 0 :]
    i = pl.program_id(0)
    copies = fetch(me, where, deep, sources, weight, sems)

    @pl.when(i == 0)
    def first():
        for copy in copies:
            copy.start()

    take_part(parts, rows_s)
    x = rows_s[...].astype(jnp.float32)
    scale = lax.rsqrt(jnp.mean(x * x, axis=-1, keepdims=True) + EPSILON)
    norm_all[...] = (x * scale * gain[...]).astype(jnp.bfloat16)

    @pl.when(i == 0)
    def arrive():
        for copy in copies:
            copy.wait()

    qkv_all[...] = dot32(norm_all[...], weight[...]).astype(jnp.bfloat16)


def take_part(parts, target):
    for n, part in enumerate(parts):

        @pl.when(pl.program_id(0) == n)
        def take(part=part):
            target[...] = part[...]


def gate_kernel(where, deep, more, me, *refs):
    parts, refs = refs[:PARTS], refs[PARTS:]
    gate_up, refs = refs[: len(where)], refs[len(where) :]
    norm_all, gate_up_all, hidden_all, weight, sems = refs[3 if more else 0 :]
    hidden_cols = hidden_all.shape[1]
    copies = fetch(me, where, deep, gate_up, weight, sems)

    @pl.when(pl.program_id(0) == 0)
    def first():
        for copy in copies:
            copy.start()
        for copy in copies:
            copy.wait()

    take_part(parts, norm_all)
    x = norm_all[...]
    width = min(512, hidden_cols)
    for at in range(0, hidden_cols, width):
        gate_at = slice(at, at + width)
        up_at = slice(hidden_cols + at, hidden_cols + at + width)
        gate = dot32(x, weight[:, gate_at])
        up = dot32(x, weight[:, up_at])
        gate_up_all[:, gate_at] = gate
        gate_up_all[:, up_at] = up
        hidden_all[:, gate_at] = (gate * (1.0 / (1.0 + jnp.exp(-gate))) * up).astype(jnp.bfloat16)


def gate_back_kernel(where, deep, more, me, *refs):
    parts, down, gate_up_all, hidden_all, refs = refs[:PARTS], *refs[PARTS : PARTS + 3], refs[PARTS + 3 :]
    gate_up, refs = refs[: len(where)], refs[len(where) :]
    grad_all, d_gate_up_all, d_norm_own, d_norm_sib, out_own, out_sib, weight, sems = refs[2 if more else 0 :]
    hidden_cols = down.shape[1]
    copies = fetch(me, where, deep, gate_up, weight, sems)
    i = pl.program_id(0)

    @pl.when(i == 0)
    def first():
        for copy in copies:
            copy.start()

    take_part(parts, grad_all)
    dy = grad_all[...]
    width = min(512, hidden_cols)
    for at in range(0, hidden_cols, width):
        gate_at = slice(at, at + width)
        up_at = slice(hidden_cols + at, hidden_cols + at + width)
        d_hidden = dot32(dy, down[:, gate_at])
        gate, up = gate_up_all[:, gate_at], gate_up_all[:, up_at]
        sigmoid = 1.0 / (1.0 + jnp.exp(-gate))
        d_gate = d_hidden * up * sigmoid * (1.0 + gate * (1.0 - sigmoid))
        d_gate_up_all[:, gate_at] = d_gate.astype(jnp.bfloat16)
        d_gate_up_all[:, up_at] = (d_hidden * (gate * sigmoid)).astype(jnp.bfloat16)
    out = times_transpose(hidden_all[...], down[...]).astype(jnp.bfloat16)

    @pl.when(i == 0)
    def arrive():
        for copy in copies:
            copy.wait()

    d_norm = times_transpose(d_gate_up_all[...], weight[...]).astype(jnp.bfloat16)

    @pl.when(i < PARTS // 2)
    def to_own():
        d_norm_own[...] = d_norm
        out_own[...] = out

    @pl.when(i >= PARTS // 2)
    def to_sibling():
        d_norm_sib[...] = d_norm
        out_sib[...] = out


def piece_call(kernel, name, k, pieces, me, parts, whole, tiled, blocks, cols, earlier, outs):
    arrays, where, deep = blocks
    width = parts[0][0].shape[1]
    tile = min(x.shape[0] // (1 + max(b for y, b in parts if y is x)) for x, _ in parts)
    own_rows = tile * PARTS // 2
    maps = {
        "all": lambda i: (k * PARTS + i, 0),
        "own": lambda i: (jnp.minimum(i, PARTS // 2 - 1), 0),
        "sibling": lambda i: (jnp.maximum(i - PARTS // 2, 0), 0),
    }

    def at_block(block):
        return lambda i: (block, 0)

    first_earlier = 1 + PARTS + len(whole) + len(tiled) + len(arrays)
    return pl.pallas_call(
        functools.partial(kernel, where, deep, bool(earlier)),
        grid=(PARTS,),
        out_shape=[
            jax.ShapeDtypeStruct((pieces * 2 * own_rows if span == "all" else own_rows, columns), kind)
            for columns, kind, span in outs
        ],
        in_specs=[
            SMEM,
            *(pl.BlockSpec((tile, width), at_block(block)) for _, block in parts),
            *(pl.BlockSpec(x.shape, lambda i: (0, 0)) for x in whole),
            *(pl.BlockSpec((tile, x.shape[1]), maps["all"]) for x in tiled),
            *[ANY] * (len(arrays) + len(earlier)),
        ],
        out_specs=[pl.BlockSpec((tile, columns), maps[span]) for columns, kind, span in outs],
        scratch_shapes=[
            pltpu.VMEM((width, cols), jnp.bfloat16),
            pltpu.SemaphoreType.DMA((len(arrays),)),
            *([pltpu.VMEM((tile, width), jnp.bfloat16)] if kernel is project_kernel else []),
        ],
        input_output_aliases={first_earlier + n: n for n in range(len(earlier))},
        compiler_params=pltpu.CompilerParams(vmem_limit_bytes=60 * 2**20),
        cost_estimate=small_cost(),
        name=f"{name}_{k}",
    )(me, *(x for x, _ in parts), *whole, *tiled, *arrays, *earlier)


def flip(x, axis):
    return lax.ppermute(x, axis, FLIP)


CROSS = [(1, 2), (2, 1)]
OUT = [(0, 1), (3, 2), (2, 0), (1, 3)]
BACK = [(1, 0), (2, 3), (0, 2), (3, 1)]


def crossed(x, perm):
    return lax.ppermute(x, ("core", "zh"), perm)


def straight():
    return lax.axis_index("core") == lax.axis_index("zh")


def swap(x):
    return jnp.where(straight(), x, crossed(x, CROSS))


def send_z(w):
    return crossed(w, OUT), crossed(w, CROSS)


def pair_of(w, out, cross):
    zh = lax.axis_index("zh")
    x = jnp.where(straight(), w, cross)
    return jnp.concatenate([jnp.where(zh == 0, x, out), jnp.where(zh == 0, out, x)], axis=0)


def give_z(part):
    zh = lax.axis_index("zh")
    half = part.shape[0] // 2
    upper, lower = part[:half], part[half:]
    return jnp.where(zh == 0, upper, lower), jnp.where(zh == 0, lower, upper)


def sum_z(keep, back, cross):
    return back.astype(jnp.float32) + jnp.where(straight(), keep, cross).astype(jnp.float32)


def shift(x, e, k):
    n = lax.axis_size("zl")
    return lax.ppermute(
        x, ("core", "zl"), [(c * n + l, (c ^ e) * n + (l + k) % n) for c in range(2) for l in range(n)]
    )


def from_near(x, k):
    n = lax.axis_size("zl")
    return lax.ppermute(x, "zl", [((j + k) % n, j) for j in range(n)])


def to_near(x, k):
    n = lax.axis_size("zl")
    return lax.ppermute(x, "zl", [(j, (j + k) % n) for j in range(n)])


def across(x, j):
    n = lax.axis_size("yx")
    return lax.ppermute(x, "yx", [(a, a ^ j) for a in range(n)])


def neighbours(x):
    count = lax.axis_size("yx")
    return [across(x, j) for j in range(1, count if count != 4 else 3)]


def diagonal(taken):
    if lax.axis_size("yx") != 4:
        return []
    half = taken[0].shape[0] // 2
    return [across(taken[1][:half], 1), across(taken[0][half:], 2)]


def blocks_of(own, taken, halves):
    deep = own.shape[0]
    arrays = [own, *taken]
    where = [(j, 0) for j in range(len(arrays))]
    for n, half in enumerate(halves):
        arrays.append(half)
        where.append((3, n * deep // 2))
    return arrays, tuple(where), deep


def in_order(blocks, cols=slice(None)):
    arrays, where, deep = blocks
    arrays = [x[:, cols] for x in arrays]
    whole = jnp.zeros((sum(x.shape[0] for x in arrays), arrays[0].shape[1]), arrays[0].dtype)
    me = lax.axis_index("yx")
    for x, (j, first) in zip(arrays, where, strict=True):
        whole = lax.dynamic_update_slice_in_dim(whole, x, (me ^ j) * deep + first, 0)
    return whole


def block_of(grad, j):
    size = grad.shape[0] // lax.axis_size("yx")
    return lax.dynamic_slice_in_dim(grad, (lax.axis_index("yx") ^ j) * size, size, 0)


def send_yx(grad):
    count = lax.axis_size("yx")
    if count != 4:
        return [across(block_of(grad, j), j) for j in range(1, count)]
    far = block_of(grad, 3)
    half = far.shape[0] // 2
    return [across(far[:half], 1), across(far[half:], 2)]


def join_yx(grad, taken):
    if lax.axis_size("yx") != 4:
        return taken, block_of(grad, 0)
    half = taken[0].shape[0]
    one, two = block_of(grad, 1), block_of(grad, 2)
    one = jnp.concatenate([one[:half], one[half:] + taken[1]], axis=0)
    two = jnp.concatenate([two[:half] + taken[0], two[half:]], axis=0)
    return [across(one, 1), across(two, 2)], block_of(grad, 0)


def total_yx(taken, own):
    total = own.astype(jnp.float32)
    for part in taken:
        total = total + part.astype(jnp.float32)
    return total.astype(jnp.bfloat16)


def body(
    tokens,
    cotangent,
    seq_lengths,
    attn_gain,
    q_weight,
    key_projection,
    value_projection,
    out_weight,
    mlp_gain,
    gate_weight,
    up_weight,
    down_weight,
):
    bf16, f32 = jnp.bfloat16, jnp.float32
    core, zl, yx = lax.axis_index("core"), lax.axis_index("zl"), lax.axis_index("yx")
    near = lax.axis_size("zl")
    others = range(1, near)
    rows = tokens.shape[0]
    group_rows = 2 * near * rows
    query_cols, key_cols = q_weight.shape[1], key_projection.shape[1]
    qkv_cols = query_cols + 2 * key_cols
    q_heads, kv_heads = query_cols // HD, key_cols // HD
    hidden_cols = gate_weight.shape[1]
    me = yx.astype(jnp.int32).reshape(1)

    qkv_shard = jnp.concatenate([q_weight, key_projection, value_projection], axis=1)
    gate_up_shard = jnp.concatenate([gate_weight, up_weight], axis=1)
    part_rows = rows // 2
    upper = swap(tokens[:part_rows])
    shard = jnp.concatenate([qkv_shard, out_weight], axis=1)
    shard_moved = send_z(shard)
    lengths = swap(seq_lengths)
    gains = lax.all_gather(jnp.stack([attn_gain, mlp_gain]), ("yx", "core"), axis=1, tiled=True).astype(f32)
    gain_one, gain_two = gains[0], gains[1]
    upper, lengths, second_part, *shard_moved = stage(upper, lengths, tokens[part_rows:], *shard_moved)

    upper_far = [from_near(upper, k) for k in others]
    lower = swap(second_part)
    pair = pair_of(shard, *shard_moved)
    taken = neighbours(pair)
    upper_sib = flip(upper, "core")

    subs = jnp.arange(group_rows // SUB, dtype=jnp.int32)
    per_device = rows // SUB
    source, within = subs // per_device, subs % per_device
    there_core, there_zl = (source % 2) ^ core, (source // 2 + zl) % near
    to_order = (there_core * near + there_zl) * per_device + within
    from_order = (((source % near - zl) % near) * 2 + ((source // near) ^ core)) * per_device + within
    place = jnp.concatenate([to_order, from_order])
    row_at, doc_start = document_layout(lengths, group_rows)
    cosine, sine = rotary_tables(row_at - doc_start)

    def bounds(size):
        tile_start = doc_start.reshape(-1, size)
        tile = jnp.arange(group_rows // size, dtype=jnp.int32)
        low = tile_start[:, 0] // size
        return low, jnp.minimum((tile_start[:, -1] + size - 1) // size, tile)

    start_row = jnp.tile(doc_start.reshape(-1, 1, SUB), (1, 1, q_heads // kv_heads))
    layout = (place, *bounds(TILE), cosine, sine, doc_start[:, None])
    layout_back = (place, *bounds(SUB), cosine, sine, start_row)
    lower, upper_sib, *moved = stage(lower, upper_sib, *upper_far, *taken, *layout, *layout_back)
    upper_far, moved = moved[: near - 1], moved[near - 1 :]
    taken, moved = moved[: len(taken)], moved[len(taken) :]
    layout, layout_back = moved[: len(layout)], moved[len(layout) :]

    lower_far = [from_near(lower, k) for k in others]
    lower_sib = flip(lower, "core")
    upper_far_sib = [flip(x, "core") for x in upper_far]
    blocks = blocks_of(pair, taken, diagonal(taken))
    gain_row = gain_one[None]
    outs = [(tokens.shape[1], bf16, "all"), (qkv_cols, bf16, "all")]
    parts = [(upper, 0), (lower, 0), (upper_sib, 0), (lower_sib, 0)]
    normed = piece_call(project_kernel, "project", 0, near, me, parts, [gain_row], [], blocks, qkv_cols, [], outs)
    gate_up_shard, *moved = stage(gate_up_shard, *lower_far, *upper_far_sib, *normed)
    lower_far, upper_far_sib, normed = moved[: near - 1], moved[near - 1 : 2 * near - 2], moved[2 * near - 2 :]

    out_pair = pair[:, qkv_cols:]
    out_far = [from_near(out_pair, k) for k in others]
    for k in others:
        parts = [(x, 0) for x in (upper_far[k - 1], lower_far[k - 1], upper_far_sib[k - 1], flip(lower_far[k - 1], "core"))]
        normed = piece_call(
            project_kernel, "project", k, near, me, parts, [gain_row], [], blocks, qkv_cols, normed, outs
        )
    norm_one, qkv = normed
    gate_up_shard, qkv, *out_far = stage(gate_up_shard, qkv, *out_far)

    gate_up_moved = send_z(gate_up_shard)
    out_taken = [x for far in out_far for x in neighbours(far)]
    context, sums = attend(qkv, 2 * near, layout, q_heads, kv_heads)
    down_shard, *moved = stage(down_weight, *context, *gate_up_moved, *out_taken)
    context, gate_up_moved, out_taken = moved[: 2 * near], moved[2 * near : 2 * near + 2], moved[2 * near + 2 :]

    quarters = {(0, 0): context[0]}
    for k in range(near):
        for e in range(2):
            if (e, k) != (0, 0):
                quarters[e, (near - k) % near] = shift(context[2 * k + e], e, k)
    gate_up_pair = pair_of(gate_up_shard, *gate_up_moved)
    gate_up_taken = neighbours(gate_up_pair)
    down_moved = send_z(down_shard)
    count = len(out_taken) // max(near - 1, 1)
    out_takens = [out_taken[n * count : (n + 1) * count] for n in range(near - 1)]
    w_out_near = jnp.concatenate(
        [
            in_order(blocks, slice(qkv_cols, qkv_cols + query_cols)),
            *(in_order(blocks_of(x, t, diagonal(t))) for x, t in zip(out_far, out_takens, strict=True)),
        ],
        axis=1,
    )
    w_out_sib = flip(w_out_near, "core")
    residual = jnp.concatenate([upper, lower], axis=0).astype(f32)
    scale_one = lax.rsqrt(jnp.mean(residual * residual, axis=-1, keepdims=True) + EPSILON)
    order = [(e, k) for e in range(2) for k in range(near)]
    w_project = in_order(blocks, slice(0, qkv_cols))
    w_out_sib, w_out_near, scale_one, w_project, *moved = stage(
        w_out_sib, w_out_near, scale_one, w_project, *[quarters[at] for at in order], *down_moved
    )
    quarters, down_moved = moved[: 2 * near], moved[2 * near :]

    own_context = jnp.concatenate(quarters[:near], axis=1)
    sib_context = jnp.concatenate(quarters[near:], axis=1)
    mid = residual + times_transpose(own_context, w_out_near) + times_transpose(sib_context, w_out_sib)
    scale_two, norm_two = norm_rows(mid, gain_two)
    norm_upper, norm_lower, cotangent, *gate_up_taken = stage(
        norm_two[:part_rows], norm_two[part_rows:], cotangent, *gate_up_taken
    )

    upper_far = [from_near(norm_upper, k) for k in others]
    upper_sib, lower_sib = flip(norm_upper, "core"), flip(norm_lower, "core")
    gate_up = blocks_of(gate_up_pair, gate_up_taken, diagonal(gate_up_taken))
    cot_upper = swap(cotangent[:part_rows])
    halves = gate_up[0][len(gate_up_taken) + 1 :]
    cot_upper, upper_sib, lower_sib, *moved = stage(cot_upper, upper_sib, lower_sib, *upper_far, *halves)
    upper_far, halves = moved[: near - 1], moved[near - 1 :]
    gate_up = ([gate_up_pair, *gate_up_taken, *halves], *gate_up[1:])

    lower_far = [from_near(norm_lower, k) for k in others]
    upper_far_sib = [flip(x, "core") for x in upper_far]
    cot_lower = swap(cotangent[part_rows:])
    cot_upper_sib = flip(cot_upper, "core")
    down_pair = pair_of(down_shard, *down_moved)
    down_taken = neighbours(down_pair)
    outs = [(norm_two.shape[1], bf16, "all"), (2 * hidden_cols, f32, "all"), (hidden_cols, bf16, "all")]
    parts = [(norm_upper, 0), (norm_lower, 0), (upper_sib, 0), (lower_sib, 0)]
    earlier = piece_call(gate_kernel, "gate", 0, near, me, parts, [], [], gate_up, 2 * hidden_cols, [], outs)
    cot_lower, cot_upper_sib, *moved = stage(
        cot_lower, cot_upper_sib, *lower_far, *upper_far_sib, *down_taken, *earlier
    )
    lower_far, upper_far_sib, moved = moved[: near - 1], moved[near - 1 : 2 * near - 2], moved[2 * near - 2 :]
    down_taken, earlier = moved[: len(down_taken)], moved[len(down_taken) :]

    cot_upper_far = [from_near(cot_upper, k) for k in others]
    cot_lower_sib = flip(cot_lower, "core")
    down_halves = diagonal(down_taken)
    for k in others:
        parts = [(x, 0) for x in (upper_far[k - 1], lower_far[k - 1], upper_far_sib[k - 1], flip(lower_far[k - 1], "core"))]
        earlier = piece_call(gate_kernel, "gate", k, near, me, parts, [], [], gate_up, 2 * hidden_cols, earlier, outs)
    cot_lower, cot_lower_sib, *moved = stage(cot_lower, cot_lower_sib, *cot_upper_far, *earlier, *down_halves)
    cot_upper_far, earlier, down_halves = moved[: near - 1], moved[near - 1 : near + 2], moved[near + 2 :]
    norm_two_all, gate_up_all, hidden_all = earlier

    cot_lower_far = [from_near(cot_lower, k) for k in others]
    cot_upper_far_sib = [flip(x, "core") for x in cot_upper_far]
    w_down = in_order(blocks_of(down_pair, down_taken, down_halves))
    width = norm_two.shape[1]
    outs = [(width, bf16, "all"), (2 * hidden_cols, bf16, "all")]
    outs += [(width, bf16, "own"), (width, bf16, "sibling")] * 2

    def way_back(k, parts, earlier):
        return piece_call(
            gate_back_kernel, "gate_back", k, near, me, [(x, 0) for x in parts], [w_down], [gate_up_all, hidden_all],
            gate_up, 2 * hidden_cols, earlier, outs,
        )

    grad_all, d_gate_up_all, *near_back = way_back(0, (cot_upper, cot_lower, cot_upper_sib, cot_lower_sib), [])
    grad_all, d_gate_up_all, *moved = stage(
        grad_all, d_gate_up_all, *near_back, *cot_lower_far, *cot_upper_far_sib
    )
    near_back, cot_lower_far, cot_upper_far_sib = moved[:4], moved[4 : near + 3], moved[near + 3 :]

    far_back = []
    for k in others:
        parts = (cot_upper_far[k - 1], cot_lower_far[k - 1], cot_upper_far_sib[k - 1], flip(cot_lower_far[k - 1], "core"))
        grad_all, d_gate_up_all, *back = way_back(k, parts, [grad_all, d_gate_up_all])
        far_back += back
    grad_all, d_gate_up_all, *far_back = stage(grad_all, d_gate_up_all, *far_back)

    def joined(own, sib):
        return own.astype(f32) + flip(sib, "core").astype(f32)

    d_norm_sent = [joined(*far_back[4 * n : 4 * n + 2]).astype(bf16) for n in range(near - 1)]
    grad_all, d_gate_up_all, *d_norm_sent = stage(grad_all, d_gate_up_all, *d_norm_sent)

    moved_upper = [to_near(d_norm_sent[k - 1][:part_rows], k) for k in others]
    grad_gate_up = rows_product(norm_two_all, d_gate_up_all).astype(bf16)
    grad_gate_up, grad_all, *moved = stage(grad_gate_up, grad_all, *moved_upper, *d_norm_sent)
    moved_upper, d_norm_sent = moved[: near - 1], moved[near - 1 :]

    moved_lower = [to_near(d_norm_sent[k - 1][part_rows:], k) for k in others]
    gate_up_sent = send_yx(grad_gate_up)
    d_norm_two = joined(*near_back[:2])
    out_far = [joined(*far_back[4 * n + 2 : 4 * n + 4]).astype(bf16) for n in range(near - 1)]
    grad_down = rows_product(grad_all, hidden_all).astype(bf16)
    grad_down, d_norm_two, *moved = stage(grad_down, d_norm_two, *moved_lower, *gate_up_sent, *out_far)
    moved_lower, gate_up_sent, out_far = (
        moved[: near - 1], moved[near - 1 : near - 1 + len(gate_up_sent)], moved[near - 1 + len(gate_up_sent) :],
    )

    gate_up_rest, gate_up_own = join_yx(grad_gate_up, gate_up_sent)
    down_part = lax.psum_scatter(grad_down, "yx", scatter_dimension=0, tiled=True)
    for one, two in zip(moved_upper, moved_lower, strict=True):
        d_norm_two = d_norm_two + jnp.concatenate([one, two], axis=0).astype(f32)
    own_cotangent = jnp.concatenate([cot_upper, cot_lower], axis=0).astype(f32)
    mid_back, _ = norm_back(mid, scale_two, gain_two, d_norm_two)
    d_mid = own_cotangent + mid_back
    d_attn = d_mid.astype(bf16)
    both = [dot32(d_attn, w).astype(bf16) for w in (w_out_near, w_out_sib)]
    d_quarters = [both[e][:, k * query_cols : (k + 1) * query_cols] for e, k in order]
    d_attn, *d_quarters = stage(d_attn, *d_quarters)

    d_context = [None] * (2 * near)
    for (e, k), x in zip(order, d_quarters, strict=True):
        d_context[(near - k) % near * 2 + e] = x if (e, k) == (0, 0) else shift(x, e, k)
    grad_out_sib = flip(rows_product(d_attn, sib_context).astype(bf16), "core")
    grad_out = (rows_product(d_attn, own_context) + grad_out_sib.astype(f32)).astype(bf16)
    output_near = mid + joined(*near_back[2:])
    grad_out, output_near, *moved = stage(grad_out, output_near, *d_context, *gate_up_rest)
    d_context, gate_up_rest = moved[: 2 * near], moved[2 * near :]

    out_moved = [to_near(out_far[k - 1], k) for k in others]
    gate_up_keep, gate_up_give = give_z(total_yx(gate_up_rest, gate_up_own))
    gate_up_home = [crossed(gate_up_give, BACK), crossed(gate_up_keep, CROSS)]
    out_part = lax.psum_scatter(grad_out, "yx", scatter_dimension=0, tiled=True)
    d_qkv = attend_back(list(range(kv_heads)), qkv, d_context, context, sums, [], layout_back, q_heads, kv_heads)
    d_qkv, *moved = stage(d_qkv, *out_moved, *gate_up_home)
    out_moved, gate_up_home = moved[: near - 1], moved[near - 1 :]

    def back_part(k):
        own, sib = (d_qkv[(2 * k + e) * rows : (2 * k + e + 1) * rows] for e in range(2))
        taken = flip(times_transpose(sib, w_project).astype(bf16), "core")
        return times_transpose(own, w_project) + taken.astype(f32)

    d_sent = [back_part(k).astype(bf16) for k in others]
    output_own = output_near
    for part in out_moved:
        output_own = output_own + part.astype(f32)
    d_qkv, down_part, out_part, output_own, *d_sent = stage(d_qkv, down_part, out_part, output_own.astype(bf16), *d_sent)

    d_upper = [to_near(d_sent[k - 1][:part_rows], k) for k in others]
    grad_project = rows_product(norm_one, d_qkv).astype(bf16)
    project_sent = send_yx(grad_project)
    total = back_part(0)
    total, grad_project, *moved = stage(total, grad_project, *d_upper, *d_sent, *project_sent)
    d_upper, d_sent, project_sent = moved[: near - 1], moved[near - 1 : 2 * near - 2], moved[2 * near - 2 :]

    d_lower = [to_near(d_sent[k - 1][part_rows:], k) for k in others]
    project_rest, project_own = join_yx(grad_project, project_sent)

    def input_part(at, moved):
        part = total[at]
        for x in moved:
            part = part + x.astype(f32)
        back, _ = norm_back(residual[at], scale_one[at], gain_one, part)
        return (d_mid[at] + back).astype(bf16)

    input_upper = input_part(slice(0, part_rows), d_upper)
    upper_crossed = crossed(input_upper, CROSS)
    total, input_upper, upper_crossed, *moved = stage(total, input_upper, upper_crossed, *d_lower, *project_rest)
    d_lower, project_rest = moved[: near - 1], moved[near - 1 :]

    input_lower = input_part(slice(part_rows, rows), d_lower)
    lower_crossed = crossed(input_lower, CROSS)
    project_keep, project_give = give_z(total_yx(project_rest, project_own))
    grad_project = sum_z(project_keep, crossed(project_give, BACK), crossed(project_keep, CROSS))
    out_quarter = out_part[:, :query_cols].astype(f32)
    for k in others:
        out_quarter = out_quarter + to_near(out_part[:, k * query_cols : (k + 1) * query_cols], k).astype(f32)
    out_keep, out_give = give_z(out_quarter.astype(bf16))
    grad_out = sum_z(out_keep, crossed(out_give, BACK), crossed(out_keep, CROSS))
    down_keep, down_give = give_z(down_part)
    grad_down = sum_z(down_keep, crossed(down_give, BACK), crossed(down_keep, CROSS))
    grad_gate_up = sum_z(gate_up_keep, *gate_up_home)
    output = jnp.where(straight(), output_own, crossed(output_own, CROSS))
    input_grad = jnp.concatenate(
        [
            jnp.where(straight(), input_upper, upper_crossed),
            jnp.where(straight(), input_lower, lower_crossed),
        ],
        axis=0,
    ).astype(f32)
    gain_grads = lax.psum(
        jnp.stack(
            [
                jnp.sum(qkv_shard.astype(f32) * grad_project, axis=1),
                jnp.sum(gate_up_shard.astype(f32) * grad_gate_up, axis=1),
            ]
        ),
        ("zh", "zl"),
    ) / jnp.stack([attn_gain, mlp_gain]).astype(f32)
    return (
        output,
        input_grad,
        gain_grads[0],
        grad_project[:, :query_cols],
        grad_project[:, query_cols : query_cols + key_cols],
        grad_project[:, query_cols + key_cols :],
        grad_out,
        gain_grads[1],
        grad_gate_up[:, :hidden_cols],
        grad_gate_up[:, hidden_cols:],
        grad_down,
    )


def solution(mesh):
    dp, tensor = mesh.shape["dp"], mesh.shape["tensor"]
    fine = Mesh(mesh.devices.reshape(dp // 2, 2, 2, tensor // 2), AXES)
    by_rows, by_dp, by_both = P(AXES, None), P(("yx", "core")), P(("yx", "core"), ("zh", "zl"))
    return jax.shard_map(
        body,
        mesh=fine,
        in_specs=(
            by_rows, by_rows, P(("yx", "core"), None), by_dp, by_both, by_both, by_both, by_both,
            by_dp, by_both, by_both, by_both,
        ),
        out_specs=(
            by_rows, by_rows, by_dp, by_both, by_both, by_both, by_both, by_dp, by_both, by_both, by_both,
        ),
        check_vma=False,
    )
```

```python
import functools
import math

import jax
import jax.numpy as jnp
import numpy as np
from jax import lax
from jax.experimental import pallas as pl
from jax.experimental.pallas import tpu as pltpu
from jax.sharding import Mesh
from jax.sharding import PartitionSpec as P

HD = 96
HALF = HD // 2
PAD = 128
PARTS = 4
SUB = 256
TILE = 512

EPSILON = 1e-05
ROTARY_BASE = 100000.0
MASKED = -1e30
LOG2E = math.log2(math.e)

AXES = ("yx", "core", "zh", "zl")
FLIP = [(0, 1), (1, 0)]


def norm_rows(values, gain):
    row_scale = lax.rsqrt(jnp.mean(values * values, axis=-1, keepdims=True) + EPSILON)
    return (row_scale, (values * row_scale * gain).astype(jnp.bfloat16))


def norm_back(values, row_scale, gain, upstream):
    weighted = upstream * gain
    inner_sum = jnp.mean(weighted * values, axis=-1, keepdims=True)
    grad_in = row_scale * weighted - values * (row_scale * row_scale * row_scale) * inner_sum
    gain_part = jnp.sum(upstream * (values * row_scale), axis=0)
    return (grad_in, gain_part)


def document_layout(lengths, group_rows):
    flat_lengths = lengths.reshape(-1)
    doc_ends = jnp.cumsum(flat_lengths)
    rows = jnp.arange(group_rows, dtype=jnp.int32)
    passed = (rows[:, None] >= doc_ends[None, :]).astype(jnp.int32)
    return (rows, jnp.sum(passed * flat_lengths[None, :], axis=1))


def rotary_tables(positions):
    exponents = jnp.arange(HALF, dtype=jnp.float32) * (2.0 / HD)
    inverse = ROTARY_BASE ** (-exponents)
    angles = positions.astype(jnp.float32)[:, None] * inverse[None, :]
    cosine, sine = jnp.cos(angles), jnp.sin(angles)
    gap = jnp.zeros((positions.shape[0], PAD // 2 - HALF), jnp.float32)
    return (
        jnp.concatenate([cosine, gap, cosine, gap], axis=1),
        jnp.concatenate([-sine, gap, sine, gap], axis=1),
    )


def rows_product(left, right):
    return lax.dot_general(
        left, right, (((0,), (0,)), ((), ())), preferred_element_type=jnp.float32
    )


def times_transpose(left, right):
    return lax.dot_general(
        left, right, (((1,), (1,)), ((), ())), preferred_element_type=jnp.float32
    )


def dot32(left, right):
    return jnp.dot(left, right, preferred_element_type=jnp.float32)


def stage(*values):
    return lax.optimization_barrier(values)


def spread(columns, heads):
    matrix = np.zeros((columns, len(heads) * PAD), np.float32)
    for at, first in enumerate(heads):
        for half in range(2):
            for i in range(HALF):
                matrix[first + half * HALF + i, at * PAD + half * (PAD // 2) + i] = 1.0
    return matrix


def turn(x, cosine, sine):
    return x * cosine + pltpu.roll(x, PAD // 2, 1) * sine


def rows_at(t, size):
    return pl.ds(pl.multiple_of(t * size, size), size)


def forward_kernel(pieces, ratio, *refs):
    place, low, full, cosine, sine, start, spread_in, gather_out = refs[:8]
    heads = spread_in.shape[0]
    refs = refs[8:]
    qkv, context, refs = refs[0], refs[1 : 1 + pieces], refs[1 + pieces :]
    log_sum, refs = refs[:heads], refs[heads:]
    q_s, k_s, v_s, s_s, top_s, acc = refs
    tiles = q_s.shape[0]
    all_subs = qkv.shape[0] // SUB
    piece_subs = all_subs // pieces
    scale = LOG2E * HD ** (-0.5)
    ones_lane = lax.broadcasted_iota(jnp.int32, (SUB, PAD), 1) == PAD - 1

    def prepare(r, carry):
        t = place[r]
        at = rows_at(t, SUB)
        cos_t, sin_t = cosine[at, :], sine[at, :]
        tile, half = t // (TILE // SUB), t % (TILE // SUB)
        for g in range(heads):
            wide = dot32(qkv[rows_at(r, SUB), :], spread_in[g])
            for h in range(ratio):
                query = turn(wide[:, h * PAD : (h + 1) * PAD], cos_t, sin_t) * scale
                first = pl.multiple_of(h * TILE + half * SUB, SUB)
                q_s[tile, g, pl.ds(first, SUB), :] = query.astype(jnp.bfloat16)
            key = turn(wide[:, ratio * PAD : (ratio + 1) * PAD], cos_t, sin_t)
            k_s[g, at, :] = key.astype(jnp.bfloat16)
            value = jnp.where(ones_lane, 1.0, wide[:, (ratio + 1) * PAD :])
            v_s[g, at, :] = value.astype(jnp.bfloat16)
        return carry

    lax.fori_loop(0, all_subs, prepare, 0)

    def query_tile(i, carry):
        starts = jnp.concatenate([start[rows_at(i, TILE), :]] * ratio, axis=0)
        top_s[...] = jnp.full_like(top_s, MASKED)

        def scores(j, masked, diagonal):
            for g in range(heads):
                s = times_transpose(q_s[i, g], k_s[g, rows_at(j, TILE), :])
                if masked:
                    key_at = lax.broadcasted_iota(jnp.int32, s.shape, 1)
                    allowed = key_at + j * TILE >= starts
                    if diagonal:
                        query_at = lax.rem(lax.broadcasted_iota(jnp.int32, s.shape, 0), TILE)
                        allowed = allowed & (key_at <= query_at)
                    s = jnp.where(allowed, s, MASKED)
                s_s[g, j] = s
                peak = s[:, :PAD]
                for c in range(1, TILE // PAD):
                    peak = jnp.maximum(peak, s[:, c * PAD : (c + 1) * PAD])
                top_s[g] = jnp.maximum(top_s[g], peak)

        def loop(first, last, masked):
            def run(j, c):
                scores(j, masked, False)
                return c

            lax.fori_loop(first, last, run, 0)

        loop(low[i], full[i], True)
        loop(full[i], i, False)
        scores(i, True, True)
        tops = [jnp.max(top_s[g], axis=1, keepdims=True) for g in range(heads)]
        acc[...] = jnp.zeros_like(acc)

        def weigh(j, c):
            for g in range(heads):
                p = jnp.exp2(s_s[g, j] - tops[g]).astype(jnp.bfloat16)
                acc[g] += dot32(p, v_s[g, rows_at(j, TILE), :])
            return c

        lax.fori_loop(low[i], i + 1, weigh, 0)
        packed = None
        for g in range(heads):
            total = acc[g][:, PAD - 1 :]
            out = acc[g] * (1.0 / total)
            sums = jnp.broadcast_to(tops[g] + jnp.log(total) * LOG2E, (ratio * TILE, PAD))
            log_sum[g][i] = sums.T[:1, :]
            wide = jnp.concatenate(
                [out[h * TILE : (h + 1) * TILE, :] for h in range(ratio)], axis=1
            ).astype(jnp.bfloat16)
            part = dot32(wide, gather_out[g])
            packed = part if packed is None else packed + part
        subs = tiles * (TILE // SUB)
        for half in range(TILE // SUB):
            r = place[subs + i * (TILE // SUB) + half]
            part = packed[half * SUB : (half + 1) * SUB, :].astype(jnp.bfloat16)
            for k in range(pieces):

                @pl.when(r // piece_subs == k)
                def store(k=k, part=part, r=r):
                    context[k][rows_at(r % piece_subs, SUB), :] = part

        return carry

    lax.fori_loop(0, tiles, query_tile, 0)


def backward_kernel(pieces, ratio, more, *refs):
    place, low, full, cosine, sine, start, refs = *refs[:6], refs[6:]
    heads = refs[0].shape[0]
    spread_in, spread_out, gather_in, refs = *refs[:3], refs[3:]
    log_sum, refs = refs[:heads], refs[heads:]
    d_context, context, qkv, refs = refs[:pieces], refs[pieces : 2 * pieces], refs[2 * pieces], refs[2 * pieces + 1 :]
    earlier, refs = (refs[0], refs[1:]) if more else (None, refs)
    d_qkv, refs = refs[0], refs[1:]
    q_s, k_s, kt_s, v_s, do_s, delta_s, log_s, dq_acc, dk_acc, dv_acc, dq_s = refs
    tiles = q_s.shape[0]
    all_subs = qkv.shape[0] // SUB
    piece_subs = all_subs // pieces
    scale = HD ** (-0.5)
    per_tile = TILE // SUB

    for k in range(pieces):

        def prepare(r, carry, k=k):
            t = place[k * piece_subs + r]
            rel = rows_at(r, SUB)
            at = rows_at(t, SUB)
            cos_t, sin_t = cosine[at, :], sine[at, :]
            for g in range(heads):
                wide = dot32(qkv[rows_at(k * piece_subs + r, SUB), :], spread_in[g])
                d_out = dot32(d_context[k][rel, :], spread_out[g])
                out = dot32(context[k][rel, :], spread_out[g])
                for h in range(ratio):
                    cols = slice(h * PAD, (h + 1) * PAD)
                    rows = slice(h * SUB, (h + 1) * SUB)
                    query = turn(wide[:, cols], cos_t, sin_t) * (scale * LOG2E)
                    q_s[t, g, rows, :] = query.astype(jnp.bfloat16)
                    do_s[t, g, rows, :] = d_out[:, cols].astype(jnp.bfloat16)
                    delta = jnp.sum((d_out[:, cols] * out[:, cols]).T, axis=0, keepdims=True)
                    delta_s[t * heads + g, :, rows] = delta
                    first = pl.multiple_of(h * TILE + t % per_tile * SUB, SUB)
                    log_s[t * heads + g, :, rows] = log_sum[g][t // per_tile, :, pl.ds(first, SUB)]
                key = turn(wide[:, ratio * PAD : (ratio + 1) * PAD], cos_t, sin_t)
                k_s[g, t] = key.astype(jnp.bfloat16)
                kt_s[g, t] = key.T.astype(jnp.bfloat16)
                v_s[g, t] = wide[:, (ratio + 1) * PAD :].astype(jnp.bfloat16)
                dk_acc[g, t] = jnp.zeros((SUB, PAD), jnp.float32)
                dv_acc[g, t] = jnp.zeros((SUB, PAD), jnp.float32)
            return carry

        lax.fori_loop(0, piece_subs, prepare, 0)

    def query_tile(i, carry):
        dq_acc[...] = jnp.zeros_like(dq_acc)

        def step(j, masked, diagonal):
            for g in range(heads):
                queries, d_out = q_s[i, g], do_s[i, g]
                s = times_transpose(k_s[g, j], queries)
                if masked:
                    key_at = lax.broadcasted_iota(jnp.int32, s.shape, 0)
                    allowed = key_at + j * SUB >= start[i]
                    if diagonal:
                        query_at = lax.rem(lax.broadcasted_iota(jnp.int32, s.shape, 1), SUB)
                        allowed = allowed & (key_at <= query_at)
                    s = jnp.where(allowed, s, MASKED)
                p = jnp.exp2(s - log_s[i * heads + g])
                d_p = times_transpose(v_s[g, j], d_out)
                d_s = (p * (d_p - delta_s[i * heads + g])).astype(jnp.bfloat16)
                dv_acc[g, j] += dot32(p.astype(jnp.bfloat16), d_out)
                dk_acc[g, j] += dot32(d_s, queries)
                dq_acc[g] += dot32(kt_s[g, j], d_s)

        def loop(first, last, masked):
            def run(j, c):
                step(j, masked, False)
                return c

            lax.fori_loop(first, last, run, 0)

        loop(low[i], full[i], True)
        loop(full[i], i, False)
        step(i, True, True)
        at = rows_at(i, SUB)
        cos_t, sin_t = cosine[at, :], sine[at, :]
        for g in range(heads):
            grad = dq_acc[g].T * scale
            for h in range(ratio):
                piece = turn(grad[h * SUB : (h + 1) * SUB, :], cos_t, -sin_t)
                dq_s[g, i, :, h * PAD : (h + 1) * PAD] = piece.astype(jnp.bfloat16)
        return carry

    lax.fori_loop(0, tiles, query_tile, 0)

    def finish(r, carry):
        t = place[r]
        at = rows_at(t, SUB)
        rel = rows_at(r, SUB)
        packed = None
        for g in range(heads):
            key = turn(dk_acc[g, t] * (1.0 / LOG2E), cosine[at, :], -sine[at, :])
            wide = jnp.concatenate(
                [dq_s[g, t], key.astype(jnp.bfloat16), dv_acc[g, t].astype(jnp.bfloat16)], axis=1
            )
            part = dot32(wide, gather_in[g])
            packed = part if packed is None else packed + part
        packed = packed.astype(jnp.bfloat16)
        d_qkv[rel, :] = packed + earlier[rel, :] if more else packed
        return carry

    lax.fori_loop(0, all_subs, finish, 0)


SMEM = pl.BlockSpec(memory_space=pltpu.SMEM)
VMEM = pl.BlockSpec(memory_space=pltpu.VMEM)
ANY = pl.BlockSpec(memory_space=pl.ANY)


def small_cost(transcendentals=0):
    return pl.CostEstimate(flops=1 << 20, bytes_accessed=1 << 16, transcendentals=transcendentals)


def head_matrices(head, q_heads, kv_heads):
    ratio = q_heads // kv_heads
    queries = [(head * ratio + r) * HD for r in range(ratio)]
    key, value = (q_heads + head) * HD, (q_heads + kv_heads + head) * HD
    inner = spread((q_heads + 2 * kv_heads) * HD, [*queries, key, value])
    outer = spread(q_heads * HD, queries)
    return jnp.asarray(inner, jnp.bfloat16), jnp.asarray(outer, jnp.bfloat16)


def stacked_matrices(q_heads, kv_heads):
    pairs = [head_matrices(head, q_heads, kv_heads) for head in range(kv_heads)]
    return jnp.stack([inner for inner, _ in pairs]), jnp.stack([outer for _, outer in pairs])


def attend(qkv, pieces, layout, q_heads, kv_heads):
    place, low, full, cosine, sine, start_column = layout
    ratio, rows = q_heads // kv_heads, qkv.shape[0]
    tiles, lanes = rows // TILE, ratio * TILE
    bf16, f32 = jnp.bfloat16, jnp.float32
    inner, outer = stacked_matrices(q_heads, kv_heads)
    outs = pl.pallas_call(
        functools.partial(forward_kernel, pieces, ratio),
        out_shape=[
            *[jax.ShapeDtypeStruct((rows // pieces, q_heads * HD), bf16)] * pieces,
            *[jax.ShapeDtypeStruct((tiles, 1, lanes), f32)] * kv_heads,
        ],
        in_specs=[SMEM] * 3 + [VMEM] * 6,
        out_specs=[VMEM] * (pieces + kv_heads),
        scratch_shapes=[
            pltpu.VMEM((tiles, kv_heads, lanes, PAD), bf16),
            pltpu.VMEM((kv_heads, rows, PAD), bf16),
            pltpu.VMEM((kv_heads, rows, PAD), bf16),
            pltpu.VMEM((kv_heads, tiles, lanes, TILE), f32),
            pltpu.VMEM((kv_heads, lanes, PAD), f32),
            pltpu.VMEM((kv_heads, lanes, PAD), f32),
        ],
        compiler_params=pltpu.CompilerParams(vmem_limit_bytes=60 * 2**20),
        cost_estimate=small_cost(),
        name="attention_forward",
    )(place, low, full, cosine, sine, start_column, inner, jnp.swapaxes(outer, 1, 2), qkv)
    return outs[:pieces], outs[pieces:]


def attend_back(heads, qkv, d_context, context, sums, earlier, layout, q_heads, kv_heads):
    place, low, full, cosine, sine, start_row = layout
    pieces, ratio, rows = len(context), q_heads // kv_heads, qkv.shape[0]
    tiles, lanes, count = rows // SUB, ratio * SUB, len(heads)
    bf16, f32 = jnp.bfloat16, jnp.float32
    inner, outer = stacked_matrices(q_heads, kv_heads)
    inner, outer = inner[heads[0] : heads[0] + count], outer[heads[0] : heads[0] + count]
    return pl.pallas_call(
        functools.partial(backward_kernel, pieces, ratio, bool(earlier)),
        out_shape=jax.ShapeDtypeStruct(qkv.shape, bf16),
        in_specs=[SMEM] * 3 + [VMEM] * (7 + count + 2 * pieces + len(earlier)),
        out_specs=VMEM,
        scratch_shapes=[
            pltpu.VMEM((tiles, count, lanes, PAD), bf16),
            pltpu.VMEM((count, tiles, SUB, PAD), bf16),
            pltpu.VMEM((count, tiles, PAD, SUB), bf16),
            pltpu.VMEM((count, tiles, SUB, PAD), bf16),
            pltpu.VMEM((tiles, count, lanes, PAD), bf16),
            pltpu.VMEM((tiles * count, 1, lanes), f32),
            pltpu.VMEM((tiles * count, 1, lanes), f32),
            pltpu.VMEM((count, PAD, lanes), f32),
            pltpu.VMEM((count, tiles, SUB, PAD), f32),
            pltpu.VMEM((count, tiles, SUB, PAD), f32),
            pltpu.VMEM((count, tiles, SUB, ratio * PAD), bf16),
        ],
        compiler_params=pltpu.CompilerParams(vmem_limit_bytes=60 * 2**20),
        cost_estimate=small_cost(),
        name=f"attention_backward_{heads[0]}",
    )(
        place, low, full, cosine, sine, start_row, inner, outer, jnp.swapaxes(inner, 1, 2),
        *[sums[h] for h in heads], *d_context, *context, qkv, *earlier,
    )


def fetch(me, where, sources, target, sems):
    copies = []
    for n, (source, (j, deep, first, column)) in enumerate(zip(sources, where, strict=True)):
        cols = min(source.shape[1], target.shape[1] - column)
        at = pl.ds(pl.multiple_of((me[0] ^ j) * deep + first, 16), source.shape[0])
        if cols != source.shape[1]:
            source = source.at[:, :cols]
        copies.append(pltpu.make_async_copy(source, target.at[at, column : column + cols], sems.at[n]))
    return copies


def take_part(parts, target):
    for n, part in enumerate(parts):

        @pl.when(pl.program_id(0) == n)
        def take(part=part):
            target[...] = part[...]


def at_first_step(copies, what):
    @pl.when(pl.program_id(0) == 0)
    def run():
        for copy in copies:
            what(copy)


def project_kernel(where, more, me, *refs):
    parts, gain, refs = refs[:PARTS], refs[PARTS], refs[PARTS + 1 :]
    sources, refs = refs[: len(where[0])], refs[len(where[0]) :]
    norm_all, qkv_all, weight, sems, rows_s = refs[2 if more else 0 :]
    copies = fetch(me, where[0], sources, weight, sems)
    at_first_step(copies, lambda copy: copy.start())
    take_part(parts, rows_s)
    x = rows_s[...].astype(jnp.float32)
    scale = lax.rsqrt(jnp.mean(x * x, axis=-1, keepdims=True) + EPSILON)
    norm_all[...] = (x * scale * gain[...]).astype(jnp.bfloat16)
    at_first_step(copies, lambda copy: copy.wait())
    qkv_all[...] = dot32(norm_all[...], weight[...]).astype(jnp.bfloat16)


def gate_kernel(where, more, me, *refs):
    parts, refs = refs[:PARTS], refs[PARTS:]
    sources, refs = refs[: len(where[0])], refs[len(where[0]) :]
    norm_all, gate_up_all, hidden_all, weight, sems = refs[3 if more else 0 :]
    hidden_cols = hidden_all.shape[1]
    copies = fetch(me, where[0], sources, weight, sems)
    at_first_step(copies, lambda copy: copy.start())
    take_part(parts, norm_all)
    at_first_step(copies, lambda copy: copy.wait())
    x = norm_all[...]
    width = min(512, hidden_cols)
    for at in range(0, hidden_cols, width):
        gate_at = slice(at, at + width)
        up_at = slice(hidden_cols + at, hidden_cols + at + width)
        gate = dot32(x, weight[:, gate_at])
        up = dot32(x, weight[:, up_at])
        gate_up_all[:, gate_at] = gate
        gate_up_all[:, up_at] = up
        hidden_all[:, gate_at] = (gate * (1.0 / (1.0 + jnp.exp(-gate))) * up).astype(jnp.bfloat16)


def gate_back_kernel(where, more, me, *refs):
    parts, gate_up_all, hidden_other, refs = refs[:PARTS], *refs[PARTS : PARTS + 2], refs[PARTS + 2 :]
    gate_up, refs = refs[: len(where[0])], refs[len(where[0]) :]
    down, refs = refs[: len(where[1])], refs[len(where[1]) :]
    refs = refs[2 if more else 0 :]
    grad_all, d_gate_up_all, d_norm_own, d_norm_sib, out_own, out_sib = refs[:6]
    w_gate_up, gate_up_sems, w_down, down_sems = refs[6:]
    hidden_cols = w_down.shape[1]
    down_copies = fetch(me, where[1], down, w_down, down_sems)
    copies = fetch(me, where[0], gate_up, w_gate_up, gate_up_sems)
    at_first_step(down_copies + copies, lambda copy: copy.start())
    take_part(parts, grad_all)
    at_first_step(down_copies, lambda copy: copy.wait())
    dy = grad_all[...]
    width = min(512, hidden_cols)
    for at in range(0, hidden_cols, width):
        gate_at = slice(at, at + width)
        up_at = slice(hidden_cols + at, hidden_cols + at + width)
        d_hidden = dot32(dy, w_down[:, gate_at])
        gate, up = gate_up_all[:, gate_at], gate_up_all[:, up_at]
        sigmoid = 1.0 / (1.0 + jnp.exp(-gate))
        d_gate = d_hidden * up * sigmoid * (1.0 + gate * (1.0 - sigmoid))
        d_gate_up_all[:, gate_at] = d_gate.astype(jnp.bfloat16)
        d_gate_up_all[:, up_at] = (d_hidden * (gate * sigmoid)).astype(jnp.bfloat16)
    out = times_transpose(hidden_other[...], w_down[...]).astype(jnp.bfloat16)
    at_first_step(copies, lambda copy: copy.wait())
    d_norm = times_transpose(d_gate_up_all[...], w_gate_up[...]).astype(jnp.bfloat16)

    @pl.when(pl.program_id(0) < PARTS // 2)
    def to_own():
        d_norm_own[...] = d_norm
        out_own[...] = out

    @pl.when(pl.program_id(0) >= PARTS // 2)
    def to_sibling():
        d_norm_sib[...] = d_norm
        out_sib[...] = out


def piece_call(kernel, name, k, pieces, me, parts, whole, tiled, fetched, earlier, outs):
    tile, width = parts[0].shape
    own_rows = tile * PARTS // 2
    maps = {
        "own": lambda i: (jnp.minimum(i, PARTS // 2 - 1), 0),
        "sibling": lambda i: (jnp.maximum(i - PARTS // 2, 0), 0),
    }

    def rows_of(piece):
        return lambda i: (piece * PARTS + i, 0)

    sources = [x for arrays, _, _ in fetched for x in arrays]
    first_earlier = 1 + PARTS + len(whole) + len(tiled) + len(sources)
    scratch = []
    for arrays, _, cols in fetched:
        scratch += [pltpu.VMEM((width, cols), jnp.bfloat16), pltpu.SemaphoreType.DMA((len(arrays),))]
    if kernel is project_kernel:
        scratch.append(pltpu.VMEM((tile, width), jnp.bfloat16))
    return pl.pallas_call(
        functools.partial(kernel, tuple(where for _, where, _ in fetched), bool(earlier)),
        grid=(PARTS,),
        out_shape=[
            jax.ShapeDtypeStruct((pieces * 2 * own_rows if span == "all" else own_rows, columns), kind)
            for columns, kind, span in outs
        ],
        in_specs=[
            SMEM,
            *[pl.BlockSpec((tile, width), lambda i: (0, 0))] * PARTS,
            *(pl.BlockSpec(x.shape, lambda i: (0, 0)) for x in whole),
            *(pl.BlockSpec((tile, x.shape[1]), rows_of(piece)) for x, piece in tiled),
            *[ANY] * (len(sources) + len(earlier)),
        ],
        out_specs=[
            pl.BlockSpec((tile, columns), rows_of(k) if span == "all" else maps[span])
            for columns, kind, span in outs
        ],
        scratch_shapes=scratch,
        input_output_aliases={first_earlier + n: n for n in range(len(earlier))},
        compiler_params=pltpu.CompilerParams(vmem_limit_bytes=60 * 2**20),
        cost_estimate=small_cost(),
        name=f"{name}_{k}",
    )(me, *parts, *whole, *(x for x, _ in tiled), *sources, *earlier)


def assemble_kernel(where, me, *refs):
    sources, whole, sems = refs[: len(where)], refs[len(where)], refs[len(where) + 1]
    copies = fetch(me, where, sources, whole, sems)
    for copy in copies:
        copy.start()
    for copy in copies:
        copy.wait()


def assemble(name, me, arrays, where, rows, cols):
    return pl.pallas_call(
        functools.partial(assemble_kernel, where),
        out_shape=jax.ShapeDtypeStruct((rows, cols), arrays[0].dtype),
        in_specs=[SMEM, *[ANY] * len(arrays)],
        out_specs=VMEM,
        scratch_shapes=[pltpu.SemaphoreType.DMA((len(arrays),))],
        compiler_params=pltpu.CompilerParams(vmem_limit_bytes=60 * 2**20),
        cost_estimate=small_cost(),
        name=name,
    )(me, *arrays)


def flip(x, axis):
    return lax.ppermute(x, axis, FLIP)


CROSS = [(1, 2), (2, 1)]
OUT = [(0, 1), (3, 2), (2, 0), (1, 3)]
BACK = [(1, 0), (2, 3), (0, 2), (3, 1)]


def crossed(x, perm):
    return lax.ppermute(x, ("core", "zh"), perm)


def straight():
    return lax.axis_index("core") == lax.axis_index("zh")


def swap(x):
    return jnp.where(straight(), x, crossed(x, CROSS))


def send_z(w):
    return crossed(w, OUT), crossed(w, CROSS)


def pair_of(w, out, cross):
    zh = lax.axis_index("zh")
    x = jnp.where(straight(), w, cross)
    return jnp.concatenate([jnp.where(zh == 0, x, out), jnp.where(zh == 0, out, x)], axis=0)


def give_z(part):
    zh = lax.axis_index("zh")
    half = part.shape[0] // 2
    upper, lower = part[:half], part[half:]
    return jnp.where(zh == 0, upper, lower), jnp.where(zh == 0, lower, upper)


def sum_z(keep, back, cross):
    return back.astype(jnp.float32) + jnp.where(straight(), keep, cross).astype(jnp.float32)


def shift(x, e, k):
    n = lax.axis_size("zl")
    return lax.ppermute(
        x, ("core", "zl"), [(c * n + l, (c ^ e) * n + (l + k) % n) for c in range(2) for l in range(n)]
    )


def from_near(x, k):
    n = lax.axis_size("zl")
    return lax.ppermute(x, "zl", [((j + k) % n, j) for j in range(n)])


def to_near(x, k):
    n = lax.axis_size("zl")
    return lax.ppermute(x, "zl", [(j, (j + k) % n) for j in range(n)])


def across(x, j):
    n = lax.axis_size("yx")
    return lax.ppermute(x, "yx", [(a, a ^ j) for a in range(n)])


def neighbours(x):
    count = lax.axis_size("yx")
    return [across(x, j) for j in range(1, count if count != 4 else 3)]


def diagonal(taken):
    if lax.axis_size("yx") != 4:
        return []
    half = taken[0].shape[0] // 2
    return [across(taken[1][:half], 1), across(taken[0][half:], 2)]


def blocks_of(own, taken, halves, column=0):
    deep = own.shape[0]
    arrays = [own, *taken, *halves]
    where = [(j, deep, 0, column) for j in range(1 + len(taken))]
    where += [(3, deep, n * deep // 2, column) for n in range(len(halves))]
    return arrays, tuple(where)


def block_of(grad, j, columns):
    size = grad.shape[0] // lax.axis_size("yx")
    first = (lax.axis_index("yx") ^ j) * size
    return lax.dynamic_slice(grad, (first, columns[0]), (size, columns[1] - columns[0]))


def send_yx(grad, columns):
    count = lax.axis_size("yx")
    if count != 4:
        return [across(block_of(grad, j, columns), j) for j in range(1, count)]
    far = block_of(grad, 3, columns)
    half = far.shape[0] // 2
    return [across(far[:half], 1), across(far[half:], 2)]


def join_yx(grad, columns, taken):
    if lax.axis_size("yx") != 4:
        return taken, block_of(grad, 0, columns)
    half = taken[0].shape[0]
    one, two = block_of(grad, 1, columns), block_of(grad, 2, columns)
    one = jnp.concatenate([one[:half], one[half:] + taken[1]], axis=0)
    two = jnp.concatenate([two[:half] + taken[0], two[half:]], axis=0)
    return [across(one, 1), across(two, 2)], block_of(grad, 0, columns)


def total_yx(taken, own):
    total = own.astype(jnp.float32)
    for part in taken:
        total = total + part.astype(jnp.float32)
    return total.astype(jnp.bfloat16)


def body(
    tokens,
    cotangent,
    seq_lengths,
    attn_gain,
    q_weight,
    key_projection,
    value_projection,
    out_weight,
    mlp_gain,
    gate_weight,
    up_weight,
    down_weight,
):
    bf16, f32 = jnp.bfloat16, jnp.float32
    core, zl, yx = lax.axis_index("core"), lax.axis_index("zl"), lax.axis_index("yx")
    near = lax.axis_size("zl")
    others = range(1, near)
    rows = tokens.shape[0]
    group_rows = 2 * near * rows
    query_cols, key_cols = q_weight.shape[1], key_projection.shape[1]
    qkv_cols = query_cols + 2 * key_cols
    q_heads, kv_heads = query_cols // HD, key_cols // HD
    hidden_cols = gate_weight.shape[1]
    me = yx.astype(jnp.int32).reshape(1)

    qkv_shard = jnp.concatenate([q_weight, key_projection, value_projection], axis=1)
    gate_up_shard = jnp.concatenate([gate_weight, up_weight], axis=1)
    part_rows = rows // 2
    upper = swap(tokens[:part_rows])
    shard = jnp.concatenate([qkv_shard, out_weight], axis=1)
    shard_moved = send_z(shard)
    lengths = swap(seq_lengths)
    gains = lax.all_gather(jnp.stack([attn_gain, mlp_gain]), ("yx", "core"), axis=1, tiled=True).astype(f32)
    upper, lengths, second_part, gains, *shard_moved = stage(upper, lengths, tokens[part_rows:], gains, *shard_moved)
    gain_one, gain_two = gains[0], gains[1]

    upper_far = [from_near(upper, k) for k in others]
    lower = swap(second_part)
    pair = pair_of(shard, *shard_moved)
    taken = neighbours(pair)
    upper_sib = flip(upper, "core")

    subs = jnp.arange(group_rows // SUB, dtype=jnp.int32)
    per_device = rows // SUB
    source, within = subs // per_device, subs % per_device
    there_core, there_zl = (source % 2) ^ core, (source // 2 + zl) % near
    to_order = (there_core * near + there_zl) * per_device + within
    from_order = (((source % near - zl) % near) * 2 + ((source // near) ^ core)) * per_device + within
    place = jnp.concatenate([to_order, from_order])
    row_at, doc_start = document_layout(lengths, group_rows)
    cosine, sine = rotary_tables(row_at - doc_start)

    def bounds(size):
        tile_start = doc_start.reshape(-1, size)
        tile = jnp.arange(group_rows // size, dtype=jnp.int32)
        low = tile_start[:, 0] // size
        return low, jnp.minimum((tile_start[:, -1] + size - 1) // size, tile)

    start_row = jnp.tile(doc_start.reshape(-1, 1, SUB), (1, 1, q_heads // kv_heads))
    layout = (place, *bounds(TILE), cosine, sine, doc_start[:, None])
    layout_back = (place, *bounds(SUB), cosine, sine, start_row)
    lower, upper_sib, *moved = stage(lower, upper_sib, *upper_far, *taken, *layout, *layout_back)
    upper_far, moved = moved[: near - 1], moved[near - 1 :]
    taken, moved = moved[: len(taken)], moved[len(taken) :]
    layout, layout_back = moved[: len(layout)], moved[len(layout) :]

    lower_far = [from_near(lower, k) for k in others]
    lower_sib = flip(lower, "core")
    upper_far_sib = [flip(x, "core") for x in upper_far]
    out_pair = pair[:, qkv_cols:]
    out_far = [from_near(out_pair, k) for k in others]
    blocks = blocks_of(pair, taken, diagonal(taken))
    projecting = [(*blocks, qkv_cols)]
    gain_row = gain_one[None]
    outs = [(tokens.shape[1], bf16, "all"), (qkv_cols, bf16, "all")]
    parts = [upper, lower, upper_sib, lower_sib]
    normed = piece_call(project_kernel, "project", 0, near, me, parts, [gain_row], [], projecting, [], outs)
    gate_up_shard, *moved = stage(gate_up_shard, *lower_far, *upper_far_sib, *out_far, *normed)
    lower_far, upper_far_sib, out_far, normed = (
        moved[: near - 1], moved[near - 1 : 2 * near - 2], moved[2 * near - 2 : 3 * near - 3], moved[3 * near - 3 :],
    )

    out_taken = [neighbours(far) for far in out_far]
    step = len(out_taken[0])
    for k in others:
        parts = [upper_far[k - 1], lower_far[k - 1], upper_far_sib[k - 1], flip(lower_far[k - 1], "core")]
        normed = piece_call(project_kernel, "project", k, near, me, parts, [gain_row], [], projecting, normed, outs)
    norm_one, qkv = normed
    gate_up_shard, qkv, *moved = stage(gate_up_shard, qkv, *(x for t in out_taken for x in t))
    out_taken = [moved[n * step : (n + 1) * step] for n in range(near - 1)]

    gate_up_moved = send_z(gate_up_shard)
    out_halves = [x for t in out_taken for x in diagonal(t)]
    context, sums = attend(qkv, 2 * near, layout, q_heads, kv_heads)
    down_shard, *moved = stage(down_weight, *context, *gate_up_moved, *out_halves)
    context, gate_up_moved, out_halves = moved[: 2 * near], moved[2 * near : 2 * near + 2], moved[2 * near + 2 :]

    quarters = {(0, 0): context[0]}
    moves = [(e, k) for k in range(near) for e in range(2)]
    for e, k in moves[1:-1]:
        quarters[e, (near - k) % near] = shift(context[2 * k + e], e, k)
    pairs = [
        pair_of(*(x[:, n * hidden_cols : (n + 1) * hidden_cols] for x in (gate_up_shard, *gate_up_moved)))
        for n in range(2)
    ]
    gate_taken = neighbours(pairs[0])
    order = list(quarters)
    last, up_pair, down_shard, *moved = stage(context[-1], pairs[1], down_shard, *quarters.values(), *out_halves)
    quarters, out_halves = dict(zip(order, moved[: len(order)], strict=True)), moved[len(order) :]

    e, k = moves[-1]
    quarters[e, (near - k) % near] = shift(last, e, k)
    down_moved = send_z(down_shard)
    step = len(out_halves) // max(near - 1, 1)
    own_parts = [x[:, qkv_cols:] for x in blocks[0]]
    parts = [blocks_of(own_parts[0], own_parts[1 : 1 + len(taken)], own_parts[1 + len(taken) :])]
    together = query_cols % 128 == 0
    for n, (x, t) in enumerate(zip(out_far, out_taken, strict=True)):
        parts.append(blocks_of(x, t, out_halves[n * step : (n + 1) * step], (n + 1) * query_cols if together else 0))
    if together:
        arrays, where = [x for some, _ in parts for x in some], tuple(w for _, some in parts for w in some)
        w_out_near = assemble("assemble_out", me, arrays, where, tokens.shape[1], near * query_cols)
    else:
        w_out_near = jnp.concatenate(
            [assemble(f"assemble_out_{n}", me, *some, tokens.shape[1], query_cols) for n, some in enumerate(parts)],
            axis=1,
        )
    w_out_sib = flip(w_out_near, "core")
    residual = jnp.concatenate([upper, lower], axis=0).astype(f32)
    scale_one = lax.rsqrt(jnp.mean(residual * residual, axis=-1, keepdims=True) + EPSILON)
    order = [(e, k) for e in range(2) for k in range(near)]
    w_out_sib, w_out_near, scale_one, up_pair, cotangent, *moved = stage(
        w_out_sib, w_out_near, scale_one, up_pair, cotangent, *[quarters[at] for at in order], *gate_taken, *down_moved
    )
    quarters, gate_taken, down_moved = moved[: 2 * near], moved[2 * near : -2], moved[-2:]

    cot_upper = swap(cotangent[:part_rows])
    own_context = jnp.concatenate(quarters[:near], axis=1)
    sib_context = jnp.concatenate(quarters[near:], axis=1)
    mid = residual + times_transpose(own_context, w_out_near) + times_transpose(sib_context, w_out_sib)
    scale_two, norm_two = norm_rows(mid, gain_two)
    norm_upper, norm_lower, cot_upper, up_pair, *gate_taken = stage(
        norm_two[:part_rows], norm_two[part_rows:], cot_upper, up_pair, *gate_taken
    )

    upper_far = [from_near(norm_upper, k) for k in others]
    gate_halves = diagonal(gate_taken)
    up_taken = neighbours(up_pair)
    upper_sib, lower_sib = flip(norm_upper, "core"), flip(norm_lower, "core")
    cot_lower = swap(cotangent[part_rows:])
    down_pair = pair_of(down_shard, *down_moved)
    w_project = assemble("assemble_project", me, *blocks, tokens.shape[1], qkv_cols)
    cot_lower, upper_sib, lower_sib, down_pair, w_project, *moved = stage(
        cot_lower, upper_sib, lower_sib, down_pair, w_project, *upper_far, *gate_halves, *up_taken
    )
    upper_far, moved = moved[: near - 1], moved[near - 1 :]
    gate_halves, up_taken = moved[: len(gate_halves)], moved[len(gate_halves) :]

    lower_far = [from_near(norm_lower, k) for k in others]
    upper_far_sib = [flip(x, "core") for x in upper_far]
    cot_upper_sib = flip(cot_upper, "core")
    up_halves = diagonal(up_taken)
    down_taken = neighbours(down_pair)
    gate_blocks = blocks_of(pairs[0], gate_taken, gate_halves)
    up_blocks = blocks_of(up_pair, up_taken, up_halves, hidden_cols)
    gate_up = ([*gate_blocks[0], *up_blocks[0]], gate_blocks[1] + up_blocks[1], 2 * hidden_cols)
    outs = [(norm_two.shape[1], bf16, "all"), (2 * hidden_cols, f32, "all"), (hidden_cols, bf16, "all")]
    parts = [norm_upper, norm_lower, upper_sib, lower_sib]
    earlier = piece_call(gate_kernel, "gate", 0, near, me, parts, [], [], [gate_up], [], outs)
    cot_lower, cot_upper_sib, *moved = stage(
        cot_lower, cot_upper_sib, *lower_far, *upper_far_sib, *down_taken, *earlier
    )
    lower_far, upper_far_sib, moved = moved[: near - 1], moved[near - 1 : 2 * near - 2], moved[2 * near - 2 :]
    down_taken, earlier = moved[: len(down_taken)], moved[len(down_taken) :]

    cot_upper_far = [from_near(cot_upper, k) for k in others]
    cot_lower_sib = flip(cot_lower, "core")
    down_halves = diagonal(down_taken)
    for k in others:
        parts = [upper_far[k - 1], lower_far[k - 1], upper_far_sib[k - 1], flip(lower_far[k - 1], "core")]
        earlier = piece_call(gate_kernel, "gate", k, near, me, parts, [], [], [gate_up], earlier, outs)
    cot_lower, cot_lower_sib, *moved = stage(cot_lower, cot_lower_sib, *cot_upper_far, *earlier, *down_halves)
    cot_upper_far, earlier, down_halves = moved[: near - 1], moved[near - 1 : near + 2], moved[near + 2 :]
    norm_two_all, gate_up_all, hidden_all = earlier

    cot_lower_far = [from_near(cot_lower, k) for k in others]
    cot_upper_far_sib = [flip(x, "core") for x in cot_upper_far]
    down = (*blocks_of(down_pair, down_taken, down_halves), hidden_cols)
    width = norm_two.shape[1]
    outs = [(width, bf16, "all"), (2 * hidden_cols, bf16, "all")]
    outs += [(width, bf16, "own"), (width, bf16, "sibling")] * 2

    def way_back(k, parts, earlier):
        tiled = [(gate_up_all, k), (hidden_all, (k + 1) % near)]
        return piece_call(gate_back_kernel, "gate_back", k, near, me, parts, [], tiled, [gate_up, down], earlier, outs)

    def joined(own, sib):
        return own.astype(f32) + flip(sib, "core").astype(f32)

    grad_all, d_gate_up_all, *near_back = way_back(0, [cot_upper, cot_lower, cot_upper_sib, cot_lower_sib], [])
    grad_all, d_gate_up_all, *moved = stage(
        grad_all, d_gate_up_all, *near_back, *cot_lower_far, *cot_upper_far_sib
    )
    near_back, cot_lower_far, cot_upper_far_sib = moved[:4], moved[4 : near + 3], moved[near + 3 :]

    out_sum = joined(*near_back[2:]).astype(bf16)
    cot_lower_far_sib = [flip(x, "core") for x in cot_lower_far]
    out_sum, *cot_lower_far_sib = stage(out_sum, *cot_lower_far_sib)
    out_upper = to_near(out_sum[:part_rows], 1 % near)
    back = []
    for k in others:
        parts = [cot_upper_far[k - 1], cot_lower_far[k - 1], cot_upper_far_sib[k - 1], cot_lower_far_sib[k - 1]]
        grad_all, d_gate_up_all, *more = way_back(k, parts, [grad_all, d_gate_up_all])
        back.append(more)
    grad_all, d_gate_up_all, out_upper, *far_back = stage(
        grad_all, d_gate_up_all, out_upper, *(x for more in back for x in more)
    )
    d_norm_sent = [joined(*far_back[4 * n : 4 * n + 2]).astype(bf16) for n in range(near - 1)]
    out_far_back = [far_back[4 * n + 2 : 4 * n + 4] for n in range(near - 1)]
    grad_all, d_gate_up_all, near_own, near_sib, *d_norm_sent = stage(
        grad_all, d_gate_up_all, *near_back[:2], *d_norm_sent
    )

    moved_upper = [to_near(d_norm_sent[k - 1][:part_rows], k) for k in others]
    grad_gate_up = rows_product(norm_two_all, d_gate_up_all).astype(bf16)
    grad_gate_up, grad_all, near_own, near_sib, *moved = stage(
        grad_gate_up, grad_all, near_own, near_sib, *moved_upper, *d_norm_sent
    )
    moved_upper, d_norm_sent = moved[: near - 1], moved[near - 1 :]

    moved_lower = [to_near(d_norm_sent[k - 1][part_rows:], k) for k in others]
    halves = [(n * hidden_cols, (n + 1) * hidden_cols) for n in range(2)]
    gate_up_sent = [send_yx(grad_gate_up, half) for half in halves]
    d_norm_two = joined(near_own, near_sib)
    grad_down = rows_product(grad_all, hidden_all).astype(bf16)
    step = len(gate_up_sent[0])
    grad_down, d_norm_two, out_sum, grad_gate_up, *moved = stage(
        grad_down, d_norm_two, out_sum, grad_gate_up, *moved_lower, *gate_up_sent[0], *gate_up_sent[1]
    )
    moved_lower, gate_sent, up_sent = moved[: near - 1], moved[near - 1 : near - 1 + step], moved[near - 1 + step :]

    gate_rest, gate_own = join_yx(grad_gate_up, halves[0], gate_sent)
    out_lower = to_near(out_sum[part_rows:], 1 % near)
    down_part = lax.psum_scatter(grad_down, "yx", scatter_dimension=0, tiled=True)
    for one, two in zip(moved_upper, moved_lower, strict=True):
        d_norm_two = d_norm_two + jnp.concatenate([one, two], axis=0).astype(f32)
    own_cotangent = jnp.concatenate([cot_upper, cot_lower], axis=0).astype(f32)
    mid_back, _ = norm_back(mid, scale_two, gain_two, d_norm_two)
    d_mid = own_cotangent + mid_back
    d_attn = d_mid.astype(bf16)
    both = [dot32(d_attn, w).astype(bf16) for w in (w_out_near, w_out_sib)]
    d_quarters = [both[e][:, k * query_cols : (k + 1) * query_cols] for e, k in order]
    d_attn, out_lower, *moved = stage(d_attn, out_lower, *d_quarters, *gate_rest)
    d_quarters, gate_rest = moved[: 2 * near], moved[2 * near :]

    d_context = [None] * (2 * near)
    d_context[0] = d_quarters[0]
    for (e, k), x in zip(order[1:-1], d_quarters[1:-1], strict=True):
        d_context[(near - k) % near * 2 + e] = shift(x, e, k)
    (e, k), at_last = order[-1], (near - order[-1][1]) % near * 2 + order[-1][0]
    known = [n for n in range(2 * near) if n != at_last]
    d_attn, last, *moved = stage(d_attn, d_quarters[-1], *(d_context[n] for n in known))
    for n, x in zip(known, moved, strict=True):
        d_context[n] = x

    d_context[at_last] = shift(last, e, k)
    up_rest, up_own = join_yx(grad_gate_up, halves[1], up_sent)
    grad_out_sib = flip(rows_product(d_attn, sib_context).astype(bf16), "core")
    grad_out = (rows_product(d_attn, own_context) + grad_out_sib.astype(f32)).astype(bf16)
    output_own = mid + joined(*out_far_back[-1]) + jnp.concatenate([out_upper, out_lower], axis=0).astype(f32)
    for n in range(near - 2):
        output_own = output_own + to_near(joined(*out_far_back[n]).astype(bf16), n + 2).astype(f32)
    output_own = output_own.astype(bf16)
    grad_out, output_own, *moved = stage(grad_out, output_own, *d_context, *up_rest)
    d_context, up_rest = moved[: 2 * near], moved[2 * near :]

    output_crossed = crossed(output_own, CROSS)
    gate_up_keep, gate_up_give = give_z(
        jnp.concatenate([total_yx(gate_rest, gate_own), total_yx(up_rest, up_own)], axis=1)
    )
    gate_up_home = [crossed(gate_up_give, BACK), crossed(gate_up_keep, CROSS)]
    out_part = lax.psum_scatter(grad_out, "yx", scatter_dimension=0, tiled=True)
    d_qkv = attend_back(list(range(kv_heads)), qkv, d_context, context, sums, [], layout_back, q_heads, kv_heads)
    d_qkv, output_crossed, down_part, out_part, *gate_up_home = stage(
        d_qkv, output_crossed, down_part, out_part, *gate_up_home
    )

    def back_part(k):
        own, sib = (d_qkv[(2 * k + e) * rows : (2 * k + e + 1) * rows] for e in range(2))
        taken = flip(times_transpose(sib, w_project).astype(bf16), "core")
        return times_transpose(own, w_project) + taken.astype(f32)

    down_keep, down_give = give_z(down_part)
    down_home = [crossed(down_give, BACK), crossed(down_keep, CROSS)]
    out_moved = [to_near(out_part[:, k * query_cols : (k + 1) * query_cols], k) for k in others]
    d_sent = [back_part(k).astype(bf16) for k in others]
    d_qkv, *moved = stage(d_qkv, *d_sent, *out_moved, *down_home)
    d_sent, out_moved, down_home = moved[: near - 1], moved[near - 1 : 2 * near - 2], moved[2 * near - 2 :]

    d_upper = [to_near(d_sent[k - 1][:part_rows], k) for k in others]
    out_quarter = out_part[:, :query_cols].astype(f32)
    for part in out_moved:
        out_quarter = out_quarter + part.astype(f32)
    out_keep, out_give = give_z(out_quarter.astype(bf16))
    out_home = [crossed(out_give, BACK), crossed(out_keep, CROSS)]
    grad_project = rows_product(norm_one, d_qkv).astype(bf16)
    project_sent = send_yx(grad_project, (0, qkv_cols))
    total = back_part(0)
    total, grad_project, *moved = stage(total, grad_project, *d_upper, *d_sent, *out_home, *project_sent)
    d_upper, d_sent, moved = moved[: near - 1], moved[near - 1 : 2 * near - 2], moved[2 * near - 2 :]
    out_home, project_sent = moved[:2], moved[2:]

    d_lower = [to_near(d_sent[k - 1][part_rows:], k) for k in others]
    project_rest, project_own = join_yx(grad_project, (0, qkv_cols), project_sent)

    def input_part(at, moved):
        part = total[at]
        for x in moved:
            part = part + x.astype(f32)
        back, _ = norm_back(residual[at], scale_one[at], gain_one, part)
        return (d_mid[at] + back).astype(bf16)

    input_upper = input_part(slice(0, part_rows), d_upper)
    upper_crossed = crossed(input_upper, CROSS)
    total, input_upper, upper_crossed, *moved = stage(total, input_upper, upper_crossed, *d_lower, *project_rest)
    d_lower, project_rest = moved[: near - 1], moved[near - 1 :]

    project_keep, project_give = give_z(total_yx(project_rest, project_own))
    project_home = [crossed(project_give, BACK), crossed(project_keep, CROSS)]
    input_lower = input_part(slice(part_rows, rows), d_lower)
    lower_crossed = crossed(input_lower, CROSS)
    grad_project = sum_z(project_keep, *project_home)
    grad_out = sum_z(out_keep, *out_home)
    grad_down = sum_z(down_keep, *down_home)
    grad_gate_up = sum_z(gate_up_keep, *gate_up_home)
    output = jnp.where(straight(), output_own, output_crossed)
    input_grad = jnp.concatenate(
        [
            jnp.where(straight(), input_upper, upper_crossed),
            jnp.where(straight(), input_lower, lower_crossed),
        ],
        axis=0,
    ).astype(f32)
    gain_grads = lax.psum(
        jnp.stack(
            [
                jnp.sum(qkv_shard.astype(f32) * grad_project, axis=1),
                jnp.sum(gate_up_shard.astype(f32) * grad_gate_up, axis=1),
            ]
        ),
        ("zh", "zl"),
    ) / jnp.stack([attn_gain, mlp_gain]).astype(f32)
    return (
        output,
        input_grad,
        gain_grads[0],
        grad_project[:, :query_cols],
        grad_project[:, query_cols : query_cols + key_cols],
        grad_project[:, query_cols + key_cols :],
        grad_out,
        gain_grads[1],
        grad_gate_up[:, :hidden_cols],
        grad_gate_up[:, hidden_cols:],
        grad_down,
    )


def solution(mesh):
    dp, tensor = mesh.shape["dp"], mesh.shape["tensor"]
    fine = Mesh(mesh.devices.reshape(dp // 2, 2, 2, tensor // 2), AXES)
    by_rows, by_dp, by_both = P(AXES, None), P(("yx", "core")), P(("yx", "core"), ("zh", "zl"))
    return jax.shard_map(
        body,
        mesh=fine,
        in_specs=(
            by_rows, by_rows, P(("yx", "core"), None), by_dp, by_both, by_both, by_both, by_both,
            by_dp, by_both, by_both, by_both,
        ),
        out_specs=(
            by_rows, by_rows, by_dp, by_both, by_both, by_both, by_both, by_dp, by_both, by_both, by_both,
        ),
        check_vma=False,
    )
```

```python
import functools
import math

import jax
import jax.numpy as jnp
import numpy as np
from jax import lax
from jax.experimental import pallas as pl
from jax.experimental.pallas import tpu as pltpu
from jax.sharding import Mesh
from jax.sharding import PartitionSpec as P

HD = 96
HALF = HD // 2
PAD = 128
PARTS = 4
SUB = 256
TILE = 512

EPSILON = 1e-05
ROTARY_BASE = 100000.0
MASKED = -1e30
LOG2E = math.log2(math.e)

AXES = ("yx", "core", "zh", "zl")
FLIP = [(0, 1), (1, 0)]


def norm_rows(values, gain):
    row_scale = lax.rsqrt(jnp.mean(values * values, axis=-1, keepdims=True) + EPSILON)
    return (row_scale, (values * row_scale * gain).astype(jnp.bfloat16))


def norm_back(values, row_scale, gain, upstream):
    weighted = upstream * gain
    inner_sum = jnp.mean(weighted * values, axis=-1, keepdims=True)
    grad_in = row_scale * weighted - values * (row_scale * row_scale * row_scale) * inner_sum
    gain_part = jnp.sum(upstream * (values * row_scale), axis=0)
    return (grad_in, gain_part)


def document_layout(lengths, group_rows):
    flat_lengths = lengths.reshape(-1)
    doc_ends = jnp.cumsum(flat_lengths)
    rows = jnp.arange(group_rows, dtype=jnp.int32)
    passed = (rows[:, None] >= doc_ends[None, :]).astype(jnp.int32)
    return (rows, jnp.sum(passed * flat_lengths[None, :], axis=1))


def rotary_tables(positions):
    exponents = jnp.arange(HALF, dtype=jnp.float32) * (2.0 / HD)
    inverse = ROTARY_BASE ** (-exponents)
    angles = positions.astype(jnp.float32)[:, None] * inverse[None, :]
    cosine, sine = jnp.cos(angles), jnp.sin(angles)
    gap = jnp.zeros((positions.shape[0], PAD // 2 - HALF), jnp.float32)
    return (
        jnp.concatenate([cosine, gap, cosine, gap], axis=1),
        jnp.concatenate([-sine, gap, sine, gap], axis=1),
    )


def rows_product(left, right):
    return lax.dot_general(
        left, right, (((0,), (0,)), ((), ())), preferred_element_type=jnp.float32
    )


def times_transpose(left, right):
    return lax.dot_general(
        left, right, (((1,), (1,)), ((), ())), preferred_element_type=jnp.float32
    )


def dot32(left, right):
    return jnp.dot(left, right, preferred_element_type=jnp.float32)


def stage(*values):
    return lax.optimization_barrier(values)


def spread(columns, heads):
    matrix = np.zeros((columns, len(heads) * PAD), np.float32)
    for at, first in enumerate(heads):
        for half in range(2):
            for i in range(HALF):
                matrix[first + half * HALF + i, at * PAD + half * (PAD // 2) + i] = 1.0
    return matrix


def turn(x, cosine, sine):
    return x * cosine + pltpu.roll(x, PAD // 2, 1) * sine


def rows_at(t, size):
    return pl.ds(pl.multiple_of(t * size, size), size)


def forward_kernel(pieces, ratio, *refs):
    place, low, full, cosine, sine, start, spread_in, gather_out = refs[:8]
    heads = spread_in.shape[0]
    refs = refs[8:]
    qkv, context, refs = refs[0], refs[1 : 1 + pieces], refs[1 + pieces :]
    log_sum, refs = refs[:heads], refs[heads:]
    q_s, k_s, v_s, s_s, top_s, acc = refs
    tiles = q_s.shape[0]
    all_subs = qkv.shape[0] // SUB
    piece_subs = all_subs // pieces
    scale = LOG2E * HD ** (-0.5)
    ones_lane = lax.broadcasted_iota(jnp.int32, (SUB, PAD), 1) == PAD - 1

    def prepare(r, carry):
        t = place[r]
        at = rows_at(t, SUB)
        cos_t, sin_t = cosine[at, :], sine[at, :]
        tile, half = t // (TILE // SUB), t % (TILE // SUB)
        for g in range(heads):
            wide = dot32(qkv[rows_at(r, SUB), :], spread_in[g])
            for h in range(ratio):
                query = turn(wide[:, h * PAD : (h + 1) * PAD], cos_t, sin_t) * scale
                first = pl.multiple_of(h * TILE + half * SUB, SUB)
                q_s[tile, g, pl.ds(first, SUB), :] = query.astype(jnp.bfloat16)
            key = turn(wide[:, ratio * PAD : (ratio + 1) * PAD], cos_t, sin_t)
            k_s[g, at, :] = key.astype(jnp.bfloat16)
            value = jnp.where(ones_lane, 1.0, wide[:, (ratio + 1) * PAD :])
            v_s[g, at, :] = value.astype(jnp.bfloat16)
        return carry

    lax.fori_loop(0, all_subs, prepare, 0)

    def query_tile(i, carry):
        starts = jnp.concatenate([start[rows_at(i, TILE), :]] * ratio, axis=0)
        top_s[...] = jnp.full_like(top_s, MASKED)

        def scores(j, masked, diagonal):
            for g in range(heads):
                s = times_transpose(q_s[i, g], k_s[g, rows_at(j, TILE), :])
                if masked:
                    key_at = lax.broadcasted_iota(jnp.int32, s.shape, 1)
                    allowed = key_at + j * TILE >= starts
                    if diagonal:
                        query_at = lax.rem(lax.broadcasted_iota(jnp.int32, s.shape, 0), TILE)
                        allowed = allowed & (key_at <= query_at)
                    s = jnp.where(allowed, s, MASKED)
                s_s[g, j] = s
                peak = s[:, :PAD]
                for c in range(1, TILE // PAD):
                    peak = jnp.maximum(peak, s[:, c * PAD : (c + 1) * PAD])
                top_s[g] = jnp.maximum(top_s[g], peak)

        def loop(first, last, masked):
            def run(j, c):
                scores(j, masked, False)
                return c

            lax.fori_loop(first, last, run, 0)

        loop(low[i], full[i], True)
        loop(full[i], i, False)
        scores(i, True, True)
        tops = [jnp.max(top_s[g], axis=1, keepdims=True) for g in range(heads)]
        acc[...] = jnp.zeros_like(acc)

        def weigh(j, c):
            for g in range(heads):
                p = jnp.exp2(s_s[g, j] - tops[g]).astype(jnp.bfloat16)
                acc[g] += dot32(p, v_s[g, rows_at(j, TILE), :])
            return c

        lax.fori_loop(low[i], i + 1, weigh, 0)
        packed = None
        for g in range(heads):
            total = acc[g][:, PAD - 1 :]
            out = acc[g] * (1.0 / total)
            sums = jnp.broadcast_to(tops[g] + jnp.log(total) * LOG2E, (ratio * TILE, PAD))
            log_sum[g][i] = sums.T[:1, :]
            wide = jnp.concatenate(
                [out[h * TILE : (h + 1) * TILE, :] for h in range(ratio)], axis=1
            ).astype(jnp.bfloat16)
            part = dot32(wide, gather_out[g])
            packed = part if packed is None else packed + part
        subs = tiles * (TILE // SUB)
        for half in range(TILE // SUB):
            r = place[subs + i * (TILE // SUB) + half]
            part = packed[half * SUB : (half + 1) * SUB, :].astype(jnp.bfloat16)
            for k in range(pieces):

                @pl.when(r // piece_subs == k)
                def store(k=k, part=part, r=r):
                    context[k][rows_at(r % piece_subs, SUB), :] = part

        return carry

    lax.fori_loop(0, tiles, query_tile, 0)


def backward_kernel(pieces, ratio, more, *refs):
    place, low, full, cosine, sine, start, refs = *refs[:6], refs[6:]
    heads = refs[0].shape[0]
    spread_in, spread_out, gather_in, refs = *refs[:3], refs[3:]
    log_sum, refs = refs[:heads], refs[heads:]
    d_context, context, qkv, refs = refs[:pieces], refs[pieces : 2 * pieces], refs[2 * pieces], refs[2 * pieces + 1 :]
    earlier, refs = (refs[0], refs[1:]) if more else (None, refs)
    d_qkv, refs = refs[0], refs[1:]
    q_s, k_s, kt_s, v_s, do_s, delta_s, log_s, dq_acc, dk_acc, dv_acc, dq_s = refs
    tiles = q_s.shape[0]
    all_subs = qkv.shape[0] // SUB
    piece_subs = all_subs // pieces
    scale = HD ** (-0.5)
    per_tile = TILE // SUB

    for k in range(pieces):

        def prepare(r, carry, k=k):
            t = place[k * piece_subs + r]
            rel = rows_at(r, SUB)
            at = rows_at(t, SUB)
            cos_t, sin_t = cosine[at, :], sine[at, :]
            for g in range(heads):
                wide = dot32(qkv[rows_at(k * piece_subs + r, SUB), :], spread_in[g])
                d_out = dot32(d_context[k][rel, :], spread_out[g])
                out = dot32(context[k][rel, :], spread_out[g])
                for h in range(ratio):
                    cols = slice(h * PAD, (h + 1) * PAD)
                    rows = slice(h * SUB, (h + 1) * SUB)
                    query = turn(wide[:, cols], cos_t, sin_t) * (scale * LOG2E)
                    q_s[t, g, rows, :] = query.astype(jnp.bfloat16)
                    do_s[t, g, rows, :] = d_out[:, cols].astype(jnp.bfloat16)
                    delta = jnp.sum((d_out[:, cols] * out[:, cols]).T, axis=0, keepdims=True)
                    delta_s[t * heads + g, :, rows] = delta
                    first = pl.multiple_of(h * TILE + t % per_tile * SUB, SUB)
                    log_s[t * heads + g, :, rows] = log_sum[g][t // per_tile, :, pl.ds(first, SUB)]
                key = turn(wide[:, ratio * PAD : (ratio + 1) * PAD], cos_t, sin_t)
                k_s[g, t] = key.astype(jnp.bfloat16)
                kt_s[g, t] = key.T.astype(jnp.bfloat16)
                v_s[g, t] = wide[:, (ratio + 1) * PAD :].astype(jnp.bfloat16)
                dk_acc[g, t] = jnp.zeros((SUB, PAD), jnp.float32)
                dv_acc[g, t] = jnp.zeros((SUB, PAD), jnp.float32)
            return carry

        lax.fori_loop(0, piece_subs, prepare, 0)

    def query_tile(i, carry):
        dq_acc[...] = jnp.zeros_like(dq_acc)

        def step(j, masked, diagonal):
            for g in range(heads):
                queries, d_out = q_s[i, g], do_s[i, g]
                s = times_transpose(k_s[g, j], queries)
                if masked:
                    key_at = lax.broadcasted_iota(jnp.int32, s.shape, 0)
                    allowed = key_at + j * SUB >= start[i]
                    if diagonal:
                        query_at = lax.rem(lax.broadcasted_iota(jnp.int32, s.shape, 1), SUB)
                        allowed = allowed & (key_at <= query_at)
                    s = jnp.where(allowed, s, MASKED)
                p = jnp.exp2(s - log_s[i * heads + g])
                d_p = times_transpose(v_s[g, j], d_out)
                d_s = (p * (d_p - delta_s[i * heads + g])).astype(jnp.bfloat16)
                dv_acc[g, j] += dot32(p.astype(jnp.bfloat16), d_out)
                dk_acc[g, j] += dot32(d_s, queries)
                dq_acc[g] += dot32(kt_s[g, j], d_s)

        def loop(first, last, masked):
            def run(j, c):
                step(j, masked, False)
                return c

            lax.fori_loop(first, last, run, 0)

        loop(low[i], full[i], True)
        loop(full[i], i, False)
        step(i, True, True)
        at = rows_at(i, SUB)
        cos_t, sin_t = cosine[at, :], sine[at, :]
        for g in range(heads):
            grad = dq_acc[g].T * scale
            for h in range(ratio):
                piece = turn(grad[h * SUB : (h + 1) * SUB, :], cos_t, -sin_t)
                dq_s[g, i, :, h * PAD : (h + 1) * PAD] = piece.astype(jnp.bfloat16)
        return carry

    lax.fori_loop(0, tiles, query_tile, 0)

    def finish(r, carry):
        t = place[r]
        at = rows_at(t, SUB)
        rel = rows_at(r, SUB)
        packed = None
        for g in range(heads):
            key = turn(dk_acc[g, t] * (1.0 / LOG2E), cosine[at, :], -sine[at, :])
            wide = jnp.concatenate(
                [dq_s[g, t], key.astype(jnp.bfloat16), dv_acc[g, t].astype(jnp.bfloat16)], axis=1
            )
            part = dot32(wide, gather_in[g])
            packed = part if packed is None else packed + part
        packed = packed.astype(jnp.bfloat16)
        d_qkv[rel, :] = packed + earlier[rel, :] if more else packed
        return carry

    lax.fori_loop(0, all_subs, finish, 0)


SMEM = pl.BlockSpec(memory_space=pltpu.SMEM)
VMEM = pl.BlockSpec(memory_space=pltpu.VMEM)
ANY = pl.BlockSpec(memory_space=pl.ANY)


def small_cost(transcendentals=0):
    return pl.CostEstimate(flops=1 << 20, bytes_accessed=1 << 16, transcendentals=transcendentals)


def head_matrices(head, q_heads, kv_heads):
    ratio = q_heads // kv_heads
    queries = [(head * ratio + r) * HD for r in range(ratio)]
    key, value = (q_heads + head) * HD, (q_heads + kv_heads + head) * HD
    inner = spread((q_heads + 2 * kv_heads) * HD, [*queries, key, value])
    outer = spread(q_heads * HD, queries)
    return jnp.asarray(inner, jnp.bfloat16), jnp.asarray(outer, jnp.bfloat16)


def stacked_matrices(q_heads, kv_heads):
    pairs = [head_matrices(head, q_heads, kv_heads) for head in range(kv_heads)]
    return jnp.stack([inner for inner, _ in pairs]), jnp.stack([outer for _, outer in pairs])


def attend(qkv, pieces, layout, q_heads, kv_heads):
    place, low, full, cosine, sine, start_column = layout
    ratio, rows = q_heads // kv_heads, qkv.shape[0]
    tiles, lanes = rows // TILE, ratio * TILE
    bf16, f32 = jnp.bfloat16, jnp.float32
    inner, outer = stacked_matrices(q_heads, kv_heads)
    outs = pl.pallas_call(
        functools.partial(forward_kernel, pieces, ratio),
        out_shape=[
            *[jax.ShapeDtypeStruct((rows // pieces, q_heads * HD), bf16)] * pieces,
            *[jax.ShapeDtypeStruct((tiles, 1, lanes), f32)] * kv_heads,
        ],
        in_specs=[SMEM] * 3 + [VMEM] * 6,
        out_specs=[VMEM] * (pieces + kv_heads),
        scratch_shapes=[
            pltpu.VMEM((tiles, kv_heads, lanes, PAD), bf16),
            pltpu.VMEM((kv_heads, rows, PAD), bf16),
            pltpu.VMEM((kv_heads, rows, PAD), bf16),
            pltpu.VMEM((kv_heads, tiles, lanes, TILE), f32),
            pltpu.VMEM((kv_heads, lanes, PAD), f32),
            pltpu.VMEM((kv_heads, lanes, PAD), f32),
        ],
        compiler_params=pltpu.CompilerParams(vmem_limit_bytes=60 * 2**20),
        cost_estimate=small_cost(),
        name="attention_forward",
    )(place, low, full, cosine, sine, start_column, inner, jnp.swapaxes(outer, 1, 2), qkv)
    return outs[:pieces], outs[pieces:]


def attend_back(heads, qkv, d_context, context, sums, earlier, layout, q_heads, kv_heads):
    place, low, full, cosine, sine, start_row = layout
    pieces, ratio, rows = len(context), q_heads // kv_heads, qkv.shape[0]
    tiles, lanes, count = rows // SUB, ratio * SUB, len(heads)
    bf16, f32 = jnp.bfloat16, jnp.float32
    inner, outer = stacked_matrices(q_heads, kv_heads)
    inner, outer = inner[heads[0] : heads[0] + count], outer[heads[0] : heads[0] + count]
    return pl.pallas_call(
        functools.partial(backward_kernel, pieces, ratio, bool(earlier)),
        out_shape=jax.ShapeDtypeStruct(qkv.shape, bf16),
        in_specs=[SMEM] * 3 + [VMEM] * (7 + count + 2 * pieces + len(earlier)),
        out_specs=VMEM,
        scratch_shapes=[
            pltpu.VMEM((tiles, count, lanes, PAD), bf16),
            pltpu.VMEM((count, tiles, SUB, PAD), bf16),
            pltpu.VMEM((count, tiles, PAD, SUB), bf16),
            pltpu.VMEM((count, tiles, SUB, PAD), bf16),
            pltpu.VMEM((tiles, count, lanes, PAD), bf16),
            pltpu.VMEM((tiles * count, 1, lanes), f32),
            pltpu.VMEM((tiles * count, 1, lanes), f32),
            pltpu.VMEM((count, PAD, lanes), f32),
            pltpu.VMEM((count, tiles, SUB, PAD), f32),
            pltpu.VMEM((count, tiles, SUB, PAD), f32),
            pltpu.VMEM((count, tiles, SUB, ratio * PAD), bf16),
        ],
        compiler_params=pltpu.CompilerParams(vmem_limit_bytes=60 * 2**20),
        cost_estimate=small_cost(),
        name=f"attention_backward_{heads[0]}",
    )(
        place, low, full, cosine, sine, start_row, inner, outer, jnp.swapaxes(inner, 1, 2),
        *[sums[h] for h in heads], *d_context, *context, qkv, *earlier,
    )


def fetch(me, where, sources, target, sems):
    copies = []
    for n, (source, (j, deep, first, column, taken)) in enumerate(zip(sources, where, strict=True)):
        cols = min(source.shape[1] - taken, target.shape[1] - column)
        at = pl.ds(pl.multiple_of((me[0] ^ j) * deep + first, 16), source.shape[0])
        if cols != source.shape[1]:
            source = source.at[:, taken : taken + cols]
        copies.append(pltpu.make_async_copy(source, target.at[at, column : column + cols], sems.at[n]))
    return copies


def take_part(parts, target):
    for n, part in enumerate(parts):

        @pl.when(pl.program_id(0) == n)
        def take(part=part):
            target[...] = part[...]


def at_first_step(copies, what):
    @pl.when(pl.program_id(0) == 0)
    def run():
        for copy in copies:
            what(copy)


def project_kernel(where, more, me, *refs):
    parts, gain, refs = refs[:PARTS], refs[PARTS], refs[PARTS + 1 :]
    sources, refs = refs[: len(where[0])], refs[len(where[0]) :]
    norm_all, qkv_all, weight, sems, rows_s = refs[2 if more else 0 :]
    copies = fetch(me, where[0], sources, weight, sems)
    at_first_step(copies, lambda copy: copy.start())
    take_part(parts, rows_s)
    x = rows_s[...].astype(jnp.float32)
    scale = lax.rsqrt(jnp.mean(x * x, axis=-1, keepdims=True) + EPSILON)
    norm_all[...] = (x * scale * gain[...]).astype(jnp.bfloat16)
    at_first_step(copies, lambda copy: copy.wait())
    qkv_all[...] = dot32(norm_all[...], weight[...]).astype(jnp.bfloat16)


def gate_kernel(where, more, me, *refs):
    parts, refs = refs[:PARTS], refs[PARTS:]
    sources, refs = refs[: len(where[0])], refs[len(where[0]) :]
    norm_all, gate_up_all, hidden_all, weight, sems = refs[3 if more else 0 :]
    hidden_cols = hidden_all.shape[1]
    copies = fetch(me, where[0], sources, weight, sems)
    at_first_step(copies, lambda copy: copy.start())
    take_part(parts, norm_all)
    at_first_step(copies, lambda copy: copy.wait())
    x = norm_all[...]
    width = min(512, hidden_cols)
    for at in range(0, hidden_cols, width):
        gate_at = slice(at, at + width)
        up_at = slice(hidden_cols + at, hidden_cols + at + width)
        gate = dot32(x, weight[:, gate_at])
        up = dot32(x, weight[:, up_at])
        gate_up_all[:, gate_at] = gate
        gate_up_all[:, up_at] = up
        hidden_all[:, gate_at] = (gate * (1.0 / (1.0 + jnp.exp(-gate))) * up).astype(jnp.bfloat16)


def gate_back_kernel(where, more, me, *refs):
    parts, gate_up_all, hidden_other, refs = refs[:PARTS], *refs[PARTS : PARTS + 2], refs[PARTS + 2 :]
    gate_up, refs = refs[: len(where[0])], refs[len(where[0]) :]
    down, refs = refs[: len(where[1])], refs[len(where[1]) :]
    refs = refs[2 if more else 0 :]
    grad_all, d_gate_up_all, d_norm_own, d_norm_sib, out_own, out_sib = refs[:6]
    w_gate_up, gate_up_sems, w_down, down_sems = refs[6:]
    hidden_cols = w_down.shape[1]
    down_copies = fetch(me, where[1], down, w_down, down_sems)
    copies = fetch(me, where[0], gate_up, w_gate_up, gate_up_sems)
    at_first_step(down_copies + copies, lambda copy: copy.start())
    take_part(parts, grad_all)
    at_first_step(down_copies, lambda copy: copy.wait())
    dy = grad_all[...]
    width = min(512, hidden_cols)
    for at in range(0, hidden_cols, width):
        gate_at = slice(at, at + width)
        up_at = slice(hidden_cols + at, hidden_cols + at + width)
        d_hidden = dot32(dy, w_down[:, gate_at])
        gate, up = gate_up_all[:, gate_at], gate_up_all[:, up_at]
        sigmoid = 1.0 / (1.0 + jnp.exp(-gate))
        d_gate = d_hidden * up * sigmoid * (1.0 + gate * (1.0 - sigmoid))
        d_gate_up_all[:, gate_at] = d_gate.astype(jnp.bfloat16)
        d_gate_up_all[:, up_at] = (d_hidden * (gate * sigmoid)).astype(jnp.bfloat16)
    out = times_transpose(hidden_other[...], w_down[...]).astype(jnp.bfloat16)
    at_first_step(copies, lambda copy: copy.wait())
    d_norm = times_transpose(d_gate_up_all[...], w_gate_up[...]).astype(jnp.bfloat16)

    @pl.when(pl.program_id(0) < PARTS // 2)
    def to_own():
        d_norm_own[...] = d_norm
        out_own[...] = out

    @pl.when(pl.program_id(0) >= PARTS // 2)
    def to_sibling():
        d_norm_sib[...] = d_norm
        out_sib[...] = out


def piece_call(kernel, name, k, pieces, me, parts, whole, tiled, fetched, earlier, outs):
    tile = min(x.shape[0] for x in parts) // (1 if len(parts) == PARTS else 2)
    width = parts[0].shape[1]
    own_rows = tile * PARTS // 2
    parts = [(x, n) for x in parts for n in range(x.shape[0] // tile)]
    maps = {
        "own": lambda i: (jnp.minimum(i, PARTS // 2 - 1), 0),
        "sibling": lambda i: (jnp.maximum(i - PARTS // 2, 0), 0),
    }

    def rows_of(piece):
        return lambda i: (piece * PARTS + i, 0)

    sources = [x for arrays, _, _ in fetched for x in arrays]
    first_earlier = 1 + PARTS + len(whole) + len(tiled) + len(sources)
    scratch = []
    for arrays, _, cols in fetched:
        scratch += [pltpu.VMEM((width, cols), jnp.bfloat16), pltpu.SemaphoreType.DMA((len(arrays),))]
    if kernel is project_kernel:
        scratch.append(pltpu.VMEM((tile, width), jnp.bfloat16))
    return pl.pallas_call(
        functools.partial(kernel, tuple(where for _, where, _ in fetched), bool(earlier)),
        grid=(PARTS,),
        out_shape=[
            jax.ShapeDtypeStruct((pieces * 2 * own_rows if span == "all" else own_rows, columns), kind)
            for columns, kind, span in outs
        ],
        in_specs=[
            SMEM,
            *(pl.BlockSpec((tile, width), functools.partial(lambda n, i: (n, 0), n)) for _, n in parts),
            *(pl.BlockSpec(x.shape, lambda i: (0, 0)) for x in whole),
            *(pl.BlockSpec((tile, x.shape[1]), rows_of(piece)) for x, piece in tiled),
            *[ANY] * (len(sources) + len(earlier)),
        ],
        out_specs=[
            pl.BlockSpec((tile, columns), rows_of(k) if span == "all" else maps[span])
            for columns, kind, span in outs
        ],
        scratch_shapes=scratch,
        input_output_aliases={first_earlier + n: n for n in range(len(earlier))},
        compiler_params=pltpu.CompilerParams(vmem_limit_bytes=60 * 2**20),
        cost_estimate=small_cost(),
        name=f"{name}_{k}",
    )(me, *(x for x, _ in parts), *whole, *(x for x, _ in tiled), *sources, *earlier)


def assemble_kernel(where, me, *refs):
    sources, whole, sems = refs[: len(where)], refs[len(where)], refs[len(where) + 1]
    copies = fetch(me, where, sources, whole, sems)
    for copy in copies:
        copy.start()
    for copy in copies:
        copy.wait()


def assemble(name, me, arrays, where, rows, cols):
    return pl.pallas_call(
        functools.partial(assemble_kernel, where),
        out_shape=jax.ShapeDtypeStruct((rows, cols), arrays[0].dtype),
        in_specs=[SMEM, *[ANY] * len(arrays)],
        out_specs=VMEM,
        scratch_shapes=[pltpu.SemaphoreType.DMA((len(arrays),))],
        compiler_params=pltpu.CompilerParams(vmem_limit_bytes=60 * 2**20),
        cost_estimate=small_cost(),
        name=name,
    )(me, *arrays)


def flip(x, axis):
    return lax.ppermute(x, axis, FLIP)


CROSS = [(1, 2), (2, 1)]
OUT = [(0, 1), (3, 2), (2, 0), (1, 3)]
BACK = [(1, 0), (2, 3), (0, 2), (3, 1)]


def crossed(x, perm):
    return lax.ppermute(x, ("core", "zh"), perm)


def straight():
    return lax.axis_index("core") == lax.axis_index("zh")


def swap(x):
    return jnp.where(straight(), x, crossed(x, CROSS))


def send_z(w):
    return crossed(w, OUT), crossed(w, CROSS)


def pair_of(w, out, cross):
    zh = lax.axis_index("zh")
    x = jnp.where(straight(), w, cross)
    return jnp.concatenate([jnp.where(zh == 0, x, out), jnp.where(zh == 0, out, x)], axis=0)


def give_z(part):
    zh = lax.axis_index("zh")
    half = part.shape[0] // 2
    upper, lower = part[:half], part[half:]
    return jnp.where(zh == 0, upper, lower), jnp.where(zh == 0, lower, upper)


def sum_z(keep, back, cross):
    return back.astype(jnp.float32) + jnp.where(straight(), keep, cross).astype(jnp.float32)


def shift(x, e, k):
    n = lax.axis_size("zl")
    return lax.ppermute(
        x, ("core", "zl"), [(c * n + l, (c ^ e) * n + (l + k) % n) for c in range(2) for l in range(n)]
    )


def from_near(x, k):
    n = lax.axis_size("zl")
    return lax.ppermute(x, "zl", [((j + k) % n, j) for j in range(n)])


def to_near(x, k):
    n = lax.axis_size("zl")
    return lax.ppermute(x, "zl", [(j, (j + k) % n) for j in range(n)])


def across(x, j):
    n = lax.axis_size("yx")
    return lax.ppermute(x, "yx", [(a, a ^ j) for a in range(n)])


def neighbours(x):
    count = lax.axis_size("yx")
    return [across(x, j) for j in range(1, count if count != 4 else 3)]


def diagonal(taken):
    if lax.axis_size("yx") != 4:
        return []
    half = taken[0].shape[0] // 2
    return [across(taken[1][:half], 1), across(taken[0][half:], 2)]


def blocks_of(own, taken, halves, column=0, source_column=0):
    deep = own.shape[0]
    arrays = [own, *taken, *halves]
    where = [(j, deep, 0, column, source_column) for j in range(1 + len(taken))]
    where += [(3, deep, n * deep // 2, column, source_column) for n in range(len(halves))]
    return arrays, tuple(where)


def whole_weight(w):
    return [w], ((0, 0, 0, 0, 0),)


def block_of(grad, j, columns):
    size = grad.shape[0] // lax.axis_size("yx")
    first = (lax.axis_index("yx") ^ j) * size
    return lax.dynamic_slice(grad, (first, columns[0]), (size, columns[1] - columns[0]))


def send_yx(grad, columns):
    count = lax.axis_size("yx")
    if count != 4:
        return [across(block_of(grad, j, columns), j) for j in range(1, count)]
    far = block_of(grad, 3, columns)
    half = far.shape[0] // 2
    return [across(far[:half], 1), across(far[half:], 2)]


def join_yx(grad, columns, taken):
    if lax.axis_size("yx") != 4:
        return taken, block_of(grad, 0, columns)
    half = taken[0].shape[0]
    one, two = block_of(grad, 1, columns), block_of(grad, 2, columns)
    one = jnp.concatenate([one[:half], one[half:] + taken[1]], axis=0)
    two = jnp.concatenate([two[:half] + taken[0], two[half:]], axis=0)
    return [across(one, 1), across(two, 2)], block_of(grad, 0, columns)


def total_yx(taken, own):
    total = own.astype(jnp.float32)
    for part in taken:
        total = total + part.astype(jnp.float32)
    return total.astype(jnp.bfloat16)


def body(
    tokens,
    cotangent,
    seq_lengths,
    attn_gain,
    q_weight,
    key_projection,
    value_projection,
    out_weight,
    mlp_gain,
    gate_weight,
    up_weight,
    down_weight,
):
    bf16, f32 = jnp.bfloat16, jnp.float32
    core, zl, yx = lax.axis_index("core"), lax.axis_index("zl"), lax.axis_index("yx")
    near = lax.axis_size("zl")
    others = range(1, near)
    rows = tokens.shape[0]
    group_rows = 2 * near * rows
    query_cols, key_cols = q_weight.shape[1], key_projection.shape[1]
    qkv_cols = query_cols + 2 * key_cols
    q_heads, kv_heads = query_cols // HD, key_cols // HD
    hidden_cols = gate_weight.shape[1]
    me = yx.astype(jnp.int32).reshape(1)

    qkv_shard = jnp.concatenate([q_weight, key_projection, value_projection], axis=1)
    gate_up_shard = jnp.concatenate([gate_weight, up_weight], axis=1)
    part_rows = rows // 2
    upper = swap(tokens[:part_rows])
    shard = jnp.concatenate([qkv_shard, out_weight], axis=1)
    shard_moved = send_z(shard)
    lengths = swap(seq_lengths)
    gains = lax.all_gather(jnp.stack([attn_gain, mlp_gain]), ("yx", "core"), axis=1, tiled=True).astype(f32)
    upper, lengths, second_part, gains, *shard_moved = stage(upper, lengths, tokens[part_rows:], gains, *shard_moved)
    gain_one, gain_two = gains[0], gains[1]

    upper_far = [from_near(upper, k) for k in others]
    lower = swap(second_part)
    pair = pair_of(shard, *shard_moved)
    taken = neighbours(pair)
    upper_sib = flip(upper, "core")

    subs = jnp.arange(group_rows // SUB, dtype=jnp.int32)
    per_device = rows // SUB
    source, within = subs // per_device, subs % per_device
    there_core, there_zl = (source % 2) ^ core, (source // 2 + zl) % near
    to_order = (there_core * near + there_zl) * per_device + within
    from_order = (((source % near - zl) % near) * 2 + ((source // near) ^ core)) * per_device + within
    place = jnp.concatenate([to_order, from_order])
    row_at, doc_start = document_layout(lengths, group_rows)
    cosine, sine = rotary_tables(row_at - doc_start)

    def bounds(size):
        tile_start = doc_start.reshape(-1, size)
        tile = jnp.arange(group_rows // size, dtype=jnp.int32)
        low = tile_start[:, 0] // size
        return low, jnp.minimum((tile_start[:, -1] + size - 1) // size, tile)

    start_row = jnp.tile(doc_start.reshape(-1, 1, SUB), (1, 1, q_heads // kv_heads))
    layout = (place, *bounds(TILE), cosine, sine, doc_start[:, None])
    layout_back = (place, *bounds(SUB), cosine, sine, start_row)
    lower, upper_sib, *moved = stage(lower, upper_sib, *upper_far, *taken, *layout, *layout_back)
    upper_far, moved = moved[: near - 1], moved[near - 1 :]
    taken, moved = moved[: len(taken)], moved[len(taken) :]
    layout, layout_back = moved[: len(layout)], moved[len(layout) :]

    lower_far = [from_near(lower, k) for k in others]
    lower_sib = flip(lower, "core")
    out_pair = pair[:, qkv_cols:]
    out_far = [from_near(out_pair, k) for k in others]
    blocks = blocks_of(pair, taken, diagonal(taken))
    projecting = [(*blocks, qkv_cols)]
    gain_row = gain_one[None]
    outs = [(tokens.shape[1], bf16, "all"), (qkv_cols, bf16, "all")]
    parts = [upper, lower, upper_sib, lower_sib]
    normed = piece_call(project_kernel, "project", 0, near, me, parts, [gain_row], [], projecting, [], outs)
    gate_up_shard, *moved = stage(gate_up_shard, *lower_far, *out_far, *normed)
    lower_far, out_far, normed = moved[: near - 1], moved[near - 1 : 2 * near - 2], moved[2 * near - 2 :]

    out_taken = [neighbours(far) for far in out_far]
    step = len(out_taken[0])
    for k in others:
        parts = [upper_far[k - 1], lower_far[k - 1], flip(upper_far[k - 1], "core"), flip(lower_far[k - 1], "core")]
        normed = piece_call(project_kernel, "project", k, near, me, parts, [gain_row], [], projecting, normed, outs)
    norm_one, qkv = normed
    gate_up_shard, qkv, *moved = stage(gate_up_shard, qkv, *(x for t in out_taken for x in t))
    out_taken = [moved[n * step : (n + 1) * step] for n in range(near - 1)]

    gate_up_moved = send_z(gate_up_shard)
    out_halves = [x for t in out_taken for x in diagonal(t)]
    context, sums = attend(qkv, 2 * near, layout, q_heads, kv_heads)
    down_shard, *moved = stage(down_weight, *context, *gate_up_moved, *out_halves)
    context, gate_up_moved, out_halves = moved[: 2 * near], moved[2 * near : 2 * near + 2], moved[2 * near + 2 :]

    quarters = {(0, 0): context[0]}
    moves = [(e, k) for k in range(near) for e in range(2)]
    for e, k in moves[1:-1]:
        quarters[e, (near - k) % near] = shift(context[2 * k + e], e, k)
    pairs = [
        pair_of(*(x[:, n * hidden_cols : (n + 1) * hidden_cols] for x in (gate_up_shard, *gate_up_moved)))
        for n in range(2)
    ]
    gate_taken = neighbours(pairs[0])
    order = list(quarters)
    last, up_pair, down_shard, *moved = stage(
        context[-1], pairs[1], down_shard, *quarters.values(), *gate_taken, *out_halves
    )
    quarters, moved = dict(zip(order, moved[: len(order)], strict=True)), moved[len(order) :]
    gate_taken, out_halves = moved[: len(gate_taken)], moved[len(gate_taken) :]

    e, k = moves[-1]
    quarters[e, (near - k) % near] = shift(last, e, k)
    up_taken = neighbours(up_pair)
    down_moved = send_z(down_shard)
    step = len(out_halves) // max(near - 1, 1)
    parts = [blocks_of(blocks[0][0], blocks[0][1 : 1 + len(taken)], blocks[0][1 + len(taken) :], 0, qkv_cols)]
    together = query_cols % 128 == 0
    for n, (x, t) in enumerate(zip(out_far, out_taken, strict=True)):
        parts.append(blocks_of(x, t, out_halves[n * step : (n + 1) * step], (n + 1) * query_cols if together else 0))
    if together:
        arrays, where = [x for some, _ in parts for x in some], tuple(w for _, some in parts for w in some)
        w_out_near = assemble("assemble_out", me, arrays, where, tokens.shape[1], near * query_cols)
    else:
        w_out_near = jnp.concatenate(
            [assemble(f"assemble_out_{n}", me, *some, tokens.shape[1], query_cols) for n, some in enumerate(parts)],
            axis=1,
        )
    w_out_sib = flip(w_out_near, "core")
    residual = jnp.concatenate([upper, lower], axis=0).astype(f32)
    scale_one = lax.rsqrt(jnp.mean(residual * residual, axis=-1, keepdims=True) + EPSILON)
    order = [(e, k) for e in range(2) for k in range(near)]
    w_out_sib, w_out_near, scale_one, cotangent, *moved = stage(
        w_out_sib, w_out_near, scale_one, cotangent, *[quarters[at] for at in order], *up_taken, *down_moved
    )
    quarters, up_taken, down_moved = moved[: 2 * near], moved[2 * near : -2], moved[-2:]

    gate_halves = diagonal(gate_taken)
    own_context = jnp.concatenate(quarters[:near], axis=1)
    sib_context = jnp.concatenate(quarters[near:], axis=1)
    mid = residual + times_transpose(own_context, w_out_near) + times_transpose(sib_context, w_out_sib)
    scale_two, norm_two = norm_rows(mid, gain_two)
    norm_two, cotangent, *gate_halves = stage(norm_two, cotangent, *gate_halves)

    upper_far = [from_near(norm_two[:part_rows], k) for k in others]
    up_halves = diagonal(up_taken)
    norm_sib = flip(norm_two, "core")
    cot_upper = crossed(cotangent[:part_rows], CROSS)
    w_down = lax.all_gather(pair_of(down_shard, *down_moved), "yx", axis=0, tiled=True)
    w_project = assemble("assemble_project", me, *blocks, tokens.shape[1], qkv_cols)
    norm_two, cotangent, cot_upper, norm_sib, w_project, *moved = stage(
        norm_two, cotangent, cot_upper, norm_sib, w_project, *upper_far, *up_halves
    )
    upper_far, up_halves = moved[: near - 1], moved[near - 1 :]

    lower_far = [from_near(norm_two[part_rows:], k) for k in others]
    upper_far_sib = [flip(x, "core") for x in upper_far]
    cot_lower = crossed(cotangent[part_rows:], CROSS)
    cot_upper = jnp.where(straight(), cotangent[:part_rows], cot_upper)
    cot_upper_sib = flip(cot_upper, "core")
    gate_blocks = blocks_of(pairs[0], gate_taken, gate_halves)
    up_blocks = blocks_of(up_pair, up_taken, up_halves, hidden_cols)
    gate_up = ([*gate_blocks[0], *up_blocks[0]], gate_blocks[1] + up_blocks[1], 2 * hidden_cols)
    outs = [(norm_two.shape[1], bf16, "all"), (2 * hidden_cols, f32, "all"), (hidden_cols, bf16, "all")]
    earlier = piece_call(gate_kernel, "gate", 0, near, me, [norm_two, norm_sib], [], [], [gate_up], [], outs)
    cot_lower, cot_upper, cot_upper_sib, *moved = stage(
        cot_lower, cot_upper, cot_upper_sib, *lower_far, *upper_far_sib, *earlier
    )
    lower_far, upper_far_sib, earlier = moved[: near - 1], moved[near - 1 : 2 * near - 2], moved[2 * near - 2 :]

    cot_upper_far = [from_near(cot_upper, k) for k in others]
    cot_lower = jnp.where(straight(), cotangent[part_rows:], cot_lower)
    cot_lower_sib = flip(cot_lower, "core")
    for k in others:
        parts = [upper_far[k - 1], lower_far[k - 1], upper_far_sib[k - 1], flip(lower_far[k - 1], "core")]
        earlier = piece_call(gate_kernel, "gate", k, near, me, parts, [], [], [gate_up], earlier, outs)
    cot_lower, cot_lower_sib, w_down, *moved = stage(cot_lower, cot_lower_sib, w_down, *cot_upper_far, *earlier)
    cot_upper_far, earlier = moved[: near - 1], moved[near - 1 :]
    norm_two_all, gate_up_all, hidden_all = earlier

    cot_lower_far = [from_near(cot_lower, k) for k in others]
    cot_upper_far_sib = [flip(x, "core") for x in cot_upper_far]
    down = (*whole_weight(w_down), hidden_cols)
    width = norm_two.shape[1]
    outs = [(width, bf16, "all"), (2 * hidden_cols, bf16, "all")]
    outs += [(width, bf16, "own"), (width, bf16, "sibling")] * 2

    def way_back(k, parts, earlier):
        tiled = [(gate_up_all, k), (hidden_all, (k + 1) % near)]
        return piece_call(gate_back_kernel, "gate_back", k, near, me, parts, [], tiled, [gate_up, down], earlier, outs)

    def joined(own, sib):
        return own.astype(f32) + flip(sib, "core").astype(f32)

    grad_all, d_gate_up_all, *near_back = way_back(0, [cot_upper, cot_lower, cot_upper_sib, cot_lower_sib], [])
    grad_all, d_gate_up_all, *moved = stage(
        grad_all, d_gate_up_all, *near_back, *cot_lower_far, *cot_upper_far_sib
    )
    near_back, cot_lower_far, cot_upper_far_sib = moved[:4], moved[4 : near + 3], moved[near + 3 :]

    out_sum = joined(*near_back[2:]).astype(bf16)
    cot_lower_far_sib = [flip(x, "core") for x in cot_lower_far]
    out_sum, *cot_lower_far_sib = stage(out_sum, *cot_lower_far_sib)
    out_upper = to_near(out_sum[:part_rows], 1 % near)
    back = []
    for k in others:
        parts = [cot_upper_far[k - 1], cot_lower_far[k - 1], cot_upper_far_sib[k - 1], cot_lower_far_sib[k - 1]]
        grad_all, d_gate_up_all, *more = way_back(k, parts, [grad_all, d_gate_up_all])
        back.append(more)
    grad_all, d_gate_up_all, out_upper, *far_back = stage(
        grad_all, d_gate_up_all, out_upper, *(x for more in back for x in more)
    )
    d_norm_sent = [joined(*far_back[4 * n : 4 * n + 2]).astype(bf16) for n in range(near - 1)]
    out_far_back = [far_back[4 * n + 2 : 4 * n + 4] for n in range(near - 1)]
    grad_all, d_gate_up_all, near_own, near_sib, *d_norm_sent = stage(
        grad_all, d_gate_up_all, *near_back[:2], *d_norm_sent
    )

    moved_upper = [to_near(d_norm_sent[k - 1][:part_rows], k) for k in others]
    grad_gate_up = rows_product(norm_two_all, d_gate_up_all).astype(bf16)
    grad_gate_up, grad_all, near_own, near_sib, *moved = stage(
        grad_gate_up, grad_all, near_own, near_sib, *moved_upper, *d_norm_sent
    )
    moved_upper, d_norm_sent = moved[: near - 1], moved[near - 1 :]

    moved_lower = [to_near(d_norm_sent[k - 1][part_rows:], k) for k in others]
    gate_up_part = lax.psum_scatter(grad_gate_up, "yx", scatter_dimension=0, tiled=True)
    d_norm_two = joined(near_own, near_sib)
    grad_down = rows_product(grad_all, hidden_all).astype(bf16)
    grad_down, d_norm_two, out_sum, *moved_lower = stage(grad_down, d_norm_two, out_sum, *moved_lower)

    out_lower = to_near(out_sum[part_rows:], 1 % near)
    down_part = lax.psum_scatter(grad_down, "yx", scatter_dimension=0, tiled=True)
    for one, two in zip(moved_upper, moved_lower, strict=True):
        d_norm_two = d_norm_two + jnp.concatenate([one, two], axis=0).astype(f32)
    own_cotangent = jnp.concatenate([cot_upper, cot_lower], axis=0).astype(f32)
    mid_back, _ = norm_back(mid, scale_two, gain_two, d_norm_two)
    d_mid = own_cotangent + mid_back
    d_attn = d_mid.astype(bf16)
    both = [dot32(d_attn, w).astype(bf16) for w in (w_out_near, w_out_sib)]
    d_quarters = [both[e][:, k * query_cols : (k + 1) * query_cols] for e, k in order]
    d_attn, out_lower, *d_quarters = stage(d_attn, out_lower, *d_quarters)

    d_context = [None] * (2 * near)
    d_context[0] = d_quarters[0]
    for (e, k), x in zip(order[1:-1], d_quarters[1:-1], strict=True):
        d_context[(near - k) % near * 2 + e] = shift(x, e, k)
    (e, k), at_last = order[-1], (near - order[-1][1]) % near * 2 + order[-1][0]
    known = [n for n in range(2 * near) if n != at_last]
    d_attn, last, *moved = stage(d_attn, d_quarters[-1], *(d_context[n] for n in known))
    for n, x in zip(known, moved, strict=True):
        d_context[n] = x

    d_context[at_last] = shift(last, e, k)
    grad_out_sib = flip(rows_product(d_attn, sib_context).astype(bf16), "core")
    grad_out = (rows_product(d_attn, own_context) + grad_out_sib.astype(f32)).astype(bf16)
    output_own = mid + joined(*out_far_back[-1]) + jnp.concatenate([out_upper, out_lower], axis=0).astype(f32)
    for n in range(near - 2):
        output_own = output_own + to_near(joined(*out_far_back[n]).astype(bf16), n + 2).astype(f32)
    output_own = output_own.astype(bf16)
    grad_out, output_own, *d_context = stage(grad_out, output_own, *d_context)

    output_crossed = crossed(output_own, CROSS)
    out_part = lax.psum_scatter(grad_out, "yx", scatter_dimension=0, tiled=True)
    d_qkv = attend_back(list(range(kv_heads)), qkv, d_context, context, sums, [], layout_back, q_heads, kv_heads)
    d_qkv, output_crossed, gate_up_part = stage(d_qkv, output_crossed, gate_up_part)

    def back_part(k):
        own, sib = (d_qkv[(2 * k + e) * rows : (2 * k + e + 1) * rows] for e in range(2))
        taken = flip(times_transpose(sib, w_project).astype(bf16), "core")
        return times_transpose(own, w_project) + taken.astype(f32)

    gate_up_keep, gate_up_give = give_z(gate_up_part)
    gate_up_back = crossed(gate_up_give, BACK)
    d_sent = [back_part(k).astype(bf16) for k in others]
    d_qkv, gate_up_back, gate_up_keep, *d_sent = stage(d_qkv, gate_up_back, gate_up_keep, *d_sent)

    d_upper = [to_near(d_sent[k - 1][:part_rows], k) for k in others]
    gate_up_cross = crossed(gate_up_keep, CROSS)
    grad_project = rows_product(norm_one, d_qkv).astype(bf16)
    project_sent = send_yx(grad_project, (0, qkv_cols))
    total = back_part(0)
    total, grad_project, gate_up_cross, down_part, *moved = stage(
        total, grad_project, gate_up_cross, down_part, *d_upper, *d_sent, *project_sent
    )
    d_upper, d_sent, project_sent = moved[: near - 1], moved[near - 1 : 2 * near - 2], moved[2 * near - 2 :]

    d_lower = [to_near(d_sent[k - 1][part_rows:], k) for k in others]
    project_rest, project_own = join_yx(grad_project, (0, qkv_cols), project_sent)
    down_keep, down_give = give_z(down_part)
    down_home = [crossed(down_give, BACK), crossed(down_keep, CROSS)]

    def input_part(at, moved):
        part = total[at]
        for x in moved:
            part = part + x.astype(f32)
        back, _ = norm_back(residual[at], scale_one[at], gain_one, part)
        return (d_mid[at] + back).astype(bf16)

    input_upper = input_part(slice(0, part_rows), d_upper)
    upper_crossed = crossed(input_upper, CROSS)
    total, input_upper, upper_crossed, out_part, *moved = stage(
        total, input_upper, upper_crossed, out_part, *d_lower, *project_rest, *down_home
    )
    d_lower, project_rest, down_home = moved[: near - 1], moved[near - 1 : -2], moved[-2:]

    project_keep, project_give = give_z(total_yx(project_rest, project_own))
    project_home = [crossed(project_give, BACK), crossed(project_keep, CROSS)]
    input_lower = input_part(slice(part_rows, rows), d_lower)
    lower_crossed = crossed(input_lower, CROSS)
    out_moved = [to_near(out_part[:, k * query_cols : (k + 1) * query_cols], k) for k in others]
    out_quarter = out_part[:, :query_cols].astype(f32)
    for part in out_moved:
        out_quarter = out_quarter + part.astype(f32)
    out_keep, out_give = give_z(out_quarter.astype(bf16))
    out_home = [crossed(out_give, BACK), crossed(out_keep, CROSS)]
    grad_project = sum_z(project_keep, *project_home)
    grad_out = sum_z(out_keep, *out_home)
    grad_down = sum_z(down_keep, *down_home)
    grad_gate_up = sum_z(gate_up_keep, gate_up_back, gate_up_cross)
    output = jnp.where(straight(), output_own, output_crossed)
    input_grad = jnp.concatenate(
        [
            jnp.where(straight(), input_upper, upper_crossed),
            jnp.where(straight(), input_lower, lower_crossed),
        ],
        axis=0,
    ).astype(f32)
    gain_grads = lax.psum(
        jnp.stack(
            [
                jnp.sum(qkv_shard.astype(f32) * grad_project, axis=1),
                jnp.sum(gate_up_shard.astype(f32) * grad_gate_up, axis=1),
            ]
        ),
        ("zh", "zl"),
    ) / jnp.stack([attn_gain, mlp_gain]).astype(f32)
    return (
        output,
        input_grad,
        gain_grads[0],
        grad_project[:, :query_cols],
        grad_project[:, query_cols : query_cols + key_cols],
        grad_project[:, query_cols + key_cols :],
        grad_out,
        gain_grads[1],
        grad_gate_up[:, :hidden_cols],
        grad_gate_up[:, hidden_cols:],
        grad_down,
    )


def solution(mesh):
    dp, tensor = mesh.shape["dp"], mesh.shape["tensor"]
    fine = Mesh(mesh.devices.reshape(dp // 2, 2, 2, tensor // 2), AXES)
    by_rows, by_dp, by_both = P(AXES, None), P(("yx", "core")), P(("yx", "core"), ("zh", "zl"))
    return jax.shard_map(
        body,
        mesh=fine,
        in_specs=(
            by_rows, by_rows, P(("yx", "core"), None), by_dp, by_both, by_both, by_both, by_both,
            by_dp, by_both, by_both, by_both,
        ),
        out_specs=(
            by_rows, by_rows, by_dp, by_both, by_both, by_both, by_both, by_dp, by_both, by_both, by_both,
        ),
        check_vma=False,
    )
```

```python
import functools
import math

import jax
import jax.numpy as jnp
import numpy as np
from jax import lax
from jax.experimental import pallas as pl
from jax.experimental.pallas import tpu as pltpu
from jax.sharding import Mesh
from jax.sharding import PartitionSpec as P

HD = 96
HALF = HD // 2
PAD = 128
STEPS = 2
SUB = 256
TILE = 512

EPSILON = 1e-05
ROTARY_BASE = 100000.0
MASKED = -1e30
LOG2E = math.log2(math.e)

AXES = ("yx", "core", "zh", "zl")
FLIP = [(0, 1), (1, 0)]


def norm_rows(values, gain):
    row_scale = lax.rsqrt(jnp.mean(values * values, axis=-1, keepdims=True) + EPSILON)
    return (row_scale, (values * row_scale * gain).astype(jnp.bfloat16))


def norm_back(values, row_scale, gain, upstream):
    weighted = upstream * gain
    inner_sum = jnp.mean(weighted * values, axis=-1, keepdims=True)
    grad_in = row_scale * weighted - values * (row_scale * row_scale * row_scale) * inner_sum
    gain_part = jnp.sum(upstream * (values * row_scale), axis=0)
    return (grad_in, gain_part)


def document_layout(lengths, group_rows):
    flat_lengths = lengths.reshape(-1)
    doc_ends = jnp.cumsum(flat_lengths)
    rows = jnp.arange(group_rows, dtype=jnp.int32)
    passed = (rows[:, None] >= doc_ends[None, :]).astype(jnp.int32)
    return (rows, jnp.sum(passed * flat_lengths[None, :], axis=1))


def rotary_tables(positions):
    exponents = jnp.arange(HALF, dtype=jnp.float32) * (2.0 / HD)
    inverse = ROTARY_BASE ** (-exponents)
    angles = positions.astype(jnp.float32)[:, None] * inverse[None, :]
    cosine, sine = jnp.cos(angles), jnp.sin(angles)
    gap = jnp.zeros((positions.shape[0], PAD // 2 - HALF), jnp.float32)
    return (
        jnp.concatenate([cosine, gap, cosine, gap], axis=1),
        jnp.concatenate([-sine, gap, sine, gap], axis=1),
    )


def rows_product(left, right):
    return lax.dot_general(
        left, right, (((0,), (0,)), ((), ())), preferred_element_type=jnp.float32
    )


def times_transpose(left, right):
    return lax.dot_general(
        left, right, (((1,), (1,)), ((), ())), preferred_element_type=jnp.float32
    )


def dot32(left, right):
    return jnp.dot(left, right, preferred_element_type=jnp.float32)


def stage(*values):
    return lax.optimization_barrier(values)


def spread(columns, heads):
    matrix = np.zeros((columns, len(heads) * PAD), np.float32)
    for at, first in enumerate(heads):
        for half in range(2):
            for i in range(HALF):
                matrix[first + half * HALF + i, at * PAD + half * (PAD // 2) + i] = 1.0
    return matrix


def turn(x, cosine, sine):
    return x * cosine + pltpu.roll(x, PAD // 2, 1) * sine


def rows_at(t, size):
    return pl.ds(pl.multiple_of(t * size, size), size)


def forward_kernel(pieces, ratio, *refs):
    place, low, full, cosine, sine, start, spread_in, gather_out = refs[:8]
    heads = spread_in.shape[0]
    refs = refs[8:]
    qkv, context, refs = refs[0], refs[1 : 1 + pieces], refs[1 + pieces :]
    log_sum, refs = refs[:heads], refs[heads:]
    q_s, k_s, v_s, s_s, top_s, acc = refs
    tiles = q_s.shape[0]
    all_subs = qkv.shape[0] // SUB
    piece_subs = all_subs // pieces
    scale = LOG2E * HD ** (-0.5)
    ones_lane = lax.broadcasted_iota(jnp.int32, (SUB, PAD), 1) == PAD - 1

    def prepare(r, carry):
        t = place[r]
        at = rows_at(t, SUB)
        cos_t, sin_t = cosine[at, :], sine[at, :]
        tile, half = t // (TILE // SUB), t % (TILE // SUB)
        for g in range(heads):
            wide = dot32(qkv[rows_at(r, SUB), :], spread_in[g])
            for h in range(ratio):
                query = turn(wide[:, h * PAD : (h + 1) * PAD], cos_t, sin_t) * scale
                first = pl.multiple_of(h * TILE + half * SUB, SUB)
                q_s[tile, g, pl.ds(first, SUB), :] = query.astype(jnp.bfloat16)
            key = turn(wide[:, ratio * PAD : (ratio + 1) * PAD], cos_t, sin_t)
            k_s[g, at, :] = key.astype(jnp.bfloat16)
            value = jnp.where(ones_lane, 1.0, wide[:, (ratio + 1) * PAD :])
            v_s[g, at, :] = value.astype(jnp.bfloat16)
        return carry

    lax.fori_loop(0, all_subs, prepare, 0)

    def query_tile(i, carry):
        starts = jnp.concatenate([start[rows_at(i, TILE), :]] * ratio, axis=0)
        top_s[...] = jnp.full_like(top_s, MASKED)

        def scores(j, masked, diagonal):
            for g in range(heads):
                s = times_transpose(q_s[i, g], k_s[g, rows_at(j, TILE), :])
                if masked:
                    key_at = lax.broadcasted_iota(jnp.int32, s.shape, 1)
                    allowed = key_at + j * TILE >= starts
                    if diagonal:
                        query_at = lax.rem(lax.broadcasted_iota(jnp.int32, s.shape, 0), TILE)
                        allowed = allowed & (key_at <= query_at)
                    s = jnp.where(allowed, s, MASKED)
                s_s[g, j] = s
                peak = s[:, :PAD]
                for c in range(1, TILE // PAD):
                    peak = jnp.maximum(peak, s[:, c * PAD : (c + 1) * PAD])
                top_s[g] = jnp.maximum(top_s[g], peak)

        def loop(first, last, masked):
            def run(j, c):
                scores(j, masked, False)
                return c

            lax.fori_loop(first, last, run, 0)

        loop(low[i], full[i], True)
        loop(full[i], i, False)
        scores(i, True, True)
        tops = [jnp.max(top_s[g], axis=1, keepdims=True) for g in range(heads)]
        acc[...] = jnp.zeros_like(acc)

        def weigh(j, c):
            for g in range(heads):
                p = jnp.exp2(s_s[g, j] - tops[g]).astype(jnp.bfloat16)
                acc[g] += dot32(p, v_s[g, rows_at(j, TILE), :])
            return c

        lax.fori_loop(low[i], i + 1, weigh, 0)
        packed = None
        for g in range(heads):
            total = acc[g][:, PAD - 1 :]
            out = acc[g] * (1.0 / total)
            sums = jnp.broadcast_to(tops[g] + jnp.log(total) * LOG2E, (ratio * TILE, PAD))
            log_sum[g][i] = sums.T[:1, :]
            wide = jnp.concatenate(
                [out[h * TILE : (h + 1) * TILE, :] for h in range(ratio)], axis=1
            ).astype(jnp.bfloat16)
            part = dot32(wide, gather_out[g])
            packed = part if packed is None else packed + part
        subs = tiles * (TILE // SUB)
        for half in range(TILE // SUB):
            r = place[subs + i * (TILE // SUB) + half]
            part = packed[half * SUB : (half + 1) * SUB, :].astype(jnp.bfloat16)
            for k in range(pieces):

                @pl.when(r // piece_subs == k)
                def store(k=k, part=part, r=r):
                    context[k][rows_at(r % piece_subs, SUB), :] = part

        return carry

    lax.fori_loop(0, tiles, query_tile, 0)


def backward_kernel(pieces, ratio, more, *refs):
    place, low, full, cosine, sine, start, refs = *refs[:6], refs[6:]
    heads = refs[0].shape[0]
    spread_in, spread_out, gather_in, refs = *refs[:3], refs[3:]
    log_sum, refs = refs[:heads], refs[heads:]
    d_context, context, qkv, refs = refs[:pieces], refs[pieces : 2 * pieces], refs[2 * pieces], refs[2 * pieces + 1 :]
    earlier, refs = (refs[0], refs[1:]) if more else (None, refs)
    d_qkv, refs = refs[0], refs[1:]
    q_s, k_s, kt_s, v_s, do_s, delta_s, log_s, dq_acc, dk_acc, dv_acc, dq_s = refs
    tiles = q_s.shape[0]
    all_subs = qkv.shape[0] // SUB
    piece_subs = all_subs // pieces
    scale = HD ** (-0.5)
    per_tile = TILE // SUB

    for k in range(pieces):

        def prepare(r, carry, k=k):
            t = place[k * piece_subs + r]
            rel = rows_at(r, SUB)
            at = rows_at(t, SUB)
            cos_t, sin_t = cosine[at, :], sine[at, :]
            for g in range(heads):
                wide = dot32(qkv[rows_at(k * piece_subs + r, SUB), :], spread_in[g])
                d_out = dot32(d_context[k][rel, :], spread_out[g])
                out = dot32(context[k][rel, :], spread_out[g])
                for h in range(ratio):
                    cols = slice(h * PAD, (h + 1) * PAD)
                    rows = slice(h * SUB, (h + 1) * SUB)
                    query = turn(wide[:, cols], cos_t, sin_t) * (scale * LOG2E)
                    q_s[t, g, rows, :] = query.astype(jnp.bfloat16)
                    do_s[t, g, rows, :] = d_out[:, cols].astype(jnp.bfloat16)
                    delta = jnp.sum((d_out[:, cols] * out[:, cols]).T, axis=0, keepdims=True)
                    delta_s[t * heads + g, :, rows] = delta
                    first = pl.multiple_of(h * TILE + t % per_tile * SUB, SUB)
                    log_s[t * heads + g, :, rows] = log_sum[g][t // per_tile, :, pl.ds(first, SUB)]
                key = turn(wide[:, ratio * PAD : (ratio + 1) * PAD], cos_t, sin_t)
                k_s[g, t] = key.astype(jnp.bfloat16)
                kt_s[g, t] = key.T.astype(jnp.bfloat16)
                v_s[g, t] = wide[:, (ratio + 1) * PAD :].astype(jnp.bfloat16)
                dk_acc[g, t] = jnp.zeros((SUB, PAD), jnp.float32)
                dv_acc[g, t] = jnp.zeros((SUB, PAD), jnp.float32)
            return carry

        lax.fori_loop(0, piece_subs, prepare, 0)

    def query_tile(i, carry):
        dq_acc[...] = jnp.zeros_like(dq_acc)

        def step(j, masked, diagonal):
            for g in range(heads):
                queries, d_out = q_s[i, g], do_s[i, g]
                s = times_transpose(k_s[g, j], queries)
                if masked:
                    key_at = lax.broadcasted_iota(jnp.int32, s.shape, 0)
                    allowed = key_at + j * SUB >= start[i]
                    if diagonal:
                        query_at = lax.rem(lax.broadcasted_iota(jnp.int32, s.shape, 1), SUB)
                        allowed = allowed & (key_at <= query_at)
                    s = jnp.where(allowed, s, MASKED)
                p = jnp.exp2(s - log_s[i * heads + g])
                d_p = times_transpose(v_s[g, j], d_out)
                d_s = (p * (d_p - delta_s[i * heads + g])).astype(jnp.bfloat16)
                dv_acc[g, j] += dot32(p.astype(jnp.bfloat16), d_out)
                dk_acc[g, j] += dot32(d_s, queries)
                dq_acc[g] += dot32(kt_s[g, j], d_s)

        def loop(first, last, masked):
            def run(j, c):
                step(j, masked, False)
                return c

            lax.fori_loop(first, last, run, 0)

        loop(low[i], full[i], True)
        loop(full[i], i, False)
        step(i, True, True)
        at = rows_at(i, SUB)
        cos_t, sin_t = cosine[at, :], sine[at, :]
        for g in range(heads):
            grad = dq_acc[g].T * scale
            for h in range(ratio):
                piece = turn(grad[h * SUB : (h + 1) * SUB, :], cos_t, -sin_t)
                dq_s[g, i, :, h * PAD : (h + 1) * PAD] = piece.astype(jnp.bfloat16)
        return carry

    lax.fori_loop(0, tiles, query_tile, 0)

    def finish(r, carry):
        t = place[r]
        at = rows_at(t, SUB)
        rel = rows_at(r, SUB)
        packed = None
        for g in range(heads):
            key = turn(dk_acc[g, t] * (1.0 / LOG2E), cosine[at, :], -sine[at, :])
            wide = jnp.concatenate(
                [dq_s[g, t], key.astype(jnp.bfloat16), dv_acc[g, t].astype(jnp.bfloat16)], axis=1
            )
            part = dot32(wide, gather_in[g])
            packed = part if packed is None else packed + part
        packed = packed.astype(jnp.bfloat16)
        d_qkv[rel, :] = packed + earlier[rel, :] if more else packed
        return carry

    lax.fori_loop(0, all_subs, finish, 0)


SMEM = pl.BlockSpec(memory_space=pltpu.SMEM)
VMEM = pl.BlockSpec(memory_space=pltpu.VMEM)
ANY = pl.BlockSpec(memory_space=pl.ANY)


def small_cost(transcendentals=0):
    return pl.CostEstimate(flops=1 << 20, bytes_accessed=1 << 16, transcendentals=transcendentals)


def head_matrices(head, q_heads, kv_heads):
    ratio = q_heads // kv_heads
    queries = [(head * ratio + r) * HD for r in range(ratio)]
    key, value = (q_heads + head) * HD, (q_heads + kv_heads + head) * HD
    inner = spread((q_heads + 2 * kv_heads) * HD, [*queries, key, value])
    outer = spread(q_heads * HD, queries)
    return jnp.asarray(inner, jnp.bfloat16), jnp.asarray(outer, jnp.bfloat16)


def stacked_matrices(q_heads, kv_heads):
    pairs = [head_matrices(head, q_heads, kv_heads) for head in range(kv_heads)]
    return jnp.stack([inner for inner, _ in pairs]), jnp.stack([outer for _, outer in pairs])


def attend(qkv, pieces, layout, q_heads, kv_heads):
    place, low, full, cosine, sine, start_column = layout
    ratio, rows = q_heads // kv_heads, qkv.shape[0]
    tiles, lanes = rows // TILE, ratio * TILE
    bf16, f32 = jnp.bfloat16, jnp.float32
    inner, outer = stacked_matrices(q_heads, kv_heads)
    outs = pl.pallas_call(
        functools.partial(forward_kernel, pieces, ratio),
        out_shape=[
            *[jax.ShapeDtypeStruct((rows // pieces, q_heads * HD), bf16)] * pieces,
            *[jax.ShapeDtypeStruct((tiles, 1, lanes), f32)] * kv_heads,
        ],
        in_specs=[SMEM] * 3 + [VMEM] * 6,
        out_specs=[VMEM] * (pieces + kv_heads),
        scratch_shapes=[
            pltpu.VMEM((tiles, kv_heads, lanes, PAD), bf16),
            pltpu.VMEM((kv_heads, rows, PAD), bf16),
            pltpu.VMEM((kv_heads, rows, PAD), bf16),
            pltpu.VMEM((kv_heads, tiles, lanes, TILE), f32),
            pltpu.VMEM((kv_heads, lanes, PAD), f32),
            pltpu.VMEM((kv_heads, lanes, PAD), f32),
        ],
        compiler_params=pltpu.CompilerParams(vmem_limit_bytes=60 * 2**20),
        cost_estimate=small_cost(),
        name="attention_forward",
    )(place, low, full, cosine, sine, start_column, inner, jnp.swapaxes(outer, 1, 2), qkv)
    return outs[:pieces], outs[pieces:]


def attend_back(heads, qkv, d_context, context, sums, earlier, layout, q_heads, kv_heads):
    place, low, full, cosine, sine, start_row = layout
    pieces, ratio, rows = len(context), q_heads // kv_heads, qkv.shape[0]
    tiles, lanes, count = rows // SUB, ratio * SUB, len(heads)
    bf16, f32 = jnp.bfloat16, jnp.float32
    inner, outer = stacked_matrices(q_heads, kv_heads)
    inner, outer = inner[heads[0] : heads[0] + count], outer[heads[0] : heads[0] + count]
    return pl.pallas_call(
        functools.partial(backward_kernel, pieces, ratio, bool(earlier)),
        out_shape=jax.ShapeDtypeStruct(qkv.shape, bf16),
        in_specs=[SMEM] * 3 + [VMEM] * (7 + count + 2 * pieces + len(earlier)),
        out_specs=VMEM,
        scratch_shapes=[
            pltpu.VMEM((tiles, count, lanes, PAD), bf16),
            pltpu.VMEM((count, tiles, SUB, PAD), bf16),
            pltpu.VMEM((count, tiles, PAD, SUB), bf16),
            pltpu.VMEM((count, tiles, SUB, PAD), bf16),
            pltpu.VMEM((tiles, count, lanes, PAD), bf16),
            pltpu.VMEM((tiles * count, 1, lanes), f32),
            pltpu.VMEM((tiles * count, 1, lanes), f32),
            pltpu.VMEM((count, PAD, lanes), f32),
            pltpu.VMEM((count, tiles, SUB, PAD), f32),
            pltpu.VMEM((count, tiles, SUB, PAD), f32),
            pltpu.VMEM((count, tiles, SUB, ratio * PAD), bf16),
        ],
        compiler_params=pltpu.CompilerParams(vmem_limit_bytes=60 * 2**20),
        cost_estimate=small_cost(),
        name=f"attention_backward_{heads[0]}",
    )(
        place, low, full, cosine, sine, start_row, inner, outer, jnp.swapaxes(inner, 1, 2),
        *[sums[h] for h in heads], *d_context, *context, qkv, *earlier,
    )


def fetch(me, where, sources, target, sems):
    copies = []
    for n, (source, (j, deep, first, column, taken)) in enumerate(zip(sources, where, strict=True)):
        cols = min(source.shape[1] - taken, target.shape[1] - column)
        at = pl.ds(pl.multiple_of((me[0] ^ j) * deep + first, 16), source.shape[0])
        if cols != source.shape[1]:
            source = source.at[:, taken : taken + cols]
        copies.append(pltpu.make_async_copy(source, target.at[at, column : column + cols], sems.at[n]))
    return copies


def take_rows(parts, target):
    rows = target.shape[0]
    at = 0
    for part in parts:

        @pl.when(pl.program_id(0) == at // rows)
        def take(part=part, at=at):
            target[at % rows : at % rows + part.shape[0], :] = part[...]

        at += part.shape[0]


def at_first_step(copies, what):
    @pl.when(pl.program_id(0) == 0)
    def run():
        for copy in copies:
            what(copy)


def project_kernel(count, where, more, me, *refs):
    parts, gain, refs = refs[:count], refs[count], refs[count + 1 :]
    sources, refs = refs[: len(where[0])], refs[len(where[0]) :]
    norm_all, qkv_all, weight, sems, rows_s = refs[2 if more else 0 :]
    copies = fetch(me, where[0], sources, weight, sems)
    at_first_step(copies, lambda copy: copy.start())
    take_rows(parts, rows_s)
    x = rows_s[...].astype(jnp.float32)
    scale = lax.rsqrt(jnp.mean(x * x, axis=-1, keepdims=True) + EPSILON)
    norm_all[...] = (x * scale * gain[...]).astype(jnp.bfloat16)
    at_first_step(copies, lambda copy: copy.wait())
    qkv_all[...] = dot32(norm_all[...], weight[...]).astype(jnp.bfloat16)


def gate_kernel(count, where, more, me, *refs):
    parts, refs = refs[:count], refs[count:]
    sources, refs = refs[: len(where[0])], refs[len(where[0]) :]
    norm_all, gate_up_all, hidden_all, weight, sems = refs[3 if more else 0 :]
    hidden_cols = hidden_all.shape[1]
    copies = fetch(me, where[0], sources, weight, sems)
    at_first_step(copies, lambda copy: copy.start())
    take_rows(parts, norm_all)
    at_first_step(copies, lambda copy: copy.wait())
    x = norm_all[...]
    width = min(512, hidden_cols)
    for at in range(0, hidden_cols, width):
        gate_at = slice(at, at + width)
        up_at = slice(hidden_cols + at, hidden_cols + at + width)
        gate = dot32(x, weight[:, gate_at])
        up = dot32(x, weight[:, up_at])
        gate_up_all[:, gate_at] = gate
        gate_up_all[:, up_at] = up
        hidden_all[:, gate_at] = (gate * (1.0 / (1.0 + jnp.exp(-gate))) * up).astype(jnp.bfloat16)


def gate_back_kernel(count, where, more, me, *refs):
    parts, gate_up_all, hidden_other, refs = refs[:count], *refs[count : count + 2], refs[count + 2 :]
    gate_up, refs = refs[: len(where[0])], refs[len(where[0]) :]
    down, refs = refs[: len(where[1])], refs[len(where[1]) :]
    refs = refs[2 if more else 0 :]
    grad_all, d_gate_up_all, d_norm_own, d_norm_sib, out_own, out_sib = refs[:6]
    w_gate_up, gate_up_sems, w_down, down_sems = refs[6:]
    hidden_cols = w_down.shape[1]
    down_copies = fetch(me, where[1], down, w_down, down_sems)
    copies = fetch(me, where[0], gate_up, w_gate_up, gate_up_sems)
    at_first_step(down_copies + copies, lambda copy: copy.start())
    take_rows(parts, grad_all)
    at_first_step(down_copies, lambda copy: copy.wait())
    dy = grad_all[...]
    width = min(512, hidden_cols)
    for at in range(0, hidden_cols, width):
        gate_at = slice(at, at + width)
        up_at = slice(hidden_cols + at, hidden_cols + at + width)
        d_hidden = dot32(dy, w_down[:, gate_at])
        gate, up = gate_up_all[:, gate_at], gate_up_all[:, up_at]
        sigmoid = 1.0 / (1.0 + jnp.exp(-gate))
        d_gate = d_hidden * up * sigmoid * (1.0 + gate * (1.0 - sigmoid))
        d_gate_up_all[:, gate_at] = d_gate.astype(jnp.bfloat16)
        d_gate_up_all[:, up_at] = (d_hidden * (gate * sigmoid)).astype(jnp.bfloat16)
    out = times_transpose(hidden_other[...], w_down[...]).astype(jnp.bfloat16)
    at_first_step(copies, lambda copy: copy.wait())
    d_norm = times_transpose(d_gate_up_all[...], w_gate_up[...]).astype(jnp.bfloat16)

    @pl.when(pl.program_id(0) == 0)
    def to_own():
        d_norm_own[...] = d_norm
        out_own[...] = out

    @pl.when(pl.program_id(0) != 0)
    def to_sibling():
        d_norm_sib[...] = d_norm
        out_sib[...] = out


def piece_call(kernel, name, k, pieces, me, parts, whole, tiled, fetched, earlier, outs):
    tile, width = sum(x.shape[0] for x in parts) // STEPS, parts[0].shape[1]
    count = len(parts)

    def rows_of(piece):
        return lambda i: (piece * STEPS + i, 0)

    sources = [x for arrays, _, _ in fetched for x in arrays]
    first_earlier = 1 + count + len(whole) + len(tiled) + len(sources)
    scratch = []
    for arrays, _, cols in fetched:
        scratch += [pltpu.VMEM((width, cols), jnp.bfloat16), pltpu.SemaphoreType.DMA((len(arrays),))]
    if kernel is project_kernel:
        scratch.append(pltpu.VMEM((tile, width), jnp.bfloat16))
    return pl.pallas_call(
        functools.partial(kernel, count, tuple(where for _, where, _ in fetched), bool(earlier)),
        grid=(STEPS,),
        out_shape=[
            jax.ShapeDtypeStruct((pieces * STEPS * tile if span == "all" else tile, columns), kind)
            for columns, kind, span in outs
        ],
        in_specs=[
            SMEM,
            *(pl.BlockSpec(x.shape, lambda i: (0, 0)) for x in parts),
            *(pl.BlockSpec(x.shape, lambda i: (0, 0)) for x in whole),
            *(pl.BlockSpec((tile, x.shape[1]), rows_of(piece)) for x, piece in tiled),
            *[ANY] * (len(sources) + len(earlier)),
        ],
        out_specs=[
            pl.BlockSpec((tile, columns), rows_of(k) if span == "all" else lambda i: (0, 0))
            for columns, kind, span in outs
        ],
        scratch_shapes=scratch,
        input_output_aliases={first_earlier + n: n for n in range(len(earlier))},
        compiler_params=pltpu.CompilerParams(vmem_limit_bytes=60 * 2**20),
        cost_estimate=small_cost(),
        name=f"{name}_{k}",
    )(me, *parts, *whole, *(x for x, _ in tiled), *sources, *earlier)


def assemble_kernel(where, me, *refs):
    sources, whole, sems = refs[: len(where)], refs[len(where)], refs[len(where) + 1]
    copies = fetch(me, where, sources, whole, sems)
    for copy in copies:
        copy.start()
    for copy in copies:
        copy.wait()


def assemble(name, me, arrays, where, rows, cols):
    return pl.pallas_call(
        functools.partial(assemble_kernel, where),
        out_shape=jax.ShapeDtypeStruct((rows, cols), arrays[0].dtype),
        in_specs=[SMEM, *[ANY] * len(arrays)],
        out_specs=VMEM,
        scratch_shapes=[pltpu.SemaphoreType.DMA((len(arrays),))],
        compiler_params=pltpu.CompilerParams(vmem_limit_bytes=60 * 2**20),
        cost_estimate=small_cost(),
        name=name,
    )(me, *arrays)


def flip(x, axis):
    return lax.ppermute(x, axis, FLIP)


CROSS = [(1, 2), (2, 1)]
OUT = [(0, 1), (3, 2), (2, 0), (1, 3)]
BACK = [(1, 0), (2, 3), (0, 2), (3, 1)]


def crossed(x, perm):
    return lax.ppermute(x, ("core", "zh"), perm)


def straight():
    return lax.axis_index("core") == lax.axis_index("zh")


def swap(x):
    return jnp.where(straight(), x, crossed(x, CROSS))


def send_z(w):
    return crossed(w, OUT), crossed(w, CROSS)


def pair_of(w, out, cross):
    zh = lax.axis_index("zh")
    x = jnp.where(straight(), w, cross)
    return jnp.concatenate([jnp.where(zh == 0, x, out), jnp.where(zh == 0, out, x)], axis=0)


def give_z(part):
    zh = lax.axis_index("zh")
    half = part.shape[0] // 2
    upper, lower = part[:half], part[half:]
    return jnp.where(zh == 0, upper, lower), jnp.where(zh == 0, lower, upper)


def sum_z(keep, back, cross):
    return back.astype(jnp.float32) + jnp.where(straight(), keep, cross).astype(jnp.float32)


def shift(x, e, k):
    n = lax.axis_size("zl")
    return lax.ppermute(
        x, ("core", "zl"), [(c * n + l, (c ^ e) * n + (l + k) % n) for c in range(2) for l in range(n)]
    )


def from_near(x, k):
    n = lax.axis_size("zl")
    return lax.ppermute(x, "zl", [((j + k) % n, j) for j in range(n)])


def to_near(x, k):
    n = lax.axis_size("zl")
    return lax.ppermute(x, "zl", [(j, (j + k) % n) for j in range(n)])


def across(x, j):
    n = lax.axis_size("yx")
    return lax.ppermute(x, "yx", [(a, a ^ j) for a in range(n)])


def neighbours(x):
    count = lax.axis_size("yx")
    return [across(x, j) for j in range(1, count if count != 4 else 3)]


def diagonal(taken):
    if lax.axis_size("yx") != 4:
        return []
    half = taken[0].shape[0] // 2
    return [across(taken[1][:half], 1), across(taken[0][half:], 2)]


def blocks_of(own, taken, halves, column=0, source_column=0):
    deep = own.shape[0]
    arrays = [own, *taken, *halves]
    where = [(j, deep, 0, column, source_column) for j in range(1 + len(taken))]
    where += [(3, deep, n * deep // 2, column, source_column) for n in range(len(halves))]
    return arrays, tuple(where)


def whole_weight(w):
    return [w], ((0, 0, 0, 0, 0),)


def block_of(grad, j, columns):
    size = grad.shape[0] // lax.axis_size("yx")
    first = (lax.axis_index("yx") ^ j) * size
    return lax.dynamic_slice(grad, (first, columns[0]), (size, columns[1] - columns[0]))


def send_yx(grad, columns):
    count = lax.axis_size("yx")
    if count != 4:
        return [across(block_of(grad, j, columns), j) for j in range(1, count)]
    far = block_of(grad, 3, columns)
    half = far.shape[0] // 2
    return [across(far[:half], 1), across(far[half:], 2)]


def join_yx(grad, columns, taken):
    if lax.axis_size("yx") != 4:
        return taken, block_of(grad, 0, columns)
    half = taken[0].shape[0]
    one, two = block_of(grad, 1, columns), block_of(grad, 2, columns)
    one = jnp.concatenate([one[:half], one[half:] + taken[1]], axis=0)
    two = jnp.concatenate([two[:half] + taken[0], two[half:]], axis=0)
    return [across(one, 1), across(two, 2)], block_of(grad, 0, columns)


def total_yx(taken, own):
    total = own.astype(jnp.float32)
    for part in taken:
        total = total + part.astype(jnp.float32)
    return total.astype(jnp.bfloat16)


def body(
    tokens,
    cotangent,
    seq_lengths,
    attn_gain,
    q_weight,
    key_projection,
    value_projection,
    out_weight,
    mlp_gain,
    gate_weight,
    up_weight,
    down_weight,
):
    bf16, f32 = jnp.bfloat16, jnp.float32
    core, zl, yx = lax.axis_index("core"), lax.axis_index("zl"), lax.axis_index("yx")
    near = lax.axis_size("zl")
    others = range(1, near)
    rows = tokens.shape[0]
    group_rows = 2 * near * rows
    query_cols, key_cols = q_weight.shape[1], key_projection.shape[1]
    qkv_cols = query_cols + 2 * key_cols
    q_heads, kv_heads = query_cols // HD, key_cols // HD
    hidden_cols = gate_weight.shape[1]
    me = yx.astype(jnp.int32).reshape(1)

    qkv_shard = jnp.concatenate([q_weight, key_projection, value_projection], axis=1)
    gate_up_shard = jnp.concatenate([gate_weight, up_weight], axis=1)
    part_rows = rows // 2
    upper = swap(tokens[:part_rows])
    shard = jnp.concatenate([qkv_shard, out_weight], axis=1)
    shard_moved = send_z(shard)
    lengths = swap(seq_lengths)
    gains = lax.all_gather(jnp.stack([attn_gain, mlp_gain]), ("yx", "core"), axis=1, tiled=True).astype(f32)
    upper, lengths, second_part, gains, *shard_moved = stage(upper, lengths, tokens[part_rows:], gains, *shard_moved)
    gain_one, gain_two = gains[0], gains[1]

    upper_far = [from_near(upper, k) for k in others]
    lower = swap(second_part)
    pair, out_pair = (
        pair_of(*(x[:, cols] for x in (shard, *shard_moved))) for cols in (slice(0, qkv_cols), slice(qkv_cols, None))
    )
    taken = neighbours(pair)
    upper_sib = flip(upper, "core")

    subs = jnp.arange(group_rows // SUB, dtype=jnp.int32)
    per_device = rows // SUB
    source, within = subs // per_device, subs % per_device
    there_core, there_zl = (source % 2) ^ core, (source // 2 + zl) % near
    to_order = (there_core * near + there_zl) * per_device + within
    from_order = (((source % near - zl) % near) * 2 + ((source // near) ^ core)) * per_device + within
    place = jnp.concatenate([to_order, from_order])
    row_at, doc_start = document_layout(lengths, group_rows)
    cosine, sine = rotary_tables(row_at - doc_start)

    def bounds(size):
        tile_start = doc_start.reshape(-1, size)
        tile = jnp.arange(group_rows // size, dtype=jnp.int32)
        low = tile_start[:, 0] // size
        return low, jnp.minimum((tile_start[:, -1] + size - 1) // size, tile)

    start_row = jnp.tile(doc_start.reshape(-1, 1, SUB), (1, 1, q_heads // kv_heads))
    layout = (place, *bounds(TILE), cosine, sine, doc_start[:, None])
    layout_back = (place, *bounds(SUB), cosine, sine, start_row)
    lower, upper_sib, out_pair, *moved = stage(lower, upper_sib, out_pair, *upper_far, *taken, *layout, *layout_back)
    upper_far, moved = moved[: near - 1], moved[near - 1 :]
    taken, moved = moved[: len(taken)], moved[len(taken) :]
    layout, layout_back = moved[: len(layout)], moved[len(layout) :]

    lower_far = [from_near(lower, k) for k in others]
    lower_sib = flip(lower, "core")
    out_far = [from_near(out_pair, k) for k in others]
    blocks = blocks_of(pair, taken, diagonal(taken))
    projecting = [(*blocks, qkv_cols)]
    gain_row = gain_one[None]
    outs = [(tokens.shape[1], bf16, "all"), (qkv_cols, bf16, "all")]
    parts = [upper, lower, upper_sib, lower_sib]
    normed = piece_call(project_kernel, "project", 0, near, me, parts, [gain_row], [], projecting, [], outs)
    gate_up_shard, *moved = stage(gate_up_shard, *lower_far, *out_far, *normed)
    lower_far, out_far, normed = moved[: near - 1], moved[near - 1 : 2 * near - 2], moved[2 * near - 2 :]

    out_own = jnp.concatenate([out_pair, *out_far], axis=1)
    out_taken = neighbours(out_own)
    for k in others:
        parts = [upper_far[k - 1], lower_far[k - 1], flip(upper_far[k - 1], "core"), flip(lower_far[k - 1], "core")]
        normed = piece_call(project_kernel, "project", k, near, me, parts, [gain_row], [], projecting, normed, outs)
    norm_one, qkv = normed
    gate_up_shard, qkv, out_own, *out_taken = stage(gate_up_shard, qkv, out_own, *out_taken)

    gate_up_moved = send_z(gate_up_shard)
    out_halves = diagonal(out_taken)
    context, sums = attend(qkv, 2 * near, layout, q_heads, kv_heads)
    down_shard, cotangent, *moved = stage(down_weight, cotangent, *context, *gate_up_moved, *out_halves)
    context, gate_up_moved, out_halves = moved[: 2 * near], moved[2 * near : 2 * near + 2], moved[2 * near + 2 :]

    quarters = {(0, 0): context[0]}
    for k in range(near):
        for e in range(2):
            if (e, k) != (0, 0):
                quarters[e, (near - k) % near] = shift(context[2 * k + e], e, k)
    pairs = [
        pair_of(*(x[:, n * hidden_cols : (n + 1) * hidden_cols] for x in (gate_up_shard, *gate_up_moved)))
        for n in range(2)
    ]
    gate_taken = neighbours(pairs[0])
    order = [(e, k) for e in range(2) for k in range(near)]
    up_pair, down_shard, cotangent, *moved = stage(
        pairs[1], down_shard, cotangent, *(quarters[at] for at in order), *gate_taken, *out_halves
    )
    quarters, moved = moved[: 2 * near], moved[2 * near :]
    gate_taken, out_halves = moved[: len(gate_taken)], moved[len(gate_taken) :]

    up_taken = neighbours(up_pair)
    cot_upper = crossed(cotangent[:part_rows], CROSS)
    w_out_near = assemble(
        "assemble_out", me, *blocks_of(out_own, out_taken, out_halves), tokens.shape[1], near * query_cols
    )
    w_out_sib = flip(w_out_near, "core")
    residual = jnp.concatenate([upper, lower], axis=0).astype(f32)
    scale_one = lax.rsqrt(jnp.mean(residual * residual, axis=-1, keepdims=True) + EPSILON)
    w_out_sib, w_out_near, scale_one, cotangent, cot_upper, down_shard, *up_taken = stage(
        w_out_sib, w_out_near, scale_one, cotangent, cot_upper, down_shard, *up_taken
    )

    gate_halves = diagonal(gate_taken)
    down_moved = send_z(down_shard)
    own_context = jnp.concatenate(quarters[:near], axis=1)
    sib_context = jnp.concatenate(quarters[near:], axis=1)
    mid = residual + times_transpose(own_context, w_out_near) + times_transpose(sib_context, w_out_sib)
    scale_two, norm_two = norm_rows(mid, gain_two)
    norm_two, cotangent, cot_upper, *moved = stage(norm_two, cotangent, cot_upper, *gate_halves, *down_moved)
    gate_halves, down_moved = moved[:-2], moved[-2:]

    upper_far = [from_near(norm_two[:part_rows], k) for k in others]
    up_halves = diagonal(up_taken)
    norm_sib = flip(norm_two, "core")
    cot_lower = crossed(cotangent[part_rows:], CROSS)
    w_down = lax.all_gather(pair_of(down_shard, *down_moved), "yx", axis=0, tiled=True)
    w_project = assemble("assemble_project", me, *blocks, tokens.shape[1], qkv_cols)
    norm_two, cotangent, cot_upper, cot_lower, norm_sib, w_project, *moved = stage(
        norm_two, cotangent, cot_upper, cot_lower, norm_sib, w_project, *upper_far, *up_halves
    )
    upper_far, up_halves = moved[: near - 1], moved[near - 1 :]

    lower_far = [from_near(norm_two[part_rows:], k) for k in others]
    upper_far_sib = [flip(x, "core") for x in upper_far]
    cot_upper = jnp.where(straight(), cotangent[:part_rows], cot_upper)
    cot_lower = jnp.where(straight(), cotangent[part_rows:], cot_lower)
    cot_upper_sib = flip(cot_upper, "core")
    gate_blocks = blocks_of(pairs[0], gate_taken, gate_halves)
    up_blocks = blocks_of(up_pair, up_taken, up_halves, hidden_cols)
    gate_up = ([*gate_blocks[0], *up_blocks[0]], gate_blocks[1] + up_blocks[1], 2 * hidden_cols)
    outs = [(norm_two.shape[1], bf16, "all"), (2 * hidden_cols, f32, "all"), (hidden_cols, bf16, "all")]
    earlier = piece_call(gate_kernel, "gate", 0, near, me, [norm_two, norm_sib], [], [], [gate_up], [], outs)
    cot_lower, cot_upper, cot_upper_sib, *moved = stage(
        cot_lower, cot_upper, cot_upper_sib, *lower_far, *upper_far_sib, *earlier
    )
    lower_far, upper_far_sib, earlier = moved[: near - 1], moved[near - 1 : 2 * near - 2], moved[2 * near - 2 :]

    cot_upper_far = [from_near(cot_upper, k) for k in others]
    cot_lower_sib = flip(cot_lower, "core")
    for k in others:
        parts = [upper_far[k - 1], lower_far[k - 1], upper_far_sib[k - 1], flip(lower_far[k - 1], "core")]
        earlier = piece_call(gate_kernel, "gate", k, near, me, parts, [], [], [gate_up], earlier, outs)
    cot_lower, cot_lower_sib, w_down, *moved = stage(cot_lower, cot_lower_sib, w_down, *cot_upper_far, *earlier)
    cot_upper_far, earlier = moved[: near - 1], moved[near - 1 :]
    norm_two_all, gate_up_all, hidden_all = earlier

    cot_lower_far = [from_near(cot_lower, k) for k in others]
    cot_upper_far_sib = [flip(x, "core") for x in cot_upper_far]
    down = (*whole_weight(w_down), hidden_cols)
    width = norm_two.shape[1]
    outs = [(width, bf16, "all"), (2 * hidden_cols, bf16, "all")]
    outs += [(width, bf16, "own"), (width, bf16, "sibling")] * 2

    def way_back(k, parts, earlier):
        tiled = [(gate_up_all, k), (hidden_all, (k + 1) % near)]
        return piece_call(gate_back_kernel, "gate_back", k, near, me, parts, [], tiled, [gate_up, down], earlier, outs)

    def joined(own, sib):
        return own.astype(f32) + flip(sib, "core").astype(f32)

    grad_all, d_gate_up_all, *near_back = way_back(0, [cot_upper, cot_lower, cot_upper_sib, cot_lower_sib], [])
    grad_all, d_gate_up_all, *moved = stage(
        grad_all, d_gate_up_all, *near_back, *cot_lower_far, *cot_upper_far_sib
    )
    near_back, cot_lower_far, cot_upper_far_sib = moved[:4], moved[4 : near + 3], moved[near + 3 :]

    out_sum = joined(*near_back[2:]).astype(bf16)
    cot_lower_far_sib = [flip(x, "core") for x in cot_lower_far]
    out_sum, *cot_lower_far_sib = stage(out_sum, *cot_lower_far_sib)
    out_upper = to_near(out_sum[:part_rows], 1 % near)
    back = []
    for k in others:
        parts = [cot_upper_far[k - 1], cot_lower_far[k - 1], cot_upper_far_sib[k - 1], cot_lower_far_sib[k - 1]]
        grad_all, d_gate_up_all, *more = way_back(k, parts, [grad_all, d_gate_up_all])
        back.append(more)
    grad_all, d_gate_up_all, out_upper, *far_back = stage(
        grad_all, d_gate_up_all, out_upper, *(x for more in back for x in more)
    )
    d_norm_sent = [joined(*far_back[4 * n : 4 * n + 2]).astype(bf16) for n in range(near - 1)]
    out_far_back = [far_back[4 * n + 2 : 4 * n + 4] for n in range(near - 1)]
    grad_all, d_gate_up_all, near_own, near_sib, *d_norm_sent = stage(
        grad_all, d_gate_up_all, *near_back[:2], *d_norm_sent
    )

    moved_upper = [to_near(d_norm_sent[k - 1][:part_rows], k) for k in others]
    grad_gate_up = rows_product(norm_two_all, d_gate_up_all).astype(bf16)
    grad_gate_up, grad_all, near_own, near_sib, *moved = stage(
        grad_gate_up, grad_all, near_own, near_sib, *moved_upper, *d_norm_sent
    )
    moved_upper, d_norm_sent = moved[: near - 1], moved[near - 1 :]

    moved_lower = [to_near(d_norm_sent[k - 1][part_rows:], k) for k in others]
    gate_up_part = lax.psum_scatter(grad_gate_up, "yx", scatter_dimension=0, tiled=True)
    d_norm_two = joined(near_own, near_sib)
    grad_down = rows_product(grad_all, hidden_all).astype(bf16)
    grad_down, d_norm_two, out_sum, *moved_lower = stage(grad_down, d_norm_two, out_sum, *moved_lower)

    out_lower = to_near(out_sum[part_rows:], 1 % near)
    down_part = lax.psum_scatter(grad_down, "yx", scatter_dimension=0, tiled=True)
    for one, two in zip(moved_upper, moved_lower, strict=True):
        d_norm_two = d_norm_two + jnp.concatenate([one, two], axis=0).astype(f32)
    own_cotangent = jnp.concatenate([cot_upper, cot_lower], axis=0).astype(f32)
    mid_back, _ = norm_back(mid, scale_two, gain_two, d_norm_two)
    d_mid = own_cotangent + mid_back
    d_attn = d_mid.astype(bf16)
    both = [dot32(d_attn, w).astype(bf16) for w in (w_out_near, w_out_sib)]
    d_quarters = [both[e][:, k * query_cols : (k + 1) * query_cols] for e, k in order]
    d_attn, out_lower, *d_quarters = stage(d_attn, out_lower, *d_quarters)

    d_context = [None] * (2 * near)
    for (e, k), x in zip(order, d_quarters, strict=True):
        d_context[(near - k) % near * 2 + e] = x if (e, k) == (0, 0) else shift(x, e, k)
    grad_out_sib = flip(rows_product(d_attn, sib_context).astype(bf16), "core")
    grad_out = (rows_product(d_attn, own_context) + grad_out_sib.astype(f32)).astype(bf16)
    output_own = mid + joined(*out_far_back[-1]) + jnp.concatenate([out_upper, out_lower], axis=0).astype(f32)
    for n in range(near - 2):
        output_own = output_own + to_near(joined(*out_far_back[n]).astype(bf16), n + 2).astype(f32)
    output_own = output_own.astype(bf16)
    grad_out, output_own, gate_up_part, *d_context = stage(grad_out, output_own, gate_up_part, *d_context)

    output_crossed = crossed(output_own, CROSS)
    gate_up_keep, gate_up_give = give_z(gate_up_part)
    gate_up_back = crossed(gate_up_give, BACK)
    out_part = lax.psum_scatter(grad_out, "yx", scatter_dimension=0, tiled=True)
    d_qkv = attend_back(list(range(kv_heads)), qkv, d_context, context, sums, [], layout_back, q_heads, kv_heads)
    d_qkv, output_crossed, gate_up_back, gate_up_keep, down_part = stage(
        d_qkv, output_crossed, gate_up_back, gate_up_keep, down_part
    )

    def back_part(k):
        own, sib = (d_qkv[(2 * k + e) * rows : (2 * k + e + 1) * rows] for e in range(2))
        taken = flip(times_transpose(sib, w_project).astype(bf16), "core")
        return times_transpose(own, w_project) + taken.astype(f32)

    gate_up_cross = crossed(gate_up_keep, CROSS)
    d_sent = [back_part(k).astype(bf16) for k in others]
    d_qkv, gate_up_cross, down_part, *d_sent = stage(d_qkv, gate_up_cross, down_part, *d_sent)

    d_upper = [to_near(d_sent[k - 1][:part_rows], k) for k in others]
    down_keep, down_give = give_z(down_part)
    down_home = [crossed(down_give, BACK), crossed(down_keep, CROSS)]
    grad_project = rows_product(norm_one, d_qkv).astype(bf16)
    project_sent = send_yx(grad_project, (0, qkv_cols))
    total = back_part(0)
    total, grad_project, *moved = stage(total, grad_project, *d_upper, *d_sent, *project_sent, *down_home)
    d_upper, d_sent, project_sent, down_home = (
        moved[: near - 1], moved[near - 1 : 2 * near - 2], moved[2 * near - 2 : -2], moved[-2:],
    )

    d_lower = [to_near(d_sent[k - 1][part_rows:], k) for k in others]
    project_rest, project_own = join_yx(grad_project, (0, qkv_cols), project_sent)

    def input_part(at, moved):
        part = total[at]
        for x in moved:
            part = part + x.astype(f32)
        back, _ = norm_back(residual[at], scale_one[at], gain_one, part)
        return (d_mid[at] + back).astype(bf16)

    input_upper = input_part(slice(0, part_rows), d_upper)
    upper_crossed = crossed(input_upper, CROSS)
    total, input_upper, upper_crossed, out_part, *moved = stage(
        total, input_upper, upper_crossed, out_part, *d_lower, *project_rest
    )
    d_lower, project_rest = moved[: near - 1], moved[near - 1 :]

    project_keep, project_give = give_z(total_yx(project_rest, project_own))
    project_home = [crossed(project_give, BACK), crossed(project_keep, CROSS)]
    input_lower = input_part(slice(part_rows, rows), d_lower)
    lower_crossed = crossed(input_lower, CROSS)
    out_moved = [to_near(out_part[:, k * query_cols : (k + 1) * query_cols], k) for k in others]
    out_quarter = out_part[:, :query_cols].astype(f32)
    for part in out_moved:
        out_quarter = out_quarter + part.astype(f32)
    out_keep, out_give = give_z(out_quarter.astype(bf16))
    out_home = [crossed(out_give, BACK), crossed(out_keep, CROSS)]
    grad_project = sum_z(project_keep, *project_home)
    grad_out = sum_z(out_keep, *out_home)
    grad_down = sum_z(down_keep, *down_home)
    grad_gate_up = sum_z(gate_up_keep, gate_up_back, gate_up_cross)
    output = jnp.where(straight(), output_own, output_crossed)
    input_grad = jnp.concatenate(
        [
            jnp.where(straight(), input_upper, upper_crossed),
            jnp.where(straight(), input_lower, lower_crossed),
        ],
        axis=0,
    ).astype(f32)
    gain_grads = lax.psum(
        jnp.stack(
            [
                jnp.sum(qkv_shard.astype(f32) * grad_project, axis=1),
                jnp.sum(gate_up_shard.astype(f32) * grad_gate_up, axis=1),
            ]
        ),
        ("zh", "zl"),
    ) / jnp.stack([attn_gain, mlp_gain]).astype(f32)
    return (
        output,
        input_grad,
        gain_grads[0],
        grad_project[:, :query_cols],
        grad_project[:, query_cols : query_cols + key_cols],
        grad_project[:, query_cols + key_cols :],
        grad_out,
        gain_grads[1],
        grad_gate_up[:, :hidden_cols],
        grad_gate_up[:, hidden_cols:],
        grad_down,
    )


def solution(mesh):
    dp, tensor = mesh.shape["dp"], mesh.shape["tensor"]
    fine = Mesh(mesh.devices.reshape(dp // 2, 2, 2, tensor // 2), AXES)
    by_rows, by_dp, by_both = P(AXES, None), P(("yx", "core")), P(("yx", "core"), ("zh", "zl"))
    return jax.shard_map(
        body,
        mesh=fine,
        in_specs=(
            by_rows, by_rows, P(("yx", "core"), None), by_dp, by_both, by_both, by_both, by_both,
            by_dp, by_both, by_both, by_both,
        ),
        out_specs=(
            by_rows, by_rows, by_dp, by_both, by_both, by_both, by_both, by_dp, by_both, by_both, by_both,
        ),
        check_vma=False,
    )
```

```python
import functools
import math

import jax
import jax.numpy as jnp
import numpy as np
from jax import lax
from jax.experimental import pallas as pl
from jax.experimental.pallas import tpu as pltpu
from jax.sharding import Mesh
from jax.sharding import PartitionSpec as P

HD = 96
HALF = HD // 2
PAD = 128
STEPS = 4
SUB = 256
TILE = 512

EPSILON = 1e-05
ROTARY_BASE = 100000.0
MASKED = -1e30
LOG2E = math.log2(math.e)

AXES = ("yx", "core", "zh", "zl")
FLIP = [(0, 1), (1, 0)]


def norm_rows(values, gain):
    row_scale = lax.rsqrt(jnp.mean(values * values, axis=-1, keepdims=True) + EPSILON)
    return (row_scale, (values * row_scale * gain).astype(jnp.bfloat16))


def norm_back(values, row_scale, gain, upstream):
    weighted = upstream * gain
    inner_sum = jnp.mean(weighted * values, axis=-1, keepdims=True)
    grad_in = row_scale * weighted - values * (row_scale * row_scale * row_scale) * inner_sum
    gain_part = jnp.sum(upstream * (values * row_scale), axis=0)
    return (grad_in, gain_part)


def document_layout(lengths, group_rows):
    flat_lengths = lengths.reshape(-1)
    doc_ends = jnp.cumsum(flat_lengths)
    rows = jnp.arange(group_rows, dtype=jnp.int32)
    passed = (rows[:, None] >= doc_ends[None, :]).astype(jnp.int32)
    return (rows, jnp.sum(passed * flat_lengths[None, :], axis=1))


def rotary_tables(positions):
    exponents = jnp.arange(HALF, dtype=jnp.float32) * (2.0 / HD)
    inverse = ROTARY_BASE ** (-exponents)
    angles = positions.astype(jnp.float32)[:, None] * inverse[None, :]
    cosine, sine = jnp.cos(angles), jnp.sin(angles)
    gap = jnp.zeros((positions.shape[0], PAD // 2 - HALF), jnp.float32)
    return (
        jnp.concatenate([cosine, gap, cosine, gap], axis=1),
        jnp.concatenate([-sine, gap, sine, gap], axis=1),
    )


def rows_product(left, right):
    return lax.dot_general(
        left, right, (((0,), (0,)), ((), ())), preferred_element_type=jnp.float32
    )


def times_transpose(left, right):
    return lax.dot_general(
        left, right, (((1,), (1,)), ((), ())), preferred_element_type=jnp.float32
    )


def dot32(left, right):
    return jnp.dot(left, right, preferred_element_type=jnp.float32)


def stage(*values):
    return lax.optimization_barrier(values)


def spread(columns, heads):
    matrix = np.zeros((columns, len(heads) * PAD), np.float32)
    for at, first in enumerate(heads):
        for half in range(2):
            for i in range(HALF):
                matrix[first + half * HALF + i, at * PAD + half * (PAD // 2) + i] = 1.0
    return matrix


def turn(x, cosine, sine):
    return x * cosine + pltpu.roll(x, PAD // 2, 1) * sine


def rows_at(t, size):
    return pl.ds(pl.multiple_of(t * size, size), size)


def forward_kernel(pieces, ratio, *refs):
    place, low, full, cosine, sine, start, spread_in, gather_out = refs[:8]
    heads = spread_in.shape[0]
    refs = refs[8:]
    qkv, context, refs = refs[0], refs[1 : 1 + pieces], refs[1 + pieces :]
    log_sum, refs = refs[:heads], refs[heads:]
    q_s, k_s, v_s, s_s, top_s, acc = refs
    tiles = q_s.shape[0]
    all_subs = qkv.shape[0] // SUB
    piece_subs = all_subs // pieces
    scale = LOG2E * HD ** (-0.5)
    ones_lane = lax.broadcasted_iota(jnp.int32, (SUB, PAD), 1) == PAD - 1

    def prepare(r, carry):
        t = place[r]
        at = rows_at(t, SUB)
        cos_t, sin_t = cosine[at, :], sine[at, :]
        tile, half = t // (TILE // SUB), t % (TILE // SUB)
        for g in range(heads):
            wide = dot32(qkv[rows_at(r, SUB), :], spread_in[g])
            for h in range(ratio):
                query = turn(wide[:, h * PAD : (h + 1) * PAD], cos_t, sin_t) * scale
                first = pl.multiple_of(h * TILE + half * SUB, SUB)
                q_s[tile, g, pl.ds(first, SUB), :] = query.astype(jnp.bfloat16)
            key = turn(wide[:, ratio * PAD : (ratio + 1) * PAD], cos_t, sin_t)
            k_s[g, at, :] = key.astype(jnp.bfloat16)
            value = jnp.where(ones_lane, 1.0, wide[:, (ratio + 1) * PAD :])
            v_s[g, at, :] = value.astype(jnp.bfloat16)
        return carry

    lax.fori_loop(0, all_subs, prepare, 0)

    def query_tile(i, carry):
        starts = jnp.concatenate([start[rows_at(i, TILE), :]] * ratio, axis=0)
        top_s[...] = jnp.full_like(top_s, MASKED)

        def scores(j, masked, diagonal):
            for g in range(heads):
                s = times_transpose(q_s[i, g], k_s[g, rows_at(j, TILE), :])
                if masked:
                    key_at = lax.broadcasted_iota(jnp.int32, s.shape, 1)
                    allowed = key_at + j * TILE >= starts
                    if diagonal:
                        query_at = lax.rem(lax.broadcasted_iota(jnp.int32, s.shape, 0), TILE)
                        allowed = allowed & (key_at <= query_at)
                    s = jnp.where(allowed, s, MASKED)
                s_s[g, j] = s
                peak = s[:, :PAD]
                for c in range(1, TILE // PAD):
                    peak = jnp.maximum(peak, s[:, c * PAD : (c + 1) * PAD])
                top_s[g] = jnp.maximum(top_s[g], peak)

        def loop(first, last, masked):
            def run(j, c):
                scores(j, masked, False)
                return c

            lax.fori_loop(first, last, run, 0)

        loop(low[i], full[i], True)
        loop(full[i], i, False)
        scores(i, True, True)
        tops = [jnp.max(top_s[g], axis=1, keepdims=True) for g in range(heads)]
        acc[...] = jnp.zeros_like(acc)

        def weigh(j, c):
            for g in range(heads):
                p = jnp.exp2(s_s[g, j] - tops[g]).astype(jnp.bfloat16)
                acc[g] += dot32(p, v_s[g, rows_at(j, TILE), :])
            return c

        lax.fori_loop(low[i], i + 1, weigh, 0)
        packed = None
        for g in range(heads):
            total = acc[g][:, PAD - 1 :]
            out = acc[g] * (1.0 / total)
            sums = jnp.broadcast_to(tops[g] + jnp.log(total) * LOG2E, (ratio * TILE, PAD))
            log_sum[g][i] = sums.T[:1, :]
            wide = jnp.concatenate(
                [out[h * TILE : (h + 1) * TILE, :] for h in range(ratio)], axis=1
            ).astype(jnp.bfloat16)
            part = dot32(wide, gather_out[g])
            packed = part if packed is None else packed + part
        subs = tiles * (TILE // SUB)
        for half in range(TILE // SUB):
            r = place[subs + i * (TILE // SUB) + half]
            part = packed[half * SUB : (half + 1) * SUB, :].astype(jnp.bfloat16)
            for k in range(pieces):

                @pl.when(r // piece_subs == k)
                def store(k=k, part=part, r=r):
                    context[k][rows_at(r % piece_subs, SUB), :] = part

        return carry

    lax.fori_loop(0, tiles, query_tile, 0)


def backward_kernel(pieces, ratio, more, *refs):
    place, low, full, cosine, sine, start, refs = *refs[:6], refs[6:]
    heads = refs[0].shape[0]
    spread_in, spread_out, gather_in, refs = *refs[:3], refs[3:]
    log_sum, refs = refs[:heads], refs[heads:]
    d_context, context, qkv, refs = refs[:pieces], refs[pieces : 2 * pieces], refs[2 * pieces], refs[2 * pieces + 1 :]
    earlier, refs = (refs[0], refs[1:]) if more else (None, refs)
    d_qkv, refs = refs[0], refs[1:]
    q_s, k_s, kt_s, v_s, do_s, delta_s, log_s, dq_acc, dk_acc, dv_acc, dq_s = refs
    tiles = q_s.shape[0]
    all_subs = qkv.shape[0] // SUB
    piece_subs = all_subs // pieces
    scale = HD ** (-0.5)
    per_tile = TILE // SUB

    for k in range(pieces):

        def prepare(r, carry, k=k):
            t = place[k * piece_subs + r]
            rel = rows_at(r, SUB)
            at = rows_at(t, SUB)
            cos_t, sin_t = cosine[at, :], sine[at, :]
            for g in range(heads):
                wide = dot32(qkv[rows_at(k * piece_subs + r, SUB), :], spread_in[g])
                d_out = dot32(d_context[k][rel, :], spread_out[g])
                out = dot32(context[k][rel, :], spread_out[g])
                for h in range(ratio):
                    cols = slice(h * PAD, (h + 1) * PAD)
                    rows = slice(h * SUB, (h + 1) * SUB)
                    query = turn(wide[:, cols], cos_t, sin_t) * (scale * LOG2E)
                    q_s[t, g, rows, :] = query.astype(jnp.bfloat16)
                    do_s[t, g, rows, :] = d_out[:, cols].astype(jnp.bfloat16)
                    delta = jnp.sum((d_out[:, cols] * out[:, cols]).T, axis=0, keepdims=True)
                    delta_s[t * heads + g, :, rows] = delta
                    first = pl.multiple_of(h * TILE + t % per_tile * SUB, SUB)
                    log_s[t * heads + g, :, rows] = log_sum[g][t // per_tile, :, pl.ds(first, SUB)]
                key = turn(wide[:, ratio * PAD : (ratio + 1) * PAD], cos_t, sin_t)
                k_s[g, t] = key.astype(jnp.bfloat16)
                kt_s[g, t] = key.T.astype(jnp.bfloat16)
                v_s[g, t] = wide[:, (ratio + 1) * PAD :].astype(jnp.bfloat16)
                dk_acc[g, t] = jnp.zeros((SUB, PAD), jnp.float32)
                dv_acc[g, t] = jnp.zeros((SUB, PAD), jnp.float32)
            return carry

        lax.fori_loop(0, piece_subs, prepare, 0)

    def query_tile(i, carry):
        dq_acc[...] = jnp.zeros_like(dq_acc)

        def step(j, masked, diagonal):
            for g in range(heads):
                queries, d_out = q_s[i, g], do_s[i, g]
                s = times_transpose(k_s[g, j], queries)
                if masked:
                    key_at = lax.broadcasted_iota(jnp.int32, s.shape, 0)
                    allowed = key_at + j * SUB >= start[i]
                    if diagonal:
                        query_at = lax.rem(lax.broadcasted_iota(jnp.int32, s.shape, 1), SUB)
                        allowed = allowed & (key_at <= query_at)
                    s = jnp.where(allowed, s, MASKED)
                p = jnp.exp2(s - log_s[i * heads + g])
                d_p = times_transpose(v_s[g, j], d_out)
                d_s = (p * (d_p - delta_s[i * heads + g])).astype(jnp.bfloat16)
                dv_acc[g, j] += dot32(p.astype(jnp.bfloat16), d_out)
                dk_acc[g, j] += dot32(d_s, queries)
                dq_acc[g] += dot32(kt_s[g, j], d_s)

        def loop(first, last, masked):
            def run(j, c):
                step(j, masked, False)
                return c

            lax.fori_loop(first, last, run, 0)

        loop(low[i], full[i], True)
        loop(full[i], i, False)
        step(i, True, True)
        at = rows_at(i, SUB)
        cos_t, sin_t = cosine[at, :], sine[at, :]
        for g in range(heads):
            grad = dq_acc[g].T * scale
            for h in range(ratio):
                piece = turn(grad[h * SUB : (h + 1) * SUB, :], cos_t, -sin_t)
                dq_s[g, i, :, h * PAD : (h + 1) * PAD] = piece.astype(jnp.bfloat16)
        return carry

    lax.fori_loop(0, tiles, query_tile, 0)

    def finish(r, carry):
        t = place[r]
        at = rows_at(t, SUB)
        rel = rows_at(r, SUB)
        packed = None
        for g in range(heads):
            key = turn(dk_acc[g, t] * (1.0 / LOG2E), cosine[at, :], -sine[at, :])
            wide = jnp.concatenate(
                [dq_s[g, t], key.astype(jnp.bfloat16), dv_acc[g, t].astype(jnp.bfloat16)], axis=1
            )
            part = dot32(wide, gather_in[g])
            packed = part if packed is None else packed + part
        packed = packed.astype(jnp.bfloat16)
        d_qkv[rel, :] = packed + earlier[rel, :] if more else packed
        return carry

    lax.fori_loop(0, all_subs, finish, 0)


SMEM = pl.BlockSpec(memory_space=pltpu.SMEM)
VMEM = pl.BlockSpec(memory_space=pltpu.VMEM)
ANY = pl.BlockSpec(memory_space=pl.ANY)


def small_cost(transcendentals=0):
    return pl.CostEstimate(flops=1 << 20, bytes_accessed=1 << 16, transcendentals=transcendentals)


def head_matrices(head, q_heads, kv_heads):
    ratio = q_heads // kv_heads
    queries = [(head * ratio + r) * HD for r in range(ratio)]
    key, value = (q_heads + head) * HD, (q_heads + kv_heads + head) * HD
    inner = spread((q_heads + 2 * kv_heads) * HD, [*queries, key, value])
    outer = spread(q_heads * HD, queries)
    return jnp.asarray(inner, jnp.bfloat16), jnp.asarray(outer, jnp.bfloat16)


def stacked_matrices(q_heads, kv_heads):
    pairs = [head_matrices(head, q_heads, kv_heads) for head in range(kv_heads)]
    return jnp.stack([inner for inner, _ in pairs]), jnp.stack([outer for _, outer in pairs])


def attend(qkv, pieces, layout, q_heads, kv_heads):
    place, low, full, cosine, sine, start_column = layout
    ratio, rows = q_heads // kv_heads, qkv.shape[0]
    tiles, lanes = rows // TILE, ratio * TILE
    bf16, f32 = jnp.bfloat16, jnp.float32
    inner, outer = stacked_matrices(q_heads, kv_heads)
    outs = pl.pallas_call(
        functools.partial(forward_kernel, pieces, ratio),
        out_shape=[
            *[jax.ShapeDtypeStruct((rows // pieces, q_heads * HD), bf16)] * pieces,
            *[jax.ShapeDtypeStruct((tiles, 1, lanes), f32)] * kv_heads,
        ],
        in_specs=[SMEM] * 3 + [VMEM] * 6,
        out_specs=[VMEM] * (pieces + kv_heads),
        scratch_shapes=[
            pltpu.VMEM((tiles, kv_heads, lanes, PAD), bf16),
            pltpu.VMEM((kv_heads, rows, PAD), bf16),
            pltpu.VMEM((kv_heads, rows, PAD), bf16),
            pltpu.VMEM((kv_heads, tiles, lanes, TILE), f32),
            pltpu.VMEM((kv_heads, lanes, PAD), f32),
            pltpu.VMEM((kv_heads, lanes, PAD), f32),
        ],
        compiler_params=pltpu.CompilerParams(vmem_limit_bytes=60 * 2**20),
        cost_estimate=small_cost(),
        name="attention_forward",
    )(place, low, full, cosine, sine, start_column, inner, jnp.swapaxes(outer, 1, 2), qkv)
    return outs[:pieces], outs[pieces:]


def attend_back(heads, qkv, d_context, context, sums, earlier, layout, q_heads, kv_heads):
    place, low, full, cosine, sine, start_row = layout
    pieces, ratio, rows = len(context), q_heads // kv_heads, qkv.shape[0]
    tiles, lanes, count = rows // SUB, ratio * SUB, len(heads)
    bf16, f32 = jnp.bfloat16, jnp.float32
    inner, outer = stacked_matrices(q_heads, kv_heads)
    inner, outer = inner[heads[0] : heads[0] + count], outer[heads[0] : heads[0] + count]
    return pl.pallas_call(
        functools.partial(backward_kernel, pieces, ratio, bool(earlier)),
        out_shape=jax.ShapeDtypeStruct(qkv.shape, bf16),
        in_specs=[SMEM] * 3 + [VMEM] * (7 + count + 2 * pieces + len(earlier)),
        out_specs=VMEM,
        scratch_shapes=[
            pltpu.VMEM((tiles, count, lanes, PAD), bf16),
            pltpu.VMEM((count, tiles, SUB, PAD), bf16),
            pltpu.VMEM((count, tiles, PAD, SUB), bf16),
            pltpu.VMEM((count, tiles, SUB, PAD), bf16),
            pltpu.VMEM((tiles, count, lanes, PAD), bf16),
            pltpu.VMEM((tiles * count, 1, lanes), f32),
            pltpu.VMEM((tiles * count, 1, lanes), f32),
            pltpu.VMEM((count, PAD, lanes), f32),
            pltpu.VMEM((count, tiles, SUB, PAD), f32),
            pltpu.VMEM((count, tiles, SUB, PAD), f32),
            pltpu.VMEM((count, tiles, SUB, ratio * PAD), bf16),
        ],
        compiler_params=pltpu.CompilerParams(vmem_limit_bytes=60 * 2**20),
        cost_estimate=small_cost(),
        name=f"attention_backward_{heads[0]}",
    )(
        place, low, full, cosine, sine, start_row, inner, outer, jnp.swapaxes(inner, 1, 2),
        *[sums[h] for h in heads], *d_context, *context, qkv, *earlier,
    )


def fetch(me, where, sources, target, sems):
    copies = []
    for n, (source, (j, deep, first, column, taken)) in enumerate(zip(sources, where, strict=True)):
        cols = min(source.shape[1] - taken, target.shape[1] - column)
        at = pl.ds(pl.multiple_of((me[0] ^ j) * deep + first, 16), source.shape[0])
        if cols != source.shape[1]:
            source = source.at[:, taken : taken + cols]
        copies.append(pltpu.make_async_copy(source, target.at[at, column : column + cols], sems.at[n]))
    return copies


def take_rows(parts, target):
    rows = target.shape[0]
    for step in range(STEPS):

        @pl.when(pl.program_id(0) == step)
        def take(step=step):
            at = 0
            for part in parts:
                first, last = max(at, step * rows), min(at + part.shape[0], (step + 1) * rows)
                if first < last:
                    target[first - step * rows : last - step * rows, :] = part[first - at : last - at, :]
                at += part.shape[0]


def at_first_step(copies, what):
    @pl.when(pl.program_id(0) == 0)
    def run():
        for copy in copies:
            what(copy)


def project_kernel(count, where, more, me, *refs):
    parts, gain, refs = refs[:count], refs[count], refs[count + 1 :]
    sources, refs = refs[: len(where[0])], refs[len(where[0]) :]
    norm_all, qkv_all, weight, sems, rows_s = refs[2 if more else 0 :]
    copies = fetch(me, where[0], sources, weight, sems)
    at_first_step(copies, lambda copy: copy.start())
    take_rows(parts, rows_s)
    x = rows_s[...].astype(jnp.float32)
    scale = lax.rsqrt(jnp.mean(x * x, axis=-1, keepdims=True) + EPSILON)
    norm_all[...] = (x * scale * gain[...]).astype(jnp.bfloat16)
    at_first_step(copies, lambda copy: copy.wait())
    qkv_all[...] = dot32(norm_all[...], weight[...]).astype(jnp.bfloat16)


def mlp_kernel(counts, where, first, last, me, *refs):
    refs = list(refs)

    def take(count):
        some, refs[:count] = refs[:count], []
        return some

    if first:
        norm_parts, grad_parts = take(counts[0]), take(counts[1])
    else:
        norm_all, grad_all, d_norm_before, out_before = take(4)
    gate_up, down = take(len(where[0])), take(len(where[1]))
    if first:
        norm_all, grad_all = take(2)
    hidden_all, d_gate_up_all = take(2)
    d_norm_refs, out_refs = take(2 if last else 1), take(2 if last else 1)
    w_gate_up, gate_up_sems, w_down, down_sems = refs
    copies = fetch(me, where[0], gate_up, w_gate_up, gate_up_sems) + fetch(me, where[1], down, w_down, down_sems)
    at_first_step(copies, lambda copy: copy.start())
    if first:
        take_rows(norm_parts, norm_all)
        take_rows(grad_parts, grad_all)
    at_first_step(copies, lambda copy: copy.wait())
    x, dy = norm_all[...], grad_all[...]
    hidden_cols = w_down.shape[1]
    width = min(512, hidden_cols)
    for at in range(0, hidden_cols, width):
        gate_at = slice(at, at + width)
        up_at = slice(hidden_cols + at, hidden_cols + at + width)
        gate = dot32(x, w_gate_up[:, gate_at])
        up = dot32(x, w_gate_up[:, up_at])
        d_hidden = dot32(dy, w_down[:, gate_at])
        sigmoid = 1.0 / (1.0 + jnp.exp(-gate))
        silu = gate * sigmoid
        hidden_all[:, gate_at] = (silu * up).astype(jnp.bfloat16)
        d_gate = d_hidden * up * sigmoid * (1.0 + gate * (1.0 - sigmoid))
        d_gate_up_all[:, gate_at] = d_gate.astype(jnp.bfloat16)
        d_gate_up_all[:, up_at] = (d_hidden * silu).astype(jnp.bfloat16)
    d_norm = times_transpose(d_gate_up_all[...], w_gate_up[...])
    out = times_transpose(hidden_all[...], w_down[...])
    if not first:
        d_norm = d_norm + d_norm_before[...].astype(jnp.float32)
        out = out + out_before[...].astype(jnp.float32)
    for n in range(len(out_refs)):

        @pl.when(pl.program_id(0) * len(out_refs) // STEPS == n)
        def store(n=n):
            d_norm_refs[n][...] = d_norm.astype(jnp.bfloat16)
            out_refs[n][...] = out.astype(jnp.bfloat16)


def mlp_call(k, count, me, norm, grad, before, gate_up, down):
    first, last = k == 0, k == count - 1
    rows, width = sum(x.shape[0] for x in norm), norm[0].shape[1]
    tile = rows // STEPS
    hidden_cols = down[2]

    def here(i):
        return (i, 0)

    def half(n):
        return lambda i: (jnp.clip(i - n * STEPS // 2, 0, STEPS // 2 - 1), 0)

    def tiles(cols):
        return pl.BlockSpec((tile, cols), here)

    sources = [*gate_up[0], *down[0]]
    if first:
        taken, specs = [*norm, *grad], [pl.BlockSpec(x.shape, lambda i: (0, 0)) for x in (*norm, *grad)]
    else:
        taken = [*norm, *grad, *before]
        specs = [tiles(width)] * 4
    shapes, out_specs = [], []
    for cols in ([width, width] if first else []) + [hidden_cols, 2 * hidden_cols]:
        shapes.append(jax.ShapeDtypeStruct((rows, cols), jnp.bfloat16))
        out_specs.append(tiles(cols))
    for _ in range(2):
        for n in range(2 if last else 1):
            shapes.append(jax.ShapeDtypeStruct((rows // 2 if last else rows, width), jnp.bfloat16))
            out_specs.append(pl.BlockSpec((tile, width), half(n) if last else here))
    return pl.pallas_call(
        functools.partial(mlp_kernel, (len(norm), len(grad)), (gate_up[1], down[1]), first, last),
        grid=(STEPS,),
        out_shape=shapes,
        in_specs=[SMEM, *specs, *[ANY] * len(sources)],
        out_specs=out_specs,
        scratch_shapes=[
            pltpu.VMEM((width, 2 * hidden_cols), jnp.bfloat16),
            pltpu.SemaphoreType.DMA((len(gate_up[0]),)),
            pltpu.VMEM((width, hidden_cols), jnp.bfloat16),
            pltpu.SemaphoreType.DMA((len(down[0]),)),
        ],
        compiler_params=pltpu.CompilerParams(vmem_limit_bytes=60 * 2**20),
        cost_estimate=small_cost(),
        name=f"mlp_{k}",
    )(me, *taken, *sources)


def project_piece(k, pieces, me, parts, gain, weight, earlier):
    tile, width = sum(x.shape[0] for x in parts) // STEPS, parts[0].shape[1]
    count = len(parts)
    arrays, where, cols = weight
    first_earlier = 2 + count + len(arrays)

    def here(i):
        return (k * STEPS + i, 0)

    return pl.pallas_call(
        functools.partial(project_kernel, count, (where,), bool(earlier)),
        grid=(STEPS,),
        out_shape=[jax.ShapeDtypeStruct((pieces * STEPS * tile, n), jnp.bfloat16) for n in (width, cols)],
        in_specs=[
            SMEM,
            *(pl.BlockSpec(x.shape, lambda i: (0, 0)) for x in (*parts, gain)),
            *[ANY] * (len(arrays) + len(earlier)),
        ],
        out_specs=[pl.BlockSpec((tile, n), here) for n in (width, cols)],
        scratch_shapes=[
            pltpu.VMEM((width, cols), jnp.bfloat16),
            pltpu.SemaphoreType.DMA((len(arrays),)),
            pltpu.VMEM((tile, width), jnp.bfloat16),
        ],
        input_output_aliases={first_earlier + n: n for n in range(len(earlier))},
        compiler_params=pltpu.CompilerParams(vmem_limit_bytes=60 * 2**20),
        cost_estimate=small_cost(),
        name=f"project_{k}",
    )(me, *parts, gain, *arrays, *earlier)


def assemble_kernel(where, me, *refs):
    sources, whole, sems = refs[: len(where)], refs[len(where)], refs[len(where) + 1]
    copies = fetch(me, where, sources, whole, sems)
    for copy in copies:
        copy.start()
    for copy in copies:
        copy.wait()


def assemble(name, me, arrays, where, rows, cols):
    return pl.pallas_call(
        functools.partial(assemble_kernel, where),
        out_shape=jax.ShapeDtypeStruct((rows, cols), arrays[0].dtype),
        in_specs=[SMEM, *[ANY] * len(arrays)],
        out_specs=VMEM,
        scratch_shapes=[pltpu.SemaphoreType.DMA((len(arrays),))],
        compiler_params=pltpu.CompilerParams(vmem_limit_bytes=60 * 2**20),
        cost_estimate=small_cost(),
        name=name,
    )(me, *arrays)


def flip(x, axis):
    return lax.ppermute(x, axis, FLIP)


CROSS = [(1, 2), (2, 1)]
OUT = [(0, 1), (3, 2), (2, 0), (1, 3)]
BACK = [(1, 0), (2, 3), (0, 2), (3, 1)]


def crossed(x, perm):
    return lax.ppermute(x, ("core", "zh"), perm)


def straight():
    return lax.axis_index("core") == lax.axis_index("zh")


def swap(x):
    return jnp.where(straight(), x, crossed(x, CROSS))


def send_z(w):
    return crossed(w, OUT), crossed(w, CROSS)


def pair_of(w, out, cross):
    zh = lax.axis_index("zh")
    x = jnp.where(straight(), w, cross)
    return jnp.concatenate([jnp.where(zh == 0, x, out), jnp.where(zh == 0, out, x)], axis=0)


def give_z(part):
    zh = lax.axis_index("zh")
    half = part.shape[0] // 2
    upper, lower = part[:half], part[half:]
    return jnp.where(zh == 0, upper, lower), jnp.where(zh == 0, lower, upper)


def sum_z(keep, back, cross):
    return back.astype(jnp.float32) + jnp.where(straight(), keep, cross).astype(jnp.float32)


def shift(x, e, k):
    n = lax.axis_size("zl")
    return lax.ppermute(
        x, ("core", "zl"), [(c * n + l, (c ^ e) * n + (l + k) % n) for c in range(2) for l in range(n)]
    )


def from_near(x, k):
    n = lax.axis_size("zl")
    return lax.ppermute(x, "zl", [((j + k) % n, j) for j in range(n)])


def to_near(x, k):
    n = lax.axis_size("zl")
    return lax.ppermute(x, "zl", [(j, (j + k) % n) for j in range(n)])


def across(x, j):
    n = lax.axis_size("yx")
    return lax.ppermute(x, "yx", [(a, a ^ j) for a in range(n)])


def neighbours(x):
    count = lax.axis_size("yx")
    return [across(x, j) for j in range(1, count if count != 4 else 3)]


def diagonal(taken):
    if lax.axis_size("yx") != 4:
        return []
    half = taken[0].shape[0] // 2
    return [across(taken[1][:half], 1), across(taken[0][half:], 2)]


def blocks_of(own, taken, halves, column=0, source_column=0):
    deep = own.shape[0]
    arrays = [own, *taken, *halves]
    where = [(j, deep, 0, column, source_column) for j in range(1 + len(taken))]
    where += [(3, deep, n * deep // 2, column, source_column) for n in range(len(halves))]
    return arrays, tuple(where)


def whole_weight(w):
    return [w], ((0, 0, 0, 0, 0),)


def block_of(grad, j, columns):
    size = grad.shape[0] // lax.axis_size("yx")
    first = (lax.axis_index("yx") ^ j) * size
    return lax.dynamic_slice(grad, (first, columns[0]), (size, columns[1] - columns[0]))


def send_yx(grad, columns):
    count = lax.axis_size("yx")
    if count != 4:
        return [across(block_of(grad, j, columns), j) for j in range(1, count)]
    far = block_of(grad, 3, columns)
    half = far.shape[0] // 2
    return [across(far[:half], 1), across(far[half:], 2)]


def join_yx(grad, columns, taken):
    if lax.axis_size("yx") != 4:
        return taken, block_of(grad, 0, columns)
    half = taken[0].shape[0]
    one, two = block_of(grad, 1, columns), block_of(grad, 2, columns)
    one = jnp.concatenate([one[:half], one[half:] + taken[1]], axis=0)
    two = jnp.concatenate([two[:half] + taken[0], two[half:]], axis=0)
    return [across(one, 1), across(two, 2)], block_of(grad, 0, columns)


def total_yx(taken, own):
    total = own.astype(jnp.float32)
    for part in taken:
        total = total + part.astype(jnp.float32)
    return total.astype(jnp.bfloat16)


def body(
    tokens,
    cotangent,
    seq_lengths,
    attn_gain,
    q_weight,
    key_projection,
    value_projection,
    out_weight,
    mlp_gain,
    gate_weight,
    up_weight,
    down_weight,
):
    bf16, f32 = jnp.bfloat16, jnp.float32
    core, zl, yx = lax.axis_index("core"), lax.axis_index("zl"), lax.axis_index("yx")
    near = lax.axis_size("zl")
    others = range(1, near)
    rows = tokens.shape[0]
    group_rows = 2 * near * rows
    query_cols, key_cols = q_weight.shape[1], key_projection.shape[1]
    qkv_cols = query_cols + 2 * key_cols
    q_heads, kv_heads = query_cols // HD, key_cols // HD
    hidden_cols = gate_weight.shape[1]
    me = yx.astype(jnp.int32).reshape(1)

    qkv_shard = jnp.concatenate([q_weight, key_projection, value_projection], axis=1)
    gate_up_shard = jnp.concatenate([gate_weight, up_weight], axis=1)
    part_rows = rows // 2
    upper = swap(tokens[:part_rows])
    shard = jnp.concatenate([qkv_shard, out_weight], axis=1)
    shard_moved = send_z(shard)
    lengths = swap(seq_lengths)
    gains = lax.all_gather(jnp.stack([attn_gain, mlp_gain]), ("yx", "core"), axis=1, tiled=True).astype(f32)
    upper, lengths, second_part, gains, *shard_moved = stage(upper, lengths, tokens[part_rows:], gains, *shard_moved)
    gain_one, gain_two = gains[0], gains[1]

    upper_far = [from_near(upper, k) for k in others]
    lower = swap(second_part)
    pair, out_pair = (
        pair_of(*(x[:, cols] for x in (shard, *shard_moved))) for cols in (slice(0, qkv_cols), slice(qkv_cols, None))
    )
    taken = neighbours(pair)
    upper_sib = flip(upper, "core")

    subs = jnp.arange(group_rows // SUB, dtype=jnp.int32)
    per_device = rows // SUB
    source, within = subs // per_device, subs % per_device
    there_core, there_zl = (source % 2) ^ core, (source // 2 + zl) % near
    to_order = (there_core * near + there_zl) * per_device + within
    from_order = (((source % near - zl) % near) * 2 + ((source // near) ^ core)) * per_device + within
    place = jnp.concatenate([to_order, from_order])
    row_at, doc_start = document_layout(lengths, group_rows)
    cosine, sine = rotary_tables(row_at - doc_start)

    def bounds(size):
        tile_start = doc_start.reshape(-1, size)
        tile = jnp.arange(group_rows // size, dtype=jnp.int32)
        low = tile_start[:, 0] // size
        return low, jnp.minimum((tile_start[:, -1] + size - 1) // size, tile)

    start_row = jnp.tile(doc_start.reshape(-1, 1, SUB), (1, 1, q_heads // kv_heads))
    layout = (place, *bounds(TILE), cosine, sine, doc_start[:, None])
    layout_back = (place, *bounds(SUB), cosine, sine, start_row)
    lower, upper_sib, out_pair, *moved = stage(lower, upper_sib, out_pair, *upper_far, *taken, *layout, *layout_back)
    upper_far, moved = moved[: near - 1], moved[near - 1 :]
    taken, moved = moved[: len(taken)], moved[len(taken) :]
    layout, layout_back = moved[: len(layout)], moved[len(layout) :]

    lower_far = [from_near(lower, k) for k in others]
    lower_sib = flip(lower, "core")
    gate_up_out = crossed(gate_up_shard, OUT)
    blocks = blocks_of(pair, taken, diagonal(taken))
    projecting = (*blocks, qkv_cols)
    gain_row = gain_one[None]
    normed = project_piece(0, near, me, [upper, lower, upper_sib, lower_sib], gain_row, projecting, [])
    gate_up_shard, gate_up_out, *moved = stage(gate_up_shard, gate_up_out, *lower_far, *normed)
    lower_far, normed = moved[: near - 1], moved[near - 1 :]

    gate_up_cross = crossed(gate_up_shard, CROSS)
    out_far = [from_near(out_pair, k) for k in others]
    for k in others:
        parts = [upper_far[k - 1], lower_far[k - 1], flip(upper_far[k - 1], "core"), flip(lower_far[k - 1], "core")]
        normed = project_piece(k, near, me, parts, gain_row, projecting, normed)
    norm_one, qkv = normed
    gate_up_cross, qkv, down_shard, *out_far = stage(gate_up_cross, qkv, down_weight, *out_far)

    gate_up_pair = pair_of(gate_up_shard, gate_up_out, gate_up_cross)
    gate_up_taken = neighbours(gate_up_pair)
    gate_up_far = [from_near(gate_up_pair, k) for k in others]
    down_moved = send_z(down_shard)
    w_out_near = lax.all_gather(jnp.concatenate([out_pair, *out_far], axis=1), "yx", axis=0, tiled=True)
    context, sums = attend(qkv, 2 * near, layout, q_heads, kv_heads)
    cotangent, *moved = stage(cotangent, *context, *down_moved, *gate_up_far, *gate_up_taken)
    context, down_moved, moved = moved[: 2 * near], moved[2 * near : 2 * near + 2], moved[2 * near + 2 :]
    gate_up_far, gate_up_taken = moved[: near - 1], moved[near - 1 :]

    quarters = {(0, 0): context[0]}
    for k in range(near):
        for e in range(2):
            if (e, k) != (0, 0):
                quarters[e, (near - k) % near] = shift(context[2 * k + e], e, k)
    order = [(e, k) for e in range(2) for k in range(near)]
    gate_up_halves = diagonal(gate_up_taken)
    down_pair = pair_of(down_weight, *down_moved)
    down_pair, cotangent, w_out_near, *moved = stage(
        down_pair, cotangent, w_out_near, *(quarters[at] for at in order), *gate_up_halves
    )
    quarters, gate_up_halves = moved[: 2 * near], moved[2 * near :]

    w_out_sib = flip(w_out_near, "core")
    down_taken = neighbours(down_pair)
    down_far = [from_near(down_pair, k) for k in others]
    cot_upper = crossed(cotangent[:part_rows], CROSS)
    residual = jnp.concatenate([upper, lower], axis=0).astype(f32)
    scale_one = lax.rsqrt(jnp.mean(residual * residual, axis=-1, keepdims=True) + EPSILON)
    w_out_sib, w_out_near, scale_one, cotangent, cot_upper, *moved = stage(
        w_out_sib, w_out_near, scale_one, cotangent, cot_upper, *down_far, *down_taken
    )
    down_far, down_taken = moved[: near - 1], moved[near - 1 :]

    gate_cols, up_cols = (slice(n * hidden_cols, (n + 1) * hidden_cols) for n in range(2))
    down_halves = diagonal(down_taken)
    cot_lower = crossed(cotangent[part_rows:], CROSS)
    gate_far_taken = [x for far in gate_up_far for x in neighbours(far[:, gate_cols])]
    own_context = jnp.concatenate(quarters[:near], axis=1)
    sib_context = jnp.concatenate(quarters[near:], axis=1)
    mid = residual + times_transpose(own_context, w_out_near) + times_transpose(sib_context, w_out_sib)
    scale_two, norm_two = norm_rows(mid, gain_two)
    cot = jnp.where(
        straight(), cotangent, jnp.concatenate([cot_upper, cot_lower], axis=0)
    )
    norm_two, cot, *moved = stage(norm_two, cot, *down_halves, *gate_far_taken)
    down_halves, gate_far_taken = moved[: len(down_halves)], moved[len(down_halves) :]
    norm_sib, cot_sib = flip(norm_two, "core"), flip(cot, "core")
    norm_sib, cot_sib, *gate_far_taken = stage(norm_sib, cot_sib, *gate_far_taken)

    def split(items):
        step = len(items) // max(near - 1, 1)
        return [items[n * step : (n + 1) * step] for n in range(near - 1)]

    gate_far_halves = [x for t in split(gate_far_taken) for x in diagonal(t)]
    up_far_taken = [x for far in gate_up_far for x in neighbours(far[:, up_cols])]
    gate_up = (*blocks_of(gate_up_pair, gate_up_taken, gate_up_halves), 2 * hidden_cols)
    down = (*blocks_of(down_pair, down_taken, down_halves), hidden_cols)
    norm_all, grad_all, hidden, d_gate_up, *sums_so_far = mlp_call(
        0, near, me, [norm_two, norm_sib], [cot, cot_sib], [], gate_up, down
    )
    norm_all, grad_all, hidden, d_gate_up, *moved = stage(
        norm_all, grad_all, hidden, d_gate_up, *sums_so_far, *gate_far_halves, *up_far_taken
    )
    sums_so_far, moved = moved[: len(sums_so_far)], moved[len(sums_so_far) :]
    gate_far_halves, up_far_taken = moved[: len(gate_far_halves)], moved[len(gate_far_halves) :]

    up_far_halves = [x for t in split(up_far_taken) for x in diagonal(t)]
    down_far_taken = [x for far in down_far for x in neighbours(far)]
    grads_gate_up = [rows_product(norm_all, d_gate_up).astype(bf16)]
    grad_all, hidden, grads_gate_up[0], *moved = stage(
        grad_all, hidden, grads_gate_up[0], *up_far_halves, *down_far_taken
    )
    up_far_halves, down_far_taken = moved[: len(up_far_halves)], moved[len(up_far_halves) :]

    gate_up_parts = [lax.psum_scatter(grads_gate_up[0], "yx", scatter_dimension=0, tiled=True)]
    down_far_halves = [x for t in split(down_far_taken) for x in diagonal(t)]
    grads_down = [rows_product(grad_all, hidden).astype(bf16)]
    norm_all, grad_all, grads_down[0], *down_far_halves = stage(norm_all, grad_all, grads_down[0], *down_far_halves)

    for k in others:
        n = k - 1
        gate_blocks = blocks_of(gate_up_far[n][:, gate_cols], split(gate_far_taken)[n], split(gate_far_halves)[n])
        up_blocks = blocks_of(gate_up_far[n][:, up_cols], split(up_far_taken)[n], split(up_far_halves)[n], hidden_cols)
        gate_up = ([*gate_blocks[0], *up_blocks[0]], gate_blocks[1] + up_blocks[1], 2 * hidden_cols)
        down = (*blocks_of(down_far[n], split(down_far_taken)[n], split(down_far_halves)[n]), hidden_cols)
        hidden, d_gate_up, *sums_so_far = mlp_call(k, near, me, [norm_all], [grad_all], sums_so_far, gate_up, down)
        if k < near - 1:
            grads_gate_up.append(rows_product(norm_all, d_gate_up).astype(bf16))
            grads_down.append(rows_product(grad_all, hidden).astype(bf16))
    d_norm_own, d_norm_sib, out_own, out_sib = sums_so_far
    d_norm_own, d_norm_sib, out_own, out_sib, hidden, d_gate_up = stage(
        d_norm_own, d_norm_sib, out_own, out_sib, hidden, d_gate_up
    )

    d_norm_two = d_norm_own.astype(f32) + flip(d_norm_sib, "core").astype(f32)
    grads_gate_up.append(rows_product(norm_all, d_gate_up).astype(bf16))
    d_norm_two, out_sib, grads_gate_up[-1] = stage(d_norm_two, out_sib, grads_gate_up[-1])
    gate_up_parts += [lax.psum_scatter(x, "yx", scatter_dimension=0, tiled=True) for x in grads_gate_up[1:]]
    mid_back, _ = norm_back(mid, scale_two, gain_two, d_norm_two)
    d_mid = cot.astype(f32) + mid_back
    d_attn = d_mid.astype(bf16)
    both = [dot32(d_attn, w).astype(bf16) for w in (w_out_near, w_out_sib)]
    d_quarters = [both[e][:, k * query_cols : (k + 1) * query_cols] for e, k in order]
    d_attn, out_sib, hidden, *d_quarters = stage(d_attn, out_sib, hidden, *d_quarters)

    d_context = [None] * (2 * near)
    for (e, k), x in zip(order, d_quarters, strict=True):
        d_context[(near - k) % near * 2 + e] = x if (e, k) == (0, 0) else shift(x, e, k)
    grads_down.append(rows_product(grad_all, hidden).astype(bf16))
    grad_out_sib = flip(rows_product(d_attn, sib_context).astype(bf16), "core")
    grad_out = (rows_product(d_attn, own_context) + grad_out_sib.astype(f32)).astype(bf16)
    output_own = (mid + out_own.astype(f32) + flip(out_sib, "core").astype(f32)).astype(bf16)
    grad_out, output_own, *moved = stage(grad_out, output_own, *d_context, *gate_up_parts, *grads_down)
    d_context, moved = moved[: 2 * near], moved[2 * near :]
    gate_up_parts, grads_down = moved[:near], moved[near:]

    output_crossed = crossed(output_own, CROSS)
    gate_up_near = [to_near(gate_up_parts[k], k) for k in others]
    w_project = assemble("assemble_project", me, *blocks, tokens.shape[1], qkv_cols)
    down_parts = [lax.psum_scatter(x, "yx", scatter_dimension=0, tiled=True) for x in grads_down]
    out_part = lax.psum_scatter(grad_out, "yx", scatter_dimension=0, tiled=True)
    d_qkv = attend_back(list(range(kv_heads)), qkv, d_context, context, sums, [], layout_back, q_heads, kv_heads)
    d_qkv, output_crossed, w_project, *moved = stage(d_qkv, output_crossed, w_project, *gate_up_near)
    gate_up_near = moved

    def summed(parts):
        total = parts[0].astype(f32)
        for part in parts[1:]:
            total = total + part.astype(f32)
        return total.astype(bf16)

    def back_part(k):
        own, sib = (d_qkv[(2 * k + e) * rows : (2 * k + e + 1) * rows] for e in range(2))
        taken = flip(times_transpose(sib, w_project).astype(bf16), "core")
        return times_transpose(own, w_project) + taken.astype(f32)

    gate_up_keep, gate_up_give = give_z(summed([gate_up_parts[0], *gate_up_near]))
    gate_up_back = crossed(gate_up_give, BACK)
    d_sent = [back_part(k).astype(bf16) for k in others]
    d_qkv, gate_up_back, gate_up_keep, *d_sent = stage(d_qkv, gate_up_back, gate_up_keep, *d_sent)

    d_upper = [to_near(d_sent[k - 1][:part_rows], k) for k in others]
    gate_up_cross = crossed(gate_up_keep, CROSS)
    grad_project = rows_product(norm_one, d_qkv).astype(bf16)
    project_sent = send_yx(grad_project, (0, qkv_cols))
    total = back_part(0)
    total, grad_project, gate_up_cross, *moved = stage(
        total, grad_project, gate_up_cross, *d_upper, *d_sent, *project_sent, *down_parts
    )
    d_upper, d_sent, moved = moved[: near - 1], moved[near - 1 : 2 * near - 2], moved[2 * near - 2 :]
    project_sent, down_parts = moved[:-near], moved[-near:]

    d_lower = [to_near(d_sent[k - 1][part_rows:], k) for k in others]
    project_rest, project_own = join_yx(grad_project, (0, qkv_cols), project_sent)
    down_near = [to_near(down_parts[k], k) for k in others]

    def input_part(at, moved):
        part = total[at]
        for x in moved:
            part = part + x.astype(f32)
        back, _ = norm_back(residual[at], scale_one[at], gain_one, part)
        return (d_mid[at] + back).astype(bf16)

    input_upper = input_part(slice(0, part_rows), d_upper)
    upper_crossed = crossed(input_upper, CROSS)
    total, input_upper, upper_crossed, out_part, *moved = stage(
        total, input_upper, upper_crossed, out_part, *d_lower, *project_rest, *down_near
    )
    d_lower, project_rest, down_near = moved[: near - 1], moved[near - 1 : -(near - 1)], moved[-(near - 1) :]

    project_keep, project_give = give_z(total_yx(project_rest, project_own))
    project_home = [crossed(project_give, BACK), crossed(project_keep, CROSS)]
    input_lower = input_part(slice(part_rows, rows), d_lower)
    lower_crossed = crossed(input_lower, CROSS)
    down_keep, down_give = give_z(summed([down_parts[0], *down_near]))
    down_home = [crossed(down_give, BACK), crossed(down_keep, CROSS)]
    out_moved = [to_near(out_part[:, k * query_cols : (k + 1) * query_cols], k) for k in others]
    out_quarter = out_part[:, :query_cols].astype(f32)
    for part in out_moved:
        out_quarter = out_quarter + part.astype(f32)
    out_keep, out_give = give_z(out_quarter.astype(bf16))
    out_home = [crossed(out_give, BACK), crossed(out_keep, CROSS)]
    grad_project = sum_z(project_keep, *project_home)
    grad_out = sum_z(out_keep, *out_home)
    grad_down = sum_z(down_keep, *down_home)
    grad_gate_up = sum_z(gate_up_keep, gate_up_back, gate_up_cross)
    output = jnp.where(straight(), output_own, output_crossed)
    input_grad = jnp.concatenate(
        [
            jnp.where(straight(), input_upper, upper_crossed),
            jnp.where(straight(), input_lower, lower_crossed),
        ],
        axis=0,
    ).astype(f32)
    gain_grads = lax.psum(
        jnp.stack(
            [
                jnp.sum(qkv_shard.astype(f32) * grad_project, axis=1),
                jnp.sum(gate_up_shard.astype(f32) * grad_gate_up, axis=1),
            ]
        ),
        ("zh", "zl"),
    ) / jnp.stack([attn_gain, mlp_gain]).astype(f32)
    return (
        output,
        input_grad,
        gain_grads[0],
        grad_project[:, :query_cols],
        grad_project[:, query_cols : query_cols + key_cols],
        grad_project[:, query_cols + key_cols :],
        grad_out,
        gain_grads[1],
        grad_gate_up[:, :hidden_cols],
        grad_gate_up[:, hidden_cols:],
        grad_down,
    )


def solution(mesh):
    dp, tensor = mesh.shape["dp"], mesh.shape["tensor"]
    fine = Mesh(mesh.devices.reshape(dp // 2, 2, 2, tensor // 2), AXES)
    by_rows, by_dp, by_both = P(AXES, None), P(("yx", "core")), P(("yx", "core"), ("zh", "zl"))
    return jax.shard_map(
        body,
        mesh=fine,
        in_specs=(
            by_rows, by_rows, P(("yx", "core"), None), by_dp, by_both, by_both, by_both, by_both,
            by_dp, by_both, by_both, by_both,
        ),
        out_specs=(
            by_rows, by_rows, by_dp, by_both, by_both, by_both, by_both, by_dp, by_both, by_both, by_both,
        ),
        check_vma=False,
    )
```

```python
import functools
import math

import jax
import jax.numpy as jnp
import numpy as np
from jax import lax
from jax.experimental import pallas as pl
from jax.experimental.pallas import tpu as pltpu
from jax.sharding import Mesh
from jax.sharding import PartitionSpec as P

HD = 96
HALF = HD // 2
PAD = 128
STEPS = 4
SUB = 256
TILE = 512

EPSILON = 1e-05
ROTARY_BASE = 100000.0
MASKED = -1e30
LOG2E = math.log2(math.e)

AXES = ("yx", "core", "zh", "zl")
FLIP = [(0, 1), (1, 0)]


def norm_rows(values, gain):
    row_scale = lax.rsqrt(jnp.mean(values * values, axis=-1, keepdims=True) + EPSILON)
    return (row_scale, (values * row_scale * gain).astype(jnp.bfloat16))


def norm_back(values, row_scale, gain, upstream):
    weighted = upstream * gain
    inner_sum = jnp.mean(weighted * values, axis=-1, keepdims=True)
    grad_in = row_scale * weighted - values * (row_scale * row_scale * row_scale) * inner_sum
    gain_part = jnp.sum(upstream * (values * row_scale), axis=0)
    return (grad_in, gain_part)


def document_layout(lengths, group_rows):
    flat_lengths = lengths.reshape(-1)
    doc_ends = jnp.cumsum(flat_lengths)
    rows = jnp.arange(group_rows, dtype=jnp.int32)
    passed = (rows[:, None] >= doc_ends[None, :]).astype(jnp.int32)
    return (rows, jnp.sum(passed * flat_lengths[None, :], axis=1))


def rotary_tables(positions):
    exponents = jnp.arange(HALF, dtype=jnp.float32) * (2.0 / HD)
    inverse = ROTARY_BASE ** (-exponents)
    angles = positions.astype(jnp.float32)[:, None] * inverse[None, :]
    cosine, sine = jnp.cos(angles), jnp.sin(angles)
    gap = jnp.zeros((positions.shape[0], PAD // 2 - HALF), jnp.float32)
    return (
        jnp.concatenate([cosine, gap, cosine, gap], axis=1),
        jnp.concatenate([-sine, gap, sine, gap], axis=1),
    )


def rows_product(left, right):
    return lax.dot_general(
        left, right, (((0,), (0,)), ((), ())), preferred_element_type=jnp.float32
    )


def times_transpose(left, right):
    return lax.dot_general(
        left, right, (((1,), (1,)), ((), ())), preferred_element_type=jnp.float32
    )


def dot32(left, right):
    return jnp.dot(left, right, preferred_element_type=jnp.float32)


def stage(*values):
    return lax.optimization_barrier(values)


def spread(columns, heads):
    matrix = np.zeros((columns, len(heads) * PAD), np.float32)
    for at, first in enumerate(heads):
        for half in range(2):
            for i in range(HALF):
                matrix[first + half * HALF + i, at * PAD + half * (PAD // 2) + i] = 1.0
    return matrix


def turn(x, cosine, sine):
    return x * cosine + pltpu.roll(x, PAD // 2, 1) * sine


def rows_at(t, size):
    return pl.ds(pl.multiple_of(t * size, size), size)


def forward_kernel(pieces, ratio, *refs):
    place, low, full, cosine, sine, start, spread_in, gather_out = refs[:8]
    heads = spread_in.shape[0]
    refs = refs[8:]
    qkv, context, refs = refs[0], refs[1 : 1 + pieces], refs[1 + pieces :]
    log_sum, refs = refs[:heads], refs[heads:]
    q_s, k_s, v_s, s_s, top_s, acc = refs
    tiles = q_s.shape[0]
    all_subs = qkv.shape[0] // SUB
    piece_subs = all_subs // pieces
    scale = LOG2E * HD ** (-0.5)
    ones_lane = lax.broadcasted_iota(jnp.int32, (SUB, PAD), 1) == PAD - 1

    def prepare(r, carry):
        t = place[r]
        at = rows_at(t, SUB)
        cos_t, sin_t = cosine[at, :], sine[at, :]
        tile, half = t // (TILE // SUB), t % (TILE // SUB)
        for g in range(heads):
            wide = dot32(qkv[rows_at(r, SUB), :], spread_in[g])
            for h in range(ratio):
                query = turn(wide[:, h * PAD : (h + 1) * PAD], cos_t, sin_t) * scale
                first = pl.multiple_of(h * TILE + half * SUB, SUB)
                q_s[tile, g, pl.ds(first, SUB), :] = query.astype(jnp.bfloat16)
            key = turn(wide[:, ratio * PAD : (ratio + 1) * PAD], cos_t, sin_t)
            k_s[g, at, :] = key.astype(jnp.bfloat16)
            value = jnp.where(ones_lane, 1.0, wide[:, (ratio + 1) * PAD :])
            v_s[g, at, :] = value.astype(jnp.bfloat16)
        return carry

    lax.fori_loop(0, all_subs, prepare, 0)

    def query_tile(i, carry):
        starts = jnp.concatenate([start[rows_at(i, TILE), :]] * ratio, axis=0)
        top_s[...] = jnp.full_like(top_s, MASKED)

        def scores(j, masked, diagonal):
            for g in range(heads):
                s = times_transpose(q_s[i, g], k_s[g, rows_at(j, TILE), :])
                if masked:
                    key_at = lax.broadcasted_iota(jnp.int32, s.shape, 1)
                    allowed = key_at + j * TILE >= starts
                    if diagonal:
                        query_at = lax.rem(lax.broadcasted_iota(jnp.int32, s.shape, 0), TILE)
                        allowed = allowed & (key_at <= query_at)
                    s = jnp.where(allowed, s, MASKED)
                s_s[g, j] = s
                peak = s[:, :PAD]
                for c in range(1, TILE // PAD):
                    peak = jnp.maximum(peak, s[:, c * PAD : (c + 1) * PAD])
                top_s[g] = jnp.maximum(top_s[g], peak)

        def loop(first, last, masked):
            def run(j, c):
                scores(j, masked, False)
                return c

            lax.fori_loop(first, last, run, 0)

        loop(low[i], full[i], True)
        loop(full[i], i, False)
        scores(i, True, True)
        tops = [jnp.max(top_s[g], axis=1, keepdims=True) for g in range(heads)]
        acc[...] = jnp.zeros_like(acc)

        def weigh(j, c):
            for g in range(heads):
                p = jnp.exp2(s_s[g, j] - tops[g]).astype(jnp.bfloat16)
                acc[g] += dot32(p, v_s[g, rows_at(j, TILE), :])
            return c

        lax.fori_loop(low[i], i + 1, weigh, 0)
        packed = None
        for g in range(heads):
            total = acc[g][:, PAD - 1 :]
            out = acc[g] * (1.0 / total)
            sums = jnp.broadcast_to(tops[g] + jnp.log(total) * LOG2E, (ratio * TILE, PAD))
            log_sum[g][i] = sums.T[:1, :]
            wide = jnp.concatenate(
                [out[h * TILE : (h + 1) * TILE, :] for h in range(ratio)], axis=1
            ).astype(jnp.bfloat16)
            part = dot32(wide, gather_out[g])
            packed = part if packed is None else packed + part
        subs = tiles * (TILE // SUB)
        for half in range(TILE // SUB):
            r = place[subs + i * (TILE // SUB) + half]
            part = packed[half * SUB : (half + 1) * SUB, :].astype(jnp.bfloat16)
            for k in range(pieces):

                @pl.when(r // piece_subs == k)
                def store(k=k, part=part, r=r):
                    context[k][rows_at(r % piece_subs, SUB), :] = part

        return carry

    lax.fori_loop(0, tiles, query_tile, 0)


def backward_kernel(pieces, ratio, more, *refs):
    place, low, full, cosine, sine, start, refs = *refs[:6], refs[6:]
    heads = refs[0].shape[0]
    spread_in, spread_out, gather_in, refs = *refs[:3], refs[3:]
    log_sum, refs = refs[:heads], refs[heads:]
    d_context, context, qkv, refs = refs[:pieces], refs[pieces : 2 * pieces], refs[2 * pieces], refs[2 * pieces + 1 :]
    earlier, refs = (refs[0], refs[1:]) if more else (None, refs)
    d_qkv, refs = refs[0], refs[1:]
    q_s, k_s, kt_s, v_s, do_s, delta_s, log_s, dq_acc, dk_acc, dv_acc, dq_s = refs
    tiles = q_s.shape[0]
    all_subs = qkv.shape[0] // SUB
    piece_subs = all_subs // pieces
    scale = HD ** (-0.5)
    per_tile = TILE // SUB

    for k in range(pieces):

        def prepare(r, carry, k=k):
            t = place[k * piece_subs + r]
            rel = rows_at(r, SUB)
            at = rows_at(t, SUB)
            cos_t, sin_t = cosine[at, :], sine[at, :]
            for g in range(heads):
                wide = dot32(qkv[rows_at(k * piece_subs + r, SUB), :], spread_in[g])
                d_out = dot32(d_context[k][rel, :], spread_out[g])
                out = dot32(context[k][rel, :], spread_out[g])
                for h in range(ratio):
                    cols = slice(h * PAD, (h + 1) * PAD)
                    rows = slice(h * SUB, (h + 1) * SUB)
                    query = turn(wide[:, cols], cos_t, sin_t) * (scale * LOG2E)
                    q_s[t, g, rows, :] = query.astype(jnp.bfloat16)
                    do_s[t, g, rows, :] = d_out[:, cols].astype(jnp.bfloat16)
                    delta = jnp.sum((d_out[:, cols] * out[:, cols]).T, axis=0, keepdims=True)
                    delta_s[t * heads + g, :, rows] = delta
                    first = pl.multiple_of(h * TILE + t % per_tile * SUB, SUB)
                    log_s[t * heads + g, :, rows] = log_sum[g][t // per_tile, :, pl.ds(first, SUB)]
                key = turn(wide[:, ratio * PAD : (ratio + 1) * PAD], cos_t, sin_t)
                k_s[g, t] = key.astype(jnp.bfloat16)
                kt_s[g, t] = key.T.astype(jnp.bfloat16)
                v_s[g, t] = wide[:, (ratio + 1) * PAD :].astype(jnp.bfloat16)
                dk_acc[g, t] = jnp.zeros((SUB, PAD), jnp.float32)
                dv_acc[g, t] = jnp.zeros((SUB, PAD), jnp.float32)
            return carry

        lax.fori_loop(0, piece_subs, prepare, 0)

    def query_tile(i, carry):
        dq_acc[...] = jnp.zeros_like(dq_acc)

        def step(j, masked, diagonal):
            for g in range(heads):
                queries, d_out = q_s[i, g], do_s[i, g]
                s = times_transpose(k_s[g, j], queries)
                if masked:
                    key_at = lax.broadcasted_iota(jnp.int32, s.shape, 0)
                    allowed = key_at + j * SUB >= start[i]
                    if diagonal:
                        query_at = lax.rem(lax.broadcasted_iota(jnp.int32, s.shape, 1), SUB)
                        allowed = allowed & (key_at <= query_at)
                    s = jnp.where(allowed, s, MASKED)
                p = jnp.exp2(s - log_s[i * heads + g])
                d_p = times_transpose(v_s[g, j], d_out)
                d_s = (p * (d_p - delta_s[i * heads + g])).astype(jnp.bfloat16)
                dv_acc[g, j] += dot32(p.astype(jnp.bfloat16), d_out)
                dk_acc[g, j] += dot32(d_s, queries)
                dq_acc[g] += dot32(kt_s[g, j], d_s)

        def loop(first, last, masked):
            def run(j, c):
                step(j, masked, False)
                return c

            lax.fori_loop(first, last, run, 0)

        loop(low[i], full[i], True)
        loop(full[i], i, False)
        step(i, True, True)
        at = rows_at(i, SUB)
        cos_t, sin_t = cosine[at, :], sine[at, :]
        for g in range(heads):
            grad = dq_acc[g].T * scale
            for h in range(ratio):
                piece = turn(grad[h * SUB : (h + 1) * SUB, :], cos_t, -sin_t)
                dq_s[g, i, :, h * PAD : (h + 1) * PAD] = piece.astype(jnp.bfloat16)
        return carry

    lax.fori_loop(0, tiles, query_tile, 0)

    def finish(r, carry):
        t = place[r]
        at = rows_at(t, SUB)
        rel = rows_at(r, SUB)
        packed = None
        for g in range(heads):
            key = turn(dk_acc[g, t] * (1.0 / LOG2E), cosine[at, :], -sine[at, :])
            wide = jnp.concatenate(
                [dq_s[g, t], key.astype(jnp.bfloat16), dv_acc[g, t].astype(jnp.bfloat16)], axis=1
            )
            part = dot32(wide, gather_in[g])
            packed = part if packed is None else packed + part
        packed = packed.astype(jnp.bfloat16)
        d_qkv[rel, :] = packed + earlier[rel, :] if more else packed
        return carry

    lax.fori_loop(0, all_subs, finish, 0)


SMEM = pl.BlockSpec(memory_space=pltpu.SMEM)
VMEM = pl.BlockSpec(memory_space=pltpu.VMEM)
ANY = pl.BlockSpec(memory_space=pl.ANY)


def small_cost(transcendentals=0):
    return pl.CostEstimate(flops=1 << 20, bytes_accessed=1 << 16, transcendentals=transcendentals)


def head_matrices(head, q_heads, kv_heads):
    ratio = q_heads // kv_heads
    queries = [(head * ratio + r) * HD for r in range(ratio)]
    key, value = (q_heads + head) * HD, (q_heads + kv_heads + head) * HD
    inner = spread((q_heads + 2 * kv_heads) * HD, [*queries, key, value])
    outer = spread(q_heads * HD, queries)
    return jnp.asarray(inner, jnp.bfloat16), jnp.asarray(outer, jnp.bfloat16)


def stacked_matrices(q_heads, kv_heads):
    pairs = [head_matrices(head, q_heads, kv_heads) for head in range(kv_heads)]
    return jnp.stack([inner for inner, _ in pairs]), jnp.stack([outer for _, outer in pairs])


def attend(qkv, pieces, layout, q_heads, kv_heads):
    place, low, full, cosine, sine, start_column = layout
    ratio, rows = q_heads // kv_heads, qkv.shape[0]
    tiles, lanes = rows // TILE, ratio * TILE
    bf16, f32 = jnp.bfloat16, jnp.float32
    inner, outer = stacked_matrices(q_heads, kv_heads)
    outs = pl.pallas_call(
        functools.partial(forward_kernel, pieces, ratio),
        out_shape=[
            *[jax.ShapeDtypeStruct((rows // pieces, q_heads * HD), bf16)] * pieces,
            *[jax.ShapeDtypeStruct((tiles, 1, lanes), f32)] * kv_heads,
        ],
        in_specs=[SMEM] * 3 + [VMEM] * 6,
        out_specs=[VMEM] * (pieces + kv_heads),
        scratch_shapes=[
            pltpu.VMEM((tiles, kv_heads, lanes, PAD), bf16),
            pltpu.VMEM((kv_heads, rows, PAD), bf16),
            pltpu.VMEM((kv_heads, rows, PAD), bf16),
            pltpu.VMEM((kv_heads, tiles, lanes, TILE), f32),
            pltpu.VMEM((kv_heads, lanes, PAD), f32),
            pltpu.VMEM((kv_heads, lanes, PAD), f32),
        ],
        compiler_params=pltpu.CompilerParams(vmem_limit_bytes=60 * 2**20),
        cost_estimate=small_cost(),
        name="attention_forward",
    )(place, low, full, cosine, sine, start_column, inner, jnp.swapaxes(outer, 1, 2), qkv)
    return outs[:pieces], outs[pieces:]


def attend_back(heads, qkv, d_context, context, sums, earlier, layout, q_heads, kv_heads):
    place, low, full, cosine, sine, start_row = layout
    pieces, ratio, rows = len(context), q_heads // kv_heads, qkv.shape[0]
    tiles, lanes, count = rows // SUB, ratio * SUB, len(heads)
    bf16, f32 = jnp.bfloat16, jnp.float32
    inner, outer = stacked_matrices(q_heads, kv_heads)
    inner, outer = inner[heads[0] : heads[0] + count], outer[heads[0] : heads[0] + count]
    return pl.pallas_call(
        functools.partial(backward_kernel, pieces, ratio, bool(earlier)),
        out_shape=jax.ShapeDtypeStruct(qkv.shape, bf16),
        in_specs=[SMEM] * 3 + [VMEM] * (7 + count + 2 * pieces + len(earlier)),
        out_specs=VMEM,
        scratch_shapes=[
            pltpu.VMEM((tiles, count, lanes, PAD), bf16),
            pltpu.VMEM((count, tiles, SUB, PAD), bf16),
            pltpu.VMEM((count, tiles, PAD, SUB), bf16),
            pltpu.VMEM((count, tiles, SUB, PAD), bf16),
            pltpu.VMEM((tiles, count, lanes, PAD), bf16),
            pltpu.VMEM((tiles * count, 1, lanes), f32),
            pltpu.VMEM((tiles * count, 1, lanes), f32),
            pltpu.VMEM((count, PAD, lanes), f32),
            pltpu.VMEM((count, tiles, SUB, PAD), f32),
            pltpu.VMEM((count, tiles, SUB, PAD), f32),
            pltpu.VMEM((count, tiles, SUB, ratio * PAD), bf16),
        ],
        compiler_params=pltpu.CompilerParams(vmem_limit_bytes=60 * 2**20),
        cost_estimate=small_cost(),
        name=f"attention_backward_{heads[0]}",
    )(
        place, low, full, cosine, sine, start_row, inner, outer, jnp.swapaxes(inner, 1, 2),
        *[sums[h] for h in heads], *d_context, *context, qkv, *earlier,
    )


def fetch(me, where, sources, target, sems):
    copies = []
    for n, (source, (j, deep, first, column, taken)) in enumerate(zip(sources, where, strict=True)):
        cols = min(source.shape[1] - taken, target.shape[1] - column)
        at = pl.ds(pl.multiple_of((me[0] ^ j) * deep + first, 16), source.shape[0])
        if cols != source.shape[1]:
            source = source.at[:, taken : taken + cols]
        copies.append(pltpu.make_async_copy(source, target.at[at, column : column + cols], sems.at[n]))
    return copies


def take_rows(parts, target):
    rows = target.shape[0]
    for step in range(STEPS):

        @pl.when(pl.program_id(0) == step)
        def take(step=step):
            at = 0
            for part in parts:
                first, last = max(at, step * rows), min(at + part.shape[0], (step + 1) * rows)
                if first < last:
                    target[first - step * rows : last - step * rows, :] = part[first - at : last - at, :]
                at += part.shape[0]


def at_first_step(copies, what):
    @pl.when(pl.program_id(0) == 0)
    def run():
        for copy in copies:
            what(copy)


def project_kernel(count, where, more, me, *refs):
    parts, gain, refs = refs[:count], refs[count], refs[count + 1 :]
    sources, refs = refs[: len(where[0])], refs[len(where[0]) :]
    norm_all, qkv_all, weight, sems, rows_s = refs[2 if more else 0 :]
    copies = fetch(me, where[0], sources, weight, sems)
    at_first_step(copies, lambda copy: copy.start())
    take_rows(parts, rows_s)
    x = rows_s[...].astype(jnp.float32)
    scale = lax.rsqrt(jnp.mean(x * x, axis=-1, keepdims=True) + EPSILON)
    norm_all[...] = (x * scale * gain[...]).astype(jnp.bfloat16)
    at_first_step(copies, lambda copy: copy.wait())
    qkv_all[...] = dot32(norm_all[...], weight[...]).astype(jnp.bfloat16)


def mlp_kernel(counts, where, first, last, me, *refs):
    refs = list(refs)

    def take(count):
        some, refs[:count] = refs[:count], []
        return some

    if first:
        norm_parts, grad_parts = take(counts[0]), take(counts[1])
    else:
        norm_all, grad_all, d_norm_before, out_before = take(4)
    gate_up, down = take(len(where[0])), take(len(where[1]))
    if first:
        norm_all, grad_all = take(2)
    hidden_all, d_gate_up_all = take(2)
    d_norm_refs, out_refs = take(2 if last else 1), take(2 if last else 1)
    w_gate_up, gate_up_sems, w_down, down_sems = refs
    copies = fetch(me, where[0], gate_up, w_gate_up, gate_up_sems) + fetch(me, where[1], down, w_down, down_sems)
    at_first_step(copies, lambda copy: copy.start())
    if first:
        take_rows(norm_parts, norm_all)
        take_rows(grad_parts, grad_all)
    at_first_step(copies, lambda copy: copy.wait())
    x, dy = norm_all[...], grad_all[...]
    hidden_cols = w_down.shape[1]
    width = min(512, hidden_cols)
    for at in range(0, hidden_cols, width):
        gate_at = slice(at, at + width)
        up_at = slice(hidden_cols + at, hidden_cols + at + width)
        gate = dot32(x, w_gate_up[:, gate_at])
        up = dot32(x, w_gate_up[:, up_at])
        d_hidden = dot32(dy, w_down[:, gate_at])
        sigmoid = 1.0 / (1.0 + jnp.exp(-gate))
        silu = gate * sigmoid
        hidden_all[:, gate_at] = (silu * up).astype(jnp.bfloat16)
        d_gate = d_hidden * up * sigmoid * (1.0 + gate * (1.0 - sigmoid))
        d_gate_up_all[:, gate_at] = d_gate.astype(jnp.bfloat16)
        d_gate_up_all[:, up_at] = (d_hidden * silu).astype(jnp.bfloat16)
    d_norm = times_transpose(d_gate_up_all[...], w_gate_up[...])
    out = times_transpose(hidden_all[...], w_down[...])
    if not first:
        d_norm = d_norm + d_norm_before[...].astype(jnp.float32)
        out = out + out_before[...].astype(jnp.float32)
    for n in range(len(out_refs)):

        @pl.when(pl.program_id(0) * len(out_refs) // STEPS == n)
        def store(n=n):
            d_norm_refs[n][...] = d_norm.astype(jnp.bfloat16)
            out_refs[n][...] = out.astype(jnp.bfloat16)


def mlp_call(k, count, me, norm, grad, before, gate_up, down):
    first, last = k == 0, k == count - 1
    rows, width = sum(x.shape[0] for x in norm), norm[0].shape[1]
    tile = rows // STEPS
    hidden_cols = down[2]

    def here(i):
        return (i, 0)

    def half(n):
        return lambda i: (jnp.clip(i - n * STEPS // 2, 0, STEPS // 2 - 1), 0)

    def tiles(cols):
        return pl.BlockSpec((tile, cols), here)

    sources = [*gate_up[0], *down[0]]
    if first:
        taken, specs = [*norm, *grad], [pl.BlockSpec(x.shape, lambda i: (0, 0)) for x in (*norm, *grad)]
    else:
        taken = [*norm, *grad, *before]
        specs = [tiles(width)] * 4
    shapes, out_specs = [], []
    for cols in ([width, width] if first else []) + [hidden_cols, 2 * hidden_cols]:
        shapes.append(jax.ShapeDtypeStruct((rows, cols), jnp.bfloat16))
        out_specs.append(tiles(cols))
    for _ in range(2):
        for n in range(2 if last else 1):
            shapes.append(jax.ShapeDtypeStruct((rows // 2 if last else rows, width), jnp.bfloat16))
            out_specs.append(pl.BlockSpec((tile, width), half(n) if last else here))
    return pl.pallas_call(
        functools.partial(mlp_kernel, (len(norm), len(grad)), (gate_up[1], down[1]), first, last),
        grid=(STEPS,),
        out_shape=shapes,
        in_specs=[SMEM, *specs, *[ANY] * len(sources)],
        out_specs=out_specs,
        scratch_shapes=[
            pltpu.VMEM((width, 2 * hidden_cols), jnp.bfloat16),
            pltpu.SemaphoreType.DMA((len(gate_up[0]),)),
            pltpu.VMEM((width, hidden_cols), jnp.bfloat16),
            pltpu.SemaphoreType.DMA((len(down[0]),)),
        ],
        compiler_params=pltpu.CompilerParams(vmem_limit_bytes=60 * 2**20),
        cost_estimate=small_cost(),
        name=f"mlp_{k}",
    )(me, *taken, *sources)


def project_piece(k, pieces, me, parts, gain, weight, earlier):
    tile, width = sum(x.shape[0] for x in parts) // STEPS, parts[0].shape[1]
    count = len(parts)
    arrays, where, cols = weight
    first_earlier = 2 + count + len(arrays)

    def here(i):
        return (k * STEPS + i, 0)

    return pl.pallas_call(
        functools.partial(project_kernel, count, (where,), bool(earlier)),
        grid=(STEPS,),
        out_shape=[jax.ShapeDtypeStruct((pieces * STEPS * tile, n), jnp.bfloat16) for n in (width, cols)],
        in_specs=[
            SMEM,
            *(pl.BlockSpec(x.shape, lambda i: (0, 0)) for x in (*parts, gain)),
            *[ANY] * (len(arrays) + len(earlier)),
        ],
        out_specs=[pl.BlockSpec((tile, n), here) for n in (width, cols)],
        scratch_shapes=[
            pltpu.VMEM((width, cols), jnp.bfloat16),
            pltpu.SemaphoreType.DMA((len(arrays),)),
            pltpu.VMEM((tile, width), jnp.bfloat16),
        ],
        input_output_aliases={first_earlier + n: n for n in range(len(earlier))},
        compiler_params=pltpu.CompilerParams(vmem_limit_bytes=60 * 2**20),
        cost_estimate=small_cost(),
        name=f"project_{k}",
    )(me, *parts, gain, *arrays, *earlier)


def assemble_kernel(where, me, *refs):
    sources, whole, sems = refs[: len(where)], refs[len(where)], refs[len(where) + 1]
    copies = fetch(me, where, sources, whole, sems)
    for copy in copies:
        copy.start()
    for copy in copies:
        copy.wait()


def assemble(name, me, arrays, where, rows, cols):
    return pl.pallas_call(
        functools.partial(assemble_kernel, where),
        out_shape=jax.ShapeDtypeStruct((rows, cols), arrays[0].dtype),
        in_specs=[SMEM, *[ANY] * len(arrays)],
        out_specs=VMEM,
        scratch_shapes=[pltpu.SemaphoreType.DMA((len(arrays),))],
        compiler_params=pltpu.CompilerParams(vmem_limit_bytes=60 * 2**20),
        cost_estimate=small_cost(),
        name=name,
    )(me, *arrays)


def flip(x, axis):
    return lax.ppermute(x, axis, FLIP)


CROSS = [(1, 2), (2, 1)]
OUT = [(0, 1), (3, 2), (2, 0), (1, 3)]
BACK = [(1, 0), (2, 3), (0, 2), (3, 1)]


def crossed(x, perm):
    return lax.ppermute(x, ("core", "zh"), perm)


def straight():
    return lax.axis_index("core") == lax.axis_index("zh")


def swap(x):
    return jnp.where(straight(), x, crossed(x, CROSS))


def send_z(w):
    return crossed(w, OUT), crossed(w, CROSS)


def pair_of(w, out, cross):
    zh = lax.axis_index("zh")
    x = jnp.where(straight(), w, cross)
    return jnp.concatenate([jnp.where(zh == 0, x, out), jnp.where(zh == 0, out, x)], axis=0)


def give_z(part):
    zh = lax.axis_index("zh")
    half = part.shape[0] // 2
    upper, lower = part[:half], part[half:]
    return jnp.where(zh == 0, upper, lower), jnp.where(zh == 0, lower, upper)


def sum_z(keep, back, cross):
    return back.astype(jnp.float32) + jnp.where(straight(), keep, cross).astype(jnp.float32)


def shift(x, e, k):
    n = lax.axis_size("zl")
    return lax.ppermute(
        x, ("core", "zl"), [(c * n + l, (c ^ e) * n + (l + k) % n) for c in range(2) for l in range(n)]
    )


def from_near(x, k):
    n = lax.axis_size("zl")
    return lax.ppermute(x, "zl", [((j + k) % n, j) for j in range(n)])


def to_near(x, k):
    n = lax.axis_size("zl")
    return lax.ppermute(x, "zl", [(j, (j + k) % n) for j in range(n)])


def across(x, j):
    n = lax.axis_size("yx")
    return lax.ppermute(x, "yx", [(a, a ^ j) for a in range(n)])


def neighbours(x):
    count = lax.axis_size("yx")
    return [across(x, j) for j in range(1, count if count != 4 else 3)]


def diagonal(taken):
    if lax.axis_size("yx") != 4:
        return []
    half = taken[0].shape[0] // 2
    return [across(taken[1][:half], 1), across(taken[0][half:], 2)]


def blocks_of(own, taken, halves, column=0, source_column=0):
    deep = own.shape[0]
    arrays = [own, *taken, *halves]
    where = [(j, deep, 0, column, source_column) for j in range(1 + len(taken))]
    where += [(3, deep, n * deep // 2, column, source_column) for n in range(len(halves))]
    return arrays, tuple(where)


def whole_weight(w):
    return [w], ((0, 0, 0, 0, 0),)


def block_of(grad, j, columns):
    size = grad.shape[0] // lax.axis_size("yx")
    first = (lax.axis_index("yx") ^ j) * size
    return lax.dynamic_slice(grad, (first, columns[0]), (size, columns[1] - columns[0]))


def send_yx(grad, columns):
    count = lax.axis_size("yx")
    if count != 4:
        return [across(block_of(grad, j, columns), j) for j in range(1, count)]
    far = block_of(grad, 3, columns)
    half = far.shape[0] // 2
    return [across(far[:half], 1), across(far[half:], 2)]


def join_yx(grad, columns, taken):
    if lax.axis_size("yx") != 4:
        return taken, block_of(grad, 0, columns)
    half = taken[0].shape[0]
    one, two = block_of(grad, 1, columns), block_of(grad, 2, columns)
    one = jnp.concatenate([one[:half], one[half:] + taken[1]], axis=0)
    two = jnp.concatenate([two[:half] + taken[0], two[half:]], axis=0)
    return [across(one, 1), across(two, 2)], block_of(grad, 0, columns)


def total_yx(taken, own):
    total = own.astype(jnp.float32)
    for part in taken:
        total = total + part.astype(jnp.float32)
    return total.astype(jnp.bfloat16)


def body(
    tokens,
    cotangent,
    seq_lengths,
    attn_gain,
    q_weight,
    key_projection,
    value_projection,
    out_weight,
    mlp_gain,
    gate_weight,
    up_weight,
    down_weight,
):
    bf16, f32 = jnp.bfloat16, jnp.float32
    core, zl, yx = lax.axis_index("core"), lax.axis_index("zl"), lax.axis_index("yx")
    near = lax.axis_size("zl")
    others = range(1, near)
    rows = tokens.shape[0]
    group_rows = 2 * near * rows
    query_cols, key_cols = q_weight.shape[1], key_projection.shape[1]
    qkv_cols = query_cols + 2 * key_cols
    q_heads, kv_heads = query_cols // HD, key_cols // HD
    hidden_cols = gate_weight.shape[1]
    me = yx.astype(jnp.int32).reshape(1)

    qkv_shard = jnp.concatenate([q_weight, key_projection, value_projection], axis=1)
    gate_up_shard = jnp.concatenate([gate_weight, up_weight], axis=1)
    part_rows = rows // 2
    upper = swap(tokens[:part_rows])
    shard = jnp.concatenate([qkv_shard, out_weight], axis=1)
    shard_moved = send_z(shard)
    lengths = swap(seq_lengths)
    gains = lax.all_gather(jnp.stack([attn_gain, mlp_gain]), ("yx", "core"), axis=1, tiled=True).astype(f32)
    upper, lengths, second_part, gains, *shard_moved = stage(upper, lengths, tokens[part_rows:], gains, *shard_moved)
    gain_one, gain_two = gains[0], gains[1]

    upper_far = [from_near(upper, k) for k in others]
    lower = swap(second_part)
    pair, out_pair = (
        pair_of(*(x[:, cols] for x in (shard, *shard_moved))) for cols in (slice(0, qkv_cols), slice(qkv_cols, None))
    )
    taken = neighbours(pair)
    upper_sib = flip(upper, "core")

    subs = jnp.arange(group_rows // SUB, dtype=jnp.int32)
    per_device = rows // SUB
    source, within = subs // per_device, subs % per_device
    there_core, there_zl = (source % 2) ^ core, (source // 2 + zl) % near
    to_order = (there_core * near + there_zl) * per_device + within
    from_order = (((source % near - zl) % near) * 2 + ((source // near) ^ core)) * per_device + within
    place = jnp.concatenate([to_order, from_order])
    row_at, doc_start = document_layout(lengths, group_rows)
    cosine, sine = rotary_tables(row_at - doc_start)

    def bounds(size):
        tile_start = doc_start.reshape(-1, size)
        tile = jnp.arange(group_rows // size, dtype=jnp.int32)
        low = tile_start[:, 0] // size
        return low, jnp.minimum((tile_start[:, -1] + size - 1) // size, tile)

    start_row = jnp.tile(doc_start.reshape(-1, 1, SUB), (1, 1, q_heads // kv_heads))
    layout = (place, *bounds(TILE), cosine, sine, doc_start[:, None])
    layout_back = (place, *bounds(SUB), cosine, sine, start_row)
    lower, upper_sib, out_pair, *moved = stage(lower, upper_sib, out_pair, *upper_far, *taken, *layout, *layout_back)
    upper_far, moved = moved[: near - 1], moved[near - 1 :]
    taken, moved = moved[: len(taken)], moved[len(taken) :]
    layout, layout_back = moved[: len(layout)], moved[len(layout) :]

    lower_far = [from_near(lower, k) for k in others]
    lower_sib = flip(lower, "core")
    gate_up_out = crossed(gate_up_shard, OUT)
    blocks = blocks_of(pair, taken, diagonal(taken))
    projecting = (*blocks, qkv_cols)
    gain_row = gain_one[None]
    normed = project_piece(0, near, me, [upper, lower, upper_sib, lower_sib], gain_row, projecting, [])
    gate_up_shard, gate_up_out, *moved = stage(gate_up_shard, gate_up_out, *lower_far, *normed)
    lower_far, normed = moved[: near - 1], moved[near - 1 :]

    gate_up_cross = crossed(gate_up_shard, CROSS)
    out_far = [from_near(out_pair, k) for k in others]
    for k in others:
        parts = [upper_far[k - 1], lower_far[k - 1], flip(upper_far[k - 1], "core"), flip(lower_far[k - 1], "core")]
        normed = project_piece(k, near, me, parts, gain_row, projecting, normed)
    norm_one, qkv = normed
    gate_up_cross, qkv, down_shard, *out_far = stage(gate_up_cross, qkv, down_weight, *out_far)

    gate_up_pair = pair_of(gate_up_shard, gate_up_out, gate_up_cross)
    gate_up_taken = neighbours(gate_up_pair)
    gate_cols, up_cols = (slice(n * hidden_cols, (n + 1) * hidden_cols) for n in range(2))
    gate_far = [from_near(gate_up_pair[:, gate_cols], k) for k in others]
    down_moved = send_z(down_shard)
    w_out_near = lax.all_gather(jnp.concatenate([out_pair, *out_far], axis=1), "yx", axis=0, tiled=True)
    context, sums = attend(qkv, 2 * near, layout, q_heads, kv_heads)
    cotangent, gate_up_pair, *moved = stage(cotangent, gate_up_pair, *context, *down_moved, *gate_far, *gate_up_taken)
    context, down_moved, moved = moved[: 2 * near], moved[2 * near : 2 * near + 2], moved[2 * near + 2 :]
    gate_far, gate_up_taken = moved[: near - 1], moved[near - 1 :]

    quarters = {(0, 0): context[0]}
    for k in range(near):
        for e in range(2):
            if (e, k) != (0, 0):
                quarters[e, (near - k) % near] = shift(context[2 * k + e], e, k)
    order = [(e, k) for e in range(2) for k in range(near)]
    gate_up_halves = diagonal(gate_up_taken)
    down_pair = pair_of(down_weight, *down_moved)
    down_pair, cotangent, w_out_near, up_pair, *moved = stage(
        down_pair, cotangent, w_out_near, gate_up_pair[:, up_cols], *(quarters[at] for at in order), *gate_up_halves
    )
    quarters, gate_up_halves = moved[: 2 * near], moved[2 * near :]

    w_out_sib = flip(w_out_near, "core")
    down_taken = neighbours(down_pair)
    up_far = [from_near(up_pair, k) for k in others]
    cot_upper = crossed(cotangent[:part_rows], CROSS)
    residual = jnp.concatenate([upper, lower], axis=0).astype(f32)
    scale_one = lax.rsqrt(jnp.mean(residual * residual, axis=-1, keepdims=True) + EPSILON)
    w_out_sib, w_out_near, scale_one, cotangent, cot_upper, *moved = stage(
        w_out_sib, w_out_near, scale_one, cotangent, cot_upper, *up_far, *gate_far, *down_taken
    )
    up_far, gate_far, down_taken = moved[: near - 1], moved[near - 1 : 2 * near - 2], moved[2 * near - 2 :]

    down_halves = diagonal(down_taken)
    cot_lower = crossed(cotangent[part_rows:], CROSS)
    gate_far_taken = [x for far in gate_far for x in neighbours(far)]
    own_context = jnp.concatenate(quarters[:near], axis=1)
    sib_context = jnp.concatenate(quarters[near:], axis=1)
    mid = residual + times_transpose(own_context, w_out_near) + times_transpose(sib_context, w_out_sib)
    scale_two, norm_two = norm_rows(mid, gain_two)
    cot = jnp.where(
        straight(), cotangent, jnp.concatenate([cot_upper, cot_lower], axis=0)
    )
    norm_two, cot, *moved = stage(norm_two, cot, *down_halves, *gate_far_taken)
    down_halves, gate_far_taken = moved[: len(down_halves)], moved[len(down_halves) :]
    norm_sib, cot_sib = flip(norm_two, "core"), flip(cot, "core")
    norm_sib, cot_sib, down_pair, *moved = stage(norm_sib, cot_sib, down_pair, *gate_far_taken, *up_far)
    gate_far_taken, up_far = moved[: len(gate_far_taken)], moved[len(gate_far_taken) :]

    def split(items):
        step = len(items) // max(near - 1, 1)
        return [items[n * step : (n + 1) * step] for n in range(near - 1)]

    gate_far_halves = [x for t in split(gate_far_taken) for x in diagonal(t)]
    up_far_taken = [x for far in up_far for x in neighbours(far)]
    down_far = [from_near(down_pair, k) for k in others]
    gate_up = (*blocks_of(gate_up_pair, gate_up_taken, gate_up_halves), 2 * hidden_cols)
    down = (*blocks_of(down_pair, down_taken, down_halves), hidden_cols)
    norm_all, grad_all, hidden, d_gate_up, *sums_so_far = mlp_call(
        0, near, me, [norm_two, norm_sib], [cot, cot_sib], [], gate_up, down
    )
    norm_all, grad_all, hidden, d_gate_up, *moved = stage(
        norm_all, grad_all, hidden, d_gate_up, *sums_so_far, *down_far, *gate_far_halves, *up_far_taken
    )
    sums_so_far, moved = moved[: len(sums_so_far)], moved[len(sums_so_far) :]
    down_far, moved = moved[: near - 1], moved[near - 1 :]
    gate_far_halves, up_far_taken = moved[: len(gate_far_halves)], moved[len(gate_far_halves) :]

    up_far_halves = [x for t in split(up_far_taken) for x in diagonal(t)]
    down_far_taken = [x for far in down_far for x in neighbours(far)]
    grads_gate_up = [rows_product(norm_all, d_gate_up).astype(bf16)]
    grad_all, hidden, grads_gate_up[0], *moved = stage(
        grad_all, hidden, grads_gate_up[0], *up_far_halves, *down_far_taken
    )
    up_far_halves, down_far_taken = moved[: len(up_far_halves)], moved[len(up_far_halves) :]

    gate_up_parts = [lax.psum_scatter(grads_gate_up[0], "yx", scatter_dimension=0, tiled=True)]
    down_far_halves = [x for t in split(down_far_taken) for x in diagonal(t)]
    grads_down = [rows_product(grad_all, hidden).astype(bf16)]
    norm_all, grad_all, grads_down[0], *down_far_halves = stage(norm_all, grad_all, grads_down[0], *down_far_halves)
    down_parts = [lax.psum_scatter(grads_down[0], "yx", scatter_dimension=0, tiled=True)]

    for k in others:
        n = k - 1
        gate_blocks = blocks_of(gate_far[n], split(gate_far_taken)[n], split(gate_far_halves)[n])
        up_blocks = blocks_of(up_far[n], split(up_far_taken)[n], split(up_far_halves)[n], hidden_cols)
        gate_up = ([*gate_blocks[0], *up_blocks[0]], gate_blocks[1] + up_blocks[1], 2 * hidden_cols)
        down = (*blocks_of(down_far[n], split(down_far_taken)[n], split(down_far_halves)[n]), hidden_cols)
        hidden, d_gate_up, *sums_so_far = mlp_call(k, near, me, [norm_all], [grad_all], sums_so_far, gate_up, down)
        if k < near - 1:
            grads_gate_up.append(rows_product(norm_all, d_gate_up).astype(bf16))
            grads_down.append(rows_product(grad_all, hidden).astype(bf16))
    d_norm_own, d_norm_sib, out_own, out_sib = sums_so_far
    d_norm_own, d_norm_sib, out_own, out_sib, hidden, d_gate_up = stage(
        d_norm_own, d_norm_sib, out_own, out_sib, hidden, d_gate_up
    )

    d_norm_two = d_norm_own.astype(f32) + flip(d_norm_sib, "core").astype(f32)
    grads_gate_up.append(rows_product(norm_all, d_gate_up).astype(bf16))
    d_norm_two, out_sib, grads_gate_up[-1] = stage(d_norm_two, out_sib, grads_gate_up[-1])
    gate_up_parts += [lax.psum_scatter(x, "yx", scatter_dimension=0, tiled=True) for x in grads_gate_up[1:]]
    mid_back, _ = norm_back(mid, scale_two, gain_two, d_norm_two)
    d_mid = cot.astype(f32) + mid_back
    d_attn = d_mid.astype(bf16)
    both = [dot32(d_attn, w).astype(bf16) for w in (w_out_near, w_out_sib)]
    d_quarters = [both[e][:, k * query_cols : (k + 1) * query_cols] for e, k in order]
    d_attn, out_sib, hidden, *d_quarters = stage(d_attn, out_sib, hidden, *d_quarters)

    d_context = [None] * (2 * near)
    for (e, k), x in zip(order, d_quarters, strict=True):
        d_context[(near - k) % near * 2 + e] = x if (e, k) == (0, 0) else shift(x, e, k)
    grads_down.append(rows_product(grad_all, hidden).astype(bf16))
    grad_out_sib = flip(rows_product(d_attn, sib_context).astype(bf16), "core")
    grad_out = (rows_product(d_attn, own_context) + grad_out_sib.astype(f32)).astype(bf16)
    output_own = (mid + out_own.astype(f32) + flip(out_sib, "core").astype(f32)).astype(bf16)
    grad_out, output_own, down_parts[0], gate_up_parts[0], *moved = stage(
        grad_out, output_own, down_parts[0], gate_up_parts[0], *d_context, *grads_down[1:]
    )
    d_context, grads_down[1:] = moved[: 2 * near], moved[2 * near :]

    output_crossed = crossed(output_own, CROSS)
    w_project = assemble("assemble_project", me, *blocks, tokens.shape[1], qkv_cols)
    down_parts += [lax.psum_scatter(x, "yx", scatter_dimension=0, tiled=True) for x in grads_down[1:]]
    out_part = lax.psum_scatter(grad_out, "yx", scatter_dimension=0, tiled=True)
    d_qkv = attend_back(list(range(kv_heads)), qkv, d_context, context, sums, [], layout_back, q_heads, kv_heads)
    d_qkv, output_crossed, w_project, *gate_up_parts = stage(d_qkv, output_crossed, w_project, *gate_up_parts)

    def summed(parts):
        total = parts[0].astype(f32)
        for part in parts[1:]:
            total = total + part.astype(f32)
        return total.astype(bf16)

    def back_part(k):
        own, sib = (d_qkv[(2 * k + e) * rows : (2 * k + e + 1) * rows] for e in range(2))
        taken = flip(times_transpose(sib, w_project).astype(bf16), "core")
        return times_transpose(own, w_project) + taken.astype(f32)

    gate_near = [to_near(gate_up_parts[k][:, gate_cols], k) for k in others]
    d_sent = [back_part(k).astype(bf16) for k in others]
    d_qkv, *moved = stage(d_qkv, *d_sent, *gate_near, *gate_up_parts)
    d_sent, gate_near, gate_up_parts = moved[: near - 1], moved[near - 1 : 2 * near - 2], moved[2 * near - 2 :]

    d_upper = [to_near(d_sent[k - 1][:part_rows], k) for k in others]
    up_near = [to_near(gate_up_parts[k][:, up_cols], k) for k in others]
    grad_project = rows_product(norm_one, d_qkv).astype(bf16)
    project_sent = send_yx(grad_project, (0, qkv_cols))
    total = back_part(0)
    gate_keep, gate_give = give_z(summed([gate_up_parts[0][:, gate_cols], *gate_near]))
    total, grad_project, gate_keep, gate_give, *moved = stage(
        total, grad_project, gate_keep, gate_give, *d_upper, *d_sent, *up_near, *project_sent
    )
    d_upper, d_sent, up_near, project_sent = (
        moved[: near - 1], moved[near - 1 : 2 * near - 2], moved[2 * near - 2 : 3 * near - 3], moved[3 * near - 3 :],
    )

    d_lower = [to_near(d_sent[k - 1][part_rows:], k) for k in others]
    project_rest, project_own = join_yx(grad_project, (0, qkv_cols), project_sent)
    gate_back = crossed(gate_give, BACK)

    def input_part(at, moved):
        part = total[at]
        for x in moved:
            part = part + x.astype(f32)
        back, _ = norm_back(residual[at], scale_one[at], gain_one, part)
        return (d_mid[at] + back).astype(bf16)

    input_upper = input_part(slice(0, part_rows), d_upper)
    upper_crossed = crossed(input_upper, CROSS)
    total, input_upper, upper_crossed, gate_back, gate_keep, out_part, *moved = stage(
        total, input_upper, upper_crossed, gate_back, gate_keep, out_part, *d_lower, *project_rest, *down_parts
    )
    d_lower, project_rest, down_parts = moved[: near - 1], moved[near - 1 : -near], moved[-near:]

    project_keep, project_give = give_z(total_yx(project_rest, project_own))
    project_home = [crossed(project_give, BACK), crossed(project_keep, CROSS)]
    input_lower = input_part(slice(part_rows, rows), d_lower)
    lower_crossed = crossed(input_lower, CROSS)
    down_near = [to_near(down_parts[k], k) for k in others]
    gate_cross = crossed(gate_keep, CROSS)
    up_keep, up_give = give_z(summed([gate_up_parts[0][:, up_cols], *up_near]))
    up_home = [crossed(up_give, BACK), crossed(up_keep, CROSS)]
    down_keep, down_give = give_z(summed([down_parts[0], *down_near]))
    down_home = [crossed(down_give, BACK), crossed(down_keep, CROSS)]
    out_moved = [to_near(out_part[:, k * query_cols : (k + 1) * query_cols], k) for k in others]
    out_quarter = out_part[:, :query_cols].astype(f32)
    for part in out_moved:
        out_quarter = out_quarter + part.astype(f32)
    out_keep, out_give = give_z(out_quarter.astype(bf16))
    out_home = [crossed(out_give, BACK), crossed(out_keep, CROSS)]
    grad_project = sum_z(project_keep, *project_home)
    grad_out = sum_z(out_keep, *out_home)
    grad_down = sum_z(down_keep, *down_home)
    grad_gate, grad_up = sum_z(gate_keep, gate_back, gate_cross), sum_z(up_keep, *up_home)
    output = jnp.where(straight(), output_own, output_crossed)
    input_grad = jnp.concatenate(
        [
            jnp.where(straight(), input_upper, upper_crossed),
            jnp.where(straight(), input_lower, lower_crossed),
        ],
        axis=0,
    ).astype(f32)
    gain_grads = lax.psum(
        jnp.stack(
            [
                jnp.sum(qkv_shard.astype(f32) * grad_project, axis=1),
                jnp.sum(gate_weight.astype(f32) * grad_gate + up_weight.astype(f32) * grad_up, axis=1),
            ]
        ),
        ("zh", "zl"),
    ) / jnp.stack([attn_gain, mlp_gain]).astype(f32)
    return (
        output,
        input_grad,
        gain_grads[0],
        grad_project[:, :query_cols],
        grad_project[:, query_cols : query_cols + key_cols],
        grad_project[:, query_cols + key_cols :],
        grad_out,
        gain_grads[1],
        grad_gate,
        grad_up,
        grad_down,
    )


def solution(mesh):
    dp, tensor = mesh.shape["dp"], mesh.shape["tensor"]
    fine = Mesh(mesh.devices.reshape(dp // 2, 2, 2, tensor // 2), AXES)
    by_rows, by_dp, by_both = P(AXES, None), P(("yx", "core")), P(("yx", "core"), ("zh", "zl"))
    return jax.shard_map(
        body,
        mesh=fine,
        in_specs=(
            by_rows, by_rows, P(("yx", "core"), None), by_dp, by_both, by_both, by_both, by_both,
            by_dp, by_both, by_both, by_both,
        ),
        out_specs=(
            by_rows, by_rows, by_dp, by_both, by_both, by_both, by_both, by_dp, by_both, by_both, by_both,
        ),
        check_vma=False,
    )
```

```python
import functools
import math

import jax
import jax.numpy as jnp
import numpy as np
from jax import lax
from jax.experimental import pallas as pl
from jax.experimental.pallas import tpu as pltpu
from jax.sharding import Mesh
from jax.sharding import PartitionSpec as P

HD = 96
HALF = HD // 2
PAD = 128
STEPS = 4
SUB = 256
TILE = 512

EPSILON = 1e-05
ROTARY_BASE = 100000.0
MASKED = -1e30
LOG2E = math.log2(math.e)

AXES = ("yx", "core", "zh", "zl")
FLIP = [(0, 1), (1, 0)]


def norm_rows(values, gain):
    row_scale = lax.rsqrt(jnp.mean(values * values, axis=-1, keepdims=True) + EPSILON)
    return (row_scale, (values * row_scale * gain).astype(jnp.bfloat16))


def norm_back(values, row_scale, gain, upstream):
    weighted = upstream * gain
    inner_sum = jnp.mean(weighted * values, axis=-1, keepdims=True)
    grad_in = row_scale * weighted - values * (row_scale * row_scale * row_scale) * inner_sum
    gain_part = jnp.sum(upstream * (values * row_scale), axis=0)
    return (grad_in, gain_part)


def document_layout(lengths, group_rows):
    flat_lengths = lengths.reshape(-1)
    doc_ends = jnp.cumsum(flat_lengths)
    rows = jnp.arange(group_rows, dtype=jnp.int32)
    passed = (rows[:, None] >= doc_ends[None, :]).astype(jnp.int32)
    return (rows, jnp.sum(passed * flat_lengths[None, :], axis=1))


def rotary_tables(positions):
    exponents = jnp.arange(HALF, dtype=jnp.float32) * (2.0 / HD)
    inverse = ROTARY_BASE ** (-exponents)
    angles = positions.astype(jnp.float32)[:, None] * inverse[None, :]
    cosine, sine = jnp.cos(angles), jnp.sin(angles)
    gap = jnp.zeros((positions.shape[0], PAD // 2 - HALF), jnp.float32)
    return (
        jnp.concatenate([cosine, gap, cosine, gap], axis=1),
        jnp.concatenate([-sine, gap, sine, gap], axis=1),
    )


def rows_product(left, right):
    return lax.dot_general(
        left, right, (((0,), (0,)), ((), ())), preferred_element_type=jnp.float32
    )


def times_transpose(left, right):
    return lax.dot_general(
        left, right, (((1,), (1,)), ((), ())), preferred_element_type=jnp.float32
    )


def dot32(left, right):
    return jnp.dot(left, right, preferred_element_type=jnp.float32)


def stage(*values):
    return lax.optimization_barrier(values)


def spread(columns, heads):
    matrix = np.zeros((columns, len(heads) * PAD), np.float32)
    for at, first in enumerate(heads):
        for half in range(2):
            for i in range(HALF):
                matrix[first + half * HALF + i, at * PAD + half * (PAD // 2) + i] = 1.0
    return matrix


def turn(x, cosine, sine):
    return x * cosine + pltpu.roll(x, PAD // 2, 1) * sine


def rows_at(t, size):
    return pl.ds(pl.multiple_of(t * size, size), size)


def forward_kernel(pieces, ratio, *refs):
    place, low, full, cosine, sine, start, spread_in, gather_out = refs[:8]
    heads = spread_in.shape[0]
    refs = refs[8:]
    qkv, context, refs = refs[0], refs[1 : 1 + pieces], refs[1 + pieces :]
    log_sum, refs = refs[:heads], refs[heads:]
    q_s, k_s, v_s, s_s, top_s, acc = refs
    tiles = q_s.shape[0]
    all_subs = qkv.shape[0] // SUB
    piece_subs = all_subs // pieces
    scale = LOG2E * HD ** (-0.5)
    ones_lane = lax.broadcasted_iota(jnp.int32, (SUB, PAD), 1) == PAD - 1

    def prepare(r, carry):
        t = place[r]
        at = rows_at(t, SUB)
        cos_t, sin_t = cosine[at, :], sine[at, :]
        tile, half = t // (TILE // SUB), t % (TILE // SUB)
        for g in range(heads):
            wide = dot32(qkv[rows_at(r, SUB), :], spread_in[g])
            for h in range(ratio):
                query = turn(wide[:, h * PAD : (h + 1) * PAD], cos_t, sin_t) * scale
                first = pl.multiple_of(h * TILE + half * SUB, SUB)
                q_s[tile, g, pl.ds(first, SUB), :] = query.astype(jnp.bfloat16)
            key = turn(wide[:, ratio * PAD : (ratio + 1) * PAD], cos_t, sin_t)
            k_s[g, at, :] = key.astype(jnp.bfloat16)
            value = jnp.where(ones_lane, 1.0, wide[:, (ratio + 1) * PAD :])
            v_s[g, at, :] = value.astype(jnp.bfloat16)
        return carry

    lax.fori_loop(0, all_subs, prepare, 0)

    def query_tile(i, carry):
        starts = jnp.concatenate([start[rows_at(i, TILE), :]] * ratio, axis=0)
        top_s[...] = jnp.full_like(top_s, MASKED)

        def scores(j, masked, diagonal):
            for g in range(heads):
                s = times_transpose(q_s[i, g], k_s[g, rows_at(j, TILE), :])
                if masked:
                    key_at = lax.broadcasted_iota(jnp.int32, s.shape, 1)
                    allowed = key_at + j * TILE >= starts
                    if diagonal:
                        query_at = lax.rem(lax.broadcasted_iota(jnp.int32, s.shape, 0), TILE)
                        allowed = allowed & (key_at <= query_at)
                    s = jnp.where(allowed, s, MASKED)
                s_s[g, j] = s
                peak = s[:, :PAD]
                for c in range(1, TILE // PAD):
                    peak = jnp.maximum(peak, s[:, c * PAD : (c + 1) * PAD])
                top_s[g] = jnp.maximum(top_s[g], peak)

        def loop(first, last, masked):
            def run(j, c):
                scores(j, masked, False)
                return c

            lax.fori_loop(first, last, run, 0)

        loop(low[i], full[i], True)
        loop(full[i], i, False)
        scores(i, True, True)
        tops = [jnp.max(top_s[g], axis=1, keepdims=True) for g in range(heads)]
        acc[...] = jnp.zeros_like(acc)

        def weigh(j, c):
            for g in range(heads):
                p = jnp.exp2(s_s[g, j] - tops[g]).astype(jnp.bfloat16)
                acc[g] += dot32(p, v_s[g, rows_at(j, TILE), :])
            return c

        lax.fori_loop(low[i], i + 1, weigh, 0)
        packed = None
        for g in range(heads):
            total = acc[g][:, PAD - 1 :]
            out = acc[g] * (1.0 / total)
            sums = jnp.broadcast_to(tops[g] + jnp.log(total) * LOG2E, (ratio * TILE, PAD))
            log_sum[g][i] = sums.T[:1, :]
            wide = jnp.concatenate(
                [out[h * TILE : (h + 1) * TILE, :] for h in range(ratio)], axis=1
            ).astype(jnp.bfloat16)
            part = dot32(wide, gather_out[g])
            packed = part if packed is None else packed + part
        subs = tiles * (TILE // SUB)
        for half in range(TILE // SUB):
            r = place[subs + i * (TILE // SUB) + half]
            part = packed[half * SUB : (half + 1) * SUB, :].astype(jnp.bfloat16)
            for k in range(pieces):

                @pl.when(r // piece_subs == k)
                def store(k=k, part=part, r=r):
                    context[k][rows_at(r % piece_subs, SUB), :] = part

        return carry

    lax.fori_loop(0, tiles, query_tile, 0)


def backward_kernel(pieces, ratio, more, *refs):
    place, low, full, cosine, sine, start, refs = *refs[:6], refs[6:]
    heads = refs[0].shape[0]
    spread_in, spread_out, gather_in, refs = *refs[:3], refs[3:]
    log_sum, refs = refs[:heads], refs[heads:]
    d_context, context, qkv, refs = refs[:pieces], refs[pieces : 2 * pieces], refs[2 * pieces], refs[2 * pieces + 1 :]
    earlier, refs = (refs[0], refs[1:]) if more else (None, refs)
    d_qkv, refs = refs[0], refs[1:]
    q_s, k_s, kt_s, v_s, do_s, delta_s, log_s, dq_acc, dk_acc, dv_acc, dq_s = refs
    tiles = q_s.shape[0]
    all_subs = qkv.shape[0] // SUB
    piece_subs = all_subs // pieces
    scale = HD ** (-0.5)
    per_tile = TILE // SUB

    for k in range(pieces):

        def prepare(r, carry, k=k):
            t = place[k * piece_subs + r]
            rel = rows_at(r, SUB)
            at = rows_at(t, SUB)
            cos_t, sin_t = cosine[at, :], sine[at, :]
            for g in range(heads):
                wide = dot32(qkv[rows_at(k * piece_subs + r, SUB), :], spread_in[g])
                d_out = dot32(d_context[k][rel, :], spread_out[g])
                out = dot32(context[k][rel, :], spread_out[g])
                for h in range(ratio):
                    cols = slice(h * PAD, (h + 1) * PAD)
                    rows = slice(h * SUB, (h + 1) * SUB)
                    query = turn(wide[:, cols], cos_t, sin_t) * (scale * LOG2E)
                    q_s[t, g, rows, :] = query.astype(jnp.bfloat16)
                    do_s[t, g, rows, :] = d_out[:, cols].astype(jnp.bfloat16)
                    delta = jnp.sum((d_out[:, cols] * out[:, cols]).T, axis=0, keepdims=True)
                    delta_s[t * heads + g, :, rows] = delta
                    first = pl.multiple_of(h * TILE + t % per_tile * SUB, SUB)
                    log_s[t * heads + g, :, rows] = log_sum[g][t // per_tile, :, pl.ds(first, SUB)]
                key = turn(wide[:, ratio * PAD : (ratio + 1) * PAD], cos_t, sin_t)
                k_s[g, t] = key.astype(jnp.bfloat16)
                kt_s[g, t] = key.T.astype(jnp.bfloat16)
                v_s[g, t] = wide[:, (ratio + 1) * PAD :].astype(jnp.bfloat16)
                dk_acc[g, t] = jnp.zeros((SUB, PAD), jnp.float32)
                dv_acc[g, t] = jnp.zeros((SUB, PAD), jnp.float32)
            return carry

        lax.fori_loop(0, piece_subs, prepare, 0)

    def query_tile(i, carry):
        dq_acc[...] = jnp.zeros_like(dq_acc)

        def step(j, masked, diagonal):
            for g in range(heads):
                queries, d_out = q_s[i, g], do_s[i, g]
                s = times_transpose(k_s[g, j], queries)
                if masked:
                    key_at = lax.broadcasted_iota(jnp.int32, s.shape, 0)
                    allowed = key_at + j * SUB >= start[i]
                    if diagonal:
                        query_at = lax.rem(lax.broadcasted_iota(jnp.int32, s.shape, 1), SUB)
                        allowed = allowed & (key_at <= query_at)
                    s = jnp.where(allowed, s, MASKED)
                p = jnp.exp2(s - log_s[i * heads + g])
                d_p = times_transpose(v_s[g, j], d_out)
                d_s = (p * (d_p - delta_s[i * heads + g])).astype(jnp.bfloat16)
                dv_acc[g, j] += dot32(p.astype(jnp.bfloat16), d_out)
                dk_acc[g, j] += dot32(d_s, queries)
                dq_acc[g] += dot32(kt_s[g, j], d_s)

        def loop(first, last, masked):
            def run(j, c):
                step(j, masked, False)
                return c

            lax.fori_loop(first, last, run, 0)

        loop(low[i], full[i], True)
        loop(full[i], i, False)
        step(i, True, True)
        at = rows_at(i, SUB)
        cos_t, sin_t = cosine[at, :], sine[at, :]
        for g in range(heads):
            grad = dq_acc[g].T * scale
            for h in range(ratio):
                piece = turn(grad[h * SUB : (h + 1) * SUB, :], cos_t, -sin_t)
                dq_s[g, i, :, h * PAD : (h + 1) * PAD] = piece.astype(jnp.bfloat16)
        return carry

    lax.fori_loop(0, tiles, query_tile, 0)

    def finish(r, carry):
        t = place[r]
        at = rows_at(t, SUB)
        rel = rows_at(r, SUB)
        packed = None
        for g in range(heads):
            key = turn(dk_acc[g, t] * (1.0 / LOG2E), cosine[at, :], -sine[at, :])
            wide = jnp.concatenate(
                [dq_s[g, t], key.astype(jnp.bfloat16), dv_acc[g, t].astype(jnp.bfloat16)], axis=1
            )
            part = dot32(wide, gather_in[g])
            packed = part if packed is None else packed + part
        packed = packed.astype(jnp.bfloat16)
        d_qkv[rel, :] = packed + earlier[rel, :] if more else packed
        return carry

    lax.fori_loop(0, all_subs, finish, 0)


SMEM = pl.BlockSpec(memory_space=pltpu.SMEM)
VMEM = pl.BlockSpec(memory_space=pltpu.VMEM)
ANY = pl.BlockSpec(memory_space=pl.ANY)


def small_cost(transcendentals=0):
    return pl.CostEstimate(flops=1 << 20, bytes_accessed=1 << 16, transcendentals=transcendentals)


def head_matrices(head, q_heads, kv_heads):
    ratio = q_heads // kv_heads
    queries = [(head * ratio + r) * HD for r in range(ratio)]
    key, value = (q_heads + head) * HD, (q_heads + kv_heads + head) * HD
    inner = spread((q_heads + 2 * kv_heads) * HD, [*queries, key, value])
    outer = spread(q_heads * HD, queries)
    return jnp.asarray(inner, jnp.bfloat16), jnp.asarray(outer, jnp.bfloat16)


def stacked_matrices(q_heads, kv_heads):
    pairs = [head_matrices(head, q_heads, kv_heads) for head in range(kv_heads)]
    return jnp.stack([inner for inner, _ in pairs]), jnp.stack([outer for _, outer in pairs])


def attend(qkv, pieces, layout, q_heads, kv_heads):
    place, low, full, cosine, sine, start_column = layout
    ratio, rows = q_heads // kv_heads, qkv.shape[0]
    tiles, lanes = rows // TILE, ratio * TILE
    bf16, f32 = jnp.bfloat16, jnp.float32
    inner, outer = stacked_matrices(q_heads, kv_heads)
    outs = pl.pallas_call(
        functools.partial(forward_kernel, pieces, ratio),
        out_shape=[
            *[jax.ShapeDtypeStruct((rows // pieces, q_heads * HD), bf16)] * pieces,
            *[jax.ShapeDtypeStruct((tiles, 1, lanes), f32)] * kv_heads,
        ],
        in_specs=[SMEM] * 3 + [VMEM] * 6,
        out_specs=[VMEM] * (pieces + kv_heads),
        scratch_shapes=[
            pltpu.VMEM((tiles, kv_heads, lanes, PAD), bf16),
            pltpu.VMEM((kv_heads, rows, PAD), bf16),
            pltpu.VMEM((kv_heads, rows, PAD), bf16),
            pltpu.VMEM((kv_heads, tiles, lanes, TILE), f32),
            pltpu.VMEM((kv_heads, lanes, PAD), f32),
            pltpu.VMEM((kv_heads, lanes, PAD), f32),
        ],
        compiler_params=pltpu.CompilerParams(vmem_limit_bytes=60 * 2**20),
        cost_estimate=small_cost(),
        name="attention_forward",
    )(place, low, full, cosine, sine, start_column, inner, jnp.swapaxes(outer, 1, 2), qkv)
    return outs[:pieces], outs[pieces:]


def attend_back(heads, qkv, d_context, context, sums, earlier, layout, q_heads, kv_heads):
    place, low, full, cosine, sine, start_row = layout
    pieces, ratio, rows = len(context), q_heads // kv_heads, qkv.shape[0]
    tiles, lanes, count = rows // SUB, ratio * SUB, len(heads)
    bf16, f32 = jnp.bfloat16, jnp.float32
    inner, outer = stacked_matrices(q_heads, kv_heads)
    inner, outer = inner[heads[0] : heads[0] + count], outer[heads[0] : heads[0] + count]
    return pl.pallas_call(
        functools.partial(backward_kernel, pieces, ratio, bool(earlier)),
        out_shape=jax.ShapeDtypeStruct(qkv.shape, bf16),
        in_specs=[SMEM] * 3 + [VMEM] * (7 + count + 2 * pieces + len(earlier)),
        out_specs=VMEM,
        scratch_shapes=[
            pltpu.VMEM((tiles, count, lanes, PAD), bf16),
            pltpu.VMEM((count, tiles, SUB, PAD), bf16),
            pltpu.VMEM((count, tiles, PAD, SUB), bf16),
            pltpu.VMEM((count, tiles, SUB, PAD), bf16),
            pltpu.VMEM((tiles, count, lanes, PAD), bf16),
            pltpu.VMEM((tiles * count, 1, lanes), f32),
            pltpu.VMEM((tiles * count, 1, lanes), f32),
            pltpu.VMEM((count, PAD, lanes), f32),
            pltpu.VMEM((count, tiles, SUB, PAD), f32),
            pltpu.VMEM((count, tiles, SUB, PAD), f32),
            pltpu.VMEM((count, tiles, SUB, ratio * PAD), bf16),
        ],
        compiler_params=pltpu.CompilerParams(vmem_limit_bytes=60 * 2**20),
        cost_estimate=small_cost(),
        name=f"attention_backward_{heads[0]}",
    )(
        place, low, full, cosine, sine, start_row, inner, outer, jnp.swapaxes(inner, 1, 2),
        *[sums[h] for h in heads], *d_context, *context, qkv, *earlier,
    )


def fetch(me, where, sources, target, sems):
    copies = []
    for n, (source, (j, deep, first, column, taken)) in enumerate(zip(sources, where, strict=True)):
        cols = min(source.shape[1] - taken, target.shape[1] - column)
        at = pl.ds(pl.multiple_of((me[0] ^ j) * deep + first, 16), source.shape[0])
        if cols != source.shape[1]:
            source = source.at[:, taken : taken + cols]
        copies.append(pltpu.make_async_copy(source, target.at[at, column : column + cols], sems.at[n]))
    return copies


def take_rows(parts, target):
    rows = target.shape[0]
    for step in range(STEPS):

        @pl.when(pl.program_id(0) == step)
        def take(step=step):
            at = 0
            for part in parts:
                first, last = max(at, step * rows), min(at + part.shape[0], (step + 1) * rows)
                if first < last:
                    target[first - step * rows : last - step * rows, :] = part[first - at : last - at, :]
                at += part.shape[0]


def at_first_step(copies, what):
    @pl.when(pl.program_id(0) == 0)
    def run():
        for copy in copies:
            what(copy)


def project_kernel(count, where, more, me, *refs):
    parts, gain, refs = refs[:count], refs[count], refs[count + 1 :]
    sources, refs = refs[: len(where[0])], refs[len(where[0]) :]
    norm_all, qkv_all, weight, sems, rows_s = refs[2 if more else 0 :]
    copies = fetch(me, where[0], sources, weight, sems)
    at_first_step(copies, lambda copy: copy.start())
    take_rows(parts, rows_s)
    x = rows_s[...].astype(jnp.float32)
    scale = lax.rsqrt(jnp.mean(x * x, axis=-1, keepdims=True) + EPSILON)
    norm_all[...] = (x * scale * gain[...]).astype(jnp.bfloat16)
    at_first_step(copies, lambda copy: copy.wait())
    qkv_all[...] = dot32(norm_all[...], weight[...]).astype(jnp.bfloat16)


def by_half(refs, value):
    for n, ref in enumerate(refs):

        @pl.when(pl.program_id(0) * 2 // STEPS == n)
        def store(ref=ref):
            ref[...] = value


def gate_kernel(count, where, more, me, *refs):
    parts, refs = refs[:count], refs[count:]
    with_out = len(where) > 1
    sources, refs = refs[: sum(map(len, where))], refs[sum(map(len, where)) :]
    norm_all, gate_up_all, hidden_all, *refs = refs[3 if more else 0 :]
    out_refs, refs = (refs[:2], refs[2:]) if with_out else ((), refs)
    weight, sems, *refs = refs
    hidden_cols = hidden_all.shape[1]
    copies = fetch(me, where[0], sources[: len(where[0])], weight, sems)
    if with_out:
        w_down, down_sems = refs
        copies += fetch(me, where[1], sources[len(where[0]) :], w_down, down_sems)
    at_first_step(copies, lambda copy: copy.start())
    take_rows(parts, norm_all)
    at_first_step(copies, lambda copy: copy.wait())
    x = norm_all[...]
    width = min(512, hidden_cols)
    for at in range(0, hidden_cols, width):
        gate_at = slice(at, at + width)
        up_at = slice(hidden_cols + at, hidden_cols + at + width)
        gate = dot32(x, weight[:, gate_at])
        up = dot32(x, weight[:, up_at])
        gate_up_all[:, gate_at] = gate
        gate_up_all[:, up_at] = up
        hidden_all[:, gate_at] = (gate * (1.0 / (1.0 + jnp.exp(-gate))) * up).astype(jnp.bfloat16)
    if with_out:
        by_half(out_refs, times_transpose(hidden_all[...], w_down[...]).astype(jnp.bfloat16))


def gate_back_kernel(count, where, more, me, *refs):
    parts, gate_up_all, hidden_here, refs = refs[:count], *refs[count : count + 2], refs[count + 2 :]
    gate_up, refs = refs[: len(where[0])], refs[len(where[0]) :]
    down, refs = refs[: len(where[1])], refs[len(where[1]) :]
    grad_all, d_gate_up_all, *refs = refs[2 if more else 0 :]
    d_norm_refs, refs = refs[:2], refs[2:]
    out_refs, refs = ((), refs) if more else (refs[:2], refs[2:])
    w_gate_up, gate_up_sems, w_down, down_sems = refs
    hidden_cols = w_down.shape[1]
    down_copies = fetch(me, where[1], down, w_down, down_sems)
    copies = fetch(me, where[0], gate_up, w_gate_up, gate_up_sems)
    at_first_step(down_copies + copies, lambda copy: copy.start())
    take_rows(parts, grad_all)
    at_first_step(down_copies, lambda copy: copy.wait())
    dy = grad_all[...]
    width = min(512, hidden_cols)
    for at in range(0, hidden_cols, width):
        gate_at = slice(at, at + width)
        up_at = slice(hidden_cols + at, hidden_cols + at + width)
        d_hidden = dot32(dy, w_down[:, gate_at])
        gate, up = gate_up_all[:, gate_at], gate_up_all[:, up_at]
        sigmoid = 1.0 / (1.0 + jnp.exp(-gate))
        d_gate = d_hidden * up * sigmoid * (1.0 + gate * (1.0 - sigmoid))
        d_gate_up_all[:, gate_at] = d_gate.astype(jnp.bfloat16)
        d_gate_up_all[:, up_at] = (d_hidden * (gate * sigmoid)).astype(jnp.bfloat16)
    if not more:
        by_half(out_refs, times_transpose(hidden_here[...], w_down[...]).astype(jnp.bfloat16))
    at_first_step(copies, lambda copy: copy.wait())
    by_half(d_norm_refs, times_transpose(d_gate_up_all[...], w_gate_up[...]).astype(jnp.bfloat16))


def piece_call(kernel, name, k, pieces, me, parts, whole, tiled, fetched, earlier, outs):
    tile, width = sum(x.shape[0] for x in parts) // STEPS, parts[0].shape[1]
    count = len(parts)

    def rows_of(piece):
        return lambda i: (piece * STEPS + i, 0)

    def half_of(span):
        first = 0 if span == "own" else STEPS // 2
        return lambda i: (jnp.clip(i - first, 0, STEPS // 2 - 1), 0)

    sources = [x for arrays, _, _ in fetched for x in arrays]
    first_earlier = 1 + count + len(whole) + len(tiled) + len(sources)
    scratch = []
    for arrays, _, cols in fetched:
        scratch += [pltpu.VMEM((width, cols), jnp.bfloat16), pltpu.SemaphoreType.DMA((len(arrays),))]
    if kernel is project_kernel:
        scratch.append(pltpu.VMEM((tile, width), jnp.bfloat16))
    return pl.pallas_call(
        functools.partial(kernel, count, tuple(where for _, where, _ in fetched), bool(earlier)),
        grid=(STEPS,),
        out_shape=[
            jax.ShapeDtypeStruct(((pieces * STEPS if span == "all" else STEPS // 2) * tile, columns), kind)
            for columns, kind, span in outs
        ],
        in_specs=[
            SMEM,
            *(pl.BlockSpec(x.shape, lambda i: (0, 0)) for x in parts),
            *(pl.BlockSpec(x.shape, lambda i: (0, 0)) for x in whole),
            *(pl.BlockSpec((tile, x.shape[1]), rows_of(piece)) for x, piece in tiled),
            *[ANY] * (len(sources) + len(earlier)),
        ],
        out_specs=[
            pl.BlockSpec((tile, columns), rows_of(k) if span == "all" else half_of(span))
            for columns, kind, span in outs
        ],
        scratch_shapes=scratch,
        input_output_aliases={first_earlier + n: n for n in range(len(earlier))},
        compiler_params=pltpu.CompilerParams(vmem_limit_bytes=60 * 2**20),
        cost_estimate=small_cost(),
        name=f"{name}_{k}",
    )(me, *parts, *whole, *(x for x, _ in tiled), *sources, *earlier)


def assemble_kernel(where, me, *refs):
    sources, whole, sems = refs[: len(where)], refs[len(where)], refs[len(where) + 1]
    copies = fetch(me, where, sources, whole, sems)
    for copy in copies:
        copy.start()
    for copy in copies:
        copy.wait()


def assemble(name, me, arrays, where, rows, cols):
    return pl.pallas_call(
        functools.partial(assemble_kernel, where),
        out_shape=jax.ShapeDtypeStruct((rows, cols), arrays[0].dtype),
        in_specs=[SMEM, *[ANY] * len(arrays)],
        out_specs=VMEM,
        scratch_shapes=[pltpu.SemaphoreType.DMA((len(arrays),))],
        compiler_params=pltpu.CompilerParams(vmem_limit_bytes=60 * 2**20),
        cost_estimate=small_cost(),
        name=name,
    )(me, *arrays)


def flip(x, axis):
    return lax.ppermute(x, axis, FLIP)


CROSS = [(1, 2), (2, 1)]
OUT = [(0, 1), (3, 2), (2, 0), (1, 3)]
BACK = [(1, 0), (2, 3), (0, 2), (3, 1)]


def crossed(x, perm):
    return lax.ppermute(x, ("core", "zh"), perm)


def straight():
    return lax.axis_index("core") == lax.axis_index("zh")


def swap(x):
    return jnp.where(straight(), x, crossed(x, CROSS))


def send_z(w):
    return crossed(w, OUT), crossed(w, CROSS)


def pair_of(w, out, cross):
    zh = lax.axis_index("zh")
    x = jnp.where(straight(), w, cross)
    return jnp.concatenate([jnp.where(zh == 0, x, out), jnp.where(zh == 0, out, x)], axis=0)


def give_z(part):
    zh = lax.axis_index("zh")
    half = part.shape[0] // 2
    upper, lower = part[:half], part[half:]
    return jnp.where(zh == 0, upper, lower), jnp.where(zh == 0, lower, upper)


def sum_z(keep, back, cross):
    return back.astype(jnp.float32) + jnp.where(straight(), keep, cross).astype(jnp.float32)


def shift(x, e, k):
    n = lax.axis_size("zl")
    return lax.ppermute(
        x, ("core", "zl"), [(c * n + l, (c ^ e) * n + (l + k) % n) for c in range(2) for l in range(n)]
    )


def from_near(x, k):
    n = lax.axis_size("zl")
    return lax.ppermute(x, "zl", [((j + k) % n, j) for j in range(n)])


def to_near(x, k):
    n = lax.axis_size("zl")
    return lax.ppermute(x, "zl", [(j, (j + k) % n) for j in range(n)])


def across(x, j):
    n = lax.axis_size("yx")
    return lax.ppermute(x, "yx", [(a, a ^ j) for a in range(n)])


def neighbours(x):
    count = lax.axis_size("yx")
    return [across(x, j) for j in range(1, count if count != 4 else 3)]


def diagonal(taken):
    if lax.axis_size("yx") != 4:
        return []
    half = taken[0].shape[0] // 2
    return [across(taken[1][:half], 1), across(taken[0][half:], 2)]


def blocks_of(own, taken, halves, column=0, source_column=0):
    deep = own.shape[0]
    arrays = [own, *taken, *halves]
    where = [(j, deep, 0, column, source_column) for j in range(1 + len(taken))]
    where += [(3, deep, n * deep // 2, column, source_column) for n in range(len(halves))]
    return arrays, tuple(where)


def whole_weight(w):
    return [w], ((0, 0, 0, 0, 0),)


def block_of(grad, j, columns):
    size = grad.shape[0] // lax.axis_size("yx")
    first = (lax.axis_index("yx") ^ j) * size
    return lax.dynamic_slice(grad, (first, columns[0]), (size, columns[1] - columns[0]))


def send_yx(grad, columns):
    count = lax.axis_size("yx")
    if count != 4:
        return [across(block_of(grad, j, columns), j) for j in range(1, count)]
    far = block_of(grad, 3, columns)
    half = far.shape[0] // 2
    return [across(far[:half], 1), across(far[half:], 2)]


def join_yx(grad, columns, taken):
    if lax.axis_size("yx") != 4:
        return taken, block_of(grad, 0, columns)
    half = taken[0].shape[0]
    one, two = block_of(grad, 1, columns), block_of(grad, 2, columns)
    one = jnp.concatenate([one[:half], one[half:] + taken[1]], axis=0)
    two = jnp.concatenate([two[:half] + taken[0], two[half:]], axis=0)
    return [across(one, 1), across(two, 2)], block_of(grad, 0, columns)


def total_yx(taken, own):
    total = own.astype(jnp.float32)
    for part in taken:
        total = total + part.astype(jnp.float32)
    return total.astype(jnp.bfloat16)


def body(
    tokens,
    cotangent,
    seq_lengths,
    attn_gain,
    q_weight,
    key_projection,
    value_projection,
    out_weight,
    mlp_gain,
    gate_weight,
    up_weight,
    down_weight,
):
    bf16, f32 = jnp.bfloat16, jnp.float32
    core, zl, yx = lax.axis_index("core"), lax.axis_index("zl"), lax.axis_index("yx")
    near = lax.axis_size("zl")
    others = range(1, near)
    rows = tokens.shape[0]
    group_rows = 2 * near * rows
    query_cols, key_cols = q_weight.shape[1], key_projection.shape[1]
    qkv_cols = query_cols + 2 * key_cols
    q_heads, kv_heads = query_cols // HD, key_cols // HD
    hidden_cols = gate_weight.shape[1]
    me = yx.astype(jnp.int32).reshape(1)

    qkv_shard = jnp.concatenate([q_weight, key_projection, value_projection], axis=1)
    gate_up_shard = jnp.concatenate([gate_weight, up_weight], axis=1)
    part_rows = rows // 2
    upper = swap(tokens[:part_rows])
    shard = jnp.concatenate([qkv_shard, out_weight], axis=1)
    shard_moved = send_z(shard)
    lengths = swap(seq_lengths)
    gains = lax.all_gather(jnp.stack([attn_gain, mlp_gain]), ("yx", "core"), axis=1, tiled=True).astype(f32)
    upper, lengths, second_part, gains, *shard_moved = stage(upper, lengths, tokens[part_rows:], gains, *shard_moved)
    gain_one, gain_two = gains[0], gains[1]

    upper_far = [from_near(upper, k) for k in others]
    lower = swap(second_part)
    pair, out_pair = (
        pair_of(*(x[:, cols] for x in (shard, *shard_moved))) for cols in (slice(0, qkv_cols), slice(qkv_cols, None))
    )
    taken = neighbours(pair)
    upper_sib = flip(upper, "core")

    subs = jnp.arange(group_rows // SUB, dtype=jnp.int32)
    per_device = rows // SUB
    source, within = subs // per_device, subs % per_device
    there_core, there_zl = (source % 2) ^ core, (source // 2 + zl) % near
    to_order = (there_core * near + there_zl) * per_device + within
    from_order = (((source % near - zl) % near) * 2 + ((source // near) ^ core)) * per_device + within
    place = jnp.concatenate([to_order, from_order])
    row_at, doc_start = document_layout(lengths, group_rows)
    cosine, sine = rotary_tables(row_at - doc_start)

    def bounds(size):
        tile_start = doc_start.reshape(-1, size)
        tile = jnp.arange(group_rows // size, dtype=jnp.int32)
        low = tile_start[:, 0] // size
        return low, jnp.minimum((tile_start[:, -1] + size - 1) // size, tile)

    start_row = jnp.tile(doc_start.reshape(-1, 1, SUB), (1, 1, q_heads // kv_heads))
    layout = (place, *bounds(TILE), cosine, sine, doc_start[:, None])
    layout_back = (place, *bounds(SUB), cosine, sine, start_row)
    lower, upper_sib, out_pair, *moved = stage(lower, upper_sib, out_pair, *upper_far, *taken, *layout, *layout_back)
    upper_far, moved = moved[: near - 1], moved[near - 1 :]
    taken, moved = moved[: len(taken)], moved[len(taken) :]
    layout, layout_back = moved[: len(layout)], moved[len(layout) :]

    lower_far = [from_near(lower, k) for k in others]
    lower_sib = flip(lower, "core")
    out_far = [from_near(out_pair, k) for k in others]
    blocks = blocks_of(pair, taken, diagonal(taken))
    projecting = [(*blocks, qkv_cols)]
    gain_row = gain_one[None]
    outs = [(tokens.shape[1], bf16, "all"), (qkv_cols, bf16, "all")]
    parts = [upper, lower, upper_sib, lower_sib]
    normed = piece_call(project_kernel, "project", 0, near, me, parts, [gain_row], [], projecting, [], outs)
    gate_up_shard, *moved = stage(gate_up_shard, *lower_far, *out_far, *normed)
    lower_far, out_far, normed = moved[: near - 1], moved[near - 1 : 2 * near - 2], moved[2 * near - 2 :]

    out_own = jnp.concatenate([out_pair, *out_far], axis=1)
    out_taken = neighbours(out_own)
    for k in others:
        parts = [upper_far[k - 1], lower_far[k - 1], flip(upper_far[k - 1], "core"), flip(lower_far[k - 1], "core")]
        normed = piece_call(project_kernel, "project", k, near, me, parts, [gain_row], [], projecting, normed, outs)
    norm_one, qkv = normed
    gate_up_shard, qkv, out_own, *out_taken = stage(gate_up_shard, qkv, out_own, *out_taken)

    gate_up_moved = send_z(gate_up_shard)
    out_halves = diagonal(out_taken)
    context, sums = attend(qkv, 2 * near, layout, q_heads, kv_heads)
    down_shard, cotangent, *moved = stage(down_weight, cotangent, *context, *gate_up_moved, *out_halves)
    context, gate_up_moved, out_halves = moved[: 2 * near], moved[2 * near : 2 * near + 2], moved[2 * near + 2 :]

    quarters = {(0, 0): context[0]}
    for k in range(near):
        for e in range(2):
            if (e, k) != (0, 0):
                quarters[e, (near - k) % near] = shift(context[2 * k + e], e, k)
    pairs = [
        pair_of(*(x[:, n * hidden_cols : (n + 1) * hidden_cols] for x in (gate_up_shard, *gate_up_moved)))
        for n in range(2)
    ]
    gate_taken = neighbours(pairs[0])
    order = [(e, k) for e in range(2) for k in range(near)]
    up_pair, down_shard, cotangent, *moved = stage(
        pairs[1], down_shard, cotangent, *(quarters[at] for at in order), *gate_taken, *out_halves
    )
    quarters, moved = moved[: 2 * near], moved[2 * near :]
    gate_taken, out_halves = moved[: len(gate_taken)], moved[len(gate_taken) :]

    up_taken = neighbours(up_pair)
    cot_upper = crossed(cotangent[:part_rows], CROSS)
    down_out = crossed(down_shard, OUT)
    w_out_near = assemble(
        "assemble_out", me, *blocks_of(out_own, out_taken, out_halves), tokens.shape[1], near * query_cols
    )
    w_out_sib = flip(w_out_near, "core")
    residual = jnp.concatenate([upper, lower], axis=0).astype(f32)
    scale_one = lax.rsqrt(jnp.mean(residual * residual, axis=-1, keepdims=True) + EPSILON)
    w_out_sib, w_out_near, scale_one, cotangent, cot_upper, down_shard, down_out, *up_taken = stage(
        w_out_sib, w_out_near, scale_one, cotangent, cot_upper, down_shard, down_out, *up_taken
    )

    gate_halves, up_halves = diagonal(gate_taken), diagonal(up_taken)
    down_cross = crossed(down_shard, CROSS)
    own_context = jnp.concatenate(quarters[:near], axis=1)
    sib_context = jnp.concatenate(quarters[near:], axis=1)
    mid = residual + times_transpose(own_context, w_out_near) + times_transpose(sib_context, w_out_sib)
    scale_two, norm_two = norm_rows(mid, gain_two)
    norm_two, cotangent, cot_upper, down_cross, *moved = stage(
        norm_two, cotangent, cot_upper, down_cross, *gate_halves, *up_halves
    )
    gate_halves, up_halves = moved[: len(gate_halves)], moved[len(gate_halves) :]
    norm_sib = flip(norm_two, "core")
    down_pair = pair_of(down_shard, down_out, down_cross)
    norm_two, norm_sib, down_pair = stage(norm_two, norm_sib, down_pair)

    upper_far = [from_near(norm_two[:part_rows], k) for k in others]
    down_taken = neighbours(down_pair)
    cot_lower = crossed(cotangent[part_rows:], CROSS)
    gate_blocks = blocks_of(pairs[0], gate_taken, gate_halves)
    up_blocks = blocks_of(up_pair, up_taken, up_halves, hidden_cols)
    gate_up = ([*gate_blocks[0], *up_blocks[0]], gate_blocks[1] + up_blocks[1], 2 * hidden_cols)
    outs = [(norm_two.shape[1], bf16, "all"), (2 * hidden_cols, f32, "all"), (hidden_cols, bf16, "all")]
    earlier = piece_call(gate_kernel, "gate", 0, near, me, [norm_two, norm_sib], [], [], [gate_up], [], outs)
    norm_two, cot_lower, *moved = stage(norm_two, cot_lower, *upper_far, *down_taken, *earlier)
    upper_far, moved = moved[: near - 1], moved[near - 1 :]
    down_taken, earlier = moved[: len(down_taken)], moved[len(down_taken) :]

    lower_far = [from_near(norm_two[part_rows:], k) for k in others]
    upper_far_sib = [flip(x, "core") for x in upper_far]
    down_halves = diagonal(down_taken)
    cot = jnp.where(straight(), cotangent, jnp.concatenate([cot_upper, cot_lower], axis=0))
    cot_sib = flip(cot, "core")
    w_project = assemble("assemble_project", me, *blocks, tokens.shape[1], qkv_cols)
    cot, cot_sib, w_project, *moved = stage(cot, cot_sib, w_project, *lower_far, *upper_far_sib, *down_halves)
    lower_far, upper_far_sib, down_halves = moved[: near - 1], moved[near - 1 : 2 * near - 2], moved[2 * near - 2 :]
    lower_far_sib = [flip(x, "core") for x in lower_far]

    cot_upper_far = [from_near(cot[:part_rows], k) for k in others]
    down = (*blocks_of(down_pair, down_taken, down_halves), hidden_cols)
    width = norm_two.shape[1]
    gate_outs, outs = outs, [(width, bf16, "all"), (2 * hidden_cols, bf16, "all")]
    halves = [(width, bf16, "own"), (width, bf16, "sibling")]

    def way_back(k, parts, earlier):
        tiled, results = [(gate_up_all, k), (hidden_all, k)], outs + halves * (1 if earlier else 2)
        return piece_call(gate_back_kernel, "gate_back", k, near, me, parts, [], tiled, [gate_up, down], earlier, results)

    def joined(own, sib):
        return own.astype(f32) + flip(sib, "core").astype(f32)

    norm_two_all, gate_up_all, hidden_all = earlier
    grad_all, d_gate_up_all, *near_back = way_back(0, [cot, cot_sib], [])
    cot, *moved = stage(
        cot, norm_two_all, gate_up_all, hidden_all, grad_all, d_gate_up_all, *near_back, *cot_upper_far, *lower_far_sib
    )
    earlier, moved = moved[:3], moved[3:]
    grad_all, d_gate_up_all, *moved = moved
    near_back, cot_upper_far, lower_far_sib = moved[:4], moved[4 : near + 3], moved[near + 3 :]

    cot_lower_far = [from_near(cot[part_rows:], k) for k in others]
    cot_upper_far_sib = [flip(x, "core") for x in cot_upper_far]
    out_far = []
    for k in others:
        parts = [upper_far[k - 1], lower_far[k - 1], upper_far_sib[k - 1], lower_far_sib[k - 1]]
        *earlier, out_own, out_sib = piece_call(
            gate_kernel, "gate", k, near, me, parts, [], [], [gate_up, down], earlier, gate_outs + halves
        )
        out_far += [out_own, out_sib]
    grad_all, d_gate_up_all, *moved = stage(
        grad_all, d_gate_up_all, *near_back, *cot_lower_far, *cot_upper_far_sib, *earlier, *out_far
    )
    near_back, cot_lower_far, moved = moved[:4], moved[4 : near + 3], moved[near + 3 :]
    cot_upper_far_sib, earlier, out_far = moved[: near - 1], moved[near - 1 : near + 2], moved[near + 2 :]
    norm_two_all, gate_up_all, hidden_all = earlier
    cot_lower_far_sib = [flip(x, "core") for x in cot_lower_far]
    out_sums = [joined(*out_far[2 * n : 2 * n + 2]).astype(bf16) for n in range(near - 1)]
    moved = stage(*cot_lower_far_sib, *out_sums)
    cot_lower_far_sib, out_sums = moved[: near - 1], moved[near - 1 :]

    out_upper = [to_near(out_sums[k - 1][:part_rows], k) for k in others]
    back = []
    for k in others:
        parts = [cot_upper_far[k - 1], cot_lower_far[k - 1], cot_upper_far_sib[k - 1], cot_lower_far_sib[k - 1]]
        grad_all, d_gate_up_all, *more = way_back(k, parts, [grad_all, d_gate_up_all])
        back.append(more)
    grad_all, d_gate_up_all, *moved = stage(grad_all, d_gate_up_all, *(x for more in back for x in more), *out_upper)
    far_back, out_upper = moved[: 2 * near - 2], moved[2 * near - 2 :]
    d_norm_sent = [joined(*far_back[2 * n : 2 * n + 2]).astype(bf16) for n in range(near - 1)]
    grad_all, d_gate_up_all, near_own, near_sib, *d_norm_sent = stage(
        grad_all, d_gate_up_all, *near_back[:2], *d_norm_sent
    )

    moved_upper = [to_near(d_norm_sent[k - 1][:part_rows], k) for k in others]
    grad_gate_up = rows_product(norm_two_all, d_gate_up_all).astype(bf16)
    grad_gate_up, grad_all, near_own, near_sib, *moved = stage(
        grad_gate_up, grad_all, near_own, near_sib, *moved_upper, *d_norm_sent
    )
    moved_upper, d_norm_sent = moved[: near - 1], moved[near - 1 :]

    moved_lower = [to_near(d_norm_sent[k - 1][part_rows:], k) for k in others]
    gate_up_part = lax.psum_scatter(grad_gate_up, "yx", scatter_dimension=0, tiled=True)
    d_norm_two = joined(near_own, near_sib)
    grad_down = rows_product(grad_all, hidden_all).astype(bf16)
    grad_down, d_norm_two, *moved = stage(grad_down, d_norm_two, *out_sums, *moved_lower)
    out_sums, moved_lower = moved[: near - 1], moved[near - 1 :]

    out_lower = [to_near(out_sums[k - 1][part_rows:], k) for k in others]
    down_part = lax.psum_scatter(grad_down, "yx", scatter_dimension=0, tiled=True)
    for one, two in zip(moved_upper, moved_lower, strict=True):
        d_norm_two = d_norm_two + jnp.concatenate([one, two], axis=0).astype(f32)
    mid_back, _ = norm_back(mid, scale_two, gain_two, d_norm_two)
    d_mid = cot.astype(f32) + mid_back
    d_attn = d_mid.astype(bf16)
    both = [dot32(d_attn, w).astype(bf16) for w in (w_out_near, w_out_sib)]
    d_quarters = [both[e][:, k * query_cols : (k + 1) * query_cols] for e, k in order]
    d_attn, *moved = stage(d_attn, *d_quarters, *out_lower)
    d_quarters, out_lower = moved[: 2 * near], moved[2 * near :]

    d_context = [None] * (2 * near)
    for (e, k), x in zip(order, d_quarters, strict=True):
        d_context[(near - k) % near * 2 + e] = x if (e, k) == (0, 0) else shift(x, e, k)
    grad_out_sib = flip(rows_product(d_attn, sib_context).astype(bf16), "core")
    grad_out = (rows_product(d_attn, own_context) + grad_out_sib.astype(f32)).astype(bf16)
    output_own = mid + joined(*near_back[2:])
    for one, two in zip(out_upper, out_lower, strict=True):
        output_own = output_own + jnp.concatenate([one, two], axis=0).astype(f32)
    output_own = output_own.astype(bf16)
    grad_out, output_own, gate_up_part, *d_context = stage(grad_out, output_own, gate_up_part, *d_context)

    output_crossed = crossed(output_own, CROSS)
    gate_up_keep, gate_up_give = give_z(gate_up_part)
    gate_up_back = crossed(gate_up_give, BACK)
    out_part = lax.psum_scatter(grad_out, "yx", scatter_dimension=0, tiled=True)
    d_qkv = attend_back(list(range(kv_heads)), qkv, d_context, context, sums, [], layout_back, q_heads, kv_heads)
    d_qkv, output_crossed, gate_up_back, gate_up_keep, down_part = stage(
        d_qkv, output_crossed, gate_up_back, gate_up_keep, down_part
    )

    def back_part(k):
        own, sib = (d_qkv[(2 * k + e) * rows : (2 * k + e + 1) * rows] for e in range(2))
        taken = flip(times_transpose(sib, w_project).astype(bf16), "core")
        return times_transpose(own, w_project) + taken.astype(f32)

    gate_up_cross = crossed(gate_up_keep, CROSS)
    d_sent = [back_part(k).astype(bf16) for k in others]
    d_qkv, gate_up_cross, down_part, *d_sent = stage(d_qkv, gate_up_cross, down_part, *d_sent)

    d_upper = [to_near(d_sent[k - 1][:part_rows], k) for k in others]
    down_keep, down_give = give_z(down_part)
    down_home = [crossed(down_give, BACK), crossed(down_keep, CROSS)]
    grad_project = rows_product(norm_one, d_qkv).astype(bf16)
    project_sent = send_yx(grad_project, (0, qkv_cols))
    total = back_part(0)
    total, grad_project, *moved = stage(total, grad_project, *d_upper, *d_sent, *project_sent, *down_home)
    d_upper, d_sent, project_sent, down_home = (
        moved[: near - 1], moved[near - 1 : 2 * near - 2], moved[2 * near - 2 : -2], moved[-2:],
    )

    d_lower = [to_near(d_sent[k - 1][part_rows:], k) for k in others]
    project_rest, project_own = join_yx(grad_project, (0, qkv_cols), project_sent)

    def input_part(at, moved):
        part = total[at]
        for x in moved:
            part = part + x.astype(f32)
        back, _ = norm_back(residual[at], scale_one[at], gain_one, part)
        return (d_mid[at] + back).astype(bf16)

    input_upper = input_part(slice(0, part_rows), d_upper)
    upper_crossed = crossed(input_upper, CROSS)
    total, input_upper, upper_crossed, out_part, *moved = stage(
        total, input_upper, upper_crossed, out_part, *d_lower, *project_rest
    )
    d_lower, project_rest = moved[: near - 1], moved[near - 1 :]

    project_keep, project_give = give_z(total_yx(project_rest, project_own))
    project_home = [crossed(project_give, BACK), crossed(project_keep, CROSS)]
    input_lower = input_part(slice(part_rows, rows), d_lower)
    lower_crossed = crossed(input_lower, CROSS)
    out_moved = [to_near(out_part[:, k * query_cols : (k + 1) * query_cols], k) for k in others]
    out_quarter = out_part[:, :query_cols].astype(f32)
    for part in out_moved:
        out_quarter = out_quarter + part.astype(f32)
    out_keep, out_give = give_z(out_quarter.astype(bf16))
    out_home = [crossed(out_give, BACK), crossed(out_keep, CROSS)]
    grad_project = sum_z(project_keep, *project_home)
    grad_out = sum_z(out_keep, *out_home)
    grad_down = sum_z(down_keep, *down_home)
    grad_gate_up = sum_z(gate_up_keep, gate_up_back, gate_up_cross)
    output = jnp.where(straight(), output_own, output_crossed)
    input_grad = jnp.concatenate(
        [
            jnp.where(straight(), input_upper, upper_crossed),
            jnp.where(straight(), input_lower, lower_crossed),
        ],
        axis=0,
    ).astype(f32)
    gain_grads = lax.psum(
        jnp.stack(
            [
                jnp.sum(qkv_shard.astype(f32) * grad_project, axis=1),
                jnp.sum(gate_up_shard.astype(f32) * grad_gate_up, axis=1),
            ]
        ),
        ("zh", "zl"),
    ) / jnp.stack([attn_gain, mlp_gain]).astype(f32)
    return (
        output,
        input_grad,
        gain_grads[0],
        grad_project[:, :query_cols],
        grad_project[:, query_cols : query_cols + key_cols],
        grad_project[:, query_cols + key_cols :],
        grad_out,
        gain_grads[1],
        grad_gate_up[:, :hidden_cols],
        grad_gate_up[:, hidden_cols:],
        grad_down,
    )


def solution(mesh):
    dp, tensor = mesh.shape["dp"], mesh.shape["tensor"]
    fine = Mesh(mesh.devices.reshape(dp // 2, 2, 2, tensor // 2), AXES)
    by_rows, by_dp, by_both = P(AXES, None), P(("yx", "core")), P(("yx", "core"), ("zh", "zl"))
    return jax.shard_map(
        body,
        mesh=fine,
        in_specs=(
            by_rows, by_rows, P(("yx", "core"), None), by_dp, by_both, by_both, by_both, by_both,
            by_dp, by_both, by_both, by_both,
        ),
        out_specs=(
            by_rows, by_rows, by_dp, by_both, by_both, by_both, by_both, by_dp, by_both, by_both, by_both,
        ),
        check_vma=False,
    )
```

```python
import functools
import math

import jax
import jax.numpy as jnp
import numpy as np
from jax import lax
from jax.experimental import pallas as pl
from jax.experimental.pallas import tpu as pltpu
from jax.sharding import Mesh
from jax.sharding import PartitionSpec as P

HD = 96
HALF = HD // 2
PAD = 128
STEPS = 4
SUB = 256
TILE = 512

EPSILON = 1e-05
ROTARY_BASE = 100000.0
MASKED = -1e30
LOG2E = math.log2(math.e)

AXES = ("yx", "core", "zh", "zl")
FLIP = [(0, 1), (1, 0)]


def norm_rows(values, gain):
    row_scale = lax.rsqrt(jnp.mean(values * values, axis=-1, keepdims=True) + EPSILON)
    return (row_scale, (values * row_scale * gain).astype(jnp.bfloat16))


def norm_back(values, row_scale, gain, upstream):
    weighted = upstream * gain
    inner_sum = jnp.mean(weighted * values, axis=-1, keepdims=True)
    grad_in = row_scale * weighted - values * (row_scale * row_scale * row_scale) * inner_sum
    gain_part = jnp.sum(upstream * (values * row_scale), axis=0)
    return (grad_in, gain_part)


def document_layout(lengths, group_rows):
    flat_lengths = lengths.reshape(-1)
    doc_ends = jnp.cumsum(flat_lengths)
    rows = jnp.arange(group_rows, dtype=jnp.int32)
    passed = (rows[:, None] >= doc_ends[None, :]).astype(jnp.int32)
    return (rows, jnp.sum(passed * flat_lengths[None, :], axis=1))


def rotary_tables(positions):
    exponents = jnp.arange(HALF, dtype=jnp.float32) * (2.0 / HD)
    inverse = ROTARY_BASE ** (-exponents)
    angles = positions.astype(jnp.float32)[:, None] * inverse[None, :]
    cosine, sine = jnp.cos(angles), jnp.sin(angles)
    gap = jnp.zeros((positions.shape[0], PAD // 2 - HALF), jnp.float32)
    return (
        jnp.concatenate([cosine, gap, cosine, gap], axis=1),
        jnp.concatenate([-sine, gap, sine, gap], axis=1),
    )


def rows_product(left, right):
    return lax.dot_general(
        left, right, (((0,), (0,)), ((), ())), preferred_element_type=jnp.float32
    )


def times_transpose(left, right):
    return lax.dot_general(
        left, right, (((1,), (1,)), ((), ())), preferred_element_type=jnp.float32
    )


def dot32(left, right):
    return jnp.dot(left, right, preferred_element_type=jnp.float32)


def stage(*values):
    return lax.optimization_barrier(values)


def spread(columns, heads):
    matrix = np.zeros((columns, len(heads) * PAD), np.float32)
    for at, first in enumerate(heads):
        for half in range(2):
            for i in range(HALF):
                matrix[first + half * HALF + i, at * PAD + half * (PAD // 2) + i] = 1.0
    return matrix


def turn(x, cosine, sine):
    return x * cosine + pltpu.roll(x, PAD // 2, 1) * sine


def rows_at(t, size):
    return pl.ds(pl.multiple_of(t * size, size), size)


def forward_kernel(pieces, ratio, *refs):
    place, low, full, cosine, sine, start, spread_in, gather_out = refs[:8]
    heads = spread_in.shape[0]
    refs = refs[8:]
    qkv, context, refs = refs[0], refs[1 : 1 + pieces], refs[1 + pieces :]
    log_sum, refs = refs[:heads], refs[heads:]
    q_s, k_s, v_s, s_s, top_s, acc = refs
    tiles = q_s.shape[0]
    all_subs = qkv.shape[0] // SUB
    piece_subs = all_subs // pieces
    scale = LOG2E * HD ** (-0.5)
    ones_lane = lax.broadcasted_iota(jnp.int32, (SUB, PAD), 1) == PAD - 1

    def prepare(r, carry):
        t = place[r]
        at = rows_at(t, SUB)
        cos_t, sin_t = cosine[at, :], sine[at, :]
        tile, half = t // (TILE // SUB), t % (TILE // SUB)
        for g in range(heads):
            wide = dot32(qkv[rows_at(r, SUB), :], spread_in[g])
            for h in range(ratio):
                query = turn(wide[:, h * PAD : (h + 1) * PAD], cos_t, sin_t) * scale
                first = pl.multiple_of(h * TILE + half * SUB, SUB)
                q_s[tile, g, pl.ds(first, SUB), :] = query.astype(jnp.bfloat16)
            key = turn(wide[:, ratio * PAD : (ratio + 1) * PAD], cos_t, sin_t)
            k_s[g, at, :] = key.astype(jnp.bfloat16)
            value = jnp.where(ones_lane, 1.0, wide[:, (ratio + 1) * PAD :])
            v_s[g, at, :] = value.astype(jnp.bfloat16)
        return carry

    lax.fori_loop(0, all_subs, prepare, 0)

    def query_tile(i, carry):
        starts = jnp.concatenate([start[rows_at(i, TILE), :]] * ratio, axis=0)
        top_s[...] = jnp.full_like(top_s, MASKED)

        def scores(j, masked, diagonal):
            for g in range(heads):
                s = times_transpose(q_s[i, g], k_s[g, rows_at(j, TILE), :])
                if masked:
                    key_at = lax.broadcasted_iota(jnp.int32, s.shape, 1)
                    allowed = key_at + j * TILE >= starts
                    if diagonal:
                        query_at = lax.rem(lax.broadcasted_iota(jnp.int32, s.shape, 0), TILE)
                        allowed = allowed & (key_at <= query_at)
                    s = jnp.where(allowed, s, MASKED)
                s_s[g, j] = s
                peak = s[:, :PAD]
                for c in range(1, TILE // PAD):
                    peak = jnp.maximum(peak, s[:, c * PAD : (c + 1) * PAD])
                top_s[g] = jnp.maximum(top_s[g], peak)

        def loop(first, last, masked):
            def run(j, c):
                scores(j, masked, False)
                return c

            lax.fori_loop(first, last, run, 0)

        loop(low[i], full[i], True)
        loop(full[i], i, False)
        scores(i, True, True)
        tops = [jnp.max(top_s[g], axis=1, keepdims=True) for g in range(heads)]
        acc[...] = jnp.zeros_like(acc)

        def weigh(j, c):
            for g in range(heads):
                p = jnp.exp2(s_s[g, j] - tops[g]).astype(jnp.bfloat16)
                acc[g] += dot32(p, v_s[g, rows_at(j, TILE), :])
            return c

        lax.fori_loop(low[i], i + 1, weigh, 0)
        packed = None
        for g in range(heads):
            total = acc[g][:, PAD - 1 :]
            out = acc[g] * (1.0 / total)
            sums = jnp.broadcast_to(tops[g] + jnp.log(total) * LOG2E, (ratio * TILE, PAD))
            log_sum[g][i] = sums.T[:1, :]
            wide = jnp.concatenate(
                [out[h * TILE : (h + 1) * TILE, :] for h in range(ratio)], axis=1
            ).astype(jnp.bfloat16)
            part = dot32(wide, gather_out[g])
            packed = part if packed is None else packed + part
        subs = tiles * (TILE // SUB)
        for half in range(TILE // SUB):
            r = place[subs + i * (TILE // SUB) + half]
            part = packed[half * SUB : (half + 1) * SUB, :].astype(jnp.bfloat16)
            for k in range(pieces):

                @pl.when(r // piece_subs == k)
                def store(k=k, part=part, r=r):
                    context[k][rows_at(r % piece_subs, SUB), :] = part

        return carry

    lax.fori_loop(0, tiles, query_tile, 0)


def backward_kernel(pieces, ratio, more, *refs):
    place, low, full, cosine, sine, start, refs = *refs[:6], refs[6:]
    heads = refs[0].shape[0]
    spread_in, spread_out, gather_in, refs = *refs[:3], refs[3:]
    log_sum, refs = refs[:heads], refs[heads:]
    d_context, context, qkv, refs = refs[:pieces], refs[pieces : 2 * pieces], refs[2 * pieces], refs[2 * pieces + 1 :]
    earlier, refs = (refs[0], refs[1:]) if more else (None, refs)
    d_qkv, refs = refs[0], refs[1:]
    q_s, k_s, kt_s, v_s, do_s, delta_s, log_s, dq_acc, dk_acc, dv_acc, dq_s = refs
    tiles = q_s.shape[0]
    all_subs = qkv.shape[0] // SUB
    piece_subs = all_subs // pieces
    scale = HD ** (-0.5)
    per_tile = TILE // SUB

    for k in range(pieces):

        def prepare(r, carry, k=k):
            t = place[k * piece_subs + r]
            rel = rows_at(r, SUB)
            at = rows_at(t, SUB)
            cos_t, sin_t = cosine[at, :], sine[at, :]
            for g in range(heads):
                wide = dot32(qkv[rows_at(k * piece_subs + r, SUB), :], spread_in[g])
                d_out = dot32(d_context[k][rel, :], spread_out[g])
                out = dot32(context[k][rel, :], spread_out[g])
                for h in range(ratio):
                    cols = slice(h * PAD, (h + 1) * PAD)
                    rows = slice(h * SUB, (h + 1) * SUB)
                    query = turn(wide[:, cols], cos_t, sin_t) * (scale * LOG2E)
                    q_s[t, g, rows, :] = query.astype(jnp.bfloat16)
                    do_s[t, g, rows, :] = d_out[:, cols].astype(jnp.bfloat16)
                    delta = jnp.sum((d_out[:, cols] * out[:, cols]).T, axis=0, keepdims=True)
                    delta_s[t * heads + g, :, rows] = delta
                    first = pl.multiple_of(h * TILE + t % per_tile * SUB, SUB)
                    log_s[t * heads + g, :, rows] = log_sum[g][t // per_tile, :, pl.ds(first, SUB)]
                key = turn(wide[:, ratio * PAD : (ratio + 1) * PAD], cos_t, sin_t)
                k_s[g, t] = key.astype(jnp.bfloat16)
                kt_s[g, t] = key.T.astype(jnp.bfloat16)
                v_s[g, t] = wide[:, (ratio + 1) * PAD :].astype(jnp.bfloat16)
                dk_acc[g, t] = jnp.zeros((SUB, PAD), jnp.float32)
                dv_acc[g, t] = jnp.zeros((SUB, PAD), jnp.float32)
            return carry

        lax.fori_loop(0, piece_subs, prepare, 0)

    def query_tile(i, carry):
        dq_acc[...] = jnp.zeros_like(dq_acc)

        def step(j, masked, diagonal):
            for g in range(heads):
                queries, d_out = q_s[i, g], do_s[i, g]
                s = times_transpose(k_s[g, j], queries)
                if masked:
                    key_at = lax.broadcasted_iota(jnp.int32, s.shape, 0)
                    allowed = key_at + j * SUB >= start[i]
                    if diagonal:
                        query_at = lax.rem(lax.broadcasted_iota(jnp.int32, s.shape, 1), SUB)
                        allowed = allowed & (key_at <= query_at)
                    s = jnp.where(allowed, s, MASKED)
                p = jnp.exp2(s - log_s[i * heads + g])
                d_p = times_transpose(v_s[g, j], d_out)
                d_s = (p * (d_p - delta_s[i * heads + g])).astype(jnp.bfloat16)
                dv_acc[g, j] += dot32(p.astype(jnp.bfloat16), d_out)
                dk_acc[g, j] += dot32(d_s, queries)
                dq_acc[g] += dot32(kt_s[g, j], d_s)

        def loop(first, last, masked):
            def run(j, c):
                step(j, masked, False)
                return c

            lax.fori_loop(first, last, run, 0)

        loop(low[i], full[i], True)
        loop(full[i], i, False)
        step(i, True, True)
        at = rows_at(i, SUB)
        cos_t, sin_t = cosine[at, :], sine[at, :]
        for g in range(heads):
            grad = dq_acc[g].T * scale
            for h in range(ratio):
                piece = turn(grad[h * SUB : (h + 1) * SUB, :], cos_t, -sin_t)
                dq_s[g, i, :, h * PAD : (h + 1) * PAD] = piece.astype(jnp.bfloat16)
        return carry

    lax.fori_loop(0, tiles, query_tile, 0)

    def finish(r, carry):
        t = place[r]
        at = rows_at(t, SUB)
        rel = rows_at(r, SUB)
        packed = None
        for g in range(heads):
            key = turn(dk_acc[g, t] * (1.0 / LOG2E), cosine[at, :], -sine[at, :])
            wide = jnp.concatenate(
                [dq_s[g, t], key.astype(jnp.bfloat16), dv_acc[g, t].astype(jnp.bfloat16)], axis=1
            )
            part = dot32(wide, gather_in[g])
            packed = part if packed is None else packed + part
        packed = packed.astype(jnp.bfloat16)
        d_qkv[rel, :] = packed + earlier[rel, :] if more else packed
        return carry

    lax.fori_loop(0, all_subs, finish, 0)


SMEM = pl.BlockSpec(memory_space=pltpu.SMEM)
VMEM = pl.BlockSpec(memory_space=pltpu.VMEM)
ANY = pl.BlockSpec(memory_space=pl.ANY)


def small_cost(transcendentals=0):
    return pl.CostEstimate(flops=1 << 20, bytes_accessed=1 << 16, transcendentals=transcendentals)


def head_matrices(head, q_heads, kv_heads):
    ratio = q_heads // kv_heads
    queries = [(head * ratio + r) * HD for r in range(ratio)]
    key, value = (q_heads + head) * HD, (q_heads + kv_heads + head) * HD
    inner = spread((q_heads + 2 * kv_heads) * HD, [*queries, key, value])
    outer = spread(q_heads * HD, queries)
    return jnp.asarray(inner, jnp.bfloat16), jnp.asarray(outer, jnp.bfloat16)


def stacked_matrices(q_heads, kv_heads):
    pairs = [head_matrices(head, q_heads, kv_heads) for head in range(kv_heads)]
    return jnp.stack([inner for inner, _ in pairs]), jnp.stack([outer for _, outer in pairs])


def attend(qkv, pieces, layout, q_heads, kv_heads):
    place, low, full, cosine, sine, start_column = layout
    ratio, rows = q_heads // kv_heads, qkv.shape[0]
    tiles, lanes = rows // TILE, ratio * TILE
    bf16, f32 = jnp.bfloat16, jnp.float32
    inner, outer = stacked_matrices(q_heads, kv_heads)
    outs = pl.pallas_call(
        functools.partial(forward_kernel, pieces, ratio),
        out_shape=[
            *[jax.ShapeDtypeStruct((rows // pieces, q_heads * HD), bf16)] * pieces,
            *[jax.ShapeDtypeStruct((tiles, 1, lanes), f32)] * kv_heads,
        ],
        in_specs=[SMEM] * 3 + [VMEM] * 6,
        out_specs=[VMEM] * (pieces + kv_heads),
        scratch_shapes=[
            pltpu.VMEM((tiles, kv_heads, lanes, PAD), bf16),
            pltpu.VMEM((kv_heads, rows, PAD), bf16),
            pltpu.VMEM((kv_heads, rows, PAD), bf16),
            pltpu.VMEM((kv_heads, tiles, lanes, TILE), f32),
            pltpu.VMEM((kv_heads, lanes, PAD), f32),
            pltpu.VMEM((kv_heads, lanes, PAD), f32),
        ],
        compiler_params=pltpu.CompilerParams(vmem_limit_bytes=60 * 2**20),
        cost_estimate=small_cost(),
        name="attention_forward",
    )(place, low, full, cosine, sine, start_column, inner, jnp.swapaxes(outer, 1, 2), qkv)
    return outs[:pieces], outs[pieces:]


def attend_back(heads, qkv, d_context, context, sums, earlier, layout, q_heads, kv_heads):
    place, low, full, cosine, sine, start_row = layout
    pieces, ratio, rows = len(context), q_heads // kv_heads, qkv.shape[0]
    tiles, lanes, count = rows // SUB, ratio * SUB, len(heads)
    bf16, f32 = jnp.bfloat16, jnp.float32
    inner, outer = stacked_matrices(q_heads, kv_heads)
    inner, outer = inner[heads[0] : heads[0] + count], outer[heads[0] : heads[0] + count]
    return pl.pallas_call(
        functools.partial(backward_kernel, pieces, ratio, bool(earlier)),
        out_shape=jax.ShapeDtypeStruct(qkv.shape, bf16),
        in_specs=[SMEM] * 3 + [VMEM] * (7 + count + 2 * pieces + len(earlier)),
        out_specs=VMEM,
        scratch_shapes=[
            pltpu.VMEM((tiles, count, lanes, PAD), bf16),
            pltpu.VMEM((count, tiles, SUB, PAD), bf16),
            pltpu.VMEM((count, tiles, PAD, SUB), bf16),
            pltpu.VMEM((count, tiles, SUB, PAD), bf16),
            pltpu.VMEM((tiles, count, lanes, PAD), bf16),
            pltpu.VMEM((tiles * count, 1, lanes), f32),
            pltpu.VMEM((tiles * count, 1, lanes), f32),
            pltpu.VMEM((count, PAD, lanes), f32),
            pltpu.VMEM((count, tiles, SUB, PAD), f32),
            pltpu.VMEM((count, tiles, SUB, PAD), f32),
            pltpu.VMEM((count, tiles, SUB, ratio * PAD), bf16),
        ],
        compiler_params=pltpu.CompilerParams(vmem_limit_bytes=60 * 2**20),
        cost_estimate=small_cost(),
        name=f"attention_backward_{heads[0]}",
    )(
        place, low, full, cosine, sine, start_row, inner, outer, jnp.swapaxes(inner, 1, 2),
        *[sums[h] for h in heads], *d_context, *context, qkv, *earlier,
    )


def fetch(me, where, sources, target, sems):
    copies = []
    for n, (source, (j, deep, first, column, taken)) in enumerate(zip(sources, where, strict=True)):
        cols = min(source.shape[1] - taken, target.shape[1] - column)
        at = pl.ds(pl.multiple_of((me[0] ^ j) * deep + first, 16), source.shape[0])
        if cols != source.shape[1]:
            source = source.at[:, taken : taken + cols]
        copies.append(pltpu.make_async_copy(source, target.at[at, column : column + cols], sems.at[n]))
    return copies


def take_rows(parts, target):
    rows = target.shape[0]
    for step in range(STEPS):

        @pl.when(pl.program_id(0) == step)
        def take(step=step):
            at = 0
            for part in parts:
                first, last = max(at, step * rows), min(at + part.shape[0], (step + 1) * rows)
                if first < last:
                    target[first - step * rows : last - step * rows, :] = part[first - at : last - at, :]
                at += part.shape[0]


def at_first_step(copies, what):
    @pl.when(pl.program_id(0) == 0)
    def run():
        for copy in copies:
            what(copy)


def project_kernel(count, where, more, me, *refs):
    parts, gain, refs = refs[:count], refs[count], refs[count + 1 :]
    sources, refs = refs[: len(where[0])], refs[len(where[0]) :]
    norm_all, qkv_all, weight, sems, rows_s = refs[2 if more else 0 :]
    copies = fetch(me, where[0], sources, weight, sems)
    at_first_step(copies, lambda copy: copy.start())
    take_rows(parts, rows_s)
    x = rows_s[...].astype(jnp.float32)
    scale = lax.rsqrt(jnp.mean(x * x, axis=-1, keepdims=True) + EPSILON)
    norm_all[...] = (x * scale * gain[...]).astype(jnp.bfloat16)
    at_first_step(copies, lambda copy: copy.wait())
    qkv_all[...] = dot32(norm_all[...], weight[...]).astype(jnp.bfloat16)


def by_half(refs, value):
    for n, ref in enumerate(refs):

        @pl.when(pl.program_id(0) * 2 // STEPS == n)
        def store(ref=ref):
            ref[...] = value


def gate_kernel(count, where, more, me, *refs):
    parts, refs = refs[:count], refs[count:]
    with_out = len(where) > 1
    sources, refs = refs[: sum(map(len, where))], refs[sum(map(len, where)) :]
    norm_all, gate_up_all, hidden_all, *refs = refs[3 if more else 0 :]
    out_refs, refs = (refs[:2], refs[2:]) if with_out else ((), refs)
    weight, sems, *refs = refs
    hidden_cols = hidden_all.shape[1]
    copies = fetch(me, where[0], sources[: len(where[0])], weight, sems)
    if with_out:
        w_down, down_sems = refs
        copies += fetch(me, where[1], sources[len(where[0]) :], w_down, down_sems)
    at_first_step(copies, lambda copy: copy.start())
    take_rows(parts, norm_all)
    at_first_step(copies, lambda copy: copy.wait())
    x = norm_all[...]
    width = min(512, hidden_cols)
    for at in range(0, hidden_cols, width):
        gate_at = slice(at, at + width)
        up_at = slice(hidden_cols + at, hidden_cols + at + width)
        gate = dot32(x, weight[:, gate_at])
        up = dot32(x, weight[:, up_at])
        gate_up_all[:, gate_at] = gate
        gate_up_all[:, up_at] = up
        hidden_all[:, gate_at] = (gate * (1.0 / (1.0 + jnp.exp(-gate))) * up).astype(jnp.bfloat16)
    if with_out:
        by_half(out_refs, times_transpose(hidden_all[...], w_down[...]).astype(jnp.bfloat16))


def gate_back_kernel(count, where, more, me, *refs):
    parts, gate_up_all, hidden_here, refs = refs[:count], *refs[count : count + 2], refs[count + 2 :]
    gate_up, refs = refs[: len(where[0])], refs[len(where[0]) :]
    down, refs = refs[: len(where[1])], refs[len(where[1]) :]
    grad_all, d_gate_up_all, *refs = refs[2 if more else 0 :]
    d_norm_refs, refs = refs[:2], refs[2:]
    out_refs, refs = ((), refs) if more else (refs[:2], refs[2:])
    w_gate_up, gate_up_sems, w_down, down_sems = refs
    hidden_cols = w_down.shape[1]
    down_copies = fetch(me, where[1], down, w_down, down_sems)
    copies = fetch(me, where[0], gate_up, w_gate_up, gate_up_sems)
    at_first_step(down_copies + copies, lambda copy: copy.start())
    take_rows(parts, grad_all)
    at_first_step(down_copies, lambda copy: copy.wait())
    dy = grad_all[...]
    width = min(512, hidden_cols)
    for at in range(0, hidden_cols, width):
        gate_at = slice(at, at + width)
        up_at = slice(hidden_cols + at, hidden_cols + at + width)
        d_hidden = dot32(dy, w_down[:, gate_at])
        gate, up = gate_up_all[:, gate_at], gate_up_all[:, up_at]
        sigmoid = 1.0 / (1.0 + jnp.exp(-gate))
        d_gate = d_hidden * up * sigmoid * (1.0 + gate * (1.0 - sigmoid))
        d_gate_up_all[:, gate_at] = d_gate.astype(jnp.bfloat16)
        d_gate_up_all[:, up_at] = (d_hidden * (gate * sigmoid)).astype(jnp.bfloat16)
    if not more:
        by_half(out_refs, times_transpose(hidden_here[...], w_down[...]).astype(jnp.bfloat16))
    at_first_step(copies, lambda copy: copy.wait())
    by_half(d_norm_refs, times_transpose(d_gate_up_all[...], w_gate_up[...]).astype(jnp.bfloat16))


def piece_call(kernel, name, k, pieces, me, parts, whole, tiled, fetched, earlier, outs):
    tile, width = sum(x.shape[0] for x in parts) // STEPS, parts[0].shape[1]
    count = len(parts)

    def rows_of(piece):
        return lambda i: (piece * STEPS + i, 0)

    def half_of(span):
        first = 0 if span == "own" else STEPS // 2
        return lambda i: (jnp.clip(i - first, 0, STEPS // 2 - 1), 0)

    sources = [x for arrays, _, _ in fetched for x in arrays]
    first_earlier = 1 + count + len(whole) + len(tiled) + len(sources)
    scratch = []
    for arrays, _, cols in fetched:
        scratch += [pltpu.VMEM((width, cols), jnp.bfloat16), pltpu.SemaphoreType.DMA((len(arrays),))]
    if kernel is project_kernel:
        scratch.append(pltpu.VMEM((tile, width), jnp.bfloat16))
    return pl.pallas_call(
        functools.partial(kernel, count, tuple(where for _, where, _ in fetched), bool(earlier)),
        grid=(STEPS,),
        out_shape=[
            jax.ShapeDtypeStruct(((pieces * STEPS if span == "all" else STEPS // 2) * tile, columns), kind)
            for columns, kind, span in outs
        ],
        in_specs=[
            SMEM,
            *(pl.BlockSpec(x.shape, lambda i: (0, 0)) for x in parts),
            *(pl.BlockSpec(x.shape, lambda i: (0, 0)) for x in whole),
            *(pl.BlockSpec((tile, x.shape[1]), rows_of(piece)) for x, piece in tiled),
            *[ANY] * (len(sources) + len(earlier)),
        ],
        out_specs=[
            pl.BlockSpec((tile, columns), rows_of(k) if span == "all" else half_of(span))
            for columns, kind, span in outs
        ],
        scratch_shapes=scratch,
        input_output_aliases={first_earlier + n: n for n in range(len(earlier))},
        compiler_params=pltpu.CompilerParams(vmem_limit_bytes=60 * 2**20),
        cost_estimate=small_cost(),
        name=f"{name}_{k}",
    )(me, *parts, *whole, *(x for x, _ in tiled), *sources, *earlier)


def assemble_kernel(where, me, *refs):
    sources, whole, sems = refs[: len(where)], refs[len(where)], refs[len(where) + 1]
    copies = fetch(me, where, sources, whole, sems)
    for copy in copies:
        copy.start()
    for copy in copies:
        copy.wait()


def assemble(name, me, arrays, where, rows, cols):
    return pl.pallas_call(
        functools.partial(assemble_kernel, where),
        out_shape=jax.ShapeDtypeStruct((rows, cols), arrays[0].dtype),
        in_specs=[SMEM, *[ANY] * len(arrays)],
        out_specs=VMEM,
        scratch_shapes=[pltpu.SemaphoreType.DMA((len(arrays),))],
        compiler_params=pltpu.CompilerParams(vmem_limit_bytes=60 * 2**20),
        cost_estimate=small_cost(),
        name=name,
    )(me, *arrays)


def flip(x, axis):
    return lax.ppermute(x, axis, FLIP)


CROSS = [(1, 2), (2, 1)]
OUT = [(0, 1), (3, 2), (2, 0), (1, 3)]
BACK = [(1, 0), (2, 3), (0, 2), (3, 1)]


def crossed(x, perm):
    return lax.ppermute(x, ("core", "zh"), perm)


def straight():
    return lax.axis_index("core") == lax.axis_index("zh")


def swap(x):
    return jnp.where(straight(), x, crossed(x, CROSS))


def send_z(w):
    return crossed(w, OUT), crossed(w, CROSS)


def pair_of(w, out, cross):
    zh = lax.axis_index("zh")
    x = jnp.where(straight(), w, cross)
    return jnp.concatenate([jnp.where(zh == 0, x, out), jnp.where(zh == 0, out, x)], axis=0)


def give_z(part):
    zh = lax.axis_index("zh")
    half = part.shape[0] // 2
    upper, lower = part[:half], part[half:]
    return jnp.where(zh == 0, upper, lower), jnp.where(zh == 0, lower, upper)


def sum_z(keep, back, cross):
    return back.astype(jnp.float32) + jnp.where(straight(), keep, cross).astype(jnp.float32)


def shift(x, e, k):
    n = lax.axis_size("zl")
    return lax.ppermute(
        x, ("core", "zl"), [(c * n + l, (c ^ e) * n + (l + k) % n) for c in range(2) for l in range(n)]
    )


def from_near(x, k):
    n = lax.axis_size("zl")
    return lax.ppermute(x, "zl", [((j + k) % n, j) for j in range(n)])


def to_near(x, k):
    n = lax.axis_size("zl")
    return lax.ppermute(x, "zl", [(j, (j + k) % n) for j in range(n)])


def across(x, j):
    n = lax.axis_size("yx")
    return lax.ppermute(x, "yx", [(a, a ^ j) for a in range(n)])


def neighbours(x):
    count = lax.axis_size("yx")
    return [across(x, j) for j in range(1, count if count != 4 else 3)]


def diagonal(taken):
    if lax.axis_size("yx") != 4:
        return []
    half = taken[0].shape[0] // 2
    return [across(taken[1][:half], 1), across(taken[0][half:], 2)]


def blocks_of(own, taken, halves, column=0, source_column=0):
    deep = own.shape[0]
    arrays = [own, *taken, *halves]
    where = [(j, deep, 0, column, source_column) for j in range(1 + len(taken))]
    where += [(3, deep, n * deep // 2, column, source_column) for n in range(len(halves))]
    return arrays, tuple(where)


def whole_weight(w):
    return [w], ((0, 0, 0, 0, 0),)


def block_of(grad, j, columns):
    size = grad.shape[0] // lax.axis_size("yx")
    first = (lax.axis_index("yx") ^ j) * size
    return lax.dynamic_slice(grad, (first, columns[0]), (size, columns[1] - columns[0]))


def send_yx(grad, columns):
    count = lax.axis_size("yx")
    if count != 4:
        return [across(block_of(grad, j, columns), j) for j in range(1, count)]
    far = block_of(grad, 3, columns)
    half = far.shape[0] // 2
    return [across(far[:half], 1), across(far[half:], 2)]


def join_yx(grad, columns, taken):
    if lax.axis_size("yx") != 4:
        return taken, block_of(grad, 0, columns)
    half = taken[0].shape[0]
    one, two = block_of(grad, 1, columns), block_of(grad, 2, columns)
    one = jnp.concatenate([one[:half], one[half:] + taken[1]], axis=0)
    two = jnp.concatenate([two[:half] + taken[0], two[half:]], axis=0)
    return [across(one, 1), across(two, 2)], block_of(grad, 0, columns)


def total_yx(taken, own):
    total = own.astype(jnp.float32)
    for part in taken:
        total = total + part.astype(jnp.float32)
    return total.astype(jnp.bfloat16)


def body(
    tokens,
    cotangent,
    seq_lengths,
    attn_gain,
    q_weight,
    key_projection,
    value_projection,
    out_weight,
    mlp_gain,
    gate_weight,
    up_weight,
    down_weight,
):
    bf16, f32 = jnp.bfloat16, jnp.float32
    core, zl, yx = lax.axis_index("core"), lax.axis_index("zl"), lax.axis_index("yx")
    near = lax.axis_size("zl")
    others = range(1, near)
    rows = tokens.shape[0]
    group_rows = 2 * near * rows
    query_cols, key_cols = q_weight.shape[1], key_projection.shape[1]
    qkv_cols = query_cols + 2 * key_cols
    q_heads, kv_heads = query_cols // HD, key_cols // HD
    hidden_cols = gate_weight.shape[1]
    me = yx.astype(jnp.int32).reshape(1)

    qkv_shard = jnp.concatenate([q_weight, key_projection, value_projection], axis=1)
    gate_up_shard = jnp.concatenate([gate_weight, up_weight], axis=1)
    part_rows = rows // 2
    upper = swap(tokens[:part_rows])
    shard_moved = send_z(qkv_shard)
    lengths = swap(seq_lengths)
    gains = lax.all_gather(jnp.stack([attn_gain, mlp_gain]), ("yx", "core"), axis=1, tiled=True).astype(f32)
    upper, lengths, second_part, gains, *shard_moved = stage(upper, lengths, tokens[part_rows:], gains, *shard_moved)
    gain_one, gain_two = gains[0], gains[1]

    upper_far = [from_near(upper, k) for k in others]
    lower = swap(second_part)
    pair = pair_of(qkv_shard, *shard_moved)
    taken = neighbours(pair)
    upper_sib = flip(upper, "core")

    subs = jnp.arange(group_rows // SUB, dtype=jnp.int32)
    per_device = rows // SUB
    source, within = subs // per_device, subs % per_device
    there_core, there_zl = (source % 2) ^ core, (source // 2 + zl) % near
    to_order = (there_core * near + there_zl) * per_device + within
    from_order = (((source % near - zl) % near) * 2 + ((source // near) ^ core)) * per_device + within
    place = jnp.concatenate([to_order, from_order])
    row_at, doc_start = document_layout(lengths, group_rows)
    cosine, sine = rotary_tables(row_at - doc_start)

    def bounds(size):
        tile_start = doc_start.reshape(-1, size)
        tile = jnp.arange(group_rows // size, dtype=jnp.int32)
        low = tile_start[:, 0] // size
        return low, jnp.minimum((tile_start[:, -1] + size - 1) // size, tile)

    start_row = jnp.tile(doc_start.reshape(-1, 1, SUB), (1, 1, q_heads // kv_heads))
    layout = (place, *bounds(TILE), cosine, sine, doc_start[:, None])
    layout_back = (place, *bounds(SUB), cosine, sine, start_row)
    lower, upper_sib, down_shard, out_shard, *moved = stage(
        lower, upper_sib, down_weight, out_weight, *upper_far, *taken, *layout, *layout_back
    )
    upper_far, moved = moved[: near - 1], moved[near - 1 :]
    taken, moved = moved[: len(taken)], moved[len(taken) :]
    layout, layout_back = moved[: len(layout)], moved[len(layout) :]

    lower_far = [from_near(lower, k) for k in others]
    lower_sib = flip(lower, "core")
    down_out = crossed(down_shard, OUT)
    blocks = blocks_of(pair, taken, diagonal(taken))
    projecting = [(*blocks, qkv_cols)]
    gain_row = gain_one[None]
    outs = [(tokens.shape[1], bf16, "all"), (qkv_cols, bf16, "all")]
    parts = [upper, lower, upper_sib, lower_sib]
    normed = piece_call(project_kernel, "project", 0, near, me, parts, [gain_row], [], projecting, [], outs)
    gate_up_shard, down_out, down_shard, out_shard, *moved = stage(
        gate_up_shard, down_out, down_shard, out_shard, *lower_far, *normed
    )
    lower_far, normed = moved[: near - 1], moved[near - 1 :]

    down_cross = crossed(down_shard, CROSS)
    out_moved = send_z(out_shard)
    for k in others:
        parts = [upper_far[k - 1], lower_far[k - 1], flip(upper_far[k - 1], "core"), flip(lower_far[k - 1], "core")]
        normed = piece_call(project_kernel, "project", k, near, me, parts, [gain_row], [], projecting, normed, outs)
    norm_one, qkv = normed
    gate_up_shard, qkv, down_cross, *out_moved = stage(gate_up_shard, qkv, down_cross, *out_moved)

    gate_up_moved = send_z(gate_up_shard)
    out_pair = pair_of(out_weight, *out_moved)
    out_far = [from_near(out_pair, k) for k in others]
    context, sums = attend(qkv, near, layout, q_heads, kv_heads)
    cotangent, *moved = stage(cotangent, *context, *gate_up_moved, *out_far)
    context, gate_up_moved, out_far = moved[:near], moved[near : near + 2], moved[near + 2 :]

    quarters = [context[0]] + [None] * (near - 1)
    for k in others:
        quarters[near - k] = to_near(context[k], k)
    cot_upper = crossed(cotangent[:part_rows], CROSS)
    pairs = [
        pair_of(*(x[:, n * hidden_cols : (n + 1) * hidden_cols] for x in (gate_up_shard, *gate_up_moved)))
        for n in range(2)
    ]
    gate_taken = neighbours(pairs[0])
    w_out = lax.all_gather(jnp.concatenate([out_pair, *out_far], axis=1), "yx", axis=0, tiled=True)
    up_pair, cotangent, cot_upper, *moved = stage(pairs[1], cotangent, cot_upper, *quarters, *gate_taken)
    quarters, gate_taken = moved[:near], moved[near:]

    up_taken = neighbours(up_pair)
    cot_lower = crossed(cotangent[part_rows:], CROSS)
    residual = jnp.concatenate([upper, lower], axis=0).astype(f32)
    scale_one = lax.rsqrt(jnp.mean(residual * residual, axis=-1, keepdims=True) + EPSILON)
    context_all = jnp.concatenate(quarters, axis=1)
    w_out, scale_one, cot_lower, context_all, *up_taken = stage(w_out, scale_one, cot_lower, context_all, *up_taken)

    gate_halves, up_halves = diagonal(gate_taken), diagonal(up_taken)
    branch_sib = flip(times_transpose(context_all[rows:], w_out).astype(bf16), "core")
    mid = residual + times_transpose(context_all[:rows], w_out) + branch_sib.astype(f32)
    scale_two, norm_two = norm_rows(mid, gain_two)
    norm_two, *moved = stage(norm_two, *gate_halves, *up_halves)
    gate_halves, up_halves = moved[: len(gate_halves)], moved[len(gate_halves) :]
    norm_sib = flip(norm_two, "core")
    cot = jnp.where(straight(), cotangent, jnp.concatenate([cot_upper, cot_lower], axis=0))
    cot_sib = flip(cot, "core")
    down_pair = pair_of(down_weight, down_out, down_cross)
    norm_two, norm_sib, cot, cot_sib, down_pair = stage(norm_two, norm_sib, cot, cot_sib, down_pair)

    upper_far = [from_near(norm_two[:part_rows], k) for k in others]
    down_taken = neighbours(down_pair)
    gate_blocks = blocks_of(pairs[0], gate_taken, gate_halves)
    up_blocks = blocks_of(up_pair, up_taken, up_halves, hidden_cols)
    gate_up = ([*gate_blocks[0], *up_blocks[0]], gate_blocks[1] + up_blocks[1], 2 * hidden_cols)
    outs = [(norm_two.shape[1], bf16, "all"), (2 * hidden_cols, f32, "all"), (hidden_cols, bf16, "all")]
    earlier = piece_call(gate_kernel, "gate", 0, near, me, [norm_two, norm_sib], [], [], [gate_up], [], outs)
    norm_two, *moved = stage(norm_two, *upper_far, *down_taken, *earlier)
    upper_far, moved = moved[: near - 1], moved[near - 1 :]
    down_taken, earlier = moved[: len(down_taken)], moved[len(down_taken) :]

    lower_far = [from_near(norm_two[part_rows:], k) for k in others]
    upper_far_sib = [flip(x, "core") for x in upper_far]
    down_halves = diagonal(down_taken)
    w_project = assemble("assemble_project", me, *blocks, tokens.shape[1], qkv_cols)
    w_project, *moved = stage(w_project, *lower_far, *upper_far_sib, *down_halves)
    lower_far, upper_far_sib, down_halves = moved[: near - 1], moved[near - 1 : 2 * near - 2], moved[2 * near - 2 :]
    lower_far_sib = [flip(x, "core") for x in lower_far]

    cot_upper_far = [from_near(cot[:part_rows], k) for k in others]
    down = (*blocks_of(down_pair, down_taken, down_halves), hidden_cols)
    width = norm_two.shape[1]
    gate_outs, outs = outs, [(width, bf16, "all"), (2 * hidden_cols, bf16, "all")]
    halves = [(width, bf16, "own"), (width, bf16, "sibling")]

    def way_back(k, parts, earlier):
        tiled, results = [(gate_up_all, k), (hidden_all, k)], outs + halves * (1 if earlier else 2)
        return piece_call(gate_back_kernel, "gate_back", k, near, me, parts, [], tiled, [gate_up, down], earlier, results)

    def joined(own, sib):
        return own.astype(f32) + flip(sib, "core").astype(f32)

    norm_two_all, gate_up_all, hidden_all = earlier
    grad_all, d_gate_up_all, *near_back = way_back(0, [cot, cot_sib], [])
    cot, *moved = stage(
        cot, norm_two_all, gate_up_all, hidden_all, grad_all, d_gate_up_all, *near_back, *cot_upper_far, *lower_far_sib
    )
    earlier, moved = moved[:3], moved[3:]
    grad_all, d_gate_up_all, *moved = moved
    near_back, cot_upper_far, lower_far_sib = moved[:4], moved[4 : near + 3], moved[near + 3 :]

    cot_lower_far = [from_near(cot[part_rows:], k) for k in others]
    cot_upper_far_sib = [flip(x, "core") for x in cot_upper_far]
    out_far = []
    for k in others:
        parts = [upper_far[k - 1], lower_far[k - 1], upper_far_sib[k - 1], lower_far_sib[k - 1]]
        *earlier, out_own, out_sib = piece_call(
            gate_kernel, "gate", k, near, me, parts, [], [], [gate_up, down], earlier, gate_outs + halves
        )
        out_far += [out_own, out_sib]
    grad_all, d_gate_up_all, *moved = stage(
        grad_all, d_gate_up_all, *near_back, *cot_lower_far, *cot_upper_far_sib, *earlier, *out_far
    )
    near_back, cot_lower_far, moved = moved[:4], moved[4 : near + 3], moved[near + 3 :]
    cot_upper_far_sib, earlier, out_far = moved[: near - 1], moved[near - 1 : near + 2], moved[near + 2 :]
    norm_two_all, gate_up_all, hidden_all = earlier
    cot_lower_far_sib = [flip(x, "core") for x in cot_lower_far]
    out_sums = [joined(*out_far[2 * n : 2 * n + 2]).astype(bf16) for n in range(near - 1)]
    moved = stage(*cot_lower_far_sib, *out_sums)
    cot_lower_far_sib, out_sums = moved[: near - 1], moved[near - 1 :]

    out_upper = [to_near(out_sums[k - 1][:part_rows], k) for k in others]
    back = []
    for k in others:
        parts = [cot_upper_far[k - 1], cot_lower_far[k - 1], cot_upper_far_sib[k - 1], cot_lower_far_sib[k - 1]]
        grad_all, d_gate_up_all, *more = way_back(k, parts, [grad_all, d_gate_up_all])
        back.append(more)
    grad_all, d_gate_up_all, *moved = stage(grad_all, d_gate_up_all, *(x for more in back for x in more), *out_upper)
    far_back, out_upper = moved[: 2 * near - 2], moved[2 * near - 2 :]
    d_norm_sent = [joined(*far_back[2 * n : 2 * n + 2]).astype(bf16) for n in range(near - 1)]
    grad_all, d_gate_up_all, near_own, near_sib, *d_norm_sent = stage(
        grad_all, d_gate_up_all, *near_back[:2], *d_norm_sent
    )

    moved_upper = [to_near(d_norm_sent[k - 1][:part_rows], k) for k in others]
    grad_gate_up = rows_product(norm_two_all, d_gate_up_all).astype(bf16)
    grad_gate_up, grad_all, near_own, near_sib, *moved = stage(
        grad_gate_up, grad_all, near_own, near_sib, *moved_upper, *d_norm_sent
    )
    moved_upper, d_norm_sent = moved[: near - 1], moved[near - 1 :]

    moved_lower = [to_near(d_norm_sent[k - 1][part_rows:], k) for k in others]
    gate_up_part = lax.psum_scatter(grad_gate_up, "yx", scatter_dimension=0, tiled=True)
    d_norm_two = joined(near_own, near_sib)
    grad_down = rows_product(grad_all, hidden_all).astype(bf16)
    grad_down, d_norm_two, *moved = stage(grad_down, d_norm_two, *out_sums, *moved_lower)
    out_sums, moved_lower = moved[: near - 1], moved[near - 1 :]

    out_lower = [to_near(out_sums[k - 1][part_rows:], k) for k in others]
    down_part = lax.psum_scatter(grad_down, "yx", scatter_dimension=0, tiled=True)
    for one, two in zip(moved_upper, moved_lower, strict=True):
        d_norm_two = d_norm_two + jnp.concatenate([one, two], axis=0).astype(f32)
    mid_back, _ = norm_back(mid, scale_two, gain_two, d_norm_two)
    d_mid = cot.astype(f32) + mid_back
    d_attn = d_mid.astype(bf16)
    d_attn_sib = flip(d_attn, "core")
    both = [dot32(x, w_out).astype(bf16) for x in (d_attn, d_attn_sib)]
    d_quarters = [
        jnp.concatenate([x[:, k * query_cols : (k + 1) * query_cols] for x in both], axis=0) for k in range(near)
    ]
    d_attn, d_attn_sib, *moved = stage(d_attn, d_attn_sib, *d_quarters, *out_lower)
    d_quarters, out_lower = moved[:near], moved[near:]

    d_context = [d_quarters[0]] + [None] * (near - 1)
    for k in others:
        d_context[near - k] = to_near(d_quarters[k], k)
    grad_out = rows_product(d_attn, context_all[:rows]) + rows_product(d_attn_sib, context_all[rows:])
    grad_out = grad_out.astype(bf16)
    output_own = mid + joined(*near_back[2:])
    for one, two in zip(out_upper, out_lower, strict=True):
        output_own = output_own + jnp.concatenate([one, two], axis=0).astype(f32)
    output_own = output_own.astype(bf16)
    grad_out, output_own, gate_up_part, *d_context = stage(grad_out, output_own, gate_up_part, *d_context)

    output_crossed = crossed(output_own, CROSS)
    gate_up_keep, gate_up_give = give_z(gate_up_part)
    gate_up_back = crossed(gate_up_give, BACK)
    out_part = lax.psum_scatter(grad_out, "yx", scatter_dimension=0, tiled=True)
    d_qkv = attend_back(list(range(kv_heads)), qkv, d_context, context, sums, [], layout_back, q_heads, kv_heads)
    d_qkv, output_crossed, gate_up_back, gate_up_keep, down_part = stage(
        d_qkv, output_crossed, gate_up_back, gate_up_keep, down_part
    )

    def back_part(k):
        own, sib = (d_qkv[(2 * k + e) * rows : (2 * k + e + 1) * rows] for e in range(2))
        taken = flip(times_transpose(sib, w_project).astype(bf16), "core")
        return times_transpose(own, w_project) + taken.astype(f32)

    gate_up_cross = crossed(gate_up_keep, CROSS)
    d_sent = [back_part(k).astype(bf16) for k in others]
    d_qkv, gate_up_cross, down_part, *d_sent = stage(d_qkv, gate_up_cross, down_part, *d_sent)

    d_upper = [to_near(d_sent[k - 1][:part_rows], k) for k in others]
    down_keep, down_give = give_z(down_part)
    down_home = [crossed(down_give, BACK), crossed(down_keep, CROSS)]
    grad_project = rows_product(norm_one, d_qkv).astype(bf16)
    project_sent = send_yx(grad_project, (0, qkv_cols))
    total = back_part(0)
    total, grad_project, *moved = stage(total, grad_project, *d_upper, *d_sent, *project_sent, *down_home)
    d_upper, d_sent, project_sent, down_home = (
        moved[: near - 1], moved[near - 1 : 2 * near - 2], moved[2 * near - 2 : -2], moved[-2:],
    )

    d_lower = [to_near(d_sent[k - 1][part_rows:], k) for k in others]
    project_rest, project_own = join_yx(grad_project, (0, qkv_cols), project_sent)

    def input_part(at, moved):
        part = total[at]
        for x in moved:
            part = part + x.astype(f32)
        back, _ = norm_back(residual[at], scale_one[at], gain_one, part)
        return (d_mid[at] + back).astype(bf16)

    input_upper = input_part(slice(0, part_rows), d_upper)
    upper_crossed = crossed(input_upper, CROSS)
    total, input_upper, upper_crossed, out_part, *moved = stage(
        total, input_upper, upper_crossed, out_part, *d_lower, *project_rest
    )
    d_lower, project_rest = moved[: near - 1], moved[near - 1 :]

    project_keep, project_give = give_z(total_yx(project_rest, project_own))
    project_home = [crossed(project_give, BACK), crossed(project_keep, CROSS)]
    input_lower = input_part(slice(part_rows, rows), d_lower)
    lower_crossed = crossed(input_lower, CROSS)
    out_moved = [to_near(out_part[:, k * query_cols : (k + 1) * query_cols], k) for k in others]
    out_quarter = out_part[:, :query_cols].astype(f32)
    for part in out_moved:
        out_quarter = out_quarter + part.astype(f32)
    out_keep, out_give = give_z(out_quarter.astype(bf16))
    out_home = [crossed(out_give, BACK), crossed(out_keep, CROSS)]
    grad_project = sum_z(project_keep, *project_home)
    grad_out = sum_z(out_keep, *out_home)
    grad_down = sum_z(down_keep, *down_home)
    grad_gate_up = sum_z(gate_up_keep, gate_up_back, gate_up_cross)
    output = jnp.where(straight(), output_own, output_crossed)
    input_grad = jnp.concatenate(
        [
            jnp.where(straight(), input_upper, upper_crossed),
            jnp.where(straight(), input_lower, lower_crossed),
        ],
        axis=0,
    ).astype(f32)
    gain_grads = lax.psum(
        jnp.stack(
            [
                jnp.sum(qkv_shard.astype(f32) * grad_project, axis=1),
                jnp.sum(gate_up_shard.astype(f32) * grad_gate_up, axis=1),
            ]
        ),
        ("zh", "zl"),
    ) / jnp.stack([attn_gain, mlp_gain]).astype(f32)
    return (
        output,
        input_grad,
        gain_grads[0],
        grad_project[:, :query_cols],
        grad_project[:, query_cols : query_cols + key_cols],
        grad_project[:, query_cols + key_cols :],
        grad_out,
        gain_grads[1],
        grad_gate_up[:, :hidden_cols],
        grad_gate_up[:, hidden_cols:],
        grad_down,
    )


def solution(mesh):
    dp, tensor = mesh.shape["dp"], mesh.shape["tensor"]
    fine = Mesh(mesh.devices.reshape(dp // 2, 2, 2, tensor // 2), AXES)
    by_rows, by_dp, by_both = P(AXES, None), P(("yx", "core")), P(("yx", "core"), ("zh", "zl"))
    return jax.shard_map(
        body,
        mesh=fine,
        in_specs=(
            by_rows, by_rows, P(("yx", "core"), None), by_dp, by_both, by_both, by_both, by_both,
            by_dp, by_both, by_both, by_both,
        ),
        out_specs=(
            by_rows, by_rows, by_dp, by_both, by_both, by_both, by_both, by_dp, by_both, by_both, by_both,
        ),
        check_vma=False,
    )
```

```python
import functools
import math

import jax
import jax.numpy as jnp
import numpy as np
from jax import lax
from jax.experimental import pallas as pl
from jax.experimental.pallas import tpu as pltpu
from jax.sharding import Mesh
from jax.sharding import PartitionSpec as P

HD = 96
HALF = HD // 2
PAD = 128
STEPS = 4
SUB = 256
TILE = 512

EPSILON = 1e-05
ROTARY_BASE = 100000.0
MASKED = -1e30
LOG2E = math.log2(math.e)

AXES = ("yx", "core", "zh", "zl")
FLIP = [(0, 1), (1, 0)]


def norm_rows(values, gain):
    row_scale = lax.rsqrt(jnp.mean(values * values, axis=-1, keepdims=True) + EPSILON)
    return (row_scale, (values * row_scale * gain).astype(jnp.bfloat16))


def norm_back(values, row_scale, gain, upstream):
    weighted = upstream * gain
    inner_sum = jnp.mean(weighted * values, axis=-1, keepdims=True)
    grad_in = row_scale * weighted - values * (row_scale * row_scale * row_scale) * inner_sum
    gain_part = jnp.sum(upstream * (values * row_scale), axis=0)
    return (grad_in, gain_part)


def document_layout(lengths, group_rows):
    flat_lengths = lengths.reshape(-1)
    doc_ends = jnp.cumsum(flat_lengths)
    rows = jnp.arange(group_rows, dtype=jnp.int32)
    passed = (rows[:, None] >= doc_ends[None, :]).astype(jnp.int32)
    return (rows, jnp.sum(passed * flat_lengths[None, :], axis=1))


def rotary_tables(positions):
    exponents = jnp.arange(HALF, dtype=jnp.float32) * (2.0 / HD)
    inverse = ROTARY_BASE ** (-exponents)
    angles = positions.astype(jnp.float32)[:, None] * inverse[None, :]
    cosine, sine = jnp.cos(angles), jnp.sin(angles)
    gap = jnp.zeros((positions.shape[0], PAD // 2 - HALF), jnp.float32)
    return (
        jnp.concatenate([cosine, gap, cosine, gap], axis=1),
        jnp.concatenate([-sine, gap, sine, gap], axis=1),
    )


def rows_product(left, right):
    return lax.dot_general(
        left, right, (((0,), (0,)), ((), ())), preferred_element_type=jnp.float32
    )


def times_transpose(left, right):
    return lax.dot_general(
        left, right, (((1,), (1,)), ((), ())), preferred_element_type=jnp.float32
    )


def dot32(left, right):
    return jnp.dot(left, right, preferred_element_type=jnp.float32)


def stage(*values):
    return lax.optimization_barrier(values)


def spread(columns, heads):
    matrix = np.zeros((columns, len(heads) * PAD), np.float32)
    for at, first in enumerate(heads):
        for half in range(2):
            for i in range(HALF):
                matrix[first + half * HALF + i, at * PAD + half * (PAD // 2) + i] = 1.0
    return matrix


def turn(x, cosine, sine):
    return x * cosine + pltpu.roll(x, PAD // 2, 1) * sine


def rows_at(t, size):
    return pl.ds(pl.multiple_of(t * size, size), size)


def forward_kernel(pieces, ratio, *refs):
    place, low, full, cosine, sine, start, spread_in, gather_out = refs[:8]
    heads = spread_in.shape[0]
    refs = refs[8:]
    qkv, context, refs = refs[0], refs[1 : 1 + pieces], refs[1 + pieces :]
    log_sum, refs = refs[:heads], refs[heads:]
    q_s, k_s, v_s, s_s, top_s, acc = refs
    tiles = q_s.shape[0]
    all_subs = qkv.shape[0] // SUB
    piece_subs = all_subs // pieces
    scale = LOG2E * HD ** (-0.5)
    ones_lane = lax.broadcasted_iota(jnp.int32, (SUB, PAD), 1) == PAD - 1

    def prepare(r, carry):
        t = place[r]
        at = rows_at(t, SUB)
        cos_t, sin_t = cosine[at, :], sine[at, :]
        tile, half = t // (TILE // SUB), t % (TILE // SUB)
        for g in range(heads):
            wide = dot32(qkv[rows_at(r, SUB), :], spread_in[g])
            for h in range(ratio):
                query = turn(wide[:, h * PAD : (h + 1) * PAD], cos_t, sin_t) * scale
                first = pl.multiple_of(h * TILE + half * SUB, SUB)
                q_s[tile, g, pl.ds(first, SUB), :] = query.astype(jnp.bfloat16)
            key = turn(wide[:, ratio * PAD : (ratio + 1) * PAD], cos_t, sin_t)
            k_s[g, at, :] = key.astype(jnp.bfloat16)
            value = jnp.where(ones_lane, 1.0, wide[:, (ratio + 1) * PAD :])
            v_s[g, at, :] = value.astype(jnp.bfloat16)
        return carry

    lax.fori_loop(0, all_subs, prepare, 0)

    def query_tile(i, carry):
        starts = jnp.concatenate([start[rows_at(i, TILE), :]] * ratio, axis=0)
        top_s[...] = jnp.full_like(top_s, MASKED)

        def scores(j, masked, diagonal):
            for g in range(heads):
                s = times_transpose(q_s[i, g], k_s[g, rows_at(j, TILE), :])
                if masked:
                    key_at = lax.broadcasted_iota(jnp.int32, s.shape, 1)
                    allowed = key_at + j * TILE >= starts
                    if diagonal:
                        query_at = lax.rem(lax.broadcasted_iota(jnp.int32, s.shape, 0), TILE)
                        allowed = allowed & (key_at <= query_at)
                    s = jnp.where(allowed, s, MASKED)
                s_s[g, j] = s
                peak = s[:, :PAD]
                for c in range(1, TILE // PAD):
                    peak = jnp.maximum(peak, s[:, c * PAD : (c + 1) * PAD])
                top_s[g] = jnp.maximum(top_s[g], peak)

        def loop(first, last, masked):
            def run(j, c):
                scores(j, masked, False)
                return c

            lax.fori_loop(first, last, run, 0)

        loop(low[i], full[i], True)
        loop(full[i], i, False)
        scores(i, True, True)
        tops = [jnp.max(top_s[g], axis=1, keepdims=True) for g in range(heads)]
        acc[...] = jnp.zeros_like(acc)

        def weigh(j, c):
            for g in range(heads):
                p = jnp.exp2(s_s[g, j] - tops[g]).astype(jnp.bfloat16)
                acc[g] += dot32(p, v_s[g, rows_at(j, TILE), :])
            return c

        lax.fori_loop(low[i], i + 1, weigh, 0)
        packed = None
        for g in range(heads):
            total = acc[g][:, PAD - 1 :]
            out = acc[g] * (1.0 / total)
            sums = jnp.broadcast_to(tops[g] + jnp.log(total) * LOG2E, (ratio * TILE, PAD))
            log_sum[g][i] = sums.T[:1, :]
            wide = jnp.concatenate(
                [out[h * TILE : (h + 1) * TILE, :] for h in range(ratio)], axis=1
            ).astype(jnp.bfloat16)
            part = dot32(wide, gather_out[g])
            packed = part if packed is None else packed + part
        subs = tiles * (TILE // SUB)
        for half in range(TILE // SUB):
            r = place[subs + i * (TILE // SUB) + half]
            part = packed[half * SUB : (half + 1) * SUB, :].astype(jnp.bfloat16)
            for k in range(pieces):

                @pl.when(r // piece_subs == k)
                def store(k=k, part=part, r=r):
                    context[k][rows_at(r % piece_subs, SUB), :] = part

        return carry

    lax.fori_loop(0, tiles, query_tile, 0)


def backward_kernel(pieces, ratio, more, *refs):
    place, low, full, cosine, sine, start, refs = *refs[:6], refs[6:]
    heads = refs[0].shape[0]
    spread_in, spread_out, gather_in, refs = *refs[:3], refs[3:]
    log_sum, refs = refs[:heads], refs[heads:]
    d_context, context, qkv, refs = refs[:pieces], refs[pieces : 2 * pieces], refs[2 * pieces], refs[2 * pieces + 1 :]
    earlier, refs = (refs[0], refs[1:]) if more else (None, refs)
    d_qkv, refs = refs[0], refs[1:]
    q_s, k_s, kt_s, v_s, do_s, delta_s, log_s, dq_acc, dk_acc, dv_acc, dq_s = refs
    tiles = q_s.shape[0]
    all_subs = qkv.shape[0] // SUB
    piece_subs = all_subs // pieces
    scale = HD ** (-0.5)
    per_tile = TILE // SUB

    for k in range(pieces):

        def prepare(r, carry, k=k):
            t = place[k * piece_subs + r]
            rel = rows_at(r, SUB)
            at = rows_at(t, SUB)
            cos_t, sin_t = cosine[at, :], sine[at, :]
            for g in range(heads):
                wide = dot32(qkv[rows_at(k * piece_subs + r, SUB), :], spread_in[g])
                d_out = dot32(d_context[k][rel, :], spread_out[g])
                out = dot32(context[k][rel, :], spread_out[g])
                for h in range(ratio):
                    cols = slice(h * PAD, (h + 1) * PAD)
                    rows = slice(h * SUB, (h + 1) * SUB)
                    query = turn(wide[:, cols], cos_t, sin_t) * (scale * LOG2E)
                    q_s[t, g, rows, :] = query.astype(jnp.bfloat16)
                    do_s[t, g, rows, :] = d_out[:, cols].astype(jnp.bfloat16)
                    delta = jnp.sum((d_out[:, cols] * out[:, cols]).T, axis=0, keepdims=True)
                    delta_s[t * heads + g, :, rows] = delta
                    first = pl.multiple_of(h * TILE + t % per_tile * SUB, SUB)
                    log_s[t * heads + g, :, rows] = log_sum[g][t // per_tile, :, pl.ds(first, SUB)]
                key = turn(wide[:, ratio * PAD : (ratio + 1) * PAD], cos_t, sin_t)
                k_s[g, t] = key.astype(jnp.bfloat16)
                kt_s[g, t] = key.T.astype(jnp.bfloat16)
                v_s[g, t] = wide[:, (ratio + 1) * PAD :].astype(jnp.bfloat16)
                dk_acc[g, t] = jnp.zeros((SUB, PAD), jnp.float32)
                dv_acc[g, t] = jnp.zeros((SUB, PAD), jnp.float32)
            return carry

        lax.fori_loop(0, piece_subs, prepare, 0)

    def query_tile(i, carry):
        dq_acc[...] = jnp.zeros_like(dq_acc)

        def step(j, masked, diagonal):
            for g in range(heads):
                queries, d_out = q_s[i, g], do_s[i, g]
                s = times_transpose(k_s[g, j], queries)
                if masked:
                    key_at = lax.broadcasted_iota(jnp.int32, s.shape, 0)
                    allowed = key_at + j * SUB >= start[i]
                    if diagonal:
                        query_at = lax.rem(lax.broadcasted_iota(jnp.int32, s.shape, 1), SUB)
                        allowed = allowed & (key_at <= query_at)
                    s = jnp.where(allowed, s, MASKED)
                p = jnp.exp2(s - log_s[i * heads + g])
                d_p = times_transpose(v_s[g, j], d_out)
                d_s = (p * (d_p - delta_s[i * heads + g])).astype(jnp.bfloat16)
                dv_acc[g, j] += dot32(p.astype(jnp.bfloat16), d_out)
                dk_acc[g, j] += dot32(d_s, queries)
                dq_acc[g] += dot32(kt_s[g, j], d_s)

        def loop(first, last, masked):
            def run(j, c):
                step(j, masked, False)
                return c

            lax.fori_loop(first, last, run, 0)

        loop(low[i], full[i], True)
        loop(full[i], i, False)
        step(i, True, True)
        at = rows_at(i, SUB)
        cos_t, sin_t = cosine[at, :], sine[at, :]
        for g in range(heads):
            grad = dq_acc[g].T * scale
            for h in range(ratio):
                piece = turn(grad[h * SUB : (h + 1) * SUB, :], cos_t, -sin_t)
                dq_s[g, i, :, h * PAD : (h + 1) * PAD] = piece.astype(jnp.bfloat16)
        return carry

    lax.fori_loop(0, tiles, query_tile, 0)

    def finish(r, carry):
        t = place[r]
        at = rows_at(t, SUB)
        rel = rows_at(r, SUB)
        packed = None
        for g in range(heads):
            key = turn(dk_acc[g, t] * (1.0 / LOG2E), cosine[at, :], -sine[at, :])
            wide = jnp.concatenate(
                [dq_s[g, t], key.astype(jnp.bfloat16), dv_acc[g, t].astype(jnp.bfloat16)], axis=1
            )
            part = dot32(wide, gather_in[g])
            packed = part if packed is None else packed + part
        packed = packed.astype(jnp.bfloat16)
        d_qkv[rel, :] = packed + earlier[rel, :] if more else packed
        return carry

    lax.fori_loop(0, all_subs, finish, 0)


SMEM = pl.BlockSpec(memory_space=pltpu.SMEM)
VMEM = pl.BlockSpec(memory_space=pltpu.VMEM)
ANY = pl.BlockSpec(memory_space=pl.ANY)


def small_cost(transcendentals=0):
    return pl.CostEstimate(flops=1 << 20, bytes_accessed=1 << 16, transcendentals=transcendentals)


def head_matrices(head, q_heads, kv_heads):
    ratio = q_heads // kv_heads
    queries = [(head * ratio + r) * HD for r in range(ratio)]
    key, value = (q_heads + head) * HD, (q_heads + kv_heads + head) * HD
    inner = spread((q_heads + 2 * kv_heads) * HD, [*queries, key, value])
    outer = spread(q_heads * HD, queries)
    return jnp.asarray(inner, jnp.bfloat16), jnp.asarray(outer, jnp.bfloat16)


def stacked_matrices(q_heads, kv_heads):
    pairs = [head_matrices(head, q_heads, kv_heads) for head in range(kv_heads)]
    return jnp.stack([inner for inner, _ in pairs]), jnp.stack([outer for _, outer in pairs])


def attend(qkv, pieces, layout, q_heads, kv_heads):
    place, low, full, cosine, sine, start_column = layout
    ratio, rows = q_heads // kv_heads, qkv.shape[0]
    tiles, lanes = rows // TILE, ratio * TILE
    bf16, f32 = jnp.bfloat16, jnp.float32
    inner, outer = stacked_matrices(q_heads, kv_heads)
    outs = pl.pallas_call(
        functools.partial(forward_kernel, pieces, ratio),
        out_shape=[
            *[jax.ShapeDtypeStruct((rows // pieces, q_heads * HD), bf16)] * pieces,
            *[jax.ShapeDtypeStruct((tiles, 1, lanes), f32)] * kv_heads,
        ],
        in_specs=[SMEM] * 3 + [VMEM] * 6,
        out_specs=[VMEM] * (pieces + kv_heads),
        scratch_shapes=[
            pltpu.VMEM((tiles, kv_heads, lanes, PAD), bf16),
            pltpu.VMEM((kv_heads, rows, PAD), bf16),
            pltpu.VMEM((kv_heads, rows, PAD), bf16),
            pltpu.VMEM((kv_heads, tiles, lanes, TILE), f32),
            pltpu.VMEM((kv_heads, lanes, PAD), f32),
            pltpu.VMEM((kv_heads, lanes, PAD), f32),
        ],
        compiler_params=pltpu.CompilerParams(vmem_limit_bytes=60 * 2**20),
        cost_estimate=small_cost(),
        name="attention_forward",
    )(place, low, full, cosine, sine, start_column, inner, jnp.swapaxes(outer, 1, 2), qkv)
    return outs[:pieces], outs[pieces:]


def attend_back(heads, qkv, d_context, context, sums, earlier, layout, q_heads, kv_heads):
    place, low, full, cosine, sine, start_row = layout
    pieces, ratio, rows = len(context), q_heads // kv_heads, qkv.shape[0]
    tiles, lanes, count = rows // SUB, ratio * SUB, len(heads)
    bf16, f32 = jnp.bfloat16, jnp.float32
    inner, outer = stacked_matrices(q_heads, kv_heads)
    inner, outer = inner[heads[0] : heads[0] + count], outer[heads[0] : heads[0] + count]
    return pl.pallas_call(
        functools.partial(backward_kernel, pieces, ratio, bool(earlier)),
        out_shape=jax.ShapeDtypeStruct(qkv.shape, bf16),
        in_specs=[SMEM] * 3 + [VMEM] * (7 + count + 2 * pieces + len(earlier)),
        out_specs=VMEM,
        scratch_shapes=[
            pltpu.VMEM((tiles, count, lanes, PAD), bf16),
            pltpu.VMEM((count, tiles, SUB, PAD), bf16),
            pltpu.VMEM((count, tiles, PAD, SUB), bf16),
            pltpu.VMEM((count, tiles, SUB, PAD), bf16),
            pltpu.VMEM((tiles, count, lanes, PAD), bf16),
            pltpu.VMEM((tiles * count, 1, lanes), f32),
            pltpu.VMEM((tiles * count, 1, lanes), f32),
            pltpu.VMEM((count, PAD, lanes), f32),
            pltpu.VMEM((count, tiles, SUB, PAD), f32),
            pltpu.VMEM((count, tiles, SUB, PAD), f32),
            pltpu.VMEM((count, tiles, SUB, ratio * PAD), bf16),
        ],
        compiler_params=pltpu.CompilerParams(vmem_limit_bytes=60 * 2**20),
        cost_estimate=small_cost(),
        name=f"attention_backward_{heads[0]}",
    )(
        place, low, full, cosine, sine, start_row, inner, outer, jnp.swapaxes(inner, 1, 2),
        *[sums[h] for h in heads], *d_context, *context, qkv, *earlier,
    )


def fetch(me, where, sources, target, sems):
    copies = []
    for n, (source, (j, deep, first, column, taken)) in enumerate(zip(sources, where, strict=True)):
        cols = min(source.shape[1] - taken, target.shape[1] - column)
        at = pl.ds(pl.multiple_of((me[0] ^ j) * deep + first, 16), source.shape[0])
        if cols != source.shape[1]:
            source = source.at[:, taken : taken + cols]
        copies.append(pltpu.make_async_copy(source, target.at[at, column : column + cols], sems.at[n]))
    return copies


def take_rows(parts, target):
    rows = target.shape[0]
    for step in range(STEPS):

        @pl.when(pl.program_id(0) == step)
        def take(step=step):
            at = 0
            for part in parts:
                first, last = max(at, step * rows), min(at + part.shape[0], (step + 1) * rows)
                if first < last:
                    target[first - step * rows : last - step * rows, :] = part[first - at : last - at, :]
                at += part.shape[0]


def at_first_step(copies, what):
    @pl.when(pl.program_id(0) == 0)
    def run():
        for copy in copies:
            what(copy)


def project_kernel(count, where, more, me, *refs):
    parts, gain, refs = refs[:count], refs[count], refs[count + 1 :]
    sources, refs = refs[: len(where[0])], refs[len(where[0]) :]
    norm_all, qkv_all, weight, sems, rows_s = refs[2 if more else 0 :]
    copies = fetch(me, where[0], sources, weight, sems)
    at_first_step(copies, lambda copy: copy.start())
    take_rows(parts, rows_s)
    x = rows_s[...].astype(jnp.float32)
    scale = lax.rsqrt(jnp.mean(x * x, axis=-1, keepdims=True) + EPSILON)
    norm_all[...] = (x * scale * gain[...]).astype(jnp.bfloat16)
    at_first_step(copies, lambda copy: copy.wait())
    qkv_all[...] = dot32(norm_all[...], weight[...]).astype(jnp.bfloat16)


def by_half(refs, value):
    for n, ref in enumerate(refs):

        @pl.when(pl.program_id(0) * 2 // STEPS == n)
        def store(ref=ref):
            ref[...] = value


def gate_kernel(count, where, more, me, *refs):
    parts, refs = refs[:count], refs[count:]
    with_out = len(where) > 1
    sources, refs = refs[: sum(map(len, where))], refs[sum(map(len, where)) :]
    norm_all, gate_up_all, hidden_all, *refs = refs[3 if more else 0 :]
    out_refs, refs = (refs[:2], refs[2:]) if with_out else ((), refs)
    weight, sems, *refs = refs
    hidden_cols = hidden_all.shape[1]
    copies = fetch(me, where[0], sources[: len(where[0])], weight, sems)
    if with_out:
        w_down, down_sems = refs
        copies += fetch(me, where[1], sources[len(where[0]) :], w_down, down_sems)
    at_first_step(copies, lambda copy: copy.start())
    take_rows(parts, norm_all)
    at_first_step(copies, lambda copy: copy.wait())
    x = norm_all[...]
    width = min(512, hidden_cols)
    for at in range(0, hidden_cols, width):
        gate_at = slice(at, at + width)
        up_at = slice(hidden_cols + at, hidden_cols + at + width)
        gate = dot32(x, weight[:, gate_at])
        up = dot32(x, weight[:, up_at])
        gate_up_all[:, gate_at] = gate
        gate_up_all[:, up_at] = up
        hidden_all[:, gate_at] = (gate * (1.0 / (1.0 + jnp.exp(-gate))) * up).astype(jnp.bfloat16)
    if with_out:
        by_half(out_refs, times_transpose(hidden_all[...], w_down[...]).astype(jnp.bfloat16))


def gate_back_kernel(count, where, more, me, *refs):
    parts, gate_up_all, hidden_here, refs = refs[:count], *refs[count : count + 2], refs[count + 2 :]
    gate_up, refs = refs[: len(where[0])], refs[len(where[0]) :]
    down, refs = refs[: len(where[1])], refs[len(where[1]) :]
    grad_all, d_gate_up_all, *refs = refs[2 if more else 0 :]
    d_norm_refs, refs = refs[:2], refs[2:]
    out_refs, refs = ((), refs) if more else (refs[:2], refs[2:])
    w_gate_up, gate_up_sems, w_down, down_sems = refs
    hidden_cols = w_down.shape[1]
    down_copies = fetch(me, where[1], down, w_down, down_sems)
    copies = fetch(me, where[0], gate_up, w_gate_up, gate_up_sems)
    at_first_step(down_copies + copies, lambda copy: copy.start())
    take_rows(parts, grad_all)
    at_first_step(down_copies, lambda copy: copy.wait())
    dy = grad_all[...]
    width = min(512, hidden_cols)
    for at in range(0, hidden_cols, width):
        gate_at = slice(at, at + width)
        up_at = slice(hidden_cols + at, hidden_cols + at + width)
        d_hidden = dot32(dy, w_down[:, gate_at])
        gate, up = gate_up_all[:, gate_at], gate_up_all[:, up_at]
        sigmoid = 1.0 / (1.0 + jnp.exp(-gate))
        d_gate = d_hidden * up * sigmoid * (1.0 + gate * (1.0 - sigmoid))
        d_gate_up_all[:, gate_at] = d_gate.astype(jnp.bfloat16)
        d_gate_up_all[:, up_at] = (d_hidden * (gate * sigmoid)).astype(jnp.bfloat16)
    if not more:
        by_half(out_refs, times_transpose(hidden_here[...], w_down[...]).astype(jnp.bfloat16))
    at_first_step(copies, lambda copy: copy.wait())
    by_half(d_norm_refs, times_transpose(d_gate_up_all[...], w_gate_up[...]).astype(jnp.bfloat16))


def piece_call(kernel, name, k, pieces, me, parts, whole, tiled, fetched, earlier, outs):
    tile, width = sum(x.shape[0] for x in parts) // STEPS, parts[0].shape[1]
    count = len(parts)

    def rows_of(piece):
        return lambda i: (piece * STEPS + i, 0)

    def half_of(span):
        first = 0 if span == "own" else STEPS // 2
        return lambda i: (jnp.clip(i - first, 0, STEPS // 2 - 1), 0)

    sources = [x for arrays, _, _ in fetched for x in arrays]
    first_earlier = 1 + count + len(whole) + len(tiled) + len(sources)
    scratch = []
    for arrays, _, cols in fetched:
        scratch += [pltpu.VMEM((width, cols), jnp.bfloat16), pltpu.SemaphoreType.DMA((len(arrays),))]
    if kernel is project_kernel:
        scratch.append(pltpu.VMEM((tile, width), jnp.bfloat16))
    return pl.pallas_call(
        functools.partial(kernel, count, tuple(where for _, where, _ in fetched), bool(earlier)),
        grid=(STEPS,),
        out_shape=[
            jax.ShapeDtypeStruct(((pieces * STEPS if span == "all" else STEPS // 2) * tile, columns), kind)
            for columns, kind, span in outs
        ],
        in_specs=[
            SMEM,
            *(pl.BlockSpec(x.shape, lambda i: (0, 0)) for x in parts),
            *(pl.BlockSpec(x.shape, lambda i: (0, 0)) for x in whole),
            *(pl.BlockSpec((tile, x.shape[1]), rows_of(piece)) for x, piece in tiled),
            *[ANY] * (len(sources) + len(earlier)),
        ],
        out_specs=[
            pl.BlockSpec((tile, columns), rows_of(k) if span == "all" else half_of(span))
            for columns, kind, span in outs
        ],
        scratch_shapes=scratch,
        input_output_aliases={first_earlier + n: n for n in range(len(earlier))},
        compiler_params=pltpu.CompilerParams(vmem_limit_bytes=60 * 2**20),
        cost_estimate=small_cost(),
        name=f"{name}_{k}",
    )(me, *parts, *whole, *(x for x, _ in tiled), *sources, *earlier)


def assemble_kernel(where, me, *refs):
    sources, whole, sems = refs[: len(where)], refs[len(where)], refs[len(where) + 1]
    copies = fetch(me, where, sources, whole, sems)
    for copy in copies:
        copy.start()
    for copy in copies:
        copy.wait()


def assemble(name, me, arrays, where, rows, cols):
    return pl.pallas_call(
        functools.partial(assemble_kernel, where),
        out_shape=jax.ShapeDtypeStruct((rows, cols), arrays[0].dtype),
        in_specs=[SMEM, *[ANY] * len(arrays)],
        out_specs=VMEM,
        scratch_shapes=[pltpu.SemaphoreType.DMA((len(arrays),))],
        compiler_params=pltpu.CompilerParams(vmem_limit_bytes=60 * 2**20),
        cost_estimate=small_cost(),
        name=name,
    )(me, *arrays)


def flip(x, axis):
    return lax.ppermute(x, axis, FLIP)


CROSS = [(1, 2), (2, 1)]
OUT = [(0, 1), (3, 2), (2, 0), (1, 3)]
BACK = [(1, 0), (2, 3), (0, 2), (3, 1)]


def crossed(x, perm):
    return lax.ppermute(x, ("core", "zh"), perm)


def straight():
    return lax.axis_index("core") == lax.axis_index("zh")


def swap(x):
    return jnp.where(straight(), x, crossed(x, CROSS))


def send_z(w):
    return crossed(w, OUT), crossed(w, CROSS)


def pair_of(w, out, cross):
    zh = lax.axis_index("zh")
    x = jnp.where(straight(), w, cross)
    return jnp.concatenate([jnp.where(zh == 0, x, out), jnp.where(zh == 0, out, x)], axis=0)


def give_z(part):
    zh = lax.axis_index("zh")
    half = part.shape[0] // 2
    upper, lower = part[:half], part[half:]
    return jnp.where(zh == 0, upper, lower), jnp.where(zh == 0, lower, upper)


def sum_z(keep, back, cross):
    return back.astype(jnp.float32) + jnp.where(straight(), keep, cross).astype(jnp.float32)


def shift(x, e, k):
    n = lax.axis_size("zl")
    return lax.ppermute(
        x, ("core", "zl"), [(c * n + l, (c ^ e) * n + (l + k) % n) for c in range(2) for l in range(n)]
    )


def from_near(x, k):
    n = lax.axis_size("zl")
    return lax.ppermute(x, "zl", [((j + k) % n, j) for j in range(n)])


def to_near(x, k):
    n = lax.axis_size("zl")
    return lax.ppermute(x, "zl", [(j, (j + k) % n) for j in range(n)])


def across(x, j):
    n = lax.axis_size("yx")
    return lax.ppermute(x, "yx", [(a, a ^ j) for a in range(n)])


def neighbours(x):
    count = lax.axis_size("yx")
    return [across(x, j) for j in range(1, count if count != 4 else 3)]


def diagonal(taken):
    if lax.axis_size("yx") != 4:
        return []
    half = taken[0].shape[0] // 2
    return [across(taken[1][:half], 1), across(taken[0][half:], 2)]


def blocks_of(own, taken, halves, column=0, source_column=0):
    deep = own.shape[0]
    arrays = [own, *taken, *halves]
    where = [(j, deep, 0, column, source_column) for j in range(1 + len(taken))]
    where += [(3, deep, n * deep // 2, column, source_column) for n in range(len(halves))]
    return arrays, tuple(where)


def whole_weight(w):
    return [w], ((0, 0, 0, 0, 0),)


def block_of(grad, j, columns):
    size = grad.shape[0] // lax.axis_size("yx")
    first = (lax.axis_index("yx") ^ j) * size
    return lax.dynamic_slice(grad, (first, columns[0]), (size, columns[1] - columns[0]))


def send_yx(grad, columns):
    count = lax.axis_size("yx")
    if count != 4:
        return [across(block_of(grad, j, columns), j) for j in range(1, count)]
    far = block_of(grad, 3, columns)
    half = far.shape[0] // 2
    return [across(far[:half], 1), across(far[half:], 2)]


def join_yx(grad, columns, taken):
    if lax.axis_size("yx") != 4:
        return taken, block_of(grad, 0, columns)
    half = taken[0].shape[0]
    one, two = block_of(grad, 1, columns), block_of(grad, 2, columns)
    one = jnp.concatenate([one[:half], one[half:] + taken[1]], axis=0)
    two = jnp.concatenate([two[:half] + taken[0], two[half:]], axis=0)
    return [across(one, 1), across(two, 2)], block_of(grad, 0, columns)


def total_yx(taken, own):
    total = own.astype(jnp.float32)
    for part in taken:
        total = total + part.astype(jnp.float32)
    return total.astype(jnp.bfloat16)


def body(
    tokens,
    cotangent,
    seq_lengths,
    attn_gain,
    q_weight,
    key_projection,
    value_projection,
    out_weight,
    mlp_gain,
    gate_weight,
    up_weight,
    down_weight,
):
    bf16, f32 = jnp.bfloat16, jnp.float32
    core, zl, yx = lax.axis_index("core"), lax.axis_index("zl"), lax.axis_index("yx")
    near = lax.axis_size("zl")
    others = range(1, near)
    rows = tokens.shape[0]
    group_rows = 2 * near * rows
    query_cols, key_cols = q_weight.shape[1], key_projection.shape[1]
    qkv_cols = query_cols + 2 * key_cols
    q_heads, kv_heads = query_cols // HD, key_cols // HD
    hidden_cols = gate_weight.shape[1]
    me = yx.astype(jnp.int32).reshape(1)

    qkv_shard = jnp.concatenate([q_weight, key_projection, value_projection], axis=1)
    gate_up_shard = jnp.concatenate([gate_weight, up_weight], axis=1)
    part_rows = rows // 2
    upper = swap(tokens[:part_rows])
    shard_moved = send_z(qkv_shard)
    lengths = swap(seq_lengths)
    gains = lax.all_gather(jnp.stack([attn_gain, mlp_gain]), ("yx", "core"), axis=1, tiled=True).astype(f32)
    upper, lengths, second_part, out_shard, gains, *shard_moved = stage(
        upper, lengths, tokens[part_rows:], out_weight, gains, *shard_moved
    )
    gain_one, gain_two = gains[0], gains[1]

    upper_far = [from_near(upper, k) for k in others]
    lower = swap(second_part)
    pair = pair_of(qkv_shard, *shard_moved)
    taken = neighbours(pair)
    out_out = crossed(out_shard, OUT)

    subs = jnp.arange(group_rows // SUB, dtype=jnp.int32)
    per_device = rows // SUB
    source, within = subs // per_device, subs % per_device
    there_core, there_zl = (source % 2) ^ core, (source // 2 + zl) % near
    to_order = (there_core * near + there_zl) * per_device + within
    from_order = (((source % near - zl) % near) * 2 + ((source // near) ^ core)) * per_device + within
    place = jnp.concatenate([to_order, from_order])
    row_at, doc_start = document_layout(lengths, group_rows)
    cosine, sine = rotary_tables(row_at - doc_start)

    def bounds(size):
        tile_start = doc_start.reshape(-1, size)
        tile = jnp.arange(group_rows // size, dtype=jnp.int32)
        low = tile_start[:, 0] // size
        return low, jnp.minimum((tile_start[:, -1] + size - 1) // size, tile)

    start_row = jnp.tile(doc_start.reshape(-1, 1, SUB), (1, 1, q_heads // kv_heads))
    layout = (place, *bounds(TILE), cosine, sine, doc_start[:, None])
    layout_back = (place, *bounds(SUB), cosine, sine, start_row)
    lower, out_out, out_shard, *moved = stage(lower, out_out, out_shard, *upper_far, *taken, *layout, *layout_back)
    upper_far, moved = moved[: near - 1], moved[near - 1 :]
    taken, moved = moved[: len(taken)], moved[len(taken) :]
    layout, layout_back = moved[: len(layout)], moved[len(layout) :]

    lower_far = [from_near(lower, k) for k in others]
    own = jnp.concatenate([upper, lower], axis=0)
    own_sib = flip(own, "core")
    out_cross = crossed(out_shard, CROSS)
    blocks = blocks_of(pair, taken, diagonal(taken))
    projecting = [(*blocks, qkv_cols)]
    gain_row = gain_one[None]
    outs = [(tokens.shape[1], bf16, "all"), (qkv_cols, bf16, "all")]
    normed = piece_call(project_kernel, "project", 0, near, me, [own, own_sib], [gain_row], [], projecting, [], outs)
    gate_up_shard, out_cross, down_shard, *moved = stage(gate_up_shard, out_cross, down_weight, *lower_far, *normed)
    lower_far, normed = moved[: near - 1], moved[near - 1 :]

    out_pair = pair_of(out_weight, out_out, out_cross)
    out_far = [from_near(out_pair, k) for k in others]
    down_moved = send_z(down_shard)
    for k in others:
        far = jnp.concatenate([upper_far[k - 1], lower_far[k - 1]], axis=0)
        parts = [far, flip(far, "core")]
        normed = piece_call(project_kernel, "project", k, near, me, parts, [gain_row], [], projecting, normed, outs)
    norm_one, qkv = normed
    gate_up_shard, qkv, out_pair, *moved = stage(gate_up_shard, qkv, out_pair, *out_far, *down_moved)
    out_far, down_moved = moved[: near - 1], moved[near - 1 :]

    gate_up_moved = send_z(gate_up_shard)
    w_out = lax.all_gather(jnp.concatenate([out_pair, *out_far], axis=1), "yx", axis=0, tiled=True)
    context, sums = attend(qkv, near, layout, q_heads, kv_heads)
    cotangent, *moved = stage(cotangent, *context, *gate_up_moved)
    context, gate_up_moved = moved[:near], moved[near:]

    quarters = [context[0]] + [None] * (near - 1)
    for k in others:
        quarters[near - k] = to_near(context[k], k)
    cot_upper = crossed(cotangent[:part_rows], CROSS)
    pairs = [
        pair_of(*(x[:, n * hidden_cols : (n + 1) * hidden_cols] for x in (gate_up_shard, *gate_up_moved)))
        for n in range(2)
    ]
    gate_taken = neighbours(pairs[0])
    residual = own.astype(f32)
    scale_one = lax.rsqrt(jnp.mean(residual * residual, axis=-1, keepdims=True) + EPSILON)
    up_pair, cotangent, cot_upper, w_out, scale_one, *moved = stage(
        pairs[1], cotangent, cot_upper, w_out, scale_one, *quarters, *gate_taken
    )
    quarters, gate_taken = moved[:near], moved[near:]

    up_taken = neighbours(up_pair)
    cot_lower = crossed(cotangent[part_rows:], CROSS)
    context_all = jnp.concatenate(quarters, axis=1)
    branch_sib = flip(times_transpose(context_all[rows:], w_out).astype(bf16), "core")
    mid = residual + times_transpose(context_all[:rows], w_out) + branch_sib.astype(f32)
    scale_two, norm_two = norm_rows(mid, gain_two)
    norm_two, cot_lower, *up_taken = stage(norm_two, cot_lower, *up_taken)

    upper_far = [from_near(norm_two[:part_rows], k) for k in others]
    gate_halves, up_halves = diagonal(gate_taken), diagonal(up_taken)
    cot = jnp.where(straight(), cotangent, jnp.concatenate([cot_upper, cot_lower], axis=0))
    down_pair = pair_of(down_weight, *down_moved)
    w_project = assemble("assemble_project", me, *blocks, tokens.shape[1], qkv_cols)
    norm_two, cot, down_pair, w_project, *moved = stage(
        norm_two, cot, down_pair, w_project, *upper_far, *gate_halves, *up_halves
    )
    upper_far, moved = moved[: near - 1], moved[near - 1 :]
    gate_halves, up_halves = moved[: len(gate_halves)], moved[len(gate_halves) :]

    lower_far = [from_near(norm_two[part_rows:], k) for k in others]
    norm_sib, cot_sib = flip(norm_two, "core"), flip(cot, "core")
    down_taken = neighbours(down_pair)
    gate_blocks = blocks_of(pairs[0], gate_taken, gate_halves)
    up_blocks = blocks_of(up_pair, up_taken, up_halves, hidden_cols)
    gate_up = ([*gate_blocks[0], *up_blocks[0]], gate_blocks[1] + up_blocks[1], 2 * hidden_cols)
    outs = [(norm_two.shape[1], bf16, "all"), (2 * hidden_cols, f32, "all"), (hidden_cols, bf16, "all")]
    earlier = piece_call(gate_kernel, "gate", 0, near, me, [norm_two, norm_sib], [], [], [gate_up], [], outs)
    cot_sib, *moved = stage(cot_sib, *lower_far, *down_taken, *earlier)
    lower_far, moved = moved[: near - 1], moved[near - 1 :]
    down_taken, earlier = moved[: len(down_taken)], moved[len(down_taken) :]

    norm_far = [jnp.concatenate(x, axis=0) for x in zip(upper_far, lower_far, strict=True)]
    norm_far_sib = [flip(x, "core") for x in norm_far]
    down_halves = diagonal(down_taken)
    cot, *moved = stage(cot, *norm_far, *norm_far_sib, *down_halves)
    norm_far, norm_far_sib, down_halves = moved[: near - 1], moved[near - 1 : 2 * near - 2], moved[2 * near - 2 :]

    cot_upper_far = [from_near(cot[:part_rows], k) for k in others]
    down = (*blocks_of(down_pair, down_taken, down_halves), hidden_cols)
    width = norm_two.shape[1]
    gate_outs, outs = outs, [(width, bf16, "all"), (2 * hidden_cols, bf16, "all")]
    halves = [(width, bf16, "own"), (width, bf16, "sibling")]

    def way_back(k, parts, earlier):
        tiled, results = [(gate_up_all, k), (hidden_all, k)], outs + halves * (1 if earlier else 2)
        return piece_call(gate_back_kernel, "gate_back", k, near, me, parts, [], tiled, [gate_up, down], earlier, results)

    def joined(own, sib):
        return own.astype(f32) + flip(sib, "core").astype(f32)

    norm_two_all, gate_up_all, hidden_all = earlier
    grad_all, d_gate_up_all, *near_back = way_back(0, [cot, cot_sib], [])
    cot, *moved = stage(
        cot, norm_two_all, gate_up_all, hidden_all, grad_all, d_gate_up_all, *near_back, *cot_upper_far
    )
    earlier, moved = moved[:3], moved[3:]
    grad_all, d_gate_up_all, *moved = moved
    near_back, cot_upper_far = moved[:4], moved[4:]

    cot_lower_far = [from_near(cot[part_rows:], k) for k in others]
    cot_upper_far_sib = [flip(x, "core") for x in cot_upper_far]
    out_far = []
    for k in others:
        parts = [norm_far[k - 1], norm_far_sib[k - 1]]
        *earlier, out_own, out_sib = piece_call(
            gate_kernel, "gate", k, near, me, parts, [], [], [gate_up, down], earlier, gate_outs + halves
        )
        out_far += [out_own, out_sib]
    grad_all, d_gate_up_all, *moved = stage(
        grad_all, d_gate_up_all, *near_back, *cot_lower_far, *cot_upper_far_sib, *earlier, *out_far
    )
    near_back, cot_lower_far, moved = moved[:4], moved[4 : near + 3], moved[near + 3 :]
    cot_upper_far_sib, earlier, out_far = moved[: near - 1], moved[near - 1 : near + 2], moved[near + 2 :]
    norm_two_all, gate_up_all, hidden_all = earlier
    cot_lower_far_sib = [flip(x, "core") for x in cot_lower_far]
    out_sums = [joined(*out_far[2 * n : 2 * n + 2]).astype(bf16) for n in range(near - 1)]
    moved = stage(*cot_lower_far_sib, *out_sums)
    cot_lower_far_sib, out_sums = moved[: near - 1], moved[near - 1 :]

    out_upper = [to_near(out_sums[k - 1][:part_rows], k) for k in others]
    back = []
    for k in others:
        parts = [cot_upper_far[k - 1], cot_lower_far[k - 1], cot_upper_far_sib[k - 1], cot_lower_far_sib[k - 1]]
        grad_all, d_gate_up_all, *more = way_back(k, parts, [grad_all, d_gate_up_all])
        back.append(more)
    grad_all, d_gate_up_all, *moved = stage(grad_all, d_gate_up_all, *(x for more in back for x in more), *out_upper)
    far_back, out_upper = moved[: 2 * near - 2], moved[2 * near - 2 :]
    d_norm_sent = [joined(*far_back[2 * n : 2 * n + 2]).astype(bf16) for n in range(near - 1)]
    grad_all, d_gate_up_all, near_own, near_sib, *d_norm_sent = stage(
        grad_all, d_gate_up_all, *near_back[:2], *d_norm_sent
    )

    moved_upper = [to_near(d_norm_sent[k - 1][:part_rows], k) for k in others]
    grad_gate, grad_up = (
        rows_product(norm_two_all, d_gate_up_all[:, n * hidden_cols : (n + 1) * hidden_cols]).astype(bf16)
        for n in range(2)
    )
    output_near = joined(*near_back[2:])
    grad_gate, grad_up, grad_all, near_own, near_sib, output_near, *moved = stage(
        grad_gate, grad_up, grad_all, near_own, near_sib, output_near, *moved_upper, *d_norm_sent
    )
    moved_upper, d_norm_sent = moved[: near - 1], moved[near - 1 :]

    moved_lower = [to_near(d_norm_sent[k - 1][part_rows:], k) for k in others]
    gate_part = lax.psum_scatter(grad_gate, "yx", scatter_dimension=0, tiled=True)
    d_norm_two = joined(near_own, near_sib)
    grad_down = rows_product(grad_all, hidden_all).astype(bf16)

    def output_part(at, moved):
        part = mid[at] + output_near[at]
        for x in moved:
            part = part + x.astype(f32)
        return part.astype(bf16)

    output_upper = output_part(slice(0, part_rows), out_upper)
    grad_down, d_norm_two, output_upper, *moved = stage(grad_down, d_norm_two, output_upper, *out_sums, *moved_lower)
    out_sums, moved_lower = moved[: near - 1], moved[near - 1 :]

    quarter = part_rows // 2
    out_lower = [[to_near(out_sums[k - 1][part_rows : part_rows + quarter], k) for k in others]]
    up_part = lax.psum_scatter(grad_up, "yx", scatter_dimension=0, tiled=True)
    for one, two in zip(moved_upper, moved_lower, strict=True):
        d_norm_two = d_norm_two + jnp.concatenate([one, two], axis=0).astype(f32)
    mid_back, _ = norm_back(mid, scale_two, gain_two, d_norm_two)
    d_mid = cot.astype(f32) + mid_back
    d_attn = d_mid.astype(bf16)
    d_attn, *moved = stage(d_attn, *out_lower[0], *out_sums)
    out_lower[0], out_sums = moved[: near - 1], moved[near - 1 :]

    out_lower.append([to_near(out_sums[k - 1][part_rows + quarter :], k) for k in others])
    d_attn_sib = flip(d_attn, "core")
    both = [dot32(x, w_out).astype(bf16) for x in (d_attn, d_attn_sib)]
    d_quarters = [
        jnp.concatenate([x[:, k * query_cols : (k + 1) * query_cols] for x in both], axis=0) for k in range(near)
    ]
    d_attn, d_attn_sib, *moved = stage(d_attn, d_attn_sib, *d_quarters, *out_lower[1])
    d_quarters, out_lower[1] = moved[:near], moved[near:]

    d_context = [d_quarters[0]] + [None] * (near - 1)
    for k in others:
        d_context[near - k] = to_near(d_quarters[k], k)
    upper_crossed = crossed(output_upper, CROSS)
    grad_out = rows_product(d_attn, context_all[:rows]) + rows_product(d_attn_sib, context_all[rows:])
    grad_out = grad_out.astype(bf16)
    output_lower = output_part(
        slice(part_rows, rows), [jnp.concatenate(x, axis=0) for x in zip(*out_lower, strict=True)]
    )
    grad_out, output_lower, gate_part, upper_crossed, *d_context = stage(
        grad_out, output_lower, gate_part, upper_crossed, *d_context
    )

    lower_crossed = crossed(output_lower, CROSS)
    output = jnp.concatenate([output_upper, output_lower], axis=0)
    gate_keep, gate_give = give_z(gate_part)
    gate_home = [crossed(gate_give, BACK), crossed(gate_keep, CROSS)]
    down_part = lax.psum_scatter(grad_down, "yx", scatter_dimension=0, tiled=True)
    out_part = lax.psum_scatter(grad_out, "yx", scatter_dimension=0, tiled=True)
    d_qkv = attend_back(list(range(kv_heads)), qkv, d_context, context, sums, [], layout_back, q_heads, kv_heads)
    d_qkv, lower_crossed, up_part, *gate_home = stage(d_qkv, lower_crossed, up_part, *gate_home)
    output = jnp.where(straight(), output, jnp.concatenate([upper_crossed, lower_crossed], axis=0))

    def back_part(k):
        own, sib = (d_qkv[(2 * k + e) * rows : (2 * k + e + 1) * rows] for e in range(2))
        taken = flip(times_transpose(sib, w_project).astype(bf16), "core")
        return times_transpose(own, w_project) + taken.astype(f32)

    up_keep, up_give = give_z(up_part)
    up_home = [crossed(up_give, BACK), crossed(up_keep, CROSS)]
    d_sent = [back_part(k).astype(bf16) for k in others]
    d_qkv, *moved = stage(d_qkv, *d_sent, *up_home)
    d_sent, up_home = moved[: near - 1], moved[near - 1 :]

    d_upper = [to_near(d_sent[k - 1][:part_rows], k) for k in others]
    grad_project = rows_product(norm_one, d_qkv).astype(bf16)
    project_sent = send_yx(grad_project, (0, qkv_cols))
    total = back_part(0)
    total, grad_project, down_part, *moved = stage(total, grad_project, down_part, *d_upper, *d_sent, *project_sent)
    d_upper, d_sent, project_sent = moved[: near - 1], moved[near - 1 : 2 * near - 2], moved[2 * near - 2 :]

    d_lower = [to_near(d_sent[k - 1][part_rows:], k) for k in others]
    project_rest, project_own = join_yx(grad_project, (0, qkv_cols), project_sent)
    down_keep, down_give = give_z(down_part)
    down_back = crossed(down_give, BACK)

    def input_part(at, moved):
        part = total[at]
        for x in moved:
            part = part + x.astype(f32)
        back, _ = norm_back(residual[at], scale_one[at], gain_one, part)
        return (d_mid[at] + back).astype(bf16)

    input_upper = input_part(slice(0, part_rows), d_upper)
    upper_crossed = crossed(input_upper, CROSS)
    total, input_upper, upper_crossed, out_part, down_back, down_keep, *moved = stage(
        total, input_upper, upper_crossed, out_part, down_back, down_keep, *d_lower, *project_rest
    )
    d_lower, project_rest = moved[: near - 1], moved[near - 1 :]
    down_cross = crossed(down_keep, CROSS)

    project_keep, project_give = give_z(total_yx(project_rest, project_own))
    project_home = [crossed(project_give, BACK), crossed(project_keep, CROSS)]
    input_lower = input_part(slice(part_rows, rows), d_lower)
    lower_crossed = crossed(input_lower, CROSS)
    out_moved = [to_near(out_part[:, k * query_cols : (k + 1) * query_cols], k) for k in others]
    out_quarter = out_part[:, :query_cols].astype(f32)
    for part in out_moved:
        out_quarter = out_quarter + part.astype(f32)
    out_keep, out_give = give_z(out_quarter.astype(bf16))
    out_home = [crossed(out_give, BACK), crossed(out_keep, CROSS)]
    grad_project = sum_z(project_keep, *project_home)
    grad_out = sum_z(out_keep, *out_home)
    grad_down = sum_z(down_keep, down_back, down_cross)
    grad_gate, grad_up = sum_z(gate_keep, *gate_home), sum_z(up_keep, *up_home)
    input_grad = jnp.concatenate(
        [
            jnp.where(straight(), input_upper, upper_crossed),
            jnp.where(straight(), input_lower, lower_crossed),
        ],
        axis=0,
    ).astype(f32)
    gain_grads = lax.psum(
        jnp.stack(
            [
                jnp.sum(qkv_shard.astype(f32) * grad_project, axis=1),
                jnp.sum(gate_weight.astype(f32) * grad_gate + up_weight.astype(f32) * grad_up, axis=1),
            ]
        ),
        ("zh", "zl"),
    ) / jnp.stack([attn_gain, mlp_gain]).astype(f32)
    return (
        output,
        input_grad,
        gain_grads[0],
        grad_project[:, :query_cols],
        grad_project[:, query_cols : query_cols + key_cols],
        grad_project[:, query_cols + key_cols :],
        grad_out,
        gain_grads[1],
        grad_gate,
        grad_up,
        grad_down,
    )


def solution(mesh):
    dp, tensor = mesh.shape["dp"], mesh.shape["tensor"]
    fine = Mesh(mesh.devices.reshape(dp // 2, 2, 2, tensor // 2), AXES)
    by_rows, by_dp, by_both = P(AXES, None), P(("yx", "core")), P(("yx", "core"), ("zh", "zl"))
    return jax.shard_map(
        body,
        mesh=fine,
        in_specs=(
            by_rows, by_rows, P(("yx", "core"), None), by_dp, by_both, by_both, by_both, by_both,
            by_dp, by_both, by_both, by_both,
        ),
        out_specs=(
            by_rows, by_rows, by_dp, by_both, by_both, by_both, by_both, by_dp, by_both, by_both, by_both,
        ),
        check_vma=False,
    )
```

```python
import functools
import math

import jax
import jax.numpy as jnp
import numpy as np
from jax import lax
from jax.experimental import pallas as pl
from jax.experimental.pallas import tpu as pltpu
from jax.sharding import Mesh
from jax.sharding import PartitionSpec as P

HD = 96
HALF = HD // 2
PAD = 128
STEPS = 4
SUB = 256
TILE = 512

EPSILON = 1e-05
ROTARY_BASE = 100000.0
MASKED = -1e30
LOG2E = math.log2(math.e)

AXES = ("yx", "core", "zh", "zl")
FLIP = [(0, 1), (1, 0)]


def norm_rows(values, gain):
    row_scale = lax.rsqrt(jnp.mean(values * values, axis=-1, keepdims=True) + EPSILON)
    return (row_scale, (values * row_scale * gain).astype(jnp.bfloat16))


def norm_back(values, row_scale, gain, upstream):
    weighted = upstream * gain
    inner_sum = jnp.mean(weighted * values, axis=-1, keepdims=True)
    grad_in = row_scale * weighted - values * (row_scale * row_scale * row_scale) * inner_sum
    gain_part = jnp.sum(upstream * (values * row_scale), axis=0)
    return (grad_in, gain_part)


def document_layout(lengths, group_rows):
    flat_lengths = lengths.reshape(-1)
    doc_ends = jnp.cumsum(flat_lengths)
    rows = jnp.arange(group_rows, dtype=jnp.int32)
    passed = (rows[:, None] >= doc_ends[None, :]).astype(jnp.int32)
    return (rows, jnp.sum(passed * flat_lengths[None, :], axis=1))


def rotary_tables(positions):
    exponents = jnp.arange(HALF, dtype=jnp.float32) * (2.0 / HD)
    inverse = ROTARY_BASE ** (-exponents)
    angles = positions.astype(jnp.float32)[:, None] * inverse[None, :]
    cosine, sine = jnp.cos(angles), jnp.sin(angles)
    gap = jnp.zeros((positions.shape[0], PAD // 2 - HALF), jnp.float32)
    return (
        jnp.concatenate([cosine, gap, cosine, gap], axis=1),
        jnp.concatenate([-sine, gap, sine, gap], axis=1),
    )


def rows_product(left, right):
    return lax.dot_general(
        left, right, (((0,), (0,)), ((), ())), preferred_element_type=jnp.float32
    )


def times_transpose(left, right):
    return lax.dot_general(
        left, right, (((1,), (1,)), ((), ())), preferred_element_type=jnp.float32
    )


def dot32(left, right):
    return jnp.dot(left, right, preferred_element_type=jnp.float32)


def stage(*values):
    return lax.optimization_barrier(values)


def spread(columns, heads):
    matrix = np.zeros((columns, len(heads) * PAD), np.float32)
    for at, first in enumerate(heads):
        for half in range(2):
            for i in range(HALF):
                matrix[first + half * HALF + i, at * PAD + half * (PAD // 2) + i] = 1.0
    return matrix


def turn(x, cosine, sine):
    return x * cosine + pltpu.roll(x, PAD // 2, 1) * sine


def rows_at(t, size):
    return pl.ds(pl.multiple_of(t * size, size), size)


def forward_kernel(pieces, ratio, *refs):
    place, low, full, cosine, sine, start, spread_in, gather_out = refs[:8]
    heads = spread_in.shape[0]
    refs = refs[8:]
    qkv, context, refs = refs[0], refs[1 : 1 + pieces], refs[1 + pieces :]
    log_sum, refs = refs[:heads], refs[heads:]
    q_s, k_s, v_s, s_s, top_s, acc = refs
    tiles = q_s.shape[0]
    all_subs = qkv.shape[0] // SUB
    piece_subs = all_subs // pieces
    scale = LOG2E * HD ** (-0.5)
    ones_lane = lax.broadcasted_iota(jnp.int32, (SUB, PAD), 1) == PAD - 1

    def prepare(r, carry):
        t = place[r]
        at = rows_at(t, SUB)
        cos_t, sin_t = cosine[at, :], sine[at, :]
        tile, half = t // (TILE // SUB), t % (TILE // SUB)
        for g in range(heads):
            wide = dot32(qkv[rows_at(r, SUB), :], spread_in[g])
            for h in range(ratio):
                query = turn(wide[:, h * PAD : (h + 1) * PAD], cos_t, sin_t) * scale
                first = pl.multiple_of(h * TILE + half * SUB, SUB)
                q_s[tile, g, pl.ds(first, SUB), :] = query.astype(jnp.bfloat16)
            key = turn(wide[:, ratio * PAD : (ratio + 1) * PAD], cos_t, sin_t)
            k_s[g, at, :] = key.astype(jnp.bfloat16)
            value = jnp.where(ones_lane, 1.0, wide[:, (ratio + 1) * PAD :])
            v_s[g, at, :] = value.astype(jnp.bfloat16)
        return carry

    lax.fori_loop(0, all_subs, prepare, 0)

    def query_tile(i, carry):
        starts = jnp.concatenate([start[rows_at(i, TILE), :]] * ratio, axis=0)
        top_s[...] = jnp.full_like(top_s, MASKED)

        def scores(j, masked, diagonal):
            for g in range(heads):
                s = times_transpose(q_s[i, g], k_s[g, rows_at(j, TILE), :])
                if masked:
                    key_at = lax.broadcasted_iota(jnp.int32, s.shape, 1)
                    allowed = key_at + j * TILE >= starts
                    if diagonal:
                        query_at = lax.rem(lax.broadcasted_iota(jnp.int32, s.shape, 0), TILE)
                        allowed = allowed & (key_at <= query_at)
                    s = jnp.where(allowed, s, MASKED)
                s_s[g, j] = s
                peak = s[:, :PAD]
                for c in range(1, TILE // PAD):
                    peak = jnp.maximum(peak, s[:, c * PAD : (c + 1) * PAD])
                top_s[g] = jnp.maximum(top_s[g], peak)

        def loop(first, last, masked):
            def run(j, c):
                scores(j, masked, False)
                return c

            lax.fori_loop(first, last, run, 0)

        loop(low[i], full[i], True)
        loop(full[i], i, False)
        scores(i, True, True)
        tops = [jnp.max(top_s[g], axis=1, keepdims=True) for g in range(heads)]
        acc[...] = jnp.zeros_like(acc)

        def weigh(j, c):
            for g in range(heads):
                p = jnp.exp2(s_s[g, j] - tops[g]).astype(jnp.bfloat16)
                acc[g] += dot32(p, v_s[g, rows_at(j, TILE), :])
            return c

        lax.fori_loop(low[i], i + 1, weigh, 0)
        packed = None
        for g in range(heads):
            total = acc[g][:, PAD - 1 :]
            out = acc[g] * (1.0 / total)
            sums = jnp.broadcast_to(tops[g] + jnp.log(total) * LOG2E, (ratio * TILE, PAD))
            log_sum[g][i] = sums.T[:1, :]
            wide = jnp.concatenate(
                [out[h * TILE : (h + 1) * TILE, :] for h in range(ratio)], axis=1
            ).astype(jnp.bfloat16)
            part = dot32(wide, gather_out[g])
            packed = part if packed is None else packed + part
        subs = tiles * (TILE // SUB)
        for half in range(TILE // SUB):
            r = place[subs + i * (TILE // SUB) + half]
            part = packed[half * SUB : (half + 1) * SUB, :].astype(jnp.bfloat16)
            for k in range(pieces):

                @pl.when(r // piece_subs == k)
                def store(k=k, part=part, r=r):
                    context[k][rows_at(r % piece_subs, SUB), :] = part

        return carry

    lax.fori_loop(0, tiles, query_tile, 0)


def backward_kernel(pieces, ratio, more, *refs):
    place, low, full, cosine, sine, start, refs = *refs[:6], refs[6:]
    heads = refs[0].shape[0]
    spread_in, spread_out, gather_in, refs = *refs[:3], refs[3:]
    log_sum, refs = refs[:heads], refs[heads:]
    d_context, context, qkv, refs = refs[:pieces], refs[pieces : 2 * pieces], refs[2 * pieces], refs[2 * pieces + 1 :]
    earlier, refs = (refs[0], refs[1:]) if more else (None, refs)
    d_qkv, refs = refs[0], refs[1:]
    q_s, k_s, kt_s, v_s, do_s, delta_s, log_s, dq_acc, dk_acc, dv_acc, dq_s = refs
    tiles = q_s.shape[0]
    all_subs = qkv.shape[0] // SUB
    piece_subs = all_subs // pieces
    scale = HD ** (-0.5)
    per_tile = TILE // SUB

    for k in range(pieces):

        def prepare(r, carry, k=k):
            t = place[k * piece_subs + r]
            rel = rows_at(r, SUB)
            at = rows_at(t, SUB)
            cos_t, sin_t = cosine[at, :], sine[at, :]
            for g in range(heads):
                wide = dot32(qkv[rows_at(k * piece_subs + r, SUB), :], spread_in[g])
                d_out = dot32(d_context[k][rel, :], spread_out[g])
                out = dot32(context[k][rel, :], spread_out[g])
                for h in range(ratio):
                    cols = slice(h * PAD, (h + 1) * PAD)
                    rows = slice(h * SUB, (h + 1) * SUB)
                    query = turn(wide[:, cols], cos_t, sin_t) * (scale * LOG2E)
                    q_s[t, g, rows, :] = query.astype(jnp.bfloat16)
                    do_s[t, g, rows, :] = d_out[:, cols].astype(jnp.bfloat16)
                    delta = jnp.sum((d_out[:, cols] * out[:, cols]).T, axis=0, keepdims=True)
                    delta_s[t * heads + g, :, rows] = delta
                    first = pl.multiple_of(h * TILE + t % per_tile * SUB, SUB)
                    log_s[t * heads + g, :, rows] = log_sum[g][t // per_tile, :, pl.ds(first, SUB)]
                key = turn(wide[:, ratio * PAD : (ratio + 1) * PAD], cos_t, sin_t)
                k_s[g, t] = key.astype(jnp.bfloat16)
                kt_s[g, t] = key.T.astype(jnp.bfloat16)
                v_s[g, t] = wide[:, (ratio + 1) * PAD :].astype(jnp.bfloat16)
                dk_acc[g, t] = jnp.zeros((SUB, PAD), jnp.float32)
                dv_acc[g, t] = jnp.zeros((SUB, PAD), jnp.float32)
            return carry

        lax.fori_loop(0, piece_subs, prepare, 0)

    def query_tile(i, carry):
        dq_acc[...] = jnp.zeros_like(dq_acc)

        def step(j, masked, diagonal):
            for g in range(heads):
                queries, d_out = q_s[i, g], do_s[i, g]
                s = times_transpose(k_s[g, j], queries)
                if masked:
                    key_at = lax.broadcasted_iota(jnp.int32, s.shape, 0)
                    allowed = key_at + j * SUB >= start[i]
                    if diagonal:
                        query_at = lax.rem(lax.broadcasted_iota(jnp.int32, s.shape, 1), SUB)
                        allowed = allowed & (key_at <= query_at)
                    s = jnp.where(allowed, s, MASKED)
                p = jnp.exp2(s - log_s[i * heads + g])
                d_p = times_transpose(v_s[g, j], d_out)
                d_s = (p * (d_p - delta_s[i * heads + g])).astype(jnp.bfloat16)
                dv_acc[g, j] += dot32(p.astype(jnp.bfloat16), d_out)
                dk_acc[g, j] += dot32(d_s, queries)
                dq_acc[g] += dot32(kt_s[g, j], d_s)

        def loop(first, last, masked):
            def run(j, c):
                step(j, masked, False)
                return c

            lax.fori_loop(first, last, run, 0)

        loop(low[i], full[i], True)
        loop(full[i], i, False)
        step(i, True, True)
        at = rows_at(i, SUB)
        cos_t, sin_t = cosine[at, :], sine[at, :]
        for g in range(heads):
            grad = dq_acc[g].T * scale
            for h in range(ratio):
                piece = turn(grad[h * SUB : (h + 1) * SUB, :], cos_t, -sin_t)
                dq_s[g, i, :, h * PAD : (h + 1) * PAD] = piece.astype(jnp.bfloat16)
        return carry

    lax.fori_loop(0, tiles, query_tile, 0)

    def finish(r, carry):
        t = place[r]
        at = rows_at(t, SUB)
        rel = rows_at(r, SUB)
        packed = None
        for g in range(heads):
            key = turn(dk_acc[g, t] * (1.0 / LOG2E), cosine[at, :], -sine[at, :])
            wide = jnp.concatenate(
                [dq_s[g, t], key.astype(jnp.bfloat16), dv_acc[g, t].astype(jnp.bfloat16)], axis=1
            )
            part = dot32(wide, gather_in[g])
            packed = part if packed is None else packed + part
        packed = packed.astype(jnp.bfloat16)
        d_qkv[rel, :] = packed + earlier[rel, :] if more else packed
        return carry

    lax.fori_loop(0, all_subs, finish, 0)


SMEM = pl.BlockSpec(memory_space=pltpu.SMEM)
VMEM = pl.BlockSpec(memory_space=pltpu.VMEM)
ANY = pl.BlockSpec(memory_space=pl.ANY)


def small_cost(transcendentals=0):
    return pl.CostEstimate(flops=1 << 20, bytes_accessed=1 << 16, transcendentals=transcendentals)


def head_matrices(head, q_heads, kv_heads):
    ratio = q_heads // kv_heads
    queries = [(head * ratio + r) * HD for r in range(ratio)]
    key, value = (q_heads + head) * HD, (q_heads + kv_heads + head) * HD
    inner = spread((q_heads + 2 * kv_heads) * HD, [*queries, key, value])
    outer = spread(q_heads * HD, queries)
    return jnp.asarray(inner, jnp.bfloat16), jnp.asarray(outer, jnp.bfloat16)


def stacked_matrices(q_heads, kv_heads):
    pairs = [head_matrices(head, q_heads, kv_heads) for head in range(kv_heads)]
    return jnp.stack([inner for inner, _ in pairs]), jnp.stack([outer for _, outer in pairs])


def attend(qkv, pieces, layout, q_heads, kv_heads):
    place, low, full, cosine, sine, start_column = layout
    ratio, rows = q_heads // kv_heads, qkv.shape[0]
    tiles, lanes = rows // TILE, ratio * TILE
    bf16, f32 = jnp.bfloat16, jnp.float32
    inner, outer = stacked_matrices(q_heads, kv_heads)
    outs = pl.pallas_call(
        functools.partial(forward_kernel, pieces, ratio),
        out_shape=[
            *[jax.ShapeDtypeStruct((rows // pieces, q_heads * HD), bf16)] * pieces,
            *[jax.ShapeDtypeStruct((tiles, 1, lanes), f32)] * kv_heads,
        ],
        in_specs=[SMEM] * 3 + [VMEM] * 6,
        out_specs=[VMEM] * (pieces + kv_heads),
        scratch_shapes=[
            pltpu.VMEM((tiles, kv_heads, lanes, PAD), bf16),
            pltpu.VMEM((kv_heads, rows, PAD), bf16),
            pltpu.VMEM((kv_heads, rows, PAD), bf16),
            pltpu.VMEM((kv_heads, tiles, lanes, TILE), f32),
            pltpu.VMEM((kv_heads, lanes, PAD), f32),
            pltpu.VMEM((kv_heads, lanes, PAD), f32),
        ],
        compiler_params=pltpu.CompilerParams(vmem_limit_bytes=60 * 2**20),
        cost_estimate=small_cost(),
        name="attention_forward",
    )(place, low, full, cosine, sine, start_column, inner, jnp.swapaxes(outer, 1, 2), qkv)
    return outs[:pieces], outs[pieces:]


def attend_back(heads, qkv, d_context, context, sums, earlier, layout, q_heads, kv_heads):
    place, low, full, cosine, sine, start_row = layout
    pieces, ratio, rows = len(context), q_heads // kv_heads, qkv.shape[0]
    tiles, lanes, count = rows // SUB, ratio * SUB, len(heads)
    bf16, f32 = jnp.bfloat16, jnp.float32
    inner, outer = stacked_matrices(q_heads, kv_heads)
    inner, outer = inner[heads[0] : heads[0] + count], outer[heads[0] : heads[0] + count]
    return pl.pallas_call(
        functools.partial(backward_kernel, pieces, ratio, bool(earlier)),
        out_shape=jax.ShapeDtypeStruct(qkv.shape, bf16),
        in_specs=[SMEM] * 3 + [VMEM] * (7 + count + 2 * pieces + len(earlier)),
        out_specs=VMEM,
        scratch_shapes=[
            pltpu.VMEM((tiles, count, lanes, PAD), bf16),
            pltpu.VMEM((count, tiles, SUB, PAD), bf16),
            pltpu.VMEM((count, tiles, PAD, SUB), bf16),
            pltpu.VMEM((count, tiles, SUB, PAD), bf16),
            pltpu.VMEM((tiles, count, lanes, PAD), bf16),
            pltpu.VMEM((tiles * count, 1, lanes), f32),
            pltpu.VMEM((tiles * count, 1, lanes), f32),
            pltpu.VMEM((count, PAD, lanes), f32),
            pltpu.VMEM((count, tiles, SUB, PAD), f32),
            pltpu.VMEM((count, tiles, SUB, PAD), f32),
            pltpu.VMEM((count, tiles, SUB, ratio * PAD), bf16),
        ],
        compiler_params=pltpu.CompilerParams(vmem_limit_bytes=60 * 2**20),
        cost_estimate=small_cost(),
        name=f"attention_backward_{heads[0]}",
    )(
        place, low, full, cosine, sine, start_row, inner, outer, jnp.swapaxes(inner, 1, 2),
        *[sums[h] for h in heads], *d_context, *context, qkv, *earlier,
    )


def fetch(me, where, sources, target, sems):
    copies = []
    for n, (source, (j, deep, first, column, taken)) in enumerate(zip(sources, where, strict=True)):
        cols = min(source.shape[1] - taken, target.shape[1] - column)
        at = pl.ds(pl.multiple_of((me[0] ^ j) * deep + first, 16), source.shape[0])
        if cols != source.shape[1]:
            source = source.at[:, taken : taken + cols]
        copies.append(pltpu.make_async_copy(source, target.at[at, column : column + cols], sems.at[n]))
    return copies


def take_rows(parts, target):
    rows = target.shape[0]
    for step in range(STEPS):

        @pl.when(pl.program_id(0) == step)
        def take(step=step):
            at = 0
            for part in parts:
                first, last = max(at, step * rows), min(at + part.shape[0], (step + 1) * rows)
                if first < last:
                    target[first - step * rows : last - step * rows, :] = part[first - at : last - at, :]
                at += part.shape[0]


def at_first_step(copies, what):
    @pl.when(pl.program_id(0) == 0)
    def run():
        for copy in copies:
            what(copy)


def project_kernel(count, where, more, me, *refs):
    parts, gain, refs = refs[:count], refs[count], refs[count + 1 :]
    sources, refs = refs[: len(where[0])], refs[len(where[0]) :]
    norm_all, qkv_all, weight, sems, rows_s = refs[2 if more else 0 :]
    copies = fetch(me, where[0], sources, weight, sems)
    at_first_step(copies, lambda copy: copy.start())
    take_rows(parts, rows_s)
    x = rows_s[...].astype(jnp.float32)
    scale = lax.rsqrt(jnp.mean(x * x, axis=-1, keepdims=True) + EPSILON)
    norm_all[...] = (x * scale * gain[...]).astype(jnp.bfloat16)
    at_first_step(copies, lambda copy: copy.wait())
    qkv_all[...] = dot32(norm_all[...], weight[...]).astype(jnp.bfloat16)


def by_half(refs, value):
    for n, ref in enumerate(refs):

        @pl.when(pl.program_id(0) * 2 // STEPS == n)
        def store(ref=ref):
            ref[...] = value


def gate_kernel(count, where, more, me, *refs):
    parts, refs = refs[:count], refs[count:]
    with_out = len(where) > 1
    sources, refs = refs[: sum(map(len, where))], refs[sum(map(len, where)) :]
    norm_all, gate_up_all, hidden_all, *refs = refs[3 if more else 0 :]
    out_refs, refs = (refs[:2], refs[2:]) if with_out else ((), refs)
    weight, sems, *refs = refs
    hidden_cols = hidden_all.shape[1]
    copies = fetch(me, where[0], sources[: len(where[0])], weight, sems)
    if with_out:
        w_down, down_sems = refs
        copies += fetch(me, where[1], sources[len(where[0]) :], w_down, down_sems)
    at_first_step(copies, lambda copy: copy.start())
    take_rows(parts, norm_all)
    at_first_step(copies, lambda copy: copy.wait())
    x = norm_all[...]
    width = min(512, hidden_cols)
    for at in range(0, hidden_cols, width):
        gate_at = slice(at, at + width)
        up_at = slice(hidden_cols + at, hidden_cols + at + width)
        gate = dot32(x, weight[:, gate_at])
        up = dot32(x, weight[:, up_at])
        gate_up_all[:, gate_at] = gate
        gate_up_all[:, up_at] = up
        hidden_all[:, gate_at] = (gate * (1.0 / (1.0 + jnp.exp(-gate))) * up).astype(jnp.bfloat16)
    if with_out:
        by_half(out_refs, times_transpose(hidden_all[...], w_down[...]).astype(jnp.bfloat16))


def gate_back_kernel(count, where, more, me, *refs):
    parts, gate_up_all, hidden_here, refs = refs[:count], *refs[count : count + 2], refs[count + 2 :]
    gate_up, refs = refs[: len(where[0])], refs[len(where[0]) :]
    down, refs = refs[: len(where[1])], refs[len(where[1]) :]
    grad_all, d_gate_up_all, *refs = refs[2 if more else 0 :]
    d_norm_refs, refs = refs[:2], refs[2:]
    out_refs, refs = ((), refs) if more else (refs[:2], refs[2:])
    w_gate_up, gate_up_sems, w_down, down_sems = refs
    hidden_cols = w_down.shape[1]
    down_copies = fetch(me, where[1], down, w_down, down_sems)
    copies = fetch(me, where[0], gate_up, w_gate_up, gate_up_sems)
    at_first_step(down_copies + copies, lambda copy: copy.start())
    take_rows(parts, grad_all)
    at_first_step(down_copies, lambda copy: copy.wait())
    dy = grad_all[...]
    width = min(512, hidden_cols)
    for at in range(0, hidden_cols, width):
        gate_at = slice(at, at + width)
        up_at = slice(hidden_cols + at, hidden_cols + at + width)
        d_hidden = dot32(dy, w_down[:, gate_at])
        gate, up = gate_up_all[:, gate_at], gate_up_all[:, up_at]
        sigmoid = 1.0 / (1.0 + jnp.exp(-gate))
        d_gate = d_hidden * up * sigmoid * (1.0 + gate * (1.0 - sigmoid))
        d_gate_up_all[:, gate_at] = d_gate.astype(jnp.bfloat16)
        d_gate_up_all[:, up_at] = (d_hidden * (gate * sigmoid)).astype(jnp.bfloat16)
    if not more:
        by_half(out_refs, times_transpose(hidden_here[...], w_down[...]).astype(jnp.bfloat16))
    at_first_step(copies, lambda copy: copy.wait())
    by_half(d_norm_refs, times_transpose(d_gate_up_all[...], w_gate_up[...]).astype(jnp.bfloat16))


def piece_call(kernel, name, k, pieces, me, parts, whole, tiled, fetched, earlier, outs):
    tile, width = sum(x.shape[0] for x in parts) // STEPS, parts[0].shape[1]
    count = len(parts)

    def rows_of(piece):
        return lambda i: (piece * STEPS + i, 0)

    def half_of(span):
        first = 0 if span == "own" else STEPS // 2
        return lambda i: (jnp.clip(i - first, 0, STEPS // 2 - 1), 0)

    sources = [x for arrays, _, _ in fetched for x in arrays]
    first_earlier = 1 + count + len(whole) + len(tiled) + len(sources)
    scratch = []
    for arrays, _, cols in fetched:
        scratch += [pltpu.VMEM((width, cols), jnp.bfloat16), pltpu.SemaphoreType.DMA((len(arrays),))]
    if kernel is project_kernel:
        scratch.append(pltpu.VMEM((tile, width), jnp.bfloat16))
    return pl.pallas_call(
        functools.partial(kernel, count, tuple(where for _, where, _ in fetched), bool(earlier)),
        grid=(STEPS,),
        out_shape=[
            jax.ShapeDtypeStruct(((pieces * STEPS if span == "all" else STEPS // 2) * tile, columns), kind)
            for columns, kind, span in outs
        ],
        in_specs=[
            SMEM,
            *(pl.BlockSpec(x.shape, lambda i: (0, 0)) for x in parts),
            *(pl.BlockSpec(x.shape, lambda i: (0, 0)) for x in whole),
            *(pl.BlockSpec((tile, x.shape[1]), rows_of(piece)) for x, piece in tiled),
            *[ANY] * (len(sources) + len(earlier)),
        ],
        out_specs=[
            pl.BlockSpec((tile, columns), rows_of(k) if span == "all" else half_of(span))
            for columns, kind, span in outs
        ],
        scratch_shapes=scratch,
        input_output_aliases={first_earlier + n: n for n in range(len(earlier))},
        compiler_params=pltpu.CompilerParams(vmem_limit_bytes=60 * 2**20),
        cost_estimate=small_cost(),
        name=f"{name}_{k}",
    )(me, *parts, *whole, *(x for x, _ in tiled), *sources, *earlier)


def assemble_kernel(where, me, *refs):
    sources, whole, sems = refs[: len(where)], refs[len(where)], refs[len(where) + 1]
    copies = fetch(me, where, sources, whole, sems)
    for copy in copies:
        copy.start()
    for copy in copies:
        copy.wait()


def assemble(name, me, arrays, where, rows, cols):
    return pl.pallas_call(
        functools.partial(assemble_kernel, where),
        out_shape=jax.ShapeDtypeStruct((rows, cols), arrays[0].dtype),
        in_specs=[SMEM, *[ANY] * len(arrays)],
        out_specs=VMEM,
        scratch_shapes=[pltpu.SemaphoreType.DMA((len(arrays),))],
        compiler_params=pltpu.CompilerParams(vmem_limit_bytes=60 * 2**20),
        cost_estimate=small_cost(),
        name=name,
    )(me, *arrays)


def flip(x, axis):
    return lax.ppermute(x, axis, FLIP)


CROSS = [(1, 2), (2, 1)]
OUT = [(0, 1), (3, 2), (2, 0), (1, 3)]
BACK = [(1, 0), (2, 3), (0, 2), (3, 1)]


def crossed(x, perm):
    return lax.ppermute(x, ("core", "zh"), perm)


def straight():
    return lax.axis_index("core") == lax.axis_index("zh")


def swap(x):
    return jnp.where(straight(), x, crossed(x, CROSS))


def send_z(w):
    return crossed(w, OUT), crossed(w, CROSS)


def pair_of(w, out, cross):
    zh = lax.axis_index("zh")
    x = jnp.where(straight(), w, cross)
    return jnp.concatenate([jnp.where(zh == 0, x, out), jnp.where(zh == 0, out, x)], axis=0)


def give_z(part):
    zh = lax.axis_index("zh")
    half = part.shape[0] // 2
    upper, lower = part[:half], part[half:]
    return jnp.where(zh == 0, upper, lower), jnp.where(zh == 0, lower, upper)


def sum_z(keep, back, cross):
    return back.astype(jnp.float32) + jnp.where(straight(), keep, cross).astype(jnp.float32)


def shift(x, e, k):
    n = lax.axis_size("zl")
    return lax.ppermute(
        x, ("core", "zl"), [(c * n + l, (c ^ e) * n + (l + k) % n) for c in range(2) for l in range(n)]
    )


def from_near(x, k):
    n = lax.axis_size("zl")
    return lax.ppermute(x, "zl", [((j + k) % n, j) for j in range(n)])


def to_near(x, k):
    n = lax.axis_size("zl")
    return lax.ppermute(x, "zl", [(j, (j + k) % n) for j in range(n)])


def across(x, j):
    n = lax.axis_size("yx")
    return lax.ppermute(x, "yx", [(a, a ^ j) for a in range(n)])


def neighbours(x):
    count = lax.axis_size("yx")
    return [across(x, j) for j in range(1, count if count != 4 else 3)]


def diagonal(taken):
    if lax.axis_size("yx") != 4:
        return []
    half = taken[0].shape[0] // 2
    return [across(taken[1][:half], 1), across(taken[0][half:], 2)]


def blocks_of(own, taken, halves, column=0, source_column=0):
    deep = own.shape[0]
    arrays = [own, *taken, *halves]
    where = [(j, deep, 0, column, source_column) for j in range(1 + len(taken))]
    where += [(3, deep, n * deep // 2, column, source_column) for n in range(len(halves))]
    return arrays, tuple(where)


def whole_weight(w):
    return [w], ((0, 0, 0, 0, 0),)


def block_of(grad, j, columns):
    size = grad.shape[0] // lax.axis_size("yx")
    first = (lax.axis_index("yx") ^ j) * size
    return lax.dynamic_slice(grad, (first, columns[0]), (size, columns[1] - columns[0]))


def send_yx(grad, columns):
    count = lax.axis_size("yx")
    if count != 4:
        return [across(block_of(grad, j, columns), j) for j in range(1, count)]
    far = block_of(grad, 3, columns)
    half = far.shape[0] // 2
    return [across(far[:half], 1), across(far[half:], 2)]


def join_yx(grad, columns, taken):
    if lax.axis_size("yx") != 4:
        return taken, block_of(grad, 0, columns)
    half = taken[0].shape[0]
    one, two = block_of(grad, 1, columns), block_of(grad, 2, columns)
    one = jnp.concatenate([one[:half], one[half:] + taken[1]], axis=0)
    two = jnp.concatenate([two[:half] + taken[0], two[half:]], axis=0)
    return [across(one, 1), across(two, 2)], block_of(grad, 0, columns)


def total_yx(taken, own):
    total = own.astype(jnp.float32)
    for part in taken:
        total = total + part.astype(jnp.float32)
    return total.astype(jnp.bfloat16)


def body(
    tokens,
    cotangent,
    seq_lengths,
    attn_gain,
    q_weight,
    key_projection,
    value_projection,
    out_weight,
    mlp_gain,
    gate_weight,
    up_weight,
    down_weight,
):
    bf16, f32 = jnp.bfloat16, jnp.float32
    core, zl, yx = lax.axis_index("core"), lax.axis_index("zl"), lax.axis_index("yx")
    near = lax.axis_size("zl")
    others = range(1, near)
    rows = tokens.shape[0]
    group_rows = 2 * near * rows
    query_cols, key_cols = q_weight.shape[1], key_projection.shape[1]
    qkv_cols = query_cols + 2 * key_cols
    q_heads, kv_heads = query_cols // HD, key_cols // HD
    hidden_cols = gate_weight.shape[1]
    me = yx.astype(jnp.int32).reshape(1)

    qkv_shard = jnp.concatenate([q_weight, key_projection, value_projection], axis=1)
    gate_up_shard = jnp.concatenate([gate_weight, up_weight], axis=1)
    part_rows = rows // 2
    upper = swap(tokens[:part_rows])
    shard_moved = send_z(qkv_shard)
    lengths = swap(seq_lengths)
    gains = lax.all_gather(jnp.stack([attn_gain, mlp_gain]), ("yx", "core"), axis=1, tiled=True).astype(f32)
    upper, lengths, second_part, out_shard, gains, *shard_moved = stage(
        upper, lengths, tokens[part_rows:], out_weight, gains, *shard_moved
    )
    gain_one, gain_two = gains[0], gains[1]

    upper_far = [from_near(upper, k) for k in others]
    lower = swap(second_part)
    pair = pair_of(qkv_shard, *shard_moved)
    taken = neighbours(pair)
    out_out = crossed(out_shard, OUT)

    subs = jnp.arange(group_rows // SUB, dtype=jnp.int32)
    per_device = rows // SUB
    source, within = subs // per_device, subs % per_device
    there_core, there_zl = (source % 2) ^ core, (source // 2 + zl) % near
    to_order = (there_core * near + there_zl) * per_device + within
    from_order = (((source % near - zl) % near) * 2 + ((source // near) ^ core)) * per_device + within
    place = jnp.concatenate([to_order, from_order])
    row_at, doc_start = document_layout(lengths, group_rows)
    cosine, sine = rotary_tables(row_at - doc_start)

    def bounds(size):
        tile_start = doc_start.reshape(-1, size)
        tile = jnp.arange(group_rows // size, dtype=jnp.int32)
        low = tile_start[:, 0] // size
        return low, jnp.minimum((tile_start[:, -1] + size - 1) // size, tile)

    start_row = jnp.tile(doc_start.reshape(-1, 1, SUB), (1, 1, q_heads // kv_heads))
    layout = (place, *bounds(TILE), cosine, sine, doc_start[:, None])
    layout_back = (place, *bounds(SUB), cosine, sine, start_row)
    lower, out_out, out_shard, *moved = stage(lower, out_out, out_shard, *upper_far, *taken, *layout, *layout_back)
    upper_far, moved = moved[: near - 1], moved[near - 1 :]
    taken, moved = moved[: len(taken)], moved[len(taken) :]
    layout, layout_back = moved[: len(layout)], moved[len(layout) :]

    lower_far = [from_near(lower, k) for k in others]
    own = jnp.concatenate([upper, lower], axis=0)
    own_sib = flip(own, "core")
    out_cross = crossed(out_shard, CROSS)
    blocks = blocks_of(pair, taken, diagonal(taken))
    projecting = [(*blocks, qkv_cols)]
    gain_row = gain_one[None]
    outs = [(tokens.shape[1], bf16, "all"), (qkv_cols, bf16, "all")]
    normed = piece_call(project_kernel, "project", 0, near, me, [own, own_sib], [gain_row], [], projecting, [], outs)
    gate_up_shard, out_cross, down_shard, *moved = stage(gate_up_shard, out_cross, down_weight, *lower_far, *normed)
    lower_far, normed = moved[: near - 1], moved[near - 1 :]

    out_pair = pair_of(out_weight, out_out, out_cross)
    out_far = [from_near(out_pair, k) for k in others]
    down_moved = send_z(down_shard)
    for k in others:
        far = jnp.concatenate([upper_far[k - 1], lower_far[k - 1]], axis=0)
        parts = [far, flip(far, "core")]
        normed = piece_call(project_kernel, "project", k, near, me, parts, [gain_row], [], projecting, normed, outs)
    norm_one, qkv = normed
    gate_up_shard, qkv, out_pair, *moved = stage(gate_up_shard, qkv, out_pair, *out_far, *down_moved)
    out_far, down_moved = moved[: near - 1], moved[near - 1 :]

    gate_up_moved = send_z(gate_up_shard)
    w_out = lax.all_gather(jnp.concatenate([out_pair, *out_far], axis=1), "yx", axis=0, tiled=True)
    context, sums = attend(qkv, near, layout, q_heads, kv_heads)
    cotangent, *moved = stage(cotangent, *context, *gate_up_moved)
    context, gate_up_moved = moved[:near], moved[near:]

    quarters = [context[0]] + [None] * (near - 1)
    for k in others:
        quarters[near - k] = to_near(context[k], k)
    cot_upper = crossed(cotangent[:part_rows], CROSS)
    pairs = [
        pair_of(*(x[:, n * hidden_cols : (n + 1) * hidden_cols] for x in (gate_up_shard, *gate_up_moved)))
        for n in range(2)
    ]
    gate_taken = neighbours(pairs[0])
    w_project = assemble("assemble_project", me, *blocks, tokens.shape[1], qkv_cols)
    residual = own.astype(f32)
    scale_one = lax.rsqrt(jnp.mean(residual * residual, axis=-1, keepdims=True) + EPSILON)
    up_pair, cotangent, cot_upper, w_out, scale_one, w_project, *moved = stage(
        pairs[1], cotangent, cot_upper, w_out, scale_one, w_project, *quarters, *gate_taken
    )
    quarters, gate_taken = moved[:near], moved[near:]

    up_taken = neighbours(up_pair)
    gate_halves = diagonal(gate_taken)
    context_all = jnp.concatenate(quarters, axis=1)
    branch_sib = flip(times_transpose(context_all[rows:], w_out).astype(bf16), "core")
    mid = residual + times_transpose(context_all[:rows], w_out) + branch_sib.astype(f32)
    scale_two, norm_two = norm_rows(mid, gain_two)
    norm_two, cotangent, *moved = stage(norm_two, cotangent, *up_taken, *gate_halves)
    up_taken, gate_halves = moved[: len(up_taken)], moved[len(up_taken) :]

    quarter = part_rows // 2
    far_quarters = [[from_near(norm_two[:quarter], k) for k in others]]
    norm_sib = flip(norm_two, "core")
    up_halves = diagonal(up_taken)
    down_pair = pair_of(down_weight, *down_moved)
    norm_two, norm_sib, down_pair, cotangent, *moved = stage(
        norm_two, norm_sib, down_pair, cotangent, *far_quarters[0], *up_halves
    )
    far_quarters[0], up_halves = moved[: near - 1], moved[near - 1 :]

    far_quarters.append([from_near(norm_two[quarter:part_rows], k) for k in others])
    cot_lower = crossed(cotangent[part_rows:], CROSS)
    down_taken = neighbours(down_pair)
    gate_blocks = blocks_of(pairs[0], gate_taken, gate_halves)
    up_blocks = blocks_of(up_pair, up_taken, up_halves, hidden_cols)
    gate_up = ([*gate_blocks[0], *up_blocks[0]], gate_blocks[1] + up_blocks[1], 2 * hidden_cols)
    gate_outs = [(norm_two.shape[1], bf16, "all"), (2 * hidden_cols, f32, "all"), (hidden_cols, bf16, "all")]
    earlier = piece_call(gate_kernel, "gate", 0, near, me, [norm_two, norm_sib], [], [], [gate_up], [], gate_outs)
    norm_two, cotangent, cot_lower, *moved = stage(
        norm_two, cotangent, cot_lower, *far_quarters[1], *down_taken, *earlier
    )
    far_quarters[1], moved = moved[: near - 1], moved[near - 1 :]
    down_taken, earlier = moved[: len(down_taken)], moved[len(down_taken) :]

    lower_far = [from_near(norm_two[part_rows:], k) for k in others]
    cot = jnp.where(straight(), cotangent, jnp.concatenate([cot_upper, cot_lower], axis=0))
    cot_sib = flip(cot, "core")
    cot_upper_far = [from_near(jnp.where(straight(), cotangent[:part_rows], cot_upper), k) for k in others]
    down_halves = diagonal(down_taken)
    down = (*blocks_of(down_pair, down_taken, down_halves), hidden_cols)
    width = norm_two.shape[1]
    outs = [(width, bf16, "all"), (2 * hidden_cols, bf16, "all")]
    halves = [(width, bf16, "own"), (width, bf16, "sibling")]

    def way_back(k, parts, earlier):
        tiled, results = [(gate_up_all, k), (hidden_all, k)], outs + halves * (1 if earlier else 2)
        return piece_call(gate_back_kernel, "gate_back", k, near, me, parts, [], tiled, [gate_up, down], earlier, results)

    def joined(own, sib):
        return own.astype(f32) + flip(sib, "core").astype(f32)

    norm_two_all, gate_up_all, hidden_all = earlier
    grad_all, d_gate_up_all, *near_back = way_back(0, [cot, cot_sib], [])
    cot, *moved = stage(
        cot, norm_two_all, gate_up_all, hidden_all, grad_all, d_gate_up_all, *near_back, *cot_upper_far, *lower_far
    )
    earlier, (grad_all, d_gate_up_all), near_back, moved = moved[:3], moved[3:5], moved[5:9], moved[9:]
    cot_upper_far, lower_far = moved[: near - 1], moved[near - 1 :]

    cot_lower_far = [from_near(cot[part_rows:], k) for k in others]
    out_far = []
    for k in others:
        norm_far = jnp.concatenate([*(x[k - 1] for x in far_quarters), lower_far[k - 1]], axis=0)
        parts = [norm_far, flip(norm_far, "core")]
        *earlier, out_own, out_sib = piece_call(
            gate_kernel, "gate", k, near, me, parts, [], [], [gate_up, down], earlier, gate_outs + halves
        )
        out_far += [out_own, out_sib]
    grad_all, d_gate_up_all, w_project, *moved = stage(
        grad_all, d_gate_up_all, w_project, *near_back, *cot_lower_far, *earlier, *out_far
    )
    near_back, cot_lower_far, moved = moved[:4], moved[4 : near + 3], moved[near + 3 :]
    earlier, out_far = moved[:3], moved[3:]
    norm_two_all, gate_up_all, hidden_all = earlier
    cot_far = [jnp.concatenate(x, axis=0) for x in zip(cot_upper_far, cot_lower_far, strict=True)]
    cot_far_sib = [flip(x, "core") for x in cot_far]
    out_sums = [joined(*out_far[2 * n : 2 * n + 2]).astype(bf16) for n in range(near - 1)]
    moved = stage(*cot_far_sib, *out_sums)
    cot_far_sib, out_sums = moved[: near - 1], moved[near - 1 :]

    out_upper = [to_near(out_sums[k - 1][:part_rows], k) for k in others]
    back = []
    for k in others:
        parts = [cot_far[k - 1], cot_far_sib[k - 1]]
        grad_all, d_gate_up_all, *more = way_back(k, parts, [grad_all, d_gate_up_all])
        back.append(more)
    grad_all, d_gate_up_all, *moved = stage(grad_all, d_gate_up_all, *(x for more in back for x in more), *out_upper)
    far_back, out_upper = moved[: 2 * near - 2], moved[2 * near - 2 :]
    d_norm_sent = [joined(*far_back[2 * n : 2 * n + 2]).astype(bf16) for n in range(near - 1)]
    grad_all, d_gate_up_all, near_own, near_sib, *d_norm_sent = stage(
        grad_all, d_gate_up_all, *near_back[:2], *d_norm_sent
    )

    moved_upper = [to_near(d_norm_sent[k - 1][:part_rows], k) for k in others]
    grad_gate, grad_up = (
        rows_product(norm_two_all, d_gate_up_all[:, n * hidden_cols : (n + 1) * hidden_cols]).astype(bf16)
        for n in range(2)
    )
    d_norm_two, output_near = joined(near_own, near_sib), joined(*near_back[2:])
    grad_gate, grad_up, grad_all, d_norm_two, output_near, *moved = stage(
        grad_gate, grad_up, grad_all, d_norm_two, output_near, *moved_upper, *d_norm_sent
    )
    moved_upper, d_norm_sent = moved[: near - 1], moved[near - 1 :]

    moved_lower = [to_near(d_norm_sent[k - 1][part_rows:], k) for k in others]
    gate_part = lax.psum_scatter(grad_gate, "yx", scatter_dimension=0, tiled=True)
    grad_down = rows_product(grad_all, hidden_all).astype(bf16)

    def output_part(at, moved):
        part = mid[at] + output_near[at]
        for x in moved:
            part = part + x.astype(f32)
        return part.astype(bf16)

    grad_down, d_norm_two, output_near, *moved = stage(grad_down, d_norm_two, output_near, *out_sums, *moved_lower)
    out_sums, moved_lower = moved[: near - 1], moved[near - 1 :]
    output_upper = output_part(slice(0, part_rows), out_upper)

    out_lower = [[to_near(out_sums[k - 1][part_rows : part_rows + quarter], k) for k in others]]
    up_part = lax.psum_scatter(grad_up, "yx", scatter_dimension=0, tiled=True)
    for one, two in zip(moved_upper, moved_lower, strict=True):
        d_norm_two = d_norm_two + jnp.concatenate([one, two], axis=0).astype(f32)
    mid_back, _ = norm_back(mid, scale_two, gain_two, d_norm_two)
    d_mid = cot.astype(f32) + mid_back
    d_attn = d_mid.astype(bf16)
    d_attn, output_upper, *moved = stage(d_attn, output_upper, *out_lower[0], *out_sums)
    out_lower[0], out_sums = moved[: near - 1], moved[near - 1 :]

    out_lower.append([to_near(out_sums[k - 1][part_rows + quarter :], k) for k in others])
    d_attn_sib = flip(d_attn, "core")
    both = [dot32(x, w_out).astype(bf16) for x in (d_attn, d_attn_sib)]
    d_quarters = [
        jnp.concatenate([x[:, k * query_cols : (k + 1) * query_cols] for x in both], axis=0) for k in range(near)
    ]
    d_attn, d_attn_sib, *moved = stage(d_attn, d_attn_sib, *d_quarters, *out_lower[1])
    d_quarters, out_lower[1] = moved[:near], moved[near:]

    d_context = [d_quarters[0]] + [None] * (near - 1)
    for k in others:
        d_context[near - k] = to_near(d_quarters[k], k)
    upper_crossed = crossed(output_upper, CROSS)
    grad_out = rows_product(d_attn, context_all[:rows]) + rows_product(d_attn_sib, context_all[rows:])
    grad_out = grad_out.astype(bf16)
    output_lower = output_part(
        slice(part_rows, rows), [jnp.concatenate(x, axis=0) for x in zip(*out_lower, strict=True)]
    )
    grad_out, output_lower, gate_part, up_part, upper_crossed, *d_context = stage(
        grad_out, output_lower, gate_part, up_part, upper_crossed, *d_context
    )

    lower_crossed = crossed(output_lower, CROSS)
    output = jnp.concatenate([output_upper, output_lower], axis=0)
    gate_keep, gate_give = give_z(gate_part)
    gate_home = [crossed(gate_give, BACK), crossed(gate_keep, CROSS)]
    up_keep, up_give = give_z(up_part)
    up_home = [crossed(up_give, BACK), crossed(up_keep, CROSS)]
    down_part = lax.psum_scatter(grad_down, "yx", scatter_dimension=0, tiled=True)
    out_part = lax.psum_scatter(grad_out, "yx", scatter_dimension=0, tiled=True)
    d_qkv = attend_back(list(range(kv_heads)), qkv, d_context, context, sums, [], layout_back, q_heads, kv_heads)
    d_qkv, lower_crossed, down_part, *moved = stage(d_qkv, lower_crossed, down_part, *gate_home, *up_home)
    gate_home, up_home = moved[:2], moved[2:]
    output = jnp.where(straight(), output, jnp.concatenate([upper_crossed, lower_crossed], axis=0))

    def back_part(k):
        own, sib = (d_qkv[(2 * k + e) * rows : (2 * k + e + 1) * rows] for e in range(2))
        taken = flip(times_transpose(sib, w_project).astype(bf16), "core")
        return times_transpose(own, w_project) + taken.astype(f32)

    down_keep, down_give = give_z(down_part)
    down_home = [crossed(down_give, BACK), crossed(down_keep, CROSS)]
    d_sent = [back_part(k).astype(bf16) for k in others]
    d_qkv, *moved = stage(d_qkv, *d_sent, *down_home)
    d_sent, down_home = moved[: near - 1], moved[near - 1 :]

    d_upper = [to_near(d_sent[k - 1][:part_rows], k) for k in others]
    grad_project = rows_product(norm_one, d_qkv).astype(bf16)
    project_sent = send_yx(grad_project, (0, qkv_cols))
    total = back_part(0)
    total, grad_project, *moved = stage(total, grad_project, *d_upper, *d_sent, *project_sent)
    d_upper, d_sent, project_sent = moved[: near - 1], moved[near - 1 : 2 * near - 2], moved[2 * near - 2 :]

    d_lower = [to_near(d_sent[k - 1][part_rows:], k) for k in others]
    project_rest, project_own = join_yx(grad_project, (0, qkv_cols), project_sent)
    out_part, *moved = stage(out_part, *d_lower, *project_rest)
    d_lower, project_rest = moved[: near - 1], moved[near - 1 :]
    d_moved = [jnp.concatenate(x, axis=0) for x in zip(d_upper, d_lower, strict=True)]
    project_keep, project_give = give_z(total_yx(project_rest, project_own))

    project_home = [crossed(project_give, BACK), crossed(project_keep, CROSS)]
    for part in d_moved:
        total = total + part.astype(f32)
    input_back, _ = norm_back(residual, scale_one, gain_one, total)
    input_own = (d_mid + input_back).astype(bf16)
    out_moved = [to_near(out_part[:, k * query_cols : (k + 1) * query_cols], k) for k in others]
    out_quarter = out_part[:, :query_cols].astype(f32)
    for part in out_moved:
        out_quarter = out_quarter + part.astype(f32)
    out_keep, out_give = give_z(out_quarter.astype(bf16))
    input_own, out_keep, out_give, *project_home = stage(input_own, out_keep, out_give, *project_home)
    out_home = [crossed(out_give, BACK), crossed(out_keep, CROSS)]
    input_grad = jnp.where(straight(), input_own, crossed(input_own, CROSS)).astype(f32)
    grad_project = sum_z(project_keep, *project_home)
    grad_out = sum_z(out_keep, *out_home)
    grad_down = sum_z(down_keep, *down_home)
    grad_gate, grad_up = sum_z(gate_keep, *gate_home), sum_z(up_keep, *up_home)
    gain_grads = lax.psum(
        jnp.stack(
            [
                jnp.sum(qkv_shard.astype(f32) * grad_project, axis=1),
                jnp.sum(gate_weight.astype(f32) * grad_gate + up_weight.astype(f32) * grad_up, axis=1),
            ]
        ),
        ("zh", "zl"),
    ) / jnp.stack([attn_gain, mlp_gain]).astype(f32)
    return (
        output,
        input_grad,
        gain_grads[0],
        grad_project[:, :query_cols],
        grad_project[:, query_cols : query_cols + key_cols],
        grad_project[:, query_cols + key_cols :],
        grad_out,
        gain_grads[1],
        grad_gate,
        grad_up,
        grad_down,
    )


def solution(mesh):
    dp, tensor = mesh.shape["dp"], mesh.shape["tensor"]
    fine = Mesh(mesh.devices.reshape(dp // 2, 2, 2, tensor // 2), AXES)
    by_rows, by_dp, by_both = P(AXES, None), P(("yx", "core")), P(("yx", "core"), ("zh", "zl"))
    return jax.shard_map(
        body,
        mesh=fine,
        in_specs=(
            by_rows, by_rows, P(("yx", "core"), None), by_dp, by_both, by_both, by_both, by_both,
            by_dp, by_both, by_both, by_both,
        ),
        out_specs=(
            by_rows, by_rows, by_dp, by_both, by_both, by_both, by_both, by_dp, by_both, by_both, by_both,
        ),
        check_vma=False,
    )
```

```python
import functools
import math

import jax
import jax.numpy as jnp
import numpy as np
from jax import lax
from jax.experimental import pallas as pl
from jax.experimental.pallas import tpu as pltpu
from jax.sharding import Mesh
from jax.sharding import PartitionSpec as P

HD = 96
HALF = HD // 2
PAD = 128
STEPS = 4
SUB = 256
TILE = 512

EPSILON = 1e-05
ROTARY_BASE = 100000.0
MASKED = -1e30
LOG2E = math.log2(math.e)

AXES = ("yx", "core", "zh", "zl")
FLIP = [(0, 1), (1, 0)]


def norm_rows(values, gain):
    row_scale = lax.rsqrt(jnp.mean(values * values, axis=-1, keepdims=True) + EPSILON)
    return (row_scale, (values * row_scale * gain).astype(jnp.bfloat16))


def norm_back(values, row_scale, gain, upstream):
    weighted = upstream * gain
    inner_sum = jnp.mean(weighted * values, axis=-1, keepdims=True)
    grad_in = row_scale * weighted - values * (row_scale * row_scale * row_scale) * inner_sum
    gain_part = jnp.sum(upstream * (values * row_scale), axis=0)
    return (grad_in, gain_part)


def document_layout(lengths, group_rows):
    flat_lengths = lengths.reshape(-1)
    doc_ends = jnp.cumsum(flat_lengths)
    rows = jnp.arange(group_rows, dtype=jnp.int32)
    passed = (rows[:, None] >= doc_ends[None, :]).astype(jnp.int32)
    return (rows, jnp.sum(passed * flat_lengths[None, :], axis=1))


def rotary_tables(positions):
    exponents = jnp.arange(HALF, dtype=jnp.float32) * (2.0 / HD)
    inverse = ROTARY_BASE ** (-exponents)
    angles = positions.astype(jnp.float32)[:, None] * inverse[None, :]
    cosine, sine = jnp.cos(angles), jnp.sin(angles)
    gap = jnp.zeros((positions.shape[0], PAD // 2 - HALF), jnp.float32)
    return (
        jnp.concatenate([cosine, gap, cosine, gap], axis=1),
        jnp.concatenate([-sine, gap, sine, gap], axis=1),
    )


def rows_product(left, right):
    return lax.dot_general(
        left, right, (((0,), (0,)), ((), ())), preferred_element_type=jnp.float32
    )


def times_transpose(left, right):
    return lax.dot_general(
        left, right, (((1,), (1,)), ((), ())), preferred_element_type=jnp.float32
    )


def dot32(left, right):
    return jnp.dot(left, right, preferred_element_type=jnp.float32)


def stage(*values):
    return lax.optimization_barrier(values)


def spread(columns, heads):
    matrix = np.zeros((columns, len(heads) * PAD), np.float32)
    for at, first in enumerate(heads):
        for half in range(2):
            for i in range(HALF):
                matrix[first + half * HALF + i, at * PAD + half * (PAD // 2) + i] = 1.0
    return matrix


def turn(x, cosine, sine):
    return x * cosine + pltpu.roll(x, PAD // 2, 1) * sine


def rows_at(t, size):
    return pl.ds(pl.multiple_of(t * size, size), size)


def forward_kernel(pieces, ratio, *refs):
    place, low, full, cosine, sine, start, spread_in, gather_out = refs[:8]
    heads = spread_in.shape[0]
    refs = refs[8:]
    qkv, context, refs = refs[0], refs[1 : 1 + pieces], refs[1 + pieces :]
    log_sum, refs = refs[:heads], refs[heads:]
    q_s, k_s, v_s, s_s, top_s, acc = refs
    tiles = q_s.shape[0]
    all_subs = qkv.shape[0] // SUB
    piece_subs = all_subs // pieces
    scale = LOG2E * HD ** (-0.5)
    ones_lane = lax.broadcasted_iota(jnp.int32, (SUB, PAD), 1) == PAD - 1

    def prepare(r, carry):
        t = place[r]
        at = rows_at(t, SUB)
        cos_t, sin_t = cosine[at, :], sine[at, :]
        tile, half = t // (TILE // SUB), t % (TILE // SUB)
        for g in range(heads):
            wide = dot32(qkv[rows_at(r, SUB), :], spread_in[g])
            for h in range(ratio):
                query = turn(wide[:, h * PAD : (h + 1) * PAD], cos_t, sin_t) * scale
                first = pl.multiple_of(h * TILE + half * SUB, SUB)
                q_s[tile, g, pl.ds(first, SUB), :] = query.astype(jnp.bfloat16)
            key = turn(wide[:, ratio * PAD : (ratio + 1) * PAD], cos_t, sin_t)
            k_s[g, at, :] = key.astype(jnp.bfloat16)
            value = jnp.where(ones_lane, 1.0, wide[:, (ratio + 1) * PAD :])
            v_s[g, at, :] = value.astype(jnp.bfloat16)
        return carry

    lax.fori_loop(0, all_subs, prepare, 0)

    def query_tile(i, carry):
        starts = jnp.concatenate([start[rows_at(i, TILE), :]] * ratio, axis=0)
        top_s[...] = jnp.full_like(top_s, MASKED)

        def scores(j, masked, diagonal):
            for g in range(heads):
                s = times_transpose(q_s[i, g], k_s[g, rows_at(j, TILE), :])
                if masked:
                    key_at = lax.broadcasted_iota(jnp.int32, s.shape, 1)
                    allowed = key_at + j * TILE >= starts
                    if diagonal:
                        query_at = lax.rem(lax.broadcasted_iota(jnp.int32, s.shape, 0), TILE)
                        allowed = allowed & (key_at <= query_at)
                    s = jnp.where(allowed, s, MASKED)
                s_s[g, j] = s
                peak = s[:, :PAD]
                for c in range(1, TILE // PAD):
                    peak = jnp.maximum(peak, s[:, c * PAD : (c + 1) * PAD])
                top_s[g] = jnp.maximum(top_s[g], peak)

        def loop(first, last, masked):
            def run(j, c):
                scores(j, masked, False)
                return c

            lax.fori_loop(first, last, run, 0)

        loop(low[i], full[i], True)
        loop(full[i], i, False)
        scores(i, True, True)
        tops = [jnp.max(top_s[g], axis=1, keepdims=True) for g in range(heads)]
        acc[...] = jnp.zeros_like(acc)

        def weigh(j, c):
            for g in range(heads):
                p = jnp.exp2(s_s[g, j] - tops[g]).astype(jnp.bfloat16)
                acc[g] += dot32(p, v_s[g, rows_at(j, TILE), :])
            return c

        lax.fori_loop(low[i], i + 1, weigh, 0)
        packed = None
        for g in range(heads):
            total = acc[g][:, PAD - 1 :]
            out = acc[g] * (1.0 / total)
            sums = jnp.broadcast_to(tops[g] + jnp.log(total) * LOG2E, (ratio * TILE, PAD))
            log_sum[g][i] = sums.T[:1, :]
            wide = jnp.concatenate(
                [out[h * TILE : (h + 1) * TILE, :] for h in range(ratio)], axis=1
            ).astype(jnp.bfloat16)
            part = dot32(wide, gather_out[g])
            packed = part if packed is None else packed + part
        subs = tiles * (TILE // SUB)
        for half in range(TILE // SUB):
            r = place[subs + i * (TILE // SUB) + half]
            part = packed[half * SUB : (half + 1) * SUB, :].astype(jnp.bfloat16)
            for k in range(pieces):

                @pl.when(r // piece_subs == k)
                def store(k=k, part=part, r=r):
                    context[k][rows_at(r % piece_subs, SUB), :] = part

        return carry

    lax.fori_loop(0, tiles, query_tile, 0)


def backward_kernel(pieces, ratio, more, *refs):
    place, low, full, cosine, sine, start, refs = *refs[:6], refs[6:]
    heads = refs[0].shape[0]
    spread_in, spread_out, gather_in, refs = *refs[:3], refs[3:]
    log_sum, refs = refs[:heads], refs[heads:]
    d_context, context, qkv, refs = refs[:pieces], refs[pieces : 2 * pieces], refs[2 * pieces], refs[2 * pieces + 1 :]
    earlier, refs = (refs[0], refs[1:]) if more else (None, refs)
    d_qkv, refs = refs[0], refs[1:]
    q_s, k_s, kt_s, v_s, do_s, delta_s, log_s, dq_acc, dk_acc, dv_acc, dq_s = refs
    tiles = q_s.shape[0]
    all_subs = qkv.shape[0] // SUB
    piece_subs = all_subs // pieces
    scale = HD ** (-0.5)
    per_tile = TILE // SUB

    for k in range(pieces):

        def prepare(r, carry, k=k):
            t = place[k * piece_subs + r]
            rel = rows_at(r, SUB)
            at = rows_at(t, SUB)
            cos_t, sin_t = cosine[at, :], sine[at, :]
            for g in range(heads):
                wide = dot32(qkv[rows_at(k * piece_subs + r, SUB), :], spread_in[g])
                d_out = dot32(d_context[k][rel, :], spread_out[g])
                out = dot32(context[k][rel, :], spread_out[g])
                for h in range(ratio):
                    cols = slice(h * PAD, (h + 1) * PAD)
                    rows = slice(h * SUB, (h + 1) * SUB)
                    query = turn(wide[:, cols], cos_t, sin_t) * (scale * LOG2E)
                    q_s[t, g, rows, :] = query.astype(jnp.bfloat16)
                    do_s[t, g, rows, :] = d_out[:, cols].astype(jnp.bfloat16)
                    delta = jnp.sum((d_out[:, cols] * out[:, cols]).T, axis=0, keepdims=True)
                    delta_s[t * heads + g, :, rows] = delta
                    first = pl.multiple_of(h * TILE + t % per_tile * SUB, SUB)
                    log_s[t * heads + g, :, rows] = log_sum[g][t // per_tile, :, pl.ds(first, SUB)]
                key = turn(wide[:, ratio * PAD : (ratio + 1) * PAD], cos_t, sin_t)
                k_s[g, t] = key.astype(jnp.bfloat16)
                kt_s[g, t] = key.T.astype(jnp.bfloat16)
                v_s[g, t] = wide[:, (ratio + 1) * PAD :].astype(jnp.bfloat16)
                dk_acc[g, t] = jnp.zeros((SUB, PAD), jnp.float32)
                dv_acc[g, t] = jnp.zeros((SUB, PAD), jnp.float32)
            return carry

        lax.fori_loop(0, piece_subs, prepare, 0)

    def query_tile(i, carry):
        dq_acc[...] = jnp.zeros_like(dq_acc)

        def step(j, masked, diagonal):
            for g in range(heads):
                queries, d_out = q_s[i, g], do_s[i, g]
                s = times_transpose(k_s[g, j], queries)
                if masked:
                    key_at = lax.broadcasted_iota(jnp.int32, s.shape, 0)
                    allowed = key_at + j * SUB >= start[i]
                    if diagonal:
                        query_at = lax.rem(lax.broadcasted_iota(jnp.int32, s.shape, 1), SUB)
                        allowed = allowed & (key_at <= query_at)
                    s = jnp.where(allowed, s, MASKED)
                p = jnp.exp2(s - log_s[i * heads + g])
                d_p = times_transpose(v_s[g, j], d_out)
                d_s = (p * (d_p - delta_s[i * heads + g])).astype(jnp.bfloat16)
                dv_acc[g, j] += dot32(p.astype(jnp.bfloat16), d_out)
                dk_acc[g, j] += dot32(d_s, queries)
                dq_acc[g] += dot32(kt_s[g, j], d_s)

        def loop(first, last, masked):
            def run(j, c):
                step(j, masked, False)
                return c

            lax.fori_loop(first, last, run, 0)

        loop(low[i], full[i], True)
        loop(full[i], i, False)
        step(i, True, True)
        at = rows_at(i, SUB)
        cos_t, sin_t = cosine[at, :], sine[at, :]
        for g in range(heads):
            grad = dq_acc[g].T * scale
            for h in range(ratio):
                piece = turn(grad[h * SUB : (h + 1) * SUB, :], cos_t, -sin_t)
                dq_s[g, i, :, h * PAD : (h + 1) * PAD] = piece.astype(jnp.bfloat16)
        return carry

    lax.fori_loop(0, tiles, query_tile, 0)

    def finish(r, carry):
        t = place[r]
        at = rows_at(t, SUB)
        rel = rows_at(r, SUB)
        packed = None
        for g in range(heads):
            key = turn(dk_acc[g, t] * (1.0 / LOG2E), cosine[at, :], -sine[at, :])
            wide = jnp.concatenate(
                [dq_s[g, t], key.astype(jnp.bfloat16), dv_acc[g, t].astype(jnp.bfloat16)], axis=1
            )
            part = dot32(wide, gather_in[g])
            packed = part if packed is None else packed + part
        packed = packed.astype(jnp.bfloat16)
        d_qkv[rel, :] = packed + earlier[rel, :] if more else packed
        return carry

    lax.fori_loop(0, all_subs, finish, 0)


SMEM = pl.BlockSpec(memory_space=pltpu.SMEM)
VMEM = pl.BlockSpec(memory_space=pltpu.VMEM)
ANY = pl.BlockSpec(memory_space=pl.ANY)


def small_cost(transcendentals=0):
    return pl.CostEstimate(flops=1 << 20, bytes_accessed=1 << 16, transcendentals=transcendentals)


def head_matrices(head, q_heads, kv_heads):
    ratio = q_heads // kv_heads
    queries = [(head * ratio + r) * HD for r in range(ratio)]
    key, value = (q_heads + head) * HD, (q_heads + kv_heads + head) * HD
    inner = spread((q_heads + 2 * kv_heads) * HD, [*queries, key, value])
    outer = spread(q_heads * HD, queries)
    return jnp.asarray(inner, jnp.bfloat16), jnp.asarray(outer, jnp.bfloat16)


def stacked_matrices(q_heads, kv_heads):
    pairs = [head_matrices(head, q_heads, kv_heads) for head in range(kv_heads)]
    return jnp.stack([inner for inner, _ in pairs]), jnp.stack([outer for _, outer in pairs])


def attend(qkv, pieces, layout, q_heads, kv_heads):
    place, low, full, cosine, sine, start_column = layout
    ratio, rows = q_heads // kv_heads, qkv.shape[0]
    tiles, lanes = rows // TILE, ratio * TILE
    bf16, f32 = jnp.bfloat16, jnp.float32
    inner, outer = stacked_matrices(q_heads, kv_heads)
    outs = pl.pallas_call(
        functools.partial(forward_kernel, pieces, ratio),
        out_shape=[
            *[jax.ShapeDtypeStruct((rows // pieces, q_heads * HD), bf16)] * pieces,
            *[jax.ShapeDtypeStruct((tiles, 1, lanes), f32)] * kv_heads,
        ],
        in_specs=[SMEM] * 3 + [VMEM] * 6,
        out_specs=[VMEM] * (pieces + kv_heads),
        scratch_shapes=[
            pltpu.VMEM((tiles, kv_heads, lanes, PAD), bf16),
            pltpu.VMEM((kv_heads, rows, PAD), bf16),
            pltpu.VMEM((kv_heads, rows, PAD), bf16),
            pltpu.VMEM((kv_heads, tiles, lanes, TILE), f32),
            pltpu.VMEM((kv_heads, lanes, PAD), f32),
            pltpu.VMEM((kv_heads, lanes, PAD), f32),
        ],
        compiler_params=pltpu.CompilerParams(vmem_limit_bytes=60 * 2**20),
        cost_estimate=small_cost(),
        name="attention_forward",
    )(place, low, full, cosine, sine, start_column, inner, jnp.swapaxes(outer, 1, 2), qkv)
    return outs[:pieces], outs[pieces:]


def attend_back(heads, qkv, d_context, context, sums, earlier, layout, q_heads, kv_heads):
    place, low, full, cosine, sine, start_row = layout
    pieces, ratio, rows = len(context), q_heads // kv_heads, qkv.shape[0]
    tiles, lanes, count = rows // SUB, ratio * SUB, len(heads)
    bf16, f32 = jnp.bfloat16, jnp.float32
    inner, outer = stacked_matrices(q_heads, kv_heads)
    inner, outer = inner[heads[0] : heads[0] + count], outer[heads[0] : heads[0] + count]
    return pl.pallas_call(
        functools.partial(backward_kernel, pieces, ratio, bool(earlier)),
        out_shape=jax.ShapeDtypeStruct(qkv.shape, bf16),
        in_specs=[SMEM] * 3 + [VMEM] * (7 + count + 2 * pieces + len(earlier)),
        out_specs=VMEM,
        scratch_shapes=[
            pltpu.VMEM((tiles, count, lanes, PAD), bf16),
            pltpu.VMEM((count, tiles, SUB, PAD), bf16),
            pltpu.VMEM((count, tiles, PAD, SUB), bf16),
            pltpu.VMEM((count, tiles, SUB, PAD), bf16),
            pltpu.VMEM((tiles, count, lanes, PAD), bf16),
            pltpu.VMEM((tiles * count, 1, lanes), f32),
            pltpu.VMEM((tiles * count, 1, lanes), f32),
            pltpu.VMEM((count, PAD, lanes), f32),
            pltpu.VMEM((count, tiles, SUB, PAD), f32),
            pltpu.VMEM((count, tiles, SUB, PAD), f32),
            pltpu.VMEM((count, tiles, SUB, ratio * PAD), bf16),
        ],
        compiler_params=pltpu.CompilerParams(vmem_limit_bytes=60 * 2**20),
        cost_estimate=small_cost(),
        name=f"attention_backward_{heads[0]}",
    )(
        place, low, full, cosine, sine, start_row, inner, outer, jnp.swapaxes(inner, 1, 2),
        *[sums[h] for h in heads], *d_context, *context, qkv, *earlier,
    )


def fetch(me, where, sources, target, sems):
    copies = []
    for n, (source, (j, deep, first, column, taken)) in enumerate(zip(sources, where, strict=True)):
        cols = min(source.shape[1] - taken, target.shape[1] - column)
        at = pl.ds(pl.multiple_of((me[0] ^ j) * deep + first, 16), source.shape[0])
        if cols != source.shape[1]:
            source = source.at[:, taken : taken + cols]
        copies.append(pltpu.make_async_copy(source, target.at[at, column : column + cols], sems.at[n]))
    return copies


def take_rows(parts, target):
    rows = target.shape[0]
    for step in range(STEPS):

        @pl.when(pl.program_id(0) == step)
        def take(step=step):
            at = 0
            for part in parts:
                first, last = max(at, step * rows), min(at + part.shape[0], (step + 1) * rows)
                if first < last:
                    target[first - step * rows : last - step * rows, :] = part[first - at : last - at, :]
                at += part.shape[0]


def at_first_step(copies, what):
    @pl.when(pl.program_id(0) == 0)
    def run():
        for copy in copies:
            what(copy)


def project_kernel(count, where, more, me, *refs):
    parts, gain, refs = refs[:count], refs[count], refs[count + 1 :]
    sources, refs = refs[: len(where[0])], refs[len(where[0]) :]
    norm_all, qkv_all, weight, sems, rows_s = refs[2 if more else 0 :]
    copies = fetch(me, where[0], sources, weight, sems)
    at_first_step(copies, lambda copy: copy.start())
    take_rows(parts, rows_s)
    x = rows_s[...].astype(jnp.float32)
    scale = lax.rsqrt(jnp.mean(x * x, axis=-1, keepdims=True) + EPSILON)
    norm_all[...] = (x * scale * gain[...]).astype(jnp.bfloat16)
    at_first_step(copies, lambda copy: copy.wait())
    qkv_all[...] = dot32(norm_all[...], weight[...]).astype(jnp.bfloat16)


def by_half(refs, value):
    for n, ref in enumerate(refs):

        @pl.when(pl.program_id(0) * 2 // STEPS == n)
        def store(ref=ref):
            ref[...] = value


def gate_kernel(count, where, more, me, *refs):
    parts, refs = refs[:count], refs[count:]
    with_out = len(where) > 1
    sources, refs = refs[: sum(map(len, where))], refs[sum(map(len, where)) :]
    norm_all, gate_up_all, hidden_all, *refs = refs[3 if more else 0 :]
    out_refs, refs = (refs[:2], refs[2:]) if with_out else ((), refs)
    weight, sems, *refs = refs
    hidden_cols = hidden_all.shape[1]
    copies = fetch(me, where[0], sources[: len(where[0])], weight, sems)
    if with_out:
        w_down, down_sems = refs
        copies += fetch(me, where[1], sources[len(where[0]) :], w_down, down_sems)
    at_first_step(copies, lambda copy: copy.start())
    take_rows(parts, norm_all)
    at_first_step(copies, lambda copy: copy.wait())
    x = norm_all[...]
    width = min(512, hidden_cols)
    for at in range(0, hidden_cols, width):
        gate_at = slice(at, at + width)
        up_at = slice(hidden_cols + at, hidden_cols + at + width)
        gate = dot32(x, weight[:, gate_at])
        up = dot32(x, weight[:, up_at])
        gate_up_all[:, gate_at] = gate
        gate_up_all[:, up_at] = up
        hidden_all[:, gate_at] = (gate * (1.0 / (1.0 + jnp.exp(-gate))) * up).astype(jnp.bfloat16)
    if with_out:
        by_half(out_refs, times_transpose(hidden_all[...], w_down[...]).astype(jnp.bfloat16))


def gate_back_kernel(count, where, more, me, *refs):
    parts, gate_up_all, hidden_here, refs = refs[:count], *refs[count : count + 2], refs[count + 2 :]
    gate_up, refs = refs[: len(where[0])], refs[len(where[0]) :]
    down, refs = refs[: len(where[1])], refs[len(where[1]) :]
    grad_all, d_gate_up_all, *refs = refs[2 if more else 0 :]
    d_norm_refs, refs = refs[:2], refs[2:]
    out_refs, refs = ((), refs) if more else (refs[:2], refs[2:])
    w_gate_up, gate_up_sems, w_down, down_sems = refs
    hidden_cols = w_down.shape[1]
    down_copies = fetch(me, where[1], down, w_down, down_sems)
    copies = fetch(me, where[0], gate_up, w_gate_up, gate_up_sems)
    at_first_step(down_copies + copies, lambda copy: copy.start())
    take_rows(parts, grad_all)
    at_first_step(down_copies, lambda copy: copy.wait())
    dy = grad_all[...]
    width = min(512, hidden_cols)
    for at in range(0, hidden_cols, width):
        gate_at = slice(at, at + width)
        up_at = slice(hidden_cols + at, hidden_cols + at + width)
        d_hidden = dot32(dy, w_down[:, gate_at])
        gate, up = gate_up_all[:, gate_at], gate_up_all[:, up_at]
        sigmoid = 1.0 / (1.0 + jnp.exp(-gate))
        d_gate = d_hidden * up * sigmoid * (1.0 + gate * (1.0 - sigmoid))
        d_gate_up_all[:, gate_at] = d_gate.astype(jnp.bfloat16)
        d_gate_up_all[:, up_at] = (d_hidden * (gate * sigmoid)).astype(jnp.bfloat16)
    if not more:
        by_half(out_refs, times_transpose(hidden_here[...], w_down[...]).astype(jnp.bfloat16))
    at_first_step(copies, lambda copy: copy.wait())
    by_half(d_norm_refs, times_transpose(d_gate_up_all[...], w_gate_up[...]).astype(jnp.bfloat16))


def piece_call(kernel, name, k, pieces, me, parts, whole, tiled, fetched, earlier, outs):
    tile, width = sum(x.shape[0] for x in parts) // STEPS, parts[0].shape[1]
    count = len(parts)

    def rows_of(piece):
        return lambda i: (piece * STEPS + i, 0)

    def half_of(span):
        first = 0 if span == "own" else STEPS // 2
        return lambda i: (jnp.clip(i - first, 0, STEPS // 2 - 1), 0)

    sources = [x for arrays, _, _ in fetched for x in arrays]
    first_earlier = 1 + count + len(whole) + len(tiled) + len(sources)
    scratch = []
    for arrays, _, cols in fetched:
        scratch += [pltpu.VMEM((width, cols), jnp.bfloat16), pltpu.SemaphoreType.DMA((len(arrays),))]
    if kernel is project_kernel:
        scratch.append(pltpu.VMEM((tile, width), jnp.bfloat16))
    return pl.pallas_call(
        functools.partial(kernel, count, tuple(where for _, where, _ in fetched), bool(earlier)),
        grid=(STEPS,),
        out_shape=[
            jax.ShapeDtypeStruct(((pieces * STEPS if span == "all" else STEPS // 2) * tile, columns), kind)
            for columns, kind, span in outs
        ],
        in_specs=[
            SMEM,
            *(pl.BlockSpec(x.shape, lambda i: (0, 0)) for x in parts),
            *(pl.BlockSpec(x.shape, lambda i: (0, 0)) for x in whole),
            *(pl.BlockSpec((tile, x.shape[1]), rows_of(piece)) for x, piece in tiled),
            *[ANY] * (len(sources) + len(earlier)),
        ],
        out_specs=[
            pl.BlockSpec((tile, columns), rows_of(k) if span == "all" else half_of(span))
            for columns, kind, span in outs
        ],
        scratch_shapes=scratch,
        input_output_aliases={first_earlier + n: n for n in range(len(earlier))},
        compiler_params=pltpu.CompilerParams(vmem_limit_bytes=60 * 2**20),
        cost_estimate=small_cost(),
        name=f"{name}_{k}",
    )(me, *parts, *whole, *(x for x, _ in tiled), *sources, *earlier)


def assemble_kernel(where, me, *refs):
    sources, whole, sems = refs[: len(where)], refs[len(where)], refs[len(where) + 1]
    copies = fetch(me, where, sources, whole, sems)
    for copy in copies:
        copy.start()
    for copy in copies:
        copy.wait()


def assemble(name, me, arrays, where, rows, cols):
    return pl.pallas_call(
        functools.partial(assemble_kernel, where),
        out_shape=jax.ShapeDtypeStruct((rows, cols), arrays[0].dtype),
        in_specs=[SMEM, *[ANY] * len(arrays)],
        out_specs=VMEM,
        scratch_shapes=[pltpu.SemaphoreType.DMA((len(arrays),))],
        compiler_params=pltpu.CompilerParams(vmem_limit_bytes=60 * 2**20),
        cost_estimate=small_cost(),
        name=name,
    )(me, *arrays)


def flip(x, axis):
    return lax.ppermute(x, axis, FLIP)


CROSS = [(1, 2), (2, 1)]
OUT = [(0, 1), (3, 2), (2, 0), (1, 3)]
BACK = [(1, 0), (2, 3), (0, 2), (3, 1)]


def crossed(x, perm):
    return lax.ppermute(x, ("core", "zh"), perm)


def straight():
    return lax.axis_index("core") == lax.axis_index("zh")


def swap(x):
    return jnp.where(straight(), x, crossed(x, CROSS))


def send_z(w):
    return crossed(w, OUT), crossed(w, CROSS)


def pair_of(w, out, cross):
    zh = lax.axis_index("zh")
    x = jnp.where(straight(), w, cross)
    return jnp.concatenate([jnp.where(zh == 0, x, out), jnp.where(zh == 0, out, x)], axis=0)


def give_z(part):
    zh = lax.axis_index("zh")
    half = part.shape[0] // 2
    upper, lower = part[:half], part[half:]
    return jnp.where(zh == 0, upper, lower), jnp.where(zh == 0, lower, upper)


def sum_z(keep, back, cross):
    return back.astype(jnp.float32) + jnp.where(straight(), keep, cross).astype(jnp.float32)


def shift(x, e, k):
    n = lax.axis_size("zl")
    return lax.ppermute(
        x, ("core", "zl"), [(c * n + l, (c ^ e) * n + (l + k) % n) for c in range(2) for l in range(n)]
    )


def from_near(x, k):
    n = lax.axis_size("zl")
    return lax.ppermute(x, "zl", [((j + k) % n, j) for j in range(n)])


def to_near(x, k):
    n = lax.axis_size("zl")
    return lax.ppermute(x, "zl", [(j, (j + k) % n) for j in range(n)])


def across(x, j):
    n = lax.axis_size("yx")
    return lax.ppermute(x, "yx", [(a, a ^ j) for a in range(n)])


def neighbours(x):
    count = lax.axis_size("yx")
    return [across(x, j) for j in range(1, count if count != 4 else 3)]


def diagonal(taken):
    if lax.axis_size("yx") != 4:
        return []
    half = taken[0].shape[0] // 2
    return [across(taken[1][:half], 1), across(taken[0][half:], 2)]


def blocks_of(own, taken, halves, column=0, source_column=0):
    deep = own.shape[0]
    arrays = [own, *taken, *halves]
    where = [(j, deep, 0, column, source_column) for j in range(1 + len(taken))]
    where += [(3, deep, n * deep // 2, column, source_column) for n in range(len(halves))]
    return arrays, tuple(where)


def whole_weight(w):
    return [w], ((0, 0, 0, 0, 0),)


def block_of(grad, j, columns):
    size = grad.shape[0] // lax.axis_size("yx")
    first = (lax.axis_index("yx") ^ j) * size
    return lax.dynamic_slice(grad, (first, columns[0]), (size, columns[1] - columns[0]))


def send_yx(grad, columns):
    count = lax.axis_size("yx")
    if count != 4:
        return [across(block_of(grad, j, columns), j) for j in range(1, count)]
    far = block_of(grad, 3, columns)
    half = far.shape[0] // 2
    return [across(far[:half], 1), across(far[half:], 2)]


def join_yx(grad, columns, taken):
    if lax.axis_size("yx") != 4:
        return taken, block_of(grad, 0, columns)
    half = taken[0].shape[0]
    one, two = block_of(grad, 1, columns), block_of(grad, 2, columns)
    one = jnp.concatenate([one[:half], one[half:] + taken[1]], axis=0)
    two = jnp.concatenate([two[:half] + taken[0], two[half:]], axis=0)
    return [across(one, 1), across(two, 2)], block_of(grad, 0, columns)


def total_yx(taken, own):
    total = own.astype(jnp.float32)
    for part in taken:
        total = total + part.astype(jnp.float32)
    return total.astype(jnp.bfloat16)


def body(
    tokens,
    cotangent,
    seq_lengths,
    attn_gain,
    q_weight,
    key_projection,
    value_projection,
    out_weight,
    mlp_gain,
    gate_weight,
    up_weight,
    down_weight,
):
    bf16, f32 = jnp.bfloat16, jnp.float32
    core, zl, yx = lax.axis_index("core"), lax.axis_index("zl"), lax.axis_index("yx")
    near = lax.axis_size("zl")
    others = range(1, near)
    rows = tokens.shape[0]
    group_rows = 2 * near * rows
    query_cols, key_cols = q_weight.shape[1], key_projection.shape[1]
    qkv_cols = query_cols + 2 * key_cols
    q_heads, kv_heads = query_cols // HD, key_cols // HD
    hidden_cols = gate_weight.shape[1]
    me = yx.astype(jnp.int32).reshape(1)

    qkv_shard = jnp.concatenate([q_weight, key_projection, value_projection], axis=1)
    gate_up_shard = jnp.concatenate([gate_weight, up_weight], axis=1)
    part_rows = rows // 2
    upper = swap(tokens[:part_rows])
    shard_moved = send_z(qkv_shard)
    lengths = swap(seq_lengths)
    gains = lax.all_gather(jnp.stack([attn_gain, mlp_gain]), ("yx", "core"), axis=1, tiled=True).astype(f32)
    upper, lengths, second_part, out_shard, gains, *shard_moved = stage(
        upper, lengths, tokens[part_rows:], out_weight, gains, *shard_moved
    )
    gain_one, gain_two = gains[0], gains[1]

    upper_far = [from_near(upper, k) for k in others]
    lower = swap(second_part)
    pair = pair_of(qkv_shard, *shard_moved)
    taken = neighbours(pair)
    out_out = crossed(out_shard, OUT)

    subs = jnp.arange(group_rows // SUB, dtype=jnp.int32)
    per_device = rows // SUB
    source, within = subs // per_device, subs % per_device
    there_core, there_zl = (source % 2) ^ core, (source // 2 + zl) % near
    to_order = (there_core * near + there_zl) * per_device + within
    from_order = (((source % near - zl) % near) * 2 + ((source // near) ^ core)) * per_device + within
    place = jnp.concatenate([to_order, from_order])
    row_at, doc_start = document_layout(lengths, group_rows)
    cosine, sine = rotary_tables(row_at - doc_start)

    def bounds(size):
        tile_start = doc_start.reshape(-1, size)
        tile = jnp.arange(group_rows // size, dtype=jnp.int32)
        low = tile_start[:, 0] // size
        return low, jnp.minimum((tile_start[:, -1] + size - 1) // size, tile)

    start_row = jnp.tile(doc_start.reshape(-1, 1, SUB), (1, 1, q_heads // kv_heads))
    layout = (place, *bounds(TILE), cosine, sine, doc_start[:, None])
    layout_back = (place, *bounds(SUB), cosine, sine, start_row)
    lower, out_out, out_shard, *moved = stage(lower, out_out, out_shard, *upper_far, *taken, *layout, *layout_back)
    upper_far, moved = moved[: near - 1], moved[near - 1 :]
    taken, moved = moved[: len(taken)], moved[len(taken) :]
    layout, layout_back = moved[: len(layout)], moved[len(layout) :]

    lower_far = [from_near(lower, k) for k in others]
    own = jnp.concatenate([upper, lower], axis=0)
    own_sib = flip(own, "core")
    out_cross = crossed(out_shard, CROSS)
    blocks = blocks_of(pair, taken, diagonal(taken))
    projecting = [(*blocks, qkv_cols)]
    gain_row = gain_one[None]
    outs = [(tokens.shape[1], bf16, "all"), (qkv_cols, bf16, "all")]
    normed = piece_call(project_kernel, "project", 0, near, me, [own, own_sib], [gain_row], [], projecting, [], outs)
    gate_up_shard, out_cross, down_shard, *moved = stage(gate_up_shard, out_cross, down_weight, *lower_far, *normed)
    lower_far, normed = moved[: near - 1], moved[near - 1 :]

    out_pair = pair_of(out_weight, out_out, out_cross)
    out_far = [from_near(out_pair, k) for k in others]
    down_out = crossed(down_shard, OUT)
    for k in others:
        far = jnp.concatenate([upper_far[k - 1], lower_far[k - 1]], axis=0)
        parts = [far, flip(far, "core")]
        normed = piece_call(project_kernel, "project", k, near, me, parts, [gain_row], [], projecting, normed, outs)
    norm_one, qkv = normed
    gate_up_shard, qkv, out_pair, down_out, *out_far = stage(gate_up_shard, qkv, out_pair, down_out, *out_far)

    gate_up_moved = send_z(gate_up_shard)
    w_out = lax.all_gather(jnp.concatenate([out_pair, *out_far], axis=1), "yx", axis=0, tiled=True)
    context, sums = attend(qkv, near, layout, q_heads, kv_heads)
    cotangent, down_shard, *moved = stage(cotangent, down_shard, *context, *gate_up_moved)
    context, gate_up_moved = moved[:near], moved[near:]

    quarters = [context[0]] + [None] * (near - 1)
    for k in others:
        quarters[near - k] = to_near(context[k], k)
    cot_upper = crossed(cotangent[:part_rows], CROSS)
    down_cross = crossed(down_shard, CROSS)
    pairs = [
        pair_of(*(x[:, n * hidden_cols : (n + 1) * hidden_cols] for x in (gate_up_shard, *gate_up_moved)))
        for n in range(2)
    ]
    gate_taken = neighbours(pairs[0])
    w_project = assemble("assemble_project", me, *blocks, tokens.shape[1], qkv_cols)
    residual = own.astype(f32)
    scale_one = lax.rsqrt(jnp.mean(residual * residual, axis=-1, keepdims=True) + EPSILON)
    up_pair, cotangent, cot_upper, down_cross, w_out, scale_one, w_project, *moved = stage(
        pairs[1], cotangent, cot_upper, down_cross, w_out, scale_one, w_project, *quarters, *gate_taken
    )
    quarters, gate_taken = moved[:near], moved[near:]

    up_taken = neighbours(up_pair)
    gate_halves = diagonal(gate_taken)
    context_all = jnp.concatenate(quarters, axis=1)
    branch_sib = flip(times_transpose(context_all[rows:], w_out).astype(bf16), "core")
    mid = residual + times_transpose(context_all[:rows], w_out) + branch_sib.astype(f32)
    scale_two, norm_two = norm_rows(mid, gain_two)
    norm_two, cotangent, *moved = stage(norm_two, cotangent, *up_taken, *gate_halves)
    up_taken, gate_halves = moved[: len(up_taken)], moved[len(up_taken) :]

    quarter = part_rows // 2
    far_quarters = [[from_near(norm_two[:quarter], k) for k in others]]
    norm_sib = flip(norm_two, "core")
    up_halves = diagonal(up_taken)
    down_pair = pair_of(down_weight, down_out, down_cross)
    norm_two, norm_sib, down_pair, cotangent, *moved = stage(
        norm_two, norm_sib, down_pair, cotangent, *far_quarters[0], *up_halves
    )
    far_quarters[0], up_halves = moved[: near - 1], moved[near - 1 :]

    far_quarters.append([from_near(norm_two[quarter:part_rows], k) for k in others])
    cot_lower = crossed(cotangent[part_rows:], CROSS)
    down_taken = neighbours(down_pair)
    gate_blocks = blocks_of(pairs[0], gate_taken, gate_halves)
    up_blocks = blocks_of(up_pair, up_taken, up_halves, hidden_cols)
    gate_up = ([*gate_blocks[0], *up_blocks[0]], gate_blocks[1] + up_blocks[1], 2 * hidden_cols)
    gate_outs = [(norm_two.shape[1], bf16, "all"), (2 * hidden_cols, f32, "all"), (hidden_cols, bf16, "all")]
    earlier = piece_call(gate_kernel, "gate", 0, near, me, [norm_two, norm_sib], [], [], [gate_up], [], gate_outs)
    norm_two, cotangent, cot_lower, *moved = stage(
        norm_two, cotangent, cot_lower, *far_quarters[1], *down_taken, *earlier
    )
    far_quarters[1], moved = moved[: near - 1], moved[near - 1 :]
    down_taken, earlier = moved[: len(down_taken)], moved[len(down_taken) :]

    lower_far = [from_near(norm_two[part_rows:], k) for k in others]
    cot = jnp.where(straight(), cotangent, jnp.concatenate([cot_upper, cot_lower], axis=0))
    cot_sib = flip(cot, "core")
    cot_upper_far = [from_near(jnp.where(straight(), cotangent[:part_rows], cot_upper), k) for k in others]
    down_halves = diagonal(down_taken)
    down = (*blocks_of(down_pair, down_taken, down_halves), hidden_cols)
    width = norm_two.shape[1]
    outs = [(width, bf16, "all"), (2 * hidden_cols, bf16, "all")]
    halves = [(width, bf16, "own"), (width, bf16, "sibling")]

    def way_back(k, parts, earlier):
        tiled, results = [(gate_up_all, k), (hidden_all, k)], outs + halves * (1 if earlier else 2)
        return piece_call(gate_back_kernel, "gate_back", k, near, me, parts, [], tiled, [gate_up, down], earlier, results)

    def joined(own, sib):
        return own.astype(f32) + flip(sib, "core").astype(f32)

    norm_two_all, gate_up_all, hidden_all = earlier
    grad_all, d_gate_up_all, *near_back = way_back(0, [cot, cot_sib], [])
    cot, *moved = stage(
        cot, norm_two_all, gate_up_all, hidden_all, grad_all, d_gate_up_all, *near_back, *cot_upper_far, *lower_far
    )
    earlier, (grad_all, d_gate_up_all), near_back, moved = moved[:3], moved[3:5], moved[5:9], moved[9:]
    cot_upper_far, lower_far = moved[: near - 1], moved[near - 1 :]

    cot_lower_far = [from_near(cot[part_rows:], k) for k in others]
    out_far = []
    for k in others:
        norm_far = jnp.concatenate([*(x[k - 1] for x in far_quarters), lower_far[k - 1]], axis=0)
        parts = [norm_far, flip(norm_far, "core")]
        *earlier, out_own, out_sib = piece_call(
            gate_kernel, "gate", k, near, me, parts, [], [], [gate_up, down], earlier, gate_outs + halves
        )
        out_far += [out_own, out_sib]
    grad_all, d_gate_up_all, w_project, *moved = stage(
        grad_all, d_gate_up_all, w_project, *near_back, *cot_lower_far, *earlier, *out_far
    )
    near_back, cot_lower_far, moved = moved[:4], moved[4 : near + 3], moved[near + 3 :]
    earlier, out_far = moved[:3], moved[3:]
    norm_two_all, gate_up_all, hidden_all = earlier
    cot_far = [jnp.concatenate(x, axis=0) for x in zip(cot_upper_far, cot_lower_far, strict=True)]
    cot_far_sib = [flip(x, "core") for x in cot_far]
    out_sums = [joined(*out_far[2 * n : 2 * n + 2]).astype(bf16) for n in range(near - 1)]
    moved = stage(*cot_far_sib, *out_sums)
    cot_far_sib, out_sums = moved[: near - 1], moved[near - 1 :]

    out_upper = [to_near(out_sums[k - 1][:part_rows], k) for k in others]
    back = []
    for k in others:
        parts = [cot_far[k - 1], cot_far_sib[k - 1]]
        grad_all, d_gate_up_all, *more = way_back(k, parts, [grad_all, d_gate_up_all])
        back.append(more)
    grad_all, d_gate_up_all, *moved = stage(grad_all, d_gate_up_all, *(x for more in back for x in more), *out_upper)
    far_back, out_upper = moved[: 2 * near - 2], moved[2 * near - 2 :]
    d_norm_sent = [joined(*far_back[2 * n : 2 * n + 2]).astype(bf16) for n in range(near - 1)]
    grad_all, d_gate_up_all, near_own, near_sib, *d_norm_sent = stage(
        grad_all, d_gate_up_all, *near_back[:2], *d_norm_sent
    )

    moved_upper = [to_near(d_norm_sent[k - 1][:part_rows], k) for k in others]
    grad_gate_up = rows_product(norm_two_all, d_gate_up_all).astype(bf16)
    grad_gate_up, grad_all, near_own, near_sib, *moved = stage(
        grad_gate_up, grad_all, near_own, near_sib, *moved_upper, *d_norm_sent
    )
    moved_upper, d_norm_sent = moved[: near - 1], moved[near - 1 :]

    moved_lower = [to_near(d_norm_sent[k - 1][part_rows:], k) for k in others]
    gate_up_part = lax.psum_scatter(grad_gate_up, "yx", scatter_dimension=0, tiled=True)
    d_norm_two = joined(near_own, near_sib)
    grad_down = rows_product(grad_all, hidden_all).astype(bf16)
    grad_down, d_norm_two, *moved = stage(grad_down, d_norm_two, *out_sums, *moved_lower)
    out_sums, moved_lower = moved[: near - 1], moved[near - 1 :]

    out_lower = [to_near(out_sums[k - 1][part_rows:], k) for k in others]
    down_part = lax.psum_scatter(grad_down, "yx", scatter_dimension=0, tiled=True)
    for one, two in zip(moved_upper, moved_lower, strict=True):
        d_norm_two = d_norm_two + jnp.concatenate([one, two], axis=0).astype(f32)
    mid_back, _ = norm_back(mid, scale_two, gain_two, d_norm_two)
    d_mid = cot.astype(f32) + mid_back
    d_attn = d_mid.astype(bf16)
    d_attn_sib = flip(d_attn, "core")
    both = [dot32(x, w_out).astype(bf16) for x in (d_attn, d_attn_sib)]
    d_quarters = [
        jnp.concatenate([x[:, k * query_cols : (k + 1) * query_cols] for x in both], axis=0) for k in range(near)
    ]
    d_attn, d_attn_sib, *moved = stage(d_attn, d_attn_sib, *d_quarters, *out_lower)
    d_quarters, out_lower = moved[:near], moved[near:]

    d_context = [d_quarters[0]] + [None] * (near - 1)
    for k in others:
        d_context[near - k] = to_near(d_quarters[k], k)
    grad_out = rows_product(d_attn, context_all[:rows]) + rows_product(d_attn_sib, context_all[rows:])
    grad_out = grad_out.astype(bf16)
    output_own = mid + joined(*near_back[2:])
    for one, two in zip(out_upper, out_lower, strict=True):
        output_own = output_own + jnp.concatenate([one, two], axis=0).astype(f32)
    output_own = output_own.astype(bf16)
    grad_out, output_own, gate_up_part, *d_context = stage(grad_out, output_own, gate_up_part, *d_context)

    output_crossed = crossed(output_own, CROSS)
    gate_up_keep, gate_up_give = give_z(gate_up_part)
    gate_up_back = crossed(gate_up_give, BACK)
    out_part = lax.psum_scatter(grad_out, "yx", scatter_dimension=0, tiled=True)
    d_qkv = attend_back(list(range(kv_heads)), qkv, d_context, context, sums, [], layout_back, q_heads, kv_heads)
    d_qkv, output_crossed, gate_up_back, gate_up_keep, down_part = stage(
        d_qkv, output_crossed, gate_up_back, gate_up_keep, down_part
    )

    def back_part(k):
        own, sib = (d_qkv[(2 * k + e) * rows : (2 * k + e + 1) * rows] for e in range(2))
        taken = flip(times_transpose(sib, w_project).astype(bf16), "core")
        return times_transpose(own, w_project) + taken.astype(f32)

    gate_up_cross = crossed(gate_up_keep, CROSS)
    d_sent = [back_part(k).astype(bf16) for k in others]
    d_qkv, gate_up_cross, down_part, *d_sent = stage(d_qkv, gate_up_cross, down_part, *d_sent)

    output = jnp.where(straight(), output_own, output_crossed)

    d_upper = [to_near(d_sent[k - 1][:part_rows], k) for k in others]
    down_keep, down_give = give_z(down_part)
    down_home = [crossed(down_give, BACK), crossed(down_keep, CROSS)]
    grad_project = rows_product(norm_one, d_qkv).astype(bf16)
    project_sent = send_yx(grad_project, (0, qkv_cols))
    total = back_part(0)
    total, grad_project, *moved = stage(total, grad_project, *d_upper, *d_sent, *project_sent, *down_home)
    d_upper, d_sent, project_sent, down_home = (
        moved[: near - 1], moved[near - 1 : 2 * near - 2], moved[2 * near - 2 : -2], moved[-2:],
    )

    d_lower = [to_near(d_sent[k - 1][part_rows:], k) for k in others]
    project_rest, project_own = join_yx(grad_project, (0, qkv_cols), project_sent)
    out_part, *moved = stage(out_part, *d_lower, *project_rest)
    d_lower, project_rest = moved[: near - 1], moved[near - 1 :]
    d_moved = [jnp.concatenate(x, axis=0) for x in zip(d_upper, d_lower, strict=True)]
    project_keep, project_give = give_z(total_yx(project_rest, project_own))

    project_home = [crossed(project_give, BACK), crossed(project_keep, CROSS)]
    for part in d_moved:
        total = total + part.astype(f32)
    input_back, _ = norm_back(residual, scale_one, gain_one, total)
    input_own = (d_mid + input_back).astype(bf16)
    out_moved = [to_near(out_part[:, k * query_cols : (k + 1) * query_cols], k) for k in others]
    out_quarter = out_part[:, :query_cols].astype(f32)
    for part in out_moved:
        out_quarter = out_quarter + part.astype(f32)
    out_keep, out_give = give_z(out_quarter.astype(bf16))
    input_own, out_keep, out_give, *project_home = stage(input_own, out_keep, out_give, *project_home)
    out_home = [crossed(out_give, BACK), crossed(out_keep, CROSS)]
    input_grad = jnp.where(straight(), input_own, crossed(input_own, CROSS)).astype(f32)
    grad_project = sum_z(project_keep, *project_home)
    grad_out = sum_z(out_keep, *out_home)
    grad_down = sum_z(down_keep, *down_home)
    grad_gate_up = sum_z(gate_up_keep, gate_up_back, gate_up_cross)
    gain_grads = lax.psum(
        jnp.stack(
            [
                jnp.sum(qkv_shard.astype(f32) * grad_project, axis=1),
                jnp.sum(gate_up_shard.astype(f32) * grad_gate_up, axis=1),
            ]
        ),
        ("zh", "zl"),
    ) / jnp.stack([attn_gain, mlp_gain]).astype(f32)
    return (
        output,
        input_grad,
        gain_grads[0],
        grad_project[:, :query_cols],
        grad_project[:, query_cols : query_cols + key_cols],
        grad_project[:, query_cols + key_cols :],
        grad_out,
        gain_grads[1],
        grad_gate_up[:, :hidden_cols],
        grad_gate_up[:, hidden_cols:],
        grad_down,
    )


def solution(mesh):
    dp, tensor = mesh.shape["dp"], mesh.shape["tensor"]
    fine = Mesh(mesh.devices.reshape(dp // 2, 2, 2, tensor // 2), AXES)
    by_rows, by_dp, by_both = P(AXES, None), P(("yx", "core")), P(("yx", "core"), ("zh", "zl"))
    return jax.shard_map(
        body,
        mesh=fine,
        in_specs=(
            by_rows, by_rows, P(("yx", "core"), None), by_dp, by_both, by_both, by_both, by_both,
            by_dp, by_both, by_both, by_both,
        ),
        out_specs=(
            by_rows, by_rows, by_dp, by_both, by_both, by_both, by_both, by_dp, by_both, by_both, by_both,
        ),
        check_vma=False,
    )
```

```python
import functools
import math

import jax
import jax.numpy as jnp
import numpy as np
from jax import lax
from jax.experimental import pallas as pl
from jax.experimental.pallas import tpu as pltpu
from jax.sharding import Mesh
from jax.sharding import PartitionSpec as P

HD = 96
HALF = HD // 2
PAD = 128
STEPS = 4
SUB = 256
TILE = 512

EPSILON = 1e-05
ROTARY_BASE = 100000.0
MASKED = -1e30
LOG2E = math.log2(math.e)

AXES = ("yx", "core", "zh", "zl")
FLIP = [(0, 1), (1, 0)]


def norm_rows(values, gain):
    row_scale = lax.rsqrt(jnp.mean(values * values, axis=-1, keepdims=True) + EPSILON)
    return (row_scale, (values * row_scale * gain).astype(jnp.bfloat16))


def norm_back(values, row_scale, gain, upstream):
    weighted = upstream * gain
    inner_sum = jnp.mean(weighted * values, axis=-1, keepdims=True)
    grad_in = row_scale * weighted - values * (row_scale * row_scale * row_scale) * inner_sum
    gain_part = jnp.sum(upstream * (values * row_scale), axis=0)
    return (grad_in, gain_part)


def document_layout(lengths, group_rows):
    flat_lengths = lengths.reshape(-1)
    doc_ends = jnp.cumsum(flat_lengths)
    rows = jnp.arange(group_rows, dtype=jnp.int32)
    passed = (rows[:, None] >= doc_ends[None, :]).astype(jnp.int32)
    return (rows, jnp.sum(passed * flat_lengths[None, :], axis=1))


def rotary_tables(positions):
    exponents = jnp.arange(HALF, dtype=jnp.float32) * (2.0 / HD)
    inverse = ROTARY_BASE ** (-exponents)
    angles = positions.astype(jnp.float32)[:, None] * inverse[None, :]
    cosine, sine = jnp.cos(angles), jnp.sin(angles)
    gap = jnp.zeros((positions.shape[0], PAD // 2 - HALF), jnp.float32)
    return (
        jnp.concatenate([cosine, gap, cosine, gap], axis=1),
        jnp.concatenate([-sine, gap, sine, gap], axis=1),
    )


def rows_product(left, right):
    return lax.dot_general(
        left, right, (((0,), (0,)), ((), ())), preferred_element_type=jnp.float32
    )


def times_transpose(left, right):
    return lax.dot_general(
        left, right, (((1,), (1,)), ((), ())), preferred_element_type=jnp.float32
    )


def dot32(left, right):
    return jnp.dot(left, right, preferred_element_type=jnp.float32)


def stage(*values):
    return lax.optimization_barrier(values)


def spread(columns, heads):
    matrix = np.zeros((columns, len(heads) * PAD), np.float32)
    for at, first in enumerate(heads):
        for half in range(2):
            for i in range(HALF):
                matrix[first + half * HALF + i, at * PAD + half * (PAD // 2) + i] = 1.0
    return matrix


def turn(x, cosine, sine):
    return x * cosine + pltpu.roll(x, PAD // 2, 1) * sine


def rows_at(t, size):
    return pl.ds(pl.multiple_of(t * size, size), size)


def forward_kernel(pieces, ratio, *refs):
    place, low, full, cosine, sine, start, spread_in, gather_out = refs[:8]
    heads = spread_in.shape[0]
    refs = refs[8:]
    qkv, context, refs = refs[0], refs[1 : 1 + pieces], refs[1 + pieces :]
    log_sum, refs = refs[:heads], refs[heads:]
    q_s, k_s, v_s, s_s, top_s, acc = refs
    tiles = q_s.shape[0]
    all_subs = qkv.shape[0] // SUB
    piece_subs = all_subs // pieces
    scale = LOG2E * HD ** (-0.5)
    ones_lane = lax.broadcasted_iota(jnp.int32, (SUB, PAD), 1) == PAD - 1

    def prepare(r, carry):
        t = place[r]
        at = rows_at(t, SUB)
        cos_t, sin_t = cosine[at, :], sine[at, :]
        tile, half = t // (TILE // SUB), t % (TILE // SUB)
        for g in range(heads):
            wide = dot32(qkv[rows_at(r, SUB), :], spread_in[g])
            for h in range(ratio):
                query = turn(wide[:, h * PAD : (h + 1) * PAD], cos_t, sin_t) * scale
                first = pl.multiple_of(h * TILE + half * SUB, SUB)
                q_s[tile, g, pl.ds(first, SUB), :] = query.astype(jnp.bfloat16)
            key = turn(wide[:, ratio * PAD : (ratio + 1) * PAD], cos_t, sin_t)
            k_s[g, at, :] = key.astype(jnp.bfloat16)
            value = jnp.where(ones_lane, 1.0, wide[:, (ratio + 1) * PAD :])
            v_s[g, at, :] = value.astype(jnp.bfloat16)
        return carry

    lax.fori_loop(0, all_subs, prepare, 0)

    def query_tile(i, carry):
        starts = jnp.concatenate([start[rows_at(i, TILE), :]] * ratio, axis=0)
        top_s[...] = jnp.full_like(top_s, MASKED)

        def scores(j, masked, diagonal):
            for g in range(heads):
                s = times_transpose(q_s[i, g], k_s[g, rows_at(j, TILE), :])
                if masked:
                    key_at = lax.broadcasted_iota(jnp.int32, s.shape, 1)
                    allowed = key_at + j * TILE >= starts
                    if diagonal:
                        query_at = lax.rem(lax.broadcasted_iota(jnp.int32, s.shape, 0), TILE)
                        allowed = allowed & (key_at <= query_at)
                    s = jnp.where(allowed, s, MASKED)
                s_s[g, j] = s
                peak = s[:, :PAD]
                for c in range(1, TILE // PAD):
                    peak = jnp.maximum(peak, s[:, c * PAD : (c + 1) * PAD])
                top_s[g] = jnp.maximum(top_s[g], peak)

        def loop(first, last, masked):
            def run(j, c):
                scores(j, masked, False)
                return c

            lax.fori_loop(first, last, run, 0)

        loop(low[i], full[i], True)
        loop(full[i], i, False)
        scores(i, True, True)
        tops = [jnp.max(top_s[g], axis=1, keepdims=True) for g in range(heads)]
        acc[...] = jnp.zeros_like(acc)

        def weigh(j, c):
            for g in range(heads):
                p = jnp.exp2(s_s[g, j] - tops[g]).astype(jnp.bfloat16)
                acc[g] += dot32(p, v_s[g, rows_at(j, TILE), :])
            return c

        lax.fori_loop(low[i], i + 1, weigh, 0)
        packed = None
        for g in range(heads):
            total = acc[g][:, PAD - 1 :]
            out = acc[g] * (1.0 / total)
            sums = jnp.broadcast_to(tops[g] + jnp.log(total) * LOG2E, (ratio * TILE, PAD))
            log_sum[g][i] = sums.T[:1, :]
            wide = jnp.concatenate(
                [out[h * TILE : (h + 1) * TILE, :] for h in range(ratio)], axis=1
            ).astype(jnp.bfloat16)
            part = dot32(wide, gather_out[g])
            packed = part if packed is None else packed + part
        subs = tiles * (TILE // SUB)
        for half in range(TILE // SUB):
            r = place[subs + i * (TILE // SUB) + half]
            part = packed[half * SUB : (half + 1) * SUB, :].astype(jnp.bfloat16)
            for k in range(pieces):

                @pl.when(r // piece_subs == k)
                def store(k=k, part=part, r=r):
                    context[k][rows_at(r % piece_subs, SUB), :] = part

        return carry

    lax.fori_loop(0, tiles, query_tile, 0)


def backward_kernel(pieces, ratio, more, *refs):
    place, low, full, cosine, sine, start, refs = *refs[:6], refs[6:]
    heads = refs[0].shape[0]
    spread_in, spread_out, gather_in, refs = *refs[:3], refs[3:]
    log_sum, refs = refs[:heads], refs[heads:]
    d_context, context, qkv, refs = refs[:pieces], refs[pieces : 2 * pieces], refs[2 * pieces], refs[2 * pieces + 1 :]
    earlier, refs = (refs[0], refs[1:]) if more else (None, refs)
    d_qkv, refs = refs[0], refs[1:]
    q_s, k_s, kt_s, v_s, do_s, delta_s, log_s, dq_acc, dk_acc, dv_acc, dq_s = refs
    tiles = q_s.shape[0]
    all_subs = qkv.shape[0] // SUB
    piece_subs = all_subs // pieces
    scale = HD ** (-0.5)
    per_tile = TILE // SUB

    for k in range(pieces):

        def prepare(r, carry, k=k):
            t = place[k * piece_subs + r]
            rel = rows_at(r, SUB)
            at = rows_at(t, SUB)
            cos_t, sin_t = cosine[at, :], sine[at, :]
            for g in range(heads):
                wide = dot32(qkv[rows_at(k * piece_subs + r, SUB), :], spread_in[g])
                d_out = dot32(d_context[k][rel, :], spread_out[g])
                out = dot32(context[k][rel, :], spread_out[g])
                for h in range(ratio):
                    cols = slice(h * PAD, (h + 1) * PAD)
                    rows = slice(h * SUB, (h + 1) * SUB)
                    query = turn(wide[:, cols], cos_t, sin_t) * (scale * LOG2E)
                    q_s[t, g, rows, :] = query.astype(jnp.bfloat16)
                    do_s[t, g, rows, :] = d_out[:, cols].astype(jnp.bfloat16)
                    delta = jnp.sum((d_out[:, cols] * out[:, cols]).T, axis=0, keepdims=True)
                    delta_s[t * heads + g, :, rows] = delta
                    first = pl.multiple_of(h * TILE + t % per_tile * SUB, SUB)
                    log_s[t * heads + g, :, rows] = log_sum[g][t // per_tile, :, pl.ds(first, SUB)]
                key = turn(wide[:, ratio * PAD : (ratio + 1) * PAD], cos_t, sin_t)
                k_s[g, t] = key.astype(jnp.bfloat16)
                kt_s[g, t] = key.T.astype(jnp.bfloat16)
                v_s[g, t] = wide[:, (ratio + 1) * PAD :].astype(jnp.bfloat16)
                dk_acc[g, t] = jnp.zeros((SUB, PAD), jnp.float32)
                dv_acc[g, t] = jnp.zeros((SUB, PAD), jnp.float32)
            return carry

        lax.fori_loop(0, piece_subs, prepare, 0)

    def query_tile(i, carry):
        dq_acc[...] = jnp.zeros_like(dq_acc)

        def step(j, masked, diagonal):
            for g in range(heads):
                queries, d_out = q_s[i, g], do_s[i, g]
                s = times_transpose(k_s[g, j], queries)
                if masked:
                    key_at = lax.broadcasted_iota(jnp.int32, s.shape, 0)
                    allowed = key_at + j * SUB >= start[i]
                    if diagonal:
                        query_at = lax.rem(lax.broadcasted_iota(jnp.int32, s.shape, 1), SUB)
                        allowed = allowed & (key_at <= query_at)
                    s = jnp.where(allowed, s, MASKED)
                p = jnp.exp2(s - log_s[i * heads + g])
                d_p = times_transpose(v_s[g, j], d_out)
                d_s = (p * (d_p - delta_s[i * heads + g])).astype(jnp.bfloat16)
                dv_acc[g, j] += dot32(p.astype(jnp.bfloat16), d_out)
                dk_acc[g, j] += dot32(d_s, queries)
                dq_acc[g] += dot32(kt_s[g, j], d_s)

        def loop(first, last, masked):
            def run(j, c):
                step(j, masked, False)
                return c

            lax.fori_loop(first, last, run, 0)

        loop(low[i], full[i], True)
        loop(full[i], i, False)
        step(i, True, True)
        at = rows_at(i, SUB)
        cos_t, sin_t = cosine[at, :], sine[at, :]
        for g in range(heads):
            grad = dq_acc[g].T * scale
            for h in range(ratio):
                piece = turn(grad[h * SUB : (h + 1) * SUB, :], cos_t, -sin_t)
                dq_s[g, i, :, h * PAD : (h + 1) * PAD] = piece.astype(jnp.bfloat16)
        return carry

    lax.fori_loop(0, tiles, query_tile, 0)

    def finish(r, carry):
        t = place[r]
        at = rows_at(t, SUB)
        rel = rows_at(r, SUB)
        packed = None
        for g in range(heads):
            key = turn(dk_acc[g, t] * (1.0 / LOG2E), cosine[at, :], -sine[at, :])
            wide = jnp.concatenate(
                [dq_s[g, t], key.astype(jnp.bfloat16), dv_acc[g, t].astype(jnp.bfloat16)], axis=1
            )
            part = dot32(wide, gather_in[g])
            packed = part if packed is None else packed + part
        packed = packed.astype(jnp.bfloat16)
        d_qkv[rel, :] = packed + earlier[rel, :] if more else packed
        return carry

    lax.fori_loop(0, all_subs, finish, 0)


SMEM = pl.BlockSpec(memory_space=pltpu.SMEM)
VMEM = pl.BlockSpec(memory_space=pltpu.VMEM)
ANY = pl.BlockSpec(memory_space=pl.ANY)


def small_cost(transcendentals=0):
    return pl.CostEstimate(flops=1 << 20, bytes_accessed=1 << 16, transcendentals=transcendentals)


def head_matrices(head, q_heads, kv_heads):
    ratio = q_heads // kv_heads
    queries = [(head * ratio + r) * HD for r in range(ratio)]
    key, value = (q_heads + head) * HD, (q_heads + kv_heads + head) * HD
    inner = spread((q_heads + 2 * kv_heads) * HD, [*queries, key, value])
    outer = spread(q_heads * HD, queries)
    return jnp.asarray(inner, jnp.bfloat16), jnp.asarray(outer, jnp.bfloat16)


def stacked_matrices(q_heads, kv_heads):
    pairs = [head_matrices(head, q_heads, kv_heads) for head in range(kv_heads)]
    return jnp.stack([inner for inner, _ in pairs]), jnp.stack([outer for _, outer in pairs])


def attend(qkv, pieces, layout, q_heads, kv_heads):
    place, low, full, cosine, sine, start_column = layout
    ratio, rows = q_heads // kv_heads, qkv.shape[0]
    tiles, lanes = rows // TILE, ratio * TILE
    bf16, f32 = jnp.bfloat16, jnp.float32
    inner, outer = stacked_matrices(q_heads, kv_heads)
    outs = pl.pallas_call(
        functools.partial(forward_kernel, pieces, ratio),
        out_shape=[
            *[jax.ShapeDtypeStruct((rows // pieces, q_heads * HD), bf16)] * pieces,
            *[jax.ShapeDtypeStruct((tiles, 1, lanes), f32)] * kv_heads,
        ],
        in_specs=[SMEM] * 3 + [VMEM] * 6,
        out_specs=[VMEM] * (pieces + kv_heads),
        scratch_shapes=[
            pltpu.VMEM((tiles, kv_heads, lanes, PAD), bf16),
            pltpu.VMEM((kv_heads, rows, PAD), bf16),
            pltpu.VMEM((kv_heads, rows, PAD), bf16),
            pltpu.VMEM((kv_heads, tiles, lanes, TILE), f32),
            pltpu.VMEM((kv_heads, lanes, PAD), f32),
            pltpu.VMEM((kv_heads, lanes, PAD), f32),
        ],
        compiler_params=pltpu.CompilerParams(vmem_limit_bytes=60 * 2**20),
        cost_estimate=small_cost(),
        name="attention_forward",
    )(place, low, full, cosine, sine, start_column, inner, jnp.swapaxes(outer, 1, 2), qkv)
    return outs[:pieces], outs[pieces:]


def attend_back(heads, qkv, d_context, context, sums, earlier, layout, q_heads, kv_heads):
    place, low, full, cosine, sine, start_row = layout
    pieces, ratio, rows = len(context), q_heads // kv_heads, qkv.shape[0]
    tiles, lanes, count = rows // SUB, ratio * SUB, len(heads)
    bf16, f32 = jnp.bfloat16, jnp.float32
    inner, outer = stacked_matrices(q_heads, kv_heads)
    inner, outer = inner[heads[0] : heads[0] + count], outer[heads[0] : heads[0] + count]
    return pl.pallas_call(
        functools.partial(backward_kernel, pieces, ratio, bool(earlier)),
        out_shape=jax.ShapeDtypeStruct(qkv.shape, bf16),
        in_specs=[SMEM] * 3 + [VMEM] * (7 + count + 2 * pieces + len(earlier)),
        out_specs=VMEM,
        scratch_shapes=[
            pltpu.VMEM((tiles, count, lanes, PAD), bf16),
            pltpu.VMEM((count, tiles, SUB, PAD), bf16),
            pltpu.VMEM((count, tiles, PAD, SUB), bf16),
            pltpu.VMEM((count, tiles, SUB, PAD), bf16),
            pltpu.VMEM((tiles, count, lanes, PAD), bf16),
            pltpu.VMEM((tiles * count, 1, lanes), f32),
            pltpu.VMEM((tiles * count, 1, lanes), f32),
            pltpu.VMEM((count, PAD, lanes), f32),
            pltpu.VMEM((count, tiles, SUB, PAD), f32),
            pltpu.VMEM((count, tiles, SUB, PAD), f32),
            pltpu.VMEM((count, tiles, SUB, ratio * PAD), bf16),
        ],
        compiler_params=pltpu.CompilerParams(vmem_limit_bytes=60 * 2**20),
        cost_estimate=small_cost(),
        name=f"attention_backward_{heads[0]}",
    )(
        place, low, full, cosine, sine, start_row, inner, outer, jnp.swapaxes(inner, 1, 2),
        *[sums[h] for h in heads], *d_context, *context, qkv, *earlier,
    )


def fetch(me, where, sources, target, sems):
    copies = []
    for n, (source, (j, deep, first, column, taken)) in enumerate(zip(sources, where, strict=True)):
        cols = min(source.shape[1] - taken, target.shape[1] - column)
        at = pl.ds(pl.multiple_of((me[0] ^ j) * deep + first, 16), source.shape[0])
        if cols != source.shape[1]:
            source = source.at[:, taken : taken + cols]
        copies.append(pltpu.make_async_copy(source, target.at[at, column : column + cols], sems.at[n]))
    return copies


def take_rows(parts, target):
    rows = target.shape[0]
    for step in range(STEPS):

        @pl.when(pl.program_id(0) == step)
        def take(step=step):
            at = 0
            for part in parts:
                first, last = max(at, step * rows), min(at + part.shape[0], (step + 1) * rows)
                if first < last:
                    target[first - step * rows : last - step * rows, :] = part[first - at : last - at, :]
                at += part.shape[0]


def at_first_step(copies, what):
    @pl.when(pl.program_id(0) == 0)
    def run():
        for copy in copies:
            what(copy)


def project_kernel(count, where, more, me, *refs):
    parts, gain, refs = refs[:count], refs[count], refs[count + 1 :]
    sources, refs = refs[: len(where[0])], refs[len(where[0]) :]
    norm_all, qkv_all, weight, sems, rows_s = refs[2 if more else 0 :]
    copies = fetch(me, where[0], sources, weight, sems)
    at_first_step(copies, lambda copy: copy.start())
    take_rows(parts, rows_s)
    x = rows_s[...].astype(jnp.float32)
    scale = lax.rsqrt(jnp.mean(x * x, axis=-1, keepdims=True) + EPSILON)
    norm_all[...] = (x * scale * gain[...]).astype(jnp.bfloat16)
    at_first_step(copies, lambda copy: copy.wait())
    qkv_all[...] = dot32(norm_all[...], weight[...]).astype(jnp.bfloat16)


def by_half(refs, value):
    for n, ref in enumerate(refs):

        @pl.when(pl.program_id(0) * 2 // STEPS == n)
        def store(ref=ref):
            ref[...] = value


def gate_kernel(count, where, more, me, *refs):
    parts, refs = refs[:count], refs[count:]
    with_out = len(where) > 1
    sources, refs = refs[: sum(map(len, where))], refs[sum(map(len, where)) :]
    norm_all, gate_up_all, hidden_all, *refs = refs[3 if more else 0 :]
    out_refs, refs = (refs[:2], refs[2:]) if with_out else ((), refs)
    weight, sems, *refs = refs
    hidden_cols = hidden_all.shape[1]
    copies = fetch(me, where[0], sources[: len(where[0])], weight, sems)
    if with_out:
        w_down, down_sems = refs
        copies += fetch(me, where[1], sources[len(where[0]) :], w_down, down_sems)
    at_first_step(copies, lambda copy: copy.start())
    take_rows(parts, norm_all)
    at_first_step(copies, lambda copy: copy.wait())
    x = norm_all[...]
    width = min(512, hidden_cols)
    for at in range(0, hidden_cols, width):
        gate_at = slice(at, at + width)
        up_at = slice(hidden_cols + at, hidden_cols + at + width)
        gate = dot32(x, weight[:, gate_at])
        up = dot32(x, weight[:, up_at])
        gate_up_all[:, gate_at] = gate
        gate_up_all[:, up_at] = up
        hidden_all[:, gate_at] = (gate * (1.0 / (1.0 + jnp.exp(-gate))) * up).astype(jnp.bfloat16)
    if with_out:
        by_half(out_refs, times_transpose(hidden_all[...], w_down[...]).astype(jnp.bfloat16))


def gate_back_kernel(count, where, more, me, *refs):
    parts, gate_up_all, hidden_here, refs = refs[:count], *refs[count : count + 2], refs[count + 2 :]
    gate_up, refs = refs[: len(where[0])], refs[len(where[0]) :]
    down, refs = refs[: len(where[1])], refs[len(where[1]) :]
    grad_all, d_gate_up_all, *refs = refs[2 if more else 0 :]
    d_norm_refs, refs = refs[:2], refs[2:]
    out_refs, refs = ((), refs) if more else (refs[:2], refs[2:])
    w_gate_up, gate_up_sems, w_down, down_sems = refs
    hidden_cols = w_down.shape[1]
    down_copies = fetch(me, where[1], down, w_down, down_sems)
    copies = fetch(me, where[0], gate_up, w_gate_up, gate_up_sems)
    at_first_step(down_copies + copies, lambda copy: copy.start())
    take_rows(parts, grad_all)
    at_first_step(down_copies, lambda copy: copy.wait())
    dy = grad_all[...]
    width = min(512, hidden_cols)
    for at in range(0, hidden_cols, width):
        gate_at = slice(at, at + width)
        up_at = slice(hidden_cols + at, hidden_cols + at + width)
        d_hidden = dot32(dy, w_down[:, gate_at])
        gate, up = gate_up_all[:, gate_at], gate_up_all[:, up_at]
        sigmoid = 1.0 / (1.0 + jnp.exp(-gate))
        d_gate = d_hidden * up * sigmoid * (1.0 + gate * (1.0 - sigmoid))
        d_gate_up_all[:, gate_at] = d_gate.astype(jnp.bfloat16)
        d_gate_up_all[:, up_at] = (d_hidden * (gate * sigmoid)).astype(jnp.bfloat16)
    if not more:
        by_half(out_refs, times_transpose(hidden_here[...], w_down[...]).astype(jnp.bfloat16))
    at_first_step(copies, lambda copy: copy.wait())
    by_half(d_norm_refs, times_transpose(d_gate_up_all[...], w_gate_up[...]).astype(jnp.bfloat16))


def piece_call(kernel, name, k, pieces, me, parts, whole, tiled, fetched, earlier, outs):
    tile, width = sum(x.shape[0] for x in parts) // STEPS, parts[0].shape[1]
    count = len(parts)

    def rows_of(piece):
        return lambda i: (piece * STEPS + i, 0)

    def half_of(span):
        first = 0 if span == "own" else STEPS // 2
        return lambda i: (jnp.clip(i - first, 0, STEPS // 2 - 1), 0)

    sources = [x for arrays, _, _ in fetched for x in arrays]
    first_earlier = 1 + count + len(whole) + len(tiled) + len(sources)
    scratch = []
    for arrays, _, cols in fetched:
        scratch += [pltpu.VMEM((width, cols), jnp.bfloat16), pltpu.SemaphoreType.DMA((len(arrays),))]
    if kernel is project_kernel:
        scratch.append(pltpu.VMEM((tile, width), jnp.bfloat16))
    return pl.pallas_call(
        functools.partial(kernel, count, tuple(where for _, where, _ in fetched), bool(earlier)),
        grid=(STEPS,),
        out_shape=[
            jax.ShapeDtypeStruct(((pieces * STEPS if span == "all" else STEPS // 2) * tile, columns), kind)
            for columns, kind, span in outs
        ],
        in_specs=[
            SMEM,
            *(pl.BlockSpec(x.shape, lambda i: (0, 0)) for x in parts),
            *(pl.BlockSpec(x.shape, lambda i: (0, 0)) for x in whole),
            *(pl.BlockSpec((tile, x.shape[1]), rows_of(piece)) for x, piece in tiled),
            *[ANY] * (len(sources) + len(earlier)),
        ],
        out_specs=[
            pl.BlockSpec((tile, columns), rows_of(k) if span == "all" else half_of(span))
            for columns, kind, span in outs
        ],
        scratch_shapes=scratch,
        input_output_aliases={first_earlier + n: n for n in range(len(earlier))},
        compiler_params=pltpu.CompilerParams(vmem_limit_bytes=60 * 2**20),
        cost_estimate=small_cost(),
        name=f"{name}_{k}",
    )(me, *parts, *whole, *(x for x, _ in tiled), *sources, *earlier)


def assemble_kernel(where, me, *refs):
    sources, whole, sems = refs[: len(where)], refs[len(where)], refs[len(where) + 1]
    copies = fetch(me, where, sources, whole, sems)
    for copy in copies:
        copy.start()
    for copy in copies:
        copy.wait()


def assemble(name, me, arrays, where, rows, cols):
    return pl.pallas_call(
        functools.partial(assemble_kernel, where),
        out_shape=jax.ShapeDtypeStruct((rows, cols), arrays[0].dtype),
        in_specs=[SMEM, *[ANY] * len(arrays)],
        out_specs=VMEM,
        scratch_shapes=[pltpu.SemaphoreType.DMA((len(arrays),))],
        compiler_params=pltpu.CompilerParams(vmem_limit_bytes=60 * 2**20),
        cost_estimate=small_cost(),
        name=name,
    )(me, *arrays)


def flip(x, axis):
    return lax.ppermute(x, axis, FLIP)


CROSS = [(1, 2), (2, 1)]
OUT = [(0, 1), (3, 2), (2, 0), (1, 3)]
BACK = [(1, 0), (2, 3), (0, 2), (3, 1)]


def crossed(x, perm):
    return lax.ppermute(x, ("core", "zh"), perm)


def straight():
    return lax.axis_index("core") == lax.axis_index("zh")


def swap(x):
    return jnp.where(straight(), x, crossed(x, CROSS))


def send_z(w):
    return crossed(w, OUT), crossed(w, CROSS)


def pair_of(w, out, cross):
    zh = lax.axis_index("zh")
    x = jnp.where(straight(), w, cross)
    return jnp.concatenate([jnp.where(zh == 0, x, out), jnp.where(zh == 0, out, x)], axis=0)


def give_z(part):
    zh = lax.axis_index("zh")
    half = part.shape[0] // 2
    upper, lower = part[:half], part[half:]
    return jnp.where(zh == 0, upper, lower), jnp.where(zh == 0, lower, upper)


def sum_z(keep, back, cross):
    return back.astype(jnp.float32) + jnp.where(straight(), keep, cross).astype(jnp.float32)


def shift(x, e, k):
    n = lax.axis_size("zl")
    return lax.ppermute(
        x, ("core", "zl"), [(c * n + l, (c ^ e) * n + (l + k) % n) for c in range(2) for l in range(n)]
    )


def from_near(x, k):
    n = lax.axis_size("zl")
    return lax.ppermute(x, "zl", [((j + k) % n, j) for j in range(n)])


def to_near(x, k):
    n = lax.axis_size("zl")
    return lax.ppermute(x, "zl", [(j, (j + k) % n) for j in range(n)])


def across(x, j):
    n = lax.axis_size("yx")
    return lax.ppermute(x, "yx", [(a, a ^ j) for a in range(n)])


def neighbours(x):
    count = lax.axis_size("yx")
    return [across(x, j) for j in range(1, count if count != 4 else 3)]


def diagonal(taken):
    if lax.axis_size("yx") != 4:
        return []
    half = taken[0].shape[0] // 2
    return [across(taken[1][:half], 1), across(taken[0][half:], 2)]


def blocks_of(own, taken, halves, column=0, source_column=0):
    deep = own.shape[0]
    arrays = [own, *taken, *halves]
    where = [(j, deep, 0, column, source_column) for j in range(1 + len(taken))]
    where += [(3, deep, n * deep // 2, column, source_column) for n in range(len(halves))]
    return arrays, tuple(where)


def whole_weight(w):
    return [w], ((0, 0, 0, 0, 0),)


def block_of(grad, j, columns):
    size = grad.shape[0] // lax.axis_size("yx")
    first = (lax.axis_index("yx") ^ j) * size
    return lax.dynamic_slice(grad, (first, columns[0]), (size, columns[1] - columns[0]))


def send_yx(grad, columns):
    count = lax.axis_size("yx")
    if count != 4:
        return [across(block_of(grad, j, columns), j) for j in range(1, count)]
    far = block_of(grad, 3, columns)
    half = far.shape[0] // 2
    return [across(far[:half], 1), across(far[half:], 2)]


def join_yx(grad, columns, taken):
    if lax.axis_size("yx") != 4:
        return taken, block_of(grad, 0, columns)
    half = taken[0].shape[0]
    one, two = block_of(grad, 1, columns), block_of(grad, 2, columns)
    one = jnp.concatenate([one[:half], one[half:] + taken[1]], axis=0)
    two = jnp.concatenate([two[:half] + taken[0], two[half:]], axis=0)
    return [across(one, 1), across(two, 2)], block_of(grad, 0, columns)


def total_yx(taken, own):
    total = own.astype(jnp.float32)
    for part in taken:
        total = total + part.astype(jnp.float32)
    return total.astype(jnp.bfloat16)


def body(
    tokens,
    cotangent,
    seq_lengths,
    attn_gain,
    q_weight,
    key_projection,
    value_projection,
    out_weight,
    mlp_gain,
    gate_weight,
    up_weight,
    down_weight,
):
    bf16, f32 = jnp.bfloat16, jnp.float32
    core, zl, yx = lax.axis_index("core"), lax.axis_index("zl"), lax.axis_index("yx")
    near = lax.axis_size("zl")
    others = range(1, near)
    rows = tokens.shape[0]
    group_rows = 2 * near * rows
    query_cols, key_cols = q_weight.shape[1], key_projection.shape[1]
    qkv_cols = query_cols + 2 * key_cols
    q_heads, kv_heads = query_cols // HD, key_cols // HD
    hidden_cols = gate_weight.shape[1]
    me = yx.astype(jnp.int32).reshape(1)

    qkv_shard = jnp.concatenate([q_weight, key_projection, value_projection], axis=1)
    gate_up_shard = jnp.concatenate([gate_weight, up_weight], axis=1)
    part_rows = rows // 2
    upper = swap(tokens[:part_rows])
    shard_moved = send_z(qkv_shard)
    lengths = swap(seq_lengths)
    gains = lax.all_gather(jnp.stack([attn_gain, mlp_gain]), ("yx", "core"), axis=1, tiled=True).astype(f32)
    upper, lengths, second_part, out_shard, gains, *shard_moved = stage(
        upper, lengths, tokens[part_rows:], out_weight, gains, *shard_moved
    )
    gain_one, gain_two = gains[0], gains[1]

    upper_far = [from_near(upper, k) for k in others]
    lower = swap(second_part)
    pair = pair_of(qkv_shard, *shard_moved)
    taken = neighbours(pair)
    out_out = crossed(out_shard, OUT)

    subs = jnp.arange(group_rows // SUB, dtype=jnp.int32)
    per_device = rows // SUB
    source, within = subs // per_device, subs % per_device
    there_core, there_zl = (source % 2) ^ core, (source // 2 + zl) % near
    to_order = (there_core * near + there_zl) * per_device + within
    from_order = (((source % near - zl) % near) * 2 + ((source // near) ^ core)) * per_device + within
    place = jnp.concatenate([to_order, from_order])
    row_at, doc_start = document_layout(lengths, group_rows)
    cosine, sine = rotary_tables(row_at - doc_start)

    def bounds(size):
        tile_start = doc_start.reshape(-1, size)
        tile = jnp.arange(group_rows // size, dtype=jnp.int32)
        low = tile_start[:, 0] // size
        return low, jnp.minimum((tile_start[:, -1] + size - 1) // size, tile)

    start_row = jnp.tile(doc_start.reshape(-1, 1, SUB), (1, 1, q_heads // kv_heads))
    layout = (place, *bounds(TILE), cosine, sine, doc_start[:, None])
    layout_back = (place, *bounds(SUB), cosine, sine, start_row)
    lower, out_out, out_shard, *moved = stage(lower, out_out, out_shard, *upper_far, *taken, *layout, *layout_back)
    upper_far, moved = moved[: near - 1], moved[near - 1 :]
    taken, moved = moved[: len(taken)], moved[len(taken) :]
    layout, layout_back = moved[: len(layout)], moved[len(layout) :]

    lower_far = [from_near(lower, k) for k in others]
    own = jnp.concatenate([upper, lower], axis=0)
    own_sib = flip(own, "core")
    out_cross = crossed(out_shard, CROSS)
    blocks = blocks_of(pair, taken, diagonal(taken))
    projecting = [(*blocks, qkv_cols)]
    gain_row = gain_one[None]
    outs = [(tokens.shape[1], bf16, "all"), (qkv_cols, bf16, "all")]
    normed = piece_call(project_kernel, "project", 0, near, me, [own, own_sib], [gain_row], [], projecting, [], outs)
    gate_up_shard, out_cross, down_shard, *moved = stage(gate_up_shard, out_cross, down_weight, *lower_far, *normed)
    lower_far, normed = moved[: near - 1], moved[near - 1 :]

    out_pair = pair_of(out_weight, out_out, out_cross)
    out_far = [from_near(out_pair, k) for k in others]
    down_out = crossed(down_shard, OUT)
    for k in others:
        far = jnp.concatenate([upper_far[k - 1], lower_far[k - 1]], axis=0)
        parts = [far, flip(far, "core")]
        normed = piece_call(project_kernel, "project", k, near, me, parts, [gain_row], [], projecting, normed, outs)
    norm_one, qkv = normed
    gate_up_shard, qkv, out_pair, down_out, *out_far = stage(gate_up_shard, qkv, out_pair, down_out, *out_far)

    gate_up_moved = send_z(gate_up_shard)
    w_out = lax.all_gather(jnp.concatenate([out_pair, *out_far], axis=1), "yx", axis=0, tiled=True)
    context, sums = attend(qkv, near, layout, q_heads, kv_heads)
    cotangent, down_shard, *moved = stage(cotangent, down_shard, *context, *gate_up_moved)
    context, gate_up_moved = moved[:near], moved[near:]

    quarters = [context[0]] + [None] * (near - 1)
    for k in others:
        quarters[near - k] = to_near(context[k], k)
    down_cross = crossed(down_shard, CROSS)
    pairs = [
        pair_of(*(x[:, n * hidden_cols : (n + 1) * hidden_cols] for x in (gate_up_shard, *gate_up_moved)))
        for n in range(2)
    ]
    gate_taken = neighbours(pairs[0])
    w_project = assemble("assemble_project", me, *blocks, tokens.shape[1], qkv_cols)
    residual = own.astype(f32)
    scale_one = lax.rsqrt(jnp.mean(residual * residual, axis=-1, keepdims=True) + EPSILON)
    up_pair, cotangent, down_cross, w_out, scale_one, w_project, *moved = stage(
        pairs[1], cotangent, down_cross, w_out, scale_one, w_project, *quarters, *gate_taken
    )
    quarters, gate_taken = moved[:near], moved[near:]

    up_taken = neighbours(up_pair)
    cot_upper = crossed(cotangent[:part_rows], CROSS)
    context_all = jnp.concatenate(quarters, axis=1)
    branch_sib = flip(times_transpose(context_all[rows:], w_out).astype(bf16), "core")
    mid = residual + times_transpose(context_all[:rows], w_out) + branch_sib.astype(f32)
    scale_two, norm_two = norm_rows(mid, gain_two)
    norm_two, cotangent, cot_upper, *up_taken = stage(norm_two, cotangent, cot_upper, *up_taken)

    upper_far = [from_near(norm_two[:part_rows], k) for k in others]
    gate_halves, up_halves = diagonal(gate_taken), diagonal(up_taken)
    down_pair = pair_of(down_weight, down_out, down_cross)
    norm_two, down_pair, cotangent, *moved = stage(norm_two, down_pair, cotangent, *upper_far, *gate_halves, *up_halves)
    upper_far, moved = moved[: near - 1], moved[near - 1 :]
    gate_halves, up_halves = moved[: len(gate_halves)], moved[len(gate_halves) :]

    lower_far = [from_near(norm_two[part_rows:], k) for k in others]
    norm_sib = flip(norm_two, "core")
    cot_lower = crossed(cotangent[part_rows:], CROSS)
    down_taken = neighbours(down_pair)
    gate_blocks = blocks_of(pairs[0], gate_taken, gate_halves)
    up_blocks = blocks_of(up_pair, up_taken, up_halves, hidden_cols)
    gate_up = ([*gate_blocks[0], *up_blocks[0]], gate_blocks[1] + up_blocks[1], 2 * hidden_cols)
    gate_outs = [(norm_two.shape[1], bf16, "all"), (2 * hidden_cols, f32, "all"), (hidden_cols, bf16, "all")]
    earlier = piece_call(gate_kernel, "gate", 0, near, me, [norm_two, norm_sib], [], [], [gate_up], [], gate_outs)
    cotangent, cot_lower, *moved = stage(cotangent, cot_lower, *lower_far, *down_taken, *earlier)
    lower_far, moved = moved[: near - 1], moved[near - 1 :]
    down_taken, earlier = moved[: len(down_taken)], moved[len(down_taken) :]

    norm_far = [jnp.concatenate(x, axis=0) for x in zip(upper_far, lower_far, strict=True)]
    norm_far_sib = [flip(x, "core") for x in norm_far]
    cot = jnp.where(straight(), cotangent, jnp.concatenate([cot_upper, cot_lower], axis=0))
    cot_sib = flip(cot, "core")
    cot_upper_far = [from_near(jnp.where(straight(), cotangent[:part_rows], cot_upper), k) for k in others]
    down_halves = diagonal(down_taken)
    down = (*blocks_of(down_pair, down_taken, down_halves), hidden_cols)
    width = norm_two.shape[1]
    outs = [(width, bf16, "all"), (2 * hidden_cols, bf16, "all")]
    halves = [(width, bf16, "own"), (width, bf16, "sibling")]

    def way_back(k, parts, earlier):
        tiled, results = [(gate_up_all, k), (hidden_all, k)], outs + halves * (1 if earlier else 2)
        return piece_call(gate_back_kernel, "gate_back", k, near, me, parts, [], tiled, [gate_up, down], earlier, results)

    def joined(own, sib):
        return own.astype(f32) + flip(sib, "core").astype(f32)

    norm_two_all, gate_up_all, hidden_all = earlier
    grad_all, d_gate_up_all, *near_back = way_back(0, [cot, cot_sib], [])
    cot, *moved = stage(
        cot, norm_two_all, gate_up_all, hidden_all, grad_all, d_gate_up_all, *near_back, *cot_upper_far, *norm_far_sib
    )
    earlier, (grad_all, d_gate_up_all), near_back, moved = moved[:3], moved[3:5], moved[5:9], moved[9:]
    cot_upper_far, norm_far_sib = moved[: near - 1], moved[near - 1 :]

    cot_lower_far = [from_near(cot[part_rows:], k) for k in others]
    out_far = []
    for k in others:
        parts = [norm_far[k - 1], norm_far_sib[k - 1]]
        *earlier, out_own, out_sib = piece_call(
            gate_kernel, "gate", k, near, me, parts, [], [], [gate_up, down], earlier, gate_outs + halves
        )
        out_far += [out_own, out_sib]
    grad_all, d_gate_up_all, w_project, *moved = stage(
        grad_all, d_gate_up_all, w_project, *near_back, *cot_lower_far, *earlier, *out_far
    )
    near_back, cot_lower_far, moved = moved[:4], moved[4 : near + 3], moved[near + 3 :]
    earlier, out_far = moved[:3], moved[3:]
    norm_two_all, gate_up_all, hidden_all = earlier
    cot_far = [jnp.concatenate(x, axis=0) for x in zip(cot_upper_far, cot_lower_far, strict=True)]
    cot_far_sib = [flip(x, "core") for x in cot_far]
    out_sums = [joined(*out_far[2 * n : 2 * n + 2]).astype(bf16) for n in range(near - 1)]
    moved = stage(*cot_far_sib, *out_sums)
    cot_far_sib, out_sums = moved[: near - 1], moved[near - 1 :]

    out_upper = [to_near(out_sums[k - 1][:part_rows], k) for k in others]
    back = []
    for k in others:
        parts = [cot_far[k - 1], cot_far_sib[k - 1]]
        grad_all, d_gate_up_all, *more = way_back(k, parts, [grad_all, d_gate_up_all])
        back.append(more)
    grad_all, d_gate_up_all, *moved = stage(grad_all, d_gate_up_all, *(x for more in back for x in more), *out_upper)
    far_back, out_upper = moved[: 2 * near - 2], moved[2 * near - 2 :]
    d_norm_sent = [joined(*far_back[2 * n : 2 * n + 2]).astype(bf16) for n in range(near - 1)]
    grad_all, d_gate_up_all, near_own, near_sib, *d_norm_sent = stage(
        grad_all, d_gate_up_all, *near_back[:2], *d_norm_sent
    )

    moved_upper = [to_near(d_norm_sent[k - 1][:part_rows], k) for k in others]
    grad_gate_up = rows_product(norm_two_all, d_gate_up_all).astype(bf16)
    grad_gate_up, grad_all, near_own, near_sib, *moved = stage(
        grad_gate_up, grad_all, near_own, near_sib, *moved_upper, *d_norm_sent
    )
    moved_upper, d_norm_sent = moved[: near - 1], moved[near - 1 :]

    moved_lower = [to_near(d_norm_sent[k - 1][part_rows:], k) for k in others]
    gate_up_part = lax.psum_scatter(grad_gate_up, "yx", scatter_dimension=0, tiled=True)
    d_norm_two = joined(near_own, near_sib)
    grad_down = rows_product(grad_all, hidden_all).astype(bf16)
    grad_down, d_norm_two, *moved = stage(grad_down, d_norm_two, *out_sums, *moved_lower)
    out_sums, moved_lower = moved[: near - 1], moved[near - 1 :]

    out_lower = [to_near(out_sums[k - 1][part_rows:], k) for k in others]
    down_part = lax.psum_scatter(grad_down, "yx", scatter_dimension=0, tiled=True)
    for one, two in zip(moved_upper, moved_lower, strict=True):
        d_norm_two = d_norm_two + jnp.concatenate([one, two], axis=0).astype(f32)
    mid_back, _ = norm_back(mid, scale_two, gain_two, d_norm_two)
    d_mid = cot.astype(f32) + mid_back
    d_attn = d_mid.astype(bf16)
    d_attn_sib = flip(d_attn, "core")
    both = [dot32(x, w_out).astype(bf16) for x in (d_attn, d_attn_sib)]
    d_quarters = [
        jnp.concatenate([x[:, k * query_cols : (k + 1) * query_cols] for x in both], axis=0) for k in range(near)
    ]
    d_attn, d_attn_sib, *moved = stage(d_attn, d_attn_sib, *d_quarters, *out_lower)
    d_quarters, out_lower = moved[:near], moved[near:]

    d_context = [d_quarters[0]] + [None] * (near - 1)
    for k in others:
        d_context[near - k] = to_near(d_quarters[k], k)
    grad_out = rows_product(d_attn, context_all[:rows]) + rows_product(d_attn_sib, context_all[rows:])
    grad_out = grad_out.astype(bf16)
    output_own = mid + joined(*near_back[2:])
    for one, two in zip(out_upper, out_lower, strict=True):
        output_own = output_own + jnp.concatenate([one, two], axis=0).astype(f32)
    output_own = output_own.astype(bf16)
    grad_out, output_own, gate_up_part, *d_context = stage(grad_out, output_own, gate_up_part, *d_context)

    output_crossed = crossed(output_own, CROSS)
    gate_up_keep, gate_up_give = give_z(gate_up_part)
    gate_up_back = crossed(gate_up_give, BACK)
    out_part = lax.psum_scatter(grad_out, "yx", scatter_dimension=0, tiled=True)
    d_qkv = attend_back(list(range(kv_heads)), qkv, d_context, context, sums, [], layout_back, q_heads, kv_heads)
    d_qkv, output_crossed, gate_up_back, gate_up_keep, down_part = stage(
        d_qkv, output_crossed, gate_up_back, gate_up_keep, down_part
    )

    def back_part(k):
        own, sib = (d_qkv[(2 * k + e) * rows : (2 * k + e + 1) * rows] for e in range(2))
        taken = flip(times_transpose(sib, w_project).astype(bf16), "core")
        return times_transpose(own, w_project) + taken.astype(f32)

    d_sent = [back_part(k).astype(bf16) for k in others]
    d_qkv, gate_up_keep, down_part, *d_sent = stage(d_qkv, gate_up_keep, down_part, *d_sent)

    output = jnp.where(straight(), output_own, output_crossed)

    d_upper = [to_near(d_sent[k - 1][:part_rows], k) for k in others]
    gate_up_cross = crossed(gate_up_keep, CROSS)
    grad_project = rows_product(norm_one, d_qkv).astype(bf16)
    project_sent = send_yx(grad_project, (0, qkv_cols))
    total = back_part(0)
    total, grad_project, gate_up_cross, down_part, *moved = stage(
        total, grad_project, gate_up_cross, down_part, *d_upper, *d_sent, *project_sent
    )
    d_upper, d_sent, project_sent = moved[: near - 1], moved[near - 1 : 2 * near - 2], moved[2 * near - 2 :]

    d_lower = [to_near(d_sent[k - 1][part_rows:], k) for k in others]
    down_keep, down_give = give_z(down_part)
    down_home = [crossed(down_give, BACK), crossed(down_keep, CROSS)]
    project_rest, project_own = join_yx(grad_project, (0, qkv_cols), project_sent)
    out_part, *moved = stage(out_part, *d_lower, *project_rest, *down_home)
    d_lower, project_rest, down_home = moved[: near - 1], moved[near - 1 : -2], moved[-2:]
    d_moved = [jnp.concatenate(x, axis=0) for x in zip(d_upper, d_lower, strict=True)]
    project_keep, project_give = give_z(total_yx(project_rest, project_own))

    project_home = [crossed(project_give, BACK), crossed(project_keep, CROSS)]
    for part in d_moved:
        total = total + part.astype(f32)
    input_back, _ = norm_back(residual, scale_one, gain_one, total)
    input_own = (d_mid + input_back).astype(bf16)
    out_moved = [to_near(out_part[:, k * query_cols : (k + 1) * query_cols], k) for k in others]
    out_quarter = out_part[:, :query_cols].astype(f32)
    for part in out_moved:
        out_quarter = out_quarter + part.astype(f32)
    out_keep, out_give = give_z(out_quarter.astype(bf16))
    input_own, out_keep, out_give, *project_home = stage(input_own, out_keep, out_give, *project_home)
    out_home = [crossed(out_give, BACK), crossed(out_keep, CROSS)]
    input_grad = jnp.where(straight(), input_own, crossed(input_own, CROSS)).astype(f32)
    grad_project = sum_z(project_keep, *project_home)
    grad_out = sum_z(out_keep, *out_home)
    grad_down = sum_z(down_keep, *down_home)
    grad_gate_up = sum_z(gate_up_keep, gate_up_back, gate_up_cross)
    gain_grads = lax.psum(
        jnp.stack(
            [
                jnp.sum(qkv_shard.astype(f32) * grad_project, axis=1),
                jnp.sum(gate_up_shard.astype(f32) * grad_gate_up, axis=1),
            ]
        ),
        ("zh", "zl"),
    ) / jnp.stack([attn_gain, mlp_gain]).astype(f32)
    return (
        output,
        input_grad,
        gain_grads[0],
        grad_project[:, :query_cols],
        grad_project[:, query_cols : query_cols + key_cols],
        grad_project[:, query_cols + key_cols :],
        grad_out,
        gain_grads[1],
        grad_gate_up[:, :hidden_cols],
        grad_gate_up[:, hidden_cols:],
        grad_down,
    )


def solution(mesh):
    dp, tensor = mesh.shape["dp"], mesh.shape["tensor"]
    fine = Mesh(mesh.devices.reshape(dp // 2, 2, 2, tensor // 2), AXES)
    by_rows, by_dp, by_both = P(AXES, None), P(("yx", "core")), P(("yx", "core"), ("zh", "zl"))
    return jax.shard_map(
        body,
        mesh=fine,
        in_specs=(
            by_rows, by_rows, P(("yx", "core"), None), by_dp, by_both, by_both, by_both, by_both,
            by_dp, by_both, by_both, by_both,
        ),
        out_specs=(
            by_rows, by_rows, by_dp, by_both, by_both, by_both, by_both, by_dp, by_both, by_both, by_both,
        ),
        check_vma=False,
    )
```

```python
import functools
import math

import jax
import jax.numpy as jnp
import numpy as np
from jax import lax
from jax.experimental import pallas as pl
from jax.experimental.pallas import tpu as pltpu
from jax.sharding import Mesh
from jax.sharding import PartitionSpec as P

HD = 96
HALF = HD // 2
PAD = 128
STEPS = 4
SUB = 256
TILE = 512

EPSILON = 1e-05
ROTARY_BASE = 100000.0
MASKED = -1e30
LOG2E = math.log2(math.e)

AXES = ("yx", "core", "zh", "zl")
FLIP = [(0, 1), (1, 0)]


def norm_rows(values, gain):
    row_scale = lax.rsqrt(jnp.mean(values * values, axis=-1, keepdims=True) + EPSILON)
    return (row_scale, (values * row_scale * gain).astype(jnp.bfloat16))


def norm_back(values, row_scale, gain, upstream):
    weighted = upstream * gain
    inner_sum = jnp.mean(weighted * values, axis=-1, keepdims=True)
    grad_in = row_scale * weighted - values * (row_scale * row_scale * row_scale) * inner_sum
    gain_part = jnp.sum(upstream * (values * row_scale), axis=0)
    return (grad_in, gain_part)


def document_layout(lengths, group_rows):
    flat_lengths = lengths.reshape(-1)
    doc_ends = jnp.cumsum(flat_lengths)
    rows = jnp.arange(group_rows, dtype=jnp.int32)
    passed = (rows[:, None] >= doc_ends[None, :]).astype(jnp.int32)
    return (rows, jnp.sum(passed * flat_lengths[None, :], axis=1))


def rotary_tables(positions):
    exponents = jnp.arange(HALF, dtype=jnp.float32) * (2.0 / HD)
    inverse = ROTARY_BASE ** (-exponents)
    angles = positions.astype(jnp.float32)[:, None] * inverse[None, :]
    cosine, sine = jnp.cos(angles), jnp.sin(angles)
    gap = jnp.zeros((positions.shape[0], PAD // 2 - HALF), jnp.float32)
    return (
        jnp.concatenate([cosine, gap, cosine, gap], axis=1),
        jnp.concatenate([-sine, gap, sine, gap], axis=1),
    )


def rows_product(left, right):
    return lax.dot_general(
        left, right, (((0,), (0,)), ((), ())), preferred_element_type=jnp.float32
    )


def times_transpose(left, right):
    return lax.dot_general(
        left, right, (((1,), (1,)), ((), ())), preferred_element_type=jnp.float32
    )


def dot32(left, right):
    return jnp.dot(left, right, preferred_element_type=jnp.float32)


def stage(*values):
    return lax.optimization_barrier(values)


def spread(columns, heads):
    matrix = np.zeros((columns, len(heads) * PAD), np.float32)
    for at, first in enumerate(heads):
        for half in range(2):
            for i in range(HALF):
                matrix[first + half * HALF + i, at * PAD + half * (PAD // 2) + i] = 1.0
    return matrix


def turn(x, cosine, sine):
    return x * cosine + pltpu.roll(x, PAD // 2, 1) * sine


def rows_at(t, size):
    return pl.ds(pl.multiple_of(t * size, size), size)


def forward_kernel(pieces, ratio, *refs):
    place, low, full, cosine, sine, start, spread_in, gather_out = refs[:8]
    heads = spread_in.shape[0]
    refs = refs[8:]
    qkv, context, refs = refs[0], refs[1 : 1 + pieces], refs[1 + pieces :]
    log_sum, refs = refs[:heads], refs[heads:]
    q_s, k_s, v_s, s_s, top_s, acc = refs
    tiles = q_s.shape[0]
    all_subs = qkv.shape[0] // SUB
    piece_subs = all_subs // pieces
    scale = LOG2E * HD ** (-0.5)
    ones_lane = lax.broadcasted_iota(jnp.int32, (SUB, PAD), 1) == PAD - 1

    def prepare(r, carry):
        t = place[r]
        at = rows_at(t, SUB)
        cos_t, sin_t = cosine[at, :], sine[at, :]
        tile, half = t // (TILE // SUB), t % (TILE // SUB)
        for g in range(heads):
            wide = dot32(qkv[rows_at(r, SUB), :], spread_in[g])
            for h in range(ratio):
                query = turn(wide[:, h * PAD : (h + 1) * PAD], cos_t, sin_t) * scale
                first = pl.multiple_of(h * TILE + half * SUB, SUB)
                q_s[tile, g, pl.ds(first, SUB), :] = query.astype(jnp.bfloat16)
            key = turn(wide[:, ratio * PAD : (ratio + 1) * PAD], cos_t, sin_t)
            k_s[g, at, :] = key.astype(jnp.bfloat16)
            value = jnp.where(ones_lane, 1.0, wide[:, (ratio + 1) * PAD :])
            v_s[g, at, :] = value.astype(jnp.bfloat16)
        return carry

    lax.fori_loop(0, all_subs, prepare, 0)

    def query_tile(i, carry):
        starts = jnp.concatenate([start[rows_at(i, TILE), :]] * ratio, axis=0)
        top_s[...] = jnp.full_like(top_s, MASKED)

        def scores(j, masked, diagonal):
            for g in range(heads):
                s = times_transpose(q_s[i, g], k_s[g, rows_at(j, TILE), :])
                if masked:
                    key_at = lax.broadcasted_iota(jnp.int32, s.shape, 1)
                    allowed = key_at + j * TILE >= starts
                    if diagonal:
                        query_at = lax.rem(lax.broadcasted_iota(jnp.int32, s.shape, 0), TILE)
                        allowed = allowed & (key_at <= query_at)
                    s = jnp.where(allowed, s, MASKED)
                s_s[g, j] = s
                peak = s[:, :PAD]
                for c in range(1, TILE // PAD):
                    peak = jnp.maximum(peak, s[:, c * PAD : (c + 1) * PAD])
                top_s[g] = jnp.maximum(top_s[g], peak)

        def loop(first, last, masked):
            def run(j, c):
                scores(j, masked, False)
                return c

            lax.fori_loop(first, last, run, 0)

        loop(low[i], full[i], True)
        loop(full[i], i, False)
        scores(i, True, True)
        tops = [jnp.max(top_s[g], axis=1, keepdims=True) for g in range(heads)]
        acc[...] = jnp.zeros_like(acc)

        def weigh(j, c):
            for g in range(heads):
                p = jnp.exp2(s_s[g, j] - tops[g]).astype(jnp.bfloat16)
                acc[g] += dot32(p, v_s[g, rows_at(j, TILE), :])
            return c

        lax.fori_loop(low[i], i + 1, weigh, 0)
        packed = None
        for g in range(heads):
            total = acc[g][:, PAD - 1 :]
            out = acc[g] * (1.0 / total)
            sums = jnp.broadcast_to(tops[g] + jnp.log(total) * LOG2E, (ratio * TILE, PAD))
            log_sum[g][i] = sums.T[:1, :]
            wide = jnp.concatenate(
                [out[h * TILE : (h + 1) * TILE, :] for h in range(ratio)], axis=1
            ).astype(jnp.bfloat16)
            part = dot32(wide, gather_out[g])
            packed = part if packed is None else packed + part
        subs = tiles * (TILE // SUB)
        for half in range(TILE // SUB):
            r = place[subs + i * (TILE // SUB) + half]
            part = packed[half * SUB : (half + 1) * SUB, :].astype(jnp.bfloat16)
            for k in range(pieces):

                @pl.when(r // piece_subs == k)
                def store(k=k, part=part, r=r):
                    context[k][rows_at(r % piece_subs, SUB), :] = part

        return carry

    lax.fori_loop(0, tiles, query_tile, 0)


def backward_kernel(pieces, ratio, more, *refs):
    place, low, full, cosine, sine, start, refs = *refs[:6], refs[6:]
    heads = refs[0].shape[0]
    spread_in, spread_out, gather_in, refs = *refs[:3], refs[3:]
    log_sum, refs = refs[:heads], refs[heads:]
    d_context, context, qkv, refs = refs[:pieces], refs[pieces : 2 * pieces], refs[2 * pieces], refs[2 * pieces + 1 :]
    earlier, refs = (refs[0], refs[1:]) if more else (None, refs)
    d_qkv, refs = refs[0], refs[1:]
    q_s, k_s, kt_s, v_s, do_s, delta_s, log_s, dq_acc, dk_acc, dv_acc, dq_s = refs
    tiles = q_s.shape[0]
    all_subs = qkv.shape[0] // SUB
    piece_subs = all_subs // pieces
    scale = HD ** (-0.5)
    per_tile = TILE // SUB

    for k in range(pieces):

        def prepare(r, carry, k=k):
            t = place[k * piece_subs + r]
            rel = rows_at(r, SUB)
            at = rows_at(t, SUB)
            cos_t, sin_t = cosine[at, :], sine[at, :]
            for g in range(heads):
                wide = dot32(qkv[rows_at(k * piece_subs + r, SUB), :], spread_in[g])
                d_out = dot32(d_context[k][rel, :], spread_out[g])
                out = dot32(context[k][rel, :], spread_out[g])
                for h in range(ratio):
                    cols = slice(h * PAD, (h + 1) * PAD)
                    rows = slice(h * SUB, (h + 1) * SUB)
                    query = turn(wide[:, cols], cos_t, sin_t) * (scale * LOG2E)
                    q_s[t, g, rows, :] = query.astype(jnp.bfloat16)
                    do_s[t, g, rows, :] = d_out[:, cols].astype(jnp.bfloat16)
                    delta = jnp.sum((d_out[:, cols] * out[:, cols]).T, axis=0, keepdims=True)
                    delta_s[t * heads + g, :, rows] = delta
                    first = pl.multiple_of(h * TILE + t % per_tile * SUB, SUB)
                    log_s[t * heads + g, :, rows] = log_sum[g][t // per_tile, :, pl.ds(first, SUB)]
                key = turn(wide[:, ratio * PAD : (ratio + 1) * PAD], cos_t, sin_t)
                k_s[g, t] = key.astype(jnp.bfloat16)
                kt_s[g, t] = key.T.astype(jnp.bfloat16)
                v_s[g, t] = wide[:, (ratio + 1) * PAD :].astype(jnp.bfloat16)
                dk_acc[g, t] = jnp.zeros((SUB, PAD), jnp.float32)
                dv_acc[g, t] = jnp.zeros((SUB, PAD), jnp.float32)
            return carry

        lax.fori_loop(0, piece_subs, prepare, 0)

    def query_tile(i, carry):
        dq_acc[...] = jnp.zeros_like(dq_acc)

        def step(j, masked, diagonal):
            for g in range(heads):
                queries, d_out = q_s[i, g], do_s[i, g]
                s = times_transpose(k_s[g, j], queries)
                if masked:
                    key_at = lax.broadcasted_iota(jnp.int32, s.shape, 0)
                    allowed = key_at + j * SUB >= start[i]
                    if diagonal:
                        query_at = lax.rem(lax.broadcasted_iota(jnp.int32, s.shape, 1), SUB)
                        allowed = allowed & (key_at <= query_at)
                    s = jnp.where(allowed, s, MASKED)
                p = jnp.exp2(s - log_s[i * heads + g])
                d_p = times_transpose(v_s[g, j], d_out)
                d_s = (p * (d_p - delta_s[i * heads + g])).astype(jnp.bfloat16)
                dv_acc[g, j] += dot32(p.astype(jnp.bfloat16), d_out)
                dk_acc[g, j] += dot32(d_s, queries)
                dq_acc[g] += dot32(kt_s[g, j], d_s)

        def loop(first, last, masked):
            def run(j, c):
                step(j, masked, False)
                return c

            lax.fori_loop(first, last, run, 0)

        loop(low[i], full[i], True)
        loop(full[i], i, False)
        step(i, True, True)
        at = rows_at(i, SUB)
        cos_t, sin_t = cosine[at, :], sine[at, :]
        for g in range(heads):
            grad = dq_acc[g].T * scale
            for h in range(ratio):
                piece = turn(grad[h * SUB : (h + 1) * SUB, :], cos_t, -sin_t)
                dq_s[g, i, :, h * PAD : (h + 1) * PAD] = piece.astype(jnp.bfloat16)
        return carry

    lax.fori_loop(0, tiles, query_tile, 0)

    def finish(r, carry):
        t = place[r]
        at = rows_at(t, SUB)
        rel = rows_at(r, SUB)
        packed = None
        for g in range(heads):
            key = turn(dk_acc[g, t] * (1.0 / LOG2E), cosine[at, :], -sine[at, :])
            wide = jnp.concatenate(
                [dq_s[g, t], key.astype(jnp.bfloat16), dv_acc[g, t].astype(jnp.bfloat16)], axis=1
            )
            part = dot32(wide, gather_in[g])
            packed = part if packed is None else packed + part
        packed = packed.astype(jnp.bfloat16)
        d_qkv[rel, :] = packed + earlier[rel, :] if more else packed
        return carry

    lax.fori_loop(0, all_subs, finish, 0)


SMEM = pl.BlockSpec(memory_space=pltpu.SMEM)
VMEM = pl.BlockSpec(memory_space=pltpu.VMEM)
ANY = pl.BlockSpec(memory_space=pl.ANY)


def small_cost(transcendentals=0):
    return pl.CostEstimate(flops=1 << 20, bytes_accessed=1 << 16, transcendentals=transcendentals)


def head_matrices(head, q_heads, kv_heads):
    ratio = q_heads // kv_heads
    queries = [(head * ratio + r) * HD for r in range(ratio)]
    key, value = (q_heads + head) * HD, (q_heads + kv_heads + head) * HD
    inner = spread((q_heads + 2 * kv_heads) * HD, [*queries, key, value])
    outer = spread(q_heads * HD, queries)
    return jnp.asarray(inner, jnp.bfloat16), jnp.asarray(outer, jnp.bfloat16)


def stacked_matrices(q_heads, kv_heads):
    pairs = [head_matrices(head, q_heads, kv_heads) for head in range(kv_heads)]
    return jnp.stack([inner for inner, _ in pairs]), jnp.stack([outer for _, outer in pairs])


def attend(qkv, pieces, layout, q_heads, kv_heads):
    place, low, full, cosine, sine, start_column = layout
    ratio, rows = q_heads // kv_heads, qkv.shape[0]
    tiles, lanes = rows // TILE, ratio * TILE
    bf16, f32 = jnp.bfloat16, jnp.float32
    inner, outer = stacked_matrices(q_heads, kv_heads)
    outs = pl.pallas_call(
        functools.partial(forward_kernel, pieces, ratio),
        out_shape=[
            *[jax.ShapeDtypeStruct((rows // pieces, q_heads * HD), bf16)] * pieces,
            *[jax.ShapeDtypeStruct((tiles, 1, lanes), f32)] * kv_heads,
        ],
        in_specs=[SMEM] * 3 + [VMEM] * 6,
        out_specs=[VMEM] * (pieces + kv_heads),
        scratch_shapes=[
            pltpu.VMEM((tiles, kv_heads, lanes, PAD), bf16),
            pltpu.VMEM((kv_heads, rows, PAD), bf16),
            pltpu.VMEM((kv_heads, rows, PAD), bf16),
            pltpu.VMEM((kv_heads, tiles, lanes, TILE), f32),
            pltpu.VMEM((kv_heads, lanes, PAD), f32),
            pltpu.VMEM((kv_heads, lanes, PAD), f32),
        ],
        compiler_params=pltpu.CompilerParams(vmem_limit_bytes=60 * 2**20),
        cost_estimate=small_cost(),
        name="attention_forward",
    )(place, low, full, cosine, sine, start_column, inner, jnp.swapaxes(outer, 1, 2), qkv)
    return outs[:pieces], outs[pieces:]


def attend_back(heads, qkv, d_context, context, sums, earlier, layout, q_heads, kv_heads):
    place, low, full, cosine, sine, start_row = layout
    pieces, ratio, rows = len(context), q_heads // kv_heads, qkv.shape[0]
    tiles, lanes, count = rows // SUB, ratio * SUB, len(heads)
    bf16, f32 = jnp.bfloat16, jnp.float32
    inner, outer = stacked_matrices(q_heads, kv_heads)
    inner, outer = inner[heads[0] : heads[0] + count], outer[heads[0] : heads[0] + count]
    return pl.pallas_call(
        functools.partial(backward_kernel, pieces, ratio, bool(earlier)),
        out_shape=jax.ShapeDtypeStruct(qkv.shape, bf16),
        in_specs=[SMEM] * 3 + [VMEM] * (7 + count + 2 * pieces + len(earlier)),
        out_specs=VMEM,
        scratch_shapes=[
            pltpu.VMEM((tiles, count, lanes, PAD), bf16),
            pltpu.VMEM((count, tiles, SUB, PAD), bf16),
            pltpu.VMEM((count, tiles, PAD, SUB), bf16),
            pltpu.VMEM((count, tiles, SUB, PAD), bf16),
            pltpu.VMEM((tiles, count, lanes, PAD), bf16),
            pltpu.VMEM((tiles * count, 1, lanes), f32),
            pltpu.VMEM((tiles * count, 1, lanes), f32),
            pltpu.VMEM((count, PAD, lanes), f32),
            pltpu.VMEM((count, tiles, SUB, PAD), f32),
            pltpu.VMEM((count, tiles, SUB, PAD), f32),
            pltpu.VMEM((count, tiles, SUB, ratio * PAD), bf16),
        ],
        compiler_params=pltpu.CompilerParams(vmem_limit_bytes=60 * 2**20),
        cost_estimate=small_cost(),
        name=f"attention_backward_{heads[0]}",
    )(
        place, low, full, cosine, sine, start_row, inner, outer, jnp.swapaxes(inner, 1, 2),
        *[sums[h] for h in heads], *d_context, *context, qkv, *earlier,
    )


def fetch(me, where, sources, target, sems):
    copies = []
    for n, (source, (j, deep, first, column, taken)) in enumerate(zip(sources, where, strict=True)):
        cols = min(source.shape[1] - taken, target.shape[1] - column)
        at = pl.ds(pl.multiple_of((me[0] ^ j) * deep + first, 16), source.shape[0])
        if cols != source.shape[1]:
            source = source.at[:, taken : taken + cols]
        copies.append(pltpu.make_async_copy(source, target.at[at, column : column + cols], sems.at[n]))
    return copies


def take_rows(parts, target):
    rows = target.shape[0]
    for step in range(STEPS):

        @pl.when(pl.program_id(0) == step)
        def take(step=step):
            at = 0
            for part in parts:
                first, last = max(at, step * rows), min(at + part.shape[0], (step + 1) * rows)
                if first < last:
                    target[first - step * rows : last - step * rows, :] = part[first - at : last - at, :]
                at += part.shape[0]


def at_first_step(copies, what):
    @pl.when(pl.program_id(0) == 0)
    def run():
        for copy in copies:
            what(copy)


def project_kernel(count, where, more, me, *refs):
    parts, gain, refs = refs[:count], refs[count], refs[count + 1 :]
    sources, refs = refs[: len(where[0])], refs[len(where[0]) :]
    norm_all, qkv_all, weight, sems, rows_s = refs[2 if more else 0 :]
    copies = fetch(me, where[0], sources, weight, sems)
    at_first_step(copies, lambda copy: copy.start())
    take_rows(parts, rows_s)
    x = rows_s[...].astype(jnp.float32)
    scale = lax.rsqrt(jnp.mean(x * x, axis=-1, keepdims=True) + EPSILON)
    norm_all[...] = (x * scale * gain[...]).astype(jnp.bfloat16)
    at_first_step(copies, lambda copy: copy.wait())
    qkv_all[...] = dot32(norm_all[...], weight[...]).astype(jnp.bfloat16)


def by_half(refs, value):
    for n, ref in enumerate(refs):

        @pl.when(pl.program_id(0) * 2 // STEPS == n)
        def store(ref=ref):
            ref[...] = value


def gate_kernel(count, where, more, me, *refs):
    parts, refs = refs[:count], refs[count:]
    with_out = len(where) > 1
    sources, refs = refs[: sum(map(len, where))], refs[sum(map(len, where)) :]
    norm_all, gate_up_all, hidden_all, *refs = refs[3 if more else 0 :]
    out_refs, refs = (refs[:2], refs[2:]) if with_out else ((), refs)
    weight, sems, *refs = refs
    hidden_cols = hidden_all.shape[1]
    copies = fetch(me, where[0], sources[: len(where[0])], weight, sems)
    if with_out:
        w_down, down_sems = refs
        copies += fetch(me, where[1], sources[len(where[0]) :], w_down, down_sems)
    at_first_step(copies, lambda copy: copy.start())
    take_rows(parts, norm_all)
    at_first_step(copies, lambda copy: copy.wait())
    x = norm_all[...]
    width = min(512, hidden_cols)
    for at in range(0, hidden_cols, width):
        gate_at = slice(at, at + width)
        up_at = slice(hidden_cols + at, hidden_cols + at + width)
        gate = dot32(x, weight[:, gate_at])
        up = dot32(x, weight[:, up_at])
        gate_up_all[:, gate_at] = gate
        gate_up_all[:, up_at] = up
        hidden_all[:, gate_at] = (gate * (1.0 / (1.0 + jnp.exp(-gate))) * up).astype(jnp.bfloat16)
    if with_out:
        by_half(out_refs, times_transpose(hidden_all[...], w_down[...]).astype(jnp.bfloat16))


def gate_back_kernel(count, where, more, me, *refs):
    parts, gate_up_all, hidden_here, refs = refs[:count], *refs[count : count + 2], refs[count + 2 :]
    gate_up, refs = refs[: len(where[0])], refs[len(where[0]) :]
    down, refs = refs[: len(where[1])], refs[len(where[1]) :]
    grad_all, d_gate_up_all, *refs = refs[2 if more else 0 :]
    d_norm_refs, refs = refs[:2], refs[2:]
    out_refs, refs = ((), refs) if more else (refs[:2], refs[2:])
    w_gate_up, gate_up_sems, w_down, down_sems = refs
    hidden_cols = w_down.shape[1]
    down_copies = fetch(me, where[1], down, w_down, down_sems)
    copies = fetch(me, where[0], gate_up, w_gate_up, gate_up_sems)
    at_first_step(down_copies + copies, lambda copy: copy.start())
    take_rows(parts, grad_all)
    at_first_step(down_copies, lambda copy: copy.wait())
    dy = grad_all[...]
    width = min(512, hidden_cols)
    for at in range(0, hidden_cols, width):
        gate_at = slice(at, at + width)
        up_at = slice(hidden_cols + at, hidden_cols + at + width)
        d_hidden = dot32(dy, w_down[:, gate_at])
        gate, up = gate_up_all[:, gate_at], gate_up_all[:, up_at]
        sigmoid = 1.0 / (1.0 + jnp.exp(-gate))
        d_gate = d_hidden * up * sigmoid * (1.0 + gate * (1.0 - sigmoid))
        d_gate_up_all[:, gate_at] = d_gate.astype(jnp.bfloat16)
        d_gate_up_all[:, up_at] = (d_hidden * (gate * sigmoid)).astype(jnp.bfloat16)
    if not more:
        by_half(out_refs, times_transpose(hidden_here[...], w_down[...]).astype(jnp.bfloat16))
    at_first_step(copies, lambda copy: copy.wait())
    by_half(d_norm_refs, times_transpose(d_gate_up_all[...], w_gate_up[...]).astype(jnp.bfloat16))


def piece_call(kernel, name, k, pieces, me, parts, whole, tiled, fetched, earlier, outs):
    tile, width = sum(x.shape[0] for x in parts) // STEPS, parts[0].shape[1]
    count = len(parts)

    def rows_of(piece):
        return lambda i: (piece * STEPS + i, 0)

    def half_of(span):
        first = 0 if span == "own" else STEPS // 2
        return lambda i: (jnp.clip(i - first, 0, STEPS // 2 - 1), 0)

    sources = [x for arrays, _, _ in fetched for x in arrays]
    first_earlier = 1 + count + len(whole) + len(tiled) + len(sources)
    scratch = []
    for arrays, _, cols in fetched:
        scratch += [pltpu.VMEM((width, cols), jnp.bfloat16), pltpu.SemaphoreType.DMA((len(arrays),))]
    if kernel is project_kernel:
        scratch.append(pltpu.VMEM((tile, width), jnp.bfloat16))
    return pl.pallas_call(
        functools.partial(kernel, count, tuple(where for _, where, _ in fetched), bool(earlier)),
        grid=(STEPS,),
        out_shape=[
            jax.ShapeDtypeStruct(((pieces * STEPS if span == "all" else STEPS // 2) * tile, columns), kind)
            for columns, kind, span in outs
        ],
        in_specs=[
            SMEM,
            *(pl.BlockSpec(x.shape, lambda i: (0, 0)) for x in parts),
            *(pl.BlockSpec(x.shape, lambda i: (0, 0)) for x in whole),
            *(pl.BlockSpec((tile, x.shape[1]), rows_of(piece)) for x, piece in tiled),
            *[ANY] * (len(sources) + len(earlier)),
        ],
        out_specs=[
            pl.BlockSpec((tile, columns), rows_of(k) if span == "all" else half_of(span))
            for columns, kind, span in outs
        ],
        scratch_shapes=scratch,
        input_output_aliases={first_earlier + n: n for n in range(len(earlier))},
        compiler_params=pltpu.CompilerParams(vmem_limit_bytes=60 * 2**20),
        cost_estimate=small_cost(),
        name=f"{name}_{k}",
    )(me, *parts, *whole, *(x for x, _ in tiled), *sources, *earlier)


def assemble_kernel(where, me, *refs):
    sources, whole, sems = refs[: len(where)], refs[len(where)], refs[len(where) + 1]
    copies = fetch(me, where, sources, whole, sems)
    for copy in copies:
        copy.start()
    for copy in copies:
        copy.wait()


def assemble(name, me, arrays, where, rows, cols):
    return pl.pallas_call(
        functools.partial(assemble_kernel, where),
        out_shape=jax.ShapeDtypeStruct((rows, cols), arrays[0].dtype),
        in_specs=[SMEM, *[ANY] * len(arrays)],
        out_specs=VMEM,
        scratch_shapes=[pltpu.SemaphoreType.DMA((len(arrays),))],
        compiler_params=pltpu.CompilerParams(vmem_limit_bytes=60 * 2**20),
        cost_estimate=small_cost(),
        name=name,
    )(me, *arrays)


def flip(x, axis):
    return lax.ppermute(x, axis, FLIP)


CROSS = [(1, 2), (2, 1)]
OUT = [(0, 1), (3, 2), (2, 0), (1, 3)]
BACK = [(1, 0), (2, 3), (0, 2), (3, 1)]


def crossed(x, perm):
    return lax.ppermute(x, ("core", "zh"), perm)


def straight():
    return lax.axis_index("core") == lax.axis_index("zh")


def swap(x):
    return jnp.where(straight(), x, crossed(x, CROSS))


def send_z(w):
    return crossed(w, OUT), crossed(w, CROSS)


def pair_of(w, out, cross):
    zh = lax.axis_index("zh")
    x = jnp.where(straight(), w, cross)
    return jnp.concatenate([jnp.where(zh == 0, x, out), jnp.where(zh == 0, out, x)], axis=0)


def give_z(part):
    zh = lax.axis_index("zh")
    half = part.shape[0] // 2
    upper, lower = part[:half], part[half:]
    return jnp.where(zh == 0, upper, lower), jnp.where(zh == 0, lower, upper)


def sum_z(keep, back, cross):
    return back.astype(jnp.float32) + jnp.where(straight(), keep, cross).astype(jnp.float32)


def shift(x, e, k):
    n = lax.axis_size("zl")
    return lax.ppermute(
        x, ("core", "zl"), [(c * n + l, (c ^ e) * n + (l + k) % n) for c in range(2) for l in range(n)]
    )


def from_near(x, k):
    n = lax.axis_size("zl")
    return lax.ppermute(x, "zl", [((j + k) % n, j) for j in range(n)])


def to_near(x, k):
    n = lax.axis_size("zl")
    return lax.ppermute(x, "zl", [(j, (j + k) % n) for j in range(n)])


def across(x, j):
    n = lax.axis_size("yx")
    return lax.ppermute(x, "yx", [(a, a ^ j) for a in range(n)])


def neighbours(x):
    count = lax.axis_size("yx")
    return [across(x, j) for j in range(1, count if count != 4 else 3)]


def diagonal(taken):
    if lax.axis_size("yx") != 4:
        return []
    half = taken[0].shape[0] // 2
    return [across(taken[1][:half], 1), across(taken[0][half:], 2)]


def blocks_of(own, taken, halves, column=0, source_column=0):
    deep = own.shape[0]
    arrays = [own, *taken, *halves]
    where = [(j, deep, 0, column, source_column) for j in range(1 + len(taken))]
    where += [(3, deep, n * deep // 2, column, source_column) for n in range(len(halves))]
    return arrays, tuple(where)


def whole_weight(w):
    return [w], ((0, 0, 0, 0, 0),)


def block_of(grad, j, columns):
    size = grad.shape[0] // lax.axis_size("yx")
    first = (lax.axis_index("yx") ^ j) * size
    return lax.dynamic_slice(grad, (first, columns[0]), (size, columns[1] - columns[0]))


def send_yx(grad, columns):
    count = lax.axis_size("yx")
    if count != 4:
        return [across(block_of(grad, j, columns), j) for j in range(1, count)]
    far = block_of(grad, 3, columns)
    half = far.shape[0] // 2
    return [across(far[:half], 1), across(far[half:], 2)]


def join_yx(grad, columns, taken):
    if lax.axis_size("yx") != 4:
        return taken, block_of(grad, 0, columns)
    half = taken[0].shape[0]
    one, two = block_of(grad, 1, columns), block_of(grad, 2, columns)
    one = jnp.concatenate([one[:half], one[half:] + taken[1]], axis=0)
    two = jnp.concatenate([two[:half] + taken[0], two[half:]], axis=0)
    return [across(one, 1), across(two, 2)], block_of(grad, 0, columns)


def total_yx(taken, own):
    total = own.astype(jnp.float32)
    for part in taken:
        total = total + part.astype(jnp.float32)
    return total.astype(jnp.bfloat16)


def body(
    tokens,
    cotangent,
    seq_lengths,
    attn_gain,
    q_weight,
    key_projection,
    value_projection,
    out_weight,
    mlp_gain,
    gate_weight,
    up_weight,
    down_weight,
):
    bf16, f32 = jnp.bfloat16, jnp.float32
    core, zl, yx = lax.axis_index("core"), lax.axis_index("zl"), lax.axis_index("yx")
    near = lax.axis_size("zl")
    others = range(1, near)
    rows = tokens.shape[0]
    group_rows = 2 * near * rows
    query_cols, key_cols = q_weight.shape[1], key_projection.shape[1]
    qkv_cols = query_cols + 2 * key_cols
    q_heads, kv_heads = query_cols // HD, key_cols // HD
    hidden_cols = gate_weight.shape[1]
    me = yx.astype(jnp.int32).reshape(1)

    qkv_shard = jnp.concatenate([q_weight, key_projection, value_projection], axis=1)
    gate_up_shard = jnp.concatenate([gate_weight, up_weight], axis=1)
    part_rows = rows // 2
    upper = swap(tokens[:part_rows])
    shard_moved = send_z(qkv_shard)
    lengths = swap(seq_lengths)
    gains = lax.all_gather(jnp.stack([attn_gain, mlp_gain]), ("yx", "core"), axis=1, tiled=True).astype(f32)
    upper, lengths, second_part, out_shard, gains, *shard_moved = stage(
        upper, lengths, tokens[part_rows:], out_weight, gains, *shard_moved
    )
    gain_one, gain_two = gains[0], gains[1]

    upper_far = [from_near(upper, k) for k in others]
    lower = swap(second_part)
    pair = pair_of(qkv_shard, *shard_moved)
    taken = neighbours(pair)
    out_out = crossed(out_shard, OUT)

    subs = jnp.arange(group_rows // SUB, dtype=jnp.int32)
    per_device = rows // SUB
    source, within = subs // per_device, subs % per_device
    there_core, there_zl = (source % 2) ^ core, (source // 2 + zl) % near
    to_order = (there_core * near + there_zl) * per_device + within
    from_order = (((source % near - zl) % near) * 2 + ((source // near) ^ core)) * per_device + within
    place = jnp.concatenate([to_order, from_order])
    row_at, doc_start = document_layout(lengths, group_rows)
    cosine, sine = rotary_tables(row_at - doc_start)

    def bounds(size):
        tile_start = doc_start.reshape(-1, size)
        tile = jnp.arange(group_rows // size, dtype=jnp.int32)
        low = tile_start[:, 0] // size
        return low, jnp.minimum((tile_start[:, -1] + size - 1) // size, tile)

    start_row = jnp.tile(doc_start.reshape(-1, 1, SUB), (1, 1, q_heads // kv_heads))
    layout = (place, *bounds(TILE), cosine, sine, doc_start[:, None])
    layout_back = (place, *bounds(SUB), cosine, sine, start_row)
    lower, out_out, out_shard, *moved = stage(lower, out_out, out_shard, *upper_far, *taken, *layout, *layout_back)
    upper_far, moved = moved[: near - 1], moved[near - 1 :]
    taken, moved = moved[: len(taken)], moved[len(taken) :]
    layout, layout_back = moved[: len(layout)], moved[len(layout) :]

    lower_far = [from_near(lower, k) for k in others]
    own = jnp.concatenate([upper, lower], axis=0)
    own_sib = flip(own, "core")
    out_cross = crossed(out_shard, CROSS)
    blocks = blocks_of(pair, taken, diagonal(taken))
    projecting = [(*blocks, qkv_cols)]
    gain_row = gain_one[None]
    outs = [(tokens.shape[1], bf16, "all"), (qkv_cols, bf16, "all")]
    normed = piece_call(project_kernel, "project", 0, near, me, [own, own_sib], [gain_row], [], projecting, [], outs)
    gate_up_shard, out_cross, down_shard, *moved = stage(gate_up_shard, out_cross, down_weight, *lower_far, *normed)
    lower_far, normed = moved[: near - 1], moved[near - 1 :]

    out_pair = pair_of(out_weight, out_out, out_cross)
    out_far = [from_near(out_pair, k) for k in others]
    down_out = crossed(down_shard, OUT)
    for k in others:
        far = jnp.concatenate([upper_far[k - 1], lower_far[k - 1]], axis=0)
        parts = [far, flip(far, "core")]
        normed = piece_call(project_kernel, "project", k, near, me, parts, [gain_row], [], projecting, normed, outs)
    norm_one, qkv = normed
    gate_up_shard, qkv, out_pair, down_out, *out_far = stage(gate_up_shard, qkv, out_pair, down_out, *out_far)

    gate_up_moved = send_z(gate_up_shard)
    w_out = lax.all_gather(jnp.concatenate([out_pair, *out_far], axis=1), "yx", axis=0, tiled=True)
    context, sums = attend(qkv, near, layout, q_heads, kv_heads)
    cotangent, down_shard, *moved = stage(cotangent, down_shard, *context, *gate_up_moved)
    context, gate_up_moved = moved[:near], moved[near:]

    quarters = [context[0]] + [None] * (near - 1)
    for k in others:
        quarters[near - k] = to_near(context[k], k)
    down_cross = crossed(down_shard, CROSS)
    gate_up_pair = pair_of(gate_up_shard, *gate_up_moved)
    gate_up_taken = neighbours(gate_up_pair)
    w_project = assemble("assemble_project", me, *blocks, tokens.shape[1], qkv_cols)
    residual = own.astype(f32)
    scale_one = lax.rsqrt(jnp.mean(residual * residual, axis=-1, keepdims=True) + EPSILON)
    cotangent, down_cross, w_out, scale_one, w_project, *moved = stage(
        cotangent, down_cross, w_out, scale_one, w_project, *quarters, *gate_up_taken
    )
    quarters, gate_up_taken = moved[:near], moved[near:]

    gate_up_halves = diagonal(gate_up_taken)
    cot_upper = crossed(cotangent[:part_rows], CROSS)
    context_all = jnp.concatenate(quarters, axis=1)
    branch_sib = flip(times_transpose(context_all[rows:], w_out).astype(bf16), "core")
    mid = residual + times_transpose(context_all[:rows], w_out) + branch_sib.astype(f32)
    scale_two, norm_two = norm_rows(mid, gain_two)
    down_pair = pair_of(down_weight, down_out, down_cross)
    norm_two, cotangent, cot_upper, down_pair, *gate_up_halves = stage(
        norm_two, cotangent, cot_upper, down_pair, *gate_up_halves
    )

    upper_far = [from_near(norm_two[:part_rows], k) for k in others]
    norm_sib = flip(norm_two, "core")
    cot_lower = crossed(cotangent[part_rows:], CROSS)
    down_taken = neighbours(down_pair)
    gate_up = (*blocks_of(gate_up_pair, gate_up_taken, gate_up_halves), 2 * hidden_cols)
    gate_outs = [(norm_two.shape[1], bf16, "all"), (2 * hidden_cols, f32, "all"), (hidden_cols, bf16, "all")]
    earlier = piece_call(gate_kernel, "gate", 0, near, me, [norm_two, norm_sib], [], [], [gate_up], [], gate_outs)
    norm_two, cotangent, cot_lower, *moved = stage(norm_two, cotangent, cot_lower, *upper_far, *down_taken, *earlier)
    upper_far, moved = moved[: near - 1], moved[near - 1 :]
    down_taken, earlier = moved[: len(down_taken)], moved[len(down_taken) :]

    lower_far = [from_near(norm_two[part_rows:], k) for k in others]
    cot = jnp.where(straight(), cotangent, jnp.concatenate([cot_upper, cot_lower], axis=0))
    cot_sib = flip(cot, "core")
    cot_upper_far = [from_near(jnp.where(straight(), cotangent[:part_rows], cot_upper), k) for k in others]
    down_halves = diagonal(down_taken)
    down = (*blocks_of(down_pair, down_taken, down_halves), hidden_cols)
    width = norm_two.shape[1]
    outs = [(width, bf16, "all"), (2 * hidden_cols, bf16, "all")]
    halves = [(width, bf16, "own"), (width, bf16, "sibling")]

    def way_back(k, parts, earlier):
        tiled, results = [(gate_up_all, k), (hidden_all, k)], outs + halves * (1 if earlier else 2)
        return piece_call(gate_back_kernel, "gate_back", k, near, me, parts, [], tiled, [gate_up, down], earlier, results)

    def joined(own, sib):
        return own.astype(f32) + flip(sib, "core").astype(f32)

    norm_two_all, gate_up_all, hidden_all = earlier
    grad_all, d_gate_up_all, *near_back = way_back(0, [cot, cot_sib], [])
    cot, *moved = stage(
        cot, norm_two_all, gate_up_all, hidden_all, grad_all, d_gate_up_all, *near_back, *cot_upper_far, *lower_far
    )
    earlier, (grad_all, d_gate_up_all), near_back, moved = moved[:3], moved[3:5], moved[5:9], moved[9:]
    cot_upper_far, lower_far = moved[: near - 1], moved[near - 1 :]

    cot_lower_far = [from_near(cot[part_rows:], k) for k in others]
    out_far = []
    for k in others:
        norm_far = jnp.concatenate([upper_far[k - 1], lower_far[k - 1]], axis=0)
        parts = [norm_far, flip(norm_far, "core")]
        *earlier, out_own, out_sib = piece_call(
            gate_kernel, "gate", k, near, me, parts, [], [], [gate_up, down], earlier, gate_outs + halves
        )
        out_far += [out_own, out_sib]
    grad_all, d_gate_up_all, w_project, *moved = stage(
        grad_all, d_gate_up_all, w_project, *near_back, *cot_lower_far, *earlier, *out_far
    )
    near_back, cot_lower_far, moved = moved[:4], moved[4 : near + 3], moved[near + 3 :]
    earlier, out_far = moved[:3], moved[3:]
    norm_two_all, gate_up_all, hidden_all = earlier
    cot_far = [jnp.concatenate(x, axis=0) for x in zip(cot_upper_far, cot_lower_far, strict=True)]
    cot_far_sib = [flip(x, "core") for x in cot_far]
    out_sums = [joined(*out_far[2 * n : 2 * n + 2]).astype(bf16) for n in range(near - 1)]
    moved = stage(*cot_far_sib, *out_sums)
    cot_far_sib, out_sums = moved[: near - 1], moved[near - 1 :]

    out_upper = [to_near(out_sums[k - 1][:part_rows], k) for k in others]
    back = []
    for k in others:
        parts = [cot_far[k - 1], cot_far_sib[k - 1]]
        grad_all, d_gate_up_all, *more = way_back(k, parts, [grad_all, d_gate_up_all])
        back.append(more)
    grad_all, d_gate_up_all, *moved = stage(
        grad_all, d_gate_up_all, *(x for more in back for x in more), *out_upper, *out_sums
    )
    far_back, moved = moved[: 2 * near - 2], moved[2 * near - 2 :]
    out_upper, out_sums = moved[: near - 1], moved[near - 1 :]
    last = part_rows + part_rows // 2
    out_third = [to_near(out_sums[k - 1][part_rows:last], k) for k in others]
    d_norm_sent = [joined(*far_back[2 * n : 2 * n + 2]).astype(bf16) for n in range(near - 1)]
    grad_all, d_gate_up_all, near_own, near_sib, *moved = stage(
        grad_all, d_gate_up_all, *near_back[:2], *d_norm_sent, *out_third
    )
    d_norm_sent, out_third = moved[: near - 1], moved[near - 1 :]

    moved_upper = [to_near(d_norm_sent[k - 1][:part_rows], k) for k in others]
    grad_gate_up = rows_product(norm_two_all, d_gate_up_all).astype(bf16)
    grad_gate_up, grad_all, near_own, near_sib, *moved = stage(
        grad_gate_up, grad_all, near_own, near_sib, *moved_upper, *d_norm_sent
    )
    moved_upper, d_norm_sent = moved[: near - 1], moved[near - 1 :]

    moved_lower = [to_near(d_norm_sent[k - 1][part_rows:], k) for k in others]
    gate_up_part = lax.psum_scatter(grad_gate_up, "yx", scatter_dimension=0, tiled=True)
    d_norm_two = joined(near_own, near_sib)
    grad_down = rows_product(grad_all, hidden_all).astype(bf16)
    grad_down, d_norm_two, *moved = stage(grad_down, d_norm_two, *out_sums, *moved_lower)
    out_sums, moved_lower = moved[: near - 1], moved[near - 1 :]

    out_lower = [to_near(out_sums[k - 1][last:], k) for k in others]
    down_part = lax.psum_scatter(grad_down, "yx", scatter_dimension=0, tiled=True)
    for one, two in zip(moved_upper, moved_lower, strict=True):
        d_norm_two = d_norm_two + jnp.concatenate([one, two], axis=0).astype(f32)
    mid_back, _ = norm_back(mid, scale_two, gain_two, d_norm_two)
    d_mid = cot.astype(f32) + mid_back
    d_attn = d_mid.astype(bf16)
    d_attn_sib = flip(d_attn, "core")
    both = [dot32(x, w_out).astype(bf16) for x in (d_attn, d_attn_sib)]
    d_quarters = [
        jnp.concatenate([x[:, k * query_cols : (k + 1) * query_cols] for x in both], axis=0) for k in range(near)
    ]
    d_attn, d_attn_sib, *moved = stage(d_attn, d_attn_sib, *d_quarters, *out_lower)
    d_quarters, out_lower = moved[:near], moved[near:]

    d_context = [d_quarters[0]] + [None] * (near - 1)
    for k in others:
        d_context[near - k] = to_near(d_quarters[k], k)
    grad_out = rows_product(d_attn, context_all[:rows]) + rows_product(d_attn_sib, context_all[rows:])
    grad_out = grad_out.astype(bf16)
    output_own = mid + joined(*near_back[2:])
    for pieces in zip(out_upper, out_third, out_lower, strict=True):
        output_own = output_own + jnp.concatenate(pieces, axis=0).astype(f32)
    output_own = output_own.astype(bf16)
    grad_out, output_own, gate_up_part, *d_context = stage(grad_out, output_own, gate_up_part, *d_context)

    output_crossed = crossed(output_own, CROSS)
    gate_up_keep, gate_up_give = give_z(gate_up_part)
    gate_up_back = crossed(gate_up_give, BACK)
    out_part = lax.psum_scatter(grad_out, "yx", scatter_dimension=0, tiled=True)
    d_qkv = attend_back(list(range(kv_heads)), qkv, d_context, context, sums, [], layout_back, q_heads, kv_heads)
    d_qkv, output_crossed, gate_up_back, gate_up_keep, down_part = stage(
        d_qkv, output_crossed, gate_up_back, gate_up_keep, down_part
    )

    def back_part(k):
        own, sib = (d_qkv[(2 * k + e) * rows : (2 * k + e + 1) * rows] for e in range(2))
        taken = flip(times_transpose(sib, w_project).astype(bf16), "core")
        return times_transpose(own, w_project) + taken.astype(f32)

    d_sent = [back_part(k).astype(bf16) for k in others]
    d_qkv, gate_up_keep, down_part, *d_sent = stage(d_qkv, gate_up_keep, down_part, *d_sent)

    output = jnp.where(straight(), output_own, output_crossed)

    d_upper = [to_near(d_sent[k - 1][:part_rows], k) for k in others]
    gate_up_cross = crossed(gate_up_keep, CROSS)
    grad_project = rows_product(norm_one, d_qkv).astype(bf16)
    project_sent = send_yx(grad_project, (0, qkv_cols))
    total = back_part(0)
    total, grad_project, gate_up_cross, down_part, *moved = stage(
        total, grad_project, gate_up_cross, down_part, *d_upper, *d_sent, *project_sent
    )
    d_upper, d_sent, project_sent = moved[: near - 1], moved[near - 1 : 2 * near - 2], moved[2 * near - 2 :]

    d_lower = [to_near(d_sent[k - 1][part_rows:], k) for k in others]
    down_keep, down_give = give_z(down_part)
    down_home = [crossed(down_give, BACK), crossed(down_keep, CROSS)]
    project_rest, project_own = join_yx(grad_project, (0, qkv_cols), project_sent)
    out_part, *moved = stage(out_part, *d_lower, *project_rest, *down_home)
    d_lower, project_rest, down_home = moved[: near - 1], moved[near - 1 : -2], moved[-2:]
    d_moved = [jnp.concatenate(x, axis=0) for x in zip(d_upper, d_lower, strict=True)]
    project_keep, project_give = give_z(total_yx(project_rest, project_own))

    project_home = [crossed(project_give, BACK), crossed(project_keep, CROSS)]
    for part in d_moved:
        total = total + part.astype(f32)
    input_back, _ = norm_back(residual, scale_one, gain_one, total)
    input_own = (d_mid + input_back).astype(bf16)
    out_moved = [to_near(out_part[:, k * query_cols : (k + 1) * query_cols], k) for k in others]
    out_quarter = out_part[:, :query_cols].astype(f32)
    for part in out_moved:
        out_quarter = out_quarter + part.astype(f32)
    out_keep, out_give = give_z(out_quarter.astype(bf16))
    input_own, out_keep, out_give, *project_home = stage(input_own, out_keep, out_give, *project_home)
    out_home = [crossed(out_give, BACK), crossed(out_keep, CROSS)]
    input_grad = jnp.where(straight(), input_own, crossed(input_own, CROSS)).astype(f32)
    grad_project = sum_z(project_keep, *project_home)
    grad_out = sum_z(out_keep, *out_home)
    grad_down = sum_z(down_keep, *down_home)
    grad_gate_up = sum_z(gate_up_keep, gate_up_back, gate_up_cross)
    gain_grads = lax.psum(
        jnp.stack(
            [
                jnp.sum(qkv_shard.astype(f32) * grad_project, axis=1),
                jnp.sum(gate_up_shard.astype(f32) * grad_gate_up, axis=1),
            ]
        ),
        ("zh", "zl"),
    ) / jnp.stack([attn_gain, mlp_gain]).astype(f32)
    return (
        output,
        input_grad,
        gain_grads[0],
        grad_project[:, :query_cols],
        grad_project[:, query_cols : query_cols + key_cols],
        grad_project[:, query_cols + key_cols :],
        grad_out,
        gain_grads[1],
        grad_gate_up[:, :hidden_cols],
        grad_gate_up[:, hidden_cols:],
        grad_down,
    )


def solution(mesh):
    dp, tensor = mesh.shape["dp"], mesh.shape["tensor"]
    fine = Mesh(mesh.devices.reshape(dp // 2, 2, 2, tensor // 2), AXES)
    by_rows, by_dp, by_both = P(AXES, None), P(("yx", "core")), P(("yx", "core"), ("zh", "zl"))
    return jax.shard_map(
        body,
        mesh=fine,
        in_specs=(
            by_rows, by_rows, P(("yx", "core"), None), by_dp, by_both, by_both, by_both, by_both,
            by_dp, by_both, by_both, by_both,
        ),
        out_specs=(
            by_rows, by_rows, by_dp, by_both, by_both, by_both, by_both, by_dp, by_both, by_both, by_both,
        ),
        check_vma=False,
    )
```

```python
import functools
import math

import jax
import jax.numpy as jnp
import numpy as np
from jax import lax
from jax.experimental import pallas as pl
from jax.experimental.pallas import tpu as pltpu
from jax.sharding import Mesh
from jax.sharding import PartitionSpec as P

HD = 96
HALF = HD // 2
PAD = 128
STEPS = 4
SUB = 256
TILE = 512

EPSILON = 1e-05
ROTARY_BASE = 100000.0
MASKED = -1e30
LOG2E = math.log2(math.e)

AXES = ("yx", "core", "zh", "zl")
FLIP = [(0, 1), (1, 0)]


def norm_rows(values, gain):
    row_scale = lax.rsqrt(jnp.mean(values * values, axis=-1, keepdims=True) + EPSILON)
    return (row_scale, (values * row_scale * gain).astype(jnp.bfloat16))


def norm_back(values, row_scale, gain, upstream):
    weighted = upstream * gain
    inner_sum = jnp.mean(weighted * values, axis=-1, keepdims=True)
    grad_in = row_scale * weighted - values * (row_scale * row_scale * row_scale) * inner_sum
    gain_part = jnp.sum(upstream * (values * row_scale), axis=0)
    return (grad_in, gain_part)


def document_layout(lengths, group_rows):
    flat_lengths = lengths.reshape(-1)
    doc_ends = jnp.cumsum(flat_lengths)
    rows = jnp.arange(group_rows, dtype=jnp.int32)
    passed = (rows[:, None] >= doc_ends[None, :]).astype(jnp.int32)
    return (rows, jnp.sum(passed * flat_lengths[None, :], axis=1))


def rotary_tables(positions):
    exponents = jnp.arange(HALF, dtype=jnp.float32) * (2.0 / HD)
    inverse = ROTARY_BASE ** (-exponents)
    angles = positions.astype(jnp.float32)[:, None] * inverse[None, :]
    cosine, sine = jnp.cos(angles), jnp.sin(angles)
    gap = jnp.zeros((positions.shape[0], PAD // 2 - HALF), jnp.float32)
    return (
        jnp.concatenate([cosine, gap, cosine, gap], axis=1),
        jnp.concatenate([-sine, gap, sine, gap], axis=1),
    )


def rows_product(left, right):
    return lax.dot_general(
        left, right, (((0,), (0,)), ((), ())), preferred_element_type=jnp.float32
    )


def times_transpose(left, right):
    return lax.dot_general(
        left, right, (((1,), (1,)), ((), ())), preferred_element_type=jnp.float32
    )


def dot32(left, right):
    return jnp.dot(left, right, preferred_element_type=jnp.float32)


def stage(*values):
    return lax.optimization_barrier(values)


def spread(columns, heads):
    matrix = np.zeros((columns, len(heads) * PAD), np.float32)
    for at, first in enumerate(heads):
        for half in range(2):
            for i in range(HALF):
                matrix[first + half * HALF + i, at * PAD + half * (PAD // 2) + i] = 1.0
    return matrix


def turn(x, cosine, sine):
    return x * cosine + pltpu.roll(x, PAD // 2, 1) * sine


def rows_at(t, size):
    return pl.ds(pl.multiple_of(t * size, size), size)


def forward_kernel(pieces, ratio, *refs):
    place, low, full, cosine, sine, start, spread_in, gather_out = refs[:8]
    heads = spread_in.shape[0]
    refs = refs[8:]
    qkv, context, refs = refs[0], refs[1 : 1 + pieces], refs[1 + pieces :]
    log_sum, refs = refs[:heads], refs[heads:]
    q_s, k_s, v_s, s_s, top_s, acc = refs
    tiles = q_s.shape[0]
    all_subs = qkv.shape[0] // SUB
    piece_subs = all_subs // pieces
    scale = LOG2E * HD ** (-0.5)
    ones_lane = lax.broadcasted_iota(jnp.int32, (SUB, PAD), 1) == PAD - 1

    def prepare(r, carry):
        t = place[r]
        at = rows_at(t, SUB)
        cos_t, sin_t = cosine[at, :], sine[at, :]
        tile, half = t // (TILE // SUB), t % (TILE // SUB)
        for g in range(heads):
            wide = dot32(qkv[rows_at(r, SUB), :], spread_in[g])
            for h in range(ratio):
                query = turn(wide[:, h * PAD : (h + 1) * PAD], cos_t, sin_t) * scale
                first = pl.multiple_of(h * TILE + half * SUB, SUB)
                q_s[tile, g, pl.ds(first, SUB), :] = query.astype(jnp.bfloat16)
            key = turn(wide[:, ratio * PAD : (ratio + 1) * PAD], cos_t, sin_t)
            k_s[g, at, :] = key.astype(jnp.bfloat16)
            value = jnp.where(ones_lane, 1.0, wide[:, (ratio + 1) * PAD :])
            v_s[g, at, :] = value.astype(jnp.bfloat16)
        return carry

    lax.fori_loop(0, all_subs, prepare, 0)

    def query_tile(i, carry):
        starts = jnp.concatenate([start[rows_at(i, TILE), :]] * ratio, axis=0)
        top_s[...] = jnp.full_like(top_s, MASKED)

        def scores(j, masked, diagonal):
            for g in range(heads):
                s = times_transpose(q_s[i, g], k_s[g, rows_at(j, TILE), :])
                if masked:
                    key_at = lax.broadcasted_iota(jnp.int32, s.shape, 1)
                    allowed = key_at + j * TILE >= starts
                    if diagonal:
                        query_at = lax.rem(lax.broadcasted_iota(jnp.int32, s.shape, 0), TILE)
                        allowed = allowed & (key_at <= query_at)
                    s = jnp.where(allowed, s, MASKED)
                s_s[g, j] = s
                peak = s[:, :PAD]
                for c in range(1, TILE // PAD):
                    peak = jnp.maximum(peak, s[:, c * PAD : (c + 1) * PAD])
                top_s[g] = jnp.maximum(top_s[g], peak)

        def loop(first, last, masked):
            def run(j, c):
                scores(j, masked, False)
                return c

            lax.fori_loop(first, last, run, 0)

        loop(low[i], full[i], True)
        loop(full[i], i, False)
        scores(i, True, True)
        tops = [jnp.max(top_s[g], axis=1, keepdims=True) for g in range(heads)]
        acc[...] = jnp.zeros_like(acc)

        def weigh(j, c):
            for g in range(heads):
                p = jnp.exp2(s_s[g, j] - tops[g]).astype(jnp.bfloat16)
                acc[g] += dot32(p, v_s[g, rows_at(j, TILE), :])
            return c

        lax.fori_loop(low[i], i + 1, weigh, 0)
        packed = None
        for g in range(heads):
            total = acc[g][:, PAD - 1 :]
            out = acc[g] * (1.0 / total)
            sums = jnp.broadcast_to(tops[g] + jnp.log(total) * LOG2E, (ratio * TILE, PAD))
            log_sum[g][i] = sums.T[:1, :]
            wide = jnp.concatenate(
                [out[h * TILE : (h + 1) * TILE, :] for h in range(ratio)], axis=1
            ).astype(jnp.bfloat16)
            part = dot32(wide, gather_out[g])
            packed = part if packed is None else packed + part
        subs = tiles * (TILE // SUB)
        for half in range(TILE // SUB):
            r = place[subs + i * (TILE // SUB) + half]
            part = packed[half * SUB : (half + 1) * SUB, :].astype(jnp.bfloat16)
            for k in range(pieces):

                @pl.when(r // piece_subs == k)
                def store(k=k, part=part, r=r):
                    context[k][rows_at(r % piece_subs, SUB), :] = part

        return carry

    lax.fori_loop(0, tiles, query_tile, 0)


def backward_kernel(pieces, ratio, more, *refs):
    place, low, full, cosine, sine, start, refs = *refs[:6], refs[6:]
    heads = refs[0].shape[0]
    spread_in, spread_out, gather_in, refs = *refs[:3], refs[3:]
    log_sum, refs = refs[:heads], refs[heads:]
    d_context, context, qkv, refs = refs[:pieces], refs[pieces : 2 * pieces], refs[2 * pieces], refs[2 * pieces + 1 :]
    earlier, refs = (refs[0], refs[1:]) if more else (None, refs)
    d_qkv, refs = refs[0], refs[1:]
    q_s, k_s, kt_s, v_s, do_s, delta_s, log_s, dq_acc, dk_acc, dv_acc, dq_s = refs
    tiles = q_s.shape[0]
    all_subs = qkv.shape[0] // SUB
    piece_subs = all_subs // pieces
    scale = HD ** (-0.5)
    per_tile = TILE // SUB

    for k in range(pieces):

        def prepare(r, carry, k=k):
            t = place[k * piece_subs + r]
            rel = rows_at(r, SUB)
            at = rows_at(t, SUB)
            cos_t, sin_t = cosine[at, :], sine[at, :]
            for g in range(heads):
                wide = dot32(qkv[rows_at(k * piece_subs + r, SUB), :], spread_in[g])
                d_out = dot32(d_context[k][rel, :], spread_out[g])
                out = dot32(context[k][rel, :], spread_out[g])
                for h in range(ratio):
                    cols = slice(h * PAD, (h + 1) * PAD)
                    rows = slice(h * SUB, (h + 1) * SUB)
                    query = turn(wide[:, cols], cos_t, sin_t) * (scale * LOG2E)
                    q_s[t, g, rows, :] = query.astype(jnp.bfloat16)
                    do_s[t, g, rows, :] = d_out[:, cols].astype(jnp.bfloat16)
                    delta = jnp.sum((d_out[:, cols] * out[:, cols]).T, axis=0, keepdims=True)
                    delta_s[t * heads + g, :, rows] = delta
                    first = pl.multiple_of(h * TILE + t % per_tile * SUB, SUB)
                    log_s[t * heads + g, :, rows] = log_sum[g][t // per_tile, :, pl.ds(first, SUB)]
                key = turn(wide[:, ratio * PAD : (ratio + 1) * PAD], cos_t, sin_t)
                k_s[g, t] = key.astype(jnp.bfloat16)
                kt_s[g, t] = key.T.astype(jnp.bfloat16)
                v_s[g, t] = wide[:, (ratio + 1) * PAD :].astype(jnp.bfloat16)
                dk_acc[g, t] = jnp.zeros((SUB, PAD), jnp.float32)
                dv_acc[g, t] = jnp.zeros((SUB, PAD), jnp.float32)
            return carry

        lax.fori_loop(0, piece_subs, prepare, 0)

    def query_tile(i, carry):
        dq_acc[...] = jnp.zeros_like(dq_acc)

        def step(j, masked, diagonal):
            for g in range(heads):
                queries, d_out = q_s[i, g], do_s[i, g]
                s = times_transpose(k_s[g, j], queries)
                if masked:
                    key_at = lax.broadcasted_iota(jnp.int32, s.shape, 0)
                    allowed = key_at + j * SUB >= start[i]
                    if diagonal:
                        query_at = lax.rem(lax.broadcasted_iota(jnp.int32, s.shape, 1), SUB)
                        allowed = allowed & (key_at <= query_at)
                    s = jnp.where(allowed, s, MASKED)
                p = jnp.exp2(s - log_s[i * heads + g])
                d_p = times_transpose(v_s[g, j], d_out)
                d_s = (p * (d_p - delta_s[i * heads + g])).astype(jnp.bfloat16)
                dv_acc[g, j] += dot32(p.astype(jnp.bfloat16), d_out)
                dk_acc[g, j] += dot32(d_s, queries)
                dq_acc[g] += dot32(kt_s[g, j], d_s)

        def loop(first, last, masked):
            def run(j, c):
                step(j, masked, False)
                return c

            lax.fori_loop(first, last, run, 0)

        loop(low[i], full[i], True)
        loop(full[i], i, False)
        step(i, True, True)
        at = rows_at(i, SUB)
        cos_t, sin_t = cosine[at, :], sine[at, :]
        for g in range(heads):
            grad = dq_acc[g].T * scale
            for h in range(ratio):
                piece = turn(grad[h * SUB : (h + 1) * SUB, :], cos_t, -sin_t)
                dq_s[g, i, :, h * PAD : (h + 1) * PAD] = piece.astype(jnp.bfloat16)
        return carry

    lax.fori_loop(0, tiles, query_tile, 0)

    def finish(r, carry):
        t = place[r]
        at = rows_at(t, SUB)
        rel = rows_at(r, SUB)
        packed = None
        for g in range(heads):
            key = turn(dk_acc[g, t] * (1.0 / LOG2E), cosine[at, :], -sine[at, :])
            wide = jnp.concatenate(
                [dq_s[g, t], key.astype(jnp.bfloat16), dv_acc[g, t].astype(jnp.bfloat16)], axis=1
            )
            part = dot32(wide, gather_in[g])
            packed = part if packed is None else packed + part
        packed = packed.astype(jnp.bfloat16)
        d_qkv[rel, :] = packed + earlier[rel, :] if more else packed
        return carry

    lax.fori_loop(0, all_subs, finish, 0)


SMEM = pl.BlockSpec(memory_space=pltpu.SMEM)
VMEM = pl.BlockSpec(memory_space=pltpu.VMEM)
ANY = pl.BlockSpec(memory_space=pl.ANY)


def small_cost(transcendentals=0):
    return pl.CostEstimate(flops=1 << 20, bytes_accessed=1 << 16, transcendentals=transcendentals)


def head_matrices(head, q_heads, kv_heads):
    ratio = q_heads // kv_heads
    queries = [(head * ratio + r) * HD for r in range(ratio)]
    key, value = (q_heads + head) * HD, (q_heads + kv_heads + head) * HD
    inner = spread((q_heads + 2 * kv_heads) * HD, [*queries, key, value])
    outer = spread(q_heads * HD, queries)
    return jnp.asarray(inner, jnp.bfloat16), jnp.asarray(outer, jnp.bfloat16)


def stacked_matrices(q_heads, kv_heads):
    pairs = [head_matrices(head, q_heads, kv_heads) for head in range(kv_heads)]
    return jnp.stack([inner for inner, _ in pairs]), jnp.stack([outer for _, outer in pairs])


def attend(qkv, pieces, layout, q_heads, kv_heads):
    place, low, full, cosine, sine, start_column = layout
    ratio, rows = q_heads // kv_heads, qkv.shape[0]
    tiles, lanes = rows // TILE, ratio * TILE
    bf16, f32 = jnp.bfloat16, jnp.float32
    inner, outer = stacked_matrices(q_heads, kv_heads)
    outs = pl.pallas_call(
        functools.partial(forward_kernel, pieces, ratio),
        out_shape=[
            *[jax.ShapeDtypeStruct((rows // pieces, q_heads * HD), bf16)] * pieces,
            *[jax.ShapeDtypeStruct((tiles, 1, lanes), f32)] * kv_heads,
        ],
        in_specs=[SMEM] * 3 + [VMEM] * 6,
        out_specs=[VMEM] * (pieces + kv_heads),
        scratch_shapes=[
            pltpu.VMEM((tiles, kv_heads, lanes, PAD), bf16),
            pltpu.VMEM((kv_heads, rows, PAD), bf16),
            pltpu.VMEM((kv_heads, rows, PAD), bf16),
            pltpu.VMEM((kv_heads, tiles, lanes, TILE), f32),
            pltpu.VMEM((kv_heads, lanes, PAD), f32),
            pltpu.VMEM((kv_heads, lanes, PAD), f32),
        ],
        compiler_params=pltpu.CompilerParams(vmem_limit_bytes=60 * 2**20),
        cost_estimate=small_cost(),
        name="attention_forward",
    )(place, low, full, cosine, sine, start_column, inner, jnp.swapaxes(outer, 1, 2), qkv)
    return outs[:pieces], outs[pieces:]


def attend_back(heads, qkv, d_context, context, sums, earlier, layout, q_heads, kv_heads):
    place, low, full, cosine, sine, start_row = layout
    pieces, ratio, rows = len(context), q_heads // kv_heads, qkv.shape[0]
    tiles, lanes, count = rows // SUB, ratio * SUB, len(heads)
    bf16, f32 = jnp.bfloat16, jnp.float32
    inner, outer = stacked_matrices(q_heads, kv_heads)
    inner, outer = inner[heads[0] : heads[0] + count], outer[heads[0] : heads[0] + count]
    return pl.pallas_call(
        functools.partial(backward_kernel, pieces, ratio, bool(earlier)),
        out_shape=jax.ShapeDtypeStruct(qkv.shape, bf16),
        in_specs=[SMEM] * 3 + [VMEM] * (7 + count + 2 * pieces + len(earlier)),
        out_specs=VMEM,
        scratch_shapes=[
            pltpu.VMEM((tiles, count, lanes, PAD), bf16),
            pltpu.VMEM((count, tiles, SUB, PAD), bf16),
            pltpu.VMEM((count, tiles, PAD, SUB), bf16),
            pltpu.VMEM((count, tiles, SUB, PAD), bf16),
            pltpu.VMEM((tiles, count, lanes, PAD), bf16),
            pltpu.VMEM((tiles * count, 1, lanes), f32),
            pltpu.VMEM((tiles * count, 1, lanes), f32),
            pltpu.VMEM((count, PAD, lanes), f32),
            pltpu.VMEM((count, tiles, SUB, PAD), f32),
            pltpu.VMEM((count, tiles, SUB, PAD), f32),
            pltpu.VMEM((count, tiles, SUB, ratio * PAD), bf16),
        ],
        compiler_params=pltpu.CompilerParams(vmem_limit_bytes=60 * 2**20),
        cost_estimate=small_cost(),
        name=f"attention_backward_{heads[0]}",
    )(
        place, low, full, cosine, sine, start_row, inner, outer, jnp.swapaxes(inner, 1, 2),
        *[sums[h] for h in heads], *d_context, *context, qkv, *earlier,
    )


def fetch(me, where, sources, target, sems):
    copies = []
    for n, (source, (j, deep, first, column, taken)) in enumerate(zip(sources, where, strict=True)):
        cols = min(source.shape[1] - taken, target.shape[1] - column)
        at = pl.ds(pl.multiple_of((me[0] ^ j) * deep + first, 16), source.shape[0])
        if cols != source.shape[1]:
            source = source.at[:, taken : taken + cols]
        copies.append(pltpu.make_async_copy(source, target.at[at, column : column + cols], sems.at[n]))
    return copies


def take_rows(parts, target):
    rows = target.shape[0]
    for step in range(STEPS):

        @pl.when(pl.program_id(0) == step)
        def take(step=step):
            at = 0
            for part in parts:
                first, last = max(at, step * rows), min(at + part.shape[0], (step + 1) * rows)
                if first < last:
                    target[first - step * rows : last - step * rows, :] = part[first - at : last - at, :]
                at += part.shape[0]


def at_first_step(copies, what):
    @pl.when(pl.program_id(0) == 0)
    def run():
        for copy in copies:
            what(copy)


def project_kernel(count, where, more, me, *refs):
    parts, gain, refs = refs[:count], refs[count], refs[count + 1 :]
    sources, refs = refs[: len(where[0])], refs[len(where[0]) :]
    norm_all, qkv_all, weight, sems, rows_s = refs[2 if more else 0 :]
    copies = fetch(me, where[0], sources, weight, sems)
    at_first_step(copies, lambda copy: copy.start())
    take_rows(parts, rows_s)
    x = rows_s[...].astype(jnp.float32)
    scale = lax.rsqrt(jnp.mean(x * x, axis=-1, keepdims=True) + EPSILON)
    norm_all[...] = (x * scale * gain[...]).astype(jnp.bfloat16)
    at_first_step(copies, lambda copy: copy.wait())
    qkv_all[...] = dot32(norm_all[...], weight[...]).astype(jnp.bfloat16)


def by_half(refs, value):
    for n, ref in enumerate(refs):

        @pl.when(pl.program_id(0) * 2 // STEPS == n)
        def store(ref=ref):
            ref[...] = value


def gate_kernel(count, where, more, me, *refs):
    parts, refs = refs[:count], refs[count:]
    with_out = len(where) > 1
    sources, refs = refs[: sum(map(len, where))], refs[sum(map(len, where)) :]
    norm_all, gate_up_all, hidden_all, *refs = refs[3 if more else 0 :]
    out_refs, refs = (refs[:2], refs[2:]) if with_out else ((), refs)
    weight, sems, *refs = refs
    hidden_cols = hidden_all.shape[1]
    copies = fetch(me, where[0], sources[: len(where[0])], weight, sems)
    if with_out:
        w_down, down_sems = refs
        copies += fetch(me, where[1], sources[len(where[0]) :], w_down, down_sems)
    at_first_step(copies, lambda copy: copy.start())
    take_rows(parts, norm_all)
    at_first_step(copies, lambda copy: copy.wait())
    x = norm_all[...]
    width = min(512, hidden_cols)
    for at in range(0, hidden_cols, width):
        gate_at = slice(at, at + width)
        up_at = slice(hidden_cols + at, hidden_cols + at + width)
        gate = dot32(x, weight[:, gate_at])
        up = dot32(x, weight[:, up_at])
        gate_up_all[:, gate_at] = gate
        gate_up_all[:, up_at] = up
        hidden_all[:, gate_at] = (gate * (1.0 / (1.0 + jnp.exp(-gate))) * up).astype(jnp.bfloat16)
    if with_out:
        by_half(out_refs, times_transpose(hidden_all[...], w_down[...]).astype(jnp.bfloat16))


def gate_back_kernel(count, where, more, me, *refs):
    parts, gate_up_all, hidden_here, refs = refs[:count], *refs[count : count + 2], refs[count + 2 :]
    gate_up, refs = refs[: len(where[0])], refs[len(where[0]) :]
    down, refs = refs[: len(where[1])], refs[len(where[1]) :]
    grad_all, d_gate_up_all, *refs = refs[2 if more else 0 :]
    d_norm_refs, refs = refs[:2], refs[2:]
    out_refs, refs = ((), refs) if more else (refs[:2], refs[2:])
    w_gate_up, gate_up_sems, w_down, down_sems = refs
    hidden_cols = w_down.shape[1]
    down_copies = fetch(me, where[1], down, w_down, down_sems)
    copies = fetch(me, where[0], gate_up, w_gate_up, gate_up_sems)
    at_first_step(down_copies + copies, lambda copy: copy.start())
    take_rows(parts, grad_all)
    at_first_step(down_copies, lambda copy: copy.wait())
    dy = grad_all[...]
    width = min(512, hidden_cols)
    for at in range(0, hidden_cols, width):
        gate_at = slice(at, at + width)
        up_at = slice(hidden_cols + at, hidden_cols + at + width)
        d_hidden = dot32(dy, w_down[:, gate_at])
        gate, up = gate_up_all[:, gate_at], gate_up_all[:, up_at]
        sigmoid = 1.0 / (1.0 + jnp.exp(-gate))
        d_gate = d_hidden * up * sigmoid * (1.0 + gate * (1.0 - sigmoid))
        d_gate_up_all[:, gate_at] = d_gate.astype(jnp.bfloat16)
        d_gate_up_all[:, up_at] = (d_hidden * (gate * sigmoid)).astype(jnp.bfloat16)
    if not more:
        by_half(out_refs, times_transpose(hidden_here[...], w_down[...]).astype(jnp.bfloat16))
    at_first_step(copies, lambda copy: copy.wait())
    by_half(d_norm_refs, times_transpose(d_gate_up_all[...], w_gate_up[...]).astype(jnp.bfloat16))


def piece_call(kernel, name, k, pieces, me, parts, whole, tiled, fetched, earlier, outs):
    tile, width = sum(x.shape[0] for x in parts) // STEPS, parts[0].shape[1]
    count = len(parts)

    def rows_of(piece):
        return lambda i: (piece * STEPS + i, 0)

    def half_of(span):
        first = 0 if span == "own" else STEPS // 2
        return lambda i: (jnp.clip(i - first, 0, STEPS // 2 - 1), 0)

    sources = [x for arrays, _, _ in fetched for x in arrays]
    first_earlier = 1 + count + len(whole) + len(tiled) + len(sources)
    scratch = []
    for arrays, _, cols in fetched:
        scratch += [pltpu.VMEM((width, cols), jnp.bfloat16), pltpu.SemaphoreType.DMA((len(arrays),))]
    if kernel is project_kernel:
        scratch.append(pltpu.VMEM((tile, width), jnp.bfloat16))
    return pl.pallas_call(
        functools.partial(kernel, count, tuple(where for _, where, _ in fetched), bool(earlier)),
        grid=(STEPS,),
        out_shape=[
            jax.ShapeDtypeStruct(((pieces * STEPS if span == "all" else STEPS // 2) * tile, columns), kind)
            for columns, kind, span in outs
        ],
        in_specs=[
            SMEM,
            *(pl.BlockSpec(x.shape, lambda i: (0, 0)) for x in parts),
            *(pl.BlockSpec(x.shape, lambda i: (0, 0)) for x in whole),
            *(pl.BlockSpec((tile, x.shape[1]), rows_of(piece)) for x, piece in tiled),
            *[ANY] * (len(sources) + len(earlier)),
        ],
        out_specs=[
            pl.BlockSpec((tile, columns), rows_of(k) if span == "all" else half_of(span))
            for columns, kind, span in outs
        ],
        scratch_shapes=scratch,
        input_output_aliases={first_earlier + n: n for n in range(len(earlier))},
        compiler_params=pltpu.CompilerParams(vmem_limit_bytes=60 * 2**20),
        cost_estimate=small_cost(),
        name=f"{name}_{k}",
    )(me, *parts, *whole, *(x for x, _ in tiled), *sources, *earlier)


def assemble_kernel(where, me, *refs):
    sources, whole, sems = refs[: len(where)], refs[len(where)], refs[len(where) + 1]
    copies = fetch(me, where, sources, whole, sems)
    for copy in copies:
        copy.start()
    for copy in copies:
        copy.wait()


def assemble(name, me, arrays, where, rows, cols):
    return pl.pallas_call(
        functools.partial(assemble_kernel, where),
        out_shape=jax.ShapeDtypeStruct((rows, cols), arrays[0].dtype),
        in_specs=[SMEM, *[ANY] * len(arrays)],
        out_specs=VMEM,
        scratch_shapes=[pltpu.SemaphoreType.DMA((len(arrays),))],
        compiler_params=pltpu.CompilerParams(vmem_limit_bytes=60 * 2**20),
        cost_estimate=small_cost(),
        name=name,
    )(me, *arrays)


def flip(x, axis):
    return lax.ppermute(x, axis, FLIP)


CROSS = [(1, 2), (2, 1)]
OUT = [(0, 1), (3, 2), (2, 0), (1, 3)]
BACK = [(1, 0), (2, 3), (0, 2), (3, 1)]


def crossed(x, perm):
    return lax.ppermute(x, ("core", "zh"), perm)


def straight():
    return lax.axis_index("core") == lax.axis_index("zh")


def swap(x):
    return jnp.where(straight(), x, crossed(x, CROSS))


def send_z(w):
    return crossed(w, OUT), crossed(w, CROSS)


def pair_of(w, out, cross):
    zh = lax.axis_index("zh")
    x = jnp.where(straight(), w, cross)
    return jnp.concatenate([jnp.where(zh == 0, x, out), jnp.where(zh == 0, out, x)], axis=0)


def give_z(part):
    zh = lax.axis_index("zh")
    half = part.shape[0] // 2
    upper, lower = part[:half], part[half:]
    return jnp.where(zh == 0, upper, lower), jnp.where(zh == 0, lower, upper)


def sum_z(keep, back, cross):
    return back.astype(jnp.float32) + jnp.where(straight(), keep, cross).astype(jnp.float32)


def shift(x, e, k):
    n = lax.axis_size("zl")
    return lax.ppermute(
        x, ("core", "zl"), [(c * n + l, (c ^ e) * n + (l + k) % n) for c in range(2) for l in range(n)]
    )


def from_near(x, k):
    n = lax.axis_size("zl")
    return lax.ppermute(x, "zl", [((j + k) % n, j) for j in range(n)])


def to_near(x, k):
    n = lax.axis_size("zl")
    return lax.ppermute(x, "zl", [(j, (j + k) % n) for j in range(n)])


def across(x, j):
    n = lax.axis_size("yx")
    return lax.ppermute(x, "yx", [(a, a ^ j) for a in range(n)])


def neighbours(x):
    count = lax.axis_size("yx")
    return [across(x, j) for j in range(1, count if count != 4 else 3)]


def diagonal(taken):
    if lax.axis_size("yx") != 4:
        return []
    half = taken[0].shape[0] // 2
    return [across(taken[1][:half], 1), across(taken[0][half:], 2)]


def blocks_of(own, taken, halves, column=0, source_column=0):
    deep = own.shape[0]
    arrays = [own, *taken, *halves]
    where = [(j, deep, 0, column, source_column) for j in range(1 + len(taken))]
    where += [(3, deep, n * deep // 2, column, source_column) for n in range(len(halves))]
    return arrays, tuple(where)


def whole_weight(w):
    return [w], ((0, 0, 0, 0, 0),)


def block_of(grad, j, columns):
    size = grad.shape[0] // lax.axis_size("yx")
    first = (lax.axis_index("yx") ^ j) * size
    return lax.dynamic_slice(grad, (first, columns[0]), (size, columns[1] - columns[0]))


def send_yx(grad, columns):
    count = lax.axis_size("yx")
    if count != 4:
        return [across(block_of(grad, j, columns), j) for j in range(1, count)]
    far = block_of(grad, 3, columns)
    half = far.shape[0] // 2
    return [across(far[:half], 1), across(far[half:], 2)]


def join_yx(grad, columns, taken):
    if lax.axis_size("yx") != 4:
        return taken, block_of(grad, 0, columns)
    half = taken[0].shape[0]
    one, two = block_of(grad, 1, columns), block_of(grad, 2, columns)
    one = jnp.concatenate([one[:half], one[half:] + taken[1]], axis=0)
    two = jnp.concatenate([two[:half] + taken[0], two[half:]], axis=0)
    return [across(one, 1), across(two, 2)], block_of(grad, 0, columns)


def total_yx(taken, own):
    total = own.astype(jnp.float32)
    for part in taken:
        total = total + part.astype(jnp.float32)
    return total.astype(jnp.bfloat16)


def body(
    tokens,
    cotangent,
    seq_lengths,
    attn_gain,
    q_weight,
    key_projection,
    value_projection,
    out_weight,
    mlp_gain,
    gate_weight,
    up_weight,
    down_weight,
):
    bf16, f32 = jnp.bfloat16, jnp.float32
    core, zl, yx = lax.axis_index("core"), lax.axis_index("zl"), lax.axis_index("yx")
    near = lax.axis_size("zl")
    others = range(1, near)
    rows = tokens.shape[0]
    group_rows = 2 * near * rows
    query_cols, key_cols = q_weight.shape[1], key_projection.shape[1]
    qkv_cols = query_cols + 2 * key_cols
    q_heads, kv_heads = query_cols // HD, key_cols // HD
    hidden_cols = gate_weight.shape[1]
    me = yx.astype(jnp.int32).reshape(1)

    qkv_shard = jnp.concatenate([q_weight, key_projection, value_projection], axis=1)
    gate_up_shard = jnp.concatenate([gate_weight, up_weight], axis=1)
    part_rows = rows // 2
    upper = swap(tokens[:part_rows])
    shard_moved = send_z(qkv_shard)
    lengths = swap(seq_lengths)
    gains = lax.all_gather(jnp.stack([attn_gain, mlp_gain]), ("yx", "core"), axis=1, tiled=True).astype(f32)
    upper, lengths, second_part, out_shard, gains, *shard_moved = stage(
        upper, lengths, tokens[part_rows:], out_weight, gains, *shard_moved
    )
    gain_one, gain_two = gains[0], gains[1]

    upper_far = [from_near(upper, k) for k in others]
    lower = swap(second_part)
    pair = pair_of(qkv_shard, *shard_moved)
    taken = neighbours(pair)
    out_out = crossed(out_shard, OUT)

    subs = jnp.arange(group_rows // SUB, dtype=jnp.int32)
    per_device = rows // SUB
    source, within = subs // per_device, subs % per_device
    there_core, there_zl = (source % 2) ^ core, (source // 2 + zl) % near
    to_order = (there_core * near + there_zl) * per_device + within
    from_order = (((source % near - zl) % near) * 2 + ((source // near) ^ core)) * per_device + within
    place = jnp.concatenate([to_order, from_order])
    row_at, doc_start = document_layout(lengths, group_rows)
    cosine, sine = rotary_tables(row_at - doc_start)

    def bounds(size):
        tile_start = doc_start.reshape(-1, size)
        tile = jnp.arange(group_rows // size, dtype=jnp.int32)
        low = tile_start[:, 0] // size
        return low, jnp.minimum((tile_start[:, -1] + size - 1) // size, tile)

    start_row = jnp.tile(doc_start.reshape(-1, 1, SUB), (1, 1, q_heads // kv_heads))
    layout = (place, *bounds(TILE), cosine, sine, doc_start[:, None])
    layout_back = (place, *bounds(SUB), cosine, sine, start_row)
    lower, out_out, out_shard, *moved = stage(lower, out_out, out_shard, *upper_far, *taken, *layout, *layout_back)
    upper_far, moved = moved[: near - 1], moved[near - 1 :]
    taken, moved = moved[: len(taken)], moved[len(taken) :]
    layout, layout_back = moved[: len(layout)], moved[len(layout) :]

    lower_far = [from_near(lower, k) for k in others]
    own = jnp.concatenate([upper, lower], axis=0)
    own_sib = flip(own, "core")
    out_cross = crossed(out_shard, CROSS)
    blocks = blocks_of(pair, taken, diagonal(taken))
    projecting = [(*blocks, qkv_cols)]
    gain_row = gain_one[None]
    outs = [(tokens.shape[1], bf16, "all"), (qkv_cols, bf16, "all")]
    normed = piece_call(project_kernel, "project", 0, near, me, [own, own_sib], [gain_row], [], projecting, [], outs)
    gate_up_shard, out_cross, down_shard, *moved = stage(gate_up_shard, out_cross, down_weight, *lower_far, *normed)
    lower_far, normed = moved[: near - 1], moved[near - 1 :]

    out_pair = pair_of(out_weight, out_out, out_cross)
    out_far = [from_near(out_pair, k) for k in others]
    down_out = crossed(down_shard, OUT)
    for k in others:
        far = jnp.concatenate([upper_far[k - 1], lower_far[k - 1]], axis=0)
        parts = [far, flip(far, "core")]
        normed = piece_call(project_kernel, "project", k, near, me, parts, [gain_row], [], projecting, normed, outs)
    norm_one, qkv = normed
    gate_up_shard, qkv, out_pair, down_out, *out_far = stage(gate_up_shard, qkv, out_pair, down_out, *out_far)

    gate_up_moved = send_z(gate_up_shard)
    w_out = lax.all_gather(jnp.concatenate([out_pair, *out_far], axis=1), "yx", axis=0, tiled=True)
    context, sums = attend(qkv, near, layout, q_heads, kv_heads)
    cotangent, down_shard, *moved = stage(cotangent, down_shard, *context, *gate_up_moved)
    context, gate_up_moved = moved[:near], moved[near:]

    quarters = [context[0]] + [None] * (near - 1)
    for k in others:
        quarters[near - k] = to_near(context[k], k)
    down_cross = crossed(down_shard, CROSS)
    gate_up_pair = pair_of(gate_up_shard, *gate_up_moved)
    gate_up_taken = neighbours(gate_up_pair)
    w_project = assemble("assemble_project", me, *blocks, tokens.shape[1], qkv_cols)
    residual = own.astype(f32)
    scale_one = lax.rsqrt(jnp.mean(residual * residual, axis=-1, keepdims=True) + EPSILON)
    cotangent, down_cross, w_out, scale_one, w_project, *moved = stage(
        cotangent, down_cross, w_out, scale_one, w_project, *quarters, *gate_up_taken
    )
    quarters, gate_up_taken = moved[:near], moved[near:]

    gate_up_halves = diagonal(gate_up_taken)
    cot_upper = crossed(cotangent[:part_rows], CROSS)
    context_all = jnp.concatenate(quarters, axis=1)
    branch_sib = flip(times_transpose(context_all[rows:], w_out).astype(bf16), "core")
    mid = residual + times_transpose(context_all[:rows], w_out) + branch_sib.astype(f32)
    scale_two, norm_two = norm_rows(mid, gain_two)
    down_pair = pair_of(down_weight, down_out, down_cross)
    norm_two, cotangent, cot_upper, down_pair, *gate_up_halves = stage(
        norm_two, cotangent, cot_upper, down_pair, *gate_up_halves
    )

    upper_far = [from_near(norm_two[:part_rows], k) for k in others]
    norm_sib = flip(norm_two, "core")
    cot_lower = crossed(cotangent[part_rows:], CROSS)
    down_taken = neighbours(down_pair)
    gate_up = (*blocks_of(gate_up_pair, gate_up_taken, gate_up_halves), 2 * hidden_cols)
    gate_outs = [(norm_two.shape[1], bf16, "all"), (2 * hidden_cols, f32, "all"), (hidden_cols, bf16, "all")]
    earlier = piece_call(gate_kernel, "gate", 0, near, me, [norm_two, norm_sib], [], [], [gate_up], [], gate_outs)
    norm_two, cotangent, cot_lower, *moved = stage(norm_two, cotangent, cot_lower, *upper_far, *down_taken, *earlier)
    upper_far, moved = moved[: near - 1], moved[near - 1 :]
    down_taken, earlier = moved[: len(down_taken)], moved[len(down_taken) :]

    lower_far = [from_near(norm_two[part_rows:], k) for k in others]
    cot = jnp.where(straight(), cotangent, jnp.concatenate([cot_upper, cot_lower], axis=0))
    cot_sib = flip(cot, "core")
    cot_upper_far = [from_near(jnp.where(straight(), cotangent[:part_rows], cot_upper), k) for k in others]
    down_halves = diagonal(down_taken)
    down = (*blocks_of(down_pair, down_taken, down_halves), hidden_cols)
    width = norm_two.shape[1]
    outs = [(width, bf16, "all"), (2 * hidden_cols, bf16, "all")]
    halves = [(width, bf16, "own"), (width, bf16, "sibling")]

    def way_back(k, parts, earlier):
        tiled, results = [(gate_up_all, k), (hidden_all, k)], outs + halves * (1 if earlier else 2)
        return piece_call(gate_back_kernel, "gate_back", k, near, me, parts, [], tiled, [gate_up, down], earlier, results)

    def joined(own, sib):
        return own.astype(f32) + flip(sib, "core").astype(f32)

    norm_two_all, gate_up_all, hidden_all = earlier
    grad_all, d_gate_up_all, *near_back = way_back(0, [cot, cot_sib], [])
    cot, *moved = stage(
        cot, norm_two_all, gate_up_all, hidden_all, grad_all, d_gate_up_all, *near_back, *cot_upper_far, *lower_far
    )
    earlier, (grad_all, d_gate_up_all), near_back, moved = moved[:3], moved[3:5], moved[5:9], moved[9:]
    cot_upper_far, lower_far = moved[: near - 1], moved[near - 1 :]

    cot_lower_far = [from_near(cot[part_rows:], k) for k in others]
    out_far = []
    for k in others:
        norm_far = jnp.concatenate([upper_far[k - 1], lower_far[k - 1]], axis=0)
        parts = [norm_far, flip(norm_far, "core")]
        *earlier, out_own, out_sib = piece_call(
            gate_kernel, "gate", k, near, me, parts, [], [], [gate_up, down], earlier, gate_outs + halves
        )
        out_far += [out_own, out_sib]
    grad_all, d_gate_up_all, w_project, *moved = stage(
        grad_all, d_gate_up_all, w_project, *near_back, *cot_lower_far, *earlier, *out_far
    )
    near_back, cot_lower_far, moved = moved[:4], moved[4 : near + 3], moved[near + 3 :]
    earlier, out_far = moved[:3], moved[3:]
    norm_two_all, gate_up_all, hidden_all = earlier
    cot_far = [jnp.concatenate(x, axis=0) for x in zip(cot_upper_far, cot_lower_far, strict=True)]
    cot_far_sib = [flip(x, "core") for x in cot_far]
    out_sums = [joined(*out_far[2 * n : 2 * n + 2]).astype(bf16) for n in range(near - 1)]
    moved = stage(*cot_far_sib, *out_sums)
    cot_far_sib, out_sums = moved[: near - 1], moved[near - 1 :]

    out_upper = [to_near(out_sums[k - 1][:part_rows], k) for k in others]
    back = []
    for k in others:
        parts = [cot_far[k - 1], cot_far_sib[k - 1]]
        grad_all, d_gate_up_all, *more = way_back(k, parts, [grad_all, d_gate_up_all])
        back.append(more)
    grad_all, d_gate_up_all, *moved = stage(
        grad_all, d_gate_up_all, *(x for more in back for x in more), *out_upper, *out_sums
    )
    far_back, moved = moved[: 2 * near - 2], moved[2 * near - 2 :]
    out_upper, out_sums = moved[: near - 1], moved[near - 1 :]
    last = part_rows + part_rows // 2
    out_third = [to_near(out_sums[k - 1][part_rows:last], k) for k in others]
    d_norm_sent = [joined(*far_back[2 * n : 2 * n + 2]).astype(bf16) for n in range(near - 1)]
    grad_all, d_gate_up_all, near_own, near_sib, *moved = stage(
        grad_all, d_gate_up_all, *near_back[:2], *d_norm_sent, *out_third
    )
    d_norm_sent, out_third = moved[: near - 1], moved[near - 1 :]

    moved_upper = [to_near(d_norm_sent[k - 1][:part_rows], k) for k in others]
    grad_gate_up = rows_product(norm_two_all, d_gate_up_all).astype(bf16)
    grad_gate_up, grad_all, near_own, near_sib, *moved = stage(
        grad_gate_up, grad_all, near_own, near_sib, *moved_upper, *d_norm_sent
    )
    moved_upper, d_norm_sent = moved[: near - 1], moved[near - 1 :]

    moved_lower = [to_near(d_norm_sent[k - 1][part_rows:], k) for k in others]
    gate_up_part = lax.psum_scatter(grad_gate_up, "yx", scatter_dimension=0, tiled=True)
    d_norm_two = joined(near_own, near_sib)
    grad_down = rows_product(grad_all, hidden_all).astype(bf16)
    grad_down, d_norm_two, *moved = stage(grad_down, d_norm_two, *out_sums, *moved_lower)
    out_sums, moved_lower = moved[: near - 1], moved[near - 1 :]

    out_lower = [to_near(out_sums[k - 1][last:], k) for k in others]
    down_part = lax.psum_scatter(grad_down, "yx", scatter_dimension=0, tiled=True)
    for one, two in zip(moved_upper, moved_lower, strict=True):
        d_norm_two = d_norm_two + jnp.concatenate([one, two], axis=0).astype(f32)
    mid_back, _ = norm_back(mid, scale_two, gain_two, d_norm_two)
    d_mid = cot.astype(f32) + mid_back
    d_attn = d_mid.astype(bf16)
    d_attn_sib = flip(d_attn, "core")
    both = [dot32(x, w_out).astype(bf16) for x in (d_attn, d_attn_sib)]
    d_quarters = [
        jnp.concatenate([x[:, k * query_cols : (k + 1) * query_cols] for x in both], axis=0) for k in range(near)
    ]
    d_attn, d_attn_sib, *moved = stage(d_attn, d_attn_sib, *d_quarters, *out_lower)
    d_quarters, out_lower = moved[:near], moved[near:]

    d_context = [d_quarters[0]] + [None] * (near - 1)
    for k in others:
        d_context[near - k] = to_near(d_quarters[k], k)
    grad_out = rows_product(d_attn, context_all[:rows]) + rows_product(d_attn_sib, context_all[rows:])
    grad_out = grad_out.astype(bf16)
    output_own = mid + joined(*near_back[2:])
    for pieces in zip(out_upper, out_third, out_lower, strict=True):
        output_own = output_own + jnp.concatenate(pieces, axis=0).astype(f32)
    output_own = output_own.astype(bf16)
    grad_out, output_own, gate_up_part, *d_context = stage(grad_out, output_own, gate_up_part, *d_context)

    output_crossed = crossed(output_own, CROSS)
    gate_up_keep, gate_up_give = give_z(gate_up_part)
    gate_up_back = crossed(gate_up_give, BACK)
    out_part = lax.psum_scatter(grad_out, "yx", scatter_dimension=0, tiled=True)
    d_qkv = attend_back(list(range(kv_heads)), qkv, d_context, context, sums, [], layout_back, q_heads, kv_heads)
    d_qkv, output_crossed, gate_up_back, gate_up_keep, down_part = stage(
        d_qkv, output_crossed, gate_up_back, gate_up_keep, down_part
    )

    def back_part(k):
        own, sib = (d_qkv[(2 * k + e) * rows : (2 * k + e + 1) * rows] for e in range(2))
        taken = flip(times_transpose(sib, w_project).astype(bf16), "core")
        return times_transpose(own, w_project) + taken.astype(f32)

    d_sent = [back_part(k).astype(bf16) for k in others]
    d_qkv, gate_up_keep, down_part, *d_sent = stage(d_qkv, gate_up_keep, down_part, *d_sent)

    output = jnp.where(straight(), output_own, output_crossed)

    d_upper = [to_near(d_sent[k - 1][:part_rows], k) for k in others]
    gate_up_cross = crossed(gate_up_keep, CROSS)
    grad_project = rows_product(norm_one, d_qkv).astype(bf16)
    project_sent = send_yx(grad_project, (0, qkv_cols))
    total = back_part(0)
    total, grad_project, gate_up_cross, down_part, *moved = stage(
        total, grad_project, gate_up_cross, down_part, *d_upper, *d_sent, *project_sent
    )
    d_upper, d_sent, project_sent = moved[: near - 1], moved[near - 1 : 2 * near - 2], moved[2 * near - 2 :]

    d_lower = [to_near(d_sent[k - 1][part_rows:], k) for k in others]
    down_keep, down_give = give_z(down_part)
    down_home = [crossed(down_give, BACK), crossed(down_keep, CROSS)]
    project_rest, project_own = join_yx(grad_project, (0, qkv_cols), project_sent)
    out_part, *moved = stage(out_part, *d_lower, *project_rest, *down_home)
    d_lower, project_rest, down_home = moved[: near - 1], moved[near - 1 : -2], moved[-2:]
    d_moved = [jnp.concatenate(x, axis=0) for x in zip(d_upper, d_lower, strict=True)]
    project_keep, project_give = give_z(total_yx(project_rest, project_own))

    project_home = [crossed(project_give, BACK), crossed(project_keep, CROSS)]
    for part in d_moved:
        total = total + part.astype(f32)
    input_back, _ = norm_back(residual, scale_one, gain_one, total)
    input_own = (d_mid + input_back).astype(bf16)
    out_moved = [to_near(out_part[:, k * query_cols : (k + 1) * query_cols], k) for k in others]
    out_quarter = out_part[:, :query_cols].astype(f32)
    for part in out_moved:
        out_quarter = out_quarter + part.astype(f32)
    out_keep, out_give = give_z(out_quarter.astype(bf16))
    out_home = [crossed(out_give, BACK), crossed(out_keep, CROSS)]
    input_grad = jnp.where(straight(), input_own, crossed(input_own, CROSS)).astype(f32)
    grad_project = sum_z(project_keep, *project_home)
    grad_out = sum_z(out_keep, *out_home)
    grad_down = sum_z(down_keep, *down_home)
    grad_gate_up = sum_z(gate_up_keep, gate_up_back, gate_up_cross)
    gain_grads = lax.psum(
        jnp.stack(
            [
                jnp.sum(qkv_shard.astype(f32) * grad_project, axis=1),
                jnp.sum(gate_up_shard.astype(f32) * grad_gate_up, axis=1),
            ]
        ),
        ("zh", "zl"),
    ) / jnp.stack([attn_gain, mlp_gain]).astype(f32)
    return (
        output,
        input_grad,
        gain_grads[0],
        grad_project[:, :query_cols],
        grad_project[:, query_cols : query_cols + key_cols],
        grad_project[:, query_cols + key_cols :],
        grad_out,
        gain_grads[1],
        grad_gate_up[:, :hidden_cols],
        grad_gate_up[:, hidden_cols:],
        grad_down,
    )


def solution(mesh):
    dp, tensor = mesh.shape["dp"], mesh.shape["tensor"]
    fine = Mesh(mesh.devices.reshape(dp // 2, 2, 2, tensor // 2), AXES)
    by_rows, by_dp, by_both = P(AXES, None), P(("yx", "core")), P(("yx", "core"), ("zh", "zl"))
    return jax.shard_map(
        body,
        mesh=fine,
        in_specs=(
            by_rows, by_rows, P(("yx", "core"), None), by_dp, by_both, by_both, by_both, by_both,
            by_dp, by_both, by_both, by_both,
        ),
        out_specs=(
            by_rows, by_rows, by_dp, by_both, by_both, by_both, by_both, by_dp, by_both, by_both, by_both,
        ),
        check_vma=False,
    )
```
